32 devices in a mesh: ctx: 4 (over y, x), fsdp: 8 (over z, core).
Axes of the slice: x: 2, y: 2, z: 4, core: 2. Of those that a mesh axis runs over, the one named last changes fastest.
Arguments:
- tokens: bfloat16 [8, 1024, 1536], P('fsdp', 'ctx'), may hold values from -6 to 6
- cotangent: bfloat16 [8, 1024, 1536], P('fsdp', 'ctx'), may hold values from -6 to 6
- doc_starts: int32 [8, 5], P('fsdp'), may hold values from 0 to 1022, as said below
- block_order: int32 [4, 2], replicated, may hold values from 0 to 7, as said below
- master_weights: float32 [1536, 24832], P(('ctx', 'fsdp')), may hold values from -0.30618622 to 0.30618622
- moment_one: float32 [1536, 24832], P(('ctx', 'fsdp'))
- moment_two: float32 [1536, 24832], P(('ctx', 'fsdp')), as said below
- gains: float32 [3200], replicated, may hold values from 0.5 to 1.5
- gains_moment_one: float32 [3200], replicated
- gains_moment_two: float32 [3200], replicated, as said below
Outputs:
- out_tokens: bfloat16 [8, 1024, 1536], P('fsdp', 'ctx')
- grad_tokens: float32 [8, 1024, 1536], P('fsdp', 'ctx')
- new_moment_one: float32 [1536, 24832], P(('ctx', 'fsdp'))
- new_moment_two: float32 [1536, 24832], P(('ctx', 'fsdp'))
- new_master: float32 [1536, 24832], P(('ctx', 'fsdp'))
- new_weights: bfloat16 [1536, 24832], P(('ctx', 'fsdp'))
- new_gains_one: float32 [3200], replicated
- new_gains_two: float32 [3200], replicated
- new_gains: float32 [3200], replicated
The draws below stay inside these ranges and needn't reach their ends.
Inputs may be any that keep to these rules, and one draw needn't show every extreme that they name: `doc_starts`: in each row entries rise strictly from 0 at the first; the third document runs from below position 128 to beyond 1024 - 128. `block_order`: rows name each block 0 to 7 once; a row holds blocks b and 7 - b. `moment_two`: entries are positive. `gains_moment_two`: entries are positive.
All inputs are finite; a program needn't handle non-finite values.
Results may differ from the reference program's by a relative error of at most 0.025.
Values may be sent and summed in bfloat16 or wider, within the bound.
A program may use at most 384 MiB of HBM per device.

```python
import jax
import jax.numpy as jnp
from jax import lax

D = 1536
HEADS = 24
KVHEADS = 8
HD = 64
FF = 6912
STEP = 10
HALF = 128
STREAM = 1024
STREAMS = 8
TOKENS = 8192
BLOCKS = 8
KBLOCK = 512
KVD = 512
QKVC = 2560
WCOLS = 24832
GAINS = 3200


def column_spread():
    column = jnp.arange(WCOLS)
    wide_std = (STREAM // 64) ** 0.5 * D ** (-0.5)
    return jnp.where(column < QKVC, D ** (-0.5), jnp.where(column < QKVC + D, wide_std, jnp.where(column < QKVC + D + 2 * FF, D ** (-0.5), FF ** (-0.5))))


def grad_size():
    column = jnp.arange(WCOLS)
    root_tokens = TOKENS ** 0.5
    return root_tokens * jnp.where(column < QKVC, 0.3, jnp.where(column < QKVC + D, 5.0 * STREAM ** (-0.5), jnp.where(column < QKVC + D + 2 * FF, 0.3, 0.6)))


def gain_grad_size():
    index_vec = jnp.arange(GAINS)
    return jnp.where(index_vec < 2 * D, 0.4 * TOKENS ** 0.5, jnp.where(index_vec < 2 * D + HD, 0.2 * (TOKENS * HEADS) ** 0.5, 0.3 * (TOKENS * KVHEADS) ** 0.5))


def draw_doc_starts(key, part):
    key = jax.random.fold_in(key, 11)
    key_list = jax.random.split(key, 5)
    head_one = jax.random.randint(key_list[0], (STREAMS,), 1, HALF // 2)
    head_two = head_one + jax.random.randint(key_list[1], (STREAMS,), 1, HALF // 2)
    tail_one = STREAM - HALF + jax.random.randint(key_list[2], (STREAMS,), 1, HALF // 2)
    tail_two = tail_one + jax.random.randint(key_list[3], (STREAMS,), 1, HALF // 2)
    chosen_row = jax.random.randint(key_list[4], (), 0, STREAMS)
    tail_two = jnp.where(jnp.arange(STREAMS) == chosen_row, STREAM - 2, tail_two)
    zero_col = jnp.zeros((STREAMS,), jnp.int32)
    return jnp.stack([zero_col, head_one, head_two, tail_one, tail_two], axis=1).astype(jnp.int32)


def draw_block_order(key, part):
    key = jax.random.fold_in(key, 23)
    key_perm, key_flip = jax.random.split(key)
    low_block = jax.random.permutation(key_perm, BLOCKS // 2).astype(jnp.int32)
    high_block = BLOCKS - 1 - low_block
    flip_order = jax.random.randint(key_flip, (BLOCKS // 2,), 0, 2)
    first_col = jnp.where(flip_order == 1, high_block, low_block)
    second_col = jnp.where(flip_order == 1, low_block, high_block)
    return jnp.stack([first_col, second_col], axis=1).astype(jnp.int32)


def draw_master_weights(key, part):
    key = jax.random.fold_in(key, 5)
    normal_vals = jax.random.truncated_normal(key, -3.0, 3.0, (D, WCOLS), jnp.float32)
    return normal_vals * column_spread()[None, :]


def draw_moment_one(key, part):
    key = jax.random.fold_in(key, 7)
    normal_vals = jax.random.truncated_normal(key, -3.0, 3.0, (D, WCOLS), jnp.float32)
    return normal_vals * (0.111 * grad_size())[None, :]


def draw_moment_two(key, part):
    key = jax.random.fold_in(key, 9)
    factor = jnp.exp(jax.random.uniform(key, (D, WCOLS), jnp.float32, jnp.log(0.5), jnp.log(2.0)))
    return 0.105 * factor * (grad_size() ** 2)[None, :]


def draw_gains_moment_one(key, part):
    key = jax.random.fold_in(key, 13)
    normal_vals = jax.random.truncated_normal(key, -3.0, 3.0, (GAINS,), jnp.float32)
    return normal_vals * 0.111 * gain_grad_size()


def draw_gains_moment_two(key, part):
    key = jax.random.fold_in(key, 17)
    factor = jnp.exp(jax.random.uniform(key, (GAINS,), jnp.float32, jnp.log(0.5), jnp.log(2.0)))
    return 0.105 * factor * gain_grad_size() ** 2


def block_scale(stream_key, dims, pieces, smallest, top_value):
    def one(axis_at, blocks):
        steps = jax.random.uniform(jax.random.fold_in(jax.random.fold_in(stream_key, 6), axis_at), (blocks,), jnp.float32, smallest / len(pieces), top_value / len(pieces))
        return jnp.repeat(jnp.exp(steps), dims[axis_at] // blocks).reshape((-1,) + (1,) * (len(dims) - axis_at - 1))

    factor_of = one(*pieces[0])
    for cut in pieces[1:]:
        factor_of = factor_of * one(*cut)
    return factor_of


def normal_values(key, extent, scale, reach, cuts=(), kind=jnp.bfloat16):
    values = scale * jax.random.normal(key, extent, jnp.float32)
    if cuts:
        values = values * block_scale(key, extent, cuts, -0.22, 0.18)
    return jnp.clip(values, -reach, reach).astype(kind)


def setup_inputs(seed: int = 0) -> dict:
    key_of = jax.random.split(jax.random.key(seed), 11)
    return {
        "tokens": normal_values(key_of[0], (STREAMS, STREAM, D), 1.0, 6.0, ((0, 8), (1, 4))),
        "cotangent": normal_values(key_of[1], (STREAMS, STREAM, D), 1.0, 6.0, ((0, 8), (1, 4))),
        "doc_starts": draw_doc_starts(jax.random.fold_in(key_of[10], 71), 0),
        "block_order": draw_block_order(jax.random.fold_in(key_of[10], 71), 0),
        "master_weights": draw_master_weights(jax.random.fold_in(key_of[10], 71), 0),
        "moment_one": draw_moment_one(jax.random.fold_in(key_of[10], 71), 0),
        "moment_two": draw_moment_two(jax.random.fold_in(key_of[10], 71), 0),
        "gains": jnp.clip(1.0 + 0.1 * jax.random.normal(key_of[7], (GAINS,), jnp.float32), 0.5, 1.5),
        "gains_moment_one": draw_gains_moment_one(jax.random.fold_in(key_of[10], 71), 0),
        "gains_moment_two": draw_gains_moment_two(jax.random.fold_in(key_of[10], 71), 0),
    }


ROPE_BASE = 1000000.0
NORM_EPS = 1e-05
MASKED_SCORE = -1e+30
BETA_ONE = 0.9
BETA_TWO = 0.95
ADAM_EPS = 1e-08
WEIGHT_DECAY = 0.1
LEARN_RATE = 0.03
GAIN_RATE = 0.5

@jax.custom_vjp
def low(v):
    return lax.optimization_barrier(v.astype(jnp.bfloat16)).astype(jnp.float32)

@jax.custom_vjp
def low_back(v):
    return v

def low_keep(v):
    return (low(v), None)

def low_pass(kept, grad):
    return (grad,)

def back_keep(v):
    return (v, None)

def back_low(kept, grad):
    return (low(grad),)
low.defvjp(low_keep, low_pass)
low_back.defvjp(back_keep, back_low)

def rms_scale(values_in, gain_vec):
    return values_in * lax.rsqrt(lax.optimization_barrier(jnp.mean(values_in * values_in, axis=-1, keepdims=True)) + NORM_EPS) * gain_vec

def inverse_freq():
    return 1.0 / ROPE_BASE ** (jnp.arange(0, HD, 2).astype(jnp.float32) / HD)

def rotate(values_in, angles):
    half_size = values_in.shape[-1] // 2
    first_half = values_in[..., :half_size]
    second_half = values_in[..., half_size:]
    cosine = jnp.cos(angles)[:, None, :]
    sine = jnp.sin(angles)[:, None, :]
    return jnp.concatenate([first_half * cosine - second_half * sine, second_half * cosine + first_half * sine], axis=-1)

def mix_heads(queries, keys_in, values_in, positions, documents):
    head_group = HEADS // KVHEADS
    block_count = STREAM // KBLOCK
    grouped = queries.reshape(block_count, KBLOCK, KVHEADS, head_group, HD)
    query_pos = positions.reshape(block_count, KBLOCK)
    query_doc = documents.reshape(block_count, KBLOCK)

    def one_block(block_item):
        query_block, block_pos, block_doc = block_item
        raw_scores = jnp.einsum('tkgd,skd->kgts', query_block, keys_in, precision=lax.Precision.HIGHEST) * HD ** (-0.5)
        scores = low_back(raw_scores)
        allowed = (block_doc[:, None] == documents[None, :]) & (positions[None, :] <= block_pos[:, None])
        masked = jnp.where(allowed, scores, MASKED_SCORE)
        top_score = lax.optimization_barrier(jnp.max(masked, axis=-1, keepdims=True))
        expo = jnp.where(allowed, jnp.exp(masked - top_score), 0.0)
        soft_weights = low(expo / lax.optimization_barrier(jnp.sum(expo, axis=-1, keepdims=True)))
        return jnp.einsum('kgts,skd->tkgd', soft_weights, values_in, precision=lax.Precision.HIGHEST)
    mixed = lax.map(jax.checkpoint(one_block), (grouped, query_pos, query_doc))
    return mixed.reshape(STREAM, D)

def layer(stream_in, flat_weights, gain_all, positions, documents, relative):
    weights = low(flat_weights)
    w_qkv = weights[:, :QKVC]
    w_out = weights[:, QKVC:QKVC + D]
    w_gu = weights[:, QKVC + D:QKVC + D + 2 * FF]
    w_down = weights[:, QKVC + D + 2 * FF:]
    g_attn = gain_all[:D]
    g_ffn = gain_all[D:2 * D]
    g_query = gain_all[2 * D:2 * D + HD]
    g_key = gain_all[2 * D + HD:]
    normed = low(rms_scale(stream_in, g_attn))
    joined_qkv = low_back(jnp.dot(normed, w_qkv, precision=lax.Precision.HIGHEST, preferred_element_type=jnp.float32))
    queries = joined_qkv[:, :D].reshape(STREAM, HEADS, HD)
    keys_in = joined_qkv[:, D:D + KVD].reshape(STREAM, KVHEADS, HD)
    values_in = low(joined_qkv[:, D + KVD:].reshape(STREAM, KVHEADS, HD))
    angles = relative[:, None] * inverse_freq()[None, :]
    queries = low(rotate(rms_scale(queries, g_query), angles))
    keys_in = low(rotate(rms_scale(keys_in, g_key), angles))
    mixed = low_back(low(mix_heads(queries, keys_in, values_in, positions, documents)))
    attended = low_back(jnp.dot(mixed, w_out.T, precision=lax.Precision.HIGHEST, preferred_element_type=jnp.float32))
    middle = stream_in + attended
    normed_two = low(rms_scale(middle, g_ffn))
    gate_up = low_back(jnp.dot(normed_two, w_gu, precision=lax.Precision.HIGHEST, preferred_element_type=jnp.float32))
    hidden = low(jax.nn.silu(gate_up[:, :FF]) * gate_up[:, FF:])
    return middle + jnp.dot(hidden, w_down.T, precision=lax.Precision.HIGHEST, preferred_element_type=jnp.float32)

def adam_update(param_now, grad_now, moment_old_one, moment_old_two, step_rate, decay_rate):
    first_new = BETA_ONE * moment_old_one + (1.0 - BETA_ONE) * grad_now
    second_new = BETA_TWO * moment_old_two + (1.0 - BETA_TWO) * grad_now * grad_now
    ratio = first_new / (1.0 - BETA_ONE ** STEP) / (jnp.sqrt(second_new / (1.0 - BETA_TWO ** STEP)) + ADAM_EPS)
    return (first_new, second_new, param_now - step_rate * (ratio + decay_rate * param_now))

def reference(tokens, cotangent, doc_starts, block_order, master_weights, moment_one, moment_two, gains, gains_moment_one, gains_moment_two):
    offsets = jnp.arange(HALF, dtype=jnp.int32)
    positions = (block_order[:, :, None] * HALF + offsets[None, None, :]).reshape(STREAM).astype(jnp.int32)

    def one_stream(running_state, stream_item):
        stream_in, stream_back, starts = stream_item
        before = starts[None, :] <= positions[:, None]
        documents = (lax.optimization_barrier(jnp.sum(before.astype(jnp.int32), axis=1)) - 1).astype(jnp.int32)
        doc_first = lax.optimization_barrier(jnp.max(jnp.where(before, starts[None, :], 0), axis=1))
        relative = (positions - doc_first).astype(jnp.float32)

        def forward(first_arg, second_arg, third_arg):
            return layer(first_arg, second_arg, third_arg, positions, documents, relative)
        result, pullback = jax.vjp(forward, stream_in.astype(jnp.float32), master_weights, gains)
        grad_in, grad_flat, grad_gain = pullback(stream_back.astype(jnp.float32))
        return ((running_state[0] + grad_flat, running_state[1] + grad_gain), (result.astype(jnp.bfloat16), grad_in))
    start_state = (jnp.zeros(master_weights.shape, jnp.float32), jnp.zeros(gains.shape, jnp.float32))
    (grad_flat, grad_gain), (outputs, grad_tokens) = lax.scan(one_stream, start_state, (tokens, cotangent, doc_starts))
    first_new, second_new, master_new = adam_update(master_weights, grad_flat, moment_one, moment_two, LEARN_RATE, WEIGHT_DECAY)
    gain_first, gain_second, gain_new = adam_update(gains, grad_gain, gains_moment_one, gains_moment_two, GAIN_RATE, 0.0)
    return (outputs, grad_tokens, first_new, second_new, master_new, master_new.astype(jnp.bfloat16), gain_first, gain_second, gain_new)
```

```python
import functools

import jax
import jax.numpy as jnp
from jax import lax
from jax.experimental import pallas as pl
from jax.experimental.pallas import tpu as pltpu
from jax.sharding import PartitionSpec as P

D = 1536
HEADS = 24
KVHEADS = 8
HD = 64
FF = 6912
STEP = 10
HALF = 128
KVD = 512
QKVC = 2560
GROUP = HEADS // KVHEADS

ROPE_BASE = 1000000.0
NORM_EPS = 1e-05
BETA_ONE = 0.9
BETA_TWO = 0.95
ADAM_EPS = 1e-08
WEIGHT_DECAY = 0.1
LEARN_RATE = 0.03
GAIN_RATE = 0.5
SCALE = HD ** (-0.5)
MESH = pl.DeviceIdType.MESH
F32 = jnp.float32
BF16 = jnp.bfloat16
VMEM_LIMIT = 60 * 1024 * 1024


def dot(left, right, left_dim, right_dim):
    return lax.dot_general(
        left, right, (((left_dim,), (right_dim,)), ((), ())), preferred_element_type=F32
    )


def exchange_kernel(kinds, ctx_size, *refs):
    count = len(kinds)
    ins, outs = refs[:count], refs[count : 2 * count]
    send_sem, recv_sem, local_sem = refs[2 * count :]
    me = lax.axis_index("ctx")
    barrier = pltpu.get_barrier_semaphore()
    for step in range(1, ctx_size):
        pl.semaphore_signal(
            barrier, inc=1, device_id={"ctx": lax.rem(me + step, ctx_size)}, device_id_type=MESH
        )
    pl.semaphore_wait(barrier, ctx_size - 1)
    copies = []
    for item in range(count):
        for step in range(1, ctx_size):
            peer = lax.rem(me + step, ctx_size)
            source = ins[item] if kinds[item] == "gather" else ins[item].at[peer]
            copy = pltpu.make_async_remote_copy(
                src_ref=source,
                dst_ref=outs[item].at[me],
                send_sem=send_sem.at[item, step],
                recv_sem=recv_sem.at[item, step],
                device_id={"ctx": peer},
                device_id_type=MESH,
            )
            copy.start()
            copies.append(copy)
        source = ins[item] if kinds[item] == "gather" else ins[item].at[me]
        copy = pltpu.make_async_copy(source, outs[item].at[me], local_sem.at[item])
        copy.start()
        copies.append(copy)
    for copy in copies:
        copy.wait()


def exchange(kinds, arrays, ctx_size, collective_id):
    shapes = [
        jax.ShapeDtypeStruct(
            (ctx_size,) + a.shape if kind == "gather" else a.shape, a.dtype
        )
        for kind, a in zip(kinds, arrays)
    ]
    return pl.pallas_call(
        functools.partial(exchange_kernel, kinds, ctx_size),
        out_shape=shapes,
        in_specs=[pl.BlockSpec(memory_space=pl.ANY)] * len(arrays),
        out_specs=[pl.BlockSpec(memory_space=pl.ANY)] * len(arrays),
        scratch_shapes=[
            pltpu.SemaphoreType.DMA((len(arrays), ctx_size)),
            pltpu.SemaphoreType.DMA((len(arrays), ctx_size)),
            pltpu.SemaphoreType.DMA((len(arrays),)),
        ],
        compiler_params=pltpu.CompilerParams(
            collective_id=collective_id, has_side_effects=True
        ),
    )(*arrays)


def head_mean(values, ones):
    high = values.astype(BF16)
    rest = (values - high.astype(F32)).astype(BF16)
    return (dot(high, ones, 1, 0) + dot(rest, ones, 1, 0)) * (1.0 / HD)


def head_ones(width):
    row = lax.broadcasted_iota(jnp.int32, (width, width), 0) // HD
    col = lax.broadcasted_iota(jnp.int32, (width, width), 1) // HD
    return jnp.where(row == col, 1.0, 0.0).astype(BF16)


def partner(values):
    width = values.shape[-1]
    lane = lax.broadcasted_iota(jnp.int32, values.shape, 1)
    return jnp.where(
        lane % HD < HD // 2,
        pltpu.roll(values, width - HD // 2, 1),
        pltpu.roll(values, HD // 2, 1),
    )


def widen(table, width):
    return jnp.concatenate([table] * (width // table.shape[-1]), axis=-1)


def rope_kernel(qk_width, blocks, place, qkv, cosine, sine, gain, q_out, k_out, v_out):
    ones = head_ones(qk_width)
    q_width = q_out.shape[1]
    for block in range(blocks):
        rows = pl.ds(pl.multiple_of(place[block] * HALF, HALF), HALF)
        to = slice(block * HALF, (block + 1) * HALF)
        values = qkv[rows, :qk_width]
        normed = values * lax.rsqrt(head_mean(values * values, ones) + NORM_EPS) * gain[...]
        turned = normed * widen(cosine[to, :], qk_width) + partner(normed) * widen(
            sine[to, :], qk_width
        )
        turned = turned.astype(BF16)
        q_out[to, :] = turned[:, :q_width]
        k_out[to, :] = turned[:, q_width:]
        v_out[to, :] = qkv[rows, qk_width:].astype(BF16)


def rope_back_kernel(
    qk_width, blocks, place, qkv, cosine, sine, gain, dq, dk, dv, out, gain_out
):
    ones = head_ones(qk_width)
    total = jnp.zeros((1, qk_width), F32)
    for block in range(blocks):
        rows = pl.ds(pl.multiple_of(place[block] * HALF, HALF), HALF)
        to = slice(block * HALF, (block + 1) * HALF)
        values = qkv[rows, :qk_width]
        root = lax.rsqrt(head_mean(values * values, ones) + NORM_EPS)
        unit = values * root
        grad = jnp.concatenate([dq[to, :], dk[to, :]], axis=1)
        grad = grad * widen(cosine[to, :], qk_width) - partner(grad) * widen(
            sine[to, :], qk_width
        )
        total = total + jnp.sum(grad * unit, axis=0, keepdims=True)
        grad = grad * gain[...]
        grad = root * (grad - unit * head_mean(grad * unit, ones))
        out[rows, :qk_width] = grad.astype(BF16)
        out[rows, qk_width:] = dv[to, :].astype(BF16)
    gain_out[...] = total


def doc_first(starts, times):
    first = jnp.zeros_like(times)
    for item in range(starts.shape[0]):
        first = jnp.where(starts[item] <= times, starts[item], first)
    return first


def block_mask(starts, block, keys):
    shape = (keys, GROUP * HALF)
    times = block * HALF + lax.broadcasted_iota(jnp.int32, (1, GROUP * HALF), 1) % HALF
    key = lax.broadcasted_iota(jnp.int32, shape, 0)
    return (key >= doc_first(starts, times)) & (key <= times)


def stack_heads(ref, rows, group):
    return jnp.concatenate(
        [
            ref[rows, (group * GROUP + h) * HD : (group * GROUP + h + 1) * HD]
            for h in range(GROUP)
        ],
        axis=0,
    )


def unstack_heads(turned):
    wide = turned.T
    return [wide[h * HALF : (h + 1) * HALF, :] for h in range(GROUP)]


def attend_kernel(blocks, groups, place, starts, q, k, v, o, lse):
    for block in range(blocks):
        rows = slice(block * HALF, (block + 1) * HALF)
        keys = (block + 1) * HALF
        mask = block_mask(starts, block, keys)
        pieces = []
        for group in range(groups):
            lanes = slice(group * HD, (group + 1) * HD)
            queries = stack_heads(q, rows, group)
            scores = dot(k[:keys, lanes], queries, 1, 1) * SCALE
            weights = jnp.where(mask, jnp.exp(scores), 0.0)
            sums = jnp.sum(weights, axis=0, keepdims=True)
            lse[block, group : group + 1, :] = jnp.log(sums)
            mixed = dot(v[:keys, lanes], weights.astype(BF16), 0, 0) / sums
            pieces += unstack_heads(mixed)
        to = pl.ds(pl.multiple_of(place[block] * HALF, HALF), HALF)
        o[to, :] = jnp.concatenate(pieces, axis=1).astype(BF16)


def attend_back_kernel(blocks, groups, place, starts, q, k, v, lse, do, dq, dk, dv):
    dk[...] = jnp.zeros_like(dk)
    dv[...] = jnp.zeros_like(dv)
    for block in range(blocks):
        rows = slice(block * HALF, (block + 1) * HALF)
        keys = (block + 1) * HALF
        mask = block_mask(starts, block, keys)
        source = pl.ds(pl.multiple_of(place[block] * HALF, HALF), HALF)
        pieces = []
        dk_add = []
        dv_add = []
        for group in range(groups):
            lanes = slice(group * HD, (group + 1) * HD)
            queries = stack_heads(q, rows, group)
            outs = stack_heads(do, source, group)
            key_rows = k[:keys, lanes]
            scores = dot(key_rows, queries, 1, 1) * SCALE
            weights = jnp.where(
                mask, jnp.exp(scores - lse[block, group : group + 1, :]), 0.0
            )
            back = dot(v[:keys, lanes], outs, 1, 1)
            delta = jnp.sum(weights * back, axis=0, keepdims=True)
            grads = (weights * (back - delta)).astype(BF16)
            pieces += unstack_heads(dot(key_rows, grads, 0, 0) * SCALE)
            dk_add.append(dot(grads, queries, 1, 0) * SCALE)
            dv_add.append(dot(weights.astype(BF16), outs, 1, 0))
        dq[rows, :] = jnp.concatenate(pieces, axis=1)
        dk[:keys, :] += jnp.concatenate(dk_add, axis=1)
        dv[:keys, :] += jnp.concatenate(dv_add, axis=1)


def local_call(kernel, out_shape, smem_count, args):
    return pl.pallas_call(
        kernel,
        out_shape=out_shape,
        in_specs=[pl.BlockSpec(memory_space=pltpu.SMEM)] * smem_count
        + [pl.BlockSpec(memory_space=pltpu.VMEM)] * (len(args) - smem_count),
        compiler_params=pltpu.CompilerParams(vmem_limit_bytes=VMEM_LIMIT),
    )(*args)


def rms_scale(values_in, gain_vec):
    return (
        values_in
        * lax.rsqrt(jnp.mean(values_in * values_in, axis=-1, keepdims=True) + NORM_EPS)
        * gain_vec
    )


def inverse_freq():
    return 1.0 / ROPE_BASE ** (jnp.arange(0, HD, 2).astype(F32) / HD)


def adam_update(param_now, grad_now, moment_old_one, moment_old_two, step_rate, decay_rate):
    first_new = BETA_ONE * moment_old_one + (1.0 - BETA_ONE) * grad_now
    second_new = BETA_TWO * moment_old_two + (1.0 - BETA_TWO) * grad_now * grad_now
    ratio = (
        first_new
        / (1.0 - BETA_ONE**STEP)
        / (jnp.sqrt(second_new / (1.0 - BETA_TWO**STEP)) + ADAM_EPS)
    )
    return (first_new, second_new, param_now - step_rate * (ratio + decay_rate * param_now))


def shards(
    tokens,
    cotangent,
    doc_starts,
    block_order,
    master_weights,
    moment_one,
    moment_two,
    gains,
    gains_moment_one,
    gains_moment_two,
):
    nctx = lax.axis_size("ctx")
    nfsdp = lax.axis_size("fsdp")
    own_rows = master_weights.shape[0]
    tok_rows = tokens.shape[1]
    stream_len = tok_rows * nctx
    blocks = stream_len // HALF
    groups = KVHEADS // nctx
    q_width = D // nctx
    kv_width = KVD // nctx
    qk_width = q_width + kv_width
    qkv_width = qk_width + kv_width
    tiles = FF // 128
    ff_tiles = -(-tiles // nctx)
    ff_width = ff_tiles * 128
    bundles = 2
    cuts = [ff_width * b // (bundles * 128) * 128 for b in range(bundles + 1)]

    low = master_weights.astype(BF16)

    def ff_part(base, index, start, stop):
        first = index * ff_width + start
        last = index * ff_width + stop
        real_first, real_last = min(first, FF), min(last, FF)
        part = low[:, base + real_first : base + real_last]
        if real_last - real_first < last - first:
            part = jnp.pad(part, ((0, 0), (0, (last - first) - (real_last - real_first))))
        return part

    def attn_part(index):
        return jnp.concatenate(
            [
                low[:, index * q_width : (index + 1) * q_width],
                low[:, D + index * kv_width : D + (index + 1) * kv_width],
                low[:, D + KVD + index * kv_width : D + KVD + (index + 1) * kv_width],
                low[:, QKVC + index * q_width : QKVC + (index + 1) * q_width],
            ],
            axis=1,
        )

    gate_base = QKVC + D
    bases = (gate_base, gate_base + FF, gate_base + 2 * FF)
    attn_send = jnp.stack([attn_part(c) for c in range(nctx)])
    ff_send = [
        jnp.stack(
            [
                jnp.concatenate(
                    [ff_part(base, c, cuts[b], cuts[b + 1]) for base in bases], axis=1
                )
                for c in range(nctx)
            ]
        )
        for b in range(bundles)
    ]

    def gather_rows(piece):
        return lax.all_gather(
            piece.reshape(nctx * own_rows, piece.shape[-1]), "fsdp", axis=0, tiled=True
        )

    def spread(active):
        return (
            active.reshape(active.shape[0], nctx, nfsdp, own_rows)
            .transpose(0, 2, 1, 3)
            .reshape(active.shape[0], D)
        )

    def unspread(active):
        return (
            active.reshape(active.shape[0], nfsdp, nctx, own_rows)
            .transpose(0, 2, 1, 3)
            .reshape(active.shape[0], D)
        )

    (attn_held,) = exchange(("swap",), [attn_send], nctx, 0)
    w_attn = gather_rows(attn_held)
    ff_held = exchange(("swap",) * bundles, ff_send, nctx, 1)
    w_ff = [gather_rows(piece) for piece in ff_held]

    order = block_order.reshape(blocks)
    place = jnp.argsort(order).astype(jnp.int32)
    starts = doc_starts[0]
    times = jnp.arange(stream_len, dtype=jnp.int32)
    first = jnp.max(jnp.where(starts[None, :] <= times[:, None], starts[None, :], 0), axis=1)
    angles = (times - first).astype(F32)[:, None] * inverse_freq()[None, :]
    cosine = jnp.concatenate([jnp.cos(angles)] * 2, axis=1)
    sine = jnp.concatenate([-jnp.sin(angles), jnp.sin(angles)], axis=1)

    g_attn = spread(gains[None, :D])[0]
    g_ffn = spread(gains[None, D : 2 * D])[0]
    g_query = gains[2 * D : 2 * D + HD]
    g_key = gains[2 * D + HD :]
    qk_gain = jnp.concatenate(
        [jnp.tile(g_query, q_width // HD), jnp.tile(g_key, kv_width // HD)]
    )[None]

    stream_in = spread(tokens[0]).astype(F32)
    back_grad = spread(cotangent[0])
    normed = rms_scale(stream_in, g_attn).astype(BF16)
    normed_all, back_all = exchange(("gather", "gather"), [normed, back_grad], nctx, 2)
    normed_all = normed_all.reshape(stream_len, D)
    back_all = back_all.reshape(stream_len, D)
    joined = dot(normed_all, w_attn[:, :qkv_width], 1, 0)
    q, k, v = local_call(
        functools.partial(rope_kernel, qk_width, blocks),
        [
            jax.ShapeDtypeStruct((stream_len, q_width), BF16),
            jax.ShapeDtypeStruct((stream_len, kv_width), BF16),
            jax.ShapeDtypeStruct((stream_len, kv_width), BF16),
        ],
        1,
        (place, joined, cosine, sine, qk_gain),
    )
    mixed, lse = local_call(
        functools.partial(attend_kernel, blocks, groups),
        [
            jax.ShapeDtypeStruct((stream_len, q_width), BF16),
            jax.ShapeDtypeStruct((blocks, groups, GROUP * HALF), F32),
        ],
        2,
        (place, starts, q, k, v),
    )
    w_out = w_attn[:, qkv_width:]

    def ctx_sum(partial, collective_id):
        (parts,) = exchange(
            ("swap",),
            [partial.astype(BF16).reshape(nctx, tok_rows, D)],
            nctx,
            collective_id,
        )
        return jnp.sum(parts.astype(F32), axis=0)

    middle = stream_in + ctx_sum(dot(mixed, w_out, 1, 1), 3)
    normed_two = rms_scale(middle, g_ffn).astype(BF16)
    (normed_two_all,) = exchange(("gather",), [normed_two], nctx, 4)
    normed_two_all = normed_two_all.reshape(stream_len, D)

    out_partial = 0.0
    back_partial = 0.0
    ff_grads = []
    for b in range(bundles):
        width = cuts[b + 1] - cuts[b]
        w_gu, w_down = w_ff[b][:, : 2 * width], w_ff[b][:, 2 * width :]
        gate_up = dot(normed_two_all, w_gu, 1, 0)
        gate, up = gate_up[:, :width], gate_up[:, width:]
        gated = jax.nn.sigmoid(gate)
        act = gate * gated
        hidden = (act * up).astype(BF16)
        back_hidden = dot(back_all, w_down, 1, 0)
        grad_gu = jnp.concatenate(
            [back_hidden * up * (gated + act * (1.0 - gated)), back_hidden * act], axis=1
        ).astype(BF16)
        out_partial = out_partial + dot(hidden, w_down, 1, 1)
        back_partial = back_partial + dot(grad_gu, w_gu, 1, 1)
        ff_grads.append(
            jnp.concatenate(
                [dot(normed_two_all, grad_gu, 0, 0), dot(back_all, hidden, 0, 0)], axis=1
            ).astype(BF16)
        )

    def sum_rows(grad):
        return lax.psum_scatter(grad, "fsdp", scatter_dimension=0, tiled=True).reshape(
            nctx, own_rows, grad.shape[-1]
        )

    grad_normed_two = ctx_sum(back_partial, 5)
    output = middle + ctx_sum(out_partial, 6)
    out_tokens = unspread(output.astype(BF16))[None]

    _, ffn_pull = jax.vjp(rms_scale, middle, g_ffn)
    grad_mid_part, grad_g_ffn = ffn_pull(grad_normed_two)
    grad_middle = back_grad.astype(F32) + grad_mid_part
    (grad_middle_all,) = exchange(("gather",), [grad_middle.astype(BF16)], nctx, 7)
    grad_middle_all = grad_middle_all.reshape(stream_len, D)
    grad_mixed = dot(grad_middle_all, w_out, 1, 0).astype(BF16)
    grad_out_rows = dot(grad_middle_all, mixed, 0, 0)
    dq, dk, dv = local_call(
        functools.partial(attend_back_kernel, blocks, groups),
        [
            jax.ShapeDtypeStruct((stream_len, q_width), F32),
            jax.ShapeDtypeStruct((stream_len, kv_width), F32),
            jax.ShapeDtypeStruct((stream_len, kv_width), F32),
        ],
        2,
        (place, starts, q, k, v, lse, grad_mixed),
    )
    grad_joined, qk_gain_grad = local_call(
        functools.partial(rope_back_kernel, qk_width, blocks),
        [
            jax.ShapeDtypeStruct((stream_len, qkv_width), BF16),
            jax.ShapeDtypeStruct((1, qk_width), F32),
        ],
        1,
        (place, joined, cosine, sine, qk_gain, dq, dk, dv),
    )
    grad_normed = ctx_sum(dot(grad_joined, w_attn[:, :qkv_width], 1, 1), 8)
    attn_grad = jnp.concatenate(
        [dot(normed_all, grad_joined, 0, 0), grad_out_rows], axis=1
    ).astype(BF16)
    _, attn_pull = jax.vjp(rms_scale, stream_in, g_attn)
    grad_in_part, grad_g_attn = attn_pull(grad_normed)
    grad_tokens = unspread(grad_middle + grad_in_part)[None]
    gain_grad = lax.psum(
        jnp.concatenate(
            [
                unspread(grad_g_attn[None])[0],
                unspread(grad_g_ffn[None])[0],
                jnp.sum(qk_gain_grad[0, :q_width].reshape(-1, HD), axis=0),
                jnp.sum(qk_gain_grad[0, q_width:].reshape(-1, HD), axis=0),
            ]
        ),
        ("ctx", "fsdp"),
    )

    ff_own = exchange(("swap",) * bundles, [sum_rows(grad) for grad in ff_grads], nctx, 9)
    (attn_own,) = exchange(("swap",), [sum_rows(attn_grad)], nctx, 10)
    columns = []
    for begin, stop in (
        (0, q_width),
        (q_width, qk_width),
        (qk_width, qkv_width),
        (qkv_width, qkv_width + q_width),
    ):
        columns += [attn_own[c, :, begin:stop] for c in range(nctx)]
    for part in range(3):
        for c in range(nctx):
            for b in range(bundles):
                width = cuts[b + 1] - cuts[b]
                real = min(max(FF - (c * ff_width + cuts[b]), 0), width)
                if real:
                    columns.append(ff_own[b][c, :, part * width : part * width + real])
    weight_grad = jnp.concatenate(columns, axis=1).astype(F32)
    first_new, second_new, master_new = adam_update(
        master_weights, weight_grad, moment_one, moment_two, LEARN_RATE, WEIGHT_DECAY
    )
    gain_first, gain_second, gain_new = adam_update(
        gains, gain_grad, gains_moment_one, gains_moment_two, GAIN_RATE, 0.0
    )
    return (
        out_tokens,
        grad_tokens,
        first_new,
        second_new,
        master_new,
        master_new.astype(BF16),
        gain_first,
        gain_second,
        gain_new,
    )


def solution(mesh):
    rows = P("fsdp", "ctx", None)
    weights = P(("ctx", "fsdp"), None)
    return jax.shard_map(
        shards,
        mesh=mesh,
        in_specs=(rows, rows, P("fsdp", None), P(), weights, weights, weights, P(), P(), P()),
        out_specs=(rows, rows, weights, weights, weights, weights, P(), P(), P()),
        check_vma=False,
    )
```

```python
import functools

import jax
import jax.numpy as jnp
from jax import lax
from jax.experimental import pallas as pl
from jax.experimental.pallas import tpu as pltpu
from jax.sharding import PartitionSpec as P

D = 1536
HEADS = 24
KVHEADS = 8
HD = 64
FF = 6912
STEP = 10
HALF = 128
KVD = 512
QKVC = 2560
GROUP = HEADS // KVHEADS

ROPE_BASE = 1000000.0
NORM_EPS = 1e-05
BETA_ONE = 0.9
BETA_TWO = 0.95
ADAM_EPS = 1e-08
WEIGHT_DECAY = 0.1
LEARN_RATE = 0.03
GAIN_RATE = 0.5
SCALE = HD ** (-0.5)
MESH = pl.DeviceIdType.MESH
F32 = jnp.float32
BF16 = jnp.bfloat16
VMEM_LIMIT = 60 * 1024 * 1024


def dot(left, right, left_dim, right_dim):
    return lax.dot_general(
        left, right, (((left_dim,), (right_dim,)), ((), ())), preferred_element_type=F32
    )


def send(source, target, sems, item, peer):
    copy = pltpu.make_async_remote_copy(
        src_ref=source,
        dst_ref=target,
        send_sem=sems[0].at[item],
        recv_sem=sems[1].at[item],
        device_id=peer,
        device_id_type=MESH,
    )
    copy.start()
    return copy


def meet(axes):
    barrier = pltpu.get_barrier_semaphore()
    total = 0
    for axis in axes:
        size = lax.axis_size(axis)
        me = lax.axis_index(axis)
        for step in range(1, size):
            pl.semaphore_signal(
                barrier,
                inc=1,
                device_id={axis: lax.rem(me + step, size)},
                device_id_type=MESH,
            )
        total += size - 1
    pl.semaphore_wait(barrier, total)


def square():
    me = lax.axis_index("ctx")
    return me, me + 1 - 2 * lax.rem(me, 2), lax.rem(me + 2, 4), 3 - me


def swap_start(source, target, sems, base):
    size = lax.axis_size("ctx")
    me = lax.axis_index("ctx")
    copies = []
    for step in range(1, size):
        peer = lax.rem(me + step, size)
        copies.append(
            send(source.at[peer], target.at[me], sems, base + step, {"ctx": peer})
        )
    return copies


def gather_start(source, target, sems, base):
    size = lax.axis_size("ctx")
    me = lax.axis_index("ctx")
    if size != 4:
        return [
            send(
                source,
                target.at[me],
                sems,
                base + step,
                {"ctx": lax.rem(me + step, size)},
            )
            for step in range(1, size)
        ]
    me, side, over, across = square()
    half = source.shape[0] // 2
    top, low = pl.ds(0, half), pl.ds(half, half)
    return [
        send(source.at[top], target.at[me, top], sems, base, {"ctx": side}),
        send(source.at[low], target.at[me, low], sems, base + 1, {"ctx": over}),
        send(source.at[low], target.at[me, low], sems, base + 2, {"ctx": side}),
        send(source.at[top], target.at[me, top], sems, base + 3, {"ctx": over}),
    ]


def gather_rest(copies, target, sems, base):
    if lax.axis_size("ctx") != 4:
        for copy in copies:
            copy.wait()
        return
    me, side, over, across = square()
    half = target.shape[1] // 2
    top, low = pl.ds(0, half), pl.ds(half, half)
    copies[0].wait_recv()
    copies.append(send(target.at[side, top], target.at[side, top], sems, base + 4, {"ctx": over}))
    copies[1].wait_recv()
    copies.append(send(target.at[over, low], target.at[over, low], sems, base + 5, {"ctx": side}))
    for copy in copies:
        copy.wait_send()
    for copy in copies[2:]:
        copy.wait_recv()


GATHER_SEMS = 8


def exchange_kernel(kinds, *refs):
    count = len(kinds)
    ins, outs = refs[:count], refs[count : 2 * count]
    send_sem, recv_sem, local_sem = refs[2 * count :]
    sems = (send_sem, recv_sem)
    me = lax.axis_index("ctx")
    meet(("ctx",))
    copies = []
    own = []
    for item in range(count):
        base = item * GATHER_SEMS
        if kinds[item] == "gather":
            copies.append(gather_start(ins[item], outs[item], sems, base))
            source = ins[item]
        else:
            copies.append(swap_start(ins[item], outs[item], sems, base))
            source = ins[item].at[me]
        copy = pltpu.make_async_copy(source, outs[item].at[me], local_sem.at[item])
        copy.start()
        own.append(copy)
    for item in range(count):
        if kinds[item] == "gather":
            gather_rest(copies[item], outs[item], sems, item * GATHER_SEMS)
        else:
            for copy in copies[item]:
                copy.wait()
    for copy in own:
        copy.wait()


def remote_params(collective_id):
    return pltpu.CompilerParams(
        collective_id=collective_id, has_side_effects=True, vmem_limit_bytes=VMEM_LIMIT
    )


def cost(micros):
    return pl.CostEstimate(flops=0, bytes_accessed=int(micros * 3.0e6), transcendentals=0)


def exchange(kinds, arrays, collective_id, micros):
    size = lax.axis_size("ctx")
    shapes = [
        jax.ShapeDtypeStruct((size,) + a.shape if kind == "gather" else a.shape, a.dtype)
        for kind, a in zip(kinds, arrays)
    ]
    sems = pltpu.SemaphoreType.DMA((len(arrays) * GATHER_SEMS,))
    return pl.pallas_call(
        functools.partial(exchange_kernel, kinds),
        out_shape=shapes,
        in_specs=[pl.BlockSpec(memory_space=pl.ANY)] * len(arrays),
        out_specs=[pl.BlockSpec(memory_space=pl.ANY)] * len(arrays),
        scratch_shapes=[sems, sems, pltpu.SemaphoreType.DMA((len(arrays),))],
        compiler_params=remote_params(collective_id),
        cost_estimate=cost(micros),
    )(*arrays)


def sum_scratch(size, rows):
    if size == 4:
        half = pltpu.VMEM((2, rows // 2, D), BF16)
        return [half, half, pltpu.VMEM((2, rows, D), BF16)]
    return [pltpu.VMEM((size, rows, D), BF16)]


def sum_start(part, bufs, sems):
    size = lax.axis_size("ctx")
    me = lax.axis_index("ctx")
    rows = part.shape[0] // size

    def block(owner, first=0, count=rows):
        return pl.ds(pl.multiple_of(owner * rows + first, rows // 2), count)

    if size != 4:
        copies = []
        for step in range(1, size):
            peer = lax.rem(me + step, size)
            copies.append(
                send(part.at[block(peer)], bufs[0].at[me], sems, step, {"ctx": peer})
            )
        return copies
    me, side, over, across = square()
    half = rows // 2
    relay, _, landed = bufs
    return [
        send(part.at[block(across, 0, half)], relay.at[0], sems, 0, {"ctx": side}),
        send(part.at[block(across, half, half)], relay.at[1], sems, 1, {"ctx": over}),
        send(
            part.at[block(side, 0, half)],
            landed.at[0, pl.ds(0, half)],
            sems,
            2,
            {"ctx": side},
        ),
        send(
            part.at[block(over, half, half)],
            landed.at[1, pl.ds(half, half)],
            sems,
            3,
            {"ctx": over},
        ),
    ]


def sum_rest(copies, part, bufs, sems):
    size = lax.axis_size("ctx")
    me = lax.axis_index("ctx")
    rows = part.shape[0] // size
    half = rows // 2

    def rows_of(owner, first):
        return pl.ds(pl.multiple_of(owner * rows + first, half), half)

    if size != 4:
        for copy in copies:
            copy.wait()

        def read(first):
            total = part[rows_of(me, first), :].astype(F32)
            for step in range(1, size):
                peer = lax.rem(me + step, size)
                total = total + bufs[0][peer, pl.ds(first, half), :].astype(F32)
            return total

        return read
    me, side, over, across = square()
    relay, passed, landed = bufs
    copies[0].wait_recv()
    passed[0] = (part[rows_of(over, 0), :].astype(F32) + relay[0].astype(F32)).astype(BF16)
    copies.append(
        send(passed.at[0], landed.at[1, pl.ds(0, half)], sems, 4, {"ctx": over})
    )
    copies[1].wait_recv()
    passed[1] = (part[rows_of(side, half), :].astype(F32) + relay[1].astype(F32)).astype(
        BF16
    )
    copies.append(
        send(passed.at[1], landed.at[0, pl.ds(half, half)], sems, 5, {"ctx": side})
    )
    for copy in copies:
        copy.wait_send()
    for copy in copies[2:]:
        copy.wait_recv()

    def read(first):
        return (
            part[rows_of(me, first), :].astype(F32)
            + landed[0, pl.ds(first, half), :].astype(F32)
            + landed[1, pl.ds(first, half), :].astype(F32)
        )

    return read


def row_scale(values):
    return lax.rsqrt(jnp.mean(values * values, axis=-1, keepdims=True) + NORM_EPS)


def middle_kernel(part, x, gain, middle, normed_all, *scratch):
    bufs, (normed, send_one, recv_one, send_two, recv_two, local) = scratch[:-6], scratch[-6:]
    me = lax.axis_index("ctx")
    meet(("ctx",))
    copies = sum_start(part, bufs, (send_one, recv_one))
    read = sum_rest(copies, part, bufs, (send_one, recv_one))
    half = x.shape[0] // 2
    for first in (0, half):
        rows = pl.ds(first, half)
        values = x[rows, :].astype(F32) + read(first)
        middle[rows, :] = values
        normed[rows, :] = (values * row_scale(values) * gain[...]).astype(BF16)
    sems = (send_two, recv_two)
    copies = gather_start(normed, normed_all, sems, 0)
    own = pltpu.make_async_copy(normed, normed_all.at[me], local)
    own.start()
    gather_rest(copies, normed_all, sems, 0)
    own.wait()


def middle_back_kernel(part, middle, dy, gain, grad, grad_all, gain_grad, *scratch):
    bufs, (low, send_one, recv_one, send_two, recv_two, local) = scratch[:-6], scratch[-6:]
    me = lax.axis_index("ctx")
    meet(("ctx",))
    copies = sum_start(part, bufs, (send_one, recv_one))
    read = sum_rest(copies, part, bufs, (send_one, recv_one))
    half = dy.shape[0] // 2
    total = jnp.zeros((1, D), F32)
    for first in (0, half):
        rows = pl.ds(first, half)
        values = middle[rows, :]
        root = row_scale(values)
        unit = values * root
        back = read(first)
        total = total + jnp.sum(back * unit, axis=0, keepdims=True)
        back = back * gain[...]
        back = root * (back - unit * jnp.mean(back * unit, axis=-1, keepdims=True))
        back = back + dy[rows, :].astype(F32)
        grad[rows, :] = back
        low[rows, :] = back.astype(BF16)
    gain_grad[...] = total
    sems = (send_two, recv_two)
    copies = gather_start(low, grad_all, sems, 0)
    own = pltpu.make_async_copy(low, grad_all.at[me], local)
    own.start()
    gather_rest(copies, grad_all, sems, 0)
    own.wait()


def last_kernel(part, x, grad, gain, ffn_gain_grad, qk_gain_grad, out, gains, *scratch):
    bufs, (ctx_box, fsdp_box, send_one, recv_one, send_two, recv_two) = (
        scratch[:-6],
        scratch[-6:],
    )
    meet(("ctx", "fsdp"))
    copies = sum_start(part, bufs, (send_one, recv_one))
    read = sum_rest(copies, part, bufs, (send_one, recv_one))
    half = x.shape[0] // 2
    total = jnp.zeros((1, D), F32)
    for first in (0, half):
        rows = pl.ds(first, half)
        values = x[rows, :].astype(F32)
        root = row_scale(values)
        unit = values * root
        back = read(first)
        total = total + jnp.sum(back * unit, axis=0, keepdims=True)
        back = back * gain[...]
        back = root * (back - unit * jnp.mean(back * unit, axis=-1, keepdims=True))
        out[rows, :] = grad[rows, :] + back
    qk_width = qk_gain_grad.shape[1]
    sems = (send_two, recv_two)
    base = 0
    for axis, box in (("ctx", ctx_box), ("fsdp", fsdp_box)):
        size = lax.axis_size(axis)
        me = lax.axis_index(axis)
        if axis == "ctx":
            box[me] = jnp.concatenate(
                [
                    total,
                    ffn_gain_grad[...],
                    jnp.concatenate(
                        [qk_gain_grad[...], jnp.zeros((1, D - qk_width), F32)], axis=1
                    ),
                    jnp.zeros((5, D), F32),
                ],
                axis=0,
            )
        else:
            box[me] = summed
        copies = [
            send(
                box.at[me],
                box.at[me],
                sems,
                base + step,
                {axis: lax.rem(me + step, size)},
            )
            for step in range(1, size)
        ]
        for copy in copies:
            copy.wait()
        base += size
        summed = box[0]
        for item in range(1, size):
            summed = summed + box[item]
    gains[...] = summed


def out_kernel(part, middle, out, *scratch):
    bufs, (send_one, recv_one) = scratch[:-2], scratch[-2:]
    meet(("ctx",))
    copies = sum_start(part, bufs, (send_one, recv_one))
    read = sum_rest(copies, part, bufs, (send_one, recv_one))
    half = middle.shape[0] // 2
    for first in (0, half):
        rows = pl.ds(first, half)
        out[rows, :] = (middle[rows, :] + read(first)).astype(BF16)


def remote_call(kernel, out_shape, args, collective_id, micros, scratch, in_hbm=()):
    return pl.pallas_call(
        kernel,
        out_shape=out_shape,
        in_specs=[pl.BlockSpec(memory_space=pltpu.VMEM)] * len(args),
        out_specs=[
            pl.BlockSpec(memory_space=pl.ANY if item in in_hbm else pltpu.VMEM)
            for item in range(len(out_shape))
        ],
        scratch_shapes=scratch,
        compiler_params=remote_params(collective_id),
        cost_estimate=cost(micros),
    )(*args)


def adam_update(param_now, grad_now, moment_old_one, moment_old_two, step_rate, decay_rate):
    first_new = BETA_ONE * moment_old_one + (1.0 - BETA_ONE) * grad_now
    second_new = BETA_TWO * moment_old_two + (1.0 - BETA_TWO) * grad_now * grad_now
    ratio = (
        first_new
        / (1.0 - BETA_ONE**STEP)
        / (jnp.sqrt(second_new / (1.0 - BETA_TWO**STEP)) + ADAM_EPS)
    )
    return (first_new, second_new, param_now - step_rate * (ratio + decay_rate * param_now))


def adam_kernel(segments, pieces, held, *refs):
    grads = refs[:pieces]
    olds = refs[pieces : pieces + 3]
    news = refs[pieces + 3 + held : pieces + 3 + held + 4]
    grad_buf, old_buf, low_buf, in_sem, out_sem = refs[pieces + 3 + held + 4 :]
    base = min(segment[3] for segment in segments)
    loads = []
    for number, (piece, index, first, column, width) in enumerate(segments):
        here = pl.ds(column - base, width)
        there = pl.ds(column, width)
        copies = [
            pltpu.make_async_copy(
                grads[piece].at[index, :, pl.ds(first, width)],
                grad_buf.at[:, here],
                in_sem.at[3, number],
            )
        ]
        copies += [
            pltpu.make_async_copy(
                olds[item].at[:, there], old_buf.at[item, :, here], in_sem.at[item, number]
            )
            for item in range(3)
        ]
        for copy in copies:
            copy.start()
        loads.append(copies)
    stores = []
    for number, (piece, index, first, column, width) in enumerate(segments):
        for copy in loads[number]:
            copy.wait()
        here = pl.ds(column - base, width)
        there = pl.ds(column, width)
        first_new, second_new, master = adam_update(
            old_buf[0, :, here],
            grad_buf[:, here].astype(F32),
            old_buf[1, :, here],
            old_buf[2, :, here],
            LEARN_RATE,
            WEIGHT_DECAY,
        )
        old_buf[0, :, here] = master
        old_buf[1, :, here] = first_new
        old_buf[2, :, here] = second_new
        low_buf[:, here] = master.astype(BF16)
        for item, source in enumerate(
            (
                old_buf.at[1, :, here],
                old_buf.at[2, :, here],
                old_buf.at[0, :, here],
                low_buf.at[:, here],
            )
        ):
            copy = pltpu.make_async_copy(
                source, news[item].at[:, there], out_sem.at[item, number]
            )
            copy.start()
            stores.append(copy)
    for copy in stores:
        copy.wait()


def adam(segments, grads, olds, held, micros):
    rows, columns = olds[0].shape
    span = max(s[3] + s[4] for s in segments) - min(s[3] for s in segments)
    held = [] if held is None else list(held)
    args = list(grads) + list(olds) + held
    return pl.pallas_call(
        functools.partial(adam_kernel, tuple(segments), len(grads), len(held)),
        out_shape=[jax.ShapeDtypeStruct((rows, columns), F32)] * 3
        + [jax.ShapeDtypeStruct((rows, columns), BF16)],
        in_specs=[pl.BlockSpec(memory_space=pl.ANY)] * len(args),
        out_specs=[pl.BlockSpec(memory_space=pl.ANY)] * 4,
        input_output_aliases={len(grads) + 3 + item: item for item in range(len(held))},
        scratch_shapes=[
            pltpu.VMEM((rows, span), BF16),
            pltpu.VMEM((3, rows, span), F32),
            pltpu.VMEM((rows, span), BF16),
            pltpu.SemaphoreType.DMA((4, len(segments))),
            pltpu.SemaphoreType.DMA((4, len(segments))),
        ],
        compiler_params=pltpu.CompilerParams(vmem_limit_bytes=VMEM_LIMIT),
        cost_estimate=cost(micros),
    )(*args)


def head_mean(values, ones):
    high = values.astype(BF16)
    rest = (values - high.astype(F32)).astype(BF16)
    return (dot(high, ones, 1, 0) + dot(rest, ones, 1, 0)) * (1.0 / HD)


def head_ones(width):
    row = lax.broadcasted_iota(jnp.int32, (width, width), 0) // HD
    col = lax.broadcasted_iota(jnp.int32, (width, width), 1) // HD
    return jnp.where(row == col, 1.0, 0.0).astype(BF16)


def partner(values):
    width = values.shape[-1]
    lane = lax.broadcasted_iota(jnp.int32, values.shape, 1)
    return jnp.where(
        lane % HD < HD // 2,
        pltpu.roll(values, width - HD // 2, 1),
        pltpu.roll(values, HD // 2, 1),
    )


def widen(table, width):
    return jnp.concatenate([table] * (width // table.shape[-1]), axis=-1)


def rope_kernel(qk_width, blocks, place, qkv, cosine, sine, gain, q_out, k_out, v_out):
    ones = head_ones(qk_width)
    q_width = q_out.shape[1]
    for block in range(blocks):
        rows = pl.ds(pl.multiple_of(place[block] * HALF, HALF), HALF)
        to = slice(block * HALF, (block + 1) * HALF)
        values = qkv[rows, :qk_width]
        normed = values * lax.rsqrt(head_mean(values * values, ones) + NORM_EPS) * gain[...]
        turned = normed * widen(cosine[to, :], qk_width) + partner(normed) * widen(
            sine[to, :], qk_width
        )
        turned = turned.astype(BF16)
        q_out[to, :] = turned[:, :q_width]
        k_out[to, :] = turned[:, q_width:]
        v_out[to, :] = qkv[rows, qk_width:].astype(BF16)


def rope_back_kernel(
    qk_width, blocks, place, qkv, cosine, sine, gain, dq, dk, dv, out, gain_out
):
    ones = head_ones(qk_width)
    total = jnp.zeros((1, qk_width), F32)
    for block in range(blocks):
        rows = pl.ds(pl.multiple_of(place[block] * HALF, HALF), HALF)
        to = slice(block * HALF, (block + 1) * HALF)
        values = qkv[rows, :qk_width]
        root = lax.rsqrt(head_mean(values * values, ones) + NORM_EPS)
        unit = values * root
        grad = jnp.concatenate([dq[to, :], dk[to, :]], axis=1)
        grad = grad * widen(cosine[to, :], qk_width) - partner(grad) * widen(
            sine[to, :], qk_width
        )
        total = total + jnp.sum(grad * unit, axis=0, keepdims=True)
        grad = grad * gain[...]
        grad = root * (grad - unit * head_mean(grad * unit, ones))
        out[rows, :qk_width] = grad.astype(BF16)
        out[rows, qk_width:] = dv[to, :].astype(BF16)
    gain_out[...] = total


def doc_first(starts, times):
    first = jnp.zeros_like(times)
    for item in range(starts.shape[0]):
        first = jnp.where(starts[item] <= times, starts[item], first)
    return first


def block_mask(starts, block, keys):
    shape = (keys, GROUP * HALF)
    times = block * HALF + lax.broadcasted_iota(jnp.int32, (1, GROUP * HALF), 1) % HALF
    key = lax.broadcasted_iota(jnp.int32, shape, 0)
    return (key >= doc_first(starts, times)) & (key <= times)


def stack_heads(ref, rows, group):
    return jnp.concatenate(
        [
            ref[rows, (group * GROUP + h) * HD : (group * GROUP + h + 1) * HD]
            for h in range(GROUP)
        ],
        axis=0,
    )


def unstack_heads(turned):
    wide = turned.T
    return [wide[h * HALF : (h + 1) * HALF, :] for h in range(GROUP)]


def attend_kernel(blocks, groups, place, starts, q, k, v, o, lse):
    for block in range(blocks):
        rows = slice(block * HALF, (block + 1) * HALF)
        keys = (block + 1) * HALF
        mask = block_mask(starts, block, keys)
        pieces = []
        for group in range(groups):
            lanes = slice(group * HD, (group + 1) * HD)
            queries = stack_heads(q, rows, group)
            scores = dot(k[:keys, lanes], queries, 1, 1) * SCALE
            weights = jnp.where(mask, jnp.exp(scores), 0.0)
            sums = jnp.sum(weights, axis=0, keepdims=True)
            lse[block, group : group + 1, :] = jnp.log(sums)
            mixed = dot(v[:keys, lanes], weights.astype(BF16), 0, 0) / sums
            pieces += unstack_heads(mixed)
        to = pl.ds(pl.multiple_of(place[block] * HALF, HALF), HALF)
        o[to, :] = jnp.concatenate(pieces, axis=1).astype(BF16)


def attend_back_kernel(blocks, groups, place, starts, q, k, v, lse, do, dq, dk, dv):
    dk[...] = jnp.zeros_like(dk)
    dv[...] = jnp.zeros_like(dv)
    for block in range(blocks):
        rows = slice(block * HALF, (block + 1) * HALF)
        keys = (block + 1) * HALF
        mask = block_mask(starts, block, keys)
        source = pl.ds(pl.multiple_of(place[block] * HALF, HALF), HALF)
        pieces = []
        dk_add = []
        dv_add = []
        for group in range(groups):
            lanes = slice(group * HD, (group + 1) * HD)
            queries = stack_heads(q, rows, group)
            outs = stack_heads(do, source, group)
            key_rows = k[:keys, lanes]
            scores = dot(key_rows, queries, 1, 1) * SCALE
            weights = jnp.where(
                mask, jnp.exp(scores - lse[block, group : group + 1, :]), 0.0
            )
            back = dot(v[:keys, lanes], outs, 1, 1)
            delta = jnp.sum(weights * back, axis=0, keepdims=True)
            grads = (weights * (back - delta)).astype(BF16)
            pieces += unstack_heads(dot(key_rows, grads, 0, 0) * SCALE)
            dk_add.append(dot(grads, queries, 1, 0) * SCALE)
            dv_add.append(dot(weights.astype(BF16), outs, 1, 0))
        dq[rows, :] = jnp.concatenate(pieces, axis=1)
        dk[:keys, :] += jnp.concatenate(dk_add, axis=1)
        dv[:keys, :] += jnp.concatenate(dv_add, axis=1)


def local_call(kernel, out_shape, smem_count, args, micros):
    return pl.pallas_call(
        kernel,
        out_shape=out_shape,
        in_specs=[pl.BlockSpec(memory_space=pltpu.SMEM)] * smem_count
        + [pl.BlockSpec(memory_space=pltpu.VMEM)] * (len(args) - smem_count),
        compiler_params=pltpu.CompilerParams(vmem_limit_bytes=VMEM_LIMIT),
        cost_estimate=cost(micros),
    )(*args)


def rms_scale(values_in, gain_vec):
    return (
        values_in
        * lax.rsqrt(jnp.mean(values_in * values_in, axis=-1, keepdims=True) + NORM_EPS)
        * gain_vec
    )


def inverse_freq():
    return 1.0 / ROPE_BASE ** (jnp.arange(0, HD, 2).astype(F32) / HD)


def shards(
    tokens,
    cotangent,
    doc_starts,
    block_order,
    master_weights,
    moment_one,
    moment_two,
    gains,
    gains_moment_one,
    gains_moment_two,
):
    nctx = lax.axis_size("ctx")
    nfsdp = lax.axis_size("fsdp")
    own_rows = master_weights.shape[0]
    tok_rows = tokens.shape[1]
    stream_len = tok_rows * nctx
    blocks = stream_len // HALF
    groups = KVHEADS // nctx
    q_width = D // nctx
    kv_width = KVD // nctx
    qk_width = q_width + kv_width
    qkv_width = qk_width + kv_width
    tiles = FF // 128
    ff_tiles = -(-tiles // nctx)
    ff_width = ff_tiles * 128
    bundles = 2
    cuts = [ff_width * b // (bundles * 128) * 128 for b in range(bundles + 1)]

    low = master_weights.astype(BF16)

    def ff_part(base, index, start, stop):
        first = index * ff_width + start
        last = index * ff_width + stop
        real_first, real_last = min(first, FF), min(last, FF)
        part = low[:, base + real_first : base + real_last]
        if real_last - real_first < last - first:
            part = jnp.pad(part, ((0, 0), (0, (last - first) - (real_last - real_first))))
        return part

    def attn_part(index):
        return jnp.concatenate(
            [
                low[:, index * q_width : (index + 1) * q_width],
                low[:, D + index * kv_width : D + (index + 1) * kv_width],
                low[:, D + KVD + index * kv_width : D + KVD + (index + 1) * kv_width],
                low[:, QKVC + index * q_width : QKVC + (index + 1) * q_width],
            ],
            axis=1,
        )

    gate_base = QKVC + D
    bases = (gate_base, gate_base + FF, gate_base + 2 * FF)
    attn_send = jnp.stack([attn_part(c) for c in range(nctx)])
    ff_send = [
        jnp.stack(
            [
                jnp.concatenate(
                    [ff_part(base, c, cuts[b], cuts[b + 1]) for base in bases], axis=1
                )
                for c in range(nctx)
            ]
        )
        for b in range(bundles)
    ]

    def gather_rows(piece):
        return lax.all_gather(
            piece.reshape(nctx * own_rows, piece.shape[-1]), "fsdp", axis=0, tiled=True
        )

    def spread(active):
        return (
            active.reshape(active.shape[0], nctx, nfsdp, own_rows)
            .transpose(0, 2, 1, 3)
            .reshape(active.shape[0], D)
        )

    def unspread(active):
        return (
            active.reshape(active.shape[0], nfsdp, nctx, own_rows)
            .transpose(0, 2, 1, 3)
            .reshape(active.shape[0], D)
        )

    g_attn = spread(gains[None, :D])
    g_ffn = spread(gains[None, D : 2 * D])
    x_low = spread(tokens[0])
    dy_low = spread(cotangent[0])
    normed = rms_scale(x_low.astype(F32), g_attn).astype(BF16)

    (attn_held,) = exchange(("swap",), [attn_send], 0, 10)
    w_attn = gather_rows(attn_held)
    attn_held, normed = lax.optimization_barrier((attn_held, normed))
    swapped = exchange(("swap", "gather", "swap"), [ff_send[0], normed, ff_send[1]], 1, 55)
    normed_all = swapped[1].reshape(stream_len, D)
    w_ff = [gather_rows(swapped[0]), gather_rows(swapped[2])]

    order = block_order.reshape(blocks)
    place = jnp.argsort(order).astype(jnp.int32)
    starts = doc_starts[0]
    times = jnp.arange(stream_len, dtype=jnp.int32)
    first = jnp.max(jnp.where(starts[None, :] <= times[:, None], starts[None, :], 0), axis=1)
    angles = (times - first).astype(F32)[:, None] * inverse_freq()[None, :]
    cosine = jnp.concatenate([jnp.cos(angles)] * 2, axis=1)
    sine = jnp.concatenate([-jnp.sin(angles), jnp.sin(angles)], axis=1)

    g_query = gains[2 * D : 2 * D + HD]
    g_key = gains[2 * D + HD :]
    qk_gain = jnp.concatenate(
        [jnp.tile(g_query, q_width // HD), jnp.tile(g_key, kv_width // HD)]
    )[None]

    dy_all = jnp.stack([dy_low] + [lax.ppermute(dy_low, "ctx", [(c, c ^ k) for c in range(nctx)]) for k in range(1, nctx)])
    me = lax.axis_index("ctx")
    dy_all = jnp.take(dy_all, jnp.arange(nctx) ^ me, axis=0).reshape(stream_len, D)
    joined = dot(normed_all, w_attn[:, :qkv_width], 1, 0)
    q, k, v = local_call(
        functools.partial(rope_kernel, qk_width, blocks),
        [
            jax.ShapeDtypeStruct((stream_len, q_width), BF16),
            jax.ShapeDtypeStruct((stream_len, kv_width), BF16),
            jax.ShapeDtypeStruct((stream_len, kv_width), BF16),
        ],
        1,
        (place, joined, cosine, sine, qk_gain),
        5,
    )
    mixed, lse = local_call(
        functools.partial(attend_kernel, blocks, groups),
        [
            jax.ShapeDtypeStruct((stream_len, q_width), BF16),
            jax.ShapeDtypeStruct((blocks, groups, GROUP * HALF), F32),
        ],
        2,
        (place, starts, q, k, v),
        9,
    )
    w_out = w_attn[:, qkv_width:]
    dma = pltpu.SemaphoreType.DMA
    sum_bufs = sum_scratch(nctx, tok_rows)
    sum_sems = [dma((GATHER_SEMS,)), dma((GATHER_SEMS,))]
    norm_scratch = (
        sum_bufs + [pltpu.VMEM((tok_rows, D), BF16)] + sum_sems + sum_sems + [dma]
    )
    own_f32 = jax.ShapeDtypeStruct((tok_rows, D), F32)
    all_low = jax.ShapeDtypeStruct((nctx, tok_rows, D), BF16)
    row_f32 = jax.ShapeDtypeStruct((1, D), F32)

    middle, normed_two_all = remote_call(
        middle_kernel,
        [own_f32, all_low],
        (dot(mixed, w_out, 1, 1).astype(BF16), x_low, g_ffn),
        2,
        57,
        norm_scratch,
        (1,),
    )
    normed_two_all = normed_two_all.reshape(stream_len, D)

    def sum_rows(grad):
        return lax.psum_scatter(grad, "fsdp", scatter_dimension=0, tiled=True).reshape(
            nctx, own_rows, grad.shape[-1]
        )

    def feed(b, x_all, dy):
        width = cuts[b + 1] - cuts[b]
        w_gu, w_down = w_ff[b][:, : 2 * width], w_ff[b][:, 2 * width :]
        gate_up = dot(x_all, w_gu, 1, 0)
        gate, up = gate_up[:, :width], gate_up[:, width:]
        gated = jax.nn.sigmoid(gate)
        act = gate * gated
        hidden = (act * up).astype(BF16)
        back_hidden = dot(dy, w_down, 1, 0)
        grad_gu = jnp.concatenate(
            [back_hidden * up * (gated + act * (1.0 - gated)), back_hidden * act], axis=1
        ).astype(BF16)
        return hidden, grad_gu, dot(hidden, w_down, 1, 1), dot(grad_gu, w_gu, 1, 1)

    def feed_grads(hidden, grad_gu, x_all, dy):
        return dot(dy, hidden, 0, 0).astype(BF16), dot(x_all, grad_gu, 0, 0).astype(BF16)

    hidden, grad_gu, out_partial, back_partial = feed(0, normed_two_all, dy_all)
    grads_first = feed_grads(hidden, grad_gu, normed_two_all, dy_all)
    grads_first, w_ff[1] = lax.optimization_barrier((grads_first, w_ff[1]))
    hidden, grad_gu, out_more, back_more = feed(1, normed_two_all, dy_all)
    out_partial = (out_partial + out_more).astype(BF16)
    back_partial = (back_partial + back_more).astype(BF16)
    ff_sums = [sum_rows(grad) for grad in grads_first]

    grad_middle, grad_middle_all, grad_g_ffn = remote_call(
        middle_back_kernel,
        [own_f32, all_low, row_f32],
        (back_partial, middle, dy_low, g_ffn),
        3,
        57,
        norm_scratch,
        (1,),
    )
    grad_middle_all = grad_middle_all.reshape(stream_len, D)
    grad_middle_all, hidden, grad_gu = lax.optimization_barrier(
        (grad_middle_all, hidden, grad_gu)
    )
    grads_second = feed_grads(hidden, grad_gu, normed_two_all, dy_all)
    grads_second, grad_middle_all = lax.optimization_barrier((grads_second, grad_middle_all))
    ff_sums += [sum_rows(grad) for grad in grads_second]

    grad_mixed = dot(grad_middle_all, w_out, 1, 0).astype(BF16)
    grad_out_rows = dot(grad_middle_all, mixed, 0, 0)
    dq, dk, dv = local_call(
        functools.partial(attend_back_kernel, blocks, groups),
        [
            jax.ShapeDtypeStruct((stream_len, q_width), F32),
            jax.ShapeDtypeStruct((stream_len, kv_width), F32),
            jax.ShapeDtypeStruct((stream_len, kv_width), F32),
        ],
        2,
        (place, starts, q, k, v, lse, grad_mixed),
        17,
    )
    grad_joined, qk_gain_grad = local_call(
        functools.partial(rope_back_kernel, qk_width, blocks),
        [
            jax.ShapeDtypeStruct((stream_len, qkv_width), BF16),
            jax.ShapeDtypeStruct((1, qk_width), F32),
        ],
        1,
        (place, joined, cosine, sine, qk_gain, dq, dk, dv),
        8,
    )
    attn_grad = jnp.concatenate(
        [dot(normed_all, grad_joined, 0, 0), grad_out_rows], axis=1
    ).astype(BF16)
    attn_sum = sum_rows(attn_grad)
    back_attn = dot(grad_joined, w_attn[:, :qkv_width], 1, 1).astype(BF16)
    back_attn, attn_grad = lax.optimization_barrier((back_attn, attn_grad))
    small = dma((nctx + nfsdp,))
    grad_tokens, gain_sums = remote_call(
        last_kernel,
        [own_f32, jax.ShapeDtypeStruct((8, D), F32)],
        (back_attn, x_low, grad_middle, g_attn, grad_g_ffn, qk_gain_grad),
        4,
        40,
        sum_bufs
        + [pltpu.VMEM((nctx, 8, D), F32), pltpu.VMEM((nfsdp, 8, D), F32)]
        + sum_sems
        + [small, small],
    )
    out_partial, gain_sums = lax.optimization_barrier((out_partial, gain_sums))
    (out_tokens,) = remote_call(
        out_kernel,
        [jax.ShapeDtypeStruct((tok_rows, D), BF16)],
        (out_partial, middle),
        5,
        30,
        sum_bufs + sum_sems,
    )
    out_tokens = unspread(out_tokens)[None]
    grad_tokens = unspread(grad_tokens)[None]
    gain_grad = jnp.concatenate(
        [
            unspread(gain_sums[:1])[0],
            unspread(gain_sums[1:2])[0],
            jnp.sum(gain_sums[2, :q_width].reshape(-1, HD), axis=0),
            jnp.sum(gain_sums[2, q_width:qk_width].reshape(-1, HD), axis=0),
        ]
    )

    swaps = ("swap", "swap")
    ff_own = list(exchange(swaps, ff_sums[:2], 6, 16))
    ff_sums[2], ff_own[0] = lax.optimization_barrier((ff_sums[2], ff_own[0]))
    ff_own += exchange(swaps, ff_sums[2:], 7, 16)
    attn_sum, ff_own[2] = lax.optimization_barrier((attn_sum, ff_own[2]))
    (attn_own,) = exchange(("swap",), [attn_sum], 8, 9)
    olds = (master_weights, moment_one, moment_two)
    segments = []
    for part in range(3):
        for c in range(nctx):
            for b in range(bundles):
                width = cuts[b + 1] - cuts[b]
                real = min(max(FF - (c * ff_width + cuts[b]), 0), width)
                if real:
                    piece, first = (2 * b, 0) if part == 2 else (2 * b + 1, part * width)
                    segments.append(
                        (piece, c, first, bases[part] + c * ff_width + cuts[b], real)
                    )
    news = adam(segments, ff_own, olds, None, 12)
    parts = (
        (0, 0, q_width),
        (q_width, D, kv_width),
        (qk_width, D + KVD, kv_width),
        (qkv_width, QKVC, q_width),
    )
    if kv_width % 128:
        attn_own = jnp.concatenate(
            [attn_own[c, :, f : f + w] for f, _, w in parts for c in range(nctx)], axis=1
        )[None]
        segments = [(0, 0, 0, 0, gate_base)]
    else:
        segments = [
            (0, c, first, base + c * width, width)
            for first, base, width in parts
            for c in range(nctx)
        ]
    first_new, second_new, master_new, low_new = adam(segments, [attn_own], olds, news, 3)
    gain_first, gain_second, gain_new = adam_update(
        gains, gain_grad, gains_moment_one, gains_moment_two, GAIN_RATE, 0.0
    )
    return (
        out_tokens,
        grad_tokens,
        first_new,
        second_new,
        master_new,
        low_new,
        gain_first,
        gain_second,
        gain_new,
    )


def solution(mesh):
    rows = P("fsdp", "ctx", None)
    weights = P(("ctx", "fsdp"), None)
    return jax.shard_map(
        shards,
        mesh=mesh,
        in_specs=(rows, rows, P("fsdp", None), P(), weights, weights, weights, P(), P(), P()),
        out_specs=(rows, rows, weights, weights, weights, weights, P(), P(), P()),
        check_vma=False,
    )
```

```python
import functools

import jax
import jax.numpy as jnp
from jax import lax
from jax.experimental import pallas as pl
from jax.experimental.pallas import tpu as pltpu
from jax.sharding import PartitionSpec as P

D = 1536
HEADS = 24
KVHEADS = 8
HD = 64
FF = 6912
STEP = 10
HALF = 128
KVD = 512
QKVC = 2560
GROUP = HEADS // KVHEADS

ROPE_BASE = 1000000.0
NORM_EPS = 1e-05
BETA_ONE = 0.9
BETA_TWO = 0.95
ADAM_EPS = 1e-08
WEIGHT_DECAY = 0.1
LEARN_RATE = 0.03
GAIN_RATE = 0.5
SCALE = HD ** (-0.5)
MESH = pl.DeviceIdType.MESH
F32 = jnp.float32
BF16 = jnp.bfloat16
VMEM_LIMIT = 60 * 1024 * 1024


def dot(left, right, left_dim, right_dim):
    return lax.dot_general(
        left, right, (((left_dim,), (right_dim,)), ((), ())), preferred_element_type=F32
    )


def send(source, target, sems, item, peer):
    copy = pltpu.make_async_remote_copy(
        src_ref=source,
        dst_ref=target,
        send_sem=sems[0].at[item],
        recv_sem=sems[1].at[item],
        device_id=peer,
        device_id_type=MESH,
    )
    copy.start()
    return copy


def meet(axes):
    barrier = pltpu.get_barrier_semaphore()
    total = 0
    for axis in axes:
        size = lax.axis_size(axis)
        me = lax.axis_index(axis)
        for step in range(1, size):
            pl.semaphore_signal(
                barrier,
                inc=1,
                device_id={axis: lax.rem(me + step, size)},
                device_id_type=MESH,
            )
        total += size - 1
    pl.semaphore_wait(barrier, total)


def square():
    me = lax.axis_index("ctx")
    return me, me + 1 - 2 * lax.rem(me, 2), lax.rem(me + 2, 4), 3 - me


def swap_start(source, target, sems, base):
    size = lax.axis_size("ctx")
    me = lax.axis_index("ctx")
    copies = []
    for step in range(1, size):
        peer = lax.rem(me + step, size)
        copies.append(
            send(source.at[peer], target.at[me], sems, base + step, {"ctx": peer})
        )
    return copies


def gather_start(source, target, sems, base):
    size = lax.axis_size("ctx")
    me = lax.axis_index("ctx")
    if size != 4:
        return [
            send(
                source,
                target.at[me],
                sems,
                base + step,
                {"ctx": lax.rem(me + step, size)},
            )
            for step in range(1, size)
        ]
    me, side, over, across = square()
    half = source.shape[0] // 2
    top, low = pl.ds(0, half), pl.ds(half, half)
    return [
        send(source.at[top], target.at[me, top], sems, base, {"ctx": side}),
        send(source.at[low], target.at[me, low], sems, base + 1, {"ctx": over}),
        send(source.at[low], target.at[me, low], sems, base + 2, {"ctx": side}),
        send(source.at[top], target.at[me, top], sems, base + 3, {"ctx": over}),
    ]


def gather_rest(copies, target, sems, base):
    if lax.axis_size("ctx") != 4:
        for copy in copies:
            copy.wait()
        return
    me, side, over, across = square()
    half = target.shape[1] // 2
    top, low = pl.ds(0, half), pl.ds(half, half)
    copies[0].wait_recv()
    copies.append(send(target.at[side, top], target.at[side, top], sems, base + 4, {"ctx": over}))
    copies[1].wait_recv()
    copies.append(send(target.at[over, low], target.at[over, low], sems, base + 5, {"ctx": side}))
    for copy in copies:
        copy.wait_send()
    for copy in copies[2:]:
        copy.wait_recv()


GATHER_SEMS = 8


def exchange_kernel(kinds, *refs):
    count = len(kinds)
    ins, outs = refs[:count], refs[count : 2 * count]
    send_sem, recv_sem, local_sem = refs[2 * count :]
    sems = (send_sem, recv_sem)
    me = lax.axis_index("ctx")
    meet(("ctx",))
    copies = []
    own = []
    for item in range(count):
        base = item * GATHER_SEMS
        if kinds[item] == "gather":
            copies.append(gather_start(ins[item], outs[item], sems, base))
            source = ins[item]
        else:
            copies.append(swap_start(ins[item], outs[item], sems, base))
            source = ins[item].at[me]
        copy = pltpu.make_async_copy(source, outs[item].at[me], local_sem.at[item])
        copy.start()
        own.append(copy)
    for item in range(count):
        if kinds[item] == "gather":
            gather_rest(copies[item], outs[item], sems, item * GATHER_SEMS)
        else:
            for copy in copies[item]:
                copy.wait()
    for copy in own:
        copy.wait()


def remote_params(collective_id):
    return pltpu.CompilerParams(
        collective_id=collective_id, has_side_effects=True, vmem_limit_bytes=VMEM_LIMIT
    )


def cost(micros):
    return pl.CostEstimate(flops=0, bytes_accessed=int(micros * 3.0e6), transcendentals=0)


def exchange(kinds, arrays, collective_id, micros):
    size = lax.axis_size("ctx")
    shapes = [
        jax.ShapeDtypeStruct((size,) + a.shape if kind == "gather" else a.shape, a.dtype)
        for kind, a in zip(kinds, arrays)
    ]
    sems = pltpu.SemaphoreType.DMA((len(arrays) * GATHER_SEMS,))
    return pl.pallas_call(
        functools.partial(exchange_kernel, kinds),
        out_shape=shapes,
        in_specs=[pl.BlockSpec(memory_space=pl.ANY)] * len(arrays),
        out_specs=[pl.BlockSpec(memory_space=pl.ANY)] * len(arrays),
        scratch_shapes=[sems, sems, pltpu.SemaphoreType.DMA((len(arrays),))],
        compiler_params=remote_params(collective_id),
        cost_estimate=cost(micros),
    )(*arrays)


def sum_scratch(size, rows):
    if size == 4:
        half = pltpu.VMEM((2, rows // 2, D), BF16)
        return [half, half, pltpu.VMEM((2, rows, D), BF16)]
    return [pltpu.VMEM((size, rows, D), BF16)]


def sum_start(part, bufs, sems):
    size = lax.axis_size("ctx")
    me = lax.axis_index("ctx")
    rows = part.shape[0] // size

    def block(owner, first=0, count=rows):
        return pl.ds(pl.multiple_of(owner * rows + first, rows // 2), count)

    if size != 4:
        copies = []
        for step in range(1, size):
            peer = lax.rem(me + step, size)
            copies.append(
                send(part.at[block(peer)], bufs[0].at[me], sems, step, {"ctx": peer})
            )
        return copies
    me, side, over, across = square()
    half = rows // 2
    relay, _, landed = bufs
    return [
        send(part.at[block(across, 0, half)], relay.at[0], sems, 0, {"ctx": side}),
        send(part.at[block(across, half, half)], relay.at[1], sems, 1, {"ctx": over}),
        send(
            part.at[block(side, 0, half)],
            landed.at[0, pl.ds(0, half)],
            sems,
            2,
            {"ctx": side},
        ),
        send(
            part.at[block(over, half, half)],
            landed.at[1, pl.ds(half, half)],
            sems,
            3,
            {"ctx": over},
        ),
    ]


def sum_rest(copies, part, bufs, sems):
    size = lax.axis_size("ctx")
    me = lax.axis_index("ctx")
    rows = part.shape[0] // size
    half = rows // 2

    def rows_of(owner, first):
        return pl.ds(pl.multiple_of(owner * rows + first, half), half)

    if size != 4:
        for copy in copies:
            copy.wait()

        def read(first):
            total = part[rows_of(me, first), :].astype(F32)
            for step in range(1, size):
                peer = lax.rem(me + step, size)
                total = total + bufs[0][peer, pl.ds(first, half), :].astype(F32)
            return total

        return read
    me, side, over, across = square()
    relay, passed, landed = bufs
    copies[0].wait_recv()
    passed[0] = (part[rows_of(over, 0), :].astype(F32) + relay[0].astype(F32)).astype(BF16)
    copies.append(
        send(passed.at[0], landed.at[1, pl.ds(0, half)], sems, 4, {"ctx": over})
    )
    copies[1].wait_recv()
    passed[1] = (part[rows_of(side, half), :].astype(F32) + relay[1].astype(F32)).astype(
        BF16
    )
    copies.append(
        send(passed.at[1], landed.at[0, pl.ds(half, half)], sems, 5, {"ctx": side})
    )
    for copy in copies:
        copy.wait_send()
    for copy in copies[2:]:
        copy.wait_recv()

    def read(first):
        return (
            part[rows_of(me, first), :].astype(F32)
            + landed[0, pl.ds(first, half), :].astype(F32)
            + landed[1, pl.ds(first, half), :].astype(F32)
        )

    return read


def row_scale(values):
    return lax.rsqrt(jnp.mean(values * values, axis=-1, keepdims=True) + NORM_EPS)


def middle_kernel(order, ordered, x, gain, middle, normed_all, *scratch):
    bufs, (part, normed, send_one, recv_one, send_two, recv_two, local) = (
        scratch[:-7],
        scratch[-7:],
    )
    me = lax.axis_index("ctx")
    for block in range(order.shape[0]):
        part[block * HALF : (block + 1) * HALF, :] = ordered[order[block]]
    meet(("ctx",))
    copies = sum_start(part, bufs, (send_one, recv_one))
    read = sum_rest(copies, part, bufs, (send_one, recv_one))
    half = x.shape[0] // 2
    for first in (0, half):
        rows = pl.ds(first, half)
        values = x[rows, :].astype(F32) + read(first)
        middle[rows, :] = values
        normed[rows, :] = (values * row_scale(values) * gain[...]).astype(BF16)
    sems = (send_two, recv_two)
    copies = gather_start(normed, normed_all, sems, 0)
    own = pltpu.make_async_copy(normed, normed_all.at[me], local)
    own.start()
    gather_rest(copies, normed_all, sems, 0)
    own.wait()


def middle_back_kernel(part, middle, dy, gain, grad, grad_all, gain_grad, *scratch):
    bufs, (low, send_one, recv_one, send_two, recv_two, local) = scratch[:-6], scratch[-6:]
    me = lax.axis_index("ctx")
    meet(("ctx",))
    copies = sum_start(part, bufs, (send_one, recv_one))
    read = sum_rest(copies, part, bufs, (send_one, recv_one))
    half = dy.shape[0] // 2
    total = jnp.zeros((1, D), F32)
    for first in (0, half):
        rows = pl.ds(first, half)
        values = middle[rows, :]
        root = row_scale(values)
        unit = values * root
        back = read(first)
        total = total + jnp.sum(back * unit, axis=0, keepdims=True)
        back = back * gain[...]
        back = root * (back - unit * jnp.mean(back * unit, axis=-1, keepdims=True))
        back = back + dy[rows, :].astype(F32)
        grad[rows, :] = back
        low[rows, :] = back.astype(BF16)
    gain_grad[...] = total
    sems = (send_two, recv_two)
    copies = gather_start(low, grad_all, sems, 0)
    own = pltpu.make_async_copy(low, grad_all.at[me], local)
    own.start()
    gather_rest(copies, grad_all, sems, 0)
    own.wait()


def line_start(grad, home, sems, base):
    me = lax.axis_index("fsdp")
    chips = lax.axis_size("fsdp") // 2
    core = lax.rem(me, 2)
    rows = grad.shape[0] // (2 * chips)
    copies = []
    for chip in range(chips):
        theirs = pl.ds(pl.multiple_of((2 * chip + 1 - core) * rows, rows), rows)
        copies.append(
            send(grad.at[theirs], home.at[chip], sems, base + chip, {"fsdp": me + 1 - 2 * core})
        )
    return copies


def line_home(copies, grad, home):
    me = lax.axis_index("fsdp")
    chips = lax.axis_size("fsdp") // 2
    core = lax.rem(me, 2)
    rows = grad.shape[0] // (2 * chips)
    for chip in range(chips):
        copies[chip].wait_recv()
        mine = pl.ds(pl.multiple_of((2 * chip + core) * rows, rows), rows)
        home[chip] = (home[chip].astype(F32) + grad[mine, :].astype(F32)).astype(BF16)


def line_copies(reach, going, coming, sems, base):
    me = lax.axis_index("fsdp")
    chips = lax.axis_size("fsdp") // 2
    chip = me // 2
    found = []
    for side, way in ((0, 1), (1, -1)):
        copy = pltpu.make_async_remote_copy(
            src_ref=going.at[side, reach],
            dst_ref=coming.at[side, reach],
            send_sem=sems[0].at[base + 2 * reach + side],
            recv_sem=sems[1].at[base + 2 * reach + side],
            device_id={"fsdp": lax.rem(me + 2 * way + 2 * chips, 2 * chips)},
            device_id_type=MESH,
        )
        if way == 1:
            sent = chip + reach <= chips - 1
            got = (chip >= 1) & (chip + reach <= chips)
            more = (chip >= 1) & sent
        else:
            sent = chip >= reach
            got = (chip <= chips - 2) & (chip + 1 >= reach)
            more = (chip <= chips - 2) & sent
        found.append((side, way, copy, sent, got, more))
    return found


def line_step(reach, home, going, coming, sems, base):
    me = lax.axis_index("fsdp")
    chips = lax.axis_size("fsdp") // 2
    chip = me // 2
    if reach < chips - 1:
        for _, _, copy, _, got, _ in line_copies(reach + 1, going, coming, sems, base):
            pl.when(got)(copy.wait_recv)
    for side, way, copy, sent, _, more in line_copies(reach, going, coming, sems, base):

        @pl.when(sent)
        def _(side=side, way=way, copy=copy, more=more):
            value = home[chip + way * reach]
            if reach < chips - 1:

                @pl.when(more)
                def _():
                    going[side, reach] = (
                        value.astype(F32) + coming[side, reach + 1].astype(F32)
                    ).astype(BF16)

                @pl.when(jnp.logical_not(more))
                def _():
                    going[side, reach] = value

            else:
                going[side, reach] = value
            copy.start()


def line_end(copies, home, going, coming, sems, base):
    me = lax.axis_index("fsdp")
    chips = lax.axis_size("fsdp") // 2
    chip = me // 2
    for side, _, copy, _, got, _ in line_copies(1, going, coming, sems, base):

        @pl.when(got)
        def _(side=side, copy=copy):
            copy.wait_recv()
            home[chip] = (home[chip].astype(F32) + coming[side, 1].astype(F32)).astype(BF16)

    for copy in copies:
        copy.wait_send()
    for reach in range(1, chips):
        for _, _, copy, sent, _, _ in line_copies(reach, going, coming, sems, base):
            pl.when(sent)(copy.wait_send)


def last_kernel(
    swaps, part, x, grad, gain, ffn_gain_grad, qk_gain_grad, attn_grad, *refs
):
    swap_in = refs[:swaps]
    out, gains, attn_own = refs[swaps : swaps + 3]
    swap_out = refs[swaps + 3 : 2 * swaps + 3]
    scratch = refs[2 * swaps + 3 :]
    bufs = scratch[:-13]
    home, going, coming, owned, ctx_box, fsdp_box = scratch[-13:-7]
    send_one, recv_one, send_two, recv_two, send_three, recv_three, local = scratch[-7:]
    ctx_size = lax.axis_size("ctx")
    chips = lax.axis_size("fsdp") // 2
    ctx_me = lax.axis_index("ctx")
    line = (send_three, recv_three)
    step_base = chips
    swap_base = step_base + 2 * chips
    meet(("ctx", "fsdp"))
    home_copies = line_start(attn_grad, home, line, 0)
    copies = sum_start(part, bufs, (send_one, recv_one))
    line_home(home_copies, attn_grad, home)
    for reach in range(chips - 1, 0, -1):
        if reach == 1:
            read = sum_rest(copies, part, bufs, (send_one, recv_one))
            swap_copies = []
            own_copies = []
            for item in range(swaps):
                swap_copies += swap_start(
                    swap_in[item], swap_out[item], line, swap_base + (item + 1) * ctx_size
                )
                copy = pltpu.make_async_copy(
                    swap_in[item].at[ctx_me], swap_out[item].at[ctx_me], local.at[item]
                )
                copy.start()
                own_copies.append(copy)
        line_step(reach, home, going, coming, line, step_base)
    half = x.shape[0] // 2
    total = jnp.zeros((1, D), F32)
    for first in (0, half):
        rows = pl.ds(first, half)
        values = x[rows, :].astype(F32)
        root = row_scale(values)
        unit = values * root
        back = read(first)
        total = total + jnp.sum(back * unit, axis=0, keepdims=True)
        back = back * gain[...]
        back = root * (back - unit * jnp.mean(back * unit, axis=-1, keepdims=True))
        out[rows, :] = grad[rows, :] + back
    qk_width = qk_gain_grad.shape[1]
    sems = (send_two, recv_two)
    base = 0
    for axis, box in (("ctx", ctx_box), ("fsdp", fsdp_box)):
        size = lax.axis_size(axis)
        me = lax.axis_index(axis)
        if axis == "ctx":
            box[me] = jnp.concatenate(
                [
                    total,
                    ffn_gain_grad[...],
                    jnp.concatenate(
                        [qk_gain_grad[...], jnp.zeros((1, D - qk_width), F32)], axis=1
                    ),
                    jnp.zeros((5, D), F32),
                ],
                axis=0,
            )
        else:
            box[me] = summed
        copies = [
            send(
                box.at[me],
                box.at[me],
                sems,
                base + step,
                {axis: lax.rem(me + step, size)},
            )
            for step in range(1, size)
        ]
        for copy in copies:
            copy.wait()
        base += size
        summed = box[0]
        for item in range(1, size):
            summed = summed + box[item]
    gains[...] = summed
    line_end(home_copies, home, going, coming, line, step_base)
    chip = lax.axis_index("fsdp") // 2
    owned_rows = owned.shape[1]
    for index in range(ctx_size):
        owned[index] = home[chip, index * owned_rows : (index + 1) * owned_rows, :]
    swap_copies += swap_start(owned, attn_own, line, swap_base)
    attn_own[ctx_me] = owned[ctx_me]
    for copy in swap_copies:
        copy.wait()
    for copy in own_copies:
        copy.wait()


def out_kernel(part, middle, out, *scratch):
    bufs, (send_one, recv_one) = scratch[:-2], scratch[-2:]
    meet(("ctx",))
    copies = sum_start(part, bufs, (send_one, recv_one))
    read = sum_rest(copies, part, bufs, (send_one, recv_one))
    half = middle.shape[0] // 2
    for first in (0, half):
        rows = pl.ds(first, half)
        out[rows, :] = (middle[rows, :] + read(first)).astype(BF16)


def remote_call(
    kernel, out_shape, args, collective_id, micros, scratch, in_hbm=(), smem=0, args_in_hbm=0
):
    return pl.pallas_call(
        kernel,
        out_shape=out_shape,
        in_specs=[pl.BlockSpec(memory_space=pltpu.SMEM)] * smem
        + [pl.BlockSpec(memory_space=pltpu.VMEM)] * (len(args) - smem - args_in_hbm)
        + [pl.BlockSpec(memory_space=pl.ANY)] * args_in_hbm,
        out_specs=[
            pl.BlockSpec(memory_space=pl.ANY if item in in_hbm else pltpu.VMEM)
            for item in range(len(out_shape))
        ],
        scratch_shapes=scratch,
        compiler_params=remote_params(collective_id),
        cost_estimate=cost(micros),
    )(*args)


def adam_update(param_now, grad_now, moment_old_one, moment_old_two, step_rate, decay_rate):
    first_new = BETA_ONE * moment_old_one + (1.0 - BETA_ONE) * grad_now
    second_new = BETA_TWO * moment_old_two + (1.0 - BETA_TWO) * grad_now * grad_now
    ratio = (
        first_new
        / (1.0 - BETA_ONE**STEP)
        / (jnp.sqrt(second_new / (1.0 - BETA_TWO**STEP)) + ADAM_EPS)
    )
    return (first_new, second_new, param_now - step_rate * (ratio + decay_rate * param_now))


def adam_kernel(segments, pieces, held, *refs):
    grads = refs[:pieces]
    olds = refs[pieces : pieces + 3]
    news = refs[pieces + 3 + held : pieces + 3 + held + 4]
    grad_buf, old_buf, low_buf, in_sem, out_sem = refs[pieces + 3 + held + 4 :]
    base = min(segment[3] for segment in segments)
    loads = []
    for number, (piece, index, first, column, width) in enumerate(segments):
        here = pl.ds(column - base, width)
        there = pl.ds(column, width)
        copies = [
            pltpu.make_async_copy(
                grads[piece].at[index, :, pl.ds(first, width)],
                grad_buf.at[:, here],
                in_sem.at[3, number],
            )
        ]
        copies += [
            pltpu.make_async_copy(
                olds[item].at[:, there], old_buf.at[item, :, here], in_sem.at[item, number]
            )
            for item in range(3)
        ]
        for copy in copies:
            copy.start()
        loads.append(copies)
    stores = []
    for number, (piece, index, first, column, width) in enumerate(segments):
        for copy in loads[number]:
            copy.wait()
        here = pl.ds(column - base, width)
        there = pl.ds(column, width)
        first_new, second_new, master = adam_update(
            old_buf[0, :, here],
            grad_buf[:, here].astype(F32),
            old_buf[1, :, here],
            old_buf[2, :, here],
            LEARN_RATE,
            WEIGHT_DECAY,
        )
        old_buf[0, :, here] = master
        old_buf[1, :, here] = first_new
        old_buf[2, :, here] = second_new
        low_buf[:, here] = master.astype(BF16)
        for item, source in enumerate(
            (
                old_buf.at[1, :, here],
                old_buf.at[2, :, here],
                old_buf.at[0, :, here],
                low_buf.at[:, here],
            )
        ):
            copy = pltpu.make_async_copy(
                source, news[item].at[:, there], out_sem.at[item, number]
            )
            copy.start()
            stores.append(copy)
    for copy in stores:
        copy.wait()


def adam(segments, grads, olds, held, micros):
    rows, columns = olds[0].shape
    span = max(s[3] + s[4] for s in segments) - min(s[3] for s in segments)
    held = [] if held is None else list(held)
    args = list(grads) + list(olds) + held
    return pl.pallas_call(
        functools.partial(adam_kernel, tuple(segments), len(grads), len(held)),
        out_shape=[jax.ShapeDtypeStruct((rows, columns), F32)] * 3
        + [jax.ShapeDtypeStruct((rows, columns), BF16)],
        in_specs=[pl.BlockSpec(memory_space=pl.ANY)] * len(args),
        out_specs=[pl.BlockSpec(memory_space=pl.ANY)] * 4,
        input_output_aliases={len(grads) + 3 + item: item for item in range(len(held))},
        scratch_shapes=[
            pltpu.VMEM((rows, span), BF16),
            pltpu.VMEM((3, rows, span), F32),
            pltpu.VMEM((rows, span), BF16),
            pltpu.SemaphoreType.DMA((4, len(segments))),
            pltpu.SemaphoreType.DMA((4, len(segments))),
        ],
        compiler_params=pltpu.CompilerParams(vmem_limit_bytes=VMEM_LIMIT),
        cost_estimate=cost(micros),
    )(*args)


def head_mean(values, ones):
    high = values.astype(BF16)
    rest = (values - high.astype(F32)).astype(BF16)
    return (dot(high, ones, 1, 0) + dot(rest, ones, 1, 0)) * (1.0 / HD)


def head_ones(width):
    row = lax.broadcasted_iota(jnp.int32, (width, width), 0) // HD
    col = lax.broadcasted_iota(jnp.int32, (width, width), 1) // HD
    return jnp.where(row == col, 1.0, 0.0).astype(BF16)


def partner(values):
    width = values.shape[-1]
    lane = lax.broadcasted_iota(jnp.int32, values.shape, 1)
    return jnp.where(
        lane % HD < HD // 2,
        pltpu.roll(values, width - HD // 2, 1),
        pltpu.roll(values, HD // 2, 1),
    )


def widen(table, width):
    return jnp.concatenate([table] * (width // table.shape[-1]), axis=-1)


def rope_back_kernel(
    qk_width, blocks, place, qk, cosine, sine, gain, dq, dk, dv, out, gain_out
):
    ones = head_ones(qk_width)
    total = jnp.zeros((1, qk_width), F32)
    for block in range(blocks):
        rows = pl.ds(pl.multiple_of(place[block] * HALF, HALF), HALF)
        to = slice(block * HALF, (block + 1) * HALF)
        values = qk[to, :]
        root = lax.rsqrt(head_mean(values * values, ones) + NORM_EPS)
        unit = values * root
        grad = jnp.concatenate([dq[to, :], dk[to, :]], axis=1)
        grad = grad * widen(cosine[to, :], qk_width) - partner(grad) * widen(
            sine[to, :], qk_width
        )
        total = total + jnp.sum(grad * unit, axis=0, keepdims=True)
        grad = grad * gain[...]
        grad = root * (grad - unit * head_mean(grad * unit, ones))
        out[rows, :qk_width] = grad.astype(BF16)
        out[rows, qk_width:] = dv[to, :].astype(BF16)
    gain_out[...] = total


def doc_first(starts, times):
    first = jnp.zeros_like(times)
    for item in range(starts.shape[0]):
        first = jnp.where(starts[item] <= times, starts[item], first)
    return first


def block_mask(starts, block, keys):
    shape = (keys, GROUP * HALF)
    times = block * HALF + lax.broadcasted_iota(jnp.int32, (1, GROUP * HALF), 1) % HALF
    key = lax.broadcasted_iota(jnp.int32, shape, 0)
    return (key >= doc_first(starts, times)) & (key <= times)


def stack_heads(ref, rows, group):
    return jnp.concatenate(
        [
            ref[rows, (group * GROUP + h) * HD : (group * GROUP + h + 1) * HD]
            for h in range(GROUP)
        ],
        axis=0,
    )


def unstack_heads(turned):
    wide = turned.T
    return [wide[h * HALF : (h + 1) * HALF, :] for h in range(GROUP)]


def attend_kernel(
    blocks,
    groups,
    place,
    starts,
    normed,
    weights_in,
    cosine,
    sine,
    gain,
    dy,
    swap_in,
    part,
    qk,
    q,
    k,
    v,
    o,
    lse,
    dy_all,
    swap_out,
    ordered,
    send_sem,
    recv_sem,
    local,
):
    sems = (send_sem, recv_sem)
    me = lax.axis_index("ctx")
    qk_width = qk.shape[1]
    q_width = q.shape[1]
    qkv_width = qk_width + v.shape[1]
    ones = head_ones(qk_width)
    meet(("ctx",))
    swap_copies = swap_start(swap_in, swap_out, sems, GATHER_SEMS)
    copies = gather_start(dy, dy_all, sems, 0)
    own_copies = [
        pltpu.make_async_copy(swap_in.at[me], swap_out.at[me], local.at[0]),
        pltpu.make_async_copy(dy, dy_all.at[me], local.at[1]),
    ]
    for copy in own_copies:
        copy.start()
    for block in range(blocks):
        ordered[block * HALF : (block + 1) * HALF, :] = normed[place[block]]
    qk[...] = dot(ordered[...], weights_in[:, :qk_width], 1, 0)
    v[...] = dot(ordered[...], weights_in[:, qk_width:qkv_width], 1, 0).astype(BF16)
    for block in range(blocks):
        to = slice(block * HALF, (block + 1) * HALF)
        values = qk[to, :]
        turned = values * lax.rsqrt(head_mean(values * values, ones) + NORM_EPS) * gain[...]
        turned = turned * widen(cosine[to, :], qk_width) + partner(turned) * widen(
            sine[to, :], qk_width
        )
        turned = turned.astype(BF16)
        q[to, :] = turned[:, :q_width]
        k[to, :] = turned[:, q_width:]
    for block in range(blocks):
        rows = slice(block * HALF, (block + 1) * HALF)
        keys = (block + 1) * HALF
        mask = block_mask(starts, block, keys)
        pieces = []
        for group in range(groups):
            lanes = slice(group * HD, (group + 1) * HD)
            queries = stack_heads(q, rows, group)
            scores = dot(k[:keys, lanes], queries, 1, 1) * SCALE
            weights = jnp.where(mask, jnp.exp(scores), 0.0)
            sums = jnp.sum(weights, axis=0, keepdims=True)
            lse[block, group : group + 1, :] = jnp.log(sums)
            mixed = dot(v[:keys, lanes], weights.astype(BF16), 0, 0) / sums
            pieces += unstack_heads(mixed)
        o[rows, :] = jnp.concatenate(pieces, axis=1).astype(BF16)
    for first in range(0, D, 512):
        part[:, first : first + 512] = dot(
            o[...], weights_in[first : first + 512, qkv_width:], 1, 1
        ).astype(BF16)
    gather_rest(copies, dy_all, sems, 0)
    for copy in swap_copies:
        copy.wait()
    for copy in own_copies:
        copy.wait()


def attend_back_kernel(blocks, groups, place, starts, q, k, v, lse, do, dq, dk, dv):
    dk[...] = jnp.zeros_like(dk)
    dv[...] = jnp.zeros_like(dv)
    for block in range(blocks):
        rows = slice(block * HALF, (block + 1) * HALF)
        keys = (block + 1) * HALF
        mask = block_mask(starts, block, keys)
        source = pl.ds(pl.multiple_of(place[block] * HALF, HALF), HALF)
        pieces = []
        dk_add = []
        dv_add = []
        for group in range(groups):
            lanes = slice(group * HD, (group + 1) * HD)
            queries = stack_heads(q, rows, group)
            outs = stack_heads(do, source, group)
            key_rows = k[:keys, lanes]
            scores = dot(key_rows, queries, 1, 1) * SCALE
            weights = jnp.where(
                mask, jnp.exp(scores - lse[block, group : group + 1, :]), 0.0
            )
            back = dot(v[:keys, lanes], outs, 1, 1)
            delta = jnp.sum(weights * back, axis=0, keepdims=True)
            grads = (weights * (back - delta)).astype(BF16)
            pieces += unstack_heads(dot(key_rows, grads, 0, 0) * SCALE)
            dk_add.append(dot(grads, queries, 1, 0) * SCALE)
            dv_add.append(dot(weights.astype(BF16), outs, 1, 0))
        dq[rows, :] = jnp.concatenate(pieces, axis=1)
        dk[:keys, :] += jnp.concatenate(dk_add, axis=1)
        dv[:keys, :] += jnp.concatenate(dv_add, axis=1)


def local_call(kernel, out_shape, smem_count, args, micros):
    return pl.pallas_call(
        kernel,
        out_shape=out_shape,
        in_specs=[pl.BlockSpec(memory_space=pltpu.SMEM)] * smem_count
        + [pl.BlockSpec(memory_space=pltpu.VMEM)] * (len(args) - smem_count),
        compiler_params=pltpu.CompilerParams(vmem_limit_bytes=VMEM_LIMIT),
        cost_estimate=cost(micros),
    )(*args)


def rms_scale(values_in, gain_vec):
    return (
        values_in
        * lax.rsqrt(jnp.mean(values_in * values_in, axis=-1, keepdims=True) + NORM_EPS)
        * gain_vec
    )


def inverse_freq():
    return 1.0 / ROPE_BASE ** (jnp.arange(0, HD, 2).astype(F32) / HD)


def shards(
    tokens,
    cotangent,
    doc_starts,
    block_order,
    master_weights,
    moment_one,
    moment_two,
    gains,
    gains_moment_one,
    gains_moment_two,
):
    nctx = lax.axis_size("ctx")
    nfsdp = lax.axis_size("fsdp")
    own_rows = master_weights.shape[0]
    tok_rows = tokens.shape[1]
    stream_len = tok_rows * nctx
    blocks = stream_len // HALF
    groups = KVHEADS // nctx
    q_width = D // nctx
    kv_width = KVD // nctx
    qk_width = q_width + kv_width
    qkv_width = qk_width + kv_width
    tiles = FF // 128
    ff_tiles = -(-tiles // nctx)
    ff_width = ff_tiles * 128
    bundles = 2
    cuts = [ff_width * b // (bundles * 128) * 128 for b in range(bundles + 1)]

    low = master_weights.astype(BF16)

    def ff_part(base, index, start, stop):
        first = index * ff_width + start
        last = index * ff_width + stop
        real_first, real_last = min(first, FF), min(last, FF)
        part = low[:, base + real_first : base + real_last]
        if real_last - real_first < last - first:
            part = jnp.pad(part, ((0, 0), (0, (last - first) - (real_last - real_first))))
        return part

    def attn_part(index):
        return jnp.concatenate(
            [
                low[:, index * q_width : (index + 1) * q_width],
                low[:, D + index * kv_width : D + (index + 1) * kv_width],
                low[:, D + KVD + index * kv_width : D + KVD + (index + 1) * kv_width],
                low[:, QKVC + index * q_width : QKVC + (index + 1) * q_width],
            ],
            axis=1,
        )

    gate_base = QKVC + D
    bases = (gate_base, gate_base + FF, gate_base + 2 * FF)
    attn_send = jnp.stack([attn_part(c) for c in range(nctx)])
    ff_send = [
        jnp.stack(
            [
                jnp.concatenate(
                    [ff_part(base, c, cuts[b], cuts[b + 1]) for base in bases], axis=1
                )
                for c in range(nctx)
            ]
        )
        for b in range(bundles)
    ]

    def gather_rows(piece):
        return lax.all_gather(
            piece.reshape(nctx * own_rows, piece.shape[-1]), "fsdp", axis=0, tiled=True
        )

    def spread(active):
        return (
            active.reshape(active.shape[0], nctx, nfsdp, own_rows)
            .transpose(0, 2, 1, 3)
            .reshape(active.shape[0], D)
        )

    def unspread(active):
        return (
            active.reshape(active.shape[0], nfsdp, nctx, own_rows)
            .transpose(0, 2, 1, 3)
            .reshape(active.shape[0], D)
        )

    g_attn = spread(gains[None, :D])
    g_ffn = spread(gains[None, D : 2 * D])
    x_low = spread(tokens[0])
    dy_low = spread(cotangent[0])
    normed = rms_scale(x_low.astype(F32), g_attn).astype(BF16)

    (attn_held,) = exchange(("swap",), [attn_send], 0, 10)
    w_attn = gather_rows(attn_held)
    first_send, attn_held = lax.optimization_barrier((ff_send[0], attn_held))
    (first_held,) = exchange(("swap",), [first_send], 1, 16)
    normed, first_held = lax.optimization_barrier((normed, first_held))
    (normed_all,) = exchange(("gather",), [normed], 2, 28)
    normed_all = normed_all.reshape(stream_len, D)

    order = block_order.reshape(blocks)
    place = jnp.argsort(order).astype(jnp.int32)
    starts = doc_starts[0]
    times = jnp.arange(stream_len, dtype=jnp.int32)
    first = jnp.max(jnp.where(starts[None, :] <= times[:, None], starts[None, :], 0), axis=1)
    angles = (times - first).astype(F32)[:, None] * inverse_freq()[None, :]
    cosine = jnp.concatenate([jnp.cos(angles)] * 2, axis=1)
    sine = jnp.concatenate([-jnp.sin(angles), jnp.sin(angles)], axis=1)

    g_query = gains[2 * D : 2 * D + HD]
    g_key = gains[2 * D + HD :]
    qk_gain = jnp.concatenate(
        [jnp.tile(g_query, q_width // HD), jnp.tile(g_key, kv_width // HD)]
    )[None]

    dma = pltpu.SemaphoreType.DMA
    all_low = jax.ShapeDtypeStruct((nctx, tok_rows, D), BF16)
    part, qk, q, k, v, mixed, lse, dy_all, second_held = remote_call(
        functools.partial(attend_kernel, blocks, groups),
        [
            jax.ShapeDtypeStruct((stream_len, D), BF16),
            jax.ShapeDtypeStruct((stream_len, qk_width), F32),
            jax.ShapeDtypeStruct((stream_len, q_width), BF16),
            jax.ShapeDtypeStruct((stream_len, kv_width), BF16),
            jax.ShapeDtypeStruct((stream_len, kv_width), BF16),
            jax.ShapeDtypeStruct((stream_len, q_width), BF16),
            jax.ShapeDtypeStruct((blocks, groups, GROUP * HALF), F32),
            all_low,
            jax.ShapeDtypeStruct(ff_send[1].shape, BF16),
        ],
        (place, starts, normed_all.reshape(blocks, HALF, D), w_attn, cosine, sine, qk_gain, dy_low, ff_send[1]),
        3,
        42,
        [
            pltpu.VMEM((stream_len, D), BF16),
            dma((GATHER_SEMS + nctx,)),
            dma((GATHER_SEMS + nctx,)),
            dma((2,)),
        ],
        (7, 8),
        2,
        2,
    )
    dy_all = dy_all.reshape(stream_len, D)
    w_ff = [gather_rows(first_held), gather_rows(second_held)]
    mixed = mixed.reshape(blocks, HALF, q_width)[order].reshape(stream_len, q_width)
    w_out = w_attn[:, qkv_width:]
    sum_bufs = sum_scratch(nctx, tok_rows)
    sum_sems = [dma((GATHER_SEMS,)), dma((GATHER_SEMS,))]
    norm_scratch = (
        sum_bufs + [pltpu.VMEM((tok_rows, D), BF16)] + sum_sems + sum_sems + [dma]
    )
    own_f32 = jax.ShapeDtypeStruct((tok_rows, D), F32)
    row_f32 = jax.ShapeDtypeStruct((1, D), F32)

    middle, normed_two_all = remote_call(
        middle_kernel,
        [own_f32, all_low],
        (order, part.reshape(blocks, HALF, D), x_low, g_ffn),
        4,
        57,
        sum_bufs + [pltpu.VMEM((stream_len, D), BF16)] + norm_scratch[len(sum_bufs) :],
        (1,),
        1,
    )
    normed_two_all = normed_two_all.reshape(stream_len, D)

    def sum_rows(grad):
        return lax.psum_scatter(grad, "fsdp", scatter_dimension=0, tiled=True).reshape(
            nctx, own_rows, grad.shape[-1]
        )

    def feed(b, x_all, dy):
        width = cuts[b + 1] - cuts[b]
        w_gu, w_down = w_ff[b][:, : 2 * width], w_ff[b][:, 2 * width :]
        gate_up = dot(x_all, w_gu, 1, 0)
        gate, up = gate_up[:, :width], gate_up[:, width:]
        gated = jax.nn.sigmoid(gate)
        act = gate * gated
        hidden = (act * up).astype(BF16)
        back_hidden = dot(dy, w_down, 1, 0)
        grad_gu = jnp.concatenate(
            [back_hidden * up * (gated + act * (1.0 - gated)), back_hidden * act], axis=1
        ).astype(BF16)
        return hidden, grad_gu, dot(hidden, w_down, 1, 1), dot(grad_gu, w_gu, 1, 1)

    hidden_one, grad_gu, out_partial, back_partial = feed(0, normed_two_all, dy_all)
    gu_grads = [dot(normed_two_all, grad_gu, 0, 0).astype(BF16)]
    gu_grads[0], w_ff[1] = lax.optimization_barrier((gu_grads[0], w_ff[1]))
    hidden_two, grad_gu, out_more, back_more = feed(1, normed_two_all, dy_all)
    out_partial = (out_partial + out_more).astype(BF16)
    back_partial = (back_partial + back_more).astype(BF16)
    gu_grads.append(dot(normed_two_all, grad_gu, 0, 0).astype(BF16))
    back_partial, gu_grads[1] = lax.optimization_barrier((back_partial, gu_grads[1]))
    ff_sums = [sum_rows(grad) for grad in gu_grads]

    grad_middle, grad_middle_all, grad_g_ffn = remote_call(
        middle_back_kernel,
        [own_f32, all_low, row_f32],
        (back_partial, middle, dy_low, g_ffn),
        5,
        57,
        norm_scratch,
        (1,),
    )
    grad_middle_all = grad_middle_all.reshape(stream_len, D)
    grad_middle_all, hidden_two = lax.optimization_barrier((grad_middle_all, hidden_two))
    hidden = jnp.concatenate([hidden_one, hidden_two], axis=1)
    down_grad = dot(dy_all, hidden, 0, 0).astype(BF16)
    down_grad, grad_middle_all = lax.optimization_barrier((down_grad, grad_middle_all))
    ff_sums.append(sum_rows(down_grad))

    grad_mixed = dot(grad_middle_all, w_out, 1, 0).astype(BF16)
    grad_out_rows = dot(grad_middle_all, mixed, 0, 0)
    dq, dk, dv = local_call(
        functools.partial(attend_back_kernel, blocks, groups),
        [
            jax.ShapeDtypeStruct((stream_len, q_width), F32),
            jax.ShapeDtypeStruct((stream_len, kv_width), F32),
            jax.ShapeDtypeStruct((stream_len, kv_width), F32),
        ],
        2,
        (place, starts, q, k, v, lse, grad_mixed),
        17,
    )
    grad_joined, qk_gain_grad = local_call(
        functools.partial(rope_back_kernel, qk_width, blocks),
        [
            jax.ShapeDtypeStruct((stream_len, qkv_width), BF16),
            jax.ShapeDtypeStruct((1, qk_width), F32),
        ],
        1,
        (place, qk, cosine, sine, qk_gain, dq, dk, dv),
        8,
    )
    attn_grad = jnp.concatenate(
        [dot(normed_all, grad_joined, 0, 0), grad_out_rows], axis=1
    ).astype(BF16)
    back_attn = dot(grad_joined, w_attn[:, :qkv_width], 1, 1).astype(BF16)
    small = dma((nctx + nfsdp,))
    chips = nfsdp // 2
    line_block = (nctx * own_rows, attn_grad.shape[1])
    line_sems = dma((3 * chips + 3 * nctx,))
    own_shape = (nctx, own_rows, attn_grad.shape[1])
    grad_tokens, gain_sums, attn_own, *gu_own = remote_call(
        functools.partial(last_kernel, 2),
        [
            own_f32,
            jax.ShapeDtypeStruct((8, D), F32),
            jax.ShapeDtypeStruct(own_shape, BF16),
            jax.ShapeDtypeStruct(ff_sums[0].shape, BF16),
            jax.ShapeDtypeStruct(ff_sums[1].shape, BF16),
        ],
        (
            back_attn,
            x_low,
            grad_middle,
            g_attn,
            grad_g_ffn,
            qk_gain_grad,
            attn_grad,
            ff_sums[0],
            ff_sums[1],
        ),
        6,
        45,
        sum_bufs
        + [
            pltpu.VMEM((chips,) + line_block, BF16),
            pltpu.VMEM((2, chips) + line_block, BF16),
            pltpu.VMEM((2, chips) + line_block, BF16),
            pltpu.VMEM(own_shape, BF16),
            pltpu.VMEM((nctx, 8, D), F32),
            pltpu.VMEM((nfsdp, 8, D), F32),
        ]
        + sum_sems
        + [small, small, line_sems, line_sems, dma((2,))],
        (3, 4),
        0,
        2,
    )
    out_partial, gain_sums = lax.optimization_barrier((out_partial, gain_sums))
    (out_tokens,) = remote_call(
        out_kernel,
        [jax.ShapeDtypeStruct((tok_rows, D), BF16)],
        (out_partial, middle),
        7,
        30,
        sum_bufs + sum_sems,
    )
    out_tokens = unspread(out_tokens)[None]
    grad_tokens = unspread(grad_tokens)[None]
    gain_grad = jnp.concatenate(
        [
            unspread(gain_sums[:1])[0],
            unspread(gain_sums[1:2])[0],
            jnp.sum(gain_sums[2, :q_width].reshape(-1, HD), axis=0),
            jnp.sum(gain_sums[2, q_width:qk_width].reshape(-1, HD), axis=0),
        ]
    )

    (down_own,) = exchange(("swap",), [ff_sums[2]], 8, 12)
    olds = (master_weights, moment_one, moment_two)
    segments = []
    for part in range(3):
        for c in range(nctx):
            for b in range(bundles):
                width = cuts[b + 1] - cuts[b]
                real = min(max(FF - (c * ff_width + cuts[b]), 0), width)
                if real:
                    piece, first = (2, cuts[b]) if part == 2 else (b, part * width)
                    segments.append(
                        (piece, c, first, bases[part] + c * ff_width + cuts[b], real)
                    )
    news = adam(segments, gu_own + [down_own], olds, None, 12)
    parts = (
        (0, 0, q_width),
        (q_width, D, kv_width),
        (qk_width, D + KVD, kv_width),
        (qkv_width, QKVC, q_width),
    )
    if kv_width % 128:
        attn_own = jnp.concatenate(
            [attn_own[c, :, f : f + w] for f, _, w in parts for c in range(nctx)], axis=1
        )[None]
        segments = [(0, 0, 0, 0, gate_base)]
    else:
        segments = [
            (0, c, first, base + c * width, width)
            for first, base, width in parts
            for c in range(nctx)
        ]
    first_new, second_new, master_new, low_new = adam(segments, [attn_own], olds, news, 3)
    gain_first, gain_second, gain_new = adam_update(
        gains, gain_grad, gains_moment_one, gains_moment_two, GAIN_RATE, 0.0
    )
    return (
        out_tokens,
        grad_tokens,
        first_new,
        second_new,
        master_new,
        low_new,
        gain_first,
        gain_second,
        gain_new,
    )


def solution(mesh):
    rows = P("fsdp", "ctx", None)
    weights = P(("ctx", "fsdp"), None)
    return jax.shard_map(
        shards,
        mesh=mesh,
        in_specs=(rows, rows, P("fsdp", None), P(), weights, weights, weights, P(), P(), P()),
        out_specs=(rows, rows, weights, weights, weights, weights, P(), P(), P()),
        check_vma=False,
    )
```

```python
import functools

import jax
import jax.numpy as jnp
from jax import lax
from jax.experimental import pallas as pl
from jax.experimental.pallas import tpu as pltpu
from jax.sharding import PartitionSpec as P

D = 1536
HEADS = 24
KVHEADS = 8
HD = 64
FF = 6912
STEP = 10
HALF = 128
KVD = 512
QKVC = 2560
GROUP = HEADS // KVHEADS

ROPE_BASE = 1000000.0
NORM_EPS = 1e-05
BETA_ONE = 0.9
BETA_TWO = 0.95
ADAM_EPS = 1e-08
WEIGHT_DECAY = 0.1
LEARN_RATE = 0.03
GAIN_RATE = 0.5
SCALE = HD ** (-0.5)
MESH = pl.DeviceIdType.MESH
F32 = jnp.float32
BF16 = jnp.bfloat16
VMEM_LIMIT = 60 * 1024 * 1024


def dot(left, right, left_dim, right_dim):
    return lax.dot_general(
        left, right, (((left_dim,), (right_dim,)), ((), ())), preferred_element_type=F32
    )


def send(source, target, sems, item, peer):
    copy = pltpu.make_async_remote_copy(
        src_ref=source,
        dst_ref=target,
        send_sem=sems[0].at[item],
        recv_sem=sems[1].at[item],
        device_id=peer,
        device_id_type=MESH,
    )
    copy.start()
    return copy


def meet(axes):
    barrier = pltpu.get_barrier_semaphore()
    total = 0
    for axis in axes:
        size = lax.axis_size(axis)
        me = lax.axis_index(axis)
        for step in range(1, size):
            pl.semaphore_signal(
                barrier,
                inc=1,
                device_id={axis: lax.rem(me + step, size)},
                device_id_type=MESH,
            )
        total += size - 1
    pl.semaphore_wait(barrier, total)


def square():
    me = lax.axis_index("ctx")
    return me, me + 1 - 2 * lax.rem(me, 2), lax.rem(me + 2, 4), 3 - me


def swap_start(source, target, sems, base):
    size = lax.axis_size("ctx")
    me = lax.axis_index("ctx")
    copies = []
    for step in range(1, size):
        peer = lax.rem(me + step, size)
        copies.append(
            send(source.at[peer], target.at[me], sems, base + step, {"ctx": peer})
        )
    return copies


def gather_start(source, target, sems, base):
    size = lax.axis_size("ctx")
    me = lax.axis_index("ctx")
    if size != 4:
        return [
            send(
                source,
                target.at[me],
                sems,
                base + step,
                {"ctx": lax.rem(me + step, size)},
            )
            for step in range(1, size)
        ]
    me, side, over, across = square()
    half = source.shape[0] // 2
    top, low = pl.ds(0, half), pl.ds(half, half)
    return [
        send(source.at[top], target.at[me, top], sems, base, {"ctx": side}),
        send(source.at[low], target.at[me, low], sems, base + 1, {"ctx": over}),
        send(source.at[low], target.at[me, low], sems, base + 2, {"ctx": side}),
        send(source.at[top], target.at[me, top], sems, base + 3, {"ctx": over}),
    ]


def gather_rest(copies, target, sems, base):
    if lax.axis_size("ctx") != 4:
        for copy in copies:
            copy.wait()
        return
    me, side, over, across = square()
    half = target.shape[1] // 2
    top, low = pl.ds(0, half), pl.ds(half, half)
    copies[0].wait_recv()
    copies.append(send(target.at[side, top], target.at[side, top], sems, base + 4, {"ctx": over}))
    copies[1].wait_recv()
    copies.append(send(target.at[over, low], target.at[over, low], sems, base + 5, {"ctx": side}))
    for copy in copies:
        copy.wait_send()
    for copy in copies[2:]:
        copy.wait_recv()


GATHER_SEMS = 8


def exchange_kernel(kinds, *refs):
    count = len(kinds)
    ins, outs = refs[:count], refs[count : 2 * count]
    send_sem, recv_sem, local_sem = refs[2 * count :]
    sems = (send_sem, recv_sem)
    me = lax.axis_index("ctx")
    meet(("ctx",))
    copies = []
    own = []
    for item in range(count):
        base = item * GATHER_SEMS
        if kinds[item] == "gather":
            copies.append(gather_start(ins[item], outs[item], sems, base))
            source = ins[item]
        else:
            copies.append(swap_start(ins[item], outs[item], sems, base))
            source = ins[item].at[me]
        copy = pltpu.make_async_copy(source, outs[item].at[me], local_sem.at[item])
        copy.start()
        own.append(copy)
    for item in range(count):
        if kinds[item] == "gather":
            gather_rest(copies[item], outs[item], sems, item * GATHER_SEMS)
        else:
            for copy in copies[item]:
                copy.wait()
    for copy in own:
        copy.wait()


def remote_params(collective_id):
    return pltpu.CompilerParams(
        collective_id=collective_id, has_side_effects=True, vmem_limit_bytes=VMEM_LIMIT
    )


def cost(micros):
    return pl.CostEstimate(flops=0, bytes_accessed=int(micros * 3.0e6), transcendentals=0)


def exchange(kinds, arrays, collective_id, micros):
    size = lax.axis_size("ctx")
    shapes = [
        jax.ShapeDtypeStruct((size,) + a.shape if kind == "gather" else a.shape, a.dtype)
        for kind, a in zip(kinds, arrays)
    ]
    sems = pltpu.SemaphoreType.DMA((len(arrays) * GATHER_SEMS,))
    return pl.pallas_call(
        functools.partial(exchange_kernel, kinds),
        out_shape=shapes,
        in_specs=[pl.BlockSpec(memory_space=pl.ANY)] * len(arrays),
        out_specs=[pl.BlockSpec(memory_space=pl.ANY)] * len(arrays),
        scratch_shapes=[sems, sems, pltpu.SemaphoreType.DMA((len(arrays),))],
        compiler_params=remote_params(collective_id),
        cost_estimate=cost(micros),
    )(*arrays)


def sum_scratch(size, rows):
    if size == 4:
        half = pltpu.VMEM((2, rows // 2, D), BF16)
        return [half, half, pltpu.VMEM((2, rows, D), BF16)]
    return [pltpu.VMEM((size, rows, D), BF16)]


def sum_start(part, bufs, sems):
    size = lax.axis_size("ctx")
    me = lax.axis_index("ctx")
    rows = part.shape[0] // size

    def block(owner, first=0, count=rows):
        return pl.ds(pl.multiple_of(owner * rows + first, rows // 2), count)

    if size != 4:
        copies = []
        for step in range(1, size):
            peer = lax.rem(me + step, size)
            copies.append(
                send(part.at[block(peer)], bufs[0].at[me], sems, step, {"ctx": peer})
            )
        return copies
    me, side, over, across = square()
    half = rows // 2
    relay, _, landed = bufs
    return [
        send(part.at[block(across, 0, half)], relay.at[0], sems, 0, {"ctx": side}),
        send(part.at[block(across, half, half)], relay.at[1], sems, 1, {"ctx": over}),
        send(
            part.at[block(side, 0, half)],
            landed.at[0, pl.ds(0, half)],
            sems,
            2,
            {"ctx": side},
        ),
        send(
            part.at[block(over, half, half)],
            landed.at[1, pl.ds(half, half)],
            sems,
            3,
            {"ctx": over},
        ),
    ]


def sum_pass(copies, part, bufs, sems):
    if lax.axis_size("ctx") != 4:
        return
    rows = part.shape[0] // 4
    half = rows // 2

    def rows_of(owner, first):
        return pl.ds(pl.multiple_of(owner * rows + first, half), half)

    me, side, over, across = square()
    relay, passed, landed = bufs
    copies[0].wait_recv()
    passed[0] = (part[rows_of(over, 0), :].astype(F32) + relay[0].astype(F32)).astype(BF16)
    copies.append(
        send(passed.at[0], landed.at[1, pl.ds(0, half)], sems, 4, {"ctx": over})
    )
    copies[1].wait_recv()
    passed[1] = (part[rows_of(side, half), :].astype(F32) + relay[1].astype(F32)).astype(
        BF16
    )
    copies.append(
        send(passed.at[1], landed.at[0, pl.ds(half, half)], sems, 5, {"ctx": side})
    )


def sum_rest(copies, part, bufs):
    size = lax.axis_size("ctx")
    me = lax.axis_index("ctx")
    rows = part.shape[0] // size
    half = rows // 2

    def rows_of(owner, first):
        return pl.ds(pl.multiple_of(owner * rows + first, half), half)

    if size != 4:
        for copy in copies:
            copy.wait()

        def read(first):
            total = part[rows_of(me, first), :].astype(F32)
            for step in range(1, size):
                peer = lax.rem(me + step, size)
                total = total + bufs[0][peer, pl.ds(first, half), :].astype(F32)
            return total

        return read
    relay, passed, landed = bufs
    for copy in copies:
        copy.wait_send()
    for copy in copies[2:]:
        copy.wait_recv()

    def read(first):
        return (
            part[rows_of(me, first), :].astype(F32)
            + landed[0, pl.ds(first, half), :].astype(F32)
            + landed[1, pl.ds(first, half), :].astype(F32)
        )

    return read


def row_scale(values):
    return lax.rsqrt(jnp.mean(values * values, axis=-1, keepdims=True) + NORM_EPS)


def middle_kernel(order, ordered, x, gain, middle, normed_all, *scratch):
    bufs, (part, normed, send_one, recv_one, send_two, recv_two, local) = (
        scratch[:-7],
        scratch[-7:],
    )
    me = lax.axis_index("ctx")
    for block in range(order.shape[0]):
        part[block * HALF : (block + 1) * HALF, :] = ordered[order[block]]
    meet(("ctx",))
    copies = sum_start(part, bufs, (send_one, recv_one))
    sum_pass(copies, part, bufs, (send_one, recv_one))
    read = sum_rest(copies, part, bufs)
    half = x.shape[0] // 2
    for first in (0, half):
        rows = pl.ds(first, half)
        values = x[rows, :].astype(F32) + read(first)
        middle[rows, :] = values
        normed[rows, :] = (values * row_scale(values) * gain[...]).astype(BF16)
    sems = (send_two, recv_two)
    copies = gather_start(normed, normed_all, sems, 0)
    own = pltpu.make_async_copy(normed, normed_all.at[me], local)
    own.start()
    gather_rest(copies, normed_all, sems, 0)
    own.wait()


def middle_back_kernel(
    part,
    middle,
    dy,
    gain,
    dy_all,
    hidden_one,
    hidden_two,
    grad,
    grad_all,
    gain_grad,
    down_grad,
    *scratch,
):
    bufs, (low, send_one, recv_one, send_two, recv_two, local) = scratch[:-6], scratch[-6:]
    me = lax.axis_index("ctx")
    meet(("ctx",))
    copies = sum_start(part, bufs, (send_one, recv_one))
    turned = dy_all[...].T
    column = 0
    for hidden in (hidden_one, hidden_two):
        width = hidden.shape[1]
        for first in range(0, width, 256):
            count = min(256, width - first)
            down_grad[:, column + first : column + first + count] = dot(
                turned, hidden[:, first : first + count], 1, 0
            ).astype(BF16)
        column += width
        if column == width:
            sum_pass(copies, part, bufs, (send_one, recv_one))
    read = sum_rest(copies, part, bufs)
    half = dy.shape[0] // 2
    total = jnp.zeros((1, D), F32)
    for first in (0, half):
        rows = pl.ds(first, half)
        values = middle[rows, :]
        root = row_scale(values)
        unit = values * root
        back = read(first)
        total = total + jnp.sum(back * unit, axis=0, keepdims=True)
        back = back * gain[...]
        back = root * (back - unit * jnp.mean(back * unit, axis=-1, keepdims=True))
        back = back + dy[rows, :].astype(F32)
        grad[rows, :] = back
        low[rows, :] = back.astype(BF16)
    gain_grad[...] = total
    sems = (send_two, recv_two)
    copies = gather_start(low, grad_all, sems, 0)
    own = pltpu.make_async_copy(low, grad_all.at[me], local)
    own.start()
    gather_rest(copies, grad_all, sems, 0)
    own.wait()


def line_start(grad, home, sems, base):
    me = lax.axis_index("fsdp")
    chips = lax.axis_size("fsdp") // 2
    core = lax.rem(me, 2)
    rows = grad.shape[0] // (2 * chips)
    copies = []
    for chip in range(chips):
        theirs = pl.ds(pl.multiple_of((2 * chip + 1 - core) * rows, rows), rows)
        copies.append(
            send(grad.at[theirs], home.at[chip], sems, base + chip, {"fsdp": me + 1 - 2 * core})
        )
    return copies


def line_home(copies, grad, home):
    me = lax.axis_index("fsdp")
    chips = lax.axis_size("fsdp") // 2
    core = lax.rem(me, 2)
    rows = grad.shape[0] // (2 * chips)
    for chip in range(chips):
        copies[chip].wait_recv()
        mine = pl.ds(pl.multiple_of((2 * chip + core) * rows, rows), rows)
        home[chip] = (home[chip].astype(F32) + grad[mine, :].astype(F32)).astype(BF16)


def line_copies(reach, going, coming, sems, base):
    me = lax.axis_index("fsdp")
    chips = lax.axis_size("fsdp") // 2
    chip = me // 2
    found = []
    for side, way in ((0, 1), (1, -1)):
        copy = pltpu.make_async_remote_copy(
            src_ref=going.at[side, reach],
            dst_ref=coming.at[side, reach],
            send_sem=sems[0].at[base + 2 * reach + side],
            recv_sem=sems[1].at[base + 2 * reach + side],
            device_id={"fsdp": lax.rem(me + 2 * way + 2 * chips, 2 * chips)},
            device_id_type=MESH,
        )
        if way == 1:
            sent = chip + reach <= chips - 1
            got = (chip >= 1) & (chip + reach <= chips)
            more = (chip >= 1) & sent
        else:
            sent = chip >= reach
            got = (chip <= chips - 2) & (chip + 1 >= reach)
            more = (chip <= chips - 2) & sent
        found.append((side, way, copy, sent, got, more))
    return found


def line_step(reach, home, going, coming, sems, base):
    me = lax.axis_index("fsdp")
    chips = lax.axis_size("fsdp") // 2
    chip = me // 2
    if reach < chips - 1:
        for _, _, copy, _, got, _ in line_copies(reach + 1, going, coming, sems, base):
            pl.when(got)(copy.wait_recv)
    for side, way, copy, sent, _, more in line_copies(reach, going, coming, sems, base):

        @pl.when(sent)
        def _(side=side, way=way, copy=copy, more=more):
            value = home[chip + way * reach]
            if reach < chips - 1:

                @pl.when(more)
                def _():
                    going[side, reach] = (
                        value.astype(F32) + coming[side, reach + 1].astype(F32)
                    ).astype(BF16)

                @pl.when(jnp.logical_not(more))
                def _():
                    going[side, reach] = value

            else:
                going[side, reach] = value
            copy.start()


def line_end(copies, home, going, coming, sems, base):
    me = lax.axis_index("fsdp")
    chips = lax.axis_size("fsdp") // 2
    chip = me // 2
    for side, _, copy, _, got, _ in line_copies(1, going, coming, sems, base):

        @pl.when(got)
        def _(side=side, copy=copy):
            copy.wait_recv()
            home[chip] = (home[chip].astype(F32) + coming[side, 1].astype(F32)).astype(BF16)

    for copy in copies:
        copy.wait_send()
    for reach in range(1, chips):
        for _, _, copy, sent, _, _ in line_copies(reach, going, coming, sems, base):
            pl.when(sent)(copy.wait_send)


def last_kernel(
    swaps, order, ordered, x, grad, gain, ffn_gain_grad, qk_gain_grad, attn_grad, *refs
):
    swap_in = refs[:swaps]
    out, gains, attn_own = refs[swaps : swaps + 3]
    swap_out = refs[swaps + 3 : 2 * swaps + 3]
    scratch = refs[2 * swaps + 3 :]
    bufs, part = scratch[:-14], scratch[-14]
    home, going, coming, owned, ctx_box, fsdp_box = scratch[-13:-7]
    send_one, recv_one, send_two, recv_two, send_three, recv_three, local = scratch[-7:]
    ctx_size = lax.axis_size("ctx")
    chips = lax.axis_size("fsdp") // 2
    ctx_me = lax.axis_index("ctx")
    line = (send_three, recv_three)
    step_base = chips
    swap_base = step_base + 2 * chips
    meet(("ctx", "fsdp"))
    home_copies = line_start(attn_grad, home, line, 0)
    for block in range(order.shape[0]):
        part[block * HALF : (block + 1) * HALF, :] = ordered[order[block]]
    copies = sum_start(part, bufs, (send_one, recv_one))
    line_home(home_copies, attn_grad, home)
    swap_copies = []
    own_copies = []
    for reach in range(chips - 1, 0, -1):
        line_step(reach, home, going, coming, line, step_base)
        if reach == chips - 1:
            sum_pass(copies, part, bufs, (send_one, recv_one))
            for item in range(swaps):
                swap_copies += swap_start(
                    swap_in[item], swap_out[item], line, swap_base + (item + 1) * ctx_size
                )
                copy = pltpu.make_async_copy(
                    swap_in[item].at[ctx_me], swap_out[item].at[ctx_me], local.at[item]
                )
                copy.start()
                own_copies.append(copy)
    read = sum_rest(copies, part, bufs)
    half = x.shape[0] // 2
    total = jnp.zeros((1, D), F32)
    for first in (0, half):
        rows = pl.ds(first, half)
        values = x[rows, :].astype(F32)
        root = row_scale(values)
        unit = values * root
        back = read(first)
        total = total + jnp.sum(back * unit, axis=0, keepdims=True)
        back = back * gain[...]
        back = root * (back - unit * jnp.mean(back * unit, axis=-1, keepdims=True))
        out[rows, :] = grad[rows, :] + back
    qk_width = qk_gain_grad.shape[1]
    sems = (send_two, recv_two)
    base = 0
    for axis, box in (("ctx", ctx_box), ("fsdp", fsdp_box)):
        size = lax.axis_size(axis)
        me = lax.axis_index(axis)
        if axis == "ctx":
            box[me] = jnp.concatenate(
                [
                    total,
                    ffn_gain_grad[...],
                    jnp.concatenate(
                        [qk_gain_grad[...], jnp.zeros((1, D - qk_width), F32)], axis=1
                    ),
                    jnp.zeros((5, D), F32),
                ],
                axis=0,
            )
        else:
            box[me] = summed
        copies = [
            send(
                box.at[me],
                box.at[me],
                sems,
                base + step,
                {axis: lax.rem(me + step, size)},
            )
            for step in range(1, size)
        ]
        for copy in copies:
            copy.wait()
        base += size
        summed = box[0]
        for item in range(1, size):
            summed = summed + box[item]
    gains[...] = summed
    line_end(home_copies, home, going, coming, line, step_base)
    chip = lax.axis_index("fsdp") // 2
    owned_rows = owned.shape[1]
    for index in range(ctx_size):
        owned[index] = home[chip, index * owned_rows : (index + 1) * owned_rows, :]
    swap_copies += swap_start(owned, attn_own, line, swap_base)
    attn_own[ctx_me] = owned[ctx_me]
    for copy in swap_copies:
        copy.wait()
    for copy in own_copies:
        copy.wait()


def remote_call(
    kernel, out_shape, args, collective_id, micros, scratch, in_hbm=(), smem=0, args_in_hbm=0
):
    return pl.pallas_call(
        kernel,
        out_shape=out_shape,
        in_specs=[pl.BlockSpec(memory_space=pltpu.SMEM)] * smem
        + [pl.BlockSpec(memory_space=pltpu.VMEM)] * (len(args) - smem - args_in_hbm)
        + [pl.BlockSpec(memory_space=pl.ANY)] * args_in_hbm,
        out_specs=[
            pl.BlockSpec(memory_space=pl.ANY if item in in_hbm else pltpu.VMEM)
            for item in range(len(out_shape))
        ],
        scratch_shapes=scratch,
        compiler_params=remote_params(collective_id),
        cost_estimate=cost(micros),
    )(*args)


def adam_update(param_now, grad_now, moment_old_one, moment_old_two, step_rate, decay_rate):
    first_new = BETA_ONE * moment_old_one + (1.0 - BETA_ONE) * grad_now
    second_new = BETA_TWO * moment_old_two + (1.0 - BETA_TWO) * grad_now * grad_now
    ratio = (
        first_new
        / (1.0 - BETA_ONE**STEP)
        / (jnp.sqrt(second_new / (1.0 - BETA_TWO**STEP)) + ADAM_EPS)
    )
    return (first_new, second_new, param_now - step_rate * (ratio + decay_rate * param_now))


def adam_kernel(segments, pieces, held, *refs):
    grads = refs[:pieces]
    olds = refs[pieces : pieces + 3]
    news = refs[pieces + 3 + held : pieces + 3 + held + 4]
    grad_buf, old_buf, low_buf, in_sem, out_sem = refs[pieces + 3 + held + 4 :]
    base = min(segment[3] for segment in segments)
    loads = []
    for number, (piece, index, first, column, width) in enumerate(segments):
        here = pl.ds(column - base, width)
        there = pl.ds(column, width)
        copies = [
            pltpu.make_async_copy(
                grads[piece].at[index, :, pl.ds(first, width)],
                grad_buf.at[:, here],
                in_sem.at[3, number],
            )
        ]
        copies += [
            pltpu.make_async_copy(
                olds[item].at[:, there], old_buf.at[item, :, here], in_sem.at[item, number]
            )
            for item in range(3)
        ]
        for copy in copies:
            copy.start()
        loads.append(copies)
    stores = []
    for number, (piece, index, first, column, width) in enumerate(segments):
        for copy in loads[number]:
            copy.wait()
        here = pl.ds(column - base, width)
        there = pl.ds(column, width)
        first_new, second_new, master = adam_update(
            old_buf[0, :, here],
            grad_buf[:, here].astype(F32),
            old_buf[1, :, here],
            old_buf[2, :, here],
            LEARN_RATE,
            WEIGHT_DECAY,
        )
        old_buf[0, :, here] = master
        old_buf[1, :, here] = first_new
        old_buf[2, :, here] = second_new
        low_buf[:, here] = master.astype(BF16)
        for item, source in enumerate(
            (
                old_buf.at[1, :, here],
                old_buf.at[2, :, here],
                old_buf.at[0, :, here],
                low_buf.at[:, here],
            )
        ):
            copy = pltpu.make_async_copy(
                source, news[item].at[:, there], out_sem.at[item, number]
            )
            copy.start()
            stores.append(copy)
    for copy in stores:
        copy.wait()


def adam(segments, grads, olds, held, micros):
    rows, columns = olds[0].shape
    span = max(s[3] + s[4] for s in segments) - min(s[3] for s in segments)
    held = [] if held is None else list(held)
    args = list(grads) + list(olds) + held
    return pl.pallas_call(
        functools.partial(adam_kernel, tuple(segments), len(grads), len(held)),
        out_shape=[jax.ShapeDtypeStruct((rows, columns), F32)] * 3
        + [jax.ShapeDtypeStruct((rows, columns), BF16)],
        in_specs=[pl.BlockSpec(memory_space=pl.ANY)] * len(args),
        out_specs=[pl.BlockSpec(memory_space=pl.ANY)] * 4,
        input_output_aliases={len(grads) + 3 + item: item for item in range(len(held))},
        scratch_shapes=[
            pltpu.VMEM((rows, span), BF16),
            pltpu.VMEM((3, rows, span), F32),
            pltpu.VMEM((rows, span), BF16),
            pltpu.SemaphoreType.DMA((4, len(segments))),
            pltpu.SemaphoreType.DMA((4, len(segments))),
        ],
        compiler_params=pltpu.CompilerParams(vmem_limit_bytes=VMEM_LIMIT),
        cost_estimate=cost(micros),
    )(*args)


def head_mean(values, ones):
    high = values.astype(BF16)
    rest = (values - high.astype(F32)).astype(BF16)
    return (dot(high, ones, 1, 0) + dot(rest, ones, 1, 0)) * (1.0 / HD)


def head_ones(width):
    row = lax.broadcasted_iota(jnp.int32, (width, width), 0) // HD
    col = lax.broadcasted_iota(jnp.int32, (width, width), 1) // HD
    return jnp.where(row == col, 1.0, 0.0).astype(BF16)


def partner(values):
    width = values.shape[-1]
    lane = lax.broadcasted_iota(jnp.int32, values.shape, 1)
    return jnp.where(
        lane % HD < HD // 2,
        pltpu.roll(values, width - HD // 2, 1),
        pltpu.roll(values, HD // 2, 1),
    )


def widen(table, width):
    return jnp.concatenate([table] * (width // table.shape[-1]), axis=-1)


def doc_first(starts, times):
    first = jnp.zeros_like(times)
    for item in range(starts.shape[0]):
        first = jnp.where(starts[item] <= times, starts[item], first)
    return first


def block_mask(starts, block, keys):
    shape = (keys, GROUP * HALF)
    times = block * HALF + lax.broadcasted_iota(jnp.int32, (1, GROUP * HALF), 1) % HALF
    key = lax.broadcasted_iota(jnp.int32, shape, 0)
    return (key >= doc_first(starts, times)) & (key <= times)


def stack_heads(ref, rows, group):
    return jnp.concatenate(
        [
            ref[rows, (group * GROUP + h) * HD : (group * GROUP + h + 1) * HD]
            for h in range(GROUP)
        ],
        axis=0,
    )


def unstack_heads(turned):
    wide = turned.T
    return [wide[h * HALF : (h + 1) * HALF, :] for h in range(GROUP)]


def attend_kernel(
    blocks,
    groups,
    place,
    starts,
    normed,
    weights_in,
    cosine,
    sine,
    gain,
    dy,
    swap_in,
    part,
    qk,
    q,
    k,
    v,
    o,
    lse,
    ordered,
    dy_all,
    swap_out,
    send_sem,
    recv_sem,
    local,
):
    sems = (send_sem, recv_sem)
    me = lax.axis_index("ctx")
    qk_width = qk.shape[1]
    q_width = q.shape[1]
    qkv_width = qk_width + v.shape[1]
    ones = head_ones(qk_width)
    meet(("ctx",))
    swap_copies = swap_start(swap_in, swap_out, sems, GATHER_SEMS)
    copies = gather_start(dy, dy_all, sems, 0)
    own_copies = [
        pltpu.make_async_copy(swap_in.at[me], swap_out.at[me], local.at[0]),
        pltpu.make_async_copy(dy, dy_all.at[me], local.at[1]),
    ]
    for copy in own_copies:
        copy.start()
    for block in range(blocks):
        ordered[block * HALF : (block + 1) * HALF, :] = normed[place[block]]
    qk[...] = dot(ordered[...], weights_in[:, :qk_width], 1, 0)
    v[...] = dot(ordered[...], weights_in[:, qk_width:qkv_width], 1, 0).astype(BF16)
    for block in range(blocks):
        to = slice(block * HALF, (block + 1) * HALF)
        values = qk[to, :]
        turned = values * lax.rsqrt(head_mean(values * values, ones) + NORM_EPS) * gain[...]
        turned = turned * widen(cosine[to, :], qk_width) + partner(turned) * widen(
            sine[to, :], qk_width
        )
        turned = turned.astype(BF16)
        q[to, :] = turned[:, :q_width]
        k[to, :] = turned[:, q_width:]
    for block in range(blocks):
        rows = slice(block * HALF, (block + 1) * HALF)
        keys = (block + 1) * HALF
        mask = block_mask(starts, block, keys)
        pieces = []
        for group in range(groups):
            lanes = slice(group * HD, (group + 1) * HD)
            queries = stack_heads(q, rows, group)
            scores = dot(k[:keys, lanes], queries, 1, 1) * SCALE
            weights = jnp.where(mask, jnp.exp(scores), 0.0)
            sums = jnp.sum(weights, axis=0, keepdims=True)
            lse[block, group : group + 1, :] = jnp.log(sums)
            mixed = dot(v[:keys, lanes], weights.astype(BF16), 0, 0) / sums
            pieces += unstack_heads(mixed)
        o[rows, :] = jnp.concatenate(pieces, axis=1).astype(BF16)
    for first in range(0, D, 512):
        part[:, first : first + 512] = dot(
            o[...], weights_in[first : first + 512, qkv_width:], 1, 1
        ).astype(BF16)
    gather_rest(copies, dy_all, sems, 0)
    for copy in swap_copies:
        copy.wait()
    for copy in own_copies:
        copy.wait()


def attend_back_kernel(
    blocks,
    groups,
    place,
    starts,
    q,
    k,
    v,
    lse,
    grad_all,
    weights_in,
    qk,
    cosine,
    sine,
    gain,
    part,
    middle,
    swap_in,
    joined,
    gain_grad,
    ordered,
    out,
    swap_out,
    *scratch,
):
    bufs = scratch[:-8]
    do, dq, dk, dv, send_one, recv_one, send_two, recv_two = scratch[-8:]
    sems = (send_one, recv_one)
    me = lax.axis_index("ctx")
    qk_width = qk.shape[1]
    q_width = q.shape[1]
    qkv_width = qk_width + v.shape[1]
    ones = head_ones(qk_width)
    meet(("ctx",))
    copies = sum_start(part, bufs, sems)
    swap_copies = swap_start(swap_in, swap_out, (send_two, recv_two), 0)
    own = pltpu.make_async_copy(swap_in.at[me], swap_out.at[me], send_two.at[0])
    own.start()
    for block in range(blocks):
        ordered[block * HALF : (block + 1) * HALF, :] = grad_all[place[block]]
    do[...] = dot(ordered[...], weights_in[:, qkv_width:], 1, 0).astype(BF16)
    dk[...] = jnp.zeros_like(dk)
    dv[...] = jnp.zeros_like(dv)
    for block in range(blocks):
        if block == blocks // 2:
            sum_pass(copies, part, bufs, sems)
        rows = slice(block * HALF, (block + 1) * HALF)
        keys = (block + 1) * HALF
        mask = block_mask(starts, block, keys)
        pieces = []
        dk_add = []
        dv_add = []
        for group in range(groups):
            lanes = slice(group * HD, (group + 1) * HD)
            queries = stack_heads(q, rows, group)
            outs = stack_heads(do, rows, group)
            key_rows = k[:keys, lanes]
            scores = dot(key_rows, queries, 1, 1) * SCALE
            weights = jnp.where(
                mask, jnp.exp(scores - lse[block, group : group + 1, :]), 0.0
            )
            back = dot(v[:keys, lanes], outs, 1, 1)
            delta = jnp.sum(weights * back, axis=0, keepdims=True)
            grads = (weights * (back - delta)).astype(BF16)
            pieces += unstack_heads(dot(key_rows, grads, 0, 0) * SCALE)
            dk_add.append(dot(grads, queries, 1, 0) * SCALE)
            dv_add.append(dot(weights.astype(BF16), outs, 1, 0))
        dq[rows, :] = jnp.concatenate(pieces, axis=1)
        dk[:keys, :] += jnp.concatenate(dk_add, axis=1)
        dv[:keys, :] += jnp.concatenate(dv_add, axis=1)
    total = jnp.zeros((1, qk_width), F32)
    for block in range(blocks):
        to = slice(block * HALF, (block + 1) * HALF)
        values = qk[to, :]
        root = lax.rsqrt(head_mean(values * values, ones) + NORM_EPS)
        unit = values * root
        grad = jnp.concatenate([dq[to, :], dk[to, :]], axis=1)
        grad = grad * widen(cosine[to, :], qk_width) - partner(grad) * widen(
            sine[to, :], qk_width
        )
        total = total + jnp.sum(grad * unit, axis=0, keepdims=True)
        grad = grad * gain[...]
        grad = root * (grad - unit * head_mean(grad * unit, ones))
        joined[to, :qk_width] = grad.astype(BF16)
        joined[to, qk_width:] = dv[to, :].astype(BF16)
    gain_grad[...] = total
    read = sum_rest(copies, part, bufs)
    half = middle.shape[0] // 2
    for first in (0, half):
        rows = pl.ds(first, half)
        out[rows, :] = (middle[rows, :] + read(first)).astype(BF16)
    for copy in swap_copies:
        copy.wait()
    own.wait()


def rms_scale(values_in, gain_vec):
    return (
        values_in
        * lax.rsqrt(jnp.mean(values_in * values_in, axis=-1, keepdims=True) + NORM_EPS)
        * gain_vec
    )


def inverse_freq():
    return 1.0 / ROPE_BASE ** (jnp.arange(0, HD, 2).astype(F32) / HD)


def shards(
    tokens,
    cotangent,
    doc_starts,
    block_order,
    master_weights,
    moment_one,
    moment_two,
    gains,
    gains_moment_one,
    gains_moment_two,
):
    nctx = lax.axis_size("ctx")
    nfsdp = lax.axis_size("fsdp")
    own_rows = master_weights.shape[0]
    tok_rows = tokens.shape[1]
    stream_len = tok_rows * nctx
    blocks = stream_len // HALF
    groups = KVHEADS // nctx
    q_width = D // nctx
    kv_width = KVD // nctx
    qk_width = q_width + kv_width
    qkv_width = qk_width + kv_width
    tiles = FF // 128
    ff_tiles = -(-tiles // nctx)
    ff_width = ff_tiles * 128
    bundles = 2
    cuts = [ff_width * b // (bundles * 128) * 128 for b in range(bundles + 1)]

    low = master_weights.astype(BF16)

    def ff_part(base, index, start, stop):
        first = index * ff_width + start
        last = index * ff_width + stop
        real_first, real_last = min(first, FF), min(last, FF)
        part = low[:, base + real_first : base + real_last]
        if real_last - real_first < last - first:
            part = jnp.pad(part, ((0, 0), (0, (last - first) - (real_last - real_first))))
        return part

    def attn_part(index):
        return jnp.concatenate(
            [
                low[:, index * q_width : (index + 1) * q_width],
                low[:, D + index * kv_width : D + (index + 1) * kv_width],
                low[:, D + KVD + index * kv_width : D + KVD + (index + 1) * kv_width],
                low[:, QKVC + index * q_width : QKVC + (index + 1) * q_width],
            ],
            axis=1,
        )

    gate_base = QKVC + D
    bases = (gate_base, gate_base + FF, gate_base + 2 * FF)
    attn_send = jnp.stack([attn_part(c) for c in range(nctx)])
    ff_send = [
        jnp.stack(
            [
                jnp.concatenate(
                    [ff_part(base, c, cuts[b], cuts[b + 1]) for base in bases], axis=1
                )
                for c in range(nctx)
            ]
        )
        for b in range(bundles)
    ]

    def gather_rows(piece):
        return lax.all_gather(
            piece.reshape(nctx * own_rows, piece.shape[-1]), "fsdp", axis=0, tiled=True
        )

    def spread(active):
        return (
            active.reshape(active.shape[0], nctx, nfsdp, own_rows)
            .transpose(0, 2, 1, 3)
            .reshape(active.shape[0], D)
        )

    def unspread(active):
        return (
            active.reshape(active.shape[0], nfsdp, nctx, own_rows)
            .transpose(0, 2, 1, 3)
            .reshape(active.shape[0], D)
        )

    g_attn = spread(gains[None, :D])
    g_ffn = spread(gains[None, D : 2 * D])
    x_low = spread(tokens[0])
    dy_low = spread(cotangent[0])
    normed = rms_scale(x_low.astype(F32), g_attn).astype(BF16)

    (attn_held,) = exchange(("swap",), [attn_send], 0, 10)
    w_attn = gather_rows(attn_held)
    first_send, attn_held = lax.optimization_barrier((ff_send[0], attn_held))
    (first_held,) = exchange(("swap",), [first_send], 1, 16)
    normed, first_held = lax.optimization_barrier((normed, first_held))
    (normed_all,) = exchange(("gather",), [normed], 2, 28)
    normed_all = normed_all.reshape(stream_len, D)

    order = block_order.reshape(blocks)
    place = jnp.argsort(order).astype(jnp.int32)
    starts = doc_starts[0]
    times = jnp.arange(stream_len, dtype=jnp.int32)
    first = jnp.max(jnp.where(starts[None, :] <= times[:, None], starts[None, :], 0), axis=1)
    angles = (times - first).astype(F32)[:, None] * inverse_freq()[None, :]
    cosine = jnp.concatenate([jnp.cos(angles)] * 2, axis=1)
    sine = jnp.concatenate([-jnp.sin(angles), jnp.sin(angles)], axis=1)

    g_query = gains[2 * D : 2 * D + HD]
    g_key = gains[2 * D + HD :]
    qk_gain = jnp.concatenate(
        [jnp.tile(g_query, q_width // HD), jnp.tile(g_key, kv_width // HD)]
    )[None]

    dma = pltpu.SemaphoreType.DMA
    all_low = jax.ShapeDtypeStruct((nctx, tok_rows, D), BF16)
    part, qk, q, k, v, mixed, lse, normed_pos, dy_all, second_held = remote_call(
        functools.partial(attend_kernel, blocks, groups),
        [
            jax.ShapeDtypeStruct((stream_len, D), BF16),
            jax.ShapeDtypeStruct((stream_len, qk_width), F32),
            jax.ShapeDtypeStruct((stream_len, q_width), BF16),
            jax.ShapeDtypeStruct((stream_len, kv_width), BF16),
            jax.ShapeDtypeStruct((stream_len, kv_width), BF16),
            jax.ShapeDtypeStruct((stream_len, q_width), BF16),
            jax.ShapeDtypeStruct((blocks, groups, GROUP * HALF), F32),
            jax.ShapeDtypeStruct((stream_len, D), BF16),
            all_low,
            jax.ShapeDtypeStruct(ff_send[1].shape, BF16),
        ],
        (place, starts, normed_all.reshape(blocks, HALF, D), w_attn, cosine, sine, qk_gain, dy_low, ff_send[1]),
        3,
        42,
        [
            dma((GATHER_SEMS + nctx,)),
            dma((GATHER_SEMS + nctx,)),
            dma((2,)),
        ],
        (8, 9),
        2,
        2,
    )
    dy_all = dy_all.reshape(stream_len, D)
    w_ff = [gather_rows(first_held), gather_rows(second_held)]
    sum_bufs = sum_scratch(nctx, tok_rows)
    sum_sems = [dma((GATHER_SEMS,)), dma((GATHER_SEMS,))]
    norm_scratch = (
        sum_bufs + [pltpu.VMEM((tok_rows, D), BF16)] + sum_sems + sum_sems + [dma]
    )
    own_f32 = jax.ShapeDtypeStruct((tok_rows, D), F32)
    row_f32 = jax.ShapeDtypeStruct((1, D), F32)

    middle, normed_two_all = remote_call(
        middle_kernel,
        [own_f32, all_low],
        (order, part.reshape(blocks, HALF, D), x_low, g_ffn),
        4,
        57,
        sum_bufs + [pltpu.VMEM((stream_len, D), BF16)] + norm_scratch[len(sum_bufs) :],
        (1,),
        1,
    )
    normed_two_all = normed_two_all.reshape(stream_len, D)

    def sum_rows(grad):
        return lax.psum_scatter(grad, "fsdp", scatter_dimension=0, tiled=True).reshape(
            nctx, own_rows, grad.shape[-1]
        )

    def feed(b, x_all, dy):
        width = cuts[b + 1] - cuts[b]
        w_gu, w_down = w_ff[b][:, : 2 * width], w_ff[b][:, 2 * width :]
        gate_up = dot(x_all, w_gu, 1, 0)
        gate, up = gate_up[:, :width], gate_up[:, width:]
        gated = jax.nn.sigmoid(gate)
        act = gate * gated
        hidden = (act * up).astype(BF16)
        back_hidden = dot(dy, w_down, 1, 0)
        grad_gu = jnp.concatenate(
            [back_hidden * up * (gated + act * (1.0 - gated)), back_hidden * act], axis=1
        ).astype(BF16)
        return hidden, grad_gu, dot(hidden, w_down, 1, 1), dot(grad_gu, w_gu, 1, 1)

    hidden_one, grad_gu, out_partial, back_partial = feed(0, normed_two_all, dy_all)
    gu_grads = [dot(normed_two_all, grad_gu, 0, 0).astype(BF16)]
    gu_grads[0], w_ff[1] = lax.optimization_barrier((gu_grads[0], w_ff[1]))
    hidden_two, grad_gu, out_more, back_more = feed(1, normed_two_all, dy_all)
    out_partial = (out_partial + out_more).astype(BF16)
    back_partial = (back_partial + back_more).astype(BF16)
    gu_grads.append(dot(normed_two_all, grad_gu, 0, 0).astype(BF16))
    back_partial, gu_grads[1] = lax.optimization_barrier((back_partial, gu_grads[1]))
    ff_sums = [sum_rows(grad) for grad in gu_grads]

    grad_middle, grad_middle_all, grad_g_ffn, down_grad = remote_call(
        middle_back_kernel,
        [own_f32, all_low, row_f32, jax.ShapeDtypeStruct((D, ff_width), BF16)],
        (back_partial, middle, dy_low, g_ffn, dy_all, hidden_one, hidden_two),
        5,
        57,
        norm_scratch,
        (1,),
    )
    ff_sums.append(sum_rows(down_grad))

    grad_joined, qk_gain_grad, grad_middle_pos, out_tokens, gu_own_one = remote_call(
        functools.partial(attend_back_kernel, blocks, groups),
        [
            jax.ShapeDtypeStruct((stream_len, qkv_width), BF16),
            jax.ShapeDtypeStruct((1, qk_width), F32),
            jax.ShapeDtypeStruct((stream_len, D), BF16),
            jax.ShapeDtypeStruct((tok_rows, D), BF16),
            jax.ShapeDtypeStruct(ff_sums[0].shape, BF16),
        ],
        (
            place,
            starts,
            q,
            k,
            v,
            lse,
            grad_middle_all.reshape(blocks, HALF, D),
            w_attn,
            qk,
            cosine,
            sine,
            qk_gain,
            out_partial,
            middle,
            ff_sums[0],
        ),
        7,
        42,
        sum_bufs
        + [
            pltpu.VMEM((stream_len, q_width), BF16),
            pltpu.VMEM((stream_len, q_width), F32),
            pltpu.VMEM((stream_len, kv_width), F32),
            pltpu.VMEM((stream_len, kv_width), F32),
        ]
        + sum_sems
        + sum_sems,
        (4,),
        2,
        1,
    )
    attn_grad = jnp.concatenate(
        [dot(normed_pos, grad_joined, 0, 0), dot(grad_middle_pos, mixed, 0, 0)], axis=1
    ).astype(BF16)
    back_attn = dot(grad_joined, w_attn[:, :qkv_width], 1, 1).astype(BF16)
    small = dma((nctx + nfsdp,))
    chips = nfsdp // 2
    line_block = (nctx * own_rows, attn_grad.shape[1])
    line_sems = dma((3 * chips + 3 * nctx,))
    own_shape = (nctx, own_rows, attn_grad.shape[1])
    grad_tokens, gain_sums, attn_own, gu_own_two = remote_call(
        functools.partial(last_kernel, 1),
        [
            own_f32,
            jax.ShapeDtypeStruct((8, D), F32),
            jax.ShapeDtypeStruct(own_shape, BF16),
            jax.ShapeDtypeStruct(ff_sums[1].shape, BF16),
        ],
        (
            order,
            back_attn.reshape(blocks, HALF, D),
            x_low,
            grad_middle,
            g_attn,
            grad_g_ffn,
            qk_gain_grad,
            attn_grad,
            ff_sums[1],
        ),
        6,
        45,
        sum_bufs
        + [
            pltpu.VMEM((stream_len, D), BF16),
            pltpu.VMEM((chips,) + line_block, BF16),
            pltpu.VMEM((2, chips) + line_block, BF16),
            pltpu.VMEM((2, chips) + line_block, BF16),
            pltpu.VMEM(own_shape, BF16),
            pltpu.VMEM((nctx, 8, D), F32),
            pltpu.VMEM((nfsdp, 8, D), F32),
        ]
        + sum_sems
        + [small, small, line_sems, line_sems, dma((2,))],
        (3,),
        1,
        1,
    )
    out_tokens = unspread(out_tokens)[None]
    grad_tokens = unspread(grad_tokens)[None]
    gain_grad = jnp.concatenate(
        [
            unspread(gain_sums[:1])[0],
            unspread(gain_sums[1:2])[0],
            jnp.sum(gain_sums[2, :q_width].reshape(-1, HD), axis=0),
            jnp.sum(gain_sums[2, q_width:qk_width].reshape(-1, HD), axis=0),
        ]
    )

    (down_own,) = exchange(("swap",), [ff_sums[2]], 8, 12)
    olds = (master_weights, moment_one, moment_two)
    segments = []
    for part in range(3):
        for c in range(nctx):
            for b in range(bundles):
                width = cuts[b + 1] - cuts[b]
                real = min(max(FF - (c * ff_width + cuts[b]), 0), width)
                if real:
                    piece, first = (2, cuts[b]) if part == 2 else (b, part * width)
                    segments.append(
                        (piece, c, first, bases[part] + c * ff_width + cuts[b], real)
                    )
    news = adam(segments, [gu_own_one, gu_own_two, down_own], olds, None, 12)
    parts = (
        (0, 0, q_width),
        (q_width, D, kv_width),
        (qk_width, D + KVD, kv_width),
        (qkv_width, QKVC, q_width),
    )
    if kv_width % 128:
        attn_own = jnp.concatenate(
            [attn_own[c, :, f : f + w] for f, _, w in parts for c in range(nctx)], axis=1
        )[None]
        segments = [(0, 0, 0, 0, gate_base)]
    else:
        segments = [
            (0, c, first, base + c * width, width)
            for first, base, width in parts
            for c in range(nctx)
        ]
    first_new, second_new, master_new, low_new = adam(segments, [attn_own], olds, news, 3)
    gain_first, gain_second, gain_new = adam_update(
        gains, gain_grad, gains_moment_one, gains_moment_two, GAIN_RATE, 0.0
    )
    return (
        out_tokens,
        grad_tokens,
        first_new,
        second_new,
        master_new,
        low_new,
        gain_first,
        gain_second,
        gain_new,
    )


def solution(mesh):
    rows = P("fsdp", "ctx", None)
    weights = P(("ctx", "fsdp"), None)
    return jax.shard_map(
        shards,
        mesh=mesh,
        in_specs=(rows, rows, P("fsdp", None), P(), weights, weights, weights, P(), P(), P()),
        out_specs=(rows, rows, weights, weights, weights, weights, P(), P(), P()),
        check_vma=False,
    )
```

```python
import functools

import jax
import jax.numpy as jnp
from jax import lax
from jax.experimental import pallas as pl
from jax.experimental.pallas import tpu as pltpu
from jax.sharding import PartitionSpec as P

D = 1536
HEADS = 24
KVHEADS = 8
HD = 64
FF = 6912
STEP = 10
HALF = 128
KVD = 512
QKVC = 2560
GROUP = HEADS // KVHEADS

ROPE_BASE = 1000000.0
NORM_EPS = 1e-05
BETA_ONE = 0.9
BETA_TWO = 0.95
ADAM_EPS = 1e-08
WEIGHT_DECAY = 0.1
LEARN_RATE = 0.03
GAIN_RATE = 0.5
SCALE = HD ** (-0.5)
MESH = pl.DeviceIdType.MESH
F32 = jnp.float32
BF16 = jnp.bfloat16
VMEM_LIMIT = 60 * 1024 * 1024


def dot(left, right, left_dim, right_dim):
    return lax.dot_general(
        left, right, (((left_dim,), (right_dim,)), ((), ())), preferred_element_type=F32
    )


def send(source, target, sems, item, peer):
    copy = pltpu.make_async_remote_copy(
        src_ref=source,
        dst_ref=target,
        send_sem=sems[0].at[item],
        recv_sem=sems[1].at[item],
        device_id=peer,
        device_id_type=MESH,
    )
    copy.start()
    return copy


def meet(axes):
    barrier = pltpu.get_barrier_semaphore()
    total = 0
    for axis in axes:
        size = lax.axis_size(axis)
        me = lax.axis_index(axis)
        for step in range(1, size):
            pl.semaphore_signal(
                barrier,
                inc=1,
                device_id={axis: lax.rem(me + step, size)},
                device_id_type=MESH,
            )
        total += size - 1
    pl.semaphore_wait(barrier, total)


def square():
    me = lax.axis_index("ctx")
    return me, me + 1 - 2 * lax.rem(me, 2), lax.rem(me + 2, 4), 3 - me


def swap_start(source, target, sems, base):
    size = lax.axis_size("ctx")
    me = lax.axis_index("ctx")
    copies = []
    for step in range(1, size):
        peer = lax.rem(me + step, size)
        copies.append(
            send(source.at[peer], target.at[me], sems, base + step, {"ctx": peer})
        )
    return copies


def gather_start(source, target, sems, base):
    size = lax.axis_size("ctx")
    me = lax.axis_index("ctx")
    if size != 4:
        return [
            send(
                source,
                target.at[me],
                sems,
                base + step,
                {"ctx": lax.rem(me + step, size)},
            )
            for step in range(1, size)
        ]
    me, side, over, across = square()
    half = source.shape[0] // 2
    top, low = pl.ds(0, half), pl.ds(half, half)
    return [
        send(source.at[top], target.at[me, top], sems, base, {"ctx": side}),
        send(source.at[low], target.at[me, low], sems, base + 1, {"ctx": over}),
        send(source.at[low], target.at[me, low], sems, base + 2, {"ctx": side}),
        send(source.at[top], target.at[me, top], sems, base + 3, {"ctx": over}),
    ]


def gather_rest(copies, target, sems, base):
    if lax.axis_size("ctx") != 4:
        for copy in copies:
            copy.wait()
        return
    me, side, over, across = square()
    half = target.shape[1] // 2
    top, low = pl.ds(0, half), pl.ds(half, half)
    copies[0].wait_recv()
    copies.append(send(target.at[side, top], target.at[side, top], sems, base + 4, {"ctx": over}))
    copies[1].wait_recv()
    copies.append(send(target.at[over, low], target.at[over, low], sems, base + 5, {"ctx": side}))
    for copy in copies:
        copy.wait_send()
    for copy in copies[2:]:
        copy.wait_recv()


GATHER_SEMS = 8


def exchange_kernel(kinds, *refs):
    count = len(kinds)
    ins, outs = refs[:count], refs[count : 2 * count]
    send_sem, recv_sem, local_sem = refs[2 * count :]
    sems = (send_sem, recv_sem)
    me = lax.axis_index("ctx")
    meet(("ctx",))
    copies = []
    own = []
    for item in range(count):
        base = item * GATHER_SEMS
        if kinds[item] == "gather":
            copies.append(gather_start(ins[item], outs[item], sems, base))
            source = ins[item]
        else:
            copies.append(swap_start(ins[item], outs[item], sems, base))
            source = ins[item].at[me]
        copy = pltpu.make_async_copy(source, outs[item].at[me], local_sem.at[item])
        copy.start()
        own.append(copy)
    for item in range(count):
        if kinds[item] == "gather":
            gather_rest(copies[item], outs[item], sems, item * GATHER_SEMS)
        else:
            for copy in copies[item]:
                copy.wait()
    for copy in own:
        copy.wait()


def remote_params(collective_id):
    return pltpu.CompilerParams(
        collective_id=collective_id, has_side_effects=True, vmem_limit_bytes=VMEM_LIMIT
    )


def cost(micros):
    return pl.CostEstimate(flops=0, bytes_accessed=int(micros * 3.0e6), transcendentals=0)


def exchange(kinds, arrays, collective_id, micros):
    size = lax.axis_size("ctx")
    shapes = [
        jax.ShapeDtypeStruct((size,) + a.shape if kind == "gather" else a.shape, a.dtype)
        for kind, a in zip(kinds, arrays)
    ]
    sems = pltpu.SemaphoreType.DMA((len(arrays) * GATHER_SEMS,))
    return pl.pallas_call(
        functools.partial(exchange_kernel, kinds),
        out_shape=shapes,
        in_specs=[pl.BlockSpec(memory_space=pl.ANY)] * len(arrays),
        out_specs=[pl.BlockSpec(memory_space=pl.ANY)] * len(arrays),
        scratch_shapes=[sems, sems, pltpu.SemaphoreType.DMA((len(arrays),))],
        compiler_params=remote_params(collective_id),
        cost_estimate=cost(micros),
    )(*arrays)


def sum_scratch(size, rows):
    if size == 4:
        half = pltpu.VMEM((2, rows // 2, D), BF16)
        return [half, half, pltpu.VMEM((2, rows, D), BF16)]
    return [pltpu.VMEM((size, rows, D), BF16)]


def sum_start(part, bufs, sems):
    size = lax.axis_size("ctx")
    me = lax.axis_index("ctx")
    rows = part.shape[0] // size

    def block(owner, first=0, count=rows):
        return pl.ds(pl.multiple_of(owner * rows + first, rows // 2), count)

    if size != 4:
        copies = []
        for step in range(1, size):
            peer = lax.rem(me + step, size)
            copies.append(
                send(part.at[block(peer)], bufs[0].at[me], sems, step, {"ctx": peer})
            )
        return copies
    me, side, over, across = square()
    half = rows // 2
    relay, _, landed = bufs
    return [
        send(part.at[block(across, 0, half)], relay.at[0], sems, 0, {"ctx": side}),
        send(part.at[block(across, half, half)], relay.at[1], sems, 1, {"ctx": over}),
        send(
            part.at[block(side, 0, half)],
            landed.at[0, pl.ds(0, half)],
            sems,
            2,
            {"ctx": side},
        ),
        send(
            part.at[block(over, half, half)],
            landed.at[1, pl.ds(half, half)],
            sems,
            3,
            {"ctx": over},
        ),
    ]


def sum_pass(copies, part, bufs, sems):
    if lax.axis_size("ctx") != 4:
        return
    rows = part.shape[0] // 4
    half = rows // 2

    def rows_of(owner, first):
        return pl.ds(pl.multiple_of(owner * rows + first, half), half)

    me, side, over, across = square()
    relay, passed, landed = bufs
    copies[0].wait_recv()
    passed[0] = (part[rows_of(over, 0), :].astype(F32) + relay[0].astype(F32)).astype(BF16)
    copies.append(
        send(passed.at[0], landed.at[1, pl.ds(0, half)], sems, 4, {"ctx": over})
    )
    copies[1].wait_recv()
    passed[1] = (part[rows_of(side, half), :].astype(F32) + relay[1].astype(F32)).astype(
        BF16
    )
    copies.append(
        send(passed.at[1], landed.at[0, pl.ds(half, half)], sems, 5, {"ctx": side})
    )


def sum_rest(copies, part, bufs):
    size = lax.axis_size("ctx")
    me = lax.axis_index("ctx")
    rows = part.shape[0] // size
    half = rows // 2

    def rows_of(owner, first):
        return pl.ds(pl.multiple_of(owner * rows + first, half), half)

    if size != 4:
        for copy in copies:
            copy.wait()

        def read(first):
            total = part[rows_of(me, first), :].astype(F32)
            for step in range(1, size):
                peer = lax.rem(me + step, size)
                total = total + bufs[0][peer, pl.ds(first, half), :].astype(F32)
            return total

        return read
    relay, passed, landed = bufs
    for copy in copies:
        copy.wait_send()
    for copy in copies[2:]:
        copy.wait_recv()

    def read(first):
        return (
            part[rows_of(me, first), :].astype(F32)
            + landed[0, pl.ds(first, half), :].astype(F32)
            + landed[1, pl.ds(first, half), :].astype(F32)
        )

    return read


def row_scale(values):
    return lax.rsqrt(jnp.mean(values * values, axis=-1, keepdims=True) + NORM_EPS)


def middle_kernel(order, ordered, x, gain, middle, normed_all, *scratch):
    bufs, (part, normed, send_one, recv_one, send_two, recv_two, local) = (
        scratch[:-7],
        scratch[-7:],
    )
    me = lax.axis_index("ctx")
    for block in range(order.shape[0]):
        part[block * HALF : (block + 1) * HALF, :] = ordered[order[block]]
    meet(("ctx",))
    copies = sum_start(part, bufs, (send_one, recv_one))
    sum_pass(copies, part, bufs, (send_one, recv_one))
    read = sum_rest(copies, part, bufs)
    half = x.shape[0] // 2
    for first in (0, half):
        rows = pl.ds(first, half)
        values = x[rows, :].astype(F32) + read(first)
        middle[rows, :] = values
        normed[rows, :] = (values * row_scale(values) * gain[...]).astype(BF16)
    sems = (send_two, recv_two)
    copies = gather_start(normed, normed_all, sems, 0)
    own = pltpu.make_async_copy(normed, normed_all.at[me], local)
    own.start()
    gather_rest(copies, normed_all, sems, 0)
    own.wait()


def load(source, target, sem):
    copy = pltpu.make_async_copy(source, target, sem)
    copy.start()
    return copy


def column_tiles(total, body):
    def step(tile, carry):
        body(pl.multiple_of(tile * 256, 256), 256)
        return carry

    lax.fori_loop(0, total // 256, step, 0)
    if total % 256:
        body(total - total % 256, total % 256)


def middle_back_kernel(
    part,
    middle,
    dy,
    gain,
    x_all,
    dy_all,
    grad_gu,
    hidden,
    w_down,
    out_part,
    grad,
    gain_grad,
    grad_all,
    weight_grad,
    out,
    *scratch,
):
    bufs = scratch[:-14]
    low, x_buf, dy_buf, gu_buf, hidden_buf, down_buf, out_buf, turned, weight_buf = scratch[-14:-5]
    send_one, recv_one, send_two, recv_two, local = scratch[-5:]
    me = lax.axis_index("ctx")
    meet(("ctx",))
    copies = sum_start(part, bufs, (send_one, recv_one))
    loads = [
        load(source, target, local.at[item])
        for item, (source, target) in enumerate(
            (
                (x_all, x_buf),
                (grad_gu, gu_buf),
                (dy_all, dy_buf),
                (hidden, hidden_buf),
                (w_down, down_buf),
                (out_part, out_buf),
            )
        )
    ]
    gu_width = grad_gu.shape[1]
    loads[0].wait()
    turned[...] = x_buf[...].T
    loads[1].wait()

    def gu_tile(first, width):
        weight_buf[:, pl.ds(first, width)] = dot(
            turned[...], gu_buf[:, pl.ds(first, width)], 1, 0
        ).astype(BF16)

    column_tiles(gu_width, gu_tile)
    sum_pass(copies, part, bufs, (send_one, recv_one))
    loads[2].wait()
    turned[...] = dy_buf[...].T
    loads[3].wait()

    def down_tile(first, width):
        weight_buf[:, pl.ds(gu_width + first, width)] = dot(
            turned[...], hidden_buf[:, pl.ds(first, width)], 1, 0
        ).astype(BF16)

    column_tiles(hidden.shape[1], down_tile)
    stores = [load(weight_buf, weight_grad, local.at[6])]
    read = sum_rest(copies, part, bufs)
    half = dy.shape[0] // 2
    total = jnp.zeros((1, D), F32)
    for first in (0, half):
        rows = pl.ds(first, half)
        values = middle[rows, :]
        root = row_scale(values)
        unit = values * root
        back = read(first)
        total = total + jnp.sum(back * unit, axis=0, keepdims=True)
        back = back * gain[...]
        back = root * (back - unit * jnp.mean(back * unit, axis=-1, keepdims=True))
        back = back + dy[rows, :].astype(F32)
        grad[rows, :] = back
        low[rows, :] = back.astype(BF16)
    gain_grad[...] = total
    sems = (send_two, recv_two)
    copies = gather_start(low, grad_all, sems, 0)
    stores.append(load(low, grad_all.at[me], local.at[7]))
    loads[4].wait()
    loads[5].wait()

    def out_tile(first, width):
        columns = pl.ds(first, width)
        out_buf[:, columns] = (
            out_buf[:, columns].astype(F32) + dot(hidden_buf[...], down_buf[columns, :], 1, 1)
        ).astype(BF16)

    column_tiles(D, out_tile)
    stores.append(load(out_buf, out, local.at[8]))
    gather_rest(copies, grad_all, sems, 0)
    for copy in stores:
        copy.wait()


def line_start(grad, home, sems, base):
    me = lax.axis_index("fsdp")
    chips = lax.axis_size("fsdp") // 2
    core = lax.rem(me, 2)
    rows = grad.shape[0] // (2 * chips)
    copies = []
    for chip in range(chips):
        theirs = pl.ds(pl.multiple_of((2 * chip + 1 - core) * rows, rows), rows)
        copies.append(
            send(grad.at[theirs], home.at[chip], sems, base + chip, {"fsdp": me + 1 - 2 * core})
        )
    return copies


def line_home(copies, grad, home):
    me = lax.axis_index("fsdp")
    chips = lax.axis_size("fsdp") // 2
    core = lax.rem(me, 2)
    rows = grad.shape[0] // (2 * chips)
    for chip in range(chips):
        copies[chip].wait_recv()
        mine = pl.ds(pl.multiple_of((2 * chip + core) * rows, rows), rows)
        home[chip] = (home[chip].astype(F32) + grad[mine, :].astype(F32)).astype(BF16)


def line_copies(reach, going, coming, sems, base):
    me = lax.axis_index("fsdp")
    chips = lax.axis_size("fsdp") // 2
    chip = me // 2
    found = []
    for side, way in ((0, 1), (1, -1)):
        copy = pltpu.make_async_remote_copy(
            src_ref=going.at[side, reach],
            dst_ref=coming.at[side, reach],
            send_sem=sems[0].at[base + 2 * reach + side],
            recv_sem=sems[1].at[base + 2 * reach + side],
            device_id={"fsdp": lax.rem(me + 2 * way + 2 * chips, 2 * chips)},
            device_id_type=MESH,
        )
        if way == 1:
            sent = chip + reach <= chips - 1
            got = (chip >= 1) & (chip + reach <= chips)
            more = (chip >= 1) & sent
        else:
            sent = chip >= reach
            got = (chip <= chips - 2) & (chip + 1 >= reach)
            more = (chip <= chips - 2) & sent
        found.append((side, way, copy, sent, got, more))
    return found


def line_step(reach, home, going, coming, sems, base):
    me = lax.axis_index("fsdp")
    chips = lax.axis_size("fsdp") // 2
    chip = me // 2
    if reach < chips - 1:
        for _, _, copy, _, got, _ in line_copies(reach + 1, going, coming, sems, base):
            pl.when(got)(copy.wait_recv)
    for side, way, copy, sent, _, more in line_copies(reach, going, coming, sems, base):

        @pl.when(sent)
        def _(side=side, way=way, copy=copy, more=more):
            value = home[chip + way * reach]
            if reach < chips - 1:

                @pl.when(more)
                def _():
                    going[side, reach] = (
                        value.astype(F32) + coming[side, reach + 1].astype(F32)
                    ).astype(BF16)

                @pl.when(jnp.logical_not(more))
                def _():
                    going[side, reach] = value

            else:
                going[side, reach] = value
            copy.start()


def line_end(copies, home, going, coming, sems, base):
    me = lax.axis_index("fsdp")
    chips = lax.axis_size("fsdp") // 2
    chip = me // 2
    for side, _, copy, _, got, _ in line_copies(1, going, coming, sems, base):

        @pl.when(got)
        def _(side=side, copy=copy):
            copy.wait_recv()
            home[chip] = (home[chip].astype(F32) + coming[side, 1].astype(F32)).astype(BF16)

    for copy in copies:
        copy.wait_send()
    for reach in range(1, chips):
        for _, _, copy, sent, _, _ in line_copies(reach, going, coming, sems, base):
            pl.when(sent)(copy.wait_send)


def last_kernel(
    swaps, order, ordered, x, grad, gain, ffn_gain_grad, qk_gain_grad, attn_grad, *refs
):
    swap_in = refs[:swaps]
    out, gains, attn_own = refs[swaps : swaps + 3]
    swap_out = refs[swaps + 3 : 2 * swaps + 3]
    scratch = refs[2 * swaps + 3 :]
    bufs, part = scratch[:-14], scratch[-14]
    home, going, coming, owned, ctx_box, fsdp_box = scratch[-13:-7]
    send_one, recv_one, send_two, recv_two, send_three, recv_three, local = scratch[-7:]
    ctx_size = lax.axis_size("ctx")
    chips = lax.axis_size("fsdp") // 2
    ctx_me = lax.axis_index("ctx")
    line = (send_three, recv_three)
    step_base = chips
    swap_base = step_base + 2 * chips
    meet(("ctx", "fsdp"))
    home_copies = line_start(attn_grad, home, line, 0)
    for block in range(order.shape[0]):
        part[block * HALF : (block + 1) * HALF, :] = ordered[order[block]]
    copies = sum_start(part, bufs, (send_one, recv_one))
    line_home(home_copies, attn_grad, home)
    swap_copies = []
    own_copies = []
    for reach in range(chips - 1, 0, -1):
        line_step(reach, home, going, coming, line, step_base)
        if reach == chips - 1:
            sum_pass(copies, part, bufs, (send_one, recv_one))
            for item in range(swaps):
                swap_copies += swap_start(
                    swap_in[item], swap_out[item], line, swap_base + (item + 1) * ctx_size
                )
                copy = pltpu.make_async_copy(
                    swap_in[item].at[ctx_me], swap_out[item].at[ctx_me], local.at[item]
                )
                copy.start()
                own_copies.append(copy)
    line_end(home_copies, home, going, coming, line, step_base)
    chip = lax.axis_index("fsdp") // 2
    owned_rows = owned.shape[1]
    for index in range(ctx_size):
        owned[index] = home[chip, index * owned_rows : (index + 1) * owned_rows, :]
    swap_copies += swap_start(owned, attn_own, line, swap_base)
    attn_own[ctx_me] = owned[ctx_me]
    read = sum_rest(copies, part, bufs)
    half = x.shape[0] // 2
    total = jnp.zeros((1, D), F32)
    for first in (0, half):
        rows = pl.ds(first, half)
        values = x[rows, :].astype(F32)
        root = row_scale(values)
        unit = values * root
        back = read(first)
        total = total + jnp.sum(back * unit, axis=0, keepdims=True)
        back = back * gain[...]
        back = root * (back - unit * jnp.mean(back * unit, axis=-1, keepdims=True))
        out[rows, :] = grad[rows, :] + back
    qk_width = qk_gain_grad.shape[1]
    sems = (send_two, recv_two)
    base = 0
    for axis, box in (("ctx", ctx_box), ("fsdp", fsdp_box)):
        size = lax.axis_size(axis)
        me = lax.axis_index(axis)
        if axis == "ctx":
            box[me] = jnp.concatenate(
                [
                    total,
                    ffn_gain_grad[...],
                    jnp.concatenate(
                        [qk_gain_grad[...], jnp.zeros((1, D - qk_width), F32)], axis=1
                    ),
                    jnp.zeros((5, D), F32),
                ],
                axis=0,
            )
        else:
            box[me] = summed
        copies = [
            send(
                box.at[me],
                box.at[me],
                sems,
                base + step,
                {axis: lax.rem(me + step, size)},
            )
            for step in range(1, size)
        ]
        for copy in copies:
            copy.wait()
        base += size
        summed = box[0]
        for item in range(1, size):
            summed = summed + box[item]
    gains[...] = summed
    for copy in swap_copies:
        copy.wait()
    for copy in own_copies:
        copy.wait()


def remote_call(
    kernel, out_shape, args, collective_id, micros, scratch, in_hbm=(), smem=0, args_in_hbm=0
):
    return pl.pallas_call(
        kernel,
        out_shape=out_shape,
        in_specs=[pl.BlockSpec(memory_space=pltpu.SMEM)] * smem
        + [pl.BlockSpec(memory_space=pltpu.VMEM)] * (len(args) - smem - args_in_hbm)
        + [pl.BlockSpec(memory_space=pl.ANY)] * args_in_hbm,
        out_specs=[
            pl.BlockSpec(memory_space=pl.ANY if item in in_hbm else pltpu.VMEM)
            for item in range(len(out_shape))
        ],
        scratch_shapes=scratch,
        compiler_params=remote_params(collective_id),
        cost_estimate=cost(micros),
    )(*args)


def adam_update(param_now, grad_now, moment_old_one, moment_old_two, step_rate, decay_rate):
    first_new = BETA_ONE * moment_old_one + (1.0 - BETA_ONE) * grad_now
    second_new = BETA_TWO * moment_old_two + (1.0 - BETA_TWO) * grad_now * grad_now
    ratio = (
        first_new
        / (1.0 - BETA_ONE**STEP)
        / (jnp.sqrt(second_new / (1.0 - BETA_TWO**STEP)) + ADAM_EPS)
    )
    return (first_new, second_new, param_now - step_rate * (ratio + decay_rate * param_now))


def adam_kernel(segments, pieces, held, *refs):
    grads = refs[:pieces]
    olds = refs[pieces : pieces + 3]
    news = refs[pieces + 3 + held : pieces + 3 + held + 4]
    grad_buf, old_buf, low_buf, in_sem, out_sem = refs[pieces + 3 + held + 4 :]
    base = min(segment[3] for segment in segments)
    loads = []
    for number, (piece, index, first, column, width) in enumerate(segments):
        here = pl.ds(column - base, width)
        there = pl.ds(column, width)
        copies = [
            pltpu.make_async_copy(
                grads[piece].at[index, :, pl.ds(first, width)],
                grad_buf.at[:, here],
                in_sem.at[3, number],
            )
        ]
        copies += [
            pltpu.make_async_copy(
                olds[item].at[:, there], old_buf.at[item, :, here], in_sem.at[item, number]
            )
            for item in range(3)
        ]
        for copy in copies:
            copy.start()
        loads.append(copies)
    stores = []
    for number, (piece, index, first, column, width) in enumerate(segments):
        for copy in loads[number]:
            copy.wait()
        here = pl.ds(column - base, width)
        there = pl.ds(column, width)
        first_new, second_new, master = adam_update(
            old_buf[0, :, here],
            grad_buf[:, here].astype(F32),
            old_buf[1, :, here],
            old_buf[2, :, here],
            LEARN_RATE,
            WEIGHT_DECAY,
        )
        old_buf[0, :, here] = master
        old_buf[1, :, here] = first_new
        old_buf[2, :, here] = second_new
        low_buf[:, here] = master.astype(BF16)
        for item, source in enumerate(
            (
                old_buf.at[1, :, here],
                old_buf.at[2, :, here],
                old_buf.at[0, :, here],
                low_buf.at[:, here],
            )
        ):
            copy = pltpu.make_async_copy(
                source, news[item].at[:, there], out_sem.at[item, number]
            )
            copy.start()
            stores.append(copy)
    for copy in stores:
        copy.wait()


def adam(segments, grads, olds, held, micros):
    rows, columns = olds[0].shape
    span = max(s[3] + s[4] for s in segments) - min(s[3] for s in segments)
    held = [] if held is None else list(held)
    args = list(grads) + list(olds) + held
    return pl.pallas_call(
        functools.partial(adam_kernel, tuple(segments), len(grads), len(held)),
        out_shape=[jax.ShapeDtypeStruct((rows, columns), F32)] * 3
        + [jax.ShapeDtypeStruct((rows, columns), BF16)],
        in_specs=[pl.BlockSpec(memory_space=pl.ANY)] * len(args),
        out_specs=[pl.BlockSpec(memory_space=pl.ANY)] * 4,
        input_output_aliases={len(grads) + 3 + item: item for item in range(len(held))},
        scratch_shapes=[
            pltpu.VMEM((rows, span), BF16),
            pltpu.VMEM((3, rows, span), F32),
            pltpu.VMEM((rows, span), BF16),
            pltpu.SemaphoreType.DMA((4, len(segments))),
            pltpu.SemaphoreType.DMA((4, len(segments))),
        ],
        compiler_params=pltpu.CompilerParams(vmem_limit_bytes=VMEM_LIMIT),
        cost_estimate=cost(micros),
    )(*args)


def head_mean(values, ones):
    high = values.astype(BF16)
    rest = (values - high.astype(F32)).astype(BF16)
    return (dot(high, ones, 1, 0) + dot(rest, ones, 1, 0)) * (1.0 / HD)


def head_ones(width):
    row = lax.broadcasted_iota(jnp.int32, (width, width), 0) // HD
    col = lax.broadcasted_iota(jnp.int32, (width, width), 1) // HD
    return jnp.where(row == col, 1.0, 0.0).astype(BF16)


def partner(values):
    width = values.shape[-1]
    lane = lax.broadcasted_iota(jnp.int32, values.shape, 1)
    return jnp.where(
        lane % HD < HD // 2,
        pltpu.roll(values, width - HD // 2, 1),
        pltpu.roll(values, HD // 2, 1),
    )


def widen(table, width):
    return jnp.concatenate([table] * (width // table.shape[-1]), axis=-1)


def doc_first(starts, times):
    first = jnp.zeros_like(times)
    for item in range(starts.shape[0]):
        first = jnp.where(starts[item] <= times, starts[item], first)
    return first


def block_mask(starts, block, keys):
    shape = (keys, GROUP * HALF)
    times = block * HALF + lax.broadcasted_iota(jnp.int32, (1, GROUP * HALF), 1) % HALF
    key = lax.broadcasted_iota(jnp.int32, shape, 0)
    return (key >= doc_first(starts, times)) & (key <= times)


def stack_heads(ref, rows, group):
    return jnp.concatenate(
        [
            ref[rows, (group * GROUP + h) * HD : (group * GROUP + h + 1) * HD]
            for h in range(GROUP)
        ],
        axis=0,
    )


def unstack_heads(turned):
    wide = turned.T
    return [wide[h * HALF : (h + 1) * HALF, :] for h in range(GROUP)]


def attend_kernel(
    blocks,
    groups,
    place,
    starts,
    normed,
    weights_in,
    cosine,
    sine,
    gain,
    dy,
    swap_in,
    part,
    qk,
    q,
    k,
    v,
    o,
    lse,
    ordered,
    dy_all,
    swap_out,
    send_sem,
    recv_sem,
    local,
):
    sems = (send_sem, recv_sem)
    me = lax.axis_index("ctx")
    qk_width = qk.shape[1]
    q_width = q.shape[1]
    qkv_width = qk_width + v.shape[1]
    ones = head_ones(qk_width)
    meet(("ctx",))
    swap_copies = swap_start(swap_in, swap_out, sems, GATHER_SEMS)
    copies = gather_start(dy, dy_all, sems, 0)
    own_copies = [
        pltpu.make_async_copy(swap_in.at[me], swap_out.at[me], local.at[0]),
        pltpu.make_async_copy(dy, dy_all.at[me], local.at[1]),
    ]
    for copy in own_copies:
        copy.start()
    for block in range(blocks):
        ordered[block * HALF : (block + 1) * HALF, :] = normed[place[block]]
    qk[...] = dot(ordered[...], weights_in[:, :qk_width], 1, 0)
    v[...] = dot(ordered[...], weights_in[:, qk_width:qkv_width], 1, 0).astype(BF16)
    for block in range(blocks):
        to = slice(block * HALF, (block + 1) * HALF)
        values = qk[to, :]
        turned = values * lax.rsqrt(head_mean(values * values, ones) + NORM_EPS) * gain[...]
        turned = turned * widen(cosine[to, :], qk_width) + partner(turned) * widen(
            sine[to, :], qk_width
        )
        turned = turned.astype(BF16)
        q[to, :] = turned[:, :q_width]
        k[to, :] = turned[:, q_width:]
    for block in range(blocks):
        rows = slice(block * HALF, (block + 1) * HALF)
        keys = (block + 1) * HALF
        mask = block_mask(starts, block, keys)
        pieces = []
        for group in range(groups):
            lanes = slice(group * HD, (group + 1) * HD)
            queries = stack_heads(q, rows, group)
            scores = dot(k[:keys, lanes], queries, 1, 1) * SCALE
            weights = jnp.where(mask, jnp.exp(scores), 0.0)
            sums = jnp.sum(weights, axis=0, keepdims=True)
            lse[block, group : group + 1, :] = jnp.log(sums)
            mixed = dot(v[:keys, lanes], weights.astype(BF16), 0, 0) / sums
            pieces += unstack_heads(mixed)
        o[rows, :] = jnp.concatenate(pieces, axis=1).astype(BF16)
    for first in range(0, D, 512):
        part[:, first : first + 512] = dot(
            o[...], weights_in[first : first + 512, qkv_width:], 1, 1
        ).astype(BF16)
    gather_rest(copies, dy_all, sems, 0)
    for copy in swap_copies:
        copy.wait()
    for copy in own_copies:
        copy.wait()


def attend_back_kernel(
    blocks,
    groups,
    place,
    starts,
    lse,
    gain,
    part,
    grad_in,
    weights_from,
    q_in,
    k_in,
    v_in,
    qk_in,
    cosine_in,
    sine_in,
    middle_in,
    swap_in,
    joined,
    gain_grad,
    ordered,
    out,
    swap_out,
    *scratch,
):
    bufs = scratch[:-18]
    grad_all, weights_in, q, k, v, qk, cosine, sine, middle = scratch[-18:-9]
    do, dq, dk, dv, send_one, recv_one, send_two, recv_two, local = scratch[-9:]
    sems = (send_one, recv_one)
    me = lax.axis_index("ctx")
    qk_width = qk.shape[1]
    q_width = q.shape[1]
    qkv_width = qk_width + v.shape[1]
    ones = head_ones(qk_width)
    meet(("ctx",))
    copies = sum_start(part, bufs, sems)
    loads = [
        load(source, target, local.at[item])
        for item, (source, target) in enumerate(
            (
                (grad_in, grad_all),
                (weights_from, weights_in),
                (q_in, q),
                (k_in, k),
                (v_in, v),
                (qk_in, qk),
                (cosine_in, cosine),
                (sine_in, sine),
                (middle_in, middle),
            )
        )
    ]
    swap_copies = swap_start(swap_in, swap_out, (send_two, recv_two), 0)
    own = load(swap_in.at[me], swap_out.at[me], local.at[9])
    for copy in loads[:5]:
        copy.wait()
    for block in range(blocks):
        ordered[block * HALF : (block + 1) * HALF, :] = grad_all[place[block]]
    do[...] = dot(ordered[...], weights_in[:, qkv_width:], 1, 0).astype(BF16)
    dk[...] = jnp.zeros_like(dk)
    dv[...] = jnp.zeros_like(dv)
    for block in range(blocks):
        if block == blocks // 2:
            sum_pass(copies, part, bufs, sems)
        rows = slice(block * HALF, (block + 1) * HALF)
        keys = (block + 1) * HALF
        mask = block_mask(starts, block, keys)
        pieces = []
        dk_add = []
        dv_add = []
        for group in range(groups):
            lanes = slice(group * HD, (group + 1) * HD)
            queries = stack_heads(q, rows, group)
            outs = stack_heads(do, rows, group)
            key_rows = k[:keys, lanes]
            scores = dot(key_rows, queries, 1, 1) * SCALE
            weights = jnp.where(
                mask, jnp.exp(scores - lse[block, group : group + 1, :]), 0.0
            )
            back = dot(v[:keys, lanes], outs, 1, 1)
            delta = jnp.sum(weights * back, axis=0, keepdims=True)
            grads = (weights * (back - delta)).astype(BF16)
            pieces += unstack_heads(dot(key_rows, grads, 0, 0) * SCALE)
            dk_add.append(dot(grads, queries, 1, 0) * SCALE)
            dv_add.append(dot(weights.astype(BF16), outs, 1, 0))
        dq[rows, :] = jnp.concatenate(pieces, axis=1)
        dk[:keys, :] += jnp.concatenate(dk_add, axis=1)
        dv[:keys, :] += jnp.concatenate(dv_add, axis=1)
    total = jnp.zeros((1, qk_width), F32)
    for copy in loads[5:]:
        copy.wait()
    for block in range(blocks):
        to = slice(block * HALF, (block + 1) * HALF)
        values = qk[to, :]
        root = lax.rsqrt(head_mean(values * values, ones) + NORM_EPS)
        unit = values * root
        grad = jnp.concatenate([dq[to, :], dk[to, :]], axis=1)
        grad = grad * widen(cosine[to, :], qk_width) - partner(grad) * widen(
            sine[to, :], qk_width
        )
        total = total + jnp.sum(grad * unit, axis=0, keepdims=True)
        grad = grad * gain[...]
        grad = root * (grad - unit * head_mean(grad * unit, ones))
        joined[to, :qk_width] = grad.astype(BF16)
        joined[to, qk_width:] = dv[to, :].astype(BF16)
    gain_grad[...] = total
    read = sum_rest(copies, part, bufs)
    half = middle.shape[0] // 2
    for first in (0, half):
        rows = pl.ds(first, half)
        out[rows, :] = (middle[rows, :] + read(first)).astype(BF16)
    for copy in swap_copies:
        copy.wait()
    own.wait()


def rms_scale(values_in, gain_vec):
    return (
        values_in
        * lax.rsqrt(jnp.mean(values_in * values_in, axis=-1, keepdims=True) + NORM_EPS)
        * gain_vec
    )


def inverse_freq():
    return 1.0 / ROPE_BASE ** (jnp.arange(0, HD, 2).astype(F32) / HD)


def shards(
    tokens,
    cotangent,
    doc_starts,
    block_order,
    master_weights,
    moment_one,
    moment_two,
    gains,
    gains_moment_one,
    gains_moment_two,
):
    nctx = lax.axis_size("ctx")
    nfsdp = lax.axis_size("fsdp")
    own_rows = master_weights.shape[0]
    tok_rows = tokens.shape[1]
    stream_len = tok_rows * nctx
    blocks = stream_len // HALF
    groups = KVHEADS // nctx
    q_width = D // nctx
    kv_width = KVD // nctx
    qk_width = q_width + kv_width
    qkv_width = qk_width + kv_width
    tiles = FF // 128
    ff_tiles = -(-tiles // nctx)
    ff_width = ff_tiles * 128
    bundles = 2
    cuts = [0, (ff_tiles * 4 + 6) // 7 * 128, ff_width]

    low = master_weights.astype(BF16)

    def ff_part(base, index, start, stop):
        first = index * ff_width + start
        last = index * ff_width + stop
        real_first, real_last = min(first, FF), min(last, FF)
        part = low[:, base + real_first : base + real_last]
        if real_last - real_first < last - first:
            part = jnp.pad(part, ((0, 0), (0, (last - first) - (real_last - real_first))))
        return part

    def attn_part(index):
        return jnp.concatenate(
            [
                low[:, index * q_width : (index + 1) * q_width],
                low[:, D + index * kv_width : D + (index + 1) * kv_width],
                low[:, D + KVD + index * kv_width : D + KVD + (index + 1) * kv_width],
                low[:, QKVC + index * q_width : QKVC + (index + 1) * q_width],
            ],
            axis=1,
        )

    gate_base = QKVC + D
    bases = (gate_base, gate_base + FF, gate_base + 2 * FF)
    attn_send = jnp.stack([attn_part(c) for c in range(nctx)])
    ff_send = [
        jnp.stack(
            [
                jnp.concatenate(
                    [ff_part(base, c, cuts[b], cuts[b + 1]) for base in bases], axis=1
                )
                for c in range(nctx)
            ]
        )
        for b in range(bundles)
    ]

    def gather_rows(piece):
        return lax.all_gather(
            piece.reshape(nctx * own_rows, piece.shape[-1]), "fsdp", axis=0, tiled=True
        )

    def spread(active):
        return (
            active.reshape(active.shape[0], nctx, nfsdp, own_rows)
            .transpose(0, 2, 1, 3)
            .reshape(active.shape[0], D)
        )

    def unspread(active):
        return (
            active.reshape(active.shape[0], nfsdp, nctx, own_rows)
            .transpose(0, 2, 1, 3)
            .reshape(active.shape[0], D)
        )

    g_attn = spread(gains[None, :D])
    g_ffn = spread(gains[None, D : 2 * D])
    x_low = spread(tokens[0])
    dy_low = spread(cotangent[0])
    normed = rms_scale(x_low.astype(F32), g_attn).astype(BF16)

    (attn_held,) = exchange(("swap",), [attn_send], 0, 10)
    w_attn = gather_rows(attn_held)
    first_send, attn_held = lax.optimization_barrier((ff_send[0], attn_held))
    (first_held,) = exchange(("swap",), [first_send], 1, 16)
    normed, first_held = lax.optimization_barrier((normed, first_held))
    (normed_all,) = exchange(("gather",), [normed], 2, 28)
    normed_all = normed_all.reshape(stream_len, D)

    order = block_order.reshape(blocks)
    place = jnp.argsort(order).astype(jnp.int32)
    starts = doc_starts[0]
    times = jnp.arange(stream_len, dtype=jnp.int32)
    first = jnp.max(jnp.where(starts[None, :] <= times[:, None], starts[None, :], 0), axis=1)
    angles = (times - first).astype(F32)[:, None] * inverse_freq()[None, :]
    cosine = jnp.concatenate([jnp.cos(angles)] * 2, axis=1)
    sine = jnp.concatenate([-jnp.sin(angles), jnp.sin(angles)], axis=1)

    g_query = gains[2 * D : 2 * D + HD]
    g_key = gains[2 * D + HD :]
    qk_gain = jnp.concatenate(
        [jnp.tile(g_query, q_width // HD), jnp.tile(g_key, kv_width // HD)]
    )[None]

    dma = pltpu.SemaphoreType.DMA
    all_low = jax.ShapeDtypeStruct((nctx, tok_rows, D), BF16)
    part, qk, q, k, v, mixed, lse, normed_pos, dy_all, second_held = remote_call(
        functools.partial(attend_kernel, blocks, groups),
        [
            jax.ShapeDtypeStruct((stream_len, D), BF16),
            jax.ShapeDtypeStruct((stream_len, qk_width), F32),
            jax.ShapeDtypeStruct((stream_len, q_width), BF16),
            jax.ShapeDtypeStruct((stream_len, kv_width), BF16),
            jax.ShapeDtypeStruct((stream_len, kv_width), BF16),
            jax.ShapeDtypeStruct((stream_len, q_width), BF16),
            jax.ShapeDtypeStruct((blocks, groups, GROUP * HALF), F32),
            jax.ShapeDtypeStruct((stream_len, D), BF16),
            all_low,
            jax.ShapeDtypeStruct(ff_send[1].shape, BF16),
        ],
        (place, starts, normed_all.reshape(blocks, HALF, D), w_attn, cosine, sine, qk_gain, dy_low, ff_send[1]),
        3,
        42,
        [
            dma((GATHER_SEMS + nctx,)),
            dma((GATHER_SEMS + nctx,)),
            dma((2,)),
        ],
        (8, 9),
        2,
        2,
    )
    dy_all = dy_all.reshape(stream_len, D)
    w_ff = [gather_rows(first_held), gather_rows(second_held)]
    sum_bufs = sum_scratch(nctx, tok_rows)
    sum_sems = [dma((GATHER_SEMS,)), dma((GATHER_SEMS,))]
    norm_scratch = (
        sum_bufs + [pltpu.VMEM((tok_rows, D), BF16)] + sum_sems + sum_sems + [dma]
    )
    own_f32 = jax.ShapeDtypeStruct((tok_rows, D), F32)
    row_f32 = jax.ShapeDtypeStruct((1, D), F32)

    middle, normed_two_all = remote_call(
        middle_kernel,
        [own_f32, all_low],
        (order, part.reshape(blocks, HALF, D), x_low, g_ffn),
        4,
        57,
        sum_bufs + [pltpu.VMEM((stream_len, D), BF16)] + norm_scratch[len(sum_bufs) :],
        (1,),
        1,
    )
    normed_two_all = normed_two_all.reshape(stream_len, D)

    def sum_rows(grad):
        return lax.psum_scatter(grad, "fsdp", scatter_dimension=0, tiled=True).reshape(
            nctx, own_rows, grad.shape[-1]
        )

    def feed(b, x_all, dy):
        width = cuts[b + 1] - cuts[b]
        w_gu, w_down = w_ff[b][:, : 2 * width], w_ff[b][:, 2 * width :]
        gate_up = dot(x_all, w_gu, 1, 0)
        gate, up = gate_up[:, :width], gate_up[:, width:]
        gated = jax.nn.sigmoid(gate)
        act = gate * gated
        hidden = (act * up).astype(BF16)
        back_hidden = dot(dy, w_down, 1, 0)
        grad_gu = jnp.concatenate(
            [back_hidden * up * (gated + act * (1.0 - gated)), back_hidden * act], axis=1
        ).astype(BF16)
        return hidden, grad_gu, dot(hidden, w_down, 1, 1), dot(grad_gu, w_gu, 1, 1)

    hidden, grad_gu, out_partial, back_partial = feed(0, normed_two_all, dy_all)
    out_partial = out_partial.astype(BF16)
    gu_grad = dot(normed_two_all, grad_gu, 0, 0).astype(BF16)
    down_grad = dot(dy_all, hidden, 0, 0).astype(BF16)
    gu_grad, down_grad, back_partial, out_partial, w_ff[1] = lax.optimization_barrier(
        (gu_grad, down_grad, back_partial, out_partial, w_ff[1])
    )
    width_two = cuts[2] - cuts[1]
    hidden, grad_gu, _, back_more = feed(1, normed_two_all, dy_all)
    back_partial = (back_partial + back_more).astype(BF16)
    ff_sums = [sum_rows(gu_grad), sum_rows(down_grad)]
    low_stream = pltpu.VMEM((stream_len, D), BF16)

    grad_middle, grad_g_ffn, grad_middle_all, last_grad, out_partial = remote_call(
        middle_back_kernel,
        [
            own_f32,
            row_f32,
            all_low,
            jax.ShapeDtypeStruct((D, 3 * width_two), BF16),
            jax.ShapeDtypeStruct((stream_len, D), BF16),
        ],
        (
            back_partial,
            middle,
            dy_low,
            g_ffn,
            normed_two_all,
            dy_all,
            grad_gu,
            hidden,
            w_ff[1][:, 2 * width_two :],
            out_partial,
        ),
        5,
        57,
        sum_bufs
        + [
            pltpu.VMEM((tok_rows, D), BF16),
            low_stream,
            low_stream,
            pltpu.VMEM((stream_len, 2 * width_two), BF16),
            pltpu.VMEM((stream_len, width_two), BF16),
            pltpu.VMEM((D, width_two), BF16),
            low_stream,
            pltpu.VMEM((D, stream_len), BF16),
            pltpu.VMEM((D, 3 * width_two), BF16),
        ]
        + sum_sems
        + sum_sems
        + [dma((9,))],
        (2, 3, 4),
        0,
        6,
    )
    ff_sums.append(sum_rows(last_grad))

    grad_joined, qk_gain_grad, grad_middle_pos, out_tokens, gu_own = remote_call(
        functools.partial(attend_back_kernel, blocks, groups),
        [
            jax.ShapeDtypeStruct((stream_len, qkv_width), BF16),
            jax.ShapeDtypeStruct((1, qk_width), F32),
            jax.ShapeDtypeStruct((stream_len, D), BF16),
            jax.ShapeDtypeStruct((tok_rows, D), BF16),
            jax.ShapeDtypeStruct(ff_sums[0].shape, BF16),
        ],
        (
            place,
            starts,
            lse,
            qk_gain,
            out_partial,
            grad_middle_all.reshape(blocks, HALF, D),
            w_attn,
            q,
            k,
            v,
            qk,
            cosine,
            sine,
            middle,
            ff_sums[0],
        ),
        7,
        42,
        sum_bufs
        + [
            pltpu.VMEM((blocks, HALF, D), BF16),
            pltpu.VMEM(w_attn.shape, BF16),
            pltpu.VMEM((stream_len, q_width), BF16),
            pltpu.VMEM((stream_len, kv_width), BF16),
            pltpu.VMEM((stream_len, kv_width), BF16),
            pltpu.VMEM((stream_len, qk_width), F32),
            pltpu.VMEM((stream_len, HD), F32),
            pltpu.VMEM((stream_len, HD), F32),
            pltpu.VMEM((tok_rows, D), F32),
            pltpu.VMEM((stream_len, q_width), BF16),
            pltpu.VMEM((stream_len, q_width), F32),
            pltpu.VMEM((stream_len, kv_width), F32),
            pltpu.VMEM((stream_len, kv_width), F32),
        ]
        + sum_sems
        + sum_sems
        + [dma((10,))],
        (4,),
        2,
        10,
    )
    attn_grad = jnp.concatenate(
        [dot(normed_pos, grad_joined, 0, 0), dot(grad_middle_pos, mixed, 0, 0)], axis=1
    ).astype(BF16)
    back_attn = dot(grad_joined, w_attn[:, :qkv_width], 1, 1).astype(BF16)
    small = dma((nctx + nfsdp,))
    chips = nfsdp // 2
    line_block = (nctx * own_rows, attn_grad.shape[1])
    line_sems = dma((3 * chips + 3 * nctx,))
    own_shape = (nctx, own_rows, attn_grad.shape[1])
    grad_tokens, gain_sums, attn_own, down_own = remote_call(
        functools.partial(last_kernel, 1),
        [
            own_f32,
            jax.ShapeDtypeStruct((8, D), F32),
            jax.ShapeDtypeStruct(own_shape, BF16),
            jax.ShapeDtypeStruct(ff_sums[1].shape, BF16),
        ],
        (
            order,
            back_attn.reshape(blocks, HALF, D),
            x_low,
            grad_middle,
            g_attn,
            grad_g_ffn,
            qk_gain_grad,
            attn_grad,
            ff_sums[1],
        ),
        6,
        45,
        sum_bufs
        + [
            pltpu.VMEM((stream_len, D), BF16),
            pltpu.VMEM((chips,) + line_block, BF16),
            pltpu.VMEM((2, chips) + line_block, BF16),
            pltpu.VMEM((2, chips) + line_block, BF16),
            pltpu.VMEM(own_shape, BF16),
            pltpu.VMEM((nctx, 8, D), F32),
            pltpu.VMEM((nfsdp, 8, D), F32),
        ]
        + sum_sems
        + [small, small, line_sems, line_sems, dma((2,))],
        (3,),
        1,
        1,
    )
    out_tokens = unspread(out_tokens)[None]
    grad_tokens = unspread(grad_tokens)[None]
    gain_grad = jnp.concatenate(
        [
            unspread(gain_sums[:1])[0],
            unspread(gain_sums[1:2])[0],
            jnp.sum(gain_sums[2, :q_width].reshape(-1, HD), axis=0),
            jnp.sum(gain_sums[2, q_width:qk_width].reshape(-1, HD), axis=0),
        ]
    )

    olds = (master_weights, moment_one, moment_two)

    def feed_segments(b, pieces):
        width = cuts[b + 1] - cuts[b]
        found = []
        for part in range(3):
            for c in range(nctx):
                column = c * ff_width + cuts[b]
                real = min(max(FF - column, 0), width)
                if real:
                    piece, first = pieces[part]
                    found.append((piece, c, first, bases[part] + column, real))
        return found

    width_one = cuts[1]
    news = adam(
        feed_segments(0, ((0, 0), (0, width_one), (1, 0))), [gu_own, down_own], olds, None, 7
    )
    parts = (
        (0, 0, q_width),
        (q_width, D, kv_width),
        (qk_width, D + KVD, kv_width),
        (qkv_width, QKVC, q_width),
    )
    if kv_width % 128:
        attn_own = jnp.concatenate(
            [attn_own[c, :, f : f + w] for f, _, w in parts for c in range(nctx)], axis=1
        )[None]
        segments = [(0, 0, 0, 0, gate_base)]
    else:
        segments = [
            (0, c, first, base + c * width, width)
            for first, base, width in parts
            for c in range(nctx)
        ]
    news = adam(segments, [attn_own], olds, news, 3)
    (last_own,) = exchange(("swap",), [ff_sums[2]], 8, 12)
    first_new, second_new, master_new, low_new = adam(
        feed_segments(1, ((0, 0), (0, width_two), (0, 2 * width_two))),
        [last_own],
        olds,
        news,
        6,
    )
    gain_first, gain_second, gain_new = adam_update(
        gains, gain_grad, gains_moment_one, gains_moment_two, GAIN_RATE, 0.0
    )
    return (
        out_tokens,
        grad_tokens,
        first_new,
        second_new,
        master_new,
        low_new,
        gain_first,
        gain_second,
        gain_new,
    )


def solution(mesh):
    rows = P("fsdp", "ctx", None)
    weights = P(("ctx", "fsdp"), None)
    return jax.shard_map(
        shards,
        mesh=mesh,
        in_specs=(rows, rows, P("fsdp", None), P(), weights, weights, weights, P(), P(), P()),
        out_specs=(rows, rows, weights, weights, weights, weights, P(), P(), P()),
        check_vma=False,
    )
```

```python
import functools

import jax
import jax.numpy as jnp
from jax import lax
from jax.experimental import pallas as pl
from jax.experimental.pallas import tpu as pltpu
from jax.sharding import PartitionSpec as P

D = 1536
HEADS = 24
KVHEADS = 8
HD = 64
FF = 6912
STEP = 10
HALF = 128
KVD = 512
QKVC = 2560
GROUP = HEADS // KVHEADS

ROPE_BASE = 1000000.0
NORM_EPS = 1e-05
BETA_ONE = 0.9
BETA_TWO = 0.95
ADAM_EPS = 1e-08
WEIGHT_DECAY = 0.1
LEARN_RATE = 0.03
GAIN_RATE = 0.5
SCALE = HD ** (-0.5)
MESH = pl.DeviceIdType.MESH
F32 = jnp.float32
BF16 = jnp.bfloat16
VMEM_LIMIT = 60 * 1024 * 1024


def dot(left, right, left_dim, right_dim):
    return lax.dot_general(
        left, right, (((left_dim,), (right_dim,)), ((), ())), preferred_element_type=F32
    )


def send(source, target, sems, item, peer):
    copy = pltpu.make_async_remote_copy(
        src_ref=source,
        dst_ref=target,
        send_sem=sems[0].at[item],
        recv_sem=sems[1].at[item],
        device_id=peer,
        device_id_type=MESH,
    )
    copy.start()
    return copy


def meet(axes):
    barrier = pltpu.get_barrier_semaphore()
    total = 0
    for axis in axes:
        size = lax.axis_size(axis)
        me = lax.axis_index(axis)
        for step in range(1, size):
            pl.semaphore_signal(
                barrier,
                inc=1,
                device_id={axis: lax.rem(me + step, size)},
                device_id_type=MESH,
            )
        total += size - 1
    pl.semaphore_wait(barrier, total)


def square():
    me = lax.axis_index("ctx")
    return me, me + 1 - 2 * lax.rem(me, 2), lax.rem(me + 2, 4), 3 - me


def swap_start(source, target, sems, base):
    size = lax.axis_size("ctx")
    me = lax.axis_index("ctx")
    copies = []
    for step in range(1, size):
        peer = lax.rem(me + step, size)
        copies.append(
            send(source.at[peer], target.at[me], sems, base + step, {"ctx": peer})
        )
    return copies


def gather_start(source, target, sems, base):
    size = lax.axis_size("ctx")
    me = lax.axis_index("ctx")
    if size != 4:
        return [
            send(
                source,
                target.at[me],
                sems,
                base + step,
                {"ctx": lax.rem(me + step, size)},
            )
            for step in range(1, size)
        ]
    me, side, over, across = square()
    half = source.shape[0] // 2
    top, low = pl.ds(0, half), pl.ds(half, half)
    return [
        send(source.at[top], target.at[me, top], sems, base, {"ctx": side}),
        send(source.at[low], target.at[me, low], sems, base + 1, {"ctx": over}),
        send(source.at[low], target.at[me, low], sems, base + 2, {"ctx": side}),
        send(source.at[top], target.at[me, top], sems, base + 3, {"ctx": over}),
    ]


def gather_pass(copies, target, sems, base):
    if lax.axis_size("ctx") != 4:
        return
    me, side, over, across = square()
    half = target.shape[1] // 2
    top, low = pl.ds(0, half), pl.ds(half, half)
    copies[0].wait_recv()
    copies.append(send(target.at[side, top], target.at[side, top], sems, base + 4, {"ctx": over}))
    copies[1].wait_recv()
    copies.append(send(target.at[over, low], target.at[over, low], sems, base + 5, {"ctx": side}))


def gather_end(copies):
    if lax.axis_size("ctx") != 4:
        for copy in copies:
            copy.wait()
        return
    for copy in copies:
        copy.wait_send()
    for copy in copies[2:]:
        copy.wait_recv()


def gather_rest(copies, target, sems, base):
    gather_pass(copies, target, sems, base)
    gather_end(copies)


def load(source, target, sem):
    copy = pltpu.make_async_copy(source, target, sem)
    copy.start()
    return copy


GATHER_SEMS = 8


def exchange_kernel(kinds, *refs):
    count = len(kinds)
    ins, outs = refs[:count], refs[count : 2 * count]
    send_sem, recv_sem, local_sem = refs[2 * count :]
    sems = (send_sem, recv_sem)
    me = lax.axis_index("ctx")
    meet(("ctx",))
    copies = []
    own = []
    for item in range(count):
        base = item * GATHER_SEMS
        if kinds[item] == "gather":
            copies.append(gather_start(ins[item], outs[item], sems, base))
            source = ins[item]
        else:
            copies.append(swap_start(ins[item], outs[item], sems, base))
            source = ins[item].at[me]
        copy = pltpu.make_async_copy(source, outs[item].at[me], local_sem.at[item])
        copy.start()
        own.append(copy)
    for item in range(count):
        if kinds[item] == "gather":
            gather_rest(copies[item], outs[item], sems, item * GATHER_SEMS)
        else:
            for copy in copies[item]:
                copy.wait()
    for copy in own:
        copy.wait()


def remote_params(collective_id):
    return pltpu.CompilerParams(
        collective_id=collective_id, has_side_effects=True, vmem_limit_bytes=VMEM_LIMIT
    )


def cost(micros):
    return pl.CostEstimate(flops=0, bytes_accessed=int(micros * 3.0e6), transcendentals=0)


def exchange(kinds, arrays, collective_id, micros):
    size = lax.axis_size("ctx")
    shapes = [
        jax.ShapeDtypeStruct((size,) + a.shape if kind == "gather" else a.shape, a.dtype)
        for kind, a in zip(kinds, arrays)
    ]
    sems = pltpu.SemaphoreType.DMA((len(arrays) * GATHER_SEMS,))
    return pl.pallas_call(
        functools.partial(exchange_kernel, kinds),
        out_shape=shapes,
        in_specs=[pl.BlockSpec(memory_space=pl.ANY)] * len(arrays),
        out_specs=[pl.BlockSpec(memory_space=pl.ANY)] * len(arrays),
        scratch_shapes=[sems, sems, pltpu.SemaphoreType.DMA((len(arrays),))],
        compiler_params=remote_params(collective_id),
        cost_estimate=cost(micros),
    )(*arrays)


def sum_scratch(size, rows):
    if size == 4:
        half = pltpu.VMEM((2, rows // 2, D), BF16)
        return [half, half, pltpu.VMEM((2, rows, D), BF16)]
    return [pltpu.VMEM((size - 1, rows, D), BF16)]


def sum_start(part, bufs, sems):
    size = lax.axis_size("ctx")
    me = lax.axis_index("ctx")
    rows = part.shape[0] // size

    def block(owner, first=0, count=rows):
        return pl.ds(pl.multiple_of(owner * rows + first, rows // 2), count)

    if size != 4:
        copies = []
        for step in range(1, size):
            peer = lax.rem(me + step, size)
            copies.append(
                send(part.at[block(peer)], bufs[0].at[step - 1], sems, step, {"ctx": peer})
            )
        return copies
    me, side, over, across = square()
    half = rows // 2
    relay, _, landed = bufs
    return [
        send(part.at[block(across, 0, half)], relay.at[0], sems, 0, {"ctx": side}),
        send(part.at[block(across, half, half)], relay.at[1], sems, 1, {"ctx": over}),
        send(
            part.at[block(side, 0, half)],
            landed.at[0, pl.ds(0, half)],
            sems,
            2,
            {"ctx": side},
        ),
        send(
            part.at[block(over, half, half)],
            landed.at[1, pl.ds(half, half)],
            sems,
            3,
            {"ctx": over},
        ),
    ]


def sum_pass(copies, part, bufs, sems):
    if lax.axis_size("ctx") != 4:
        return
    rows = part.shape[0] // 4
    half = rows // 2

    def rows_of(owner, first):
        return pl.ds(pl.multiple_of(owner * rows + first, half), half)

    me, side, over, across = square()
    relay, passed, landed = bufs
    copies[0].wait_recv()
    passed[0] = (part[rows_of(over, 0), :].astype(F32) + relay[0].astype(F32)).astype(BF16)
    copies.append(
        send(passed.at[0], landed.at[1, pl.ds(0, half)], sems, 4, {"ctx": over})
    )
    copies[1].wait_recv()
    passed[1] = (part[rows_of(side, half), :].astype(F32) + relay[1].astype(F32)).astype(
        BF16
    )
    copies.append(
        send(passed.at[1], landed.at[0, pl.ds(half, half)], sems, 5, {"ctx": side})
    )


def sum_rest(copies, part, bufs):
    size = lax.axis_size("ctx")
    me = lax.axis_index("ctx")
    rows = part.shape[0] // size
    half = rows // 2

    def rows_of(owner, first):
        return pl.ds(pl.multiple_of(owner * rows + first, half), half)

    if size != 4:
        for copy in copies:
            copy.wait()

        def read(first):
            total = part[rows_of(me, first), :].astype(F32)
            for step in range(1, size):
                total = total + bufs[0][step - 1, pl.ds(first, half), :].astype(F32)
            return total

        return read
    relay, passed, landed = bufs
    for copy in copies:
        copy.wait_send()
    for copy in copies[2:]:
        copy.wait_recv()

    def read(first):
        return (
            part[rows_of(me, first), :].astype(F32)
            + landed[0, pl.ds(first, half), :].astype(F32)
            + landed[1, pl.ds(first, half), :].astype(F32)
        )

    return read


def row_scale(values):
    return lax.rsqrt(jnp.mean(values * values, axis=-1, keepdims=True) + NORM_EPS)


def first_kernel(
    starts, origin, x, dy, gain, freq, x_low, dy_low, table, normed_all, *scratch
):
    move, normed, send_one, recv_one, local = scratch
    me = lax.axis_index("ctx")
    row = lax.broadcasted_iota(jnp.int32, move.shape, 0)
    move[...] = jnp.where(row == origin[...], 1.0, 0.0).astype(BF16)
    values = dot(x[...], move[...], 1, 0)
    x_low[...] = values.astype(BF16)
    normed[...] = (values * row_scale(values) * gain[...]).astype(BF16)
    meet(("ctx",))
    sems = (send_one, recv_one)
    copies = gather_start(normed, normed_all, sems, 0)
    own = load(normed, normed_all.at[me], local)
    dy_low[...] = dot(dy[...], move[...], 1, 0).astype(BF16)
    gather_pass(copies, normed_all, sems, 0)
    times = lax.broadcasted_iota(jnp.int32, (table.shape[0], 1), 0)
    angles = (times - doc_first(starts, times)).astype(F32) * freq[...]
    lane = lax.broadcasted_iota(jnp.int32, angles.shape, 1)
    sine = jnp.sin(angles)
    sine = jnp.where(lane % HD < HD // 2, -sine, sine)
    table[...] = jnp.where(lane < HD, jnp.cos(angles), sine)
    gather_end(copies)
    own.wait()


def middle_kernel(part, x, gain, middle, normed_all, *scratch):
    bufs, (normed, send_one, recv_one, send_two, recv_two, local) = scratch[:-6], scratch[-6:]
    me = lax.axis_index("ctx")
    meet(("ctx",))
    copies = sum_start(part, bufs, (send_one, recv_one))
    sum_pass(copies, part, bufs, (send_one, recv_one))
    read = sum_rest(copies, part, bufs)
    half = x.shape[0] // 2
    for first in (0, half):
        rows = pl.ds(first, half)
        values = x[rows, :].astype(F32) + read(first)
        middle[rows, :] = values
        normed[rows, :] = (values * row_scale(values) * gain[...]).astype(BF16)
    sems = (send_two, recv_two)
    copies = gather_start(normed, normed_all, sems, 0)
    own = load(normed, normed_all.at[me], local)
    gather_rest(copies, normed_all, sems, 0)
    own.wait()


def column_tiles(total, body):
    def step(tile, carry):
        body(pl.multiple_of(tile * 256, 256), 256)
        return carry

    lax.fori_loop(0, total // 256, step, 0)
    if total % 256:
        body(total - total % 256, total % 256)


def turn(source, target):
    for first in range(0, source.shape[0], HALF):
        rows = slice(first, first + HALF)
        target[:, rows] = source[rows, :].T


def middle_back_kernel(
    part,
    middle,
    dy,
    gain,
    down_grad,
    x_all,
    dy_all,
    grad_gu,
    hidden,
    w_down,
    out_part,
    grad,
    gain_grad,
    down_sum,
    grad_all,
    weight_grad,
    out,
    *scratch,
):
    bufs = scratch[:-18]
    low, x_buf, gu_buf, hidden_buf, down_buf, out_buf, turned, weight_buf = scratch[-18:-10]
    home, going, coming, send_one, recv_one, send_two, recv_two, send_three, recv_three, local = (
        scratch[-10:]
    )
    me = lax.axis_index("ctx")
    chips = lax.axis_size("fsdp") // 2
    line = (send_three, recv_three)
    meet(("ctx", "fsdp"))
    copies = sum_start(part, bufs, (send_one, recv_one))
    home_copies = line_start(down_grad, home, line, 0)
    loads = [
        load(source, target, local.at[item])
        for item, (source, target) in enumerate(
            (
                (x_all, x_buf),
                (grad_gu, gu_buf),
                (hidden, hidden_buf),
                (w_down, down_buf),
                (out_part, out_buf),
            )
        )
    ]
    gu_width = grad_gu.shape[1]
    loads[0].wait()
    turn(x_buf, turned)
    loads.append(load(dy_all, x_buf, local.at[5]))
    line_home(home_copies, down_grad, home)
    line_step(chips - 1, home, going, coming, line, chips)
    loads[1].wait()

    def gu_tile(first, width):
        weight_buf[:, pl.ds(first, width)] = dot(
            turned[...], gu_buf[:, pl.ds(first, width)], 1, 0
        ).astype(BF16)

    column_tiles(gu_width, gu_tile)
    sum_pass(copies, part, bufs, (send_one, recv_one))
    loads[5].wait()
    turn(x_buf, turned)
    loads[2].wait()

    def down_tile(first, width):
        weight_buf[:, pl.ds(gu_width + first, width)] = dot(
            turned[...], hidden_buf[:, pl.ds(first, width)], 1, 0
        ).astype(BF16)

    column_tiles(hidden.shape[1], down_tile)
    stores = [load(weight_buf, weight_grad, local.at[6])]
    if chips > 2:
        line_step(chips - 2, home, going, coming, line, chips)
    read = sum_rest(copies, part, bufs)
    half = dy.shape[0] // 2
    total = jnp.zeros((1, D), F32)
    for first in (0, half):
        rows = pl.ds(first, half)
        values = middle[rows, :]
        root = row_scale(values)
        unit = values * root
        back = read(first)
        total = total + jnp.sum(back * unit, axis=0, keepdims=True)
        back = back * gain[...]
        back = root * (back - unit * jnp.mean(back * unit, axis=-1, keepdims=True))
        back = back + dy[rows, :].astype(F32)
        grad[rows, :] = back
        low[rows, :] = back.astype(BF16)
    gain_grad[...] = total
    sems = (send_two, recv_two)
    copies = gather_start(low, grad_all, sems, 0)
    stores.append(load(low, grad_all.at[me], local.at[7]))
    loads[3].wait()
    loads[4].wait()

    def out_tile(first, width):
        columns = pl.ds(first, width)
        out_buf[:, columns] = (
            out_buf[:, columns].astype(F32) + dot(hidden_buf[...], down_buf[columns, :], 1, 1)
        ).astype(BF16)

    column_tiles(D, out_tile)
    stores.append(load(out_buf, out, local.at[8]))
    gather_pass(copies, grad_all, sems, 0)
    for reach in range(min(chips - 1, max(chips - 3, 1)), 0, -1):
        line_step(reach, home, going, coming, line, chips)
    gather_end(copies)
    line_end(home_copies, home, going, coming, line, chips)
    chip = lax.axis_index("fsdp") // 2
    rows = down_sum.shape[1]
    for index in range(down_sum.shape[0]):
        down_sum[index] = home[chip, index * rows : (index + 1) * rows, :]
    for copy in stores:
        copy.wait()


def line_start(grad, home, sems, base):
    me = lax.axis_index("fsdp")
    chips = lax.axis_size("fsdp") // 2
    core = lax.rem(me, 2)
    rows = grad.shape[0] // (2 * chips)
    copies = []
    for chip in range(chips):
        theirs = pl.ds(pl.multiple_of((2 * chip + 1 - core) * rows, rows), rows)
        copies.append(
            send(grad.at[theirs], home.at[chip], sems, base + chip, {"fsdp": me + 1 - 2 * core})
        )
    return copies


def line_home(copies, grad, home):
    me = lax.axis_index("fsdp")
    chips = lax.axis_size("fsdp") // 2
    core = lax.rem(me, 2)
    rows = grad.shape[0] // (2 * chips)
    for chip in range(chips):
        copies[chip].wait_recv()
        mine = pl.ds(pl.multiple_of((2 * chip + core) * rows, rows), rows)
        home[chip] = (home[chip].astype(F32) + grad[mine, :].astype(F32)).astype(BF16)


def line_copies(reach, going, coming, sems, base):
    me = lax.axis_index("fsdp")
    chips = lax.axis_size("fsdp") // 2
    chip = me // 2
    found = []
    for side, way in ((0, 1), (1, -1)):
        copy = pltpu.make_async_remote_copy(
            src_ref=going.at[side, reach - 1],
            dst_ref=coming.at[side, reach - 1],
            send_sem=sems[0].at[base + 2 * reach + side],
            recv_sem=sems[1].at[base + 2 * reach + side],
            device_id={"fsdp": lax.rem(me + 2 * way + 2 * chips, 2 * chips)},
            device_id_type=MESH,
        )
        if way == 1:
            sent = chip + reach <= chips - 1
            got = (chip >= 1) & (chip + reach <= chips)
            more = (chip >= 1) & sent
        else:
            sent = chip >= reach
            got = (chip <= chips - 2) & (chip + 1 >= reach)
            more = (chip <= chips - 2) & sent
        found.append((side, way, copy, sent, got, more))
    return found


def line_step(reach, home, going, coming, sems, base):
    me = lax.axis_index("fsdp")
    chips = lax.axis_size("fsdp") // 2
    chip = me // 2
    if reach < chips - 1:
        for _, _, copy, _, got, _ in line_copies(reach + 1, going, coming, sems, base):
            pl.when(got)(copy.wait_recv)
    for side, way, copy, sent, _, more in line_copies(reach, going, coming, sems, base):

        @pl.when(sent)
        def _(side=side, way=way, copy=copy, more=more):
            value = home[chip + way * reach]
            if reach < chips - 1:

                @pl.when(more)
                def _():
                    going[side, reach - 1] = (
                        value.astype(F32) + coming[side, reach].astype(F32)
                    ).astype(BF16)

                @pl.when(jnp.logical_not(more))
                def _():
                    going[side, reach - 1] = value

            else:
                going[side, reach - 1] = value
            copy.start()


def line_end(copies, home, going, coming, sems, base):
    me = lax.axis_index("fsdp")
    chips = lax.axis_size("fsdp") // 2
    chip = me // 2
    for side, _, copy, _, got, _ in line_copies(1, going, coming, sems, base):

        @pl.when(got)
        def _(side=side, copy=copy):
            copy.wait_recv()
            home[chip] = (home[chip].astype(F32) + coming[side, 0].astype(F32)).astype(BF16)

    for copy in copies:
        copy.wait_send()
    for reach in range(1, chips):
        for _, _, copy, sent, _, _ in line_copies(reach, going, coming, sems, base):
            pl.when(sent)(copy.wait_send)


def remote_call(
    kernel, out_shape, args, collective_id, micros, scratch, in_hbm=(), smem=0, args_in_hbm=0
):
    return pl.pallas_call(
        kernel,
        out_shape=out_shape,
        in_specs=[pl.BlockSpec(memory_space=pltpu.SMEM)] * smem
        + [pl.BlockSpec(memory_space=pltpu.VMEM)] * (len(args) - smem - args_in_hbm)
        + [pl.BlockSpec(memory_space=pl.ANY)] * args_in_hbm,
        out_specs=[
            pl.BlockSpec(memory_space=pl.ANY if item in in_hbm else pltpu.VMEM)
            for item in range(len(out_shape))
        ],
        scratch_shapes=scratch,
        compiler_params=remote_params(collective_id),
        cost_estimate=cost(micros),
    )(*args)


def adam_update(param_now, grad_now, moment_old_one, moment_old_two, step_rate, decay_rate):
    first_new = BETA_ONE * moment_old_one + (1.0 - BETA_ONE) * grad_now
    second_new = BETA_TWO * moment_old_two + (1.0 - BETA_TWO) * grad_now * grad_now
    ratio = (
        first_new
        / (1.0 - BETA_ONE**STEP)
        / (jnp.sqrt(second_new / (1.0 - BETA_TWO**STEP)) + ADAM_EPS)
    )
    return (first_new, second_new, param_now - step_rate * (ratio + decay_rate * param_now))


def adam_kernel(segments, pieces, held, *refs):
    grads = refs[:pieces]
    olds = refs[pieces : pieces + 3]
    news = refs[pieces + 3 + held : pieces + 3 + held + 4]
    grad_buf, old_buf, low_buf, in_sem, out_sem = refs[pieces + 3 + held + 4 :]
    base = min(segment[3] for segment in segments)
    loads = []
    for number, (piece, index, first, column, width) in enumerate(segments):
        here = pl.ds(column - base, width)
        there = pl.ds(column, width)
        copies = [
            pltpu.make_async_copy(
                grads[piece].at[index, :, pl.ds(first, width)],
                grad_buf.at[:, here],
                in_sem.at[3, number],
            )
        ]
        copies += [
            pltpu.make_async_copy(
                olds[item].at[:, there], old_buf.at[item, :, here], in_sem.at[item, number]
            )
            for item in range(3)
        ]
        for copy in copies:
            copy.start()
        loads.append(copies)
    stores = []
    for number, (piece, index, first, column, width) in enumerate(segments):
        for copy in loads[number]:
            copy.wait()
        here = pl.ds(column - base, width)
        there = pl.ds(column, width)
        first_new, second_new, master = adam_update(
            old_buf[0, :, here],
            grad_buf[:, here].astype(F32),
            old_buf[1, :, here],
            old_buf[2, :, here],
            LEARN_RATE,
            WEIGHT_DECAY,
        )
        old_buf[0, :, here] = master
        old_buf[1, :, here] = first_new
        old_buf[2, :, here] = second_new
        low_buf[:, here] = master.astype(BF16)
        for item, source in enumerate(
            (
                old_buf.at[1, :, here],
                old_buf.at[2, :, here],
                old_buf.at[0, :, here],
                low_buf.at[:, here],
            )
        ):
            copy = pltpu.make_async_copy(
                source, news[item].at[:, there], out_sem.at[item, number]
            )
            copy.start()
            stores.append(copy)
    for copy in stores:
        copy.wait()


def adam(segments, grads, olds, held, micros):
    rows, columns = olds[0].shape
    span = max(s[3] + s[4] for s in segments) - min(s[3] for s in segments)
    held = [] if held is None else list(held)
    args = list(grads) + list(olds) + held
    return pl.pallas_call(
        functools.partial(adam_kernel, tuple(segments), len(grads), len(held)),
        out_shape=[jax.ShapeDtypeStruct((rows, columns), F32)] * 3
        + [jax.ShapeDtypeStruct((rows, columns), BF16)],
        in_specs=[pl.BlockSpec(memory_space=pl.ANY)] * len(args),
        out_specs=[pl.BlockSpec(memory_space=pl.ANY)] * 4,
        input_output_aliases={len(grads) + 3 + item: item for item in range(len(held))},
        scratch_shapes=[
            pltpu.VMEM((rows, span), BF16),
            pltpu.VMEM((3, rows, span), F32),
            pltpu.VMEM((rows, span), BF16),
            pltpu.SemaphoreType.DMA((4, len(segments))),
            pltpu.SemaphoreType.DMA((4, len(segments))),
        ],
        compiler_params=pltpu.CompilerParams(vmem_limit_bytes=VMEM_LIMIT),
        cost_estimate=cost(micros),
    )(*args)


def head_mean(values, ones):
    high = values.astype(BF16)
    rest = (values - high.astype(F32)).astype(BF16)
    return (dot(high, ones, 1, 0) + dot(rest, ones, 1, 0)) * (1.0 / HD)


def head_ones(width):
    row = lax.broadcasted_iota(jnp.int32, (width, width), 0) // HD
    col = lax.broadcasted_iota(jnp.int32, (width, width), 1) // HD
    return jnp.where(row == col, 1.0, 0.0).astype(BF16)


def partner(values):
    width = values.shape[-1]
    lane = lax.broadcasted_iota(jnp.int32, values.shape, 1)
    return jnp.where(
        lane % HD < HD // 2,
        pltpu.roll(values, width - HD // 2, 1),
        pltpu.roll(values, HD // 2, 1),
    )


def widen(table, width):
    return [
        jnp.concatenate([part] * (width // HD), axis=-1)
        for part in (table[:, :HD], table[:, HD:])
    ]


def doc_first(starts, times):
    first = jnp.zeros_like(times)
    for item in range(starts.shape[0]):
        first = jnp.where(starts[item] <= times, starts[item], first)
    return first


def block_mask(starts, block, keys):
    shape = (keys, GROUP * HALF)
    times = block * HALF + lax.broadcasted_iota(jnp.int32, (1, GROUP * HALF), 1) % HALF
    key = lax.broadcasted_iota(jnp.int32, shape, 0)
    return (key >= doc_first(starts, times)) & (key <= times)


def stack_heads(ref, rows, group):
    return jnp.concatenate(
        [
            ref[rows, (group * GROUP + h) * HD : (group * GROUP + h + 1) * HD]
            for h in range(GROUP)
        ],
        axis=0,
    )


def unstack_heads(turned):
    wide = turned.T
    return [wide[h * HALF : (h + 1) * HALF, :] for h in range(GROUP)]


def attend_kernel(
    blocks,
    groups,
    place,
    order,
    starts,
    table,
    gain,
    normed_in,
    weights_from,
    dy,
    swap_in,
    part,
    qk,
    q,
    k,
    v,
    o_held,
    lse,
    dy_all,
    swap_out,
    normed,
    weights_in,
    joined,
    o,
    send_sem,
    recv_sem,
    local,
):
    sems = (send_sem, recv_sem)
    me = lax.axis_index("ctx")
    qk_width = qk.shape[1]
    q_width = q.shape[1]
    qkv_width = qk_width + v.shape[1]
    ones = head_ones(qk_width)
    meet(("ctx",))
    loads = [
        load(normed_in, normed, local.at[0]),
        load(weights_from, weights_in, local.at[1]),
    ]
    swap_copies = swap_start(swap_in, swap_out, sems, GATHER_SEMS)
    copies = gather_start(dy, dy_all, sems, 0)
    own_copies = [
        load(swap_in.at[me], swap_out.at[me], local.at[2]),
        load(dy, dy_all.at[me], local.at[3]),
    ]
    for copy in loads:
        copy.wait()
    for block in range(blocks):
        joined[block] = dot(
            normed[block * HALF : (block + 1) * HALF, :], weights_in[:, :qkv_width], 1, 0
        )
    for block in range(blocks):
        to = slice(block * HALF, (block + 1) * HALF)
        values = joined[place[block]]
        v[to, :] = values[:, qk_width:].astype(BF16)
        values = values[:, :qk_width]
        qk[to, :] = values
        turned = values * lax.rsqrt(head_mean(values * values, ones) + NORM_EPS) * gain[...]
        cosine, sine = widen(table[to, :], qk_width)
        turned = turned * cosine + partner(turned) * sine
        turned = turned.astype(BF16)
        q[to, :] = turned[:, :q_width]
        k[to, :] = turned[:, q_width:]
    for block in range(blocks):
        rows = slice(block * HALF, (block + 1) * HALF)
        keys = (block + 1) * HALF
        mask = block_mask(starts, block, keys)
        pieces = []
        for group in range(groups):
            lanes = slice(group * HD, (group + 1) * HD)
            queries = stack_heads(q, rows, group)
            scores = dot(k[:keys, lanes], queries, 1, 1) * SCALE
            weights = jnp.where(mask, jnp.exp(scores), 0.0)
            sums = jnp.sum(weights, axis=0, keepdims=True)
            lse[block, group : group + 1, :] = jnp.log(sums)
            mixed = dot(v[:keys, lanes], weights.astype(BF16), 0, 0) / sums
            pieces += unstack_heads(mixed)
        o[block] = jnp.concatenate(pieces, axis=1).astype(BF16)
    for block in range(blocks):
        o_held[block * HALF : (block + 1) * HALF, :] = o[order[block]]
    for first in range(0, D, 512):
        part[:, first : first + 512] = dot(
            o_held[...], weights_in[first : first + 512, qkv_width:], 1, 1
        ).astype(BF16)
    gather_rest(copies, dy_all, sems, 0)
    for copy in swap_copies:
        copy.wait()
    for copy in own_copies:
        copy.wait()


def tail_kernel(
    blocks,
    groups,
    swaps,
    place,
    order,
    starts,
    lse,
    gain,
    attn_gain,
    ffn_gain_grad,
    out_part,
    *refs,
):
    sources, normed, refs = refs[:11], refs[11], refs[12:]
    swap_in, refs = refs[:swaps], refs[swaps:]
    out, grad_tokens, gains, attn_own = refs[:4]
    swap_out, refs = refs[4 : 4 + swaps], refs[4 + swaps :]
    targets, refs = refs[:11], refs[11:]
    grad_all, weights_in, q, k, v, o, qk, table, middle, x, grad_middle = targets
    size = lax.axis_size("ctx")
    count = 3 if size == 4 else 1
    bufs, back_bufs, refs = refs[:count], refs[count : 2 * count], refs[2 * count :]
    do, dq, dkv, joined, turned, part, attn_grad = refs[:7]
    home, going, coming, owned, ctx_box, fsdp_box = refs[7:13]
    send_one, recv_one, send_two, recv_two, send_three, recv_three = refs[13:19]
    send_four, recv_four, local = refs[19:]
    out_sems, back_sems = (send_one, recv_one), (send_two, recv_two)
    line, small = (send_three, recv_three), (send_four, recv_four)
    me = lax.axis_index("ctx")
    chips = lax.axis_size("fsdp") // 2
    step_base = chips
    swap_base = step_base + 2 * chips
    qk_width = qk.shape[2]
    qkv_width = qk_width + v.shape[1]
    ones = head_ones(qk_width)
    first_load = load(out_part, part, local.at[15])
    meet(("ctx", "fsdp"))
    first_load.wait()
    out_copies = sum_start(part, bufs, out_sems)
    loads = [
        load(source, target, local.at[item])
        for item, (source, target) in enumerate(zip(sources, targets))
    ]
    swap_copies = []
    own_copies = []
    for item in range(swaps):
        swap_copies += swap_start(
            swap_in[item], swap_out[item], line, swap_base + (item + 1) * size
        )
        own_copies.append(
            load(swap_in[item].at[me], swap_out[item].at[me], local.at[13 + item])
        )
    for copy in loads[:6]:
        copy.wait()
    for block in range(blocks):
        do[block * HALF : (block + 1) * HALF, :] = dot(
            grad_all[place[block]], weights_in[:, qkv_width:], 1, 0
        ).astype(BF16)
    for block in range(blocks):
        turned[:, block * HALF : (block + 1) * HALF] = grad_all[block].T
    for first in range(0, D, 512):
        rows = slice(first, first + 512)
        attn_grad[rows, qkv_width:] = dot(turned[rows, :], o[...], 1, 0).astype(BF16)
    loads.append(load(normed, grad_all, local.at[12]))
    dkv[...] = jnp.zeros_like(dkv)
    for block in range(blocks):
        if block == blocks // 2:
            sum_pass(out_copies, part, bufs, out_sems)
        rows = slice(block * HALF, (block + 1) * HALF)
        keys = (block + 1) * HALF
        mask = block_mask(starts, block, keys)
        pieces = []
        dk_add = []
        dv_add = []
        for group in range(groups):
            lanes = slice(group * HD, (group + 1) * HD)
            queries = stack_heads(q, rows, group)
            outs = stack_heads(do, rows, group)
            key_rows = k[:keys, lanes]
            scores = dot(key_rows, queries, 1, 1) * SCALE
            weights = jnp.where(
                mask, jnp.exp(scores - lse[block, group : group + 1, :]), 0.0
            )
            back = dot(v[:keys, lanes], outs, 1, 1)
            delta = jnp.sum(weights * back, axis=0, keepdims=True)
            grads = (weights * (back - delta)).astype(BF16)
            pieces += unstack_heads(dot(key_rows, grads, 0, 0) * SCALE)
            dk_add.append(dot(grads, queries, 1, 0) * SCALE)
            dv_add.append(dot(weights.astype(BF16), outs, 1, 0))
        dq[block] = jnp.concatenate(pieces, axis=1)
        dkv[: block + 1] += jnp.concatenate(dk_add + dv_add, axis=1).reshape(
            (block + 1,) + dkv.shape[1:]
        )
    gain_row = jnp.zeros((1, qk_width), F32)
    for copy in loads[6:]:
        copy.wait()
    for block in range(blocks):
        here = order[block]
        values = qk[here]
        root = lax.rsqrt(head_mean(values * values, ones) + NORM_EPS)
        unit = values * root
        grad_kv = dkv[here]
        kv_width = grad_kv.shape[1] // 2
        grad = jnp.concatenate([dq[here], grad_kv[:, :kv_width]], axis=1)
        cosine, sine = widen(table[here], qk_width)
        grad = grad * cosine - partner(grad) * sine
        gain_row = gain_row + jnp.sum(grad * unit, axis=0, keepdims=True)
        grad = grad * gain[...]
        grad = root * (grad - unit * head_mean(grad * unit, ones))
        joined[block * HALF : (block + 1) * HALF, :] = jnp.concatenate(
            [grad, grad_kv[:, kv_width:]], axis=1
        ).astype(BF16)
    read = sum_rest(out_copies, part, bufs)
    half = middle.shape[0] // 2
    for first in (0, half):
        rows = pl.ds(first, half)
        out[rows, :] = (middle[rows, :] + read(first)).astype(BF16)
    for first in range(0, D, 512):
        part[:, first : first + 512] = dot(
            joined[...], weights_in[first : first + 512, :qkv_width], 1, 1
        ).astype(BF16)
    back_copies = sum_start(part, back_bufs, back_sems)
    for block in range(blocks):
        turned[:, block * HALF : (block + 1) * HALF] = grad_all[block].T
    for first in range(0, D, 512):
        rows = slice(first, first + 512)
        attn_grad[rows, :qkv_width] = dot(turned[rows, :], joined[...], 1, 0).astype(BF16)
    home_copies = line_start(attn_grad, home, line, 0)
    line_home(home_copies, attn_grad, home)
    line_step(chips - 1, home, going, coming, line, step_base)
    sum_pass(back_copies, part, back_bufs, back_sems)
    for reach in range(chips - 2, 0, -1):
        line_step(reach, home, going, coming, line, step_base)
    read = sum_rest(back_copies, part, back_bufs)
    total = jnp.zeros((1, D), F32)
    for first in (0, half):
        rows = pl.ds(first, half)
        values = x[rows, :].astype(F32)
        root = row_scale(values)
        unit = values * root
        back = read(first)
        total = total + jnp.sum(back * unit, axis=0, keepdims=True)
        back = back * attn_gain[...]
        back = root * (back - unit * jnp.mean(back * unit, axis=-1, keepdims=True))
        grad_tokens[rows, :] = grad_middle[rows, :] + back
    line_end(home_copies, home, going, coming, line, step_base)
    chip = lax.axis_index("fsdp") // 2
    owned_rows = owned.shape[1]
    for index in range(size):
        owned[index] = home[chip, index * owned_rows : (index + 1) * owned_rows, :]
    swap_copies += swap_start(owned, attn_own, line, swap_base)
    attn_own[me] = owned[me]
    base = 0
    for axis, box in (("ctx", ctx_box), ("fsdp", fsdp_box)):
        axis_size = lax.axis_size(axis)
        index = lax.axis_index(axis)
        if axis == "ctx":
            box[index] = jnp.concatenate(
                [
                    total,
                    ffn_gain_grad[...],
                    jnp.concatenate([gain_row, jnp.zeros((1, D - qk_width), F32)], axis=1),
                    jnp.zeros((5, D), F32),
                ],
                axis=0,
            )
        else:
            box[index] = summed
        copies = [
            send(
                box.at[index],
                box.at[index],
                small,
                base + step,
                {axis: lax.rem(index + step, axis_size)},
            )
            for step in range(1, axis_size)
        ]
        for copy in copies:
            copy.wait()
        base += axis_size
        summed = box[0]
        for item in range(1, axis_size):
            summed = summed + box[item]
    gains[...] = summed
    for copy in swap_copies:
        copy.wait()
    for copy in own_copies:
        copy.wait()


def rms_scale(values_in, gain_vec):
    return (
        values_in
        * lax.rsqrt(jnp.mean(values_in * values_in, axis=-1, keepdims=True) + NORM_EPS)
        * gain_vec
    )


def inverse_freq():
    return 1.0 / ROPE_BASE ** (jnp.arange(0, HD, 2).astype(F32) / HD)


def shards(
    tokens,
    cotangent,
    doc_starts,
    block_order,
    master_weights,
    moment_one,
    moment_two,
    gains,
    gains_moment_one,
    gains_moment_two,
):
    nctx = lax.axis_size("ctx")
    nfsdp = lax.axis_size("fsdp")
    own_rows = master_weights.shape[0]
    tok_rows = tokens.shape[1]
    stream_len = tok_rows * nctx
    blocks = stream_len // HALF
    groups = KVHEADS // nctx
    q_width = D // nctx
    kv_width = KVD // nctx
    qk_width = q_width + kv_width
    qkv_width = qk_width + kv_width
    tiles = FF // 128
    ff_tiles = -(-tiles // nctx)
    ff_width = ff_tiles * 128
    bundles = 2
    cuts = [0, (ff_tiles * 4 + 6) // 7 * 128, ff_width]

    low = master_weights.astype(BF16)

    def ff_part(base, index, start, stop):
        first = index * ff_width + start
        last = index * ff_width + stop
        real_first, real_last = min(first, FF), min(last, FF)
        part = low[:, base + real_first : base + real_last]
        if real_last - real_first < last - first:
            part = jnp.pad(part, ((0, 0), (0, (last - first) - (real_last - real_first))))
        return part

    def attn_part(index):
        return jnp.concatenate(
            [
                low[:, index * q_width : (index + 1) * q_width],
                low[:, D + index * kv_width : D + (index + 1) * kv_width],
                low[:, D + KVD + index * kv_width : D + KVD + (index + 1) * kv_width],
                low[:, QKVC + index * q_width : QKVC + (index + 1) * q_width],
            ],
            axis=1,
        )

    gate_base = QKVC + D
    bases = (gate_base, gate_base + FF, gate_base + 2 * FF)
    attn_send = jnp.stack([attn_part(c) for c in range(nctx)])
    ff_send = [
        jnp.stack(
            [
                jnp.concatenate(
                    [ff_part(base, c, cuts[b], cuts[b + 1]) for base in bases], axis=1
                )
                for c in range(nctx)
            ]
        )
        for b in range(bundles)
    ]

    def gather_rows(piece):
        return lax.all_gather(
            piece.reshape(nctx * own_rows, piece.shape[-1]), "fsdp", axis=0, tiled=True
        )

    def spread(active):
        return (
            active.reshape(active.shape[0], nctx, nfsdp, own_rows)
            .transpose(0, 2, 1, 3)
            .reshape(active.shape[0], D)
        )

    def unspread(active):
        return (
            active.reshape(active.shape[0], nfsdp, nctx, own_rows)
            .transpose(0, 2, 1, 3)
            .reshape(active.shape[0], D)
        )

    dma = pltpu.SemaphoreType.DMA
    all_low = jax.ShapeDtypeStruct((nctx, tok_rows, D), BF16)
    own_low = jax.ShapeDtypeStruct((tok_rows, D), BF16)
    own_f32 = jax.ShapeDtypeStruct((tok_rows, D), F32)
    row_f32 = jax.ShapeDtypeStruct((1, D), F32)
    g_attn = spread(gains[None, :D])
    g_ffn = spread(gains[None, D : 2 * D])
    order = block_order.reshape(blocks)
    place = jnp.argsort(order).astype(jnp.int32)
    starts = doc_starts[0]

    (attn_held,) = exchange(("swap",), [attn_send], 0, 10)
    w_attn = gather_rows(attn_held)
    first_send, attn_held = lax.optimization_barrier((ff_send[0], attn_held))
    (first_held,) = exchange(("swap",), [first_send], 1, 16)
    table_shape = jax.ShapeDtypeStruct((stream_len, 2 * HD), F32)
    origin = spread(jnp.arange(D, dtype=jnp.int32)[None])
    starts_late, first_held = lax.optimization_barrier((starts, first_held))
    x_low, dy_low, table, normed_all = remote_call(
        first_kernel,
        [own_low, own_low, table_shape, all_low],
        (
            starts_late,
            origin,
            tokens[0],
            cotangent[0],
            g_attn,
            jnp.tile(inverse_freq(), 4)[None],
        ),
        2,
        33,
        [
            pltpu.VMEM((D, D), BF16),
            pltpu.VMEM((tok_rows, D), BF16),
            dma((GATHER_SEMS,)),
            dma((GATHER_SEMS,)),
            dma,
        ],
        (3,),
        1,
    )
    normed_all = normed_all.reshape(stream_len, D)

    g_query = gains[2 * D : 2 * D + HD]
    g_key = gains[2 * D + HD :]
    qk_gain = jnp.concatenate(
        [jnp.tile(g_query, q_width // HD), jnp.tile(g_key, kv_width // HD)]
    )[None]

    low_stream = pltpu.VMEM((stream_len, D), BF16)
    heads_low = pltpu.VMEM((stream_len, q_width), BF16)
    part, qk, q, k, v, mixed, lse, dy_all, second_held = remote_call(
        functools.partial(attend_kernel, blocks, groups),
        [
            jax.ShapeDtypeStruct((stream_len, D), BF16),
            jax.ShapeDtypeStruct((stream_len, qk_width), F32),
            jax.ShapeDtypeStruct((stream_len, q_width), BF16),
            jax.ShapeDtypeStruct((stream_len, kv_width), BF16),
            jax.ShapeDtypeStruct((stream_len, kv_width), BF16),
            jax.ShapeDtypeStruct((stream_len, q_width), BF16),
            jax.ShapeDtypeStruct((blocks, groups, GROUP * HALF), F32),
            all_low,
            jax.ShapeDtypeStruct(ff_send[1].shape, BF16),
        ],
        (place, order, starts, table, qk_gain, normed_all, w_attn, dy_low, ff_send[1]),
        3,
        42,
        [
            low_stream,
            pltpu.VMEM(w_attn.shape, BF16),
            pltpu.VMEM((blocks, HALF, qkv_width), F32),
            pltpu.VMEM((blocks, HALF, q_width), BF16),
            dma((GATHER_SEMS + nctx,)),
            dma((GATHER_SEMS + nctx,)),
            dma((4,)),
        ],
        (7, 8),
        3,
        4,
    )
    dy_all = dy_all.reshape(stream_len, D)
    w_ff = [gather_rows(first_held), gather_rows(second_held)]
    sum_bufs = sum_scratch(nctx, tok_rows)
    sum_sems = [dma((GATHER_SEMS,)), dma((GATHER_SEMS,))]
    norm_scratch = (
        sum_bufs + [pltpu.VMEM((tok_rows, D), BF16)] + sum_sems + sum_sems + [dma]
    )

    middle, normed_two_all = remote_call(
        middle_kernel,
        [own_f32, all_low],
        (part, x_low, g_ffn),
        4,
        57,
        norm_scratch,
        (1,),
    )
    normed_two_all = normed_two_all.reshape(stream_len, D)

    def sum_rows(grad):
        return lax.psum_scatter(grad, "fsdp", scatter_dimension=0, tiled=True).reshape(
            nctx, own_rows, grad.shape[-1]
        )

    def feed(b, x_all, dy):
        width = cuts[b + 1] - cuts[b]
        w_gu, w_down = w_ff[b][:, : 2 * width], w_ff[b][:, 2 * width :]
        gate_up = dot(x_all, w_gu, 1, 0)
        gate, up = gate_up[:, :width], gate_up[:, width:]
        gated = jax.nn.sigmoid(gate)
        act = gate * gated
        hidden = (act * up).astype(BF16)
        back_hidden = dot(dy, w_down, 1, 0)
        grad_gu = jnp.concatenate(
            [back_hidden * up * (gated + act * (1.0 - gated)), back_hidden * act], axis=1
        ).astype(BF16)
        return hidden, grad_gu, dot(hidden, w_down, 1, 1), dot(grad_gu, w_gu, 1, 1)

    hidden, grad_gu, out_partial, back_partial = feed(0, normed_two_all, dy_all)
    out_partial = out_partial.astype(BF16)
    gu_grad = dot(normed_two_all, grad_gu, 0, 0).astype(BF16)
    down_grad = dot(dy_all, hidden, 0, 0).astype(BF16)
    gu_grad, down_grad, back_partial, out_partial, w_ff[1] = lax.optimization_barrier(
        (gu_grad, down_grad, back_partial, out_partial, w_ff[1])
    )
    width_two = cuts[2] - cuts[1]
    hidden, grad_gu, _, back_more = feed(1, normed_two_all, dy_all)
    back_partial = (back_partial + back_more).astype(BF16)
    gu_sum = sum_rows(gu_grad)
    chips = nfsdp // 2

    def line_scratch(columns):
        block = (nctx * own_rows, columns)
        travel = pltpu.VMEM((2, chips - 1) + block, BF16)
        return [pltpu.VMEM((chips,) + block, BF16), travel, travel]

    grad_middle, grad_g_ffn, down_sum, grad_middle_all, last_grad, out_partial = remote_call(
        middle_back_kernel,
        [
            own_f32,
            row_f32,
            jax.ShapeDtypeStruct((nctx, own_rows, cuts[1]), BF16),
            all_low,
            jax.ShapeDtypeStruct((D, 3 * width_two), BF16),
            jax.ShapeDtypeStruct((stream_len, D), BF16),
        ],
        (
            back_partial,
            middle,
            dy_low,
            g_ffn,
            down_grad,
            normed_two_all,
            dy_all,
            grad_gu,
            hidden,
            w_ff[1][:, 2 * width_two :],
            out_partial,
        ),
        5,
        57,
        sum_bufs
        + [
            pltpu.VMEM((tok_rows, D), BF16),
            low_stream,
            pltpu.VMEM((stream_len, 2 * width_two), BF16),
            pltpu.VMEM((stream_len, width_two), BF16),
            pltpu.VMEM((D, width_two), BF16),
            low_stream,
            pltpu.VMEM((D, stream_len), BF16),
            pltpu.VMEM((D, 3 * width_two), BF16),
        ]
        + line_scratch(cuts[1])
        + sum_sems
        + sum_sems
        + [dma((3 * chips,)), dma((3 * chips,)), dma((9,))],
        (3, 4, 5),
        0,
        6,
    )
    last_sum = sum_rows(last_grad)

    small = dma((nctx + nfsdp,))
    line_sems = dma((3 * chips + 3 * nctx,))
    own_shape = (nctx, own_rows, qkv_width + q_width)
    sources = (
        grad_middle_all.reshape(blocks, HALF, D),
        w_attn,
        q,
        k,
        v,
        mixed,
        qk.reshape(blocks, HALF, qk_width),
        table.reshape(blocks, HALF, 2 * HD),
        middle,
        x_low,
        grad_middle,
    )
    out_tokens, grad_tokens, gain_sums, attn_own, gu_own, down_own = remote_call(
        functools.partial(tail_kernel, blocks, groups, 2),
        [
            own_low,
            own_f32,
            jax.ShapeDtypeStruct((8, D), F32),
            jax.ShapeDtypeStruct(own_shape, BF16),
            jax.ShapeDtypeStruct(gu_sum.shape, BF16),
            jax.ShapeDtypeStruct(down_sum.shape, BF16),
        ],
        (place, order, starts, lse, qk_gain, g_attn, grad_g_ffn, out_partial)
        + sources
        + (normed_all.reshape(blocks, HALF, D), gu_sum, down_sum),
        6,
        90,
        [pltpu.VMEM(source.shape, source.dtype) for source in sources]
        + sum_bufs
        + sum_bufs
        + [
            heads_low,
            pltpu.VMEM((blocks, HALF, q_width), F32),
            pltpu.VMEM((blocks, HALF, 2 * kv_width), F32),
            pltpu.VMEM((stream_len, qkv_width), BF16),
            pltpu.VMEM((D, stream_len), BF16),
            low_stream,
            pltpu.VMEM((D, qkv_width + q_width), BF16),
        ]
        + line_scratch(qkv_width + q_width)
        + [
            pltpu.VMEM(own_shape, BF16),
            pltpu.VMEM((nctx, 8, D), F32),
            pltpu.VMEM((nfsdp, 8, D), F32),
        ]
        + sum_sems
        + sum_sems
        + [line_sems, line_sems, small, small, dma((16,))],
        (4, 5),
        3,
        15,
    )
    out_tokens = unspread(out_tokens)[None]
    grad_tokens = unspread(grad_tokens)[None]
    gain_grad = jnp.concatenate(
        [
            unspread(gain_sums[:1])[0],
            unspread(gain_sums[1:2])[0],
            jnp.sum(gain_sums[2, :q_width].reshape(-1, HD), axis=0),
            jnp.sum(gain_sums[2, q_width:qk_width].reshape(-1, HD), axis=0),
        ]
    )

    olds = (master_weights, moment_one, moment_two)

    def feed_segments(b, pieces):
        width = cuts[b + 1] - cuts[b]
        found = []
        for part in range(3):
            for c in range(nctx):
                column = c * ff_width + cuts[b]
                real = min(max(FF - column, 0), width)
                if real:
                    piece, first = pieces[part]
                    found.append((piece, c, first, bases[part] + column, real))
        return found

    width_one = cuts[1]
    news = adam(
        feed_segments(0, ((0, 0), (0, width_one), (1, 0))), [gu_own, down_own], olds, None, 7
    )
    parts = (
        (0, 0, q_width),
        (q_width, D, kv_width),
        (qk_width, D + KVD, kv_width),
        (qkv_width, QKVC, q_width),
    )
    if kv_width % 128:
        attn_own = jnp.concatenate(
            [attn_own[c, :, f : f + w] for f, _, w in parts for c in range(nctx)], axis=1
        )[None]
        segments = [(0, 0, 0, 0, gate_base)]
    else:
        segments = [
            (0, c, first, base + c * width, width)
            for first, base, width in parts
            for c in range(nctx)
        ]
    news = adam(segments, [attn_own], olds, news, 3)
    (last_own,) = exchange(("swap",), [last_sum], 8, 12)
    first_new, second_new, master_new, low_new = adam(
        feed_segments(1, ((0, 0), (0, width_two), (0, 2 * width_two))),
        [last_own],
        olds,
        news,
        6,
    )
    gain_first, gain_second, gain_new = adam_update(
        gains, gain_grad, gains_moment_one, gains_moment_two, GAIN_RATE, 0.0
    )
    return (
        out_tokens,
        grad_tokens,
        first_new,
        second_new,
        master_new,
        low_new,
        gain_first,
        gain_second,
        gain_new,
    )


def solution(mesh):
    rows = P("fsdp", "ctx", None)
    weights = P(("ctx", "fsdp"), None)
    return jax.shard_map(
        shards,
        mesh=mesh,
        in_specs=(rows, rows, P("fsdp", None), P(), weights, weights, weights, P(), P(), P()),
        out_specs=(rows, rows, weights, weights, weights, weights, P(), P(), P()),
        check_vma=False,
    )
```

```python
import functools

import jax
import jax.numpy as jnp
from jax import lax
from jax.experimental import pallas as pl
from jax.experimental.pallas import tpu as pltpu
from jax.sharding import PartitionSpec as P

D = 1536
HEADS = 24
KVHEADS = 8
HD = 64
FF = 6912
STEP = 10
HALF = 128
KVD = 512
QKVC = 2560
GROUP = HEADS // KVHEADS

ROPE_BASE = 1000000.0
NORM_EPS = 1e-05
BETA_ONE = 0.9
BETA_TWO = 0.95
ADAM_EPS = 1e-08
WEIGHT_DECAY = 0.1
LEARN_RATE = 0.03
GAIN_RATE = 0.5
SCALE = HD ** (-0.5)
MESH = pl.DeviceIdType.MESH
F32 = jnp.float32
BF16 = jnp.bfloat16
VMEM_LIMIT = 60 * 1024 * 1024


def dot(left, right, left_dim, right_dim):
    return lax.dot_general(
        left, right, (((left_dim,), (right_dim,)), ((), ())), preferred_element_type=F32
    )


def send(source, target, sems, item, peer):
    copy = pltpu.make_async_remote_copy(
        src_ref=source,
        dst_ref=target,
        send_sem=sems[0].at[item],
        recv_sem=sems[1].at[item],
        device_id=peer,
        device_id_type=MESH,
    )
    copy.start()
    return copy


def meet(axes):
    barrier = pltpu.get_barrier_semaphore()
    total = 0
    for axis in axes:
        size = lax.axis_size(axis)
        me = lax.axis_index(axis)
        for step in range(1, size):
            pl.semaphore_signal(
                barrier,
                inc=1,
                device_id={axis: lax.rem(me + step, size)},
                device_id_type=MESH,
            )
        total += size - 1
    pl.semaphore_wait(barrier, total)


def square():
    me = lax.axis_index("ctx")
    return me, me + 1 - 2 * lax.rem(me, 2), lax.rem(me + 2, 4), 3 - me


def swap_start(source, target, sems, base):
    size = lax.axis_size("ctx")
    me = lax.axis_index("ctx")
    copies = []
    for step in range(1, size):
        peer = lax.rem(me + step, size)
        copies.append(
            send(source.at[peer], target.at[me], sems, base + step, {"ctx": peer})
        )
    return copies


def gather_start(source, target, sems, base):
    size = lax.axis_size("ctx")
    me = lax.axis_index("ctx")
    if size != 4:
        return [
            send(
                source,
                target.at[me],
                sems,
                base + step,
                {"ctx": lax.rem(me + step, size)},
            )
            for step in range(1, size)
        ]
    me, side, over, across = square()
    half = source.shape[0] // 2
    top, low = pl.ds(0, half), pl.ds(half, half)
    return [
        send(source.at[top], target.at[me, top], sems, base, {"ctx": side}),
        send(source.at[low], target.at[me, low], sems, base + 1, {"ctx": over}),
        send(source.at[low], target.at[me, low], sems, base + 2, {"ctx": side}),
        send(source.at[top], target.at[me, top], sems, base + 3, {"ctx": over}),
    ]


def gather_pass(copies, target, sems, base):
    if lax.axis_size("ctx") != 4:
        return
    me, side, over, across = square()
    half = target.shape[1] // 2
    top, low = pl.ds(0, half), pl.ds(half, half)
    copies[0].wait_recv()
    copies.append(send(target.at[side, top], target.at[side, top], sems, base + 4, {"ctx": over}))
    copies[1].wait_recv()
    copies.append(send(target.at[over, low], target.at[over, low], sems, base + 5, {"ctx": side}))


def gather_end(copies):
    if lax.axis_size("ctx") != 4:
        for copy in copies:
            copy.wait()
        return
    for copy in copies:
        copy.wait_send()
    for copy in copies[2:]:
        copy.wait_recv()


def gather_rest(copies, target, sems, base):
    gather_pass(copies, target, sems, base)
    gather_end(copies)


def load(source, target, sem):
    copy = pltpu.make_async_copy(source, target, sem)
    copy.start()
    return copy


GATHER_SEMS = 8


def exchange_kernel(kinds, *refs):
    count = len(kinds)
    ins, outs = refs[:count], refs[count : 2 * count]
    send_sem, recv_sem, local_sem = refs[2 * count :]
    sems = (send_sem, recv_sem)
    me = lax.axis_index("ctx")
    meet(("ctx",))
    copies = []
    own = []
    for item in range(count):
        base = item * GATHER_SEMS
        if kinds[item] == "gather":
            copies.append(gather_start(ins[item], outs[item], sems, base))
            source = ins[item]
        else:
            copies.append(swap_start(ins[item], outs[item], sems, base))
            source = ins[item].at[me]
        copy = pltpu.make_async_copy(source, outs[item].at[me], local_sem.at[item])
        copy.start()
        own.append(copy)
    for item in range(count):
        if kinds[item] == "gather":
            gather_rest(copies[item], outs[item], sems, item * GATHER_SEMS)
        else:
            for copy in copies[item]:
                copy.wait()
    for copy in own:
        copy.wait()


def remote_params(collective_id):
    return pltpu.CompilerParams(
        collective_id=collective_id, has_side_effects=True, vmem_limit_bytes=VMEM_LIMIT
    )


def cost(micros):
    return pl.CostEstimate(flops=0, bytes_accessed=int(micros * 3.0e6), transcendentals=0)


def exchange(kinds, arrays, collective_id, micros):
    size = lax.axis_size("ctx")
    shapes = [
        jax.ShapeDtypeStruct((size,) + a.shape if kind == "gather" else a.shape, a.dtype)
        for kind, a in zip(kinds, arrays)
    ]
    sems = pltpu.SemaphoreType.DMA((len(arrays) * GATHER_SEMS,))
    return pl.pallas_call(
        functools.partial(exchange_kernel, kinds),
        out_shape=shapes,
        in_specs=[pl.BlockSpec(memory_space=pl.ANY)] * len(arrays),
        out_specs=[pl.BlockSpec(memory_space=pl.ANY)] * len(arrays),
        scratch_shapes=[sems, sems, pltpu.SemaphoreType.DMA((len(arrays),))],
        compiler_params=remote_params(collective_id),
        cost_estimate=cost(micros),
    )(*arrays)


def sum_scratch(size, rows):
    if size == 4:
        half = pltpu.VMEM((2, rows // 2, D), BF16)
        return [half, half, pltpu.VMEM((2, rows, D), BF16)]
    return [pltpu.VMEM((size - 1, rows, D), BF16)]


def sum_start(part, bufs, sems):
    size = lax.axis_size("ctx")
    me = lax.axis_index("ctx")
    rows = part.shape[0] // size

    def block(owner, first=0, count=rows):
        return pl.ds(pl.multiple_of(owner * rows + first, rows // 2), count)

    if size != 4:
        copies = []
        for step in range(1, size):
            peer = lax.rem(me + step, size)
            copies.append(
                send(part.at[block(peer)], bufs[0].at[step - 1], sems, step, {"ctx": peer})
            )
        return copies
    me, side, over, across = square()
    half = rows // 2
    relay, _, landed = bufs
    return [
        send(part.at[block(across, 0, half)], relay.at[0], sems, 0, {"ctx": side}),
        send(part.at[block(across, half, half)], relay.at[1], sems, 1, {"ctx": over}),
        send(
            part.at[block(side, 0, half)],
            landed.at[0, pl.ds(0, half)],
            sems,
            2,
            {"ctx": side},
        ),
        send(
            part.at[block(over, half, half)],
            landed.at[1, pl.ds(half, half)],
            sems,
            3,
            {"ctx": over},
        ),
    ]


def sum_pass(copies, part, bufs, sems):
    if lax.axis_size("ctx") != 4:
        return
    rows = part.shape[0] // 4
    half = rows // 2

    def rows_of(owner, first):
        return pl.ds(pl.multiple_of(owner * rows + first, half), half)

    me, side, over, across = square()
    relay, passed, landed = bufs
    copies[0].wait_recv()
    passed[0] = (part[rows_of(over, 0), :].astype(F32) + relay[0].astype(F32)).astype(BF16)
    copies.append(
        send(passed.at[0], landed.at[1, pl.ds(0, half)], sems, 4, {"ctx": over})
    )
    copies[1].wait_recv()
    passed[1] = (part[rows_of(side, half), :].astype(F32) + relay[1].astype(F32)).astype(
        BF16
    )
    copies.append(
        send(passed.at[1], landed.at[0, pl.ds(half, half)], sems, 5, {"ctx": side})
    )


def sum_rest(copies, part, bufs):
    size = lax.axis_size("ctx")
    me = lax.axis_index("ctx")
    rows = part.shape[0] // size
    half = rows // 2

    def rows_of(owner, first):
        return pl.ds(pl.multiple_of(owner * rows + first, half), half)

    if size != 4:
        for copy in copies:
            copy.wait()

        def read(first):
            total = part[rows_of(me, first), :].astype(F32)
            for step in range(1, size):
                total = total + bufs[0][step - 1, pl.ds(first, half), :].astype(F32)
            return total

        return read
    relay, passed, landed = bufs
    for copy in copies:
        copy.wait_send()
    for copy in copies[2:]:
        copy.wait_recv()

    def read(first):
        return (
            part[rows_of(me, first), :].astype(F32)
            + landed[0, pl.ds(first, half), :].astype(F32)
            + landed[1, pl.ds(first, half), :].astype(F32)
        )

    return read


def row_scale(values):
    return lax.rsqrt(jnp.mean(values * values, axis=-1, keepdims=True) + NORM_EPS)


def first_kernel(
    starts, origin, x, dy, gain, freq, x_low, dy_low, table, normed_all, *scratch
):
    move, normed, send_one, recv_one, local = scratch
    me = lax.axis_index("ctx")
    row = lax.broadcasted_iota(jnp.int32, move.shape, 0)
    move[...] = jnp.where(row == origin[...], 1.0, 0.0).astype(BF16)
    values = dot(x[...], move[...], 1, 0)
    x_low[...] = values.astype(BF16)
    normed[...] = (values * row_scale(values) * gain[...]).astype(BF16)
    meet(("ctx",))
    sems = (send_one, recv_one)
    copies = gather_start(normed, normed_all, sems, 0)
    own = load(normed, normed_all.at[me], local)
    dy_low[...] = dot(dy[...], move[...], 1, 0).astype(BF16)
    gather_pass(copies, normed_all, sems, 0)
    times = lax.broadcasted_iota(jnp.int32, (table.shape[0], 1), 0)
    angles = (times - doc_first(starts, times)).astype(F32) * freq[...]
    lane = lax.broadcasted_iota(jnp.int32, angles.shape, 1)
    sine = jnp.sin(angles)
    sine = jnp.where(lane % HD < HD // 2, -sine, sine)
    table[...] = jnp.where(lane < HD, jnp.cos(angles), sine)
    gather_end(copies)
    own.wait()


def middle_kernel(part, x, gain, middle, normed_all, *scratch):
    bufs, (normed, send_one, recv_one, send_two, recv_two, local) = scratch[:-6], scratch[-6:]
    me = lax.axis_index("ctx")
    meet(("ctx",))
    copies = sum_start(part, bufs, (send_one, recv_one))
    sum_pass(copies, part, bufs, (send_one, recv_one))
    read = sum_rest(copies, part, bufs)
    half = x.shape[0] // 2
    for first in (0, half):
        rows = pl.ds(first, half)
        values = x[rows, :].astype(F32) + read(first)
        middle[rows, :] = values
        normed[rows, :] = (values * row_scale(values) * gain[...]).astype(BF16)
    sems = (send_two, recv_two)
    copies = gather_start(normed, normed_all, sems, 0)
    own = load(normed, normed_all.at[me], local)
    gather_rest(copies, normed_all, sems, 0)
    own.wait()


def column_tiles(total, body):
    def step(tile, carry):
        body(pl.multiple_of(tile * 256, 256), 256)
        return carry

    lax.fori_loop(0, total // 256, step, 0)
    if total % 256:
        body(total - total % 256, total % 256)


def turn(source, target):
    for first in range(0, source.shape[0], HALF):
        rows = slice(first, first + HALF)
        target[:, rows] = source[rows, :].T


def middle_back_kernel(
    part,
    middle,
    dy,
    gain,
    x_all,
    dy_all,
    hidden_one,
    hidden_two,
    grad_gu,
    w_one,
    w_two,
    grad,
    gain_grad,
    down_sum,
    grad_all,
    weight_grad,
    out,
    *scratch,
):
    bufs = scratch[:-20]
    low, x_buf, gu_buf, turned, weight_buf, down_grad, out_buf = scratch[-20:-13]
    hidden_bufs, down_bufs = scratch[-13:-11], scratch[-11:-9]
    home, travel, send_one, recv_one, send_two, recv_two, send_three, recv_three, local = (
        scratch[-9:]
    )
    going, coming = travel.at[0], travel.at[1]
    me = lax.axis_index("ctx")
    chips = lax.axis_size("fsdp") // 2
    line = (send_three, recv_three)
    meet(("ctx", "fsdp"))
    copies = sum_start(part, bufs, (send_one, recv_one))
    width_one, width_two = hidden_one.shape[1], hidden_two.shape[1]
    gu_width = grad_gu.shape[1]
    loads = [
        load(source, target, local.at[item])
        for item, (source, target) in enumerate(
            (
                (dy_all, x_buf),
                (hidden_one, hidden_bufs[0]),
                (hidden_two, hidden_bufs[1]),
                (grad_gu, gu_buf),
                (w_one.at[:, pl.ds(2 * width_one, width_one)], down_bufs[0]),
                (w_two.at[:, pl.ds(2 * width_two, width_two)], down_bufs[1]),
            )
        )
    ]
    loads[0].wait()
    turn(x_buf, turned)
    loads.append(load(x_all, x_buf, local.at[6]))
    loads[1].wait()

    def product(target, column, right):
        def tile(first, width):
            target[:, pl.ds(column + first, width)] = dot(
                turned[...], right[:, pl.ds(first, width)], 1, 0
            ).astype(BF16)

        column_tiles(right.shape[1], tile)

    product(down_grad, 0, hidden_bufs[0])
    home_copies = line_start(down_grad, home, line, 0)
    sum_pass(copies, part, bufs, (send_one, recv_one))
    loads[2].wait()
    product(weight_buf, gu_width, hidden_bufs[1])
    line_home(home_copies, down_grad, home)
    line_step(chips - 1, home, going, coming, line, chips)
    loads[6].wait()
    turn(x_buf, turned)
    loads[3].wait()
    product(weight_buf, 0, gu_buf)
    stores = [load(weight_buf, weight_grad, local.at[7])]
    read = sum_rest(copies, part, bufs)
    half = dy.shape[0] // 2
    total = jnp.zeros((1, D), F32)
    for first in (0, half):
        rows = pl.ds(first, half)
        values = middle[rows, :]
        root = row_scale(values)
        unit = values * root
        back = read(first)
        total = total + jnp.sum(back * unit, axis=0, keepdims=True)
        back = back * gain[...]
        back = root * (back - unit * jnp.mean(back * unit, axis=-1, keepdims=True))
        back = back + dy[rows, :].astype(F32)
        grad[rows, :] = back
        low[rows, :] = back.astype(BF16)
    gain_grad[...] = total
    sems = (send_two, recv_two)
    copies = gather_start(low, grad_all, sems, 0)
    stores.append(load(low, grad_all.at[me], local.at[8]))
    if chips > 2:
        line_step(chips - 2, home, going, coming, line, chips)
    loads[4].wait()
    loads[5].wait()

    def out_tile(first, width):
        columns = pl.ds(first, width)
        out_buf[:, columns] = (
            dot(hidden_bufs[0][...], down_bufs[0][columns, :], 1, 1)
            + dot(hidden_bufs[1][...], down_bufs[1][columns, :], 1, 1)
        ).astype(BF16)

    column_tiles(D, out_tile)
    stores.append(load(out_buf, out, local.at[9]))
    gather_pass(copies, grad_all, sems, 0)
    for reach in range(min(chips - 1, max(chips - 3, 1)), 0, -1):
        line_step(reach, home, going, coming, line, chips)
    gather_end(copies)
    line_end(home_copies, home, going, coming, line, chips)
    chip = lax.axis_index("fsdp") // 2
    rows = down_sum.shape[1]
    for index in range(down_sum.shape[0]):
        down_sum[index] = home[chip, index * rows : (index + 1) * rows, :]
    for copy in stores:
        copy.wait()


def line_start(grad, home, sems, base):
    me = lax.axis_index("fsdp")
    chips = lax.axis_size("fsdp") // 2
    core = lax.rem(me, 2)
    rows = grad.shape[0] // (2 * chips)
    copies = []
    for chip in range(chips):
        theirs = pl.ds(pl.multiple_of((2 * chip + 1 - core) * rows, rows), rows)
        copies.append(
            send(grad.at[theirs], home.at[chip], sems, base + chip, {"fsdp": me + 1 - 2 * core})
        )
    return copies


def line_home(copies, grad, home):
    me = lax.axis_index("fsdp")
    chips = lax.axis_size("fsdp") // 2
    core = lax.rem(me, 2)
    rows = grad.shape[0] // (2 * chips)
    for chip in range(chips):
        copies[chip].wait_recv()
        mine = pl.ds(pl.multiple_of((2 * chip + core) * rows, rows), rows)
        home[chip] = (home[chip].astype(F32) + grad[mine, :].astype(F32)).astype(BF16)


def line_copies(reach, going, coming, sems, base):
    me = lax.axis_index("fsdp")
    chips = lax.axis_size("fsdp") // 2
    chip = me // 2
    found = []
    for side, way in ((0, 1), (1, -1)):
        copy = pltpu.make_async_remote_copy(
            src_ref=going.at[side, reach - 1],
            dst_ref=coming.at[side, reach - 1],
            send_sem=sems[0].at[base + 2 * reach + side],
            recv_sem=sems[1].at[base + 2 * reach + side],
            device_id={"fsdp": lax.rem(me + 2 * way + 2 * chips, 2 * chips)},
            device_id_type=MESH,
        )
        if way == 1:
            sent = chip + reach <= chips - 1
            got = (chip >= 1) & (chip + reach <= chips)
            more = (chip >= 1) & sent
        else:
            sent = chip >= reach
            got = (chip <= chips - 2) & (chip + 1 >= reach)
            more = (chip <= chips - 2) & sent
        found.append((side, way, copy, sent, got, more))
    return found


def line_step(reach, home, going, coming, sems, base):
    me = lax.axis_index("fsdp")
    chips = lax.axis_size("fsdp") // 2
    chip = me // 2
    if reach < chips - 1:
        for _, _, copy, _, got, _ in line_copies(reach + 1, going, coming, sems, base):
            pl.when(got)(copy.wait_recv)
    for side, way, copy, sent, _, more in line_copies(reach, going, coming, sems, base):

        @pl.when(sent)
        def _(side=side, way=way, copy=copy, more=more):
            value = home[chip + way * reach]
            if reach < chips - 1:

                @pl.when(more)
                def _():
                    going[side, reach - 1] = (
                        value.astype(F32) + coming[side, reach].astype(F32)
                    ).astype(BF16)

                @pl.when(jnp.logical_not(more))
                def _():
                    going[side, reach - 1] = value

            else:
                going[side, reach - 1] = value
            copy.start()


def line_end(copies, home, going, coming, sems, base):
    me = lax.axis_index("fsdp")
    chips = lax.axis_size("fsdp") // 2
    chip = me // 2
    for side, _, copy, _, got, _ in line_copies(1, going, coming, sems, base):

        @pl.when(got)
        def _(side=side, copy=copy):
            copy.wait_recv()
            home[chip] = (home[chip].astype(F32) + coming[side, 0].astype(F32)).astype(BF16)

    for copy in copies:
        copy.wait_send()
    for reach in range(1, chips):
        for _, _, copy, sent, _, _ in line_copies(reach, going, coming, sems, base):
            pl.when(sent)(copy.wait_send)


def remote_call(
    kernel, out_shape, args, collective_id, micros, scratch, in_hbm=(), smem=0, args_in_hbm=0
):
    return pl.pallas_call(
        kernel,
        out_shape=out_shape,
        in_specs=[pl.BlockSpec(memory_space=pltpu.SMEM)] * smem
        + [pl.BlockSpec(memory_space=pltpu.VMEM)] * (len(args) - smem - args_in_hbm)
        + [pl.BlockSpec(memory_space=pl.ANY)] * args_in_hbm,
        out_specs=[
            pl.BlockSpec(memory_space=pl.ANY if item in in_hbm else pltpu.VMEM)
            for item in range(len(out_shape))
        ],
        scratch_shapes=scratch,
        compiler_params=remote_params(collective_id),
        cost_estimate=cost(micros),
    )(*args)


def adam_update(param_now, grad_now, moment_old_one, moment_old_two, step_rate, decay_rate):
    first_new = BETA_ONE * moment_old_one + (1.0 - BETA_ONE) * grad_now
    second_new = BETA_TWO * moment_old_two + (1.0 - BETA_TWO) * grad_now * grad_now
    ratio = (
        first_new
        / (1.0 - BETA_ONE**STEP)
        / (jnp.sqrt(second_new / (1.0 - BETA_TWO**STEP)) + ADAM_EPS)
    )
    return (first_new, second_new, param_now - step_rate * (ratio + decay_rate * param_now))


def adam_kernel(segments, pieces, held, *refs):
    me = lax.axis_index("ctx")
    grads = refs[:pieces]
    olds = refs[pieces : pieces + 3]
    news = refs[pieces + 3 + held : pieces + 3 + held + 4]
    grad_buf, old_buf, low_buf, in_sem, out_sem = refs[pieces + 3 + held + 4 :]
    base = min(segment[3] for segment in segments)
    loads = []
    for number, (piece, index, first, column, width) in enumerate(segments):
        here = pl.ds(column - base, width)
        there = pl.ds(column, width)
        columns = pl.ds(first, width)
        copies = []
        for number_from, source in enumerate(grads):
            if piece not in (None, number_from):
                continue
            copy = pltpu.make_async_copy(
                source.at[:, columns] if piece is None else source.at[index, :, columns],
                grad_buf.at[:, here],
                in_sem.at[3, number],
            )
            if piece is None:
                pl.when(me == index ^ number_from)(copy.start)
            else:
                copy.start()
        loads.append([copy])
        copies += [
            pltpu.make_async_copy(
                olds[item].at[:, there], old_buf.at[item, :, here], in_sem.at[item, number]
            )
            for item in range(3)
        ]
        for copy in copies:
            copy.start()
        loads[-1] += copies
    stores = []
    for number, (piece, index, first, column, width) in enumerate(segments):
        for copy in loads[number]:
            copy.wait()
        here = pl.ds(column - base, width)
        there = pl.ds(column, width)
        first_new, second_new, master = adam_update(
            old_buf[0, :, here],
            grad_buf[:, here].astype(F32),
            old_buf[1, :, here],
            old_buf[2, :, here],
            LEARN_RATE,
            WEIGHT_DECAY,
        )
        old_buf[0, :, here] = master
        old_buf[1, :, here] = first_new
        old_buf[2, :, here] = second_new
        low_buf[:, here] = master.astype(BF16)
        for item, source in enumerate(
            (
                old_buf.at[1, :, here],
                old_buf.at[2, :, here],
                old_buf.at[0, :, here],
                low_buf.at[:, here],
            )
        ):
            copy = pltpu.make_async_copy(
                source, news[item].at[:, there], out_sem.at[item, number]
            )
            copy.start()
            stores.append(copy)
    for copy in stores:
        copy.wait()


def adam(segments, grads, olds, held, micros):
    rows, columns = olds[0].shape
    span = max(s[3] + s[4] for s in segments) - min(s[3] for s in segments)
    held = [] if held is None else list(held)
    args = list(grads) + list(olds) + held
    return pl.pallas_call(
        functools.partial(adam_kernel, tuple(segments), len(grads), len(held)),
        out_shape=[jax.ShapeDtypeStruct((rows, columns), F32)] * 3
        + [jax.ShapeDtypeStruct((rows, columns), BF16)],
        in_specs=[pl.BlockSpec(memory_space=pl.ANY)] * len(args),
        out_specs=[pl.BlockSpec(memory_space=pl.ANY)] * 4,
        input_output_aliases={len(grads) + 3 + item: item for item in range(len(held))},
        scratch_shapes=[
            pltpu.VMEM((rows, span), BF16),
            pltpu.VMEM((3, rows, span), F32),
            pltpu.VMEM((rows, span), BF16),
            pltpu.SemaphoreType.DMA((4, len(segments))),
            pltpu.SemaphoreType.DMA((4, len(segments))),
        ],
        compiler_params=pltpu.CompilerParams(vmem_limit_bytes=VMEM_LIMIT),
        cost_estimate=cost(micros),
    )(*args)


def head_mean(values, ones):
    high = values.astype(BF16)
    rest = (values - high.astype(F32)).astype(BF16)
    return (dot(high, ones, 1, 0) + dot(rest, ones, 1, 0)) * (1.0 / HD)


def head_ones(width):
    row = lax.broadcasted_iota(jnp.int32, (width, width), 0) // HD
    col = lax.broadcasted_iota(jnp.int32, (width, width), 1) // HD
    return jnp.where(row == col, 1.0, 0.0).astype(BF16)


def partner(values):
    width = values.shape[-1]
    lane = lax.broadcasted_iota(jnp.int32, values.shape, 1)
    return jnp.where(
        lane % HD < HD // 2,
        pltpu.roll(values, width - HD // 2, 1),
        pltpu.roll(values, HD // 2, 1),
    )


def widen(table, width):
    return [
        jnp.concatenate([part] * (width // HD), axis=-1)
        for part in (table[:, :HD], table[:, HD:])
    ]


def doc_first(starts, times):
    first = jnp.zeros_like(times)
    for item in range(starts.shape[0]):
        first = jnp.where(starts[item] <= times, starts[item], first)
    return first


def block_mask(starts, block, keys):
    shape = (keys, GROUP * HALF)
    times = block * HALF + lax.broadcasted_iota(jnp.int32, (1, GROUP * HALF), 1) % HALF
    key = lax.broadcasted_iota(jnp.int32, shape, 0)
    return (key >= doc_first(starts, times)) & (key <= times)


def stack_heads(ref, rows, group):
    return jnp.concatenate(
        [
            ref[rows, (group * GROUP + h) * HD : (group * GROUP + h + 1) * HD]
            for h in range(GROUP)
        ],
        axis=0,
    )


def unstack_heads(turned):
    wide = turned.T
    return [wide[h * HALF : (h + 1) * HALF, :] for h in range(GROUP)]


def attend_kernel(
    blocks,
    groups,
    place,
    order,
    starts,
    table,
    gain,
    normed_in,
    weights_from,
    dy,
    swap_in,
    part,
    qk,
    q,
    k,
    v,
    o_held,
    lse,
    dy_all,
    swap_out,
    normed,
    weights_in,
    joined,
    o,
    send_sem,
    recv_sem,
    local,
):
    sems = (send_sem, recv_sem)
    me = lax.axis_index("ctx")
    qk_width = qk.shape[1]
    q_width = q.shape[1]
    qkv_width = qk_width + v.shape[1]
    ones = head_ones(qk_width)
    meet(("ctx",))
    loads = [
        load(normed_in, normed, local.at[0]),
        load(weights_from, weights_in, local.at[1]),
    ]
    swap_copies = swap_start(swap_in, swap_out, sems, GATHER_SEMS)
    copies = gather_start(dy, dy_all, sems, 0)
    own_copies = [
        load(swap_in.at[me], swap_out.at[me], local.at[2]),
        load(dy, dy_all.at[me], local.at[3]),
    ]
    for copy in loads:
        copy.wait()
    for block in range(blocks):
        joined[block] = dot(
            normed[block * HALF : (block + 1) * HALF, :], weights_in[:, :qkv_width], 1, 0
        )
    for block in range(blocks):
        to = slice(block * HALF, (block + 1) * HALF)
        values = joined[place[block]]
        v[to, :] = values[:, qk_width:].astype(BF16)
        values = values[:, :qk_width]
        qk[to, :] = values
        turned = values * lax.rsqrt(head_mean(values * values, ones) + NORM_EPS) * gain[...]
        cosine, sine = widen(table[to, :], qk_width)
        turned = turned * cosine + partner(turned) * sine
        turned = turned.astype(BF16)
        q[to, :] = turned[:, :q_width]
        k[to, :] = turned[:, q_width:]
    for block in range(blocks):
        rows = slice(block * HALF, (block + 1) * HALF)
        keys = (block + 1) * HALF
        mask = block_mask(starts, block, keys)
        pieces = []
        for group in range(groups):
            lanes = slice(group * HD, (group + 1) * HD)
            queries = stack_heads(q, rows, group)
            scores = dot(k[:keys, lanes], queries, 1, 1) * SCALE
            weights = jnp.where(mask, jnp.exp(scores), 0.0)
            sums = jnp.sum(weights, axis=0, keepdims=True)
            lse[block, group : group + 1, :] = jnp.log(sums)
            mixed = dot(v[:keys, lanes], weights.astype(BF16), 0, 0) / sums
            pieces += unstack_heads(mixed)
        o[block] = jnp.concatenate(pieces, axis=1).astype(BF16)
    for block in range(blocks):
        o_held[block * HALF : (block + 1) * HALF, :] = o[order[block]]
    for first in range(0, D, 512):
        part[:, first : first + 512] = dot(
            o_held[...], weights_in[first : first + 512, qkv_width:], 1, 1
        ).astype(BF16)
    gather_rest(copies, dy_all, sems, 0)
    for copy in swap_copies:
        copy.wait()
    for copy in own_copies:
        copy.wait()


def tail_kernel(
    blocks,
    groups,
    swaps,
    place,
    order,
    starts,
    lse,
    gain,
    attn_gain,
    ffn_gain_grad,
    out_part,
    *refs,
):
    sources, normed, refs = refs[:11], refs[11], refs[12:]
    swap_in, refs = refs[:swaps], refs[swaps:]
    out, grad_tokens, gains, attn_own = refs[:4]
    swap_out, refs = refs[4 : 4 + swaps], refs[4 + swaps :]
    targets, refs = refs[:11], refs[11:]
    grad_all, weights_in, q, k, v, o, qk, table, middle, x, grad_middle = targets
    size = lax.axis_size("ctx")
    count = 3 if size == 4 else 1
    bufs, back_bufs, refs = refs[:count], refs[count : 2 * count], refs[2 * count :]
    do, dq, dkv, joined, turned, part, attn_grad = refs[:7]
    home, travel, owned, ctx_box, fsdp_box = refs[7:12]
    send_one, recv_one, send_two, recv_two, send_three, recv_three = refs[12:18]
    send_four, recv_four, local = refs[18:]
    going, coming = travel.at[0], travel.at[1]
    out_sems, back_sems = (send_one, recv_one), (send_two, recv_two)
    line, small = (send_three, recv_three), (send_four, recv_four)
    me = lax.axis_index("ctx")
    chips = lax.axis_size("fsdp") // 2
    step_base = chips
    swap_base = step_base + 2 * chips
    qk_width = qk.shape[2]
    qkv_width = qk_width + v.shape[1]
    ones = head_ones(qk_width)
    first_load = load(out_part, part, local.at[15])
    meet(("ctx", "fsdp"))
    first_load.wait()
    out_copies = sum_start(part, bufs, out_sems)
    loads = [
        load(source, target, local.at[item])
        for item, (source, target) in enumerate(zip(sources, targets))
    ]
    swap_copies = []
    own_copies = []
    for item in range(swaps):
        swap_copies += swap_start(
            swap_in[item], swap_out[item], line, swap_base + (item + 1) * size
        )
        own_copies.append(
            load(swap_in[item].at[me], swap_out[item].at[me], local.at[13 + item])
        )
    for copy in loads[:6]:
        copy.wait()
    for block in range(blocks):
        do[block * HALF : (block + 1) * HALF, :] = dot(
            grad_all[place[block]], weights_in[:, qkv_width:], 1, 0
        ).astype(BF16)
    for block in range(blocks):
        turned[:, block * HALF : (block + 1) * HALF] = grad_all[block].T
    for first in range(0, D, 512):
        rows = slice(first, first + 512)
        attn_grad[rows, qkv_width:] = dot(turned[rows, :], o[...], 1, 0).astype(BF16)
    loads.append(load(normed, grad_all, local.at[12]))
    dkv[...] = jnp.zeros_like(dkv)
    for block in range(blocks):
        if block == blocks // 2:
            sum_pass(out_copies, part, bufs, out_sems)
        rows = slice(block * HALF, (block + 1) * HALF)
        keys = (block + 1) * HALF
        mask = block_mask(starts, block, keys)
        pieces = []
        dk_add = []
        dv_add = []
        for group in range(groups):
            lanes = slice(group * HD, (group + 1) * HD)
            queries = stack_heads(q, rows, group)
            outs = stack_heads(do, rows, group)
            key_rows = k[:keys, lanes]
            scores = dot(key_rows, queries, 1, 1) * SCALE
            weights = jnp.where(
                mask, jnp.exp(scores - lse[block, group : group + 1, :]), 0.0
            )
            back = dot(v[:keys, lanes], outs, 1, 1)
            delta = jnp.sum(weights * back, axis=0, keepdims=True)
            grads = (weights * (back - delta)).astype(BF16)
            pieces += unstack_heads(dot(key_rows, grads, 0, 0) * SCALE)
            dk_add.append(dot(grads, queries, 1, 0) * SCALE)
            dv_add.append(dot(weights.astype(BF16), outs, 1, 0))
        dq[block] = jnp.concatenate(pieces, axis=1)
        dkv[: block + 1] += jnp.concatenate(dk_add + dv_add, axis=1).reshape(
            (block + 1,) + dkv.shape[1:]
        )
    gain_row = jnp.zeros((1, qk_width), F32)
    for copy in loads[6:]:
        copy.wait()
    for block in range(blocks):
        here = order[block]
        values = qk[here]
        root = lax.rsqrt(head_mean(values * values, ones) + NORM_EPS)
        unit = values * root
        grad_kv = dkv[here]
        kv_width = grad_kv.shape[1] // 2
        grad = jnp.concatenate([dq[here], grad_kv[:, :kv_width]], axis=1)
        cosine, sine = widen(table[here], qk_width)
        grad = grad * cosine - partner(grad) * sine
        gain_row = gain_row + jnp.sum(grad * unit, axis=0, keepdims=True)
        grad = grad * gain[...]
        grad = root * (grad - unit * head_mean(grad * unit, ones))
        joined[block * HALF : (block + 1) * HALF, :] = jnp.concatenate(
            [grad, grad_kv[:, kv_width:]], axis=1
        ).astype(BF16)
    read = sum_rest(out_copies, part, bufs)
    half = middle.shape[0] // 2
    for first in (0, half):
        rows = pl.ds(first, half)
        out[rows, :] = (middle[rows, :] + read(first)).astype(BF16)
    for first in range(0, D, 512):
        part[:, first : first + 512] = dot(
            joined[...], weights_in[first : first + 512, :qkv_width], 1, 1
        ).astype(BF16)
    back_copies = sum_start(part, back_bufs, back_sems)
    for block in range(blocks):
        turned[:, block * HALF : (block + 1) * HALF] = grad_all[block].T
    for first in range(0, D, 512):
        rows = slice(first, first + 512)
        attn_grad[rows, :qkv_width] = dot(turned[rows, :], joined[...], 1, 0).astype(BF16)
    home_copies = line_start(attn_grad, home, line, 0)
    line_home(home_copies, attn_grad, home)
    line_step(chips - 1, home, going, coming, line, step_base)
    sum_pass(back_copies, part, back_bufs, back_sems)
    for reach in range(chips - 2, 0, -1):
        line_step(reach, home, going, coming, line, step_base)
    read = sum_rest(back_copies, part, back_bufs)
    total = jnp.zeros((1, D), F32)
    for first in (0, half):
        rows = pl.ds(first, half)
        values = x[rows, :].astype(F32)
        root = row_scale(values)
        unit = values * root
        back = read(first)
        total = total + jnp.sum(back * unit, axis=0, keepdims=True)
        back = back * attn_gain[...]
        back = root * (back - unit * jnp.mean(back * unit, axis=-1, keepdims=True))
        grad_tokens[rows, :] = grad_middle[rows, :] + back
    line_end(home_copies, home, going, coming, line, step_base)
    chip = lax.axis_index("fsdp") // 2
    owned_rows = owned.shape[1]
    for index in range(size):
        owned[index] = home[chip, index * owned_rows : (index + 1) * owned_rows, :]
    swap_copies += swap_start(owned, attn_own, line, swap_base)
    attn_own[me] = owned[me]
    base = 0
    for axis, box in (("ctx", ctx_box), ("fsdp", fsdp_box)):
        axis_size = lax.axis_size(axis)
        index = lax.axis_index(axis)
        if axis == "ctx":
            box[index] = jnp.concatenate(
                [
                    total,
                    ffn_gain_grad[...],
                    jnp.concatenate([gain_row, jnp.zeros((1, D - qk_width), F32)], axis=1),
                    jnp.zeros((5, D), F32),
                ],
                axis=0,
            )
        else:
            box[index] = summed
        copies = [
            send(
                box.at[index],
                box.at[index],
                small,
                base + step,
                {axis: lax.rem(index + step, axis_size)},
            )
            for step in range(1, axis_size)
        ]
        for copy in copies:
            copy.wait()
        base += axis_size
        summed = box[0]
        for item in range(1, axis_size):
            summed = summed + box[item]
    gains[...] = summed
    for copy in swap_copies:
        copy.wait()
    for copy in own_copies:
        copy.wait()


def rms_scale(values_in, gain_vec):
    return (
        values_in
        * lax.rsqrt(jnp.mean(values_in * values_in, axis=-1, keepdims=True) + NORM_EPS)
        * gain_vec
    )


def inverse_freq():
    return 1.0 / ROPE_BASE ** (jnp.arange(0, HD, 2).astype(F32) / HD)


def shards(
    tokens,
    cotangent,
    doc_starts,
    block_order,
    master_weights,
    moment_one,
    moment_two,
    gains,
    gains_moment_one,
    gains_moment_two,
):
    nctx = lax.axis_size("ctx")
    nfsdp = lax.axis_size("fsdp")
    own_rows = master_weights.shape[0]
    tok_rows = tokens.shape[1]
    stream_len = tok_rows * nctx
    blocks = stream_len // HALF
    groups = KVHEADS // nctx
    q_width = D // nctx
    kv_width = KVD // nctx
    qk_width = q_width + kv_width
    qkv_width = qk_width + kv_width
    tiles = FF // 128
    ff_tiles = -(-tiles // nctx)
    ff_width = ff_tiles * 128
    bundles = 2
    cuts = [0, (ff_tiles * 9 + 7) // 14 * 128, ff_width]

    low = master_weights.astype(BF16)

    def ff_part(base, index, start, stop):
        first = index * ff_width + start
        last = index * ff_width + stop
        real_first, real_last = min(first, FF), min(last, FF)
        part = low[:, base + real_first : base + real_last]
        if real_last - real_first < last - first:
            part = jnp.pad(part, ((0, 0), (0, (last - first) - (real_last - real_first))))
        return part

    def attn_part(index):
        return jnp.concatenate(
            [
                low[:, index * q_width : (index + 1) * q_width],
                low[:, D + index * kv_width : D + (index + 1) * kv_width],
                low[:, D + KVD + index * kv_width : D + KVD + (index + 1) * kv_width],
                low[:, QKVC + index * q_width : QKVC + (index + 1) * q_width],
            ],
            axis=1,
        )

    gate_base = QKVC + D
    bases = (gate_base, gate_base + FF, gate_base + 2 * FF)
    attn_send = jnp.stack([attn_part(c) for c in range(nctx)])
    ff_send = [
        jnp.stack(
            [
                jnp.concatenate(
                    [ff_part(base, c, cuts[b], cuts[b + 1]) for base in bases], axis=1
                )
                for c in range(nctx)
            ]
        )
        for b in range(bundles)
    ]

    def gather_rows(piece):
        return lax.all_gather(
            piece.reshape(nctx * own_rows, piece.shape[-1]), "fsdp", axis=0, tiled=True
        )

    def spread(active):
        return (
            active.reshape(active.shape[0], nctx, nfsdp, own_rows)
            .transpose(0, 2, 1, 3)
            .reshape(active.shape[0], D)
        )

    def unspread(active):
        return (
            active.reshape(active.shape[0], nfsdp, nctx, own_rows)
            .transpose(0, 2, 1, 3)
            .reshape(active.shape[0], D)
        )

    dma = pltpu.SemaphoreType.DMA
    all_low = jax.ShapeDtypeStruct((nctx, tok_rows, D), BF16)
    own_low = jax.ShapeDtypeStruct((tok_rows, D), BF16)
    own_f32 = jax.ShapeDtypeStruct((tok_rows, D), F32)
    row_f32 = jax.ShapeDtypeStruct((1, D), F32)
    g_attn = spread(gains[None, :D])
    g_ffn = spread(gains[None, D : 2 * D])
    order = block_order.reshape(blocks)
    place = jnp.argsort(order).astype(jnp.int32)
    starts = doc_starts[0]

    (attn_held,) = exchange(("swap",), [attn_send], 0, 10)
    w_attn = gather_rows(attn_held)
    first_send, attn_held = lax.optimization_barrier((ff_send[0], attn_held))
    (first_held,) = exchange(("swap",), [first_send], 1, 16)
    table_shape = jax.ShapeDtypeStruct((stream_len, 2 * HD), F32)
    origin = spread(jnp.arange(D, dtype=jnp.int32)[None])
    starts_late, first_held = lax.optimization_barrier((starts, first_held))
    x_low, dy_low, table, normed_all = remote_call(
        first_kernel,
        [own_low, own_low, table_shape, all_low],
        (
            starts_late,
            origin,
            tokens[0],
            cotangent[0],
            g_attn,
            jnp.tile(inverse_freq(), 4)[None],
        ),
        2,
        33,
        [
            pltpu.VMEM((D, D), BF16),
            pltpu.VMEM((tok_rows, D), BF16),
            dma((GATHER_SEMS,)),
            dma((GATHER_SEMS,)),
            dma,
        ],
        (3,),
        1,
    )
    normed_all = normed_all.reshape(stream_len, D)

    g_query = gains[2 * D : 2 * D + HD]
    g_key = gains[2 * D + HD :]
    qk_gain = jnp.concatenate(
        [jnp.tile(g_query, q_width // HD), jnp.tile(g_key, kv_width // HD)]
    )[None]

    low_stream = pltpu.VMEM((stream_len, D), BF16)
    heads_low = pltpu.VMEM((stream_len, q_width), BF16)
    part, qk, q, k, v, mixed, lse, dy_all, second_held = remote_call(
        functools.partial(attend_kernel, blocks, groups),
        [
            jax.ShapeDtypeStruct((stream_len, D), BF16),
            jax.ShapeDtypeStruct((stream_len, qk_width), F32),
            jax.ShapeDtypeStruct((stream_len, q_width), BF16),
            jax.ShapeDtypeStruct((stream_len, kv_width), BF16),
            jax.ShapeDtypeStruct((stream_len, kv_width), BF16),
            jax.ShapeDtypeStruct((stream_len, q_width), BF16),
            jax.ShapeDtypeStruct((blocks, groups, GROUP * HALF), F32),
            all_low,
            jax.ShapeDtypeStruct(ff_send[1].shape, BF16),
        ],
        (place, order, starts, table, qk_gain, normed_all, w_attn, dy_low, ff_send[1]),
        3,
        42,
        [
            low_stream,
            pltpu.VMEM(w_attn.shape, BF16),
            pltpu.VMEM((blocks, HALF, qkv_width), F32),
            pltpu.VMEM((blocks, HALF, q_width), BF16),
            dma((GATHER_SEMS + nctx,)),
            dma((GATHER_SEMS + nctx,)),
            dma((4,)),
        ],
        (7, 8),
        3,
        4,
    )
    dy_all = dy_all.reshape(stream_len, D)
    w_ff = [gather_rows(first_held), gather_rows(second_held)]
    sum_bufs = sum_scratch(nctx, tok_rows)
    sum_sems = [dma((GATHER_SEMS,)), dma((GATHER_SEMS,))]
    norm_scratch = (
        sum_bufs + [pltpu.VMEM((tok_rows, D), BF16)] + sum_sems + sum_sems + [dma]
    )

    middle, normed_two_all = remote_call(
        middle_kernel,
        [own_f32, all_low],
        (part, x_low, g_ffn),
        4,
        57,
        norm_scratch,
        (1,),
    )
    normed_two_all = normed_two_all.reshape(stream_len, D)

    def sum_rows(grad):
        return lax.psum_scatter(grad, "fsdp", scatter_dimension=0, tiled=True).reshape(
            nctx, own_rows, grad.shape[-1]
        )

    def feed(b, x_all, dy):
        width = cuts[b + 1] - cuts[b]
        w_gu, w_down = w_ff[b][:, : 2 * width], w_ff[b][:, 2 * width :]
        gate_up = dot(x_all, w_gu, 1, 0).astype(BF16)
        gate, up = gate_up[:, :width].astype(F32), gate_up[:, width:].astype(F32)
        gated = jax.nn.sigmoid(gate)
        act = gate * gated
        hidden = (act * up).astype(BF16)
        back_hidden = dot(dy, w_down, 1, 0)
        grad_gu = jnp.concatenate(
            [back_hidden * up * (gated + act * (1.0 - gated)), back_hidden * act], axis=1
        ).astype(BF16)
        return hidden, grad_gu, dot(grad_gu, w_gu, 1, 1)

    hidden_one, grad_gu, back_partial = feed(0, normed_two_all, dy_all)
    gu_grad = dot(normed_two_all, grad_gu, 0, 0).astype(BF16)
    gu_grad, back_partial, w_ff[1] = lax.optimization_barrier((gu_grad, back_partial, w_ff[1]))
    width_two = cuts[2] - cuts[1]
    hidden_two, grad_gu, back_more = feed(1, normed_two_all, dy_all)
    back_partial = (back_partial + back_more).astype(BF16)
    gu_sum = sum_rows(gu_grad)
    chips = nfsdp // 2

    def line_scratch(columns):
        block = (nctx * own_rows, columns)
        return [pltpu.VMEM((chips,) + block, BF16), pltpu.VMEM((2, 2, chips - 1) + block, BF16)]

    grad_middle, grad_g_ffn, down_sum, grad_middle_all, last_grad, out_partial = remote_call(
        middle_back_kernel,
        [
            own_f32,
            row_f32,
            jax.ShapeDtypeStruct((nctx, own_rows, cuts[1]), BF16),
            all_low,
            jax.ShapeDtypeStruct((D, 3 * width_two), BF16),
            jax.ShapeDtypeStruct((stream_len, D), BF16),
        ],
        (
            back_partial,
            middle,
            dy_low,
            g_ffn,
            normed_two_all,
            dy_all,
            hidden_one,
            hidden_two,
            grad_gu,
            w_ff[0],
            w_ff[1],
        ),
        5,
        57,
        sum_bufs
        + [
            pltpu.VMEM((tok_rows, D), BF16),
            low_stream,
            pltpu.VMEM((stream_len, 2 * width_two), BF16),
            pltpu.VMEM((D, stream_len), BF16),
            pltpu.VMEM((D, 3 * width_two), BF16),
            pltpu.VMEM((D, cuts[1]), BF16),
            low_stream,
            pltpu.VMEM((stream_len, cuts[1]), BF16),
            pltpu.VMEM((stream_len, width_two), BF16),
            pltpu.VMEM((D, cuts[1]), BF16),
            pltpu.VMEM((D, width_two), BF16),
        ]
        + line_scratch(cuts[1])
        + sum_sems
        + sum_sems
        + [dma((3 * chips,)), dma((3 * chips,)), dma((10,))],
        (3, 4, 5),
        0,
        7,
    )
    last_sum = sum_rows(last_grad)

    small = dma((nctx + nfsdp,))
    line_sems = dma((3 * chips + 3 * nctx,))
    own_shape = (nctx, own_rows, qkv_width + q_width)
    sources = (
        grad_middle_all.reshape(blocks, HALF, D),
        w_attn,
        q,
        k,
        v,
        mixed,
        qk.reshape(blocks, HALF, qk_width),
        table.reshape(blocks, HALF, 2 * HD),
        middle,
        x_low,
        grad_middle,
    )
    out_tokens, grad_tokens, gain_sums, attn_own, gu_own, down_own = remote_call(
        functools.partial(tail_kernel, blocks, groups, 2),
        [
            own_low,
            own_f32,
            jax.ShapeDtypeStruct((8, D), F32),
            jax.ShapeDtypeStruct(own_shape, BF16),
            jax.ShapeDtypeStruct(gu_sum.shape, BF16),
            jax.ShapeDtypeStruct(down_sum.shape, BF16),
        ],
        (place, order, starts, lse, qk_gain, g_attn, grad_g_ffn, out_partial)
        + sources
        + (normed_all.reshape(blocks, HALF, D), gu_sum, down_sum),
        6,
        90,
        [pltpu.VMEM(source.shape, source.dtype) for source in sources]
        + sum_bufs
        + sum_bufs
        + [
            heads_low,
            pltpu.VMEM((blocks, HALF, q_width), F32),
            pltpu.VMEM((blocks, HALF, 2 * kv_width), F32),
            pltpu.VMEM((stream_len, qkv_width), BF16),
            pltpu.VMEM((D, stream_len), BF16),
            low_stream,
            pltpu.VMEM((D, qkv_width + q_width), BF16),
        ]
        + line_scratch(qkv_width + q_width)
        + [
            pltpu.VMEM(own_shape, BF16),
            pltpu.VMEM((nctx, 8, D), F32),
            pltpu.VMEM((nfsdp, 8, D), F32),
        ]
        + sum_sems
        + sum_sems
        + [line_sems, line_sems, small, small, dma((16,))],
        (4, 5),
        3,
        15,
    )
    out_tokens = unspread(out_tokens)[None]
    grad_tokens = unspread(grad_tokens)[None]
    gain_grad = jnp.concatenate(
        [
            unspread(gain_sums[:1])[0],
            unspread(gain_sums[1:2])[0],
            jnp.sum(gain_sums[2, :q_width].reshape(-1, HD), axis=0),
            jnp.sum(gain_sums[2, q_width:qk_width].reshape(-1, HD), axis=0),
        ]
    )

    olds = (master_weights, moment_one, moment_two)

    def feed_segments(b, pieces):
        width = cuts[b + 1] - cuts[b]
        found = []
        for part in range(3):
            for c in range(nctx):
                column = c * ff_width + cuts[b]
                real = min(max(FF - column, 0), width)
                if real:
                    piece, first = pieces[part]
                    found.append((piece, c, first, bases[part] + column, real))
        return found

    width_one = cuts[1]
    last_own = [
        lax.ppermute(
            lax.dynamic_index_in_dim(last_sum, lax.axis_index("ctx") ^ k, 0, keepdims=False),
            "ctx",
            [(c, c ^ k) for c in range(nctx)],
        )
        if k
        else lax.dynamic_index_in_dim(last_sum, lax.axis_index("ctx"), 0, keepdims=False)
        for k in range(nctx)
    ]
    news = adam(
        feed_segments(0, ((0, 0), (0, width_one), (1, 0))), [gu_own, down_own], olds, None, 7
    )
    parts = (
        (0, 0, q_width),
        (q_width, D, kv_width),
        (qk_width, D + KVD, kv_width),
        (qkv_width, QKVC, q_width),
    )
    if kv_width % 128:
        attn_own = jnp.concatenate(
            [attn_own[c, :, f : f + w] for f, _, w in parts for c in range(nctx)], axis=1
        )[None]
        segments = [(0, 0, 0, 0, gate_base)]
    else:
        segments = [
            (0, c, first, base + c * width, width)
            for first, base, width in parts
            for c in range(nctx)
        ]
    news = adam(segments, [attn_own], olds, news, 3)
    first_new, second_new, master_new, low_new = adam(
        feed_segments(1, ((None, 0), (None, width_two), (None, 2 * width_two))),
        last_own,
        olds,
        news,
        6,
    )
    gain_first, gain_second, gain_new = adam_update(
        gains, gain_grad, gains_moment_one, gains_moment_two, GAIN_RATE, 0.0
    )
    return (
        out_tokens,
        grad_tokens,
        first_new,
        second_new,
        master_new,
        low_new,
        gain_first,
        gain_second,
        gain_new,
    )


def solution(mesh):
    rows = P("fsdp", "ctx", None)
    weights = P(("ctx", "fsdp"), None)
    return jax.shard_map(
        shards,
        mesh=mesh,
        in_specs=(rows, rows, P("fsdp", None), P(), weights, weights, weights, P(), P(), P()),
        out_specs=(rows, rows, weights, weights, weights, weights, P(), P(), P()),
        check_vma=False,
    )
```

```python
import functools

import jax
import jax.numpy as jnp
from jax import lax
from jax.experimental import pallas as pl
from jax.experimental.pallas import tpu as pltpu
from jax.sharding import PartitionSpec as P

D = 1536
HEADS = 24
KVHEADS = 8
HD = 64
FF = 6912
STEP = 10
HALF = 128
KVD = 512
QKVC = 2560
GROUP = HEADS // KVHEADS

ROPE_BASE = 1000000.0
NORM_EPS = 1e-05
BETA_ONE = 0.9
BETA_TWO = 0.95
ADAM_EPS = 1e-08
WEIGHT_DECAY = 0.1
LEARN_RATE = 0.03
GAIN_RATE = 0.5
SCALE = HD ** (-0.5)
MESH = pl.DeviceIdType.MESH
F32 = jnp.float32
BF16 = jnp.bfloat16
VMEM_LIMIT = 60 * 1024 * 1024


def dot(left, right, left_dim, right_dim):
    return lax.dot_general(
        left, right, (((left_dim,), (right_dim,)), ((), ())), preferred_element_type=F32
    )


def send(source, target, sems, item, peer):
    copy = pltpu.make_async_remote_copy(
        src_ref=source,
        dst_ref=target,
        send_sem=sems[0].at[item],
        recv_sem=sems[1].at[item],
        device_id=peer,
        device_id_type=MESH,
    )
    copy.start()
    return copy


def meet(axes):
    barrier = pltpu.get_barrier_semaphore()
    total = 0
    for axis in axes:
        size = lax.axis_size(axis)
        me = lax.axis_index(axis)
        for step in range(1, size):
            pl.semaphore_signal(
                barrier,
                inc=1,
                device_id={axis: lax.rem(me + step, size)},
                device_id_type=MESH,
            )
        total += size - 1
    pl.semaphore_wait(barrier, total)


def square():
    me = lax.axis_index("ctx")
    return me, me + 1 - 2 * lax.rem(me, 2), lax.rem(me + 2, 4), 3 - me


def swap_start(source, target, sems, base):
    size = lax.axis_size("ctx")
    me = lax.axis_index("ctx")
    copies = []
    for step in range(1, size):
        peer = lax.rem(me + step, size)
        copies.append(
            send(source.at[peer], target.at[me], sems, base + step, {"ctx": peer})
        )
    return copies


def gather_start(source, target, sems, base):
    size = lax.axis_size("ctx")
    me = lax.axis_index("ctx")
    if size != 4:
        return [
            send(
                source,
                target.at[me],
                sems,
                base + step,
                {"ctx": lax.rem(me + step, size)},
            )
            for step in range(1, size)
        ]
    me, side, over, across = square()
    half = source.shape[0] // 2
    top, low = pl.ds(0, half), pl.ds(half, half)
    return [
        send(source.at[top], target.at[me, top], sems, base, {"ctx": side}),
        send(source.at[low], target.at[me, low], sems, base + 1, {"ctx": over}),
        send(source.at[low], target.at[me, low], sems, base + 2, {"ctx": side}),
        send(source.at[top], target.at[me, top], sems, base + 3, {"ctx": over}),
    ]


def gather_pass(copies, target, sems, base):
    if lax.axis_size("ctx") != 4:
        return
    me, side, over, across = square()
    half = target.shape[1] // 2
    top, low = pl.ds(0, half), pl.ds(half, half)
    copies[0].wait_recv()
    copies.append(send(target.at[side, top], target.at[side, top], sems, base + 4, {"ctx": over}))
    copies[1].wait_recv()
    copies.append(send(target.at[over, low], target.at[over, low], sems, base + 5, {"ctx": side}))


def gather_end(copies):
    if lax.axis_size("ctx") != 4:
        for copy in copies:
            copy.wait()
        return
    for copy in copies:
        copy.wait_send()
    for copy in copies[2:]:
        copy.wait_recv()


def gather_rest(copies, target, sems, base):
    gather_pass(copies, target, sems, base)
    gather_end(copies)


def load(source, target, sem):
    copy = pltpu.make_async_copy(source, target, sem)
    copy.start()
    return copy


GATHER_SEMS = 8


def exchange_kernel(kinds, *refs):
    count = len(kinds)
    ins, outs = refs[:count], refs[count : 2 * count]
    send_sem, recv_sem, local_sem = refs[2 * count :]
    sems = (send_sem, recv_sem)
    me = lax.axis_index("ctx")
    meet(("ctx",))
    copies = []
    own = []
    for item in range(count):
        base = item * GATHER_SEMS
        if kinds[item] == "gather":
            copies.append(gather_start(ins[item], outs[item], sems, base))
            source = ins[item]
        else:
            copies.append(swap_start(ins[item], outs[item], sems, base))
            source = ins[item].at[me]
        copy = pltpu.make_async_copy(source, outs[item].at[me], local_sem.at[item])
        copy.start()
        own.append(copy)
    for item in range(count):
        if kinds[item] == "gather":
            gather_rest(copies[item], outs[item], sems, item * GATHER_SEMS)
        else:
            for copy in copies[item]:
                copy.wait()
    for copy in own:
        copy.wait()


def remote_params(collective_id):
    return pltpu.CompilerParams(
        collective_id=collective_id, has_side_effects=True, vmem_limit_bytes=VMEM_LIMIT
    )


def cost(micros):
    return pl.CostEstimate(flops=0, bytes_accessed=int(micros * 3.0e6), transcendentals=0)


def exchange(kinds, arrays, collective_id, micros):
    size = lax.axis_size("ctx")
    shapes = [
        jax.ShapeDtypeStruct((size,) + a.shape if kind == "gather" else a.shape, a.dtype)
        for kind, a in zip(kinds, arrays)
    ]
    sems = pltpu.SemaphoreType.DMA((len(arrays) * GATHER_SEMS,))
    return pl.pallas_call(
        functools.partial(exchange_kernel, kinds),
        out_shape=shapes,
        in_specs=[pl.BlockSpec(memory_space=pl.ANY)] * len(arrays),
        out_specs=[pl.BlockSpec(memory_space=pl.ANY)] * len(arrays),
        scratch_shapes=[sems, sems, pltpu.SemaphoreType.DMA((len(arrays),))],
        compiler_params=remote_params(collective_id),
        cost_estimate=cost(micros),
    )(*arrays)


def sum_scratch(size, rows):
    if size == 4:
        half = pltpu.VMEM((2, rows // 2, D), BF16)
        return [half, half, pltpu.VMEM((2, rows, D), BF16)]
    return [pltpu.VMEM((size - 1, rows, D), BF16)]


def sum_start(part, bufs, sems):
    size = lax.axis_size("ctx")
    me = lax.axis_index("ctx")
    rows = part.shape[0] // size

    def block(owner, first=0, count=rows):
        return pl.ds(pl.multiple_of(owner * rows + first, rows // 2), count)

    if size != 4:
        copies = []
        for step in range(1, size):
            peer = lax.rem(me + step, size)
            copies.append(
                send(part.at[block(peer)], bufs[0].at[step - 1], sems, step, {"ctx": peer})
            )
        return copies
    me, side, over, across = square()
    half = rows // 2
    relay, _, landed = bufs
    return [
        send(part.at[block(across, 0, half)], relay.at[0], sems, 0, {"ctx": side}),
        send(part.at[block(across, half, half)], relay.at[1], sems, 1, {"ctx": over}),
        send(
            part.at[block(side, 0, half)],
            landed.at[0, pl.ds(0, half)],
            sems,
            2,
            {"ctx": side},
        ),
        send(
            part.at[block(over, half, half)],
            landed.at[1, pl.ds(half, half)],
            sems,
            3,
            {"ctx": over},
        ),
    ]


def sum_pass(copies, part, bufs, sems):
    if lax.axis_size("ctx") != 4:
        return
    rows = part.shape[0] // 4
    half = rows // 2

    def rows_of(owner, first):
        return pl.ds(pl.multiple_of(owner * rows + first, half), half)

    me, side, over, across = square()
    relay, passed, landed = bufs
    copies[0].wait_recv()
    passed[0] = (part[rows_of(over, 0), :].astype(F32) + relay[0].astype(F32)).astype(BF16)
    copies.append(
        send(passed.at[0], landed.at[1, pl.ds(0, half)], sems, 4, {"ctx": over})
    )
    copies[1].wait_recv()
    passed[1] = (part[rows_of(side, half), :].astype(F32) + relay[1].astype(F32)).astype(
        BF16
    )
    copies.append(
        send(passed.at[1], landed.at[0, pl.ds(half, half)], sems, 5, {"ctx": side})
    )


def sum_rest(copies, part, bufs):
    size = lax.axis_size("ctx")
    me = lax.axis_index("ctx")
    rows = part.shape[0] // size
    half = rows // 2

    def rows_of(owner, first):
        return pl.ds(pl.multiple_of(owner * rows + first, half), half)

    if size != 4:
        for copy in copies:
            copy.wait()

        def read(first):
            total = part[rows_of(me, first), :].astype(F32)
            for step in range(1, size):
                total = total + bufs[0][step - 1, pl.ds(first, half), :].astype(F32)
            return total

        return read
    relay, passed, landed = bufs
    for copy in copies:
        copy.wait_send()
    for copy in copies[2:]:
        copy.wait_recv()

    def read(first):
        return (
            part[rows_of(me, first), :].astype(F32)
            + landed[0, pl.ds(first, half), :].astype(F32)
            + landed[1, pl.ds(first, half), :].astype(F32)
        )

    return read


def row_scale(values):
    return lax.rsqrt(jnp.mean(values * values, axis=-1, keepdims=True) + NORM_EPS)


def first_kernel(
    starts, origin, x, dy, gain, freq, x_low, dy_low, table, normed_all, *scratch
):
    move, normed, send_one, recv_one, local = scratch
    me = lax.axis_index("ctx")
    row = lax.broadcasted_iota(jnp.int32, move.shape, 0)
    move[...] = jnp.where(row == origin[...], 1.0, 0.0).astype(BF16)
    values = dot(x[...], move[...], 1, 0)
    x_low[...] = values.astype(BF16)
    normed[...] = (values * row_scale(values) * gain[...]).astype(BF16)
    meet(("ctx",))
    sems = (send_one, recv_one)
    copies = gather_start(normed, normed_all, sems, 0)
    own = load(normed, normed_all.at[me], local)
    dy_low[...] = dot(dy[...], move[...], 1, 0).astype(BF16)
    gather_pass(copies, normed_all, sems, 0)
    times = lax.broadcasted_iota(jnp.int32, (table.shape[0], 1), 0)
    angles = (times - doc_first(starts, times)).astype(F32) * freq[...]
    lane = lax.broadcasted_iota(jnp.int32, angles.shape, 1)
    sine = jnp.sin(angles)
    sine = jnp.where(lane % HD < HD // 2, -sine, sine)
    table[...] = jnp.where(lane < HD, jnp.cos(angles), sine)
    gather_end(copies)
    own.wait()


def middle_kernel(part, x, gain, middle, normed_all, *scratch):
    bufs, (normed, send_one, recv_one, send_two, recv_two, local) = scratch[:-6], scratch[-6:]
    me = lax.axis_index("ctx")
    meet(("ctx",))
    copies = sum_start(part, bufs, (send_one, recv_one))
    sum_pass(copies, part, bufs, (send_one, recv_one))
    read = sum_rest(copies, part, bufs)
    half = x.shape[0] // 2
    for first in (0, half):
        rows = pl.ds(first, half)
        values = x[rows, :].astype(F32) + read(first)
        middle[rows, :] = values
        normed[rows, :] = (values * row_scale(values) * gain[...]).astype(BF16)
    sems = (send_two, recv_two)
    copies = gather_start(normed, normed_all, sems, 0)
    own = load(normed, normed_all.at[me], local)
    gather_rest(copies, normed_all, sems, 0)
    own.wait()


def column_tiles(total, body):
    def step(tile, carry):
        body(pl.multiple_of(tile * 256, 256), 256)
        return carry

    lax.fori_loop(0, total // 256, step, 0)
    if total % 256:
        body(total - total % 256, total % 256)


def turn(source, target):
    for first in range(0, source.shape[0], HALF):
        rows = slice(first, first + HALF)
        target[:, rows] = source[rows, :].T


def middle_back_kernel(
    part,
    middle,
    dy,
    gain,
    x_all,
    dy_all,
    hidden_one,
    hidden_two,
    grad_gu,
    w_one,
    w_two,
    grad,
    gain_grad,
    down_sum,
    grad_all,
    weight_grad,
    out,
    *scratch,
):
    bufs = scratch[:-20]
    low, x_buf, gu_buf, turned, weight_buf, down_grad, out_buf = scratch[-20:-13]
    hidden_bufs, down_bufs = scratch[-13:-11], scratch[-11:-9]
    home, travel, send_one, recv_one, send_two, recv_two, send_three, recv_three, local = (
        scratch[-9:]
    )
    going, coming = travel.at[0], travel.at[1]
    me = lax.axis_index("ctx")
    chips = lax.axis_size("fsdp") // 2
    line = (send_three, recv_three)
    meet(("ctx", "fsdp"))
    copies = sum_start(part, bufs, (send_one, recv_one))
    width_one, width_two = hidden_one.shape[1], hidden_two.shape[1]
    gu_width = grad_gu.shape[1]
    loads = [
        load(source, target, local.at[item])
        for item, (source, target) in enumerate(
            (
                (dy_all, x_buf),
                (hidden_one, hidden_bufs[0]),
                (hidden_two, hidden_bufs[1]),
                (grad_gu, gu_buf),
                (w_one.at[:, pl.ds(2 * width_one, width_one)], down_bufs[0]),
                (w_two.at[:, pl.ds(2 * width_two, width_two)], down_bufs[1]),
            )
        )
    ]
    loads[0].wait()
    turn(x_buf, turned)
    loads.append(load(x_all, x_buf, local.at[6]))
    loads[1].wait()

    def product(target, column, right):
        def tile(first, width):
            target[:, pl.ds(column + first, width)] = dot(
                turned[...], right[:, pl.ds(first, width)], 1, 0
            ).astype(BF16)

        column_tiles(right.shape[1], tile)

    product(down_grad, 0, hidden_bufs[0])
    home_copies = line_start(down_grad, home, line, 0)
    sum_pass(copies, part, bufs, (send_one, recv_one))
    loads[2].wait()
    product(weight_buf, gu_width, hidden_bufs[1])
    line_home(home_copies, down_grad, home)
    line_step(chips - 1, home, going, coming, line, chips)
    loads[6].wait()
    turn(x_buf, turned)
    loads[3].wait()
    product(weight_buf, 0, gu_buf)
    stores = [load(weight_buf, weight_grad, local.at[7])]
    read = sum_rest(copies, part, bufs)
    half = dy.shape[0] // 2
    total = jnp.zeros((1, D), F32)
    for first in (0, half):
        rows = pl.ds(first, half)
        values = middle[rows, :]
        root = row_scale(values)
        unit = values * root
        back = read(first)
        total = total + jnp.sum(back * unit, axis=0, keepdims=True)
        back = back * gain[...]
        back = root * (back - unit * jnp.mean(back * unit, axis=-1, keepdims=True))
        back = back + dy[rows, :].astype(F32)
        grad[rows, :] = back
        low[rows, :] = back.astype(BF16)
    gain_grad[...] = total
    sems = (send_two, recv_two)
    copies = gather_start(low, grad_all, sems, 0)
    stores.append(load(low, grad_all.at[me], local.at[8]))
    if chips > 2:
        line_step(chips - 2, home, going, coming, line, chips)
    loads[4].wait()
    loads[5].wait()

    def out_tile(first, width):
        columns = pl.ds(first, width)
        out_buf[:, columns] = (
            dot(hidden_bufs[0][...], down_bufs[0][columns, :], 1, 1)
            + dot(hidden_bufs[1][...], down_bufs[1][columns, :], 1, 1)
        ).astype(BF16)

    column_tiles(D, out_tile)
    stores.append(load(out_buf, out, local.at[9]))
    gather_pass(copies, grad_all, sems, 0)
    for reach in range(min(chips - 1, max(chips - 3, 1)), 0, -1):
        line_step(reach, home, going, coming, line, chips)
    gather_end(copies)
    line_end(home_copies, home, going, coming, line, chips)
    chip = lax.axis_index("fsdp") // 2
    rows = down_sum.shape[1]
    for index in range(down_sum.shape[0]):
        down_sum[index] = home[chip, index * rows : (index + 1) * rows, :]
    for copy in stores:
        copy.wait()


def line_start(grad, home, sems, base):
    me = lax.axis_index("fsdp")
    chips = lax.axis_size("fsdp") // 2
    core = lax.rem(me, 2)
    rows = grad.shape[0] // (2 * chips)
    copies = []
    for chip in range(chips):
        theirs = pl.ds(pl.multiple_of((2 * chip + 1 - core) * rows, rows), rows)
        copies.append(
            send(grad.at[theirs], home.at[chip], sems, base + chip, {"fsdp": me + 1 - 2 * core})
        )
    return copies


def line_home(copies, grad, home):
    me = lax.axis_index("fsdp")
    chips = lax.axis_size("fsdp") // 2
    core = lax.rem(me, 2)
    rows = grad.shape[0] // (2 * chips)
    for chip in range(chips):
        copies[chip].wait_recv()
        mine = pl.ds(pl.multiple_of((2 * chip + core) * rows, rows), rows)
        home[chip] = (home[chip].astype(F32) + grad[mine, :].astype(F32)).astype(BF16)


def line_copies(reach, going, coming, sems, base):
    me = lax.axis_index("fsdp")
    chips = lax.axis_size("fsdp") // 2
    chip = me // 2
    found = []
    for side, way in ((0, 1), (1, -1)):
        copy = pltpu.make_async_remote_copy(
            src_ref=going.at[side, reach - 1],
            dst_ref=coming.at[side, reach - 1],
            send_sem=sems[0].at[base + 2 * reach + side],
            recv_sem=sems[1].at[base + 2 * reach + side],
            device_id={"fsdp": lax.rem(me + 2 * way + 2 * chips, 2 * chips)},
            device_id_type=MESH,
        )
        if way == 1:
            sent = chip + reach <= chips - 1
            got = (chip >= 1) & (chip + reach <= chips)
            more = (chip >= 1) & sent
        else:
            sent = chip >= reach
            got = (chip <= chips - 2) & (chip + 1 >= reach)
            more = (chip <= chips - 2) & sent
        found.append((side, way, copy, sent, got, more))
    return found


def line_step(reach, home, going, coming, sems, base):
    me = lax.axis_index("fsdp")
    chips = lax.axis_size("fsdp") // 2
    chip = me // 2
    if reach < chips - 1:
        for _, _, copy, _, got, _ in line_copies(reach + 1, going, coming, sems, base):
            pl.when(got)(copy.wait_recv)
    for side, way, copy, sent, _, more in line_copies(reach, going, coming, sems, base):

        @pl.when(sent)
        def _(side=side, way=way, copy=copy, more=more):
            value = home[chip + way * reach]
            if reach < chips - 1:

                @pl.when(more)
                def _():
                    going[side, reach - 1] = (
                        value.astype(F32) + coming[side, reach].astype(F32)
                    ).astype(BF16)

                @pl.when(jnp.logical_not(more))
                def _():
                    going[side, reach - 1] = value

            else:
                going[side, reach - 1] = value
            copy.start()


def line_end(copies, home, going, coming, sems, base):
    me = lax.axis_index("fsdp")
    chips = lax.axis_size("fsdp") // 2
    chip = me // 2
    for side, _, copy, _, got, _ in line_copies(1, going, coming, sems, base):

        @pl.when(got)
        def _(side=side, copy=copy):
            copy.wait_recv()
            home[chip] = (home[chip].astype(F32) + coming[side, 0].astype(F32)).astype(BF16)

    for copy in copies:
        copy.wait_send()
    for reach in range(1, chips):
        for _, _, copy, sent, _, _ in line_copies(reach, going, coming, sems, base):
            pl.when(sent)(copy.wait_send)


def remote_call(
    kernel, out_shape, args, collective_id, micros, scratch, in_hbm=(), smem=0, args_in_hbm=0
):
    return pl.pallas_call(
        kernel,
        out_shape=out_shape,
        in_specs=[pl.BlockSpec(memory_space=pltpu.SMEM)] * smem
        + [pl.BlockSpec(memory_space=pltpu.VMEM)] * (len(args) - smem - args_in_hbm)
        + [pl.BlockSpec(memory_space=pl.ANY)] * args_in_hbm,
        out_specs=[
            pl.BlockSpec(memory_space=pl.ANY if item in in_hbm else pltpu.VMEM)
            for item in range(len(out_shape))
        ],
        scratch_shapes=scratch,
        compiler_params=remote_params(collective_id),
        cost_estimate=cost(micros),
    )(*args)


def adam_update(param_now, grad_now, moment_old_one, moment_old_two, step_rate, decay_rate):
    first_new = BETA_ONE * moment_old_one + (1.0 - BETA_ONE) * grad_now
    second_new = BETA_TWO * moment_old_two + (1.0 - BETA_TWO) * grad_now * grad_now
    ratio = (
        first_new
        / (1.0 - BETA_ONE**STEP)
        / (jnp.sqrt(second_new / (1.0 - BETA_TWO**STEP)) + ADAM_EPS)
    )
    return (first_new, second_new, param_now - step_rate * (ratio + decay_rate * param_now))


def adam_kernel(segments, pieces, held, *refs):
    me = lax.axis_index("ctx")
    grads = refs[:pieces]
    olds = refs[pieces : pieces + 3]
    news = refs[pieces + 3 + held : pieces + 3 + held + 4]
    grad_buf, old_buf, low_buf, in_sem, out_sem = refs[pieces + 3 + held + 4 :]
    base = min(segment[3] for segment in segments)
    loads = []
    for number, (piece, index, first, column, width) in enumerate(segments):
        here = pl.ds(column - base, width)
        there = pl.ds(column, width)
        columns = pl.ds(first, width)
        copies = []
        for number_from, source in enumerate(grads):
            if piece not in (None, number_from):
                continue
            copy = pltpu.make_async_copy(
                source.at[:, columns] if piece is None else source.at[index, :, columns],
                grad_buf.at[:, here],
                in_sem.at[3, number],
            )
            if piece is None:
                pl.when(me == index ^ number_from)(copy.start)
            else:
                copy.start()
        loads.append([copy])
        copies += [
            pltpu.make_async_copy(
                olds[item].at[:, there], old_buf.at[item, :, here], in_sem.at[item, number]
            )
            for item in range(3)
        ]
        for copy in copies:
            copy.start()
        loads[-1] += copies
    stores = []
    for number, (piece, index, first, column, width) in enumerate(segments):
        for copy in loads[number]:
            copy.wait()
        here = pl.ds(column - base, width)
        there = pl.ds(column, width)
        first_new, second_new, master = adam_update(
            old_buf[0, :, here],
            grad_buf[:, here].astype(F32),
            old_buf[1, :, here],
            old_buf[2, :, here],
            LEARN_RATE,
            WEIGHT_DECAY,
        )
        old_buf[0, :, here] = master
        old_buf[1, :, here] = first_new
        old_buf[2, :, here] = second_new
        low_buf[:, here] = master.astype(BF16)
        for item, source in enumerate(
            (
                old_buf.at[1, :, here],
                old_buf.at[2, :, here],
                old_buf.at[0, :, here],
                low_buf.at[:, here],
            )
        ):
            copy = pltpu.make_async_copy(
                source, news[item].at[:, there], out_sem.at[item, number]
            )
            copy.start()
            stores.append(copy)
    for copy in stores:
        copy.wait()


def adam(segments, grads, olds, held, micros):
    rows, columns = olds[0].shape
    span = max(s[3] + s[4] for s in segments) - min(s[3] for s in segments)
    held = [] if held is None else list(held)
    args = list(grads) + list(olds) + held
    return pl.pallas_call(
        functools.partial(adam_kernel, tuple(segments), len(grads), len(held)),
        out_shape=[jax.ShapeDtypeStruct((rows, columns), F32)] * 3
        + [jax.ShapeDtypeStruct((rows, columns), BF16)],
        in_specs=[pl.BlockSpec(memory_space=pl.ANY)] * len(args),
        out_specs=[pl.BlockSpec(memory_space=pl.ANY)] * 4,
        input_output_aliases={len(grads) + 3 + item: item for item in range(len(held))},
        scratch_shapes=[
            pltpu.VMEM((rows, span), BF16),
            pltpu.VMEM((3, rows, span), F32),
            pltpu.VMEM((rows, span), BF16),
            pltpu.SemaphoreType.DMA((4, len(segments))),
            pltpu.SemaphoreType.DMA((4, len(segments))),
        ],
        compiler_params=pltpu.CompilerParams(vmem_limit_bytes=VMEM_LIMIT),
        cost_estimate=cost(micros),
    )(*args)


def head_mean(values, ones):
    high = values.astype(BF16)
    rest = (values - high.astype(F32)).astype(BF16)
    return (dot(high, ones, 1, 0) + dot(rest, ones, 1, 0)) * (1.0 / HD)


def head_ones(width):
    row = lax.broadcasted_iota(jnp.int32, (width, width), 0) // HD
    col = lax.broadcasted_iota(jnp.int32, (width, width), 1) // HD
    return jnp.where(row == col, 1.0, 0.0).astype(BF16)


def partner(values):
    width = values.shape[-1]
    lane = lax.broadcasted_iota(jnp.int32, values.shape, 1)
    return jnp.where(
        lane % HD < HD // 2,
        pltpu.roll(values, width - HD // 2, 1),
        pltpu.roll(values, HD // 2, 1),
    )


def widen(table, width):
    return [
        jnp.concatenate([part] * (width // HD), axis=-1)
        for part in (table[:, :HD], table[:, HD:])
    ]


def doc_first(starts, times):
    first = jnp.zeros_like(times)
    for item in range(starts.shape[0]):
        first = jnp.where(starts[item] <= times, starts[item], first)
    return first


def block_mask(starts, block, keys):
    shape = (keys, GROUP * HALF)
    times = block * HALF + lax.broadcasted_iota(jnp.int32, (1, GROUP * HALF), 1) % HALF
    key = lax.broadcasted_iota(jnp.int32, shape, 0)
    return (key >= doc_first(starts, times)) & (key <= times)


def stack_heads(ref, rows, group):
    return jnp.concatenate(
        [
            ref[rows, (group * GROUP + h) * HD : (group * GROUP + h + 1) * HD]
            for h in range(GROUP)
        ],
        axis=0,
    )


def unstack_heads(turned):
    wide = turned.T
    return [wide[h * HALF : (h + 1) * HALF, :] for h in range(GROUP)]


def attend_kernel(
    blocks,
    groups,
    place,
    order,
    starts,
    table,
    gain,
    normed_in,
    weights_from,
    dy,
    swap_in,
    part,
    qk,
    q,
    k,
    v,
    o_held,
    lse,
    dy_all,
    swap_out,
    normed,
    weights_in,
    joined,
    o,
    send_sem,
    recv_sem,
    local,
):
    sems = (send_sem, recv_sem)
    me = lax.axis_index("ctx")
    qk_width = qk.shape[1]
    q_width = q.shape[1]
    qkv_width = qk_width + v.shape[1]
    ones = head_ones(qk_width)
    meet(("ctx",))
    loads = [
        load(normed_in, normed, local.at[0]),
        load(weights_from, weights_in, local.at[1]),
    ]
    swap_copies = swap_start(swap_in, swap_out, sems, GATHER_SEMS)
    copies = gather_start(dy, dy_all, sems, 0)
    own_copies = [
        load(swap_in.at[me], swap_out.at[me], local.at[2]),
        load(dy, dy_all.at[me], local.at[3]),
    ]
    for copy in loads:
        copy.wait()
    for block in range(blocks):
        joined[block] = dot(
            normed[block * HALF : (block + 1) * HALF, :], weights_in[:, :qkv_width], 1, 0
        )
    for block in range(blocks):
        to = slice(block * HALF, (block + 1) * HALF)
        values = joined[place[block]]
        v[to, :] = values[:, qk_width:].astype(BF16)
        values = values[:, :qk_width]
        qk[to, :] = values
        turned = values * lax.rsqrt(head_mean(values * values, ones) + NORM_EPS) * gain[...]
        cosine, sine = widen(table[to, :], qk_width)
        turned = turned * cosine + partner(turned) * sine
        turned = turned.astype(BF16)
        q[to, :] = turned[:, :q_width]
        k[to, :] = turned[:, q_width:]
    for block in range(blocks):
        rows = slice(block * HALF, (block + 1) * HALF)
        keys = (block + 1) * HALF
        mask = block_mask(starts, block, keys)
        pieces = []
        for group in range(groups):
            lanes = slice(group * HD, (group + 1) * HD)
            queries = stack_heads(q, rows, group)
            scores = dot(k[:keys, lanes], queries, 1, 1) * SCALE
            weights = jnp.where(mask, jnp.exp(scores), 0.0)
            sums = jnp.sum(weights, axis=0, keepdims=True)
            lse[block, group : group + 1, :] = jnp.log(sums)
            mixed = dot(v[:keys, lanes], weights.astype(BF16), 0, 0) / sums
            pieces += unstack_heads(mixed)
        o[block] = jnp.concatenate(pieces, axis=1).astype(BF16)
    for block in range(blocks):
        o_held[block * HALF : (block + 1) * HALF, :] = o[order[block]]
    for first in range(0, D, 512):
        part[:, first : first + 512] = dot(
            o_held[...], weights_in[first : first + 512, qkv_width:], 1, 1
        ).astype(BF16)
    gather_rest(copies, dy_all, sems, 0)
    for copy in swap_copies:
        copy.wait()
    for copy in own_copies:
        copy.wait()


def tail_kernel(
    blocks,
    groups,
    swaps,
    place,
    order,
    starts,
    lse,
    gain,
    attn_gain,
    ffn_gain_grad,
    out_part,
    *refs,
):
    sources, normed, refs = refs[:11], refs[11], refs[12:]
    swap_in, refs = refs[:swaps], refs[swaps:]
    out, grad_tokens, gains, attn_own = refs[:4]
    swap_out, refs = refs[4 : 4 + swaps], refs[4 + swaps :]
    targets, refs = refs[:11], refs[11:]
    grad_all, weights_in, q, k, v, o, qk, table, middle, x, grad_middle = targets
    size = lax.axis_size("ctx")
    count = 3 if size == 4 else 1
    bufs, back_bufs, refs = refs[:count], refs[count : 2 * count], refs[2 * count :]
    do, dq, dkv, joined, turned, part, attn_grad = refs[:7]
    home, travel, owned, ctx_box, fsdp_box = refs[7:12]
    send_one, recv_one, send_two, recv_two, send_three, recv_three = refs[12:18]
    send_four, recv_four, local = refs[18:]
    going, coming = travel.at[0], travel.at[1]
    out_sems, back_sems = (send_one, recv_one), (send_two, recv_two)
    line, small = (send_three, recv_three), (send_four, recv_four)
    me = lax.axis_index("ctx")
    chips = lax.axis_size("fsdp") // 2
    step_base = chips
    swap_base = step_base + 2 * chips
    qk_width = qk.shape[2]
    qkv_width = qk_width + v.shape[1]
    ones = head_ones(qk_width)
    first_load = load(out_part, part, local.at[15])
    meet(("ctx", "fsdp"))
    first_load.wait()
    out_copies = sum_start(part, bufs, out_sems)
    loads = [
        load(source, target, local.at[item])
        for item, (source, target) in enumerate(zip(sources, targets))
    ]
    swap_copies = []
    own_copies = []
    for item in range(swaps):
        swap_copies += swap_start(
            swap_in[item], swap_out[item], line, swap_base + (item + 1) * size
        )
        own_copies.append(
            load(swap_in[item].at[me], swap_out[item].at[me], local.at[13 + item])
        )
    for copy in loads[:6]:
        copy.wait()
    for block in range(blocks):
        do[block * HALF : (block + 1) * HALF, :] = dot(
            grad_all[place[block]], weights_in[:, qkv_width:], 1, 0
        ).astype(BF16)
    for block in range(blocks):
        turned[:, block * HALF : (block + 1) * HALF] = grad_all[block].T
    for first in range(0, D, 512):
        rows = slice(first, first + 512)
        attn_grad[rows, qkv_width:] = dot(turned[rows, :], o[...], 1, 0).astype(BF16)
    loads.append(load(normed, grad_all, local.at[12]))
    dkv[...] = jnp.zeros_like(dkv)
    for block in range(blocks):
        if block == blocks // 2:
            sum_pass(out_copies, part, bufs, out_sems)
        rows = slice(block * HALF, (block + 1) * HALF)
        keys = (block + 1) * HALF
        mask = block_mask(starts, block, keys)
        pieces = []
        dk_add = []
        dv_add = []
        for group in range(groups):
            lanes = slice(group * HD, (group + 1) * HD)
            queries = stack_heads(q, rows, group)
            outs = stack_heads(do, rows, group)
            key_rows = k[:keys, lanes]
            scores = dot(key_rows, queries, 1, 1) * SCALE
            weights = jnp.where(
                mask, jnp.exp(scores - lse[block, group : group + 1, :]), 0.0
            )
            back = dot(v[:keys, lanes], outs, 1, 1)
            delta = jnp.sum(weights * back, axis=0, keepdims=True)
            grads = (weights * (back - delta)).astype(BF16)
            pieces += unstack_heads(dot(key_rows, grads, 0, 0) * SCALE)
            dk_add.append(dot(grads, queries, 1, 0) * SCALE)
            dv_add.append(dot(weights.astype(BF16), outs, 1, 0))
        dq[block] = jnp.concatenate(pieces, axis=1)
        dkv[: block + 1] += jnp.concatenate(dk_add + dv_add, axis=1).reshape(
            (block + 1,) + dkv.shape[1:]
        )
    gain_row = jnp.zeros((1, qk_width), F32)
    for copy in loads[6:]:
        copy.wait()
    for block in range(blocks):
        here = order[block]
        values = qk[here]
        root = lax.rsqrt(head_mean(values * values, ones) + NORM_EPS)
        unit = values * root
        grad_kv = dkv[here]
        kv_width = grad_kv.shape[1] // 2
        grad = jnp.concatenate([dq[here], grad_kv[:, :kv_width]], axis=1)
        cosine, sine = widen(table[here], qk_width)
        grad = grad * cosine - partner(grad) * sine
        gain_row = gain_row + jnp.sum(grad * unit, axis=0, keepdims=True)
        grad = grad * gain[...]
        grad = root * (grad - unit * head_mean(grad * unit, ones))
        joined[block * HALF : (block + 1) * HALF, :] = jnp.concatenate(
            [grad, grad_kv[:, kv_width:]], axis=1
        ).astype(BF16)
    read = sum_rest(out_copies, part, bufs)
    half = middle.shape[0] // 2
    for first in (0, half):
        rows = pl.ds(first, half)
        out[rows, :] = (middle[rows, :] + read(first)).astype(BF16)
    for first in range(0, D, 512):
        part[:, first : first + 512] = dot(
            joined[...], weights_in[first : first + 512, :qkv_width], 1, 1
        ).astype(BF16)
    back_copies = sum_start(part, back_bufs, back_sems)
    for block in range(blocks):
        turned[:, block * HALF : (block + 1) * HALF] = grad_all[block].T
    for first in range(0, D, 512):
        rows = slice(first, first + 512)
        attn_grad[rows, :qkv_width] = dot(turned[rows, :], joined[...], 1, 0).astype(BF16)
    home_copies = line_start(attn_grad, home, line, 0)
    line_home(home_copies, attn_grad, home)
    line_step(chips - 1, home, going, coming, line, step_base)
    sum_pass(back_copies, part, back_bufs, back_sems)
    for reach in range(chips - 2, 0, -1):
        line_step(reach, home, going, coming, line, step_base)
    read = sum_rest(back_copies, part, back_bufs)
    total = jnp.zeros((1, D), F32)
    for first in (0, half):
        rows = pl.ds(first, half)
        values = x[rows, :].astype(F32)
        root = row_scale(values)
        unit = values * root
        back = read(first)
        total = total + jnp.sum(back * unit, axis=0, keepdims=True)
        back = back * attn_gain[...]
        back = root * (back - unit * jnp.mean(back * unit, axis=-1, keepdims=True))
        grad_tokens[rows, :] = grad_middle[rows, :] + back
    line_end(home_copies, home, going, coming, line, step_base)
    chip = lax.axis_index("fsdp") // 2
    owned_rows = owned.shape[1]
    for index in range(size):
        owned[index] = home[chip, index * owned_rows : (index + 1) * owned_rows, :]
    swap_copies += swap_start(owned, attn_own, line, swap_base)
    attn_own[me] = owned[me]
    base = 0
    for axis, box in (("ctx", ctx_box), ("fsdp", fsdp_box)):
        axis_size = lax.axis_size(axis)
        index = lax.axis_index(axis)
        if axis == "ctx":
            box[index] = jnp.concatenate(
                [
                    total,
                    ffn_gain_grad[...],
                    jnp.concatenate([gain_row, jnp.zeros((1, D - qk_width), F32)], axis=1),
                    jnp.zeros((5, D), F32),
                ],
                axis=0,
            )
        else:
            box[index] = summed
        copies = [
            send(
                box.at[index],
                box.at[index],
                small,
                base + step,
                {axis: lax.rem(index + step, axis_size)},
            )
            for step in range(1, axis_size)
        ]
        for copy in copies:
            copy.wait()
        base += axis_size
        summed = box[0]
        for item in range(1, axis_size):
            summed = summed + box[item]
    gains[...] = summed
    for copy in swap_copies:
        copy.wait()
    for copy in own_copies:
        copy.wait()


def rms_scale(values_in, gain_vec):
    return (
        values_in
        * lax.rsqrt(jnp.mean(values_in * values_in, axis=-1, keepdims=True) + NORM_EPS)
        * gain_vec
    )


def inverse_freq():
    return 1.0 / ROPE_BASE ** (jnp.arange(0, HD, 2).astype(F32) / HD)


def shards(
    tokens,
    cotangent,
    doc_starts,
    block_order,
    master_weights,
    moment_one,
    moment_two,
    gains,
    gains_moment_one,
    gains_moment_two,
):
    nctx = lax.axis_size("ctx")
    nfsdp = lax.axis_size("fsdp")
    own_rows = master_weights.shape[0]
    tok_rows = tokens.shape[1]
    stream_len = tok_rows * nctx
    blocks = stream_len // HALF
    groups = KVHEADS // nctx
    q_width = D // nctx
    kv_width = KVD // nctx
    qk_width = q_width + kv_width
    qkv_width = qk_width + kv_width
    tiles = FF // 128
    ff_tiles = -(-tiles // nctx)
    ff_width = ff_tiles * 128
    bundles = 2
    cuts = [0, (ff_tiles * 5 + 3) // 7 * 128, ff_width]

    low = master_weights.astype(BF16)

    def ff_part(base, index, start, stop):
        first = index * ff_width + start
        last = index * ff_width + stop
        real_first, real_last = min(first, FF), min(last, FF)
        part = low[:, base + real_first : base + real_last]
        if real_last - real_first < last - first:
            part = jnp.pad(part, ((0, 0), (0, (last - first) - (real_last - real_first))))
        return part

    def attn_part(index):
        return jnp.concatenate(
            [
                low[:, index * q_width : (index + 1) * q_width],
                low[:, D + index * kv_width : D + (index + 1) * kv_width],
                low[:, D + KVD + index * kv_width : D + KVD + (index + 1) * kv_width],
                low[:, QKVC + index * q_width : QKVC + (index + 1) * q_width],
            ],
            axis=1,
        )

    gate_base = QKVC + D
    bases = (gate_base, gate_base + FF, gate_base + 2 * FF)
    attn_send = jnp.stack([attn_part(c) for c in range(nctx)])
    ff_send = [
        jnp.stack(
            [
                jnp.concatenate(
                    [ff_part(base, c, cuts[b], cuts[b + 1]) for base in bases], axis=1
                )
                for c in range(nctx)
            ]
        )
        for b in range(bundles)
    ]

    def gather_rows(piece):
        return lax.all_gather(
            piece.reshape(nctx * own_rows, piece.shape[-1]), "fsdp", axis=0, tiled=True
        )

    def spread(active):
        return (
            active.reshape(active.shape[0], nctx, nfsdp, own_rows)
            .transpose(0, 2, 1, 3)
            .reshape(active.shape[0], D)
        )

    def unspread(active):
        return (
            active.reshape(active.shape[0], nfsdp, nctx, own_rows)
            .transpose(0, 2, 1, 3)
            .reshape(active.shape[0], D)
        )

    dma = pltpu.SemaphoreType.DMA
    all_low = jax.ShapeDtypeStruct((nctx, tok_rows, D), BF16)
    own_low = jax.ShapeDtypeStruct((tok_rows, D), BF16)
    own_f32 = jax.ShapeDtypeStruct((tok_rows, D), F32)
    row_f32 = jax.ShapeDtypeStruct((1, D), F32)
    g_attn = spread(gains[None, :D])
    g_ffn = spread(gains[None, D : 2 * D])
    order = block_order.reshape(blocks)
    place = jnp.argsort(order).astype(jnp.int32)
    starts = doc_starts[0]

    (attn_held,) = exchange(("swap",), [attn_send], 0, 10)
    w_attn = gather_rows(attn_held)
    first_send, attn_held = lax.optimization_barrier((ff_send[0], attn_held))
    (first_held,) = exchange(("swap",), [first_send], 1, 16)
    table_shape = jax.ShapeDtypeStruct((stream_len, 2 * HD), F32)
    origin = spread(jnp.arange(D, dtype=jnp.int32)[None])
    starts_late, first_held = lax.optimization_barrier((starts, first_held))
    x_low, dy_low, table, normed_all = remote_call(
        first_kernel,
        [own_low, own_low, table_shape, all_low],
        (
            starts_late,
            origin,
            tokens[0],
            cotangent[0],
            g_attn,
            jnp.tile(inverse_freq(), 4)[None],
        ),
        2,
        33,
        [
            pltpu.VMEM((D, D), BF16),
            pltpu.VMEM((tok_rows, D), BF16),
            dma((GATHER_SEMS,)),
            dma((GATHER_SEMS,)),
            dma,
        ],
        (3,),
        1,
    )
    normed_all = normed_all.reshape(stream_len, D)

    g_query = gains[2 * D : 2 * D + HD]
    g_key = gains[2 * D + HD :]
    qk_gain = jnp.concatenate(
        [jnp.tile(g_query, q_width // HD), jnp.tile(g_key, kv_width // HD)]
    )[None]

    low_stream = pltpu.VMEM((stream_len, D), BF16)
    heads_low = pltpu.VMEM((stream_len, q_width), BF16)
    part, qk, q, k, v, mixed, lse, dy_all, second_held = remote_call(
        functools.partial(attend_kernel, blocks, groups),
        [
            jax.ShapeDtypeStruct((stream_len, D), BF16),
            jax.ShapeDtypeStruct((stream_len, qk_width), F32),
            jax.ShapeDtypeStruct((stream_len, q_width), BF16),
            jax.ShapeDtypeStruct((stream_len, kv_width), BF16),
            jax.ShapeDtypeStruct((stream_len, kv_width), BF16),
            jax.ShapeDtypeStruct((stream_len, q_width), BF16),
            jax.ShapeDtypeStruct((blocks, groups, GROUP * HALF), F32),
            all_low,
            jax.ShapeDtypeStruct(ff_send[1].shape, BF16),
        ],
        (place, order, starts, table, qk_gain, normed_all, w_attn, dy_low, ff_send[1]),
        3,
        42,
        [
            low_stream,
            pltpu.VMEM(w_attn.shape, BF16),
            pltpu.VMEM((blocks, HALF, qkv_width), F32),
            pltpu.VMEM((blocks, HALF, q_width), BF16),
            dma((GATHER_SEMS + nctx,)),
            dma((GATHER_SEMS + nctx,)),
            dma((4,)),
        ],
        (7, 8),
        3,
        4,
    )
    dy_all = dy_all.reshape(stream_len, D)
    w_ff = [gather_rows(first_held), gather_rows(second_held)]
    sum_bufs = sum_scratch(nctx, tok_rows)
    sum_sems = [dma((GATHER_SEMS,)), dma((GATHER_SEMS,))]
    norm_scratch = (
        sum_bufs + [pltpu.VMEM((tok_rows, D), BF16)] + sum_sems + sum_sems + [dma]
    )

    middle, normed_two_all = remote_call(
        middle_kernel,
        [own_f32, all_low],
        (part, x_low, g_ffn),
        4,
        57,
        norm_scratch,
        (1,),
    )
    normed_two_all = normed_two_all.reshape(stream_len, D)

    def sum_rows(grad):
        return lax.psum_scatter(grad, "fsdp", scatter_dimension=0, tiled=True).reshape(
            nctx, own_rows, grad.shape[-1]
        )

    def feed(b, x_all, dy):
        width = cuts[b + 1] - cuts[b]
        w_gu, w_down = w_ff[b][:, : 2 * width], w_ff[b][:, 2 * width :]
        gate_up = dot(x_all, w_gu, 1, 0).astype(BF16)
        gate, up = gate_up[:, :width].astype(F32), gate_up[:, width:].astype(F32)
        gated = jax.nn.sigmoid(gate)
        act = gate * gated
        hidden = (act * up).astype(BF16)
        back_hidden = dot(dy, w_down, 1, 0)
        grad_gu = jnp.concatenate(
            [back_hidden * up * (gated + act * (1.0 - gated)), back_hidden * act], axis=1
        ).astype(BF16)
        return hidden, grad_gu, dot(grad_gu, w_gu, 1, 1)

    hidden_one, grad_gu, back_partial = feed(0, normed_two_all, dy_all)
    gu_grad = dot(normed_two_all, grad_gu, 0, 0).astype(BF16)
    gu_grad, back_partial, w_ff[1] = lax.optimization_barrier((gu_grad, back_partial, w_ff[1]))
    width_two = cuts[2] - cuts[1]
    hidden_two, grad_gu, back_more = feed(1, normed_two_all, dy_all)
    back_partial = (back_partial + back_more).astype(BF16)
    gu_sum = sum_rows(gu_grad)
    chips = nfsdp // 2

    def line_scratch(columns):
        block = (nctx * own_rows, columns)
        return [pltpu.VMEM((chips,) + block, BF16), pltpu.VMEM((2, 2, chips - 1) + block, BF16)]

    grad_middle, grad_g_ffn, down_sum, grad_middle_all, last_grad, out_partial = remote_call(
        middle_back_kernel,
        [
            own_f32,
            row_f32,
            jax.ShapeDtypeStruct((nctx, own_rows, cuts[1]), BF16),
            all_low,
            jax.ShapeDtypeStruct((D, 3 * width_two), BF16),
            jax.ShapeDtypeStruct((stream_len, D), BF16),
        ],
        (
            back_partial,
            middle,
            dy_low,
            g_ffn,
            normed_two_all,
            dy_all,
            hidden_one,
            hidden_two,
            grad_gu,
            w_ff[0],
            w_ff[1],
        ),
        5,
        57,
        sum_bufs
        + [
            pltpu.VMEM((tok_rows, D), BF16),
            low_stream,
            pltpu.VMEM((stream_len, 2 * width_two), BF16),
            pltpu.VMEM((D, stream_len), BF16),
            pltpu.VMEM((D, 3 * width_two), BF16),
            pltpu.VMEM((D, cuts[1]), BF16),
            low_stream,
            pltpu.VMEM((stream_len, cuts[1]), BF16),
            pltpu.VMEM((stream_len, width_two), BF16),
            pltpu.VMEM((D, cuts[1]), BF16),
            pltpu.VMEM((D, width_two), BF16),
        ]
        + line_scratch(cuts[1])
        + sum_sems
        + sum_sems
        + [dma((3 * chips,)), dma((3 * chips,)), dma((10,))],
        (3, 4, 5),
        0,
        7,
    )
    last_sum = sum_rows(last_grad)

    small = dma((nctx + nfsdp,))
    line_sems = dma((3 * chips + 3 * nctx,))
    own_shape = (nctx, own_rows, qkv_width + q_width)
    sources = (
        grad_middle_all.reshape(blocks, HALF, D),
        w_attn,
        q,
        k,
        v,
        mixed,
        qk.reshape(blocks, HALF, qk_width),
        table.reshape(blocks, HALF, 2 * HD),
        middle,
        x_low,
        grad_middle,
    )
    out_tokens, grad_tokens, gain_sums, attn_own, gu_own, down_own = remote_call(
        functools.partial(tail_kernel, blocks, groups, 2),
        [
            own_low,
            own_f32,
            jax.ShapeDtypeStruct((8, D), F32),
            jax.ShapeDtypeStruct(own_shape, BF16),
            jax.ShapeDtypeStruct(gu_sum.shape, BF16),
            jax.ShapeDtypeStruct(down_sum.shape, BF16),
        ],
        (place, order, starts, lse, qk_gain, g_attn, grad_g_ffn, out_partial)
        + sources
        + (normed_all.reshape(blocks, HALF, D), gu_sum, down_sum),
        6,
        90,
        [pltpu.VMEM(source.shape, source.dtype) for source in sources]
        + sum_bufs
        + sum_bufs
        + [
            heads_low,
            pltpu.VMEM((blocks, HALF, q_width), F32),
            pltpu.VMEM((blocks, HALF, 2 * kv_width), F32),
            pltpu.VMEM((stream_len, qkv_width), BF16),
            pltpu.VMEM((D, stream_len), BF16),
            low_stream,
            pltpu.VMEM((D, qkv_width + q_width), BF16),
        ]
        + line_scratch(qkv_width + q_width)
        + [
            pltpu.VMEM(own_shape, BF16),
            pltpu.VMEM((nctx, 8, D), F32),
            pltpu.VMEM((nfsdp, 8, D), F32),
        ]
        + sum_sems
        + sum_sems
        + [line_sems, line_sems, small, small, dma((16,))],
        (4, 5),
        3,
        15,
    )
    last_sum, gain_sums = lax.optimization_barrier((last_sum, gain_sums))
    out_tokens = unspread(out_tokens)[None]
    grad_tokens = unspread(grad_tokens)[None]
    gain_grad = jnp.concatenate(
        [
            unspread(gain_sums[:1])[0],
            unspread(gain_sums[1:2])[0],
            jnp.sum(gain_sums[2, :q_width].reshape(-1, HD), axis=0),
            jnp.sum(gain_sums[2, q_width:qk_width].reshape(-1, HD), axis=0),
        ]
    )

    olds = (master_weights, moment_one, moment_two)

    def feed_segments(b, pieces):
        width = cuts[b + 1] - cuts[b]
        found = []
        for part in range(3):
            for c in range(nctx):
                column = c * ff_width + cuts[b]
                real = min(max(FF - column, 0), width)
                if real:
                    piece, first = pieces[part]
                    found.append((piece, c, first, bases[part] + column, real))
        return found

    width_one = cuts[1]
    last_own = [
        lax.ppermute(
            lax.dynamic_index_in_dim(last_sum, lax.axis_index("ctx") ^ k, 0, keepdims=False),
            "ctx",
            [(c, c ^ k) for c in range(nctx)],
        )
        if k
        else lax.dynamic_index_in_dim(last_sum, lax.axis_index("ctx"), 0, keepdims=False)
        for k in range(nctx)
    ]
    news = adam(
        feed_segments(0, ((0, 0), (0, width_one), (1, 0))), [gu_own, down_own], olds, None, 7
    )
    parts = (
        (0, 0, q_width),
        (q_width, D, kv_width),
        (qk_width, D + KVD, kv_width),
        (qkv_width, QKVC, q_width),
    )
    if kv_width % 128:
        attn_own = jnp.concatenate(
            [attn_own[c, :, f : f + w] for f, _, w in parts for c in range(nctx)], axis=1
        )[None]
        segments = [(0, 0, 0, 0, gate_base)]
    else:
        segments = [
            (0, c, first, base + c * width, width)
            for first, base, width in parts
            for c in range(nctx)
        ]
    news = adam(segments, [attn_own], olds, news, 3)
    first_new, second_new, master_new, low_new = adam(
        feed_segments(1, ((None, 0), (None, width_two), (None, 2 * width_two))),
        last_own,
        olds,
        news,
        6,
    )
    gain_first, gain_second, gain_new = adam_update(
        gains, gain_grad, gains_moment_one, gains_moment_two, GAIN_RATE, 0.0
    )
    return (
        out_tokens,
        grad_tokens,
        first_new,
        second_new,
        master_new,
        low_new,
        gain_first,
        gain_second,
        gain_new,
    )


def solution(mesh):
    rows = P("fsdp", "ctx", None)
    weights = P(("ctx", "fsdp"), None)
    return jax.shard_map(
        shards,
        mesh=mesh,
        in_specs=(rows, rows, P("fsdp", None), P(), weights, weights, weights, P(), P(), P()),
        out_specs=(rows, rows, weights, weights, weights, weights, P(), P(), P()),
        check_vma=False,
    )
```

```python
import functools

import jax
import jax.numpy as jnp
from jax import lax
from jax.experimental import pallas as pl
from jax.experimental.pallas import tpu as pltpu
from jax.sharding import PartitionSpec as P

D = 1536
HEADS = 24
KVHEADS = 8
HD = 64
FF = 6912
STEP = 10
HALF = 128
KVD = 512
QKVC = 2560
GROUP = HEADS // KVHEADS

ROPE_BASE = 1000000.0
NORM_EPS = 1e-05
BETA_ONE = 0.9
BETA_TWO = 0.95
ADAM_EPS = 1e-08
WEIGHT_DECAY = 0.1
LEARN_RATE = 0.03
GAIN_RATE = 0.5
SCALE = HD ** (-0.5)
MESH = pl.DeviceIdType.MESH
F32 = jnp.float32
BF16 = jnp.bfloat16
VMEM_LIMIT = 60 * 1024 * 1024


def dot(left, right, left_dim, right_dim):
    return lax.dot_general(
        left, right, (((left_dim,), (right_dim,)), ((), ())), preferred_element_type=F32
    )


def send(source, target, sems, item, peer):
    copy = pltpu.make_async_remote_copy(
        src_ref=source,
        dst_ref=target,
        send_sem=sems[0].at[item],
        recv_sem=sems[1].at[item],
        device_id=peer,
        device_id_type=MESH,
    )
    copy.start()
    return copy


def meet(axes):
    barrier = pltpu.get_barrier_semaphore()
    total = 0
    for axis in axes:
        size = lax.axis_size(axis)
        me = lax.axis_index(axis)
        for step in range(1, size):
            pl.semaphore_signal(
                barrier,
                inc=1,
                device_id={axis: lax.rem(me + step, size)},
                device_id_type=MESH,
            )
        total += size - 1
    pl.semaphore_wait(barrier, total)


def square():
    me = lax.axis_index("ctx")
    return me, me + 1 - 2 * lax.rem(me, 2), lax.rem(me + 2, 4), 3 - me


def swap_start(source, target, sems, base):
    size = lax.axis_size("ctx")
    me = lax.axis_index("ctx")
    copies = []
    for step in range(1, size):
        peer = lax.rem(me + step, size)
        copies.append(
            send(source.at[peer], target.at[me], sems, base + step, {"ctx": peer})
        )
    return copies


def gather_start(source, target, sems, base):
    size = lax.axis_size("ctx")
    me = lax.axis_index("ctx")
    if size != 4:
        return [
            send(
                source,
                target.at[me],
                sems,
                base + step,
                {"ctx": lax.rem(me + step, size)},
            )
            for step in range(1, size)
        ]
    me, side, over, across = square()
    half = source.shape[0] // 2
    top, low = pl.ds(0, half), pl.ds(half, half)
    return [
        send(source.at[top], target.at[me, top], sems, base, {"ctx": side}),
        send(source.at[low], target.at[me, low], sems, base + 1, {"ctx": over}),
        send(source.at[low], target.at[me, low], sems, base + 2, {"ctx": side}),
        send(source.at[top], target.at[me, top], sems, base + 3, {"ctx": over}),
    ]


def gather_pass(copies, target, sems, base):
    if lax.axis_size("ctx") != 4:
        return
    me, side, over, across = square()
    half = target.shape[1] // 2
    top, low = pl.ds(0, half), pl.ds(half, half)
    copies[0].wait_recv()
    copies.append(send(target.at[side, top], target.at[side, top], sems, base + 4, {"ctx": over}))
    copies[1].wait_recv()
    copies.append(send(target.at[over, low], target.at[over, low], sems, base + 5, {"ctx": side}))


def gather_end(copies):
    if lax.axis_size("ctx") != 4:
        for copy in copies:
            copy.wait()
        return
    for copy in copies:
        copy.wait_send()
    for copy in copies[2:]:
        copy.wait_recv()


def gather_rest(copies, target, sems, base):
    gather_pass(copies, target, sems, base)
    gather_end(copies)


def load(source, target, sem):
    copy = pltpu.make_async_copy(source, target, sem)
    copy.start()
    return copy


GATHER_SEMS = 8


def exchange_kernel(kinds, *refs):
    count = len(kinds)
    ins, outs = refs[:count], refs[count : 2 * count]
    send_sem, recv_sem, local_sem = refs[2 * count :]
    sems = (send_sem, recv_sem)
    me = lax.axis_index("ctx")
    meet(("ctx",))
    copies = []
    own = []
    for item in range(count):
        base = item * GATHER_SEMS
        if kinds[item] == "gather":
            copies.append(gather_start(ins[item], outs[item], sems, base))
            source = ins[item]
        else:
            copies.append(swap_start(ins[item], outs[item], sems, base))
            source = ins[item].at[me]
        copy = pltpu.make_async_copy(source, outs[item].at[me], local_sem.at[item])
        copy.start()
        own.append(copy)
    for item in range(count):
        if kinds[item] == "gather":
            gather_rest(copies[item], outs[item], sems, item * GATHER_SEMS)
        else:
            for copy in copies[item]:
                copy.wait()
    for copy in own:
        copy.wait()


def remote_params(collective_id):
    return pltpu.CompilerParams(
        collective_id=collective_id, has_side_effects=True, vmem_limit_bytes=VMEM_LIMIT
    )


def cost(micros):
    return pl.CostEstimate(flops=0, bytes_accessed=int(micros * 3.0e6), transcendentals=0)


def exchange(kinds, arrays, collective_id, micros):
    size = lax.axis_size("ctx")
    shapes = [
        jax.ShapeDtypeStruct((size,) + a.shape if kind == "gather" else a.shape, a.dtype)
        for kind, a in zip(kinds, arrays)
    ]
    sems = pltpu.SemaphoreType.DMA((len(arrays) * GATHER_SEMS,))
    return pl.pallas_call(
        functools.partial(exchange_kernel, kinds),
        out_shape=shapes,
        in_specs=[pl.BlockSpec(memory_space=pl.ANY)] * len(arrays),
        out_specs=[pl.BlockSpec(memory_space=pl.ANY)] * len(arrays),
        scratch_shapes=[sems, sems, pltpu.SemaphoreType.DMA((len(arrays),))],
        compiler_params=remote_params(collective_id),
        cost_estimate=cost(micros),
    )(*arrays)


def sum_scratch(size, rows):
    if size == 4:
        half = pltpu.VMEM((2, rows // 2, D), BF16)
        return [half, half, pltpu.VMEM((2, rows, D), BF16)]
    return [pltpu.VMEM((size - 1, rows, D), BF16)]


def sum_start(part, bufs, sems):
    size = lax.axis_size("ctx")
    me = lax.axis_index("ctx")
    rows = part.shape[0] // size

    def block(owner, first=0, count=rows):
        return pl.ds(pl.multiple_of(owner * rows + first, rows // 2), count)

    if size != 4:
        copies = []
        for step in range(1, size):
            peer = lax.rem(me + step, size)
            copies.append(
                send(part.at[block(peer)], bufs[0].at[step - 1], sems, step, {"ctx": peer})
            )
        return copies
    me, side, over, across = square()
    half = rows // 2
    relay, _, landed = bufs
    return [
        send(part.at[block(across, 0, half)], relay.at[0], sems, 0, {"ctx": side}),
        send(part.at[block(across, half, half)], relay.at[1], sems, 1, {"ctx": over}),
        send(
            part.at[block(side, 0, half)],
            landed.at[0, pl.ds(0, half)],
            sems,
            2,
            {"ctx": side},
        ),
        send(
            part.at[block(over, half, half)],
            landed.at[1, pl.ds(half, half)],
            sems,
            3,
            {"ctx": over},
        ),
    ]


def sum_pass(copies, part, bufs, sems):
    if lax.axis_size("ctx") != 4:
        return
    rows = part.shape[0] // 4
    half = rows // 2

    def rows_of(owner, first):
        return pl.ds(pl.multiple_of(owner * rows + first, half), half)

    me, side, over, across = square()
    relay, passed, landed = bufs
    copies[0].wait_recv()
    passed[0] = (part[rows_of(over, 0), :].astype(F32) + relay[0].astype(F32)).astype(BF16)
    copies.append(
        send(passed.at[0], landed.at[1, pl.ds(0, half)], sems, 4, {"ctx": over})
    )
    copies[1].wait_recv()
    passed[1] = (part[rows_of(side, half), :].astype(F32) + relay[1].astype(F32)).astype(
        BF16
    )
    copies.append(
        send(passed.at[1], landed.at[0, pl.ds(half, half)], sems, 5, {"ctx": side})
    )


def sum_rest(copies, part, bufs):
    size = lax.axis_size("ctx")
    me = lax.axis_index("ctx")
    rows = part.shape[0] // size
    half = rows // 2

    def rows_of(owner, first):
        return pl.ds(pl.multiple_of(owner * rows + first, half), half)

    if size != 4:
        for copy in copies:
            copy.wait()

        def read(first):
            total = part[rows_of(me, first), :].astype(F32)
            for step in range(1, size):
                total = total + bufs[0][step - 1, pl.ds(first, half), :].astype(F32)
            return total

        return read
    relay, passed, landed = bufs
    for copy in copies:
        copy.wait_send()
    for copy in copies[2:]:
        copy.wait_recv()

    def read(first):
        return (
            part[rows_of(me, first), :].astype(F32)
            + landed[0, pl.ds(first, half), :].astype(F32)
            + landed[1, pl.ds(first, half), :].astype(F32)
        )

    return read


def row_scale(values):
    return lax.rsqrt(jnp.mean(values * values, axis=-1, keepdims=True) + NORM_EPS)


def first_kernel(
    starts, origin, x, dy, gain, freq, x_low, dy_low, table, normed_all, *scratch
):
    move, normed, send_one, recv_one, local = scratch
    me = lax.axis_index("ctx")
    row = lax.broadcasted_iota(jnp.int32, move.shape, 0)
    move[...] = jnp.where(row == origin[...], 1.0, 0.0).astype(BF16)
    values = dot(x[...], move[...], 1, 0)
    x_low[...] = values.astype(BF16)
    normed[...] = (values * row_scale(values) * gain[...]).astype(BF16)
    meet(("ctx",))
    sems = (send_one, recv_one)
    copies = gather_start(normed, normed_all, sems, 0)
    own = load(normed, normed_all.at[me], local)
    dy_low[...] = dot(dy[...], move[...], 1, 0).astype(BF16)
    gather_pass(copies, normed_all, sems, 0)
    times = lax.broadcasted_iota(jnp.int32, (table.shape[0], 1), 0)
    angles = (times - doc_first(starts, times)).astype(F32) * freq[...]
    lane = lax.broadcasted_iota(jnp.int32, angles.shape, 1)
    sine = jnp.sin(angles)
    sine = jnp.where(lane % HD < HD // 2, -sine, sine)
    table[...] = jnp.where(lane < HD, jnp.cos(angles), sine)
    gather_end(copies)
    own.wait()


def middle_kernel(part, x, gain, middle, normed_all, *scratch):
    bufs, (normed, send_one, recv_one, send_two, recv_two, local) = scratch[:-6], scratch[-6:]
    me = lax.axis_index("ctx")
    meet(("ctx",))
    copies = sum_start(part, bufs, (send_one, recv_one))
    sum_pass(copies, part, bufs, (send_one, recv_one))
    read = sum_rest(copies, part, bufs)
    half = x.shape[0] // 2
    for first in (0, half):
        rows = pl.ds(first, half)
        values = x[rows, :].astype(F32) + read(first)
        middle[rows, :] = values
        normed[rows, :] = (values * row_scale(values) * gain[...]).astype(BF16)
    sems = (send_two, recv_two)
    copies = gather_start(normed, normed_all, sems, 0)
    own = load(normed, normed_all.at[me], local)
    gather_rest(copies, normed_all, sems, 0)
    own.wait()


def column_tiles(total, body):
    def step(tile, carry):
        body(pl.multiple_of(tile * 256, 256), 256)
        return carry

    lax.fori_loop(0, total // 256, step, 0)
    if total % 256:
        body(total - total % 256, total % 256)


def turn(source, target):
    for first in range(0, source.shape[0], HALF):
        rows = slice(first, first + HALF)
        target[:, rows] = source[rows, :].T


def middle_back_kernel(
    part,
    middle,
    dy,
    gain,
    x_all,
    dy_all,
    hidden_one,
    hidden_two,
    grad_gu,
    w_one,
    w_two,
    grad,
    gain_grad,
    grad_all,
    weight_grad,
    out,
    *scratch,
):
    bufs = scratch[:-15]
    low, x_buf, gu_buf, turned, weight_buf, out_buf = scratch[-15:-9]
    hidden_bufs, down_bufs = scratch[-9:-7], scratch[-7:-5]
    send_one, recv_one, send_two, recv_two, local = scratch[-5:]
    me = lax.axis_index("ctx")
    meet(("ctx",))
    copies = sum_start(part, bufs, (send_one, recv_one))
    width_one, width_two = hidden_one.shape[1], hidden_two.shape[1]
    gu_width = grad_gu.shape[1]
    loads = [
        load(source, target, local.at[item])
        for item, (source, target) in enumerate(
            (
                (dy_all, x_buf),
                (hidden_one, hidden_bufs[0]),
                (hidden_two, hidden_bufs[1]),
                (grad_gu, gu_buf),
                (w_one.at[:, pl.ds(2 * width_one, width_one)], down_bufs[0]),
                (w_two.at[:, pl.ds(2 * width_two, width_two)], down_bufs[1]),
            )
        )
    ]
    loads[0].wait()
    turn(x_buf, turned)
    loads.append(load(x_all, x_buf, local.at[6]))
    loads[1].wait()

    def product(target, column, right):
        def tile(first, width):
            target[:, pl.ds(column + first, width)] = dot(
                turned[...], right[:, pl.ds(first, width)], 1, 0
            ).astype(BF16)

        column_tiles(right.shape[1], tile)

    product(weight_buf, gu_width, hidden_bufs[0])
    sum_pass(copies, part, bufs, (send_one, recv_one))
    loads[2].wait()
    product(weight_buf, gu_width + width_one, hidden_bufs[1])
    loads[6].wait()
    turn(x_buf, turned)
    loads[3].wait()
    product(weight_buf, 0, gu_buf)
    stores = [load(weight_buf, weight_grad, local.at[7])]
    read = sum_rest(copies, part, bufs)
    half = dy.shape[0] // 2
    total = jnp.zeros((1, D), F32)
    for first in (0, half):
        rows = pl.ds(first, half)
        values = middle[rows, :]
        root = row_scale(values)
        unit = values * root
        back = read(first)
        total = total + jnp.sum(back * unit, axis=0, keepdims=True)
        back = back * gain[...]
        back = root * (back - unit * jnp.mean(back * unit, axis=-1, keepdims=True))
        back = back + dy[rows, :].astype(F32)
        grad[rows, :] = back
        low[rows, :] = back.astype(BF16)
    gain_grad[...] = total
    sems = (send_two, recv_two)
    copies = gather_start(low, grad_all, sems, 0)
    stores.append(load(low, grad_all.at[me], local.at[8]))
    loads[4].wait()
    loads[5].wait()

    def out_tile(first, width):
        columns = pl.ds(first, width)
        out_buf[:, columns] = (
            dot(hidden_bufs[0][...], down_bufs[0][columns, :], 1, 1)
            + dot(hidden_bufs[1][...], down_bufs[1][columns, :], 1, 1)
        ).astype(BF16)

    column_tiles(D, out_tile)
    stores.append(load(out_buf, out, local.at[9]))
    gather_pass(copies, grad_all, sems, 0)
    gather_end(copies)
    for copy in stores:
        copy.wait()


def line_start(grad, home, sems, base):
    me = lax.axis_index("fsdp")
    chips = lax.axis_size("fsdp") // 2
    core = lax.rem(me, 2)
    rows = grad.shape[0] // (2 * chips)
    copies = []
    for chip in range(chips):
        theirs = pl.ds(pl.multiple_of((2 * chip + 1 - core) * rows, rows), rows)
        copies.append(
            send(grad.at[theirs], home.at[chip], sems, base + chip, {"fsdp": me + 1 - 2 * core})
        )
    return copies


def line_home(copies, grad, home):
    me = lax.axis_index("fsdp")
    chips = lax.axis_size("fsdp") // 2
    core = lax.rem(me, 2)
    rows = grad.shape[0] // (2 * chips)
    for chip in range(chips):
        copies[chip].wait_recv()
        mine = pl.ds(pl.multiple_of((2 * chip + core) * rows, rows), rows)
        home[chip] = (home[chip].astype(F32) + grad[mine, :].astype(F32)).astype(BF16)


def line_copies(reach, going, coming, sems, base):
    me = lax.axis_index("fsdp")
    chips = lax.axis_size("fsdp") // 2
    chip = me // 2
    found = []
    for side, way in ((0, 1), (1, -1)):
        copy = pltpu.make_async_remote_copy(
            src_ref=going.at[side, reach - 1],
            dst_ref=coming.at[side, reach - 1],
            send_sem=sems[0].at[base + 2 * reach + side],
            recv_sem=sems[1].at[base + 2 * reach + side],
            device_id={"fsdp": lax.rem(me + 2 * way + 2 * chips, 2 * chips)},
            device_id_type=MESH,
        )
        if way == 1:
            sent = chip + reach <= chips - 1
            got = (chip >= 1) & (chip + reach <= chips)
            more = (chip >= 1) & sent
        else:
            sent = chip >= reach
            got = (chip <= chips - 2) & (chip + 1 >= reach)
            more = (chip <= chips - 2) & sent
        found.append((side, way, copy, sent, got, more))
    return found


def line_step(reach, home, going, coming, sems, base):
    me = lax.axis_index("fsdp")
    chips = lax.axis_size("fsdp") // 2
    chip = me // 2
    if reach < chips - 1:
        for _, _, copy, _, got, _ in line_copies(reach + 1, going, coming, sems, base):
            pl.when(got)(copy.wait_recv)
    for side, way, copy, sent, _, more in line_copies(reach, going, coming, sems, base):

        @pl.when(sent)
        def _(side=side, way=way, copy=copy, more=more):
            value = home[chip + way * reach]
            if reach < chips - 1:

                @pl.when(more)
                def _():
                    going[side, reach - 1] = (
                        value.astype(F32) + coming[side, reach].astype(F32)
                    ).astype(BF16)

                @pl.when(jnp.logical_not(more))
                def _():
                    going[side, reach - 1] = value

            else:
                going[side, reach - 1] = value
            copy.start()


def line_end(copies, home, going, coming, sems, base):
    me = lax.axis_index("fsdp")
    chips = lax.axis_size("fsdp") // 2
    chip = me // 2
    for side, _, copy, _, got, _ in line_copies(1, going, coming, sems, base):

        @pl.when(got)
        def _(side=side, copy=copy):
            copy.wait_recv()
            home[chip] = (home[chip].astype(F32) + coming[side, 0].astype(F32)).astype(BF16)

    for copy in copies:
        copy.wait_send()
    for reach in range(1, chips):
        for _, _, copy, sent, _, _ in line_copies(reach, going, coming, sems, base):
            pl.when(sent)(copy.wait_send)


def remote_call(
    kernel, out_shape, args, collective_id, micros, scratch, in_hbm=(), smem=0, args_in_hbm=0
):
    return pl.pallas_call(
        kernel,
        out_shape=out_shape,
        in_specs=[pl.BlockSpec(memory_space=pltpu.SMEM)] * smem
        + [pl.BlockSpec(memory_space=pltpu.VMEM)] * (len(args) - smem - args_in_hbm)
        + [pl.BlockSpec(memory_space=pl.ANY)] * args_in_hbm,
        out_specs=[
            pl.BlockSpec(memory_space=pl.ANY if item in in_hbm else pltpu.VMEM)
            for item in range(len(out_shape))
        ],
        scratch_shapes=scratch,
        compiler_params=remote_params(collective_id),
        cost_estimate=cost(micros),
    )(*args)


def adam_update(param_now, grad_now, moment_old_one, moment_old_two, step_rate, decay_rate):
    first_new = BETA_ONE * moment_old_one + (1.0 - BETA_ONE) * grad_now
    second_new = BETA_TWO * moment_old_two + (1.0 - BETA_TWO) * grad_now * grad_now
    ratio = (
        first_new
        / (1.0 - BETA_ONE**STEP)
        / (jnp.sqrt(second_new / (1.0 - BETA_TWO**STEP)) + ADAM_EPS)
    )
    return (first_new, second_new, param_now - step_rate * (ratio + decay_rate * param_now))


def adam_kernel(segments, pieces, held, *refs):
    me = lax.axis_index("ctx")
    grads = refs[:pieces]
    olds = refs[pieces : pieces + 3]
    news = refs[pieces + 3 + held : pieces + 3 + held + 4]
    grad_buf, old_buf, low_buf, in_sem, out_sem = refs[pieces + 3 + held + 4 :]
    base = min(segment[3] for segment in segments)
    loads = []
    for number, (piece, index, first, column, width) in enumerate(segments):
        here = pl.ds(column - base, width)
        there = pl.ds(column, width)
        columns = pl.ds(first, width)
        copies = []
        for number_from, source in enumerate(grads):
            if piece not in (None, number_from):
                continue
            copy = pltpu.make_async_copy(
                source.at[:, columns] if piece is None else source.at[index, :, columns],
                grad_buf.at[:, here],
                in_sem.at[3, number],
            )
            if piece is None:
                pl.when(me == index ^ number_from)(copy.start)
            else:
                copy.start()
        loads.append([copy])
        copies += [
            pltpu.make_async_copy(
                olds[item].at[:, there], old_buf.at[item, :, here], in_sem.at[item, number]
            )
            for item in range(3)
        ]
        for copy in copies:
            copy.start()
        loads[-1] += copies
    stores = []
    for number, (piece, index, first, column, width) in enumerate(segments):
        for copy in loads[number]:
            copy.wait()
        here = pl.ds(column - base, width)
        there = pl.ds(column, width)
        first_new, second_new, master = adam_update(
            old_buf[0, :, here],
            grad_buf[:, here].astype(F32),
            old_buf[1, :, here],
            old_buf[2, :, here],
            LEARN_RATE,
            WEIGHT_DECAY,
        )
        old_buf[0, :, here] = master
        old_buf[1, :, here] = first_new
        old_buf[2, :, here] = second_new
        low_buf[:, here] = master.astype(BF16)
        for item, source in enumerate(
            (
                old_buf.at[1, :, here],
                old_buf.at[2, :, here],
                old_buf.at[0, :, here],
                low_buf.at[:, here],
            )
        ):
            copy = pltpu.make_async_copy(
                source, news[item].at[:, there], out_sem.at[item, number]
            )
            copy.start()
            stores.append(copy)
    for copy in stores:
        copy.wait()


def adam(segments, grads, olds, held, micros):
    rows, columns = olds[0].shape
    span = max(s[3] + s[4] for s in segments) - min(s[3] for s in segments)
    held = [] if held is None else list(held)
    args = list(grads) + list(olds) + held
    return pl.pallas_call(
        functools.partial(adam_kernel, tuple(segments), len(grads), len(held)),
        out_shape=[jax.ShapeDtypeStruct((rows, columns), F32)] * 3
        + [jax.ShapeDtypeStruct((rows, columns), BF16)],
        in_specs=[pl.BlockSpec(memory_space=pl.ANY)] * len(args),
        out_specs=[pl.BlockSpec(memory_space=pl.ANY)] * 4,
        input_output_aliases={len(grads) + 3 + item: item for item in range(len(held))},
        scratch_shapes=[
            pltpu.VMEM((rows, span), BF16),
            pltpu.VMEM((3, rows, span), F32),
            pltpu.VMEM((rows, span), BF16),
            pltpu.SemaphoreType.DMA((4, len(segments))),
            pltpu.SemaphoreType.DMA((4, len(segments))),
        ],
        compiler_params=pltpu.CompilerParams(vmem_limit_bytes=VMEM_LIMIT),
        cost_estimate=cost(micros),
    )(*args)


def head_mean(values, ones):
    high = values.astype(BF16)
    rest = (values - high.astype(F32)).astype(BF16)
    return (dot(high, ones, 1, 0) + dot(rest, ones, 1, 0)) * (1.0 / HD)


def head_ones(width):
    row = lax.broadcasted_iota(jnp.int32, (width, width), 0) // HD
    col = lax.broadcasted_iota(jnp.int32, (width, width), 1) // HD
    return jnp.where(row == col, 1.0, 0.0).astype(BF16)


def partner(values):
    width = values.shape[-1]
    lane = lax.broadcasted_iota(jnp.int32, values.shape, 1)
    return jnp.where(
        lane % HD < HD // 2,
        pltpu.roll(values, width - HD // 2, 1),
        pltpu.roll(values, HD // 2, 1),
    )


def widen(table, width):
    return [
        jnp.concatenate([part] * (width // HD), axis=-1)
        for part in (table[:, :HD], table[:, HD:])
    ]


def doc_first(starts, times):
    first = jnp.zeros_like(times)
    for item in range(starts.shape[0]):
        first = jnp.where(starts[item] <= times, starts[item], first)
    return first


def block_mask(starts, block, keys):
    shape = (keys, GROUP * HALF)
    times = block * HALF + lax.broadcasted_iota(jnp.int32, (1, GROUP * HALF), 1) % HALF
    key = lax.broadcasted_iota(jnp.int32, shape, 0)
    return (key >= doc_first(starts, times)) & (key <= times)


def stack_heads(ref, rows, group):
    return jnp.concatenate(
        [
            ref[rows, (group * GROUP + h) * HD : (group * GROUP + h + 1) * HD]
            for h in range(GROUP)
        ],
        axis=0,
    )


def unstack_heads(turned):
    wide = turned.T
    return [wide[h * HALF : (h + 1) * HALF, :] for h in range(GROUP)]


def attend_kernel(
    blocks,
    groups,
    place,
    order,
    starts,
    table,
    gain,
    normed_in,
    weights_from,
    dy,
    swap_in,
    part,
    qk,
    q,
    k,
    v,
    o_held,
    lse,
    dy_all,
    swap_out,
    normed,
    weights_in,
    joined,
    o,
    send_sem,
    recv_sem,
    local,
):
    sems = (send_sem, recv_sem)
    me = lax.axis_index("ctx")
    qk_width = qk.shape[1]
    q_width = q.shape[1]
    qkv_width = qk_width + v.shape[1]
    ones = head_ones(qk_width)
    meet(("ctx",))
    loads = [
        load(normed_in, normed, local.at[0]),
        load(weights_from, weights_in, local.at[1]),
    ]
    swap_copies = swap_start(swap_in, swap_out, sems, GATHER_SEMS)
    copies = gather_start(dy, dy_all, sems, 0)
    own_copies = [
        load(swap_in.at[me], swap_out.at[me], local.at[2]),
        load(dy, dy_all.at[me], local.at[3]),
    ]
    for copy in loads:
        copy.wait()
    for block in range(blocks):
        joined[block] = dot(
            normed[block * HALF : (block + 1) * HALF, :], weights_in[:, :qkv_width], 1, 0
        )
    for block in range(blocks):
        to = slice(block * HALF, (block + 1) * HALF)
        values = joined[place[block]]
        v[to, :] = values[:, qk_width:].astype(BF16)
        values = values[:, :qk_width]
        qk[to, :] = values
        turned = values * lax.rsqrt(head_mean(values * values, ones) + NORM_EPS) * gain[...]
        cosine, sine = widen(table[to, :], qk_width)
        turned = turned * cosine + partner(turned) * sine
        turned = turned.astype(BF16)
        q[to, :] = turned[:, :q_width]
        k[to, :] = turned[:, q_width:]
    for block in range(blocks):
        rows = slice(block * HALF, (block + 1) * HALF)
        keys = (block + 1) * HALF
        mask = block_mask(starts, block, keys)
        pieces = []
        for group in range(groups):
            lanes = slice(group * HD, (group + 1) * HD)
            queries = stack_heads(q, rows, group)
            scores = dot(k[:keys, lanes], queries, 1, 1) * SCALE
            weights = jnp.where(mask, jnp.exp(scores), 0.0)
            sums = jnp.sum(weights, axis=0, keepdims=True)
            lse[block, group : group + 1, :] = jnp.log(sums)
            mixed = dot(v[:keys, lanes], weights.astype(BF16), 0, 0) / sums
            pieces += unstack_heads(mixed)
        o[block] = jnp.concatenate(pieces, axis=1).astype(BF16)
    for block in range(blocks):
        o_held[block * HALF : (block + 1) * HALF, :] = o[order[block]]
    for first in range(0, D, 512):
        part[:, first : first + 512] = dot(
            o_held[...], weights_in[first : first + 512, qkv_width:], 1, 1
        ).astype(BF16)
    gather_rest(copies, dy_all, sems, 0)
    for copy in swap_copies:
        copy.wait()
    for copy in own_copies:
        copy.wait()


def tail_kernel(
    blocks,
    groups,
    swaps,
    place,
    order,
    starts,
    lse,
    gain,
    attn_gain,
    ffn_gain_grad,
    out_part,
    *refs,
):
    sources, normed, refs = refs[:11], refs[11], refs[12:]
    swap_in, refs = refs[:swaps], refs[swaps:]
    out, grad_tokens, gains, attn_own = refs[:4]
    swap_out, refs = refs[4 : 4 + swaps], refs[4 + swaps :]
    targets, refs = refs[:11], refs[11:]
    grad_all, weights_in, q, k, v, o, qk, table, middle, x, grad_middle = targets
    size = lax.axis_size("ctx")
    count = 3 if size == 4 else 1
    bufs, back_bufs, refs = refs[:count], refs[count : 2 * count], refs[2 * count :]
    do, dq, dkv, joined, turned, part, attn_grad = refs[:7]
    home, travel, owned, ctx_box, fsdp_box = refs[7:12]
    send_one, recv_one, send_two, recv_two, send_three, recv_three = refs[12:18]
    send_four, recv_four, local = refs[18:]
    going, coming = travel.at[0], travel.at[1]
    out_sems, back_sems = (send_one, recv_one), (send_two, recv_two)
    line, small = (send_three, recv_three), (send_four, recv_four)
    me = lax.axis_index("ctx")
    chips = lax.axis_size("fsdp") // 2
    step_base = chips
    swap_base = step_base + 2 * chips
    qk_width = qk.shape[2]
    qkv_width = qk_width + v.shape[1]
    ones = head_ones(qk_width)
    first_load = load(out_part, part, local.at[15])
    meet(("ctx", "fsdp"))
    first_load.wait()
    out_copies = sum_start(part, bufs, out_sems)
    loads = [
        load(source, target, local.at[item])
        for item, (source, target) in enumerate(zip(sources, targets))
    ]
    swap_copies = []
    own_copies = []
    for item in range(swaps):
        swap_copies += swap_start(
            swap_in[item], swap_out[item], line, swap_base + (item + 1) * size
        )
        own_copies.append(
            load(swap_in[item].at[me], swap_out[item].at[me], local.at[13 + item])
        )
    for copy in loads[:6]:
        copy.wait()
    for block in range(blocks):
        do[block * HALF : (block + 1) * HALF, :] = dot(
            grad_all[place[block]], weights_in[:, qkv_width:], 1, 0
        ).astype(BF16)
    for block in range(blocks):
        turned[:, block * HALF : (block + 1) * HALF] = grad_all[block].T
    for first in range(0, D, 512):
        rows = slice(first, first + 512)
        attn_grad[rows, qkv_width:] = dot(turned[rows, :], o[...], 1, 0).astype(BF16)
    loads.append(load(normed, grad_all, local.at[12]))
    dkv[...] = jnp.zeros_like(dkv)
    for block in range(blocks):
        if block == blocks // 2:
            sum_pass(out_copies, part, bufs, out_sems)
        rows = slice(block * HALF, (block + 1) * HALF)
        keys = (block + 1) * HALF
        mask = block_mask(starts, block, keys)
        pieces = []
        dk_add = []
        dv_add = []
        for group in range(groups):
            lanes = slice(group * HD, (group + 1) * HD)
            queries = stack_heads(q, rows, group)
            outs = stack_heads(do, rows, group)
            key_rows = k[:keys, lanes]
            scores = dot(key_rows, queries, 1, 1) * SCALE
            weights = jnp.where(
                mask, jnp.exp(scores - lse[block, group : group + 1, :]), 0.0
            )
            back = dot(v[:keys, lanes], outs, 1, 1)
            delta = jnp.sum(weights * back, axis=0, keepdims=True)
            grads = (weights * (back - delta)).astype(BF16)
            pieces += unstack_heads(dot(key_rows, grads, 0, 0) * SCALE)
            dk_add.append(dot(grads, queries, 1, 0) * SCALE)
            dv_add.append(dot(weights.astype(BF16), outs, 1, 0))
        dq[block] = jnp.concatenate(pieces, axis=1)
        dkv[: block + 1] += jnp.concatenate(dk_add + dv_add, axis=1).reshape(
            (block + 1,) + dkv.shape[1:]
        )
    gain_row = jnp.zeros((1, qk_width), F32)
    for copy in loads[6:]:
        copy.wait()
    for block in range(blocks):
        here = order[block]
        values = qk[here]
        root = lax.rsqrt(head_mean(values * values, ones) + NORM_EPS)
        unit = values * root
        grad_kv = dkv[here]
        kv_width = grad_kv.shape[1] // 2
        grad = jnp.concatenate([dq[here], grad_kv[:, :kv_width]], axis=1)
        cosine, sine = widen(table[here], qk_width)
        grad = grad * cosine - partner(grad) * sine
        gain_row = gain_row + jnp.sum(grad * unit, axis=0, keepdims=True)
        grad = grad * gain[...]
        grad = root * (grad - unit * head_mean(grad * unit, ones))
        joined[block * HALF : (block + 1) * HALF, :] = jnp.concatenate(
            [grad, grad_kv[:, kv_width:]], axis=1
        ).astype(BF16)
    read = sum_rest(out_copies, part, bufs)
    half = middle.shape[0] // 2
    for first in (0, half):
        rows = pl.ds(first, half)
        out[rows, :] = (middle[rows, :] + read(first)).astype(BF16)
    for first in range(0, D, 512):
        part[:, first : first + 512] = dot(
            joined[...], weights_in[first : first + 512, :qkv_width], 1, 1
        ).astype(BF16)
    back_copies = sum_start(part, back_bufs, back_sems)
    for block in range(blocks):
        turned[:, block * HALF : (block + 1) * HALF] = grad_all[block].T
    for first in range(0, D, 512):
        rows = slice(first, first + 512)
        attn_grad[rows, :qkv_width] = dot(turned[rows, :], joined[...], 1, 0).astype(BF16)
    home_copies = line_start(attn_grad, home, line, 0)
    line_home(home_copies, attn_grad, home)
    line_step(chips - 1, home, going, coming, line, step_base)
    sum_pass(back_copies, part, back_bufs, back_sems)
    for reach in range(chips - 2, 1, -1):
        line_step(reach, home, going, coming, line, step_base)
    read = sum_rest(back_copies, part, back_bufs)
    total = jnp.zeros((1, D), F32)
    for first in (0, half):
        rows = pl.ds(first, half)
        values = x[rows, :].astype(F32)
        root = row_scale(values)
        unit = values * root
        back = read(first)
        total = total + jnp.sum(back * unit, axis=0, keepdims=True)
        back = back * attn_gain[...]
        back = root * (back - unit * jnp.mean(back * unit, axis=-1, keepdims=True))
        grad_tokens[rows, :] = grad_middle[rows, :] + back

    def spread_start(axis, box, value, base):
        index = lax.axis_index(axis)
        axis_size = lax.axis_size(axis)
        box[index] = value
        return [
            send(
                box.at[index],
                box.at[index],
                small,
                base + step,
                {axis: lax.rem(index + step, axis_size)},
            )
            for step in range(1, axis_size)
        ]

    def spread_end(copies, box):
        for copy in copies:
            copy.wait()
        summed = box[0]
        for item in range(1, box.shape[0]):
            summed = summed + box[item]
        return summed

    ctx_copies = spread_start(
        "ctx",
        ctx_box,
        jnp.concatenate(
            [
                total,
                ffn_gain_grad[...],
                jnp.concatenate([gain_row, jnp.zeros((1, D - qk_width), F32)], axis=1),
                jnp.zeros((5, D), F32),
            ],
            axis=0,
        ),
        0,
    )
    line_step(1, home, going, coming, line, step_base)
    fsdp_copies = spread_start("fsdp", fsdp_box, spread_end(ctx_copies, ctx_box), size)
    line_end(home_copies, home, going, coming, line, step_base)
    chip = lax.axis_index("fsdp") // 2
    owned_rows = owned.shape[1]
    for index in range(size):
        owned[index] = home[chip, index * owned_rows : (index + 1) * owned_rows, :]
    swap_copies += swap_start(owned, attn_own, line, swap_base)
    attn_own[me] = owned[me]
    gains[...] = spread_end(fsdp_copies, fsdp_box)
    for copy in swap_copies:
        copy.wait()
    for copy in own_copies:
        copy.wait()


def rms_scale(values_in, gain_vec):
    return (
        values_in
        * lax.rsqrt(jnp.mean(values_in * values_in, axis=-1, keepdims=True) + NORM_EPS)
        * gain_vec
    )


def inverse_freq():
    return 1.0 / ROPE_BASE ** (jnp.arange(0, HD, 2).astype(F32) / HD)


def shards(
    tokens,
    cotangent,
    doc_starts,
    block_order,
    master_weights,
    moment_one,
    moment_two,
    gains,
    gains_moment_one,
    gains_moment_two,
):
    nctx = lax.axis_size("ctx")
    nfsdp = lax.axis_size("fsdp")
    own_rows = master_weights.shape[0]
    tok_rows = tokens.shape[1]
    stream_len = tok_rows * nctx
    blocks = stream_len // HALF
    groups = KVHEADS // nctx
    q_width = D // nctx
    kv_width = KVD // nctx
    qk_width = q_width + kv_width
    qkv_width = qk_width + kv_width
    tiles = FF // 128
    ff_tiles = -(-tiles // nctx)
    ff_width = ff_tiles * 128
    bundles = 2
    cuts = [0, (ff_tiles * 5 + 3) // 7 * 128, ff_width]

    low = master_weights.astype(BF16)

    def ff_part(base, index, start, stop):
        first = index * ff_width + start
        last = index * ff_width + stop
        real_first, real_last = min(first, FF), min(last, FF)
        part = low[:, base + real_first : base + real_last]
        if real_last - real_first < last - first:
            part = jnp.pad(part, ((0, 0), (0, (last - first) - (real_last - real_first))))
        return part

    def attn_part(index):
        return jnp.concatenate(
            [
                low[:, index * q_width : (index + 1) * q_width],
                low[:, D + index * kv_width : D + (index + 1) * kv_width],
                low[:, D + KVD + index * kv_width : D + KVD + (index + 1) * kv_width],
                low[:, QKVC + index * q_width : QKVC + (index + 1) * q_width],
            ],
            axis=1,
        )

    gate_base = QKVC + D
    bases = (gate_base, gate_base + FF, gate_base + 2 * FF)
    attn_send = jnp.stack([attn_part(c) for c in range(nctx)])
    ff_send = [
        jnp.stack(
            [
                jnp.concatenate(
                    [ff_part(base, c, cuts[b], cuts[b + 1]) for base in bases], axis=1
                )
                for c in range(nctx)
            ]
        )
        for b in range(bundles)
    ]

    def gather_rows(piece):
        return lax.all_gather(
            piece.reshape(nctx * own_rows, piece.shape[-1]), "fsdp", axis=0, tiled=True
        )

    def spread(active):
        return (
            active.reshape(active.shape[0], nctx, nfsdp, own_rows)
            .transpose(0, 2, 1, 3)
            .reshape(active.shape[0], D)
        )

    def unspread(active):
        return (
            active.reshape(active.shape[0], nfsdp, nctx, own_rows)
            .transpose(0, 2, 1, 3)
            .reshape(active.shape[0], D)
        )

    dma = pltpu.SemaphoreType.DMA
    all_low = jax.ShapeDtypeStruct((nctx, tok_rows, D), BF16)
    own_low = jax.ShapeDtypeStruct((tok_rows, D), BF16)
    own_f32 = jax.ShapeDtypeStruct((tok_rows, D), F32)
    row_f32 = jax.ShapeDtypeStruct((1, D), F32)
    g_attn = spread(gains[None, :D])
    g_ffn = spread(gains[None, D : 2 * D])
    order = block_order.reshape(blocks)
    place = jnp.argsort(order).astype(jnp.int32)
    starts = doc_starts[0]

    (attn_held,) = exchange(("swap",), [attn_send], 0, 10)
    w_attn = gather_rows(attn_held)
    first_send, attn_held = lax.optimization_barrier((ff_send[0], attn_held))
    (first_held,) = exchange(("swap",), [first_send], 1, 16)
    table_shape = jax.ShapeDtypeStruct((stream_len, 2 * HD), F32)
    origin = spread(jnp.arange(D, dtype=jnp.int32)[None])
    starts_late, first_held = lax.optimization_barrier((starts, first_held))
    x_low, dy_low, table, normed_all = remote_call(
        first_kernel,
        [own_low, own_low, table_shape, all_low],
        (
            starts_late,
            origin,
            tokens[0],
            cotangent[0],
            g_attn,
            jnp.tile(inverse_freq(), 4)[None],
        ),
        2,
        33,
        [
            pltpu.VMEM((D, D), BF16),
            pltpu.VMEM((tok_rows, D), BF16),
            dma((GATHER_SEMS,)),
            dma((GATHER_SEMS,)),
            dma,
        ],
        (3,),
        1,
    )
    normed_all = normed_all.reshape(stream_len, D)

    g_query = gains[2 * D : 2 * D + HD]
    g_key = gains[2 * D + HD :]
    qk_gain = jnp.concatenate(
        [jnp.tile(g_query, q_width // HD), jnp.tile(g_key, kv_width // HD)]
    )[None]

    low_stream = pltpu.VMEM((stream_len, D), BF16)
    heads_low = pltpu.VMEM((stream_len, q_width), BF16)
    part, qk, q, k, v, mixed, lse, dy_all, second_held = remote_call(
        functools.partial(attend_kernel, blocks, groups),
        [
            jax.ShapeDtypeStruct((stream_len, D), BF16),
            jax.ShapeDtypeStruct((stream_len, qk_width), F32),
            jax.ShapeDtypeStruct((stream_len, q_width), BF16),
            jax.ShapeDtypeStruct((stream_len, kv_width), BF16),
            jax.ShapeDtypeStruct((stream_len, kv_width), BF16),
            jax.ShapeDtypeStruct((stream_len, q_width), BF16),
            jax.ShapeDtypeStruct((blocks, groups, GROUP * HALF), F32),
            all_low,
            jax.ShapeDtypeStruct(ff_send[1].shape, BF16),
        ],
        (place, order, starts, table, qk_gain, normed_all, w_attn, dy_low, ff_send[1]),
        3,
        42,
        [
            low_stream,
            pltpu.VMEM(w_attn.shape, BF16),
            pltpu.VMEM((blocks, HALF, qkv_width), F32),
            pltpu.VMEM((blocks, HALF, q_width), BF16),
            dma((GATHER_SEMS + nctx,)),
            dma((GATHER_SEMS + nctx,)),
            dma((4,)),
        ],
        (7, 8),
        3,
        4,
    )
    dy_all = dy_all.reshape(stream_len, D)
    w_ff = [gather_rows(first_held), gather_rows(second_held)]
    sum_bufs = sum_scratch(nctx, tok_rows)
    sum_sems = [dma((GATHER_SEMS,)), dma((GATHER_SEMS,))]
    norm_scratch = (
        sum_bufs + [pltpu.VMEM((tok_rows, D), BF16)] + sum_sems + sum_sems + [dma]
    )

    middle, normed_two_all = remote_call(
        middle_kernel,
        [own_f32, all_low],
        (part, x_low, g_ffn),
        4,
        57,
        norm_scratch,
        (1,),
    )
    normed_two_all = normed_two_all.reshape(stream_len, D)

    def sum_rows(grad):
        return lax.psum_scatter(grad, "fsdp", scatter_dimension=0, tiled=True).reshape(
            nctx, own_rows, grad.shape[-1]
        )

    def feed(b, x_all, dy):
        width = cuts[b + 1] - cuts[b]
        w_gu, w_down = w_ff[b][:, : 2 * width], w_ff[b][:, 2 * width :]
        gate_up = dot(x_all, w_gu, 1, 0).astype(BF16)
        gate, up = gate_up[:, :width].astype(F32), gate_up[:, width:].astype(F32)
        gated = jax.nn.sigmoid(gate)
        act = gate * gated
        hidden = (act * up).astype(BF16)
        back_hidden = dot(dy, w_down, 1, 0)
        grad_gu = jnp.concatenate(
            [back_hidden * up * (gated + act * (1.0 - gated)), back_hidden * act], axis=1
        ).astype(BF16)
        return hidden, grad_gu, dot(grad_gu, w_gu, 1, 1)

    hidden_one, grad_gu, back_partial = feed(0, normed_two_all, dy_all)
    gu_grad = dot(normed_two_all, grad_gu, 0, 0).astype(BF16)
    gu_grad, back_partial, w_ff[1] = lax.optimization_barrier((gu_grad, back_partial, w_ff[1]))
    width_two = cuts[2] - cuts[1]
    hidden_two, grad_gu, back_more = feed(1, normed_two_all, dy_all)
    back_partial = (back_partial + back_more).astype(BF16)
    gu_sum = sum_rows(gu_grad)
    chips = nfsdp // 2

    def line_scratch(columns):
        block = (nctx * own_rows, columns)
        return [pltpu.VMEM((chips,) + block, BF16), pltpu.VMEM((2, 2, chips - 1) + block, BF16)]

    grad_middle, grad_g_ffn, grad_middle_all, last_grad, out_partial = remote_call(
        middle_back_kernel,
        [
            own_f32,
            row_f32,
            all_low,
            jax.ShapeDtypeStruct((D, 2 * width_two + ff_width), BF16),
            jax.ShapeDtypeStruct((stream_len, D), BF16),
        ],
        (
            back_partial,
            middle,
            dy_low,
            g_ffn,
            normed_two_all,
            dy_all,
            hidden_one,
            hidden_two,
            grad_gu,
            w_ff[0],
            w_ff[1],
        ),
        5,
        57,
        sum_bufs
        + [
            pltpu.VMEM((tok_rows, D), BF16),
            low_stream,
            pltpu.VMEM((stream_len, 2 * width_two), BF16),
            pltpu.VMEM((D, stream_len), BF16),
            pltpu.VMEM((D, 2 * width_two + ff_width), BF16),
            low_stream,
            pltpu.VMEM((stream_len, cuts[1]), BF16),
            pltpu.VMEM((stream_len, width_two), BF16),
            pltpu.VMEM((D, cuts[1]), BF16),
            pltpu.VMEM((D, width_two), BF16),
        ]
        + sum_sems
        + sum_sems
        + [dma((10,))],
        (2, 3, 4),
        0,
        7,
    )
    last_sum = sum_rows(last_grad)

    small = dma((nctx + nfsdp,))
    line_sems = dma((3 * chips + 3 * nctx,))
    own_shape = (nctx, own_rows, qkv_width + q_width)
    sources = (
        grad_middle_all.reshape(blocks, HALF, D),
        w_attn,
        q,
        k,
        v,
        mixed,
        qk.reshape(blocks, HALF, qk_width),
        table.reshape(blocks, HALF, 2 * HD),
        middle,
        x_low,
        grad_middle,
    )
    out_tokens, grad_tokens, gain_sums, attn_own, gu_own = remote_call(
        functools.partial(tail_kernel, blocks, groups, 1),
        [
            own_low,
            own_f32,
            jax.ShapeDtypeStruct((8, D), F32),
            jax.ShapeDtypeStruct(own_shape, BF16),
            jax.ShapeDtypeStruct(gu_sum.shape, BF16),
        ],
        (place, order, starts, lse, qk_gain, g_attn, grad_g_ffn, out_partial)
        + sources
        + (normed_all.reshape(blocks, HALF, D), gu_sum),
        6,
        90,
        [pltpu.VMEM(source.shape, source.dtype) for source in sources]
        + sum_bufs
        + sum_bufs
        + [
            heads_low,
            pltpu.VMEM((blocks, HALF, q_width), F32),
            pltpu.VMEM((blocks, HALF, 2 * kv_width), F32),
            pltpu.VMEM((stream_len, qkv_width), BF16),
            pltpu.VMEM((D, stream_len), BF16),
            low_stream,
            pltpu.VMEM((D, qkv_width + q_width), BF16),
        ]
        + line_scratch(qkv_width + q_width)
        + [
            pltpu.VMEM(own_shape, BF16),
            pltpu.VMEM((nctx, 8, D), F32),
            pltpu.VMEM((nfsdp, 8, D), F32),
        ]
        + sum_sems
        + sum_sems
        + [line_sems, line_sems, small, small, dma((16,))],
        (4,),
        3,
        14,
    )
    last_sum, gain_sums = lax.optimization_barrier((last_sum, gain_sums))
    out_tokens = unspread(out_tokens)[None]
    grad_tokens = unspread(grad_tokens)[None]
    gain_grad = jnp.concatenate(
        [
            unspread(gain_sums[:1])[0],
            unspread(gain_sums[1:2])[0],
            jnp.sum(gain_sums[2, :q_width].reshape(-1, HD), axis=0),
            jnp.sum(gain_sums[2, q_width:qk_width].reshape(-1, HD), axis=0),
        ]
    )

    olds = (master_weights, moment_one, moment_two)

    def feed_segments(b, pieces):
        width = cuts[b + 1] - cuts[b]
        found = []
        for part in pieces:
            for c in range(nctx):
                column = c * ff_width + cuts[b]
                real = min(max(FF - column, 0), width)
                if real:
                    piece, first = pieces[part]
                    found.append((piece, c, first, bases[part] + column, real))
        return found

    width_one = cuts[1]
    last_own = [
        lax.ppermute(
            lax.dynamic_index_in_dim(last_sum, lax.axis_index("ctx") ^ k, 0, keepdims=False),
            "ctx",
            [(c, c ^ k) for c in range(nctx)],
        )
        if k
        else lax.dynamic_index_in_dim(last_sum, lax.axis_index("ctx"), 0, keepdims=False)
        for k in range(nctx)
    ]
    news = adam(
        feed_segments(0, {0: (0, 0), 1: (0, width_one)}), [gu_own], olds, None, 7
    )
    parts = (
        (0, 0, q_width),
        (q_width, D, kv_width),
        (qk_width, D + KVD, kv_width),
        (qkv_width, QKVC, q_width),
    )
    if kv_width % 128:
        attn_own = jnp.concatenate(
            [attn_own[c, :, f : f + w] for f, _, w in parts for c in range(nctx)], axis=1
        )[None]
        segments = [(0, 0, 0, 0, gate_base)]
    else:
        segments = [
            (0, c, first, base + c * width, width)
            for first, base, width in parts
            for c in range(nctx)
        ]
    news = adam(segments, [attn_own], olds, news, 3)
    first_new, second_new, master_new, low_new = adam(
        feed_segments(1, {0: (None, 0), 1: (None, width_two), 2: (None, 2 * width_two + width_one)})
        + feed_segments(0, {2: (None, 2 * width_two)}),
        last_own,
        olds,
        news,
        6,
    )
    gain_first, gain_second, gain_new = adam_update(
        gains, gain_grad, gains_moment_one, gains_moment_two, GAIN_RATE, 0.0
    )
    return (
        out_tokens,
        grad_tokens,
        first_new,
        second_new,
        master_new,
        low_new,
        gain_first,
        gain_second,
        gain_new,
    )


def solution(mesh):
    rows = P("fsdp", "ctx", None)
    weights = P(("ctx", "fsdp"), None)
    return jax.shard_map(
        shards,
        mesh=mesh,
        in_specs=(rows, rows, P("fsdp", None), P(), weights, weights, weights, P(), P(), P()),
        out_specs=(rows, rows, weights, weights, weights, weights, P(), P(), P()),
        check_vma=False,
    )
```

```python
import functools

import jax
import jax.numpy as jnp
from jax import lax
from jax.experimental import pallas as pl
from jax.experimental.pallas import tpu as pltpu
from jax.sharding import PartitionSpec as P

D = 1536
HEADS = 24
KVHEADS = 8
HD = 64
FF = 6912
STEP = 10
HALF = 128
KVD = 512
QKVC = 2560
GROUP = HEADS // KVHEADS

ROPE_BASE = 1000000.0
NORM_EPS = 1e-05
BETA_ONE = 0.9
BETA_TWO = 0.95
ADAM_EPS = 1e-08
WEIGHT_DECAY = 0.1
LEARN_RATE = 0.03
GAIN_RATE = 0.5
SCALE = HD ** (-0.5)
MESH = pl.DeviceIdType.MESH
F32 = jnp.float32
BF16 = jnp.bfloat16
VMEM_LIMIT = 60 * 1024 * 1024


def dot(left, right, left_dim, right_dim):
    return lax.dot_general(
        left, right, (((left_dim,), (right_dim,)), ((), ())), preferred_element_type=F32
    )


def send(source, target, sems, item, peer):
    copy = pltpu.make_async_remote_copy(
        src_ref=source,
        dst_ref=target,
        send_sem=sems[0].at[item],
        recv_sem=sems[1].at[item],
        device_id=peer,
        device_id_type=MESH,
    )
    copy.start()
    return copy


def meet(axes):
    barrier = pltpu.get_barrier_semaphore()
    total = 0
    for axis in axes:
        size = lax.axis_size(axis)
        me = lax.axis_index(axis)
        for step in range(1, size):
            pl.semaphore_signal(
                barrier,
                inc=1,
                device_id={axis: lax.rem(me + step, size)},
                device_id_type=MESH,
            )
        total += size - 1
    pl.semaphore_wait(barrier, total)


def square():
    me = lax.axis_index("ctx")
    return me, me + 1 - 2 * lax.rem(me, 2), lax.rem(me + 2, 4), 3 - me


def swap_start(source, target, sems, base):
    size = lax.axis_size("ctx")
    me = lax.axis_index("ctx")
    copies = []
    for step in range(1, size):
        peer = lax.rem(me + step, size)
        copies.append(
            send(source.at[peer], target.at[me], sems, base + step, {"ctx": peer})
        )
    return copies


def gather_start(source, target, sems, base):
    size = lax.axis_size("ctx")
    me = lax.axis_index("ctx")
    if size != 4:
        return [
            send(
                source,
                target.at[me],
                sems,
                base + step,
                {"ctx": lax.rem(me + step, size)},
            )
            for step in range(1, size)
        ]
    me, side, over, across = square()
    half = source.shape[0] // 2
    top, low = pl.ds(0, half), pl.ds(half, half)
    return [
        send(source.at[top], target.at[me, top], sems, base, {"ctx": side}),
        send(source.at[low], target.at[me, low], sems, base + 1, {"ctx": over}),
        send(source.at[low], target.at[me, low], sems, base + 2, {"ctx": side}),
        send(source.at[top], target.at[me, top], sems, base + 3, {"ctx": over}),
    ]


def gather_pass(copies, target, sems, base):
    if lax.axis_size("ctx") != 4:
        return
    me, side, over, across = square()
    half = target.shape[1] // 2
    top, low = pl.ds(0, half), pl.ds(half, half)
    copies[0].wait_recv()
    copies.append(send(target.at[side, top], target.at[side, top], sems, base + 4, {"ctx": over}))
    copies[1].wait_recv()
    copies.append(send(target.at[over, low], target.at[over, low], sems, base + 5, {"ctx": side}))


def gather_end(copies):
    if lax.axis_size("ctx") != 4:
        for copy in copies:
            copy.wait()
        return
    for copy in copies:
        copy.wait_send()
    for copy in copies[2:]:
        copy.wait_recv()


def gather_rest(copies, target, sems, base):
    gather_pass(copies, target, sems, base)
    gather_end(copies)


def load(source, target, sem):
    copy = pltpu.make_async_copy(source, target, sem)
    copy.start()
    return copy


GATHER_SEMS = 8


def exchange_kernel(kinds, *refs):
    count = len(kinds)
    ins, outs = refs[:count], refs[count : 2 * count]
    send_sem, recv_sem, local_sem = refs[2 * count :]
    sems = (send_sem, recv_sem)
    me = lax.axis_index("ctx")
    meet(("ctx",))
    copies = []
    own = []
    for item in range(count):
        base = item * GATHER_SEMS
        if kinds[item] == "gather":
            copies.append(gather_start(ins[item], outs[item], sems, base))
            source = ins[item]
        else:
            copies.append(swap_start(ins[item], outs[item], sems, base))
            source = ins[item].at[me]
        copy = pltpu.make_async_copy(source, outs[item].at[me], local_sem.at[item])
        copy.start()
        own.append(copy)
    for item in range(count):
        if kinds[item] == "gather":
            gather_rest(copies[item], outs[item], sems, item * GATHER_SEMS)
        else:
            for copy in copies[item]:
                copy.wait()
    for copy in own:
        copy.wait()


def remote_params(collective_id):
    return pltpu.CompilerParams(
        collective_id=collective_id, has_side_effects=True, vmem_limit_bytes=VMEM_LIMIT
    )


def cost(micros):
    return pl.CostEstimate(flops=0, bytes_accessed=int(micros * 3.0e6), transcendentals=0)


def exchange(kinds, arrays, collective_id, micros):
    size = lax.axis_size("ctx")
    shapes = [
        jax.ShapeDtypeStruct((size,) + a.shape if kind == "gather" else a.shape, a.dtype)
        for kind, a in zip(kinds, arrays)
    ]
    sems = pltpu.SemaphoreType.DMA((len(arrays) * GATHER_SEMS,))
    return pl.pallas_call(
        functools.partial(exchange_kernel, kinds),
        out_shape=shapes,
        in_specs=[pl.BlockSpec(memory_space=pl.ANY)] * len(arrays),
        out_specs=[pl.BlockSpec(memory_space=pl.ANY)] * len(arrays),
        scratch_shapes=[sems, sems, pltpu.SemaphoreType.DMA((len(arrays),))],
        compiler_params=remote_params(collective_id),
        cost_estimate=cost(micros),
    )(*arrays)


def sum_scratch(size, rows):
    if size == 4:
        half = pltpu.VMEM((2, rows // 2, D), BF16)
        return [half, half, pltpu.VMEM((2, rows, D), BF16)]
    return [pltpu.VMEM((size - 1, rows, D), BF16)]


def sum_start(part, bufs, sems):
    size = lax.axis_size("ctx")
    me = lax.axis_index("ctx")
    rows = part.shape[0] // size

    def block(owner, first=0, count=rows):
        return pl.ds(pl.multiple_of(owner * rows + first, rows // 2), count)

    if size != 4:
        copies = []
        for step in range(1, size):
            peer = lax.rem(me + step, size)
            copies.append(
                send(part.at[block(peer)], bufs[0].at[step - 1], sems, step, {"ctx": peer})
            )
        return copies
    me, side, over, across = square()
    half = rows // 2
    relay, _, landed = bufs
    return [
        send(part.at[block(across, 0, half)], relay.at[0], sems, 0, {"ctx": side}),
        send(part.at[block(across, half, half)], relay.at[1], sems, 1, {"ctx": over}),
        send(
            part.at[block(side, 0, half)],
            landed.at[0, pl.ds(0, half)],
            sems,
            2,
            {"ctx": side},
        ),
        send(
            part.at[block(over, half, half)],
            landed.at[1, pl.ds(half, half)],
            sems,
            3,
            {"ctx": over},
        ),
    ]


def sum_pass(copies, part, bufs, sems):
    if lax.axis_size("ctx") != 4:
        return
    rows = part.shape[0] // 4
    half = rows // 2

    def rows_of(owner, first):
        return pl.ds(pl.multiple_of(owner * rows + first, half), half)

    me, side, over, across = square()
    relay, passed, landed = bufs
    copies[0].wait_recv()
    passed[0] = (part[rows_of(over, 0), :].astype(F32) + relay[0].astype(F32)).astype(BF16)
    copies.append(
        send(passed.at[0], landed.at[1, pl.ds(0, half)], sems, 4, {"ctx": over})
    )
    copies[1].wait_recv()
    passed[1] = (part[rows_of(side, half), :].astype(F32) + relay[1].astype(F32)).astype(
        BF16
    )
    copies.append(
        send(passed.at[1], landed.at[0, pl.ds(half, half)], sems, 5, {"ctx": side})
    )


def sum_rest(copies, part, bufs):
    size = lax.axis_size("ctx")
    me = lax.axis_index("ctx")
    rows = part.shape[0] // size
    half = rows // 2

    def rows_of(owner, first):
        return pl.ds(pl.multiple_of(owner * rows + first, half), half)

    if size != 4:
        for copy in copies:
            copy.wait()

        def read(first):
            total = part[rows_of(me, first), :].astype(F32)
            for step in range(1, size):
                total = total + bufs[0][step - 1, pl.ds(first, half), :].astype(F32)
            return total

        return read
    relay, passed, landed = bufs
    for copy in copies:
        copy.wait_send()
    for copy in copies[2:]:
        copy.wait_recv()

    def read(first):
        return (
            part[rows_of(me, first), :].astype(F32)
            + landed[0, pl.ds(first, half), :].astype(F32)
            + landed[1, pl.ds(first, half), :].astype(F32)
        )

    return read


def row_scale(values):
    return lax.rsqrt(jnp.mean(values * values, axis=-1, keepdims=True) + NORM_EPS)


def first_kernel(
    starts, origin, x, dy, gain, freq, x_low, dy_low, table, normed_all, *scratch
):
    move, normed, send_one, recv_one, local = scratch
    me = lax.axis_index("ctx")
    row = lax.broadcasted_iota(jnp.int32, move.shape, 0)
    move[...] = jnp.where(row == origin[...], 1.0, 0.0).astype(BF16)
    values = dot(x[...], move[...], 1, 0)
    x_low[...] = values.astype(BF16)
    normed[...] = (values * row_scale(values) * gain[...]).astype(BF16)
    meet(("ctx",))
    sems = (send_one, recv_one)
    copies = gather_start(normed, normed_all, sems, 0)
    own = load(normed, normed_all.at[me], local)
    dy_low[...] = dot(dy[...], move[...], 1, 0).astype(BF16)
    gather_pass(copies, normed_all, sems, 0)
    times = lax.broadcasted_iota(jnp.int32, (table.shape[0], 1), 0)
    angles = (times - doc_first(starts, times)).astype(F32) * freq[...]
    lane = lax.broadcasted_iota(jnp.int32, angles.shape, 1)
    sine = jnp.sin(angles)
    sine = jnp.where(lane % HD < HD // 2, -sine, sine)
    table[...] = jnp.where(lane < HD, jnp.cos(angles), sine)
    gather_end(copies)
    own.wait()


def middle_kernel(part, x, gain, middle, normed_all, *scratch):
    bufs, (normed, send_one, recv_one, send_two, recv_two, local) = scratch[:-6], scratch[-6:]
    me = lax.axis_index("ctx")
    meet(("ctx",))
    copies = sum_start(part, bufs, (send_one, recv_one))
    sum_pass(copies, part, bufs, (send_one, recv_one))
    read = sum_rest(copies, part, bufs)
    half = x.shape[0] // 2
    for first in (0, half):
        rows = pl.ds(first, half)
        values = x[rows, :].astype(F32) + read(first)
        middle[rows, :] = values
        normed[rows, :] = (values * row_scale(values) * gain[...]).astype(BF16)
    sems = (send_two, recv_two)
    copies = gather_start(normed, normed_all, sems, 0)
    own = load(normed, normed_all.at[me], local)
    gather_rest(copies, normed_all, sems, 0)
    own.wait()


def column_tiles(total, body):
    def step(tile, carry):
        body(pl.multiple_of(tile * 256, 256), 256)
        return carry

    lax.fori_loop(0, total // 256, step, 0)
    if total % 256:
        body(total - total % 256, total % 256)


def turn(source, target):
    for first in range(0, source.shape[0], HALF):
        rows = slice(first, first + HALF)
        target[:, rows] = source[rows, :].T


def middle_back_kernel(
    part,
    middle,
    dy,
    gain,
    x_all,
    dy_all,
    hidden_one,
    hidden_two,
    grad_gu,
    w_one,
    w_two,
    grad,
    gain_grad,
    down_sum,
    grad_all,
    weight_grad,
    out,
    *scratch,
):
    bufs = scratch[:-20]
    low, x_buf, gu_buf, turned, weight_buf, down_grad, out_buf = scratch[-20:-13]
    hidden_bufs, down_bufs = scratch[-13:-11], scratch[-11:-9]
    home, travel, send_one, recv_one, send_two, recv_two, send_three, recv_three, local = (
        scratch[-9:]
    )
    going, coming = travel.at[0], travel.at[1]
    me = lax.axis_index("ctx")
    chips = lax.axis_size("fsdp") // 2
    line = (send_three, recv_three)
    meet(("ctx", "fsdp"))
    copies = sum_start(part, bufs, (send_one, recv_one))
    width_one, width_two = hidden_one.shape[1], hidden_two.shape[1]
    gu_width = grad_gu.shape[1]
    loads = [
        load(source, target, local.at[item])
        for item, (source, target) in enumerate(
            (
                (dy_all, x_buf),
                (hidden_one, hidden_bufs[0]),
                (hidden_two, hidden_bufs[1]),
                (grad_gu, gu_buf),
                (w_one.at[:, pl.ds(2 * width_one, width_one)], down_bufs[0]),
                (w_two.at[:, pl.ds(2 * width_two, width_two)], down_bufs[1]),
            )
        )
    ]
    loads[0].wait()
    turn(x_buf, turned)
    loads.append(load(x_all, x_buf, local.at[6]))
    loads[1].wait()

    def product(target, column, right, begin=0, count=None):
        def tile(first, width):
            target[:, pl.ds(column + first, width)] = dot(
                turned[...], right[:, pl.ds(begin + first, width)], 1, 0
            ).astype(BF16)

        column_tiles(right.shape[1] if count is None else count, tile)

    width_line = down_grad.shape[1]
    product(down_grad, 0, hidden_bufs[0], 0, width_line)
    home_copies = line_start(down_grad, home, line, 0)
    product(weight_buf, gu_width, hidden_bufs[0], width_line, width_one - width_line)
    sum_pass(copies, part, bufs, (send_one, recv_one))
    line_home(home_copies, down_grad, home)
    line_step(chips - 1, home, going, coming, line, chips)
    loads[2].wait()
    product(weight_buf, gu_width + width_one - width_line, hidden_bufs[1])
    loads[6].wait()
    turn(x_buf, turned)
    loads[3].wait()
    product(weight_buf, 0, gu_buf)
    stores = [load(weight_buf, weight_grad, local.at[7])]
    if chips > 2:
        line_step(chips - 2, home, going, coming, line, chips)
    read = sum_rest(copies, part, bufs)
    half = dy.shape[0] // 2
    total = jnp.zeros((1, D), F32)
    for first in (0, half):
        rows = pl.ds(first, half)
        values = middle[rows, :]
        root = row_scale(values)
        unit = values * root
        back = read(first)
        total = total + jnp.sum(back * unit, axis=0, keepdims=True)
        back = back * gain[...]
        back = root * (back - unit * jnp.mean(back * unit, axis=-1, keepdims=True))
        back = back + dy[rows, :].astype(F32)
        grad[rows, :] = back
        low[rows, :] = back.astype(BF16)
    gain_grad[...] = total
    sems = (send_two, recv_two)
    copies = gather_start(low, grad_all, sems, 0)
    stores.append(load(low, grad_all.at[me], local.at[8]))
    loads[4].wait()
    loads[5].wait()

    def out_tile(first, width):
        columns = pl.ds(first, width)
        out_buf[:, columns] = (
            dot(hidden_bufs[0][...], down_bufs[0][columns, :], 1, 1)
            + dot(hidden_bufs[1][...], down_bufs[1][columns, :], 1, 1)
        ).astype(BF16)

    column_tiles(D, out_tile)
    stores.append(load(out_buf, out, local.at[9]))
    gather_pass(copies, grad_all, sems, 0)
    for reach in range(min(chips - 1, max(chips - 3, 1)), 0, -1):
        line_step(reach, home, going, coming, line, chips)
    line_end(home_copies, home, going, coming, line, chips)
    chip = lax.axis_index("fsdp") // 2
    rows = down_sum.shape[1]
    for index in range(down_sum.shape[0]):
        down_sum[index] = home[chip, index * rows : (index + 1) * rows, :]
    gather_end(copies)
    for copy in stores:
        copy.wait()


def line_start(grad, home, sems, base):
    me = lax.axis_index("fsdp")
    chips = lax.axis_size("fsdp") // 2
    core = lax.rem(me, 2)
    rows = grad.shape[0] // (2 * chips)
    copies = []
    for chip in range(chips):
        theirs = pl.ds(pl.multiple_of((2 * chip + 1 - core) * rows, rows), rows)
        copies.append(
            send(grad.at[theirs], home.at[chip], sems, base + chip, {"fsdp": me + 1 - 2 * core})
        )
    return copies


def line_home(copies, grad, home):
    me = lax.axis_index("fsdp")
    chips = lax.axis_size("fsdp") // 2
    core = lax.rem(me, 2)
    rows = grad.shape[0] // (2 * chips)
    for chip in range(chips):
        copies[chip].wait_recv()
        mine = pl.ds(pl.multiple_of((2 * chip + core) * rows, rows), rows)
        home[chip] = (home[chip].astype(F32) + grad[mine, :].astype(F32)).astype(BF16)


def line_copies(reach, going, coming, sems, base):
    me = lax.axis_index("fsdp")
    chips = lax.axis_size("fsdp") // 2
    chip = me // 2
    found = []
    for side, way in ((0, 1), (1, -1)):
        copy = pltpu.make_async_remote_copy(
            src_ref=going.at[side, reach - 1],
            dst_ref=coming.at[side, reach - 1],
            send_sem=sems[0].at[base + 2 * reach + side],
            recv_sem=sems[1].at[base + 2 * reach + side],
            device_id={"fsdp": lax.rem(me + 2 * way + 2 * chips, 2 * chips)},
            device_id_type=MESH,
        )
        if way == 1:
            sent = chip + reach <= chips - 1
            got = (chip >= 1) & (chip + reach <= chips)
            more = (chip >= 1) & sent
        else:
            sent = chip >= reach
            got = (chip <= chips - 2) & (chip + 1 >= reach)
            more = (chip <= chips - 2) & sent
        found.append((side, way, copy, sent, got, more))
    return found


def line_step(reach, home, going, coming, sems, base):
    me = lax.axis_index("fsdp")
    chips = lax.axis_size("fsdp") // 2
    chip = me // 2
    if reach < chips - 1:
        for _, _, copy, _, got, _ in line_copies(reach + 1, going, coming, sems, base):
            pl.when(got)(copy.wait_recv)
    for side, way, copy, sent, _, more in line_copies(reach, going, coming, sems, base):

        @pl.when(sent)
        def _(side=side, way=way, copy=copy, more=more):
            value = home[chip + way * reach]
            if reach < chips - 1:

                @pl.when(more)
                def _():
                    going[side, reach - 1] = (
                        value.astype(F32) + coming[side, reach].astype(F32)
                    ).astype(BF16)

                @pl.when(jnp.logical_not(more))
                def _():
                    going[side, reach - 1] = value

            else:
                going[side, reach - 1] = value
            copy.start()


def line_end(copies, home, going, coming, sems, base):
    me = lax.axis_index("fsdp")
    chips = lax.axis_size("fsdp") // 2
    chip = me // 2
    for side, _, copy, _, got, _ in line_copies(1, going, coming, sems, base):

        @pl.when(got)
        def _(side=side, copy=copy):
            copy.wait_recv()
            home[chip] = (home[chip].astype(F32) + coming[side, 0].astype(F32)).astype(BF16)

    for copy in copies:
        copy.wait_send()
    for reach in range(1, chips):
        for _, _, copy, sent, _, _ in line_copies(reach, going, coming, sems, base):
            pl.when(sent)(copy.wait_send)


def remote_call(
    kernel, out_shape, args, collective_id, micros, scratch, in_hbm=(), smem=0, args_in_hbm=0
):
    return pl.pallas_call(
        kernel,
        out_shape=out_shape,
        in_specs=[pl.BlockSpec(memory_space=pltpu.SMEM)] * smem
        + [pl.BlockSpec(memory_space=pltpu.VMEM)] * (len(args) - smem - args_in_hbm)
        + [pl.BlockSpec(memory_space=pl.ANY)] * args_in_hbm,
        out_specs=[
            pl.BlockSpec(memory_space=pl.ANY if item in in_hbm else pltpu.VMEM)
            for item in range(len(out_shape))
        ],
        scratch_shapes=scratch,
        compiler_params=remote_params(collective_id),
        cost_estimate=cost(micros),
    )(*args)


def adam_update(param_now, grad_now, moment_old_one, moment_old_two, step_rate, decay_rate):
    first_new = BETA_ONE * moment_old_one + (1.0 - BETA_ONE) * grad_now
    second_new = BETA_TWO * moment_old_two + (1.0 - BETA_TWO) * grad_now * grad_now
    ratio = (
        first_new
        / (1.0 - BETA_ONE**STEP)
        / (jnp.sqrt(second_new / (1.0 - BETA_TWO**STEP)) + ADAM_EPS)
    )
    return (first_new, second_new, param_now - step_rate * (ratio + decay_rate * param_now))


def adam_kernel(segments, pieces, held, *refs):
    me = lax.axis_index("ctx")
    grads = refs[:pieces]
    olds = refs[pieces : pieces + 3]
    news = refs[pieces + 3 + held : pieces + 3 + held + 4]
    grad_buf, old_buf, low_buf, in_sem, out_sem = refs[pieces + 3 + held + 4 :]
    base = min(segment[3] for segment in segments)
    loads = []
    for number, (piece, index, first, column, width) in enumerate(segments):
        here = pl.ds(column - base, width)
        there = pl.ds(column, width)
        columns = pl.ds(first, width)
        copies = []
        for number_from, source in enumerate(grads):
            if piece not in (None, number_from):
                continue
            copy = pltpu.make_async_copy(
                source.at[:, columns] if piece is None else source.at[index, :, columns],
                grad_buf.at[:, here],
                in_sem.at[3, number],
            )
            if piece is None:
                pl.when(me == index ^ number_from)(copy.start)
            else:
                copy.start()
        loads.append([copy])
        copies += [
            pltpu.make_async_copy(
                olds[item].at[:, there], old_buf.at[item, :, here], in_sem.at[item, number]
            )
            for item in range(3)
        ]
        for copy in copies:
            copy.start()
        loads[-1] += copies
    stores = []
    for number, (piece, index, first, column, width) in enumerate(segments):
        for copy in loads[number]:
            copy.wait()
        here = pl.ds(column - base, width)
        there = pl.ds(column, width)
        first_new, second_new, master = adam_update(
            old_buf[0, :, here],
            grad_buf[:, here].astype(F32),
            old_buf[1, :, here],
            old_buf[2, :, here],
            LEARN_RATE,
            WEIGHT_DECAY,
        )
        old_buf[0, :, here] = master
        old_buf[1, :, here] = first_new
        old_buf[2, :, here] = second_new
        low_buf[:, here] = master.astype(BF16)
        for item, source in enumerate(
            (
                old_buf.at[1, :, here],
                old_buf.at[2, :, here],
                old_buf.at[0, :, here],
                low_buf.at[:, here],
            )
        ):
            copy = pltpu.make_async_copy(
                source, news[item].at[:, there], out_sem.at[item, number]
            )
            copy.start()
            stores.append(copy)
    for copy in stores:
        copy.wait()


def adam(segments, grads, olds, held, micros):
    rows, columns = olds[0].shape
    span = max(s[3] + s[4] for s in segments) - min(s[3] for s in segments)
    held = [] if held is None else list(held)
    args = list(grads) + list(olds) + held
    return pl.pallas_call(
        functools.partial(adam_kernel, tuple(segments), len(grads), len(held)),
        out_shape=[jax.ShapeDtypeStruct((rows, columns), F32)] * 3
        + [jax.ShapeDtypeStruct((rows, columns), BF16)],
        in_specs=[pl.BlockSpec(memory_space=pl.ANY)] * len(args),
        out_specs=[pl.BlockSpec(memory_space=pl.ANY)] * 4,
        input_output_aliases={len(grads) + 3 + item: item for item in range(len(held))},
        scratch_shapes=[
            pltpu.VMEM((rows, span), BF16),
            pltpu.VMEM((3, rows, span), F32),
            pltpu.VMEM((rows, span), BF16),
            pltpu.SemaphoreType.DMA((4, len(segments))),
            pltpu.SemaphoreType.DMA((4, len(segments))),
        ],
        compiler_params=pltpu.CompilerParams(vmem_limit_bytes=VMEM_LIMIT),
        cost_estimate=cost(micros),
    )(*args)


def head_mean(values, ones):
    high = values.astype(BF16)
    rest = (values - high.astype(F32)).astype(BF16)
    return (dot(high, ones, 1, 0) + dot(rest, ones, 1, 0)) * (1.0 / HD)


def head_ones(width):
    row = lax.broadcasted_iota(jnp.int32, (width, width), 0) // HD
    col = lax.broadcasted_iota(jnp.int32, (width, width), 1) // HD
    return jnp.where(row == col, 1.0, 0.0).astype(BF16)


def partner(values):
    width = values.shape[-1]
    lane = lax.broadcasted_iota(jnp.int32, values.shape, 1)
    return jnp.where(
        lane % HD < HD // 2,
        pltpu.roll(values, width - HD // 2, 1),
        pltpu.roll(values, HD // 2, 1),
    )


def widen(table, width):
    return [
        jnp.concatenate([part] * (width // HD), axis=-1)
        for part in (table[:, :HD], table[:, HD:])
    ]


def doc_first(starts, times):
    first = jnp.zeros_like(times)
    for item in range(starts.shape[0]):
        first = jnp.where(starts[item] <= times, starts[item], first)
    return first


def block_mask(starts, block, keys):
    shape = (keys, GROUP * HALF)
    times = block * HALF + lax.broadcasted_iota(jnp.int32, (1, GROUP * HALF), 1) % HALF
    key = lax.broadcasted_iota(jnp.int32, shape, 0)
    return (key >= doc_first(starts, times)) & (key <= times)


def stack_heads(ref, rows, group):
    return jnp.concatenate(
        [
            ref[rows, (group * GROUP + h) * HD : (group * GROUP + h + 1) * HD]
            for h in range(GROUP)
        ],
        axis=0,
    )


def unstack_heads(turned):
    wide = turned.T
    return [wide[h * HALF : (h + 1) * HALF, :] for h in range(GROUP)]


def attend_kernel(
    blocks,
    groups,
    place,
    order,
    starts,
    table,
    gain,
    normed_in,
    weights_from,
    dy,
    swap_in,
    part,
    qk,
    q,
    k,
    v,
    o_held,
    lse,
    dy_all,
    swap_out,
    normed,
    weights_in,
    joined,
    o,
    send_sem,
    recv_sem,
    local,
):
    sems = (send_sem, recv_sem)
    me = lax.axis_index("ctx")
    qk_width = qk.shape[1]
    q_width = q.shape[1]
    qkv_width = qk_width + v.shape[1]
    ones = head_ones(qk_width)
    meet(("ctx",))
    loads = [
        load(normed_in, normed, local.at[0]),
        load(weights_from, weights_in, local.at[1]),
    ]
    swap_copies = swap_start(swap_in, swap_out, sems, GATHER_SEMS)
    copies = gather_start(dy, dy_all, sems, 0)
    own_copies = [
        load(swap_in.at[me], swap_out.at[me], local.at[2]),
        load(dy, dy_all.at[me], local.at[3]),
    ]
    for copy in loads:
        copy.wait()
    for block in range(blocks):
        joined[block] = dot(
            normed[block * HALF : (block + 1) * HALF, :], weights_in[:, :qkv_width], 1, 0
        )
    for block in range(blocks):
        to = slice(block * HALF, (block + 1) * HALF)
        values = joined[place[block]]
        v[to, :] = values[:, qk_width:].astype(BF16)
        values = values[:, :qk_width]
        qk[to, :] = values
        turned = values * lax.rsqrt(head_mean(values * values, ones) + NORM_EPS) * gain[...]
        cosine, sine = widen(table[to, :], qk_width)
        turned = turned * cosine + partner(turned) * sine
        turned = turned.astype(BF16)
        q[to, :] = turned[:, :q_width]
        k[to, :] = turned[:, q_width:]
    for block in range(blocks):
        rows = slice(block * HALF, (block + 1) * HALF)
        keys = (block + 1) * HALF
        mask = block_mask(starts, block, keys)
        pieces = []
        for group in range(groups):
            lanes = slice(group * HD, (group + 1) * HD)
            queries = stack_heads(q, rows, group)
            scores = dot(k[:keys, lanes], queries, 1, 1) * SCALE
            weights = jnp.where(mask, jnp.exp(scores), 0.0)
            sums = jnp.sum(weights, axis=0, keepdims=True)
            lse[block, group : group + 1, :] = jnp.log(sums)
            mixed = dot(v[:keys, lanes], weights.astype(BF16), 0, 0) / sums
            pieces += unstack_heads(mixed)
        o[block] = jnp.concatenate(pieces, axis=1).astype(BF16)
    for block in range(blocks):
        o_held[block * HALF : (block + 1) * HALF, :] = o[order[block]]
    for first in range(0, D, 512):
        part[:, first : first + 512] = dot(
            o_held[...], weights_in[first : first + 512, qkv_width:], 1, 1
        ).astype(BF16)
    gather_rest(copies, dy_all, sems, 0)
    for copy in swap_copies:
        copy.wait()
    for copy in own_copies:
        copy.wait()


def attend_back_kernel(
    blocks,
    groups,
    place,
    order,
    starts,
    lse,
    gain,
    part,
    *refs,
):
    sources, refs = refs[:9], refs[9:]
    out, joined, gain_grad, out_grad = refs[:4]
    targets, refs = refs[4:13], refs[13:]
    grad_all, weights_in, q, k, v, o, qk, table, middle = targets
    bufs, (do, dq, dkv, turned, send_one, recv_one, local) = refs[:-7], refs[-7:]
    out_sems = (send_one, recv_one)
    qk_width = qk.shape[2]
    qkv_width = qk_width + v.shape[1]
    ones = head_ones(qk_width)
    meet(("ctx",))
    out_copies = sum_start(part, bufs, out_sems)
    loads = [
        load(source, target, local.at[item])
        for item, (source, target) in enumerate(zip(sources, targets))
    ]
    for copy in loads[:6]:
        copy.wait()
    for block in range(blocks):
        do[block * HALF : (block + 1) * HALF, :] = dot(
            grad_all[place[block]], weights_in[:, qkv_width:], 1, 0
        ).astype(BF16)
    for block in range(blocks):
        turned[:, block * HALF : (block + 1) * HALF] = grad_all[block].T
    for first in range(0, D, 512):
        rows = slice(first, first + 512)
        out_grad[rows, :] = dot(turned[rows, :], o[...], 1, 0).astype(BF16)
    dkv[...] = jnp.zeros_like(dkv)
    for block in range(blocks):
        if block == blocks // 2:
            sum_pass(out_copies, part, bufs, out_sems)
        rows = slice(block * HALF, (block + 1) * HALF)
        keys = (block + 1) * HALF
        mask = block_mask(starts, block, keys)
        pieces = []
        dk_add = []
        dv_add = []
        for group in range(groups):
            lanes = slice(group * HD, (group + 1) * HD)
            queries = stack_heads(q, rows, group)
            outs = stack_heads(do, rows, group)
            key_rows = k[:keys, lanes]
            scores = dot(key_rows, queries, 1, 1) * SCALE
            weights = jnp.where(
                mask, jnp.exp(scores - lse[block, group : group + 1, :]), 0.0
            )
            back = dot(v[:keys, lanes], outs, 1, 1)
            delta = jnp.sum(weights * back, axis=0, keepdims=True)
            grads = (weights * (back - delta)).astype(BF16)
            pieces += unstack_heads(dot(key_rows, grads, 0, 0) * SCALE)
            dk_add.append(dot(grads, queries, 1, 0) * SCALE)
            dv_add.append(dot(weights.astype(BF16), outs, 1, 0))
        dq[block] = jnp.concatenate(pieces, axis=1)
        dkv[: block + 1] += jnp.concatenate(dk_add + dv_add, axis=1).reshape(
            (block + 1,) + dkv.shape[1:]
        )
    gain_row = jnp.zeros((1, qk_width), F32)
    for copy in loads[6:]:
        copy.wait()
    for block in range(blocks):
        here = order[block]
        values = qk[here]
        root = lax.rsqrt(head_mean(values * values, ones) + NORM_EPS)
        unit = values * root
        grad_kv = dkv[here]
        kv_width = grad_kv.shape[1] // 2
        grad = jnp.concatenate([dq[here], grad_kv[:, :kv_width]], axis=1)
        cosine, sine = widen(table[here], qk_width)
        grad = grad * cosine - partner(grad) * sine
        gain_row = gain_row + jnp.sum(grad * unit, axis=0, keepdims=True)
        grad = grad * gain[...]
        grad = root * (grad - unit * head_mean(grad * unit, ones))
        joined[block * HALF : (block + 1) * HALF, :] = jnp.concatenate(
            [grad, grad_kv[:, kv_width:]], axis=1
        ).astype(BF16)
    gain_grad[...] = gain_row
    read = sum_rest(out_copies, part, bufs)
    half = middle.shape[0] // 2
    for first in (0, half):
        rows = pl.ds(first, half)
        out[rows, :] = (middle[rows, :] + read(first)).astype(BF16)


def tail_kernel(
    swaps,
    joined,
    out_grad,
    gain_row,
    attn_gain,
    ffn_gain_grad,
    *refs,
):
    sources, refs = refs[:4], refs[4:]
    swap_in, refs = refs[:swaps], refs[swaps:]
    grad_tokens, gains, attn_own = refs[:3]
    swap_out, refs = refs[3 : 3 + swaps], refs[3 + swaps :]
    targets, refs = refs[:4], refs[4:]
    weights_in, normed, x, grad_middle = targets
    back_bufs, refs = refs[:-15], refs[-15:]
    turned, part, attn_grad, home, travel, owned, ctx_box, fsdp_box = refs[:8]
    send_two, recv_two, send_three, recv_three, send_four, recv_four, local = refs[8:]
    going, coming = travel.at[0], travel.at[1]
    back_sems = (send_two, recv_two)
    line, small = (send_three, recv_three), (send_four, recv_four)
    size = lax.axis_size("ctx")
    me = lax.axis_index("ctx")
    chips = lax.axis_size("fsdp") // 2
    step_base = chips
    swap_base = step_base + 2 * chips
    qkv_width = joined.shape[1]
    qk_width = gain_row.shape[1]
    half = x.shape[0] // 2
    loads = [
        load(source, target, local.at[item])
        for item, (source, target) in enumerate(zip(sources, targets))
    ]
    meet(("ctx", "fsdp"))
    swap_copies = []
    own_copies = []
    for item in range(swaps):
        swap_copies += swap_start(
            swap_in[item], swap_out[item], line, swap_base + (item + 1) * size
        )
        own_copies.append(
            load(swap_in[item].at[me], swap_out[item].at[me], local.at[4 + item])
        )
    for copy in loads:
        copy.wait()
    for first in range(0, D, 512):
        part[:, first : first + 512] = dot(
            joined[...], weights_in[first : first + 512, :qkv_width], 1, 1
        ).astype(BF16)
    back_copies = sum_start(part, back_bufs, back_sems)
    turn(normed, turned)
    for first in range(0, D, 512):
        rows = slice(first, first + 512)
        attn_grad[rows, :qkv_width] = dot(turned[rows, :], joined[...], 1, 0).astype(BF16)
    attn_grad[:, qkv_width:] = out_grad[...]
    home_copies = line_start(attn_grad, home, line, 0)
    line_home(home_copies, attn_grad, home)
    line_step(chips - 1, home, going, coming, line, step_base)
    sum_pass(back_copies, part, back_bufs, back_sems)
    for reach in range(chips - 2, 1, -1):
        line_step(reach, home, going, coming, line, step_base)
    read = sum_rest(back_copies, part, back_bufs)
    total = jnp.zeros((1, D), F32)
    for first in (0, half):
        rows = pl.ds(first, half)
        values = x[rows, :].astype(F32)
        root = row_scale(values)
        unit = values * root
        back = read(first)
        total = total + jnp.sum(back * unit, axis=0, keepdims=True)
        back = back * attn_gain[...]
        back = root * (back - unit * jnp.mean(back * unit, axis=-1, keepdims=True))
        grad_tokens[rows, :] = grad_middle[rows, :] + back

    def spread_start(axis, box, value, base):
        index = lax.axis_index(axis)
        axis_size = lax.axis_size(axis)
        box[index] = value
        return [
            send(
                box.at[index],
                box.at[index],
                small,
                base + step,
                {axis: lax.rem(index + step, axis_size)},
            )
            for step in range(1, axis_size)
        ]

    def spread_end(copies, box):
        for copy in copies:
            copy.wait()
        summed = box[0]
        for item in range(1, box.shape[0]):
            summed = summed + box[item]
        return summed

    ctx_copies = spread_start(
        "ctx",
        ctx_box,
        jnp.concatenate(
            [
                total,
                ffn_gain_grad[...],
                jnp.concatenate([gain_row[...], jnp.zeros((1, D - qk_width), F32)], axis=1),
                jnp.zeros((5, D), F32),
            ],
            axis=0,
        ),
        0,
    )
    line_step(1, home, going, coming, line, step_base)
    fsdp_copies = spread_start("fsdp", fsdp_box, spread_end(ctx_copies, ctx_box), size)
    line_end(home_copies, home, going, coming, line, step_base)
    chip = lax.axis_index("fsdp") // 2
    owned_rows = owned.shape[1]
    for index in range(size):
        owned[index] = home[chip, index * owned_rows : (index + 1) * owned_rows, :]
    swap_copies += swap_start(owned, attn_own, line, swap_base)
    attn_own[me] = owned[me]
    gains[...] = spread_end(fsdp_copies, fsdp_box)
    for copy in swap_copies:
        copy.wait()
    for copy in own_copies:
        copy.wait()


def rms_scale(values_in, gain_vec):
    return (
        values_in
        * lax.rsqrt(jnp.mean(values_in * values_in, axis=-1, keepdims=True) + NORM_EPS)
        * gain_vec
    )


def inverse_freq():
    return 1.0 / ROPE_BASE ** (jnp.arange(0, HD, 2).astype(F32) / HD)


def shards(
    tokens,
    cotangent,
    doc_starts,
    block_order,
    master_weights,
    moment_one,
    moment_two,
    gains,
    gains_moment_one,
    gains_moment_two,
):
    nctx = lax.axis_size("ctx")
    nfsdp = lax.axis_size("fsdp")
    own_rows = master_weights.shape[0]
    tok_rows = tokens.shape[1]
    stream_len = tok_rows * nctx
    blocks = stream_len // HALF
    groups = KVHEADS // nctx
    q_width = D // nctx
    kv_width = KVD // nctx
    qk_width = q_width + kv_width
    qkv_width = qk_width + kv_width
    tiles = FF // 128
    ff_tiles = -(-tiles // nctx)
    ff_width = ff_tiles * 128
    bundles = 2
    cuts = [0, (ff_tiles * 5 + 3) // 7 * 128, ff_width]

    low = master_weights.astype(BF16)

    def ff_part(base, index, start, stop):
        first = index * ff_width + start
        last = index * ff_width + stop
        real_first, real_last = min(first, FF), min(last, FF)
        part = low[:, base + real_first : base + real_last]
        if real_last - real_first < last - first:
            part = jnp.pad(part, ((0, 0), (0, (last - first) - (real_last - real_first))))
        return part

    def attn_part(index):
        return jnp.concatenate(
            [
                low[:, index * q_width : (index + 1) * q_width],
                low[:, D + index * kv_width : D + (index + 1) * kv_width],
                low[:, D + KVD + index * kv_width : D + KVD + (index + 1) * kv_width],
                low[:, QKVC + index * q_width : QKVC + (index + 1) * q_width],
            ],
            axis=1,
        )

    gate_base = QKVC + D
    bases = (gate_base, gate_base + FF, gate_base + 2 * FF)
    attn_send = jnp.stack([attn_part(c) for c in range(nctx)])
    ff_send = [
        jnp.stack(
            [
                jnp.concatenate(
                    [ff_part(base, c, cuts[b], cuts[b + 1]) for base in bases], axis=1
                )
                for c in range(nctx)
            ]
        )
        for b in range(bundles)
    ]

    def gather_rows(piece):
        return lax.all_gather(
            piece.reshape(nctx * own_rows, piece.shape[-1]), "fsdp", axis=0, tiled=True
        )

    def spread(active):
        return (
            active.reshape(active.shape[0], nctx, nfsdp, own_rows)
            .transpose(0, 2, 1, 3)
            .reshape(active.shape[0], D)
        )

    def unspread(active):
        return (
            active.reshape(active.shape[0], nfsdp, nctx, own_rows)
            .transpose(0, 2, 1, 3)
            .reshape(active.shape[0], D)
        )

    dma = pltpu.SemaphoreType.DMA
    all_low = jax.ShapeDtypeStruct((nctx, tok_rows, D), BF16)
    own_low = jax.ShapeDtypeStruct((tok_rows, D), BF16)
    own_f32 = jax.ShapeDtypeStruct((tok_rows, D), F32)
    row_f32 = jax.ShapeDtypeStruct((1, D), F32)
    g_attn = spread(gains[None, :D])
    g_ffn = spread(gains[None, D : 2 * D])
    order = block_order.reshape(blocks)
    place = jnp.argsort(order).astype(jnp.int32)
    starts = doc_starts[0]

    (attn_held,) = exchange(("swap",), [attn_send], 0, 10)
    w_attn = gather_rows(attn_held)
    first_send, attn_held = lax.optimization_barrier((ff_send[0], attn_held))
    (first_held,) = exchange(("swap",), [first_send], 1, 16)
    table_shape = jax.ShapeDtypeStruct((stream_len, 2 * HD), F32)
    origin = spread(jnp.arange(D, dtype=jnp.int32)[None])
    starts_late, first_held = lax.optimization_barrier((starts, first_held))
    x_low, dy_low, table, normed_all = remote_call(
        first_kernel,
        [own_low, own_low, table_shape, all_low],
        (
            starts_late,
            origin,
            tokens[0],
            cotangent[0],
            g_attn,
            jnp.tile(inverse_freq(), 4)[None],
        ),
        2,
        33,
        [
            pltpu.VMEM((D, D), BF16),
            pltpu.VMEM((tok_rows, D), BF16),
            dma((GATHER_SEMS,)),
            dma((GATHER_SEMS,)),
            dma,
        ],
        (3,),
        1,
    )
    normed_all = normed_all.reshape(stream_len, D)

    g_query = gains[2 * D : 2 * D + HD]
    g_key = gains[2 * D + HD :]
    qk_gain = jnp.concatenate(
        [jnp.tile(g_query, q_width // HD), jnp.tile(g_key, kv_width // HD)]
    )[None]

    low_stream = pltpu.VMEM((stream_len, D), BF16)
    heads_low = pltpu.VMEM((stream_len, q_width), BF16)
    part, qk, q, k, v, mixed, lse, dy_all, second_held = remote_call(
        functools.partial(attend_kernel, blocks, groups),
        [
            jax.ShapeDtypeStruct((stream_len, D), BF16),
            jax.ShapeDtypeStruct((stream_len, qk_width), F32),
            jax.ShapeDtypeStruct((stream_len, q_width), BF16),
            jax.ShapeDtypeStruct((stream_len, kv_width), BF16),
            jax.ShapeDtypeStruct((stream_len, kv_width), BF16),
            jax.ShapeDtypeStruct((stream_len, q_width), BF16),
            jax.ShapeDtypeStruct((blocks, groups, GROUP * HALF), F32),
            all_low,
            jax.ShapeDtypeStruct(ff_send[1].shape, BF16),
        ],
        (place, order, starts, table, qk_gain, normed_all, w_attn, dy_low, ff_send[1]),
        3,
        42,
        [
            low_stream,
            pltpu.VMEM(w_attn.shape, BF16),
            pltpu.VMEM((blocks, HALF, qkv_width), F32),
            pltpu.VMEM((blocks, HALF, q_width), BF16),
            dma((GATHER_SEMS + nctx,)),
            dma((GATHER_SEMS + nctx,)),
            dma((4,)),
        ],
        (7, 8),
        3,
        4,
    )
    dy_all = dy_all.reshape(stream_len, D)
    w_ff = [gather_rows(first_held), gather_rows(second_held)]
    sum_bufs = sum_scratch(nctx, tok_rows)
    sum_sems = [dma((GATHER_SEMS,)), dma((GATHER_SEMS,))]
    norm_scratch = (
        sum_bufs + [pltpu.VMEM((tok_rows, D), BF16)] + sum_sems + sum_sems + [dma]
    )

    middle, normed_two_all = remote_call(
        middle_kernel,
        [own_f32, all_low],
        (part, x_low, g_ffn),
        4,
        57,
        norm_scratch,
        (1,),
    )
    normed_two_all = normed_two_all.reshape(stream_len, D)

    def sum_rows(grad):
        return lax.psum_scatter(grad, "fsdp", scatter_dimension=0, tiled=True).reshape(
            nctx, own_rows, grad.shape[-1]
        )

    def feed(b, x_all, dy):
        width = cuts[b + 1] - cuts[b]
        w_gu, w_down = w_ff[b][:, : 2 * width], w_ff[b][:, 2 * width :]
        gate_up = dot(x_all, w_gu, 1, 0).astype(BF16)
        gate, up = gate_up[:, :width].astype(F32), gate_up[:, width:].astype(F32)
        gated = jax.nn.sigmoid(gate)
        act = gate * gated
        hidden = (act * up).astype(BF16)
        back_hidden = dot(dy, w_down, 1, 0)
        grad_gu = jnp.concatenate(
            [back_hidden * up * (gated + act * (1.0 - gated)), back_hidden * act], axis=1
        ).astype(BF16)
        return hidden, grad_gu, dot(grad_gu, w_gu, 1, 1)

    hidden_one, grad_gu, back_partial = feed(0, normed_two_all, dy_all)
    gu_grad = dot(normed_two_all, grad_gu, 0, 0).astype(BF16)
    gu_grad, back_partial, w_ff[1] = lax.optimization_barrier((gu_grad, back_partial, w_ff[1]))
    width_two = cuts[2] - cuts[1]
    width_line = cuts[1] * 3 // 5 // 128 * 128
    last_width = 2 * width_two + ff_width - width_line
    hidden_two, grad_gu, back_more = feed(1, normed_two_all, dy_all)
    back_partial = (back_partial + back_more).astype(BF16)
    gu_sum = sum_rows(gu_grad)
    chips = nfsdp // 2

    def line_scratch(columns):
        block = (nctx * own_rows, columns)
        return [pltpu.VMEM((chips,) + block, BF16), pltpu.VMEM((2, 2, chips - 1) + block, BF16)]

    grad_middle, grad_g_ffn, down_sum, grad_middle_all, last_grad, out_partial = remote_call(
        middle_back_kernel,
        [
            own_f32,
            row_f32,
            jax.ShapeDtypeStruct((nctx, own_rows, width_line), BF16),
            all_low,
            jax.ShapeDtypeStruct((D, last_width), BF16),
            jax.ShapeDtypeStruct((stream_len, D), BF16),
        ],
        (
            back_partial,
            middle,
            dy_low,
            g_ffn,
            normed_two_all,
            dy_all,
            hidden_one,
            hidden_two,
            grad_gu,
            w_ff[0],
            w_ff[1],
        ),
        5,
        57,
        sum_bufs
        + [
            pltpu.VMEM((tok_rows, D), BF16),
            low_stream,
            pltpu.VMEM((stream_len, 2 * width_two), BF16),
            pltpu.VMEM((D, stream_len), BF16),
            pltpu.VMEM((D, last_width), BF16),
            pltpu.VMEM((D, width_line), BF16),
            low_stream,
            pltpu.VMEM((stream_len, cuts[1]), BF16),
            pltpu.VMEM((stream_len, width_two), BF16),
            pltpu.VMEM((D, cuts[1]), BF16),
            pltpu.VMEM((D, width_two), BF16),
        ]
        + line_scratch(width_line)
        + sum_sems
        + sum_sems
        + [dma((3 * chips,)), dma((3 * chips,)), dma((10,))],
        (3, 4, 5),
        0,
        7,
    )
    last_sum = sum_rows(last_grad)

    small = dma((nctx + nfsdp,))
    line_sems = dma((3 * chips + 3 * nctx,))
    own_shape = (nctx, own_rows, qkv_width + q_width)
    sources = (
        grad_middle_all.reshape(blocks, HALF, D),
        w_attn,
        q,
        k,
        v,
        mixed,
        qk.reshape(blocks, HALF, qk_width),
        table.reshape(blocks, HALF, 2 * HD),
        middle,
    )
    out_tokens, grad_joined, qk_gain_grad, out_grad = remote_call(
        functools.partial(attend_back_kernel, blocks, groups),
        [
            own_low,
            jax.ShapeDtypeStruct((stream_len, qkv_width), BF16),
            jax.ShapeDtypeStruct((1, qk_width), F32),
            jax.ShapeDtypeStruct((D, q_width), BF16),
        ],
        (place, order, starts, lse, qk_gain, out_partial) + sources,
        6,
        45,
        [pltpu.VMEM(source.shape, source.dtype) for source in sources]
        + sum_bufs
        + [
            heads_low,
            pltpu.VMEM((blocks, HALF, q_width), F32),
            pltpu.VMEM((blocks, HALF, 2 * kv_width), F32),
            pltpu.VMEM((D, stream_len), BF16),
        ]
        + sum_sems
        + [dma((9,))],
        (),
        3,
        9,
    )
    sources = (w_attn, normed_all, x_low, grad_middle)
    grad_tokens, gain_sums, attn_own, gu_own, down_own = remote_call(
        functools.partial(tail_kernel, 2),
        [
            own_f32,
            jax.ShapeDtypeStruct((8, D), F32),
            jax.ShapeDtypeStruct(own_shape, BF16),
            jax.ShapeDtypeStruct(gu_sum.shape, BF16),
            jax.ShapeDtypeStruct(down_sum.shape, BF16),
        ],
        (grad_joined, out_grad, qk_gain_grad, g_attn, grad_g_ffn) + sources + (gu_sum, down_sum),
        7,
        75,
        [pltpu.VMEM(source.shape, source.dtype) for source in sources]
        + sum_bufs
        + [
            pltpu.VMEM((D, stream_len), BF16),
            low_stream,
            pltpu.VMEM((D, qkv_width + q_width), BF16),
        ]
        + line_scratch(qkv_width + q_width)
        + [
            pltpu.VMEM(own_shape, BF16),
            pltpu.VMEM((nctx, 8, D), F32),
            pltpu.VMEM((nfsdp, 8, D), F32),
        ]
        + sum_sems
        + [line_sems, line_sems, small, small, dma((6,))],
        (3, 4),
        0,
        6,
    )
    last_sum, gain_sums, gu_own = lax.optimization_barrier((last_sum, gain_sums, gu_own))
    out_tokens = unspread(out_tokens)[None]
    grad_tokens = unspread(grad_tokens)[None]
    gain_grad = jnp.concatenate(
        [
            unspread(gain_sums[:1])[0],
            unspread(gain_sums[1:2])[0],
            jnp.sum(gain_sums[2, :q_width].reshape(-1, HD), axis=0),
            jnp.sum(gain_sums[2, q_width:qk_width].reshape(-1, HD), axis=0),
        ]
    )

    olds = (master_weights, moment_one, moment_two)

    def feed_segments(b, pieces, start, stop):
        found = []
        for part in pieces:
            for c in range(nctx):
                column = c * ff_width + cuts[b] + start
                real = min(max(FF - column, 0), stop - start)
                if real:
                    piece, first = pieces[part]
                    found.append((piece, c, first, bases[part] + column, real))
        return found

    width_one = cuts[1]
    last_own = [
        lax.ppermute(
            lax.dynamic_index_in_dim(last_sum, lax.axis_index("ctx") ^ k, 0, keepdims=False),
            "ctx",
            [(c, c ^ k) for c in range(nctx)],
        )
        if k
        else lax.dynamic_index_in_dim(last_sum, lax.axis_index("ctx"), 0, keepdims=False)
        for k in range(nctx)
    ]
    news = adam(
        feed_segments(0, {0: (0, 0), 1: (0, width_one)}, 0, width_one)
        + feed_segments(0, {2: (1, 0)}, 0, width_line),
        [gu_own, down_own],
        olds,
        None,
        7,
    )
    parts = (
        (0, 0, q_width),
        (q_width, D, kv_width),
        (qk_width, D + KVD, kv_width),
        (qkv_width, QKVC, q_width),
    )
    if kv_width % 128:
        attn_own = jnp.concatenate(
            [attn_own[c, :, f : f + w] for f, _, w in parts for c in range(nctx)], axis=1
        )[None]
        segments = [(0, 0, 0, 0, gate_base)]
    else:
        segments = [
            (0, c, first, base + c * width, width)
            for first, base, width in parts
            for c in range(nctx)
        ]
    news = adam(segments, [attn_own], olds, news, 3)
    first_new, second_new, master_new, low_new = adam(
        feed_segments(
            1,
            {0: (None, 0), 1: (None, width_two), 2: (None, last_width - width_two)},
            0,
            width_two,
        )
        + feed_segments(0, {2: (None, 2 * width_two)}, width_line, width_one),
        last_own,
        olds,
        news,
        6,
    )
    gain_first, gain_second, gain_new = adam_update(
        gains, gain_grad, gains_moment_one, gains_moment_two, GAIN_RATE, 0.0
    )
    return (
        out_tokens,
        grad_tokens,
        first_new,
        second_new,
        master_new,
        low_new,
        gain_first,
        gain_second,
        gain_new,
    )


def solution(mesh):
    rows = P("fsdp", "ctx", None)
    weights = P(("ctx", "fsdp"), None)
    return jax.shard_map(
        shards,
        mesh=mesh,
        in_specs=(rows, rows, P("fsdp", None), P(), weights, weights, weights, P(), P(), P()),
        out_specs=(rows, rows, weights, weights, weights, weights, P(), P(), P()),
        check_vma=False,
    )
```

```python
import functools

import jax
import jax.numpy as jnp
from jax import lax
from jax.experimental import pallas as pl
from jax.experimental.pallas import tpu as pltpu
from jax.sharding import PartitionSpec as P

D = 1536
HEADS = 24
KVHEADS = 8
HD = 64
FF = 6912
STEP = 10
HALF = 128
KVD = 512
QKVC = 2560
GROUP = HEADS // KVHEADS

ROPE_BASE = 1000000.0
NORM_EPS = 1e-05
BETA_ONE = 0.9
BETA_TWO = 0.95
ADAM_EPS = 1e-08
WEIGHT_DECAY = 0.1
LEARN_RATE = 0.03
GAIN_RATE = 0.5
SCALE = HD ** (-0.5)
MESH = pl.DeviceIdType.MESH
F32 = jnp.float32
BF16 = jnp.bfloat16
VMEM_LIMIT = 60 * 1024 * 1024


def dot(left, right, left_dim, right_dim):
    return lax.dot_general(
        left, right, (((left_dim,), (right_dim,)), ((), ())), preferred_element_type=F32
    )


def send(source, target, sems, item, peer):
    copy = pltpu.make_async_remote_copy(
        src_ref=source,
        dst_ref=target,
        send_sem=sems[0].at[item],
        recv_sem=sems[1].at[item],
        device_id=peer,
        device_id_type=MESH,
    )
    copy.start()
    return copy


def meet(axes):
    barrier = pltpu.get_barrier_semaphore()
    total = 0
    for axis in axes:
        size = lax.axis_size(axis)
        me = lax.axis_index(axis)
        for step in range(1, size):
            pl.semaphore_signal(
                barrier,
                inc=1,
                device_id={axis: lax.rem(me + step, size)},
                device_id_type=MESH,
            )
        total += size - 1
    pl.semaphore_wait(barrier, total)


def square():
    me = lax.axis_index("ctx")
    return me, me + 1 - 2 * lax.rem(me, 2), lax.rem(me + 2, 4), 3 - me


def swap_start(source, target, sems, base):
    size = lax.axis_size("ctx")
    me = lax.axis_index("ctx")
    copies = []
    for step in range(1, size):
        peer = lax.rem(me + step, size)
        copies.append(
            send(source.at[peer], target.at[me], sems, base + step, {"ctx": peer})
        )
    return copies


def gather_start(source, target, sems, base):
    size = lax.axis_size("ctx")
    me = lax.axis_index("ctx")
    if size != 4:
        return [
            send(
                source,
                target.at[me],
                sems,
                base + step,
                {"ctx": lax.rem(me + step, size)},
            )
            for step in range(1, size)
        ]
    me, side, over, across = square()
    half = source.shape[0] // 2
    top, low = pl.ds(0, half), pl.ds(half, half)
    return [
        send(source.at[top], target.at[me, top], sems, base, {"ctx": side}),
        send(source.at[low], target.at[me, low], sems, base + 1, {"ctx": over}),
        send(source.at[low], target.at[me, low], sems, base + 2, {"ctx": side}),
        send(source.at[top], target.at[me, top], sems, base + 3, {"ctx": over}),
    ]


def gather_pass(copies, target, sems, base):
    if lax.axis_size("ctx") != 4:
        return
    me, side, over, across = square()
    half = target.shape[1] // 2
    top, low = pl.ds(0, half), pl.ds(half, half)
    copies[0].wait_recv()
    copies.append(send(target.at[side, top], target.at[side, top], sems, base + 4, {"ctx": over}))
    copies[1].wait_recv()
    copies.append(send(target.at[over, low], target.at[over, low], sems, base + 5, {"ctx": side}))


def gather_end(copies):
    if lax.axis_size("ctx") != 4:
        for copy in copies:
            copy.wait()
        return
    for copy in copies:
        copy.wait_send()
    for copy in copies[2:]:
        copy.wait_recv()


def gather_rest(copies, target, sems, base):
    gather_pass(copies, target, sems, base)
    gather_end(copies)


def load(source, target, sem):
    copy = pltpu.make_async_copy(source, target, sem)
    copy.start()
    return copy


GATHER_SEMS = 8


def exchange_kernel(kinds, *refs):
    count = len(kinds)
    ins, outs = refs[:count], refs[count : 2 * count]
    send_sem, recv_sem, local_sem = refs[2 * count :]
    sems = (send_sem, recv_sem)
    me = lax.axis_index("ctx")
    meet(("ctx",))
    copies = []
    own = []
    for item in range(count):
        base = item * GATHER_SEMS
        if kinds[item] == "gather":
            copies.append(gather_start(ins[item], outs[item], sems, base))
            source = ins[item]
        else:
            copies.append(swap_start(ins[item], outs[item], sems, base))
            source = ins[item].at[me]
        copy = pltpu.make_async_copy(source, outs[item].at[me], local_sem.at[item])
        copy.start()
        own.append(copy)
    for item in range(count):
        if kinds[item] == "gather":
            gather_rest(copies[item], outs[item], sems, item * GATHER_SEMS)
        else:
            for copy in copies[item]:
                copy.wait()
    for copy in own:
        copy.wait()


def remote_params(collective_id):
    return pltpu.CompilerParams(
        collective_id=collective_id, has_side_effects=True, vmem_limit_bytes=VMEM_LIMIT
    )


def cost(micros):
    return pl.CostEstimate(flops=0, bytes_accessed=int(micros * 3.0e6), transcendentals=0)


def exchange(kinds, arrays, collective_id, micros):
    size = lax.axis_size("ctx")
    shapes = [
        jax.ShapeDtypeStruct((size,) + a.shape if kind == "gather" else a.shape, a.dtype)
        for kind, a in zip(kinds, arrays)
    ]
    sems = pltpu.SemaphoreType.DMA((len(arrays) * GATHER_SEMS,))
    return pl.pallas_call(
        functools.partial(exchange_kernel, kinds),
        out_shape=shapes,
        in_specs=[pl.BlockSpec(memory_space=pl.ANY)] * len(arrays),
        out_specs=[pl.BlockSpec(memory_space=pl.ANY)] * len(arrays),
        scratch_shapes=[sems, sems, pltpu.SemaphoreType.DMA((len(arrays),))],
        compiler_params=remote_params(collective_id),
        cost_estimate=cost(micros),
    )(*arrays)


def sum_scratch(size, rows):
    if size == 4:
        half = pltpu.VMEM((2, rows // 2, D), BF16)
        return [half, half, pltpu.VMEM((2, rows, D), BF16)]
    return [pltpu.VMEM((size - 1, rows, D), BF16)]


def sum_start(part, bufs, sems):
    size = lax.axis_size("ctx")
    me = lax.axis_index("ctx")
    rows = part.shape[0] // size

    def block(owner, first=0, count=rows):
        return pl.ds(pl.multiple_of(owner * rows + first, rows // 2), count)

    if size != 4:
        copies = []
        for step in range(1, size):
            peer = lax.rem(me + step, size)
            copies.append(
                send(part.at[block(peer)], bufs[0].at[step - 1], sems, step, {"ctx": peer})
            )
        return copies
    me, side, over, across = square()
    half = rows // 2
    relay, _, landed = bufs
    return [
        send(part.at[block(across, 0, half)], relay.at[0], sems, 0, {"ctx": side}),
        send(part.at[block(across, half, half)], relay.at[1], sems, 1, {"ctx": over}),
        send(
            part.at[block(side, 0, half)],
            landed.at[0, pl.ds(0, half)],
            sems,
            2,
            {"ctx": side},
        ),
        send(
            part.at[block(over, half, half)],
            landed.at[1, pl.ds(half, half)],
            sems,
            3,
            {"ctx": over},
        ),
    ]


def sum_pass(copies, part, bufs, sems):
    if lax.axis_size("ctx") != 4:
        return
    rows = part.shape[0] // 4
    half = rows // 2

    def rows_of(owner, first):
        return pl.ds(pl.multiple_of(owner * rows + first, half), half)

    me, side, over, across = square()
    relay, passed, landed = bufs
    copies[0].wait_recv()
    passed[0] = (part[rows_of(over, 0), :].astype(F32) + relay[0].astype(F32)).astype(BF16)
    copies.append(
        send(passed.at[0], landed.at[1, pl.ds(0, half)], sems, 4, {"ctx": over})
    )
    copies[1].wait_recv()
    passed[1] = (part[rows_of(side, half), :].astype(F32) + relay[1].astype(F32)).astype(
        BF16
    )
    copies.append(
        send(passed.at[1], landed.at[0, pl.ds(half, half)], sems, 5, {"ctx": side})
    )


def sum_rest(copies, part, bufs):
    size = lax.axis_size("ctx")
    me = lax.axis_index("ctx")
    rows = part.shape[0] // size
    half = rows // 2

    def rows_of(owner, first):
        return pl.ds(pl.multiple_of(owner * rows + first, half), half)

    if size != 4:
        for copy in copies:
            copy.wait()

        def read(first):
            total = part[rows_of(me, first), :].astype(F32)
            for step in range(1, size):
                total = total + bufs[0][step - 1, pl.ds(first, half), :].astype(F32)
            return total

        return read
    relay, passed, landed = bufs
    for copy in copies:
        copy.wait_send()
    for copy in copies[2:]:
        copy.wait_recv()

    def read(first):
        return (
            part[rows_of(me, first), :].astype(F32)
            + landed[0, pl.ds(first, half), :].astype(F32)
            + landed[1, pl.ds(first, half), :].astype(F32)
        )

    return read


def row_scale(values):
    return lax.rsqrt(jnp.mean(values * values, axis=-1, keepdims=True) + NORM_EPS)


def first_kernel(
    starts, origin, x, dy, gain, freq, x_low, dy_low, table, normed_all, *scratch
):
    move, normed, send_one, recv_one, local = scratch
    me = lax.axis_index("ctx")
    row = lax.broadcasted_iota(jnp.int32, move.shape, 0)
    move[...] = jnp.where(row == origin[...], 1.0, 0.0).astype(BF16)
    values = dot(x[...], move[...], 1, 0)
    x_low[...] = values.astype(BF16)
    normed[...] = (values * row_scale(values) * gain[...]).astype(BF16)
    meet(("ctx",))
    sems = (send_one, recv_one)
    copies = gather_start(normed, normed_all, sems, 0)
    own = load(normed, normed_all.at[me], local)
    dy_low[...] = dot(dy[...], move[...], 1, 0).astype(BF16)
    gather_pass(copies, normed_all, sems, 0)
    times = lax.broadcasted_iota(jnp.int32, (table.shape[0], 1), 0)
    angles = (times - doc_first(starts, times)).astype(F32) * freq[...]
    lane = lax.broadcasted_iota(jnp.int32, angles.shape, 1)
    sine = jnp.sin(angles)
    sine = jnp.where(lane % HD < HD // 2, -sine, sine)
    table[...] = jnp.where(lane < HD, jnp.cos(angles), sine)
    gather_end(copies)
    own.wait()


def middle_kernel(part, x, gain, middle, normed_all, *scratch):
    bufs, (normed, send_one, recv_one, send_two, recv_two, local) = scratch[:-6], scratch[-6:]
    me = lax.axis_index("ctx")
    meet(("ctx",))
    copies = sum_start(part, bufs, (send_one, recv_one))
    sum_pass(copies, part, bufs, (send_one, recv_one))
    read = sum_rest(copies, part, bufs)
    half = x.shape[0] // 2
    for first in (0, half):
        rows = pl.ds(first, half)
        values = x[rows, :].astype(F32) + read(first)
        middle[rows, :] = values
        normed[rows, :] = (values * row_scale(values) * gain[...]).astype(BF16)
    sems = (send_two, recv_two)
    copies = gather_start(normed, normed_all, sems, 0)
    own = load(normed, normed_all.at[me], local)
    gather_rest(copies, normed_all, sems, 0)
    own.wait()


def column_tiles(total, body):
    def step(tile, carry):
        body(pl.multiple_of(tile * 256, 256), 256)
        return carry

    lax.fori_loop(0, total // 256, step, 0)
    if total % 256:
        body(total - total % 256, total % 256)


def turn(source, target):
    for first in range(0, source.shape[0], HALF):
        rows = slice(first, first + HALF)
        target[:, rows] = source[rows, :].T


def middle_back_kernel(
    part,
    middle,
    dy,
    gain,
    x_all,
    dy_all,
    hidden_one,
    hidden_two,
    grad_gu,
    w_one,
    w_two,
    grad,
    gain_grad,
    down_sum,
    grad_all,
    rest_grad,
    weight_grad,
    out,
    *scratch,
):
    bufs = scratch[:-21]
    low, x_buf, gu_buf, turned, weight_buf, rest_buf, down_grad, out_buf = scratch[-21:-13]
    hidden_bufs, down_bufs = scratch[-13:-11], scratch[-11:-9]
    home, travel, send_one, recv_one, send_two, recv_two, send_three, recv_three, local = (
        scratch[-9:]
    )
    going, coming = travel.at[0], travel.at[1]
    me = lax.axis_index("ctx")
    chips = lax.axis_size("fsdp") // 2
    line = (send_three, recv_three)
    meet(("ctx", "fsdp"))
    copies = sum_start(part, bufs, (send_one, recv_one))
    width_one, width_two = hidden_one.shape[1], hidden_two.shape[1]
    gu_width = grad_gu.shape[1]
    loads = [
        load(source, target, local.at[item])
        for item, (source, target) in enumerate(
            (
                (dy_all, x_buf),
                (hidden_one, hidden_bufs[0]),
                (hidden_two, hidden_bufs[1]),
                (grad_gu, gu_buf),
                (w_one.at[:, pl.ds(2 * width_one, width_one)], down_bufs[0]),
                (w_two.at[:, pl.ds(2 * width_two, width_two)], down_bufs[1]),
            )
        )
    ]
    loads[0].wait()
    turn(x_buf, turned)
    loads.append(load(x_all, x_buf, local.at[6]))
    loads[1].wait()

    def product(target, column, right, begin=0, count=None):
        def tile(first, width):
            target[:, pl.ds(column + first, width)] = dot(
                turned[...], right[:, pl.ds(begin + first, width)], 1, 0
            ).astype(BF16)

        column_tiles(right.shape[1] if count is None else count, tile)

    width_line = down_grad.shape[1]
    product(down_grad, 0, hidden_bufs[0], 0, width_line)
    home_copies = line_start(down_grad, home, line, 0)
    product(rest_buf, 0, hidden_bufs[0], width_line, width_one - width_line)
    stores = [load(rest_buf, rest_grad, local.at[10])]
    sum_pass(copies, part, bufs, (send_one, recv_one))
    line_home(home_copies, down_grad, home)
    line_step(chips - 1, home, going, coming, line, chips)
    loads[2].wait()
    product(weight_buf, gu_width, hidden_bufs[1])
    loads[6].wait()
    turn(x_buf, turned)
    loads[3].wait()
    product(weight_buf, 0, gu_buf)
    stores.append(load(weight_buf, weight_grad, local.at[7]))
    if chips > 2:
        line_step(chips - 2, home, going, coming, line, chips)
    read = sum_rest(copies, part, bufs)
    half = dy.shape[0] // 2
    total = jnp.zeros((1, D), F32)
    for first in (0, half):
        rows = pl.ds(first, half)
        values = middle[rows, :]
        root = row_scale(values)
        unit = values * root
        back = read(first)
        total = total + jnp.sum(back * unit, axis=0, keepdims=True)
        back = back * gain[...]
        back = root * (back - unit * jnp.mean(back * unit, axis=-1, keepdims=True))
        back = back + dy[rows, :].astype(F32)
        grad[rows, :] = back
        low[rows, :] = back.astype(BF16)
    gain_grad[...] = total
    sems = (send_two, recv_two)
    copies = gather_start(low, grad_all, sems, 0)
    stores.append(load(low, grad_all.at[me], local.at[8]))
    loads[4].wait()
    loads[5].wait()

    def out_tile(first, width):
        columns = pl.ds(first, width)
        out_buf[:, columns] = (
            dot(hidden_bufs[0][...], down_bufs[0][columns, :], 1, 1)
            + dot(hidden_bufs[1][...], down_bufs[1][columns, :], 1, 1)
        ).astype(BF16)

    column_tiles(D, out_tile)
    stores.append(load(out_buf, out, local.at[9]))
    gather_pass(copies, grad_all, sems, 0)
    for reach in range(min(chips - 1, max(chips - 3, 1)), 0, -1):
        line_step(reach, home, going, coming, line, chips)
    line_end(home_copies, home, going, coming, line, chips)
    chip = lax.axis_index("fsdp") // 2
    rows = down_sum.shape[1]
    for index in range(down_sum.shape[0]):
        down_sum[index] = home[chip, index * rows : (index + 1) * rows, :]
    gather_end(copies)
    for copy in stores:
        copy.wait()


def line_start(grad, home, sems, base):
    me = lax.axis_index("fsdp")
    chips = lax.axis_size("fsdp") // 2
    core = lax.rem(me, 2)
    rows = grad.shape[0] // (2 * chips)
    copies = []
    for chip in range(chips):
        theirs = pl.ds(pl.multiple_of((2 * chip + 1 - core) * rows, rows), rows)
        copies.append(
            send(grad.at[theirs], home.at[chip], sems, base + chip, {"fsdp": me + 1 - 2 * core})
        )
    return copies


def line_home(copies, grad, home):
    me = lax.axis_index("fsdp")
    chips = lax.axis_size("fsdp") // 2
    core = lax.rem(me, 2)
    rows = grad.shape[0] // (2 * chips)
    for chip in range(chips):
        copies[chip].wait_recv()
        mine = pl.ds(pl.multiple_of((2 * chip + core) * rows, rows), rows)
        home[chip] = (home[chip].astype(F32) + grad[mine, :].astype(F32)).astype(BF16)


def line_copies(reach, going, coming, sems, base):
    me = lax.axis_index("fsdp")
    chips = lax.axis_size("fsdp") // 2
    chip = me // 2
    found = []
    for side, way in ((0, 1), (1, -1)):
        copy = pltpu.make_async_remote_copy(
            src_ref=going.at[side, reach - 1],
            dst_ref=coming.at[side, reach - 1],
            send_sem=sems[0].at[base + 2 * reach + side],
            recv_sem=sems[1].at[base + 2 * reach + side],
            device_id={"fsdp": lax.rem(me + 2 * way + 2 * chips, 2 * chips)},
            device_id_type=MESH,
        )
        if way == 1:
            sent = chip + reach <= chips - 1
            got = (chip >= 1) & (chip + reach <= chips)
            more = (chip >= 1) & sent
        else:
            sent = chip >= reach
            got = (chip <= chips - 2) & (chip + 1 >= reach)
            more = (chip <= chips - 2) & sent
        found.append((side, way, copy, sent, got, more))
    return found


def line_step(reach, home, going, coming, sems, base):
    me = lax.axis_index("fsdp")
    chips = lax.axis_size("fsdp") // 2
    chip = me // 2
    if reach < chips - 1:
        for _, _, copy, _, got, _ in line_copies(reach + 1, going, coming, sems, base):
            pl.when(got)(copy.wait_recv)
    for side, way, copy, sent, _, more in line_copies(reach, going, coming, sems, base):

        @pl.when(sent)
        def _(side=side, way=way, copy=copy, more=more):
            value = home[chip + way * reach]
            if reach < chips - 1:

                @pl.when(more)
                def _():
                    going[side, reach - 1] = (
                        value.astype(F32) + coming[side, reach].astype(F32)
                    ).astype(BF16)

                @pl.when(jnp.logical_not(more))
                def _():
                    going[side, reach - 1] = value

            else:
                going[side, reach - 1] = value
            copy.start()


def line_end(copies, home, going, coming, sems, base):
    me = lax.axis_index("fsdp")
    chips = lax.axis_size("fsdp") // 2
    chip = me // 2
    for side, _, copy, _, got, _ in line_copies(1, going, coming, sems, base):

        @pl.when(got)
        def _(side=side, copy=copy):
            copy.wait_recv()
            home[chip] = (home[chip].astype(F32) + coming[side, 0].astype(F32)).astype(BF16)

    for copy in copies:
        copy.wait_send()
    for reach in range(1, chips):
        for _, _, copy, sent, _, _ in line_copies(reach, going, coming, sems, base):
            pl.when(sent)(copy.wait_send)


def remote_call(
    kernel, out_shape, args, collective_id, micros, scratch, in_hbm=(), smem=0, args_in_hbm=0
):
    return pl.pallas_call(
        kernel,
        out_shape=out_shape,
        in_specs=[pl.BlockSpec(memory_space=pltpu.SMEM)] * smem
        + [pl.BlockSpec(memory_space=pltpu.VMEM)] * (len(args) - smem - args_in_hbm)
        + [pl.BlockSpec(memory_space=pl.ANY)] * args_in_hbm,
        out_specs=[
            pl.BlockSpec(memory_space=pl.ANY if item in in_hbm else pltpu.VMEM)
            for item in range(len(out_shape))
        ],
        scratch_shapes=scratch,
        compiler_params=remote_params(collective_id),
        cost_estimate=cost(micros),
    )(*args)


def adam_update(param_now, grad_now, moment_old_one, moment_old_two, step_rate, decay_rate):
    first_new = BETA_ONE * moment_old_one + (1.0 - BETA_ONE) * grad_now
    second_new = BETA_TWO * moment_old_two + (1.0 - BETA_TWO) * grad_now * grad_now
    ratio = (
        first_new
        / (1.0 - BETA_ONE**STEP)
        / (jnp.sqrt(second_new / (1.0 - BETA_TWO**STEP)) + ADAM_EPS)
    )
    return (first_new, second_new, param_now - step_rate * (ratio + decay_rate * param_now))


def adam_kernel(segments, pieces, held, *refs):
    me = lax.axis_index("ctx")
    grads = refs[:pieces]
    olds = refs[pieces : pieces + 3]
    news = refs[pieces + 3 + held : pieces + 3 + held + 4]
    grad_buf, old_buf, low_buf, in_sem, out_sem = refs[pieces + 3 + held + 4 :]
    base = min(segment[3] for segment in segments)
    loads = []
    for number, (piece, index, first, column, width) in enumerate(segments):
        here = pl.ds(column - base, width)
        there = pl.ds(column, width)
        columns = pl.ds(first, width)
        copies = []
        for number_from, source in enumerate(grads):
            if piece not in (None, number_from):
                continue
            copy = pltpu.make_async_copy(
                source.at[:, columns] if piece is None else source.at[index, :, columns],
                grad_buf.at[:, here],
                in_sem.at[3, number],
            )
            if piece is None:
                pl.when(me == index ^ number_from)(copy.start)
            else:
                copy.start()
        loads.append([copy])
        copies += [
            pltpu.make_async_copy(
                olds[item].at[:, there], old_buf.at[item, :, here], in_sem.at[item, number]
            )
            for item in range(3)
        ]
        for copy in copies:
            copy.start()
        loads[-1] += copies
    stores = []
    for number, (piece, index, first, column, width) in enumerate(segments):
        for copy in loads[number]:
            copy.wait()
        here = pl.ds(column - base, width)
        there = pl.ds(column, width)
        first_new, second_new, master = adam_update(
            old_buf[0, :, here],
            grad_buf[:, here].astype(F32),
            old_buf[1, :, here],
            old_buf[2, :, here],
            LEARN_RATE,
            WEIGHT_DECAY,
        )
        old_buf[0, :, here] = master
        old_buf[1, :, here] = first_new
        old_buf[2, :, here] = second_new
        low_buf[:, here] = master.astype(BF16)
        for item, source in enumerate(
            (
                old_buf.at[1, :, here],
                old_buf.at[2, :, here],
                old_buf.at[0, :, here],
                low_buf.at[:, here],
            )
        ):
            copy = pltpu.make_async_copy(
                source, news[item].at[:, there], out_sem.at[item, number]
            )
            copy.start()
            stores.append(copy)
    for copy in stores:
        copy.wait()


def adam(segments, grads, olds, held, micros):
    rows, columns = olds[0].shape
    span = max(s[3] + s[4] for s in segments) - min(s[3] for s in segments)
    held = [] if held is None else list(held)
    args = list(grads) + list(olds) + held
    return pl.pallas_call(
        functools.partial(adam_kernel, tuple(segments), len(grads), len(held)),
        out_shape=[jax.ShapeDtypeStruct((rows, columns), F32)] * 3
        + [jax.ShapeDtypeStruct((rows, columns), BF16)],
        in_specs=[pl.BlockSpec(memory_space=pl.ANY)] * len(args),
        out_specs=[pl.BlockSpec(memory_space=pl.ANY)] * 4,
        input_output_aliases={len(grads) + 3 + item: item for item in range(len(held))},
        scratch_shapes=[
            pltpu.VMEM((rows, span), BF16),
            pltpu.VMEM((3, rows, span), F32),
            pltpu.VMEM((rows, span), BF16),
            pltpu.SemaphoreType.DMA((4, len(segments))),
            pltpu.SemaphoreType.DMA((4, len(segments))),
        ],
        compiler_params=pltpu.CompilerParams(vmem_limit_bytes=VMEM_LIMIT),
        cost_estimate=cost(micros),
    )(*args)


def head_mean(values, ones):
    high = values.astype(BF16)
    rest = (values - high.astype(F32)).astype(BF16)
    return (dot(high, ones, 1, 0) + dot(rest, ones, 1, 0)) * (1.0 / HD)


def head_ones(width):
    row = lax.broadcasted_iota(jnp.int32, (width, width), 0) // HD
    col = lax.broadcasted_iota(jnp.int32, (width, width), 1) // HD
    return jnp.where(row == col, 1.0, 0.0).astype(BF16)


def partner(values):
    width = values.shape[-1]
    lane = lax.broadcasted_iota(jnp.int32, values.shape, 1)
    return jnp.where(
        lane % HD < HD // 2,
        pltpu.roll(values, width - HD // 2, 1),
        pltpu.roll(values, HD // 2, 1),
    )


def widen(table, width):
    return [
        jnp.concatenate([part] * (width // HD), axis=-1)
        for part in (table[:, :HD], table[:, HD:])
    ]


def doc_first(starts, times):
    first = jnp.zeros_like(times)
    for item in range(starts.shape[0]):
        first = jnp.where(starts[item] <= times, starts[item], first)
    return first


def block_mask(starts, block, keys):
    shape = (keys, GROUP * HALF)
    times = block * HALF + lax.broadcasted_iota(jnp.int32, (1, GROUP * HALF), 1) % HALF
    key = lax.broadcasted_iota(jnp.int32, shape, 0)
    return (key >= doc_first(starts, times)) & (key <= times)


def stack_heads(ref, rows, group):
    return jnp.concatenate(
        [
            ref[rows, (group * GROUP + h) * HD : (group * GROUP + h + 1) * HD]
            for h in range(GROUP)
        ],
        axis=0,
    )


def unstack_heads(turned):
    wide = turned.T
    return [wide[h * HALF : (h + 1) * HALF, :] for h in range(GROUP)]


def attend_kernel(
    blocks,
    groups,
    place,
    order,
    starts,
    table,
    gain,
    normed_in,
    weights_from,
    dy,
    swap_in,
    part,
    qk,
    q,
    k,
    v,
    o_held,
    lse,
    dy_all,
    swap_out,
    normed,
    weights_in,
    joined,
    o,
    send_sem,
    recv_sem,
    local,
):
    sems = (send_sem, recv_sem)
    me = lax.axis_index("ctx")
    qk_width = qk.shape[1]
    q_width = q.shape[1]
    qkv_width = qk_width + v.shape[1]
    ones = head_ones(qk_width)
    meet(("ctx",))
    loads = [
        load(normed_in, normed, local.at[0]),
        load(weights_from, weights_in, local.at[1]),
    ]
    swap_copies = swap_start(swap_in, swap_out, sems, GATHER_SEMS)
    copies = gather_start(dy, dy_all, sems, 0)
    own_copies = [
        load(swap_in.at[me], swap_out.at[me], local.at[2]),
        load(dy, dy_all.at[me], local.at[3]),
    ]
    for copy in loads:
        copy.wait()
    for block in range(blocks):
        joined[block] = dot(
            normed[block * HALF : (block + 1) * HALF, :], weights_in[:, :qkv_width], 1, 0
        )
    for block in range(blocks):
        to = slice(block * HALF, (block + 1) * HALF)
        values = joined[place[block]]
        v[to, :] = values[:, qk_width:].astype(BF16)
        values = values[:, :qk_width]
        qk[to, :] = values
        turned = values * lax.rsqrt(head_mean(values * values, ones) + NORM_EPS) * gain[...]
        cosine, sine = widen(table[to, :], qk_width)
        turned = turned * cosine + partner(turned) * sine
        turned = turned.astype(BF16)
        q[to, :] = turned[:, :q_width]
        k[to, :] = turned[:, q_width:]
    for block in range(blocks):
        rows = slice(block * HALF, (block + 1) * HALF)
        keys = (block + 1) * HALF
        mask = block_mask(starts, block, keys)
        pieces = []
        for group in range(groups):
            lanes = slice(group * HD, (group + 1) * HD)
            queries = stack_heads(q, rows, group)
            scores = dot(k[:keys, lanes], queries, 1, 1) * SCALE
            weights = jnp.where(mask, jnp.exp(scores), 0.0)
            sums = jnp.sum(weights, axis=0, keepdims=True)
            lse[block, group : group + 1, :] = jnp.log(sums)
            mixed = dot(v[:keys, lanes], weights.astype(BF16), 0, 0) / sums
            pieces += unstack_heads(mixed)
        o[block] = jnp.concatenate(pieces, axis=1).astype(BF16)
    for block in range(blocks):
        o_held[block * HALF : (block + 1) * HALF, :] = o[order[block]]
    for first in range(0, D, 512):
        part[:, first : first + 512] = dot(
            o_held[...], weights_in[first : first + 512, qkv_width:], 1, 1
        ).astype(BF16)
    gather_rest(copies, dy_all, sems, 0)
    for copy in swap_copies:
        copy.wait()
    for copy in own_copies:
        copy.wait()


def attend_back_kernel(
    blocks,
    groups,
    place,
    order,
    starts,
    lse,
    gain,
    part,
    rest_grad,
    *refs,
):
    sources, refs = refs[:9], refs[9:]
    out, joined, gain_grad, out_grad, rest_sum = refs[:5]
    targets, refs = refs[5:14], refs[14:]
    grad_all, weights_in, q, k, v, o, qk, table, middle = targets
    bufs, (do, dq, dkv, turned, home, travel) = refs[:-11], refs[-11:-5]
    send_one, recv_one, send_two, recv_two, local = refs[-5:]
    going, coming = travel.at[0], travel.at[1]
    line = (send_two, recv_two)
    chips = lax.axis_size("fsdp") // 2
    out_sems = (send_one, recv_one)
    qk_width = qk.shape[2]
    qkv_width = qk_width + v.shape[1]
    ones = head_ones(qk_width)
    meet(("ctx", "fsdp"))
    home_copies = line_start(rest_grad, home, line, 0)
    out_copies = sum_start(part, bufs, out_sems)
    loads = [
        load(source, target, local.at[item])
        for item, (source, target) in enumerate(zip(sources, targets))
    ]
    for copy in loads[:6]:
        copy.wait()
    for block in range(blocks):
        do[block * HALF : (block + 1) * HALF, :] = dot(
            grad_all[place[block]], weights_in[:, qkv_width:], 1, 0
        ).astype(BF16)
    for block in range(blocks):
        turned[:, block * HALF : (block + 1) * HALF] = grad_all[block].T
    for first in range(0, D, 512):
        rows = slice(first, first + 512)
        out_grad[rows, :] = dot(turned[rows, :], o[...], 1, 0).astype(BF16)
    dkv[...] = jnp.zeros_like(dkv)
    line_home(home_copies, rest_grad, home)
    line_step(chips - 1, home, going, coming, line, chips)
    reach = chips - 2
    for block in range(blocks):
        if block == blocks // 2:
            sum_pass(out_copies, part, bufs, out_sems)
        if block >= blocks * 3 // 4 and reach > 1:
            line_step(reach, home, going, coming, line, chips)
            reach -= 1
        rows = slice(block * HALF, (block + 1) * HALF)
        keys = (block + 1) * HALF
        mask = block_mask(starts, block, keys)
        pieces = []
        dk_add = []
        dv_add = []
        for group in range(groups):
            lanes = slice(group * HD, (group + 1) * HD)
            queries = stack_heads(q, rows, group)
            outs = stack_heads(do, rows, group)
            key_rows = k[:keys, lanes]
            scores = dot(key_rows, queries, 1, 1) * SCALE
            weights = jnp.where(
                mask, jnp.exp(scores - lse[block, group : group + 1, :]), 0.0
            )
            back = dot(v[:keys, lanes], outs, 1, 1)
            delta = jnp.sum(weights * back, axis=0, keepdims=True)
            grads = (weights * (back - delta)).astype(BF16)
            pieces += unstack_heads(dot(key_rows, grads, 0, 0) * SCALE)
            dk_add.append(dot(grads, queries, 1, 0) * SCALE)
            dv_add.append(dot(weights.astype(BF16), outs, 1, 0))
        dq[block] = jnp.concatenate(pieces, axis=1)
        dkv[: block + 1] += jnp.concatenate(dk_add + dv_add, axis=1).reshape(
            (block + 1,) + dkv.shape[1:]
        )
    for step in range(reach, 0, -1):
        line_step(step, home, going, coming, line, chips)
    gain_row = jnp.zeros((1, qk_width), F32)
    for copy in loads[6:]:
        copy.wait()
    for block in range(blocks):
        here = order[block]
        values = qk[here]
        root = lax.rsqrt(head_mean(values * values, ones) + NORM_EPS)
        unit = values * root
        grad_kv = dkv[here]
        kv_width = grad_kv.shape[1] // 2
        grad = jnp.concatenate([dq[here], grad_kv[:, :kv_width]], axis=1)
        cosine, sine = widen(table[here], qk_width)
        grad = grad * cosine - partner(grad) * sine
        gain_row = gain_row + jnp.sum(grad * unit, axis=0, keepdims=True)
        grad = grad * gain[...]
        grad = root * (grad - unit * head_mean(grad * unit, ones))
        joined[block * HALF : (block + 1) * HALF, :] = jnp.concatenate(
            [grad, grad_kv[:, kv_width:]], axis=1
        ).astype(BF16)
    gain_grad[...] = gain_row
    read = sum_rest(out_copies, part, bufs)
    half = middle.shape[0] // 2
    for first in (0, half):
        rows = pl.ds(first, half)
        out[rows, :] = (middle[rows, :] + read(first)).astype(BF16)
    line_end(home_copies, home, going, coming, line, chips)
    chip = lax.axis_index("fsdp") // 2
    owned_rows = rest_sum.shape[1]
    for index in range(rest_sum.shape[0]):
        rest_sum[index] = home[chip, index * owned_rows : (index + 1) * owned_rows, :]


def tail_kernel(
    swaps,
    joined,
    out_grad,
    gain_row,
    attn_gain,
    ffn_gain_grad,
    *refs,
):
    sources, refs = refs[:4], refs[4:]
    swap_in, refs = refs[:swaps], refs[swaps:]
    grad_tokens, gains, attn_own = refs[:3]
    swap_out, refs = refs[3 : 3 + swaps], refs[3 + swaps :]
    targets, refs = refs[:4], refs[4:]
    weights_in, normed, x, grad_middle = targets
    back_bufs, refs = refs[:-15], refs[-15:]
    turned, part, attn_grad, home, travel, owned, ctx_box, fsdp_box = refs[:8]
    send_two, recv_two, send_three, recv_three, send_four, recv_four, local = refs[8:]
    going, coming = travel.at[0], travel.at[1]
    back_sems = (send_two, recv_two)
    line, small = (send_three, recv_three), (send_four, recv_four)
    size = lax.axis_size("ctx")
    me = lax.axis_index("ctx")
    chips = lax.axis_size("fsdp") // 2
    step_base = chips
    swap_base = step_base + 2 * chips
    qkv_width = joined.shape[1]
    qk_width = gain_row.shape[1]
    half = x.shape[0] // 2
    loads = [
        load(source, target, local.at[item])
        for item, (source, target) in enumerate(zip(sources, targets))
    ]
    meet(("ctx", "fsdp"))
    swap_copies = []
    own_copies = []
    for item in range(swaps):
        swap_copies += swap_start(
            swap_in[item], swap_out[item], line, swap_base + (item + 1) * size
        )
        own_copies.append(
            load(swap_in[item].at[me], swap_out[item].at[me], local.at[4 + item])
        )
    for copy in loads:
        copy.wait()
    for first in range(0, D, 512):
        part[:, first : first + 512] = dot(
            joined[...], weights_in[first : first + 512, :qkv_width], 1, 1
        ).astype(BF16)
    back_copies = sum_start(part, back_bufs, back_sems)
    turn(normed, turned)
    for first in range(0, D, 512):
        rows = slice(first, first + 512)
        attn_grad[rows, :qkv_width] = dot(turned[rows, :], joined[...], 1, 0).astype(BF16)
    attn_grad[:, qkv_width:] = out_grad[...]
    home_copies = line_start(attn_grad, home, line, 0)
    line_home(home_copies, attn_grad, home)
    line_step(chips - 1, home, going, coming, line, step_base)
    sum_pass(back_copies, part, back_bufs, back_sems)
    for reach in range(chips - 2, 1, -1):
        line_step(reach, home, going, coming, line, step_base)
    read = sum_rest(back_copies, part, back_bufs)
    total = jnp.zeros((1, D), F32)
    for first in (0, half):
        rows = pl.ds(first, half)
        values = x[rows, :].astype(F32)
        root = row_scale(values)
        unit = values * root
        back = read(first)
        total = total + jnp.sum(back * unit, axis=0, keepdims=True)
        back = back * attn_gain[...]
        back = root * (back - unit * jnp.mean(back * unit, axis=-1, keepdims=True))
        grad_tokens[rows, :] = grad_middle[rows, :] + back

    def spread_start(axis, box, value, base):
        index = lax.axis_index(axis)
        axis_size = lax.axis_size(axis)
        box[index] = value
        return [
            send(
                box.at[index],
                box.at[index],
                small,
                base + step,
                {axis: lax.rem(index + step, axis_size)},
            )
            for step in range(1, axis_size)
        ]

    def spread_end(copies, box):
        for copy in copies:
            copy.wait()
        summed = box[0]
        for item in range(1, box.shape[0]):
            summed = summed + box[item]
        return summed

    ctx_copies = spread_start(
        "ctx",
        ctx_box,
        jnp.concatenate(
            [
                total,
                ffn_gain_grad[...],
                jnp.concatenate([gain_row[...], jnp.zeros((1, D - qk_width), F32)], axis=1),
                jnp.zeros((5, D), F32),
            ],
            axis=0,
        ),
        0,
    )
    line_step(1, home, going, coming, line, step_base)
    fsdp_copies = spread_start("fsdp", fsdp_box, spread_end(ctx_copies, ctx_box), size)
    line_end(home_copies, home, going, coming, line, step_base)
    chip = lax.axis_index("fsdp") // 2
    owned_rows = owned.shape[1]
    for index in range(size):
        owned[index] = home[chip, index * owned_rows : (index + 1) * owned_rows, :]
    swap_copies += swap_start(owned, attn_own, line, swap_base)
    attn_own[me] = owned[me]
    gains[...] = spread_end(fsdp_copies, fsdp_box)
    for copy in swap_copies:
        copy.wait()
    for copy in own_copies:
        copy.wait()


def rms_scale(values_in, gain_vec):
    return (
        values_in
        * lax.rsqrt(jnp.mean(values_in * values_in, axis=-1, keepdims=True) + NORM_EPS)
        * gain_vec
    )


def inverse_freq():
    return 1.0 / ROPE_BASE ** (jnp.arange(0, HD, 2).astype(F32) / HD)


def shards(
    tokens,
    cotangent,
    doc_starts,
    block_order,
    master_weights,
    moment_one,
    moment_two,
    gains,
    gains_moment_one,
    gains_moment_two,
):
    nctx = lax.axis_size("ctx")
    nfsdp = lax.axis_size("fsdp")
    own_rows = master_weights.shape[0]
    tok_rows = tokens.shape[1]
    stream_len = tok_rows * nctx
    blocks = stream_len // HALF
    groups = KVHEADS // nctx
    q_width = D // nctx
    kv_width = KVD // nctx
    qk_width = q_width + kv_width
    qkv_width = qk_width + kv_width
    tiles = FF // 128
    ff_tiles = -(-tiles // nctx)
    ff_width = ff_tiles * 128
    bundles = 2
    cuts = [0, (ff_tiles * 5 + 3) // 7 * 128, ff_width]

    low = master_weights.astype(BF16)

    def ff_part(base, index, start, stop):
        first = index * ff_width + start
        last = index * ff_width + stop
        real_first, real_last = min(first, FF), min(last, FF)
        part = low[:, base + real_first : base + real_last]
        if real_last - real_first < last - first:
            part = jnp.pad(part, ((0, 0), (0, (last - first) - (real_last - real_first))))
        return part

    def attn_part(index):
        return jnp.concatenate(
            [
                low[:, index * q_width : (index + 1) * q_width],
                low[:, D + index * kv_width : D + (index + 1) * kv_width],
                low[:, D + KVD + index * kv_width : D + KVD + (index + 1) * kv_width],
                low[:, QKVC + index * q_width : QKVC + (index + 1) * q_width],
            ],
            axis=1,
        )

    gate_base = QKVC + D
    bases = (gate_base, gate_base + FF, gate_base + 2 * FF)
    attn_send = jnp.stack([attn_part(c) for c in range(nctx)])
    ff_send = [
        jnp.stack(
            [
                jnp.concatenate(
                    [ff_part(base, c, cuts[b], cuts[b + 1]) for base in bases], axis=1
                )
                for c in range(nctx)
            ]
        )
        for b in range(bundles)
    ]

    def gather_rows(piece):
        return lax.all_gather(
            piece.reshape(nctx * own_rows, piece.shape[-1]), "fsdp", axis=0, tiled=True
        )

    def spread(active):
        return (
            active.reshape(active.shape[0], nctx, nfsdp, own_rows)
            .transpose(0, 2, 1, 3)
            .reshape(active.shape[0], D)
        )

    def unspread(active):
        return (
            active.reshape(active.shape[0], nfsdp, nctx, own_rows)
            .transpose(0, 2, 1, 3)
            .reshape(active.shape[0], D)
        )

    dma = pltpu.SemaphoreType.DMA
    all_low = jax.ShapeDtypeStruct((nctx, tok_rows, D), BF16)
    own_low = jax.ShapeDtypeStruct((tok_rows, D), BF16)
    own_f32 = jax.ShapeDtypeStruct((tok_rows, D), F32)
    row_f32 = jax.ShapeDtypeStruct((1, D), F32)
    g_attn = spread(gains[None, :D])
    g_ffn = spread(gains[None, D : 2 * D])
    order = block_order.reshape(blocks)
    place = jnp.argsort(order).astype(jnp.int32)
    starts = doc_starts[0]

    (attn_held,) = exchange(("swap",), [attn_send], 0, 10)
    w_attn = gather_rows(attn_held)
    first_send, attn_held = lax.optimization_barrier((ff_send[0], attn_held))
    (first_held,) = exchange(("swap",), [first_send], 1, 16)
    table_shape = jax.ShapeDtypeStruct((stream_len, 2 * HD), F32)
    origin = spread(jnp.arange(D, dtype=jnp.int32)[None])
    starts_late, first_held = lax.optimization_barrier((starts, first_held))
    x_low, dy_low, table, normed_all = remote_call(
        first_kernel,
        [own_low, own_low, table_shape, all_low],
        (
            starts_late,
            origin,
            tokens[0],
            cotangent[0],
            g_attn,
            jnp.tile(inverse_freq(), 4)[None],
        ),
        2,
        33,
        [
            pltpu.VMEM((D, D), BF16),
            pltpu.VMEM((tok_rows, D), BF16),
            dma((GATHER_SEMS,)),
            dma((GATHER_SEMS,)),
            dma,
        ],
        (3,),
        1,
    )
    normed_all = normed_all.reshape(stream_len, D)

    g_query = gains[2 * D : 2 * D + HD]
    g_key = gains[2 * D + HD :]
    qk_gain = jnp.concatenate(
        [jnp.tile(g_query, q_width // HD), jnp.tile(g_key, kv_width // HD)]
    )[None]

    low_stream = pltpu.VMEM((stream_len, D), BF16)
    heads_low = pltpu.VMEM((stream_len, q_width), BF16)
    part, qk, q, k, v, mixed, lse, dy_all, second_held = remote_call(
        functools.partial(attend_kernel, blocks, groups),
        [
            jax.ShapeDtypeStruct((stream_len, D), BF16),
            jax.ShapeDtypeStruct((stream_len, qk_width), F32),
            jax.ShapeDtypeStruct((stream_len, q_width), BF16),
            jax.ShapeDtypeStruct((stream_len, kv_width), BF16),
            jax.ShapeDtypeStruct((stream_len, kv_width), BF16),
            jax.ShapeDtypeStruct((stream_len, q_width), BF16),
            jax.ShapeDtypeStruct((blocks, groups, GROUP * HALF), F32),
            all_low,
            jax.ShapeDtypeStruct(ff_send[1].shape, BF16),
        ],
        (place, order, starts, table, qk_gain, normed_all, w_attn, dy_low, ff_send[1]),
        3,
        42,
        [
            low_stream,
            pltpu.VMEM(w_attn.shape, BF16),
            pltpu.VMEM((blocks, HALF, qkv_width), F32),
            pltpu.VMEM((blocks, HALF, q_width), BF16),
            dma((GATHER_SEMS + nctx,)),
            dma((GATHER_SEMS + nctx,)),
            dma((4,)),
        ],
        (7, 8),
        3,
        4,
    )
    dy_all = dy_all.reshape(stream_len, D)
    w_ff = [gather_rows(first_held), gather_rows(second_held)]
    sum_bufs = sum_scratch(nctx, tok_rows)
    sum_sems = [dma((GATHER_SEMS,)), dma((GATHER_SEMS,))]
    norm_scratch = (
        sum_bufs + [pltpu.VMEM((tok_rows, D), BF16)] + sum_sems + sum_sems + [dma]
    )

    middle, normed_two_all = remote_call(
        middle_kernel,
        [own_f32, all_low],
        (part, x_low, g_ffn),
        4,
        57,
        norm_scratch,
        (1,),
    )
    normed_two_all = normed_two_all.reshape(stream_len, D)

    def sum_rows(grad):
        return lax.psum_scatter(grad, "fsdp", scatter_dimension=0, tiled=True).reshape(
            nctx, own_rows, grad.shape[-1]
        )

    def feed(b, x_all, dy):
        width = cuts[b + 1] - cuts[b]
        w_gu, w_down = w_ff[b][:, : 2 * width], w_ff[b][:, 2 * width :]
        gate_up = dot(x_all, w_gu, 1, 0).astype(BF16)
        gate, up = gate_up[:, :width].astype(F32), gate_up[:, width:].astype(F32)
        gated = jax.nn.sigmoid(gate)
        act = gate * gated
        hidden = (act * up).astype(BF16)
        back_hidden = dot(dy, w_down, 1, 0)
        grad_gu = jnp.concatenate(
            [back_hidden * up * (gated + act * (1.0 - gated)), back_hidden * act], axis=1
        ).astype(BF16)
        return hidden, grad_gu, dot(grad_gu, w_gu, 1, 1)

    hidden_one, grad_gu, back_partial = feed(0, normed_two_all, dy_all)
    gu_grad = dot(normed_two_all, grad_gu, 0, 0).astype(BF16)
    gu_grad, back_partial, w_ff[1] = lax.optimization_barrier((gu_grad, back_partial, w_ff[1]))
    width_two = cuts[2] - cuts[1]
    width_line = cuts[1] * 3 // 5 // 128 * 128
    width_rest = cuts[1] - width_line
    hidden_two, grad_gu, back_more = feed(1, normed_two_all, dy_all)
    back_partial = (back_partial + back_more).astype(BF16)
    gu_sum = sum_rows(gu_grad)
    chips = nfsdp // 2

    def line_scratch(columns):
        block = (nctx * own_rows, columns)
        return [pltpu.VMEM((chips,) + block, BF16), pltpu.VMEM((2, 2, chips - 1) + block, BF16)]

    (
        grad_middle,
        grad_g_ffn,
        down_sum,
        grad_middle_all,
        rest_grad,
        last_grad,
        out_partial,
    ) = remote_call(
        middle_back_kernel,
        [
            own_f32,
            row_f32,
            jax.ShapeDtypeStruct((nctx, own_rows, width_line), BF16),
            all_low,
            jax.ShapeDtypeStruct((D, width_rest), BF16),
            jax.ShapeDtypeStruct((D, 3 * width_two), BF16),
            jax.ShapeDtypeStruct((stream_len, D), BF16),
        ],
        (
            back_partial,
            middle,
            dy_low,
            g_ffn,
            normed_two_all,
            dy_all,
            hidden_one,
            hidden_two,
            grad_gu,
            w_ff[0],
            w_ff[1],
        ),
        5,
        57,
        sum_bufs
        + [
            pltpu.VMEM((tok_rows, D), BF16),
            low_stream,
            pltpu.VMEM((stream_len, 2 * width_two), BF16),
            pltpu.VMEM((D, stream_len), BF16),
            pltpu.VMEM((D, 3 * width_two), BF16),
            pltpu.VMEM((D, width_rest), BF16),
            pltpu.VMEM((D, width_line), BF16),
            low_stream,
            pltpu.VMEM((stream_len, cuts[1]), BF16),
            pltpu.VMEM((stream_len, width_two), BF16),
            pltpu.VMEM((D, cuts[1]), BF16),
            pltpu.VMEM((D, width_two), BF16),
        ]
        + line_scratch(width_line)
        + sum_sems
        + sum_sems
        + [dma((3 * chips,)), dma((3 * chips,)), dma((11,))],
        (3, 4, 5, 6),
        0,
        7,
    )
    last_sum = sum_rows(last_grad)

    small = dma((nctx + nfsdp,))
    line_sems = dma((3 * chips + 4 * nctx,))
    own_shape = (nctx, own_rows, qkv_width + q_width)
    sources = (
        grad_middle_all.reshape(blocks, HALF, D),
        w_attn,
        q,
        k,
        v,
        mixed,
        qk.reshape(blocks, HALF, qk_width),
        table.reshape(blocks, HALF, 2 * HD),
        middle,
    )
    out_tokens, grad_joined, qk_gain_grad, out_grad, rest_sum = remote_call(
        functools.partial(attend_back_kernel, blocks, groups),
        [
            own_low,
            jax.ShapeDtypeStruct((stream_len, qkv_width), BF16),
            jax.ShapeDtypeStruct((1, qk_width), F32),
            jax.ShapeDtypeStruct((D, q_width), BF16),
            jax.ShapeDtypeStruct((nctx, own_rows, width_rest), BF16),
        ],
        (place, order, starts, lse, qk_gain, out_partial, rest_grad) + sources,
        6,
        45,
        [pltpu.VMEM(source.shape, source.dtype) for source in sources]
        + sum_bufs
        + [
            heads_low,
            pltpu.VMEM((blocks, HALF, q_width), F32),
            pltpu.VMEM((blocks, HALF, 2 * kv_width), F32),
            pltpu.VMEM((D, stream_len), BF16),
        ]
        + line_scratch(width_rest)
        + sum_sems
        + [dma((3 * chips,)), dma((3 * chips,)), dma((9,))],
        (),
        3,
        9,
    )
    sources = (w_attn, normed_all, x_low, grad_middle)
    grad_tokens, gain_sums, attn_own, gu_own, down_own, rest_own = remote_call(
        functools.partial(tail_kernel, 3),
        [
            own_f32,
            jax.ShapeDtypeStruct((8, D), F32),
            jax.ShapeDtypeStruct(own_shape, BF16),
            jax.ShapeDtypeStruct(gu_sum.shape, BF16),
            jax.ShapeDtypeStruct(down_sum.shape, BF16),
            jax.ShapeDtypeStruct(rest_sum.shape, BF16),
        ],
        (grad_joined, out_grad, qk_gain_grad, g_attn, grad_g_ffn) + sources + (gu_sum, down_sum, rest_sum),
        7,
        75,
        [pltpu.VMEM(source.shape, source.dtype) for source in sources]
        + sum_bufs
        + [
            pltpu.VMEM((D, stream_len), BF16),
            low_stream,
            pltpu.VMEM((D, qkv_width + q_width), BF16),
        ]
        + line_scratch(qkv_width + q_width)
        + [
            pltpu.VMEM(own_shape, BF16),
            pltpu.VMEM((nctx, 8, D), F32),
            pltpu.VMEM((nfsdp, 8, D), F32),
        ]
        + sum_sems
        + [line_sems, line_sems, small, small, dma((7,))],
        (3, 4, 5),
        0,
        7,
    )
    last_sum, gain_sums, gu_own = lax.optimization_barrier((last_sum, gain_sums, gu_own))
    out_tokens = unspread(out_tokens)[None]
    grad_tokens = unspread(grad_tokens)[None]
    gain_grad = jnp.concatenate(
        [
            unspread(gain_sums[:1])[0],
            unspread(gain_sums[1:2])[0],
            jnp.sum(gain_sums[2, :q_width].reshape(-1, HD), axis=0),
            jnp.sum(gain_sums[2, q_width:qk_width].reshape(-1, HD), axis=0),
        ]
    )

    olds = (master_weights, moment_one, moment_two)

    def feed_segments(b, pieces, start, stop):
        found = []
        for part in pieces:
            for c in range(nctx):
                column = c * ff_width + cuts[b] + start
                real = min(max(FF - column, 0), stop - start)
                if real:
                    piece, first = pieces[part]
                    found.append((piece, c, first, bases[part] + column, real))
        return found

    width_one = cuts[1]
    last_own = [
        lax.ppermute(
            lax.dynamic_index_in_dim(last_sum, lax.axis_index("ctx") ^ k, 0, keepdims=False),
            "ctx",
            [(c, c ^ k) for c in range(nctx)],
        )
        if k
        else lax.dynamic_index_in_dim(last_sum, lax.axis_index("ctx"), 0, keepdims=False)
        for k in range(nctx)
    ]
    parts = (
        (0, 0, q_width),
        (q_width, D, kv_width),
        (qk_width, D + KVD, kv_width),
        (qkv_width, QKVC, q_width),
    )
    if kv_width % 128:
        attn_own = jnp.concatenate(
            [attn_own[c, :, f : f + w] for f, _, w in parts for c in range(nctx)], axis=1
        )[None]
        segments = [(0, 0, 0, 0, gate_base)]
    else:
        segments = [
            (0, c, first, base + c * width, width)
            for first, base, width in parts
            for c in range(nctx)
        ]
    news = adam(
        segments
        + feed_segments(0, {0: (1, 0), 1: (1, width_one)}, 0, width_one)
        + feed_segments(0, {2: (2, 0)}, 0, width_line)
        + feed_segments(0, {2: (3, 0)}, width_line, width_one),
        [attn_own, gu_own, down_own, rest_own],
        olds,
        None,
        10,
    )
    first_new, second_new, master_new, low_new = adam(
        feed_segments(
            1, {0: (None, 0), 1: (None, width_two), 2: (None, 2 * width_two)}, 0, width_two
        ),
        last_own,
        olds,
        news,
        6,
    )
    gain_first, gain_second, gain_new = adam_update(
        gains, gain_grad, gains_moment_one, gains_moment_two, GAIN_RATE, 0.0
    )
    return (
        out_tokens,
        grad_tokens,
        first_new,
        second_new,
        master_new,
        low_new,
        gain_first,
        gain_second,
        gain_new,
    )


def solution(mesh):
    rows = P("fsdp", "ctx", None)
    weights = P(("ctx", "fsdp"), None)
    return jax.shard_map(
        shards,
        mesh=mesh,
        in_specs=(rows, rows, P("fsdp", None), P(), weights, weights, weights, P(), P(), P()),
        out_specs=(rows, rows, weights, weights, weights, weights, P(), P(), P()),
        check_vma=False,
    )
```

```python
import functools

import jax
import jax.numpy as jnp
from jax import lax
from jax.experimental import pallas as pl
from jax.experimental.pallas import tpu as pltpu
from jax.sharding import PartitionSpec as P

D = 1536
HEADS = 24
KVHEADS = 8
HD = 64
FF = 6912
STEP = 10
HALF = 128
KVD = 512
QKVC = 2560
GROUP = HEADS // KVHEADS

ROPE_BASE = 1000000.0
NORM_EPS = 1e-05
BETA_ONE = 0.9
BETA_TWO = 0.95
ADAM_EPS = 1e-08
WEIGHT_DECAY = 0.1
LEARN_RATE = 0.03
GAIN_RATE = 0.5
SCALE = HD ** (-0.5)
MESH = pl.DeviceIdType.MESH
F32 = jnp.float32
BF16 = jnp.bfloat16
VMEM_LIMIT = 60 * 1024 * 1024


def dot(left, right, left_dim, right_dim):
    return lax.dot_general(
        left, right, (((left_dim,), (right_dim,)), ((), ())), preferred_element_type=F32
    )


def send(source, target, sems, item, peer):
    copy = pltpu.make_async_remote_copy(
        src_ref=source,
        dst_ref=target,
        send_sem=sems[0].at[item],
        recv_sem=sems[1].at[item],
        device_id=peer,
        device_id_type=MESH,
    )
    copy.start()
    return copy


def meet(axes):
    barrier = pltpu.get_barrier_semaphore()
    total = 0
    for axis in axes:
        size = lax.axis_size(axis)
        me = lax.axis_index(axis)
        for step in range(1, size):
            pl.semaphore_signal(
                barrier,
                inc=1,
                device_id={axis: lax.rem(me + step, size)},
                device_id_type=MESH,
            )
        total += size - 1
    pl.semaphore_wait(barrier, total)


def square():
    me = lax.axis_index("ctx")
    return me, me + 1 - 2 * lax.rem(me, 2), lax.rem(me + 2, 4), 3 - me


def swap_start(source, target, sems, base):
    size = lax.axis_size("ctx")
    me = lax.axis_index("ctx")
    copies = []
    for step in range(1, size):
        peer = lax.rem(me + step, size)
        copies.append(
            send(source.at[peer], target.at[me], sems, base + step, {"ctx": peer})
        )
    return copies


def gather_start(source, target, sems, base):
    size = lax.axis_size("ctx")
    me = lax.axis_index("ctx")
    if size != 4:
        return [
            send(
                source,
                target.at[me],
                sems,
                base + step,
                {"ctx": lax.rem(me + step, size)},
            )
            for step in range(1, size)
        ]
    me, side, over, across = square()
    half = source.shape[0] // 2
    top, low = pl.ds(0, half), pl.ds(half, half)
    return [
        send(source.at[top], target.at[me, top], sems, base, {"ctx": side}),
        send(source.at[low], target.at[me, low], sems, base + 1, {"ctx": over}),
        send(source.at[low], target.at[me, low], sems, base + 2, {"ctx": side}),
        send(source.at[top], target.at[me, top], sems, base + 3, {"ctx": over}),
    ]


def gather_pass(copies, target, sems, base):
    if lax.axis_size("ctx") != 4:
        return
    me, side, over, across = square()
    half = target.shape[1] // 2
    top, low = pl.ds(0, half), pl.ds(half, half)
    copies[0].wait_recv()
    copies.append(send(target.at[side, top], target.at[side, top], sems, base + 4, {"ctx": over}))
    copies[1].wait_recv()
    copies.append(send(target.at[over, low], target.at[over, low], sems, base + 5, {"ctx": side}))


def gather_end(copies):
    if lax.axis_size("ctx") != 4:
        for copy in copies:
            copy.wait()
        return
    for copy in copies:
        copy.wait_send()
    for copy in copies[2:]:
        copy.wait_recv()


def gather_rest(copies, target, sems, base):
    gather_pass(copies, target, sems, base)
    gather_end(copies)


def load(source, target, sem):
    copy = pltpu.make_async_copy(source, target, sem)
    copy.start()
    return copy


GATHER_SEMS = 8


def exchange_kernel(kinds, *refs):
    count = len(kinds)
    ins, outs = refs[:count], refs[count : 2 * count]
    send_sem, recv_sem, local_sem = refs[2 * count :]
    sems = (send_sem, recv_sem)
    me = lax.axis_index("ctx")
    meet(("ctx",))
    copies = []
    own = []
    for item in range(count):
        base = item * GATHER_SEMS
        if kinds[item] == "gather":
            copies.append(gather_start(ins[item], outs[item], sems, base))
            source = ins[item]
        else:
            copies.append(swap_start(ins[item], outs[item], sems, base))
            source = ins[item].at[me]
        copy = pltpu.make_async_copy(source, outs[item].at[me], local_sem.at[item])
        copy.start()
        own.append(copy)
    for item in range(count):
        if kinds[item] == "gather":
            gather_rest(copies[item], outs[item], sems, item * GATHER_SEMS)
        else:
            for copy in copies[item]:
                copy.wait()
    for copy in own:
        copy.wait()


def remote_params(collective_id):
    return pltpu.CompilerParams(
        collective_id=collective_id, has_side_effects=True, vmem_limit_bytes=VMEM_LIMIT
    )


def cost(micros):
    return pl.CostEstimate(flops=0, bytes_accessed=int(micros * 3.0e6), transcendentals=0)


def exchange(kinds, arrays, collective_id, micros):
    size = lax.axis_size("ctx")
    shapes = [
        jax.ShapeDtypeStruct((size,) + a.shape if kind == "gather" else a.shape, a.dtype)
        for kind, a in zip(kinds, arrays)
    ]
    sems = pltpu.SemaphoreType.DMA((len(arrays) * GATHER_SEMS,))
    return pl.pallas_call(
        functools.partial(exchange_kernel, kinds),
        out_shape=shapes,
        in_specs=[pl.BlockSpec(memory_space=pl.ANY)] * len(arrays),
        out_specs=[pl.BlockSpec(memory_space=pl.ANY)] * len(arrays),
        scratch_shapes=[sems, sems, pltpu.SemaphoreType.DMA((len(arrays),))],
        compiler_params=remote_params(collective_id),
        cost_estimate=cost(micros),
    )(*arrays)


def sum_scratch(size, rows):
    if size == 4:
        half = pltpu.VMEM((2, rows // 2, D), BF16)
        return [half, half, pltpu.VMEM((2, rows, D), BF16)]
    return [pltpu.VMEM((size - 1, rows, D), BF16)]


def sum_start(part, bufs, sems):
    size = lax.axis_size("ctx")
    me = lax.axis_index("ctx")
    rows = part.shape[0] // size

    def block(owner, first=0, count=rows):
        return pl.ds(pl.multiple_of(owner * rows + first, rows // 2), count)

    if size != 4:
        copies = []
        for step in range(1, size):
            peer = lax.rem(me + step, size)
            copies.append(
                send(part.at[block(peer)], bufs[0].at[step - 1], sems, step, {"ctx": peer})
            )
        return copies
    me, side, over, across = square()
    half = rows // 2
    relay, _, landed = bufs
    return [
        send(part.at[block(across, 0, half)], relay.at[0], sems, 0, {"ctx": side}),
        send(part.at[block(across, half, half)], relay.at[1], sems, 1, {"ctx": over}),
        send(
            part.at[block(side, 0, half)],
            landed.at[0, pl.ds(0, half)],
            sems,
            2,
            {"ctx": side},
        ),
        send(
            part.at[block(over, half, half)],
            landed.at[1, pl.ds(half, half)],
            sems,
            3,
            {"ctx": over},
        ),
    ]


def sum_pass(copies, part, bufs, sems):
    if lax.axis_size("ctx") != 4:
        return
    rows = part.shape[0] // 4
    half = rows // 2

    def rows_of(owner, first):
        return pl.ds(pl.multiple_of(owner * rows + first, half), half)

    me, side, over, across = square()
    relay, passed, landed = bufs
    copies[0].wait_recv()
    passed[0] = (part[rows_of(over, 0), :].astype(F32) + relay[0].astype(F32)).astype(BF16)
    copies.append(
        send(passed.at[0], landed.at[1, pl.ds(0, half)], sems, 4, {"ctx": over})
    )
    copies[1].wait_recv()
    passed[1] = (part[rows_of(side, half), :].astype(F32) + relay[1].astype(F32)).astype(
        BF16
    )
    copies.append(
        send(passed.at[1], landed.at[0, pl.ds(half, half)], sems, 5, {"ctx": side})
    )


def sum_rest(copies, part, bufs):
    size = lax.axis_size("ctx")
    me = lax.axis_index("ctx")
    rows = part.shape[0] // size
    half = rows // 2

    def rows_of(owner, first):
        return pl.ds(pl.multiple_of(owner * rows + first, half), half)

    if size != 4:
        for copy in copies:
            copy.wait()

        def read(first):
            total = part[rows_of(me, first), :].astype(F32)
            for step in range(1, size):
                total = total + bufs[0][step - 1, pl.ds(first, half), :].astype(F32)
            return total

        return read
    relay, passed, landed = bufs
    for copy in copies:
        copy.wait_send()
    for copy in copies[2:]:
        copy.wait_recv()

    def read(first):
        return (
            part[rows_of(me, first), :].astype(F32)
            + landed[0, pl.ds(first, half), :].astype(F32)
            + landed[1, pl.ds(first, half), :].astype(F32)
        )

    return read


def row_scale(values):
    return lax.rsqrt(jnp.mean(values * values, axis=-1, keepdims=True) + NORM_EPS)


def shard_copies(reach, held, rows, sems, base):
    me = lax.axis_index("fsdp")
    chips = lax.axis_size("fsdp") // 2
    chip = me // 2

    def along(steps):
        return lax.rem(me + 2 * steps + 2 * chips * chips, 2 * chips)

    found = []
    for side, way in ((0, 1), (1, -1)):
        number = base + 4 * (reach - 1) + 2 * side
        start = chip - way * (reach - 1)
        origin = chip - way * reach
        to_next = pltpu.make_async_remote_copy(
            src_ref=held if reach == 1 else rows.at[along(-way * (reach - 1))],
            dst_ref=rows.at[along(-way * (reach - 1))],
            send_sem=sems[0].at[number],
            recv_sem=sems[1].at[number],
            device_id={"fsdp": along(way)},
            device_id_type=MESH,
        )
        to_mate = pltpu.make_async_remote_copy(
            src_ref=rows.at[along(-way * reach)],
            dst_ref=rows.at[along(-way * reach)],
            send_sem=sems[0].at[number + 1],
            recv_sem=sems[1].at[number + 1],
            device_id={"fsdp": me + 1 - 2 * lax.rem(me, 2)},
            device_id_type=MESH,
        )
        if way == 1:
            sent = (start >= 0) & (chip <= chips - 2)
            got = origin >= 0
        else:
            sent = (start <= chips - 1) & (chip >= 1)
            got = origin <= chips - 1
        found.append((to_next, sent, got, to_mate))
    return found


def first_kernel(
    starts,
    origin,
    x,
    dy,
    gain,
    freq,
    attn_send,
    ff_send,
    x_low,
    dy_low,
    normed,
    table,
    attn_held,
    attn_rows,
    ff_held,
    *scratch,
):
    move, send_one, recv_one, send_two, recv_two, local = scratch
    me = lax.axis_index("ctx")
    row_me = lax.axis_index("fsdp")
    size = lax.axis_size("ctx")
    chips = lax.axis_size("fsdp") // 2
    swaps, line = (send_one, recv_one), (send_two, recv_two)
    meet(("ctx", "fsdp"))
    attn_copies = swap_start(attn_send, attn_held, swaps, 0)
    own = load(attn_send.at[me], attn_held.at[me], local.at[0])
    ff_copies = swap_start(ff_send, ff_held, swaps, size)
    own_ff = load(ff_send.at[me], ff_held.at[me], local.at[1])
    row = lax.broadcasted_iota(jnp.int32, move.shape, 0)
    move[...] = jnp.where(row == origin[...], 1.0, 0.0).astype(BF16)
    own.wait()
    for copy in attn_copies:
        copy.wait()
    mate = send(
        attn_held,
        attn_rows.at[row_me],
        line,
        4 * (chips - 1),
        {"fsdp": row_me + 1 - 2 * lax.rem(row_me, 2)},
    )
    own_rows = load(attn_held, attn_rows.at[row_me], local.at[2])
    for to_next, sent, _, _ in shard_copies(1, attn_held, attn_rows, line, 0):
        pl.when(sent)(to_next.start)
    values = dot(x[...], move[...], 1, 0)
    x_low[...] = values.astype(BF16)
    normed[...] = (values * row_scale(values) * gain[...]).astype(BF16)
    dy_low[...] = dot(dy[...], move[...], 1, 0).astype(BF16)
    for reach in range(1, chips):
        for to_next, _, got, to_mate in shard_copies(reach, attn_held, attn_rows, line, 0):

            @pl.when(got)
            def _(to_next=to_next, to_mate=to_mate):
                to_next.wait_recv()
                to_mate.start()

        if reach + 1 < chips:
            for to_next, sent, _, _ in shard_copies(reach + 1, attn_held, attn_rows, line, 0):
                pl.when(sent)(to_next.start)
        if reach == 1:
            times = lax.broadcasted_iota(jnp.int32, (table.shape[0], 1), 0)
            angles = (times - doc_first(starts, times)).astype(F32) * freq[...]
            lane = lax.broadcasted_iota(jnp.int32, angles.shape, 1)
            sine = jnp.sin(angles)
            sine = jnp.where(lane % HD < HD // 2, -sine, sine)
            table[...] = jnp.where(lane < HD, jnp.cos(angles), sine)
    mate.wait()
    own_rows.wait()
    for reach in range(1, chips):
        for to_next, sent, got, to_mate in shard_copies(reach, attn_held, attn_rows, line, 0):
            pl.when(sent)(to_next.wait_send)
            pl.when(got)(to_mate.wait)
    for copy in ff_copies:
        copy.wait()
    own_ff.wait()


def middle_kernel(part, x, gain, middle, normed_all, *scratch):
    bufs, (normed, send_one, recv_one, send_two, recv_two, local) = scratch[:-6], scratch[-6:]
    me = lax.axis_index("ctx")
    meet(("ctx",))
    copies = sum_start(part, bufs, (send_one, recv_one))
    sum_pass(copies, part, bufs, (send_one, recv_one))
    read = sum_rest(copies, part, bufs)
    half = x.shape[0] // 2
    for first in (0, half):
        rows = pl.ds(first, half)
        values = x[rows, :].astype(F32) + read(first)
        middle[rows, :] = values
        normed[rows, :] = (values * row_scale(values) * gain[...]).astype(BF16)
    sems = (send_two, recv_two)
    copies = gather_start(normed, normed_all, sems, 0)
    own = load(normed, normed_all.at[me], local)
    gather_rest(copies, normed_all, sems, 0)
    own.wait()


def column_tiles(total, body):
    def step(tile, carry):
        body(pl.multiple_of(tile * 256, 256), 256)
        return carry

    lax.fori_loop(0, total // 256, step, 0)
    if total % 256:
        body(total - total % 256, total % 256)


def turn(source, target):
    for first in range(0, source.shape[0], HALF):
        rows = slice(first, first + HALF)
        target[:, rows] = source[rows, :].T


def middle_back_kernel(
    part,
    middle,
    dy,
    gain,
    x_all,
    dy_all,
    hidden_one,
    hidden_two,
    grad_gu,
    w_one,
    w_two,
    grad,
    gain_grad,
    down_sum,
    grad_all,
    rest_grad,
    weight_grad,
    out,
    *scratch,
):
    bufs = scratch[:-21]
    low, x_buf, gu_buf, turned, weight_buf, rest_buf, down_grad, out_buf = scratch[-21:-13]
    hidden_bufs, down_bufs = scratch[-13:-11], scratch[-11:-9]
    home, travel, send_one, recv_one, send_two, recv_two, send_three, recv_three, local = (
        scratch[-9:]
    )
    going, coming = travel.at[0], travel.at[1]
    me = lax.axis_index("ctx")
    chips = lax.axis_size("fsdp") // 2
    line = (send_three, recv_three)
    meet(("ctx", "fsdp"))
    copies = sum_start(part, bufs, (send_one, recv_one))
    width_one, width_two = hidden_one.shape[1], hidden_two.shape[1]
    gu_width = grad_gu.shape[1]
    loads = [
        load(source, target, local.at[item])
        for item, (source, target) in enumerate(
            (
                (dy_all, x_buf),
                (hidden_one, hidden_bufs[0]),
                (hidden_two, hidden_bufs[1]),
                (grad_gu, gu_buf),
                (w_one.at[:, pl.ds(2 * width_one, width_one)], down_bufs[0]),
                (w_two.at[:, pl.ds(2 * width_two, width_two)], down_bufs[1]),
            )
        )
    ]
    loads[0].wait()
    turn(x_buf, turned)
    loads.append(load(x_all, x_buf, local.at[6]))
    loads[1].wait()

    def product(target, column, right, begin=0, count=None):
        def tile(first, width):
            target[:, pl.ds(column + first, width)] = dot(
                turned[...], right[:, pl.ds(begin + first, width)], 1, 0
            ).astype(BF16)

        column_tiles(right.shape[1] if count is None else count, tile)

    width_line = down_grad.shape[1]
    product(down_grad, 0, hidden_bufs[0], 0, width_line)
    home_copies = line_start(down_grad, home, line, 0)
    product(rest_buf, 0, hidden_bufs[0], width_line, width_one - width_line)
    stores = [load(rest_buf, rest_grad, local.at[10])]
    sum_pass(copies, part, bufs, (send_one, recv_one))
    line_home(home_copies, down_grad, home)
    line_step(chips - 1, home, going, coming, line, chips)
    loads[2].wait()
    product(weight_buf, gu_width, hidden_bufs[1])
    loads[6].wait()
    turn(x_buf, turned)
    loads[3].wait()
    product(weight_buf, 0, gu_buf)
    stores.append(load(weight_buf, weight_grad, local.at[7]))
    if chips > 2:
        line_step(chips - 2, home, going, coming, line, chips)
    read = sum_rest(copies, part, bufs)
    half = dy.shape[0] // 2
    total = jnp.zeros((1, D), F32)
    for first in (0, half):
        rows = pl.ds(first, half)
        values = middle[rows, :]
        root = row_scale(values)
        unit = values * root
        back = read(first)
        total = total + jnp.sum(back * unit, axis=0, keepdims=True)
        back = back * gain[...]
        back = root * (back - unit * jnp.mean(back * unit, axis=-1, keepdims=True))
        back = back + dy[rows, :].astype(F32)
        grad[rows, :] = back
        low[rows, :] = back.astype(BF16)
    gain_grad[...] = total
    sems = (send_two, recv_two)
    copies = gather_start(low, grad_all, sems, 0)
    stores.append(load(low, grad_all.at[me], local.at[8]))
    loads[4].wait()
    loads[5].wait()

    def out_tile(first, width):
        columns = pl.ds(first, width)
        out_buf[:, columns] = (
            dot(hidden_bufs[0][...], down_bufs[0][columns, :], 1, 1)
            + dot(hidden_bufs[1][...], down_bufs[1][columns, :], 1, 1)
        ).astype(BF16)

    column_tiles(D, out_tile)
    stores.append(load(out_buf, out, local.at[9]))
    gather_pass(copies, grad_all, sems, 0)
    for reach in range(min(chips - 1, max(chips - 3, 1)), 0, -1):
        line_step(reach, home, going, coming, line, chips)
    line_end(home_copies, home, going, coming, line, chips)
    chip = lax.axis_index("fsdp") // 2
    rows = down_sum.shape[1]
    for index in range(down_sum.shape[0]):
        down_sum[index] = home[chip, index * rows : (index + 1) * rows, :]
    gather_end(copies)
    for copy in stores:
        copy.wait()


def line_start(grad, home, sems, base):
    me = lax.axis_index("fsdp")
    chips = lax.axis_size("fsdp") // 2
    core = lax.rem(me, 2)
    rows = grad.shape[0] // (2 * chips)
    copies = []
    for chip in range(chips):
        theirs = pl.ds(pl.multiple_of((2 * chip + 1 - core) * rows, rows), rows)
        copies.append(
            send(grad.at[theirs], home.at[chip], sems, base + chip, {"fsdp": me + 1 - 2 * core})
        )
    return copies


def line_home(copies, grad, home):
    me = lax.axis_index("fsdp")
    chips = lax.axis_size("fsdp") // 2
    core = lax.rem(me, 2)
    rows = grad.shape[0] // (2 * chips)
    for chip in range(chips):
        copies[chip].wait_recv()
        mine = pl.ds(pl.multiple_of((2 * chip + core) * rows, rows), rows)
        home[chip] = (home[chip].astype(F32) + grad[mine, :].astype(F32)).astype(BF16)


def line_copies(reach, going, coming, sems, base):
    me = lax.axis_index("fsdp")
    chips = lax.axis_size("fsdp") // 2
    chip = me // 2
    found = []
    for side, way in ((0, 1), (1, -1)):
        copy = pltpu.make_async_remote_copy(
            src_ref=going.at[side, reach - 1],
            dst_ref=coming.at[side, reach - 1],
            send_sem=sems[0].at[base + 2 * reach + side],
            recv_sem=sems[1].at[base + 2 * reach + side],
            device_id={"fsdp": lax.rem(me + 2 * way + 2 * chips, 2 * chips)},
            device_id_type=MESH,
        )
        if way == 1:
            sent = chip + reach <= chips - 1
            got = (chip >= 1) & (chip + reach <= chips)
            more = (chip >= 1) & sent
        else:
            sent = chip >= reach
            got = (chip <= chips - 2) & (chip + 1 >= reach)
            more = (chip <= chips - 2) & sent
        found.append((side, way, copy, sent, got, more))
    return found


def line_step(reach, home, going, coming, sems, base):
    me = lax.axis_index("fsdp")
    chips = lax.axis_size("fsdp") // 2
    chip = me // 2
    if reach < chips - 1:
        for _, _, copy, _, got, _ in line_copies(reach + 1, going, coming, sems, base):
            pl.when(got)(copy.wait_recv)
    for side, way, copy, sent, _, more in line_copies(reach, going, coming, sems, base):

        @pl.when(sent)
        def _(side=side, way=way, copy=copy, more=more):
            value = home[chip + way * reach]
            if reach < chips - 1:

                @pl.when(more)
                def _():
                    going[side, reach - 1] = (
                        value.astype(F32) + coming[side, reach].astype(F32)
                    ).astype(BF16)

                @pl.when(jnp.logical_not(more))
                def _():
                    going[side, reach - 1] = value

            else:
                going[side, reach - 1] = value
            copy.start()


def line_end(copies, home, going, coming, sems, base):
    me = lax.axis_index("fsdp")
    chips = lax.axis_size("fsdp") // 2
    chip = me // 2
    for side, _, copy, _, got, _ in line_copies(1, going, coming, sems, base):

        @pl.when(got)
        def _(side=side, copy=copy):
            copy.wait_recv()
            home[chip] = (home[chip].astype(F32) + coming[side, 0].astype(F32)).astype(BF16)

    for copy in copies:
        copy.wait_send()
    for reach in range(1, chips):
        for _, _, copy, sent, _, _ in line_copies(reach, going, coming, sems, base):
            pl.when(sent)(copy.wait_send)


def remote_call(
    kernel, out_shape, args, collective_id, micros, scratch, in_hbm=(), smem=0, args_in_hbm=0
):
    return pl.pallas_call(
        kernel,
        out_shape=out_shape,
        in_specs=[pl.BlockSpec(memory_space=pltpu.SMEM)] * smem
        + [pl.BlockSpec(memory_space=pltpu.VMEM)] * (len(args) - smem - args_in_hbm)
        + [pl.BlockSpec(memory_space=pl.ANY)] * args_in_hbm,
        out_specs=[
            pl.BlockSpec(memory_space=pl.ANY if item in in_hbm else pltpu.VMEM)
            for item in range(len(out_shape))
        ],
        scratch_shapes=scratch,
        compiler_params=remote_params(collective_id),
        cost_estimate=cost(micros),
    )(*args)


def adam_update(param_now, grad_now, moment_old_one, moment_old_two, step_rate, decay_rate):
    first_new = BETA_ONE * moment_old_one + (1.0 - BETA_ONE) * grad_now
    second_new = BETA_TWO * moment_old_two + (1.0 - BETA_TWO) * grad_now * grad_now
    ratio = (first_new * (1.0 / (1.0 - BETA_ONE**STEP))) / (
        jnp.sqrt(second_new * (1.0 / (1.0 - BETA_TWO**STEP))) + ADAM_EPS
    )
    return (first_new, second_new, param_now - step_rate * (ratio + decay_rate * param_now))


def joined_ranges(segments):
    ranges = []
    for number in sorted(range(len(segments)), key=lambda n: segments[n][3]):
        column, width = segments[number][3:]
        if ranges and ranges[-1][0] + ranges[-1][1] == column:
            first, so_far, numbers = ranges[-1]
            ranges[-1] = (first, so_far + width, numbers + (number,))
        else:
            ranges.append((column, width, (number,)))
    return ranges


def adam_kernel(segments, pieces, held, *refs):
    me = lax.axis_index("ctx")
    grads = refs[:pieces]
    olds = refs[pieces : pieces + 3]
    news = refs[pieces + 3 + held : pieces + 3 + held + 4]
    grad_buf, old_buf, low_buf, grad_sem, in_sem, out_sem = refs[pieces + 3 + held + 4 :]
    base = min(segment[3] for segment in segments)
    ranges = joined_ranges(segments)
    loads = []
    for place, (column, width, numbers) in enumerate(ranges):
        here, there = pl.ds(column - base, width), pl.ds(column, width)
        copies = [
            load(olds[item].at[:, there], old_buf.at[item, :, here], in_sem.at[item, place])
            for item in range(3)
        ]
        for number in numbers:
            piece, index, first, start, count = segments[number]
            columns = pl.ds(first, count)
            for source_number, source in enumerate(grads):
                if piece not in (None, source_number):
                    continue
                copy = pltpu.make_async_copy(
                    source.at[:, columns] if piece is None else source.at[index, :, columns],
                    grad_buf.at[:, pl.ds(start - base, count)],
                    grad_sem.at[number],
                )
                if piece is None:
                    pl.when(me == index ^ source_number)(copy.start)
                else:
                    copy.start()
            copies.append(copy)
        loads.append(copies)
    stores = []
    for place, (column, width, numbers) in enumerate(ranges):
        for copy in loads[place]:
            copy.wait()
        here, there = pl.ds(column - base, width), pl.ds(column, width)
        for first in range(0, width, 256):
            part = pl.ds(column - base + first, min(256, width - first))
            first_new, second_new, master = adam_update(
                old_buf[0, :, part],
                grad_buf[:, part].astype(F32),
                old_buf[1, :, part],
                old_buf[2, :, part],
                LEARN_RATE,
                WEIGHT_DECAY,
            )
            old_buf[0, :, part] = master
            old_buf[1, :, part] = first_new
            old_buf[2, :, part] = second_new
            low_buf[:, part] = master.astype(BF16)
        for item, source in enumerate(
            (
                old_buf.at[1, :, here],
                old_buf.at[2, :, here],
                old_buf.at[0, :, here],
                low_buf.at[:, here],
            )
        ):
            stores.append(load(source, news[item].at[:, there], out_sem.at[item, place]))
    for copy in stores:
        copy.wait()


def adam(segments, grads, olds, held, micros):
    rows, columns = olds[0].shape
    span = max(s[3] + s[4] for s in segments) - min(s[3] for s in segments)
    held = [] if held is None else list(held)
    args = list(grads) + list(olds) + held
    return pl.pallas_call(
        functools.partial(adam_kernel, tuple(segments), len(grads), len(held)),
        out_shape=[jax.ShapeDtypeStruct((rows, columns), F32)] * 3
        + [jax.ShapeDtypeStruct((rows, columns), BF16)],
        in_specs=[pl.BlockSpec(memory_space=pl.ANY)] * len(args),
        out_specs=[pl.BlockSpec(memory_space=pl.ANY)] * 4,
        input_output_aliases={len(grads) + 3 + item: item for item in range(len(held))},
        scratch_shapes=[
            pltpu.VMEM((rows, span), BF16),
            pltpu.VMEM((3, rows, span), F32),
            pltpu.VMEM((rows, span), BF16),
            pltpu.SemaphoreType.DMA((len(segments),)),
            pltpu.SemaphoreType.DMA((3, len(segments))),
            pltpu.SemaphoreType.DMA((4, len(segments))),
        ],
        compiler_params=pltpu.CompilerParams(vmem_limit_bytes=VMEM_LIMIT),
        cost_estimate=cost(micros),
    )(*args)


def head_mean(values, ones):
    high = values.astype(BF16)
    rest = (values - high.astype(F32)).astype(BF16)
    return (dot(high, ones, 1, 0) + dot(rest, ones, 1, 0)) * (1.0 / HD)


def head_ones(width):
    row = lax.broadcasted_iota(jnp.int32, (width, width), 0) // HD
    col = lax.broadcasted_iota(jnp.int32, (width, width), 1) // HD
    return jnp.where(row == col, 1.0, 0.0).astype(BF16)


def partner(values):
    width = values.shape[-1]
    lane = lax.broadcasted_iota(jnp.int32, values.shape, 1)
    return jnp.where(
        lane % HD < HD // 2,
        pltpu.roll(values, width - HD // 2, 1),
        pltpu.roll(values, HD // 2, 1),
    )


def widen(table, width):
    return [
        jnp.concatenate([part] * (width // HD), axis=-1)
        for part in (table[:, :HD], table[:, HD:])
    ]


def doc_first(starts, times):
    first = jnp.zeros_like(times)
    for item in range(starts.shape[0]):
        first = jnp.where(starts[item] <= times, starts[item], first)
    return first


def block_mask(starts, block, keys):
    shape = (keys, GROUP * HALF)
    times = block * HALF + lax.broadcasted_iota(jnp.int32, (1, GROUP * HALF), 1) % HALF
    key = lax.broadcasted_iota(jnp.int32, shape, 0)
    return (key >= doc_first(starts, times)) & (key <= times)


def stack_heads(ref, rows, group):
    return jnp.concatenate(
        [
            ref[rows, (group * GROUP + h) * HD : (group * GROUP + h + 1) * HD]
            for h in range(GROUP)
        ],
        axis=0,
    )


def unstack_heads(turned):
    wide = turned.T
    return [wide[h * HALF : (h + 1) * HALF, :] for h in range(GROUP)]


def attend_kernel(
    blocks,
    groups,
    place,
    order,
    starts,
    table,
    gain,
    normed_in,
    weights_from,
    dy,
    swap_in,
    part,
    qk,
    q,
    k,
    v,
    o_held,
    lse,
    dy_all,
    swap_out,
    normed,
    weights_in,
    joined,
    o,
    send_sem,
    recv_sem,
    local,
):
    sems = (send_sem, recv_sem)
    me = lax.axis_index("ctx")
    qk_width = qk.shape[1]
    q_width = q.shape[1]
    qkv_width = qk_width + v.shape[1]
    ones = head_ones(qk_width)
    meet(("ctx",))
    loads = [
        load(normed_in, normed, local.at[0]),
        load(weights_from, weights_in, local.at[1]),
    ]
    swap_copies = swap_start(swap_in, swap_out, sems, GATHER_SEMS)
    copies = gather_start(dy, dy_all, sems, 0)
    own_copies = [
        load(swap_in.at[me], swap_out.at[me], local.at[2]),
        load(dy, dy_all.at[me], local.at[3]),
    ]
    for copy in loads:
        copy.wait()
    for block in range(blocks):
        joined[block] = dot(
            normed[block * HALF : (block + 1) * HALF, :], weights_in[:, :qkv_width], 1, 0
        )
    for block in range(blocks):
        to = slice(block * HALF, (block + 1) * HALF)
        values = joined[place[block]]
        v[to, :] = values[:, qk_width:].astype(BF16)
        values = values[:, :qk_width]
        qk[to, :] = values
        turned = values * lax.rsqrt(head_mean(values * values, ones) + NORM_EPS) * gain[...]
        cosine, sine = widen(table[to, :], qk_width)
        turned = turned * cosine + partner(turned) * sine
        turned = turned.astype(BF16)
        q[to, :] = turned[:, :q_width]
        k[to, :] = turned[:, q_width:]
    for block in range(blocks):
        rows = slice(block * HALF, (block + 1) * HALF)
        keys = (block + 1) * HALF
        mask = block_mask(starts, block, keys)
        pieces = []
        for group in range(groups):
            lanes = slice(group * HD, (group + 1) * HD)
            queries = stack_heads(q, rows, group)
            scores = dot(k[:keys, lanes], queries, 1, 1) * SCALE
            weights = jnp.where(mask, jnp.exp(scores), 0.0)
            sums = jnp.sum(weights, axis=0, keepdims=True)
            lse[block, group : group + 1, :] = jnp.log(sums)
            mixed = dot(v[:keys, lanes], weights.astype(BF16), 0, 0) / sums
            pieces += unstack_heads(mixed)
        o[block] = jnp.concatenate(pieces, axis=1).astype(BF16)
    for block in range(blocks):
        o_held[block * HALF : (block + 1) * HALF, :] = o[order[block]]
    for first in range(0, D, 512):
        part[:, first : first + 512] = dot(
            o_held[...], weights_in[first : first + 512, qkv_width:], 1, 1
        ).astype(BF16)
    gather_rest(copies, dy_all, sems, 0)
    for copy in swap_copies:
        copy.wait()
    for copy in own_copies:
        copy.wait()


def attend_back_kernel(
    blocks,
    groups,
    place,
    order,
    starts,
    lse,
    gain,
    part,
    rest_grad,
    *refs,
):
    sources, refs = refs[:9], refs[9:]
    out, joined, gain_grad, out_grad, rest_sum = refs[:5]
    targets, refs = refs[5:14], refs[14:]
    grad_all, weights_in, q, k, v, o, qk, table, middle = targets
    bufs, (do, dq, dkv, turned, home, travel) = refs[:-11], refs[-11:-5]
    send_one, recv_one, send_two, recv_two, local = refs[-5:]
    going, coming = travel.at[0], travel.at[1]
    line = (send_two, recv_two)
    chips = lax.axis_size("fsdp") // 2
    out_sems = (send_one, recv_one)
    qk_width = qk.shape[2]
    qkv_width = qk_width + v.shape[1]
    ones = head_ones(qk_width)
    meet(("ctx", "fsdp"))
    home_copies = line_start(rest_grad, home, line, 0)
    out_copies = sum_start(part, bufs, out_sems)
    loads = [
        load(source, target, local.at[item])
        for item, (source, target) in enumerate(zip(sources, targets))
    ]
    for copy in loads[:6]:
        copy.wait()
    for block in range(blocks):
        do[block * HALF : (block + 1) * HALF, :] = dot(
            grad_all[place[block]], weights_in[:, qkv_width:], 1, 0
        ).astype(BF16)
    for block in range(blocks):
        turned[:, block * HALF : (block + 1) * HALF] = grad_all[block].T
    for first in range(0, D, 512):
        rows = slice(first, first + 512)
        out_grad[rows, :] = dot(turned[rows, :], o[...], 1, 0).astype(BF16)
    dkv[...] = jnp.zeros_like(dkv)
    line_home(home_copies, rest_grad, home)
    line_step(chips - 1, home, going, coming, line, chips)
    reach = chips - 2
    for block in range(blocks):
        if block == blocks // 2:
            sum_pass(out_copies, part, bufs, out_sems)
        if block >= blocks * 3 // 4 and reach > 1:
            line_step(reach, home, going, coming, line, chips)
            reach -= 1
        rows = slice(block * HALF, (block + 1) * HALF)
        keys = (block + 1) * HALF
        mask = block_mask(starts, block, keys)
        pieces = []
        dk_add = []
        dv_add = []
        for group in range(groups):
            lanes = slice(group * HD, (group + 1) * HD)
            queries = stack_heads(q, rows, group)
            outs = stack_heads(do, rows, group)
            key_rows = k[:keys, lanes]
            scores = dot(key_rows, queries, 1, 1) * SCALE
            weights = jnp.where(
                mask, jnp.exp(scores - lse[block, group : group + 1, :]), 0.0
            )
            back = dot(v[:keys, lanes], outs, 1, 1)
            delta = jnp.sum(weights * back, axis=0, keepdims=True)
            grads = (weights * (back - delta)).astype(BF16)
            pieces += unstack_heads(dot(key_rows, grads, 0, 0) * SCALE)
            dk_add.append(dot(grads, queries, 1, 0) * SCALE)
            dv_add.append(dot(weights.astype(BF16), outs, 1, 0))
        dq[block] = jnp.concatenate(pieces, axis=1)
        dkv[: block + 1] += jnp.concatenate(dk_add + dv_add, axis=1).reshape(
            (block + 1,) + dkv.shape[1:]
        )
    for step in range(reach, 0, -1):
        line_step(step, home, going, coming, line, chips)
    gain_row = jnp.zeros((1, qk_width), F32)
    for copy in loads[6:]:
        copy.wait()
    for block in range(blocks):
        here = order[block]
        values = qk[here]
        root = lax.rsqrt(head_mean(values * values, ones) + NORM_EPS)
        unit = values * root
        grad_kv = dkv[here]
        kv_width = grad_kv.shape[1] // 2
        grad = jnp.concatenate([dq[here], grad_kv[:, :kv_width]], axis=1)
        cosine, sine = widen(table[here], qk_width)
        grad = grad * cosine - partner(grad) * sine
        gain_row = gain_row + jnp.sum(grad * unit, axis=0, keepdims=True)
        grad = grad * gain[...]
        grad = root * (grad - unit * head_mean(grad * unit, ones))
        joined[block * HALF : (block + 1) * HALF, :] = jnp.concatenate(
            [grad, grad_kv[:, kv_width:]], axis=1
        ).astype(BF16)
    gain_grad[...] = gain_row
    read = sum_rest(out_copies, part, bufs)
    half = middle.shape[0] // 2
    for first in (0, half):
        rows = pl.ds(first, half)
        out[rows, :] = (middle[rows, :] + read(first)).astype(BF16)
    line_end(home_copies, home, going, coming, line, chips)
    chip = lax.axis_index("fsdp") // 2
    owned_rows = rest_sum.shape[1]
    for index in range(rest_sum.shape[0]):
        rest_sum[index] = home[chip, index * owned_rows : (index + 1) * owned_rows, :]


def tail_kernel(
    swaps,
    joined,
    out_grad,
    gain_row,
    attn_gain,
    ffn_gain_grad,
    *refs,
):
    sources, refs = refs[:4], refs[4:]
    swap_in, refs = refs[:swaps], refs[swaps:]
    grad_tokens, gains, attn_own = refs[:3]
    swap_out, refs = refs[3 : 3 + swaps], refs[3 + swaps :]
    targets, refs = refs[:4], refs[4:]
    weights_in, normed, x, grad_middle = targets
    back_bufs, refs = refs[:-15], refs[-15:]
    turned, part, attn_grad, home, travel, owned, ctx_box, fsdp_box = refs[:8]
    send_two, recv_two, send_three, recv_three, send_four, recv_four, local = refs[8:]
    going, coming = travel.at[0], travel.at[1]
    back_sems = (send_two, recv_two)
    line, small = (send_three, recv_three), (send_four, recv_four)
    size = lax.axis_size("ctx")
    me = lax.axis_index("ctx")
    chips = lax.axis_size("fsdp") // 2
    step_base = chips
    swap_base = step_base + 2 * chips
    qkv_width = joined.shape[1]
    qk_width = gain_row.shape[1]
    half = x.shape[0] // 2
    loads = [
        load(source, target, local.at[item])
        for item, (source, target) in enumerate(zip(sources, targets))
    ]
    meet(("ctx", "fsdp"))
    swap_copies = []
    own_copies = []
    for item in range(swaps):
        swap_copies += swap_start(
            swap_in[item], swap_out[item], line, swap_base + (item + 1) * size
        )
        own_copies.append(
            load(swap_in[item].at[me], swap_out[item].at[me], local.at[4 + item])
        )
    for copy in loads:
        copy.wait()
    for first in range(0, D, 512):
        part[:, first : first + 512] = dot(
            joined[...], weights_in[first : first + 512, :qkv_width], 1, 1
        ).astype(BF16)
    back_copies = sum_start(part, back_bufs, back_sems)
    turn(normed, turned)
    for first in range(0, D, 512):
        rows = slice(first, first + 512)
        attn_grad[rows, :qkv_width] = dot(turned[rows, :], joined[...], 1, 0).astype(BF16)
    attn_grad[:, qkv_width:] = out_grad[...]
    home_copies = line_start(attn_grad, home, line, 0)
    line_home(home_copies, attn_grad, home)
    line_step(chips - 1, home, going, coming, line, step_base)
    sum_pass(back_copies, part, back_bufs, back_sems)
    for reach in range(chips - 2, 1, -1):
        line_step(reach, home, going, coming, line, step_base)
    read = sum_rest(back_copies, part, back_bufs)
    total = jnp.zeros((1, D), F32)
    for first in (0, half):
        rows = pl.ds(first, half)
        values = x[rows, :].astype(F32)
        root = row_scale(values)
        unit = values * root
        back = read(first)
        total = total + jnp.sum(back * unit, axis=0, keepdims=True)
        back = back * attn_gain[...]
        back = root * (back - unit * jnp.mean(back * unit, axis=-1, keepdims=True))
        grad_tokens[rows, :] = grad_middle[rows, :] + back

    def spread_start(axis, box, value, base):
        index = lax.axis_index(axis)
        axis_size = lax.axis_size(axis)
        box[index] = value
        return [
            send(
                box.at[index],
                box.at[index],
                small,
                base + step,
                {axis: lax.rem(index + step, axis_size)},
            )
            for step in range(1, axis_size)
        ]

    def spread_end(copies, box):
        for copy in copies:
            copy.wait()
        summed = box[0]
        for item in range(1, box.shape[0]):
            summed = summed + box[item]
        return summed

    ctx_copies = spread_start(
        "ctx",
        ctx_box,
        jnp.concatenate(
            [
                total,
                ffn_gain_grad[...],
                jnp.concatenate([gain_row[...], jnp.zeros((1, D - qk_width), F32)], axis=1),
                jnp.zeros((5, D), F32),
            ],
            axis=0,
        ),
        0,
    )
    line_step(1, home, going, coming, line, step_base)
    fsdp_copies = spread_start("fsdp", fsdp_box, spread_end(ctx_copies, ctx_box), size)
    line_end(home_copies, home, going, coming, line, step_base)
    chip = lax.axis_index("fsdp") // 2
    owned_rows = owned.shape[1]
    for index in range(size):
        owned[index] = home[chip, index * owned_rows : (index + 1) * owned_rows, :]
    swap_copies += swap_start(owned, attn_own, line, swap_base)
    attn_own[me] = owned[me]
    gains[...] = spread_end(fsdp_copies, fsdp_box)
    for copy in swap_copies:
        copy.wait()
    for copy in own_copies:
        copy.wait()


def rms_scale(values_in, gain_vec):
    return (
        values_in
        * lax.rsqrt(jnp.mean(values_in * values_in, axis=-1, keepdims=True) + NORM_EPS)
        * gain_vec
    )


def inverse_freq():
    return 1.0 / ROPE_BASE ** (jnp.arange(0, HD, 2).astype(F32) / HD)


def shards(
    tokens,
    cotangent,
    doc_starts,
    block_order,
    master_weights,
    moment_one,
    moment_two,
    gains,
    gains_moment_one,
    gains_moment_two,
):
    nctx = lax.axis_size("ctx")
    nfsdp = lax.axis_size("fsdp")
    own_rows = master_weights.shape[0]
    tok_rows = tokens.shape[1]
    stream_len = tok_rows * nctx
    blocks = stream_len // HALF
    groups = KVHEADS // nctx
    q_width = D // nctx
    kv_width = KVD // nctx
    qk_width = q_width + kv_width
    qkv_width = qk_width + kv_width
    tiles = FF // 128
    ff_tiles = -(-tiles // nctx)
    ff_width = ff_tiles * 128
    bundles = 2
    cuts = [0, (ff_tiles * 5 + 3) // 7 * 128, ff_width]

    low = master_weights.astype(BF16)

    def ff_part(base, index, start, stop):
        first = index * ff_width + start
        last = index * ff_width + stop
        real_first, real_last = min(first, FF), min(last, FF)
        part = low[:, base + real_first : base + real_last]
        if real_last - real_first < last - first:
            part = jnp.pad(part, ((0, 0), (0, (last - first) - (real_last - real_first))))
        return part

    def attn_part(index):
        return jnp.concatenate(
            [
                low[:, index * q_width : (index + 1) * q_width],
                low[:, D + index * kv_width : D + (index + 1) * kv_width],
                low[:, D + KVD + index * kv_width : D + KVD + (index + 1) * kv_width],
                low[:, QKVC + index * q_width : QKVC + (index + 1) * q_width],
            ],
            axis=1,
        )

    gate_base = QKVC + D
    bases = (gate_base, gate_base + FF, gate_base + 2 * FF)
    attn_send = jnp.stack([attn_part(c) for c in range(nctx)])
    ff_send = [
        jnp.stack(
            [
                jnp.concatenate(
                    [ff_part(base, c, cuts[b], cuts[b + 1]) for base in bases], axis=1
                )
                for c in range(nctx)
            ]
        )
        for b in range(bundles)
    ]

    def gather_rows(piece):
        return lax.all_gather(
            piece.reshape(nctx * own_rows, piece.shape[-1]), "fsdp", axis=0, tiled=True
        )

    def spread(active):
        return (
            active.reshape(active.shape[0], nctx, nfsdp, own_rows)
            .transpose(0, 2, 1, 3)
            .reshape(active.shape[0], D)
        )

    def unspread(active):
        return (
            active.reshape(active.shape[0], nfsdp, nctx, own_rows)
            .transpose(0, 2, 1, 3)
            .reshape(active.shape[0], D)
        )

    dma = pltpu.SemaphoreType.DMA
    all_low = jax.ShapeDtypeStruct((nctx, tok_rows, D), BF16)
    own_low = jax.ShapeDtypeStruct((tok_rows, D), BF16)
    own_f32 = jax.ShapeDtypeStruct((tok_rows, D), F32)
    row_f32 = jax.ShapeDtypeStruct((1, D), F32)
    g_attn = spread(gains[None, :D])
    g_ffn = spread(gains[None, D : 2 * D])
    order = block_order.reshape(blocks)
    place = jnp.argsort(order).astype(jnp.int32)
    starts = doc_starts[0]
    chips = nfsdp // 2
    line_sems = dma((4 * chips,))
    x_low, dy_low, normed, table, _, w_attn, first_held = remote_call(
        first_kernel,
        [
            own_low,
            own_low,
            own_low,
            jax.ShapeDtypeStruct((stream_len, 2 * HD), F32),
            jax.ShapeDtypeStruct(attn_send.shape, BF16),
            jax.ShapeDtypeStruct((nfsdp,) + attn_send.shape, BF16),
            jax.ShapeDtypeStruct(ff_send[0].shape, BF16),
        ],
        (
            starts,
            spread(jnp.arange(D, dtype=jnp.int32)[None]),
            tokens[0],
            cotangent[0],
            g_attn,
            jnp.tile(inverse_freq(), 4)[None],
            attn_send,
            ff_send[0],
        ),
        0,
        38,
        [
            pltpu.VMEM((D, D), BF16),
            dma((2 * nctx,)),
            dma((2 * nctx,)),
            line_sems,
            line_sems,
            dma((3,)),
        ],
        (4, 5, 6),
        1,
        2,
    )
    w_attn = w_attn.reshape(D, attn_send.shape[-1])
    normed, first_held = lax.optimization_barrier((normed, first_held))
    (normed_all,) = exchange(("gather",), [normed], 2, 29)
    normed_all = normed_all.reshape(stream_len, D)


    g_query = gains[2 * D : 2 * D + HD]
    g_key = gains[2 * D + HD :]
    qk_gain = jnp.concatenate(
        [jnp.tile(g_query, q_width // HD), jnp.tile(g_key, kv_width // HD)]
    )[None]

    low_stream = pltpu.VMEM((stream_len, D), BF16)
    heads_low = pltpu.VMEM((stream_len, q_width), BF16)
    part, qk, q, k, v, mixed, lse, dy_all, second_held = remote_call(
        functools.partial(attend_kernel, blocks, groups),
        [
            jax.ShapeDtypeStruct((stream_len, D), BF16),
            jax.ShapeDtypeStruct((stream_len, qk_width), F32),
            jax.ShapeDtypeStruct((stream_len, q_width), BF16),
            jax.ShapeDtypeStruct((stream_len, kv_width), BF16),
            jax.ShapeDtypeStruct((stream_len, kv_width), BF16),
            jax.ShapeDtypeStruct((stream_len, q_width), BF16),
            jax.ShapeDtypeStruct((blocks, groups, GROUP * HALF), F32),
            all_low,
            jax.ShapeDtypeStruct(ff_send[1].shape, BF16),
        ],
        (place, order, starts, table, qk_gain, normed_all, w_attn, dy_low, ff_send[1]),
        3,
        42,
        [
            low_stream,
            pltpu.VMEM(w_attn.shape, BF16),
            pltpu.VMEM((blocks, HALF, qkv_width), F32),
            pltpu.VMEM((blocks, HALF, q_width), BF16),
            dma((GATHER_SEMS + nctx,)),
            dma((GATHER_SEMS + nctx,)),
            dma((4,)),
        ],
        (7, 8),
        3,
        4,
    )
    dy_all = dy_all.reshape(stream_len, D)
    w_ff = [gather_rows(first_held), gather_rows(second_held)]
    sum_bufs = sum_scratch(nctx, tok_rows)
    sum_sems = [dma((GATHER_SEMS,)), dma((GATHER_SEMS,))]
    norm_scratch = (
        sum_bufs + [pltpu.VMEM((tok_rows, D), BF16)] + sum_sems + sum_sems + [dma]
    )

    middle, normed_two_all = remote_call(
        middle_kernel,
        [own_f32, all_low],
        (part, x_low, g_ffn),
        4,
        57,
        norm_scratch,
        (1,),
    )
    normed_two_all = normed_two_all.reshape(stream_len, D)

    def sum_rows(grad):
        return lax.psum_scatter(grad, "fsdp", scatter_dimension=0, tiled=True).reshape(
            nctx, own_rows, grad.shape[-1]
        )

    def feed(b, x_all, dy):
        width = cuts[b + 1] - cuts[b]
        w_gu, w_down = w_ff[b][:, : 2 * width], w_ff[b][:, 2 * width :]
        gate_up = dot(x_all, w_gu, 1, 0).astype(BF16)
        gate, up = gate_up[:, :width].astype(F32), gate_up[:, width:].astype(F32)
        gated = jax.nn.sigmoid(gate)
        act = gate * gated
        hidden = (act * up).astype(BF16)
        back_hidden = dot(dy, w_down, 1, 0)
        grad_gu = jnp.concatenate(
            [back_hidden * up * (gated + act * (1.0 - gated)), back_hidden * act], axis=1
        ).astype(BF16)
        return hidden, grad_gu, dot(grad_gu, w_gu, 1, 1)

    hidden_one, grad_gu, back_partial = feed(0, normed_two_all, dy_all)
    gu_grad = dot(normed_two_all, grad_gu, 0, 0).astype(BF16)
    gu_grad, back_partial, w_ff[1] = lax.optimization_barrier((gu_grad, back_partial, w_ff[1]))
    width_two = cuts[2] - cuts[1]
    width_line = cuts[1] * 3 // 5 // 128 * 128
    width_rest = cuts[1] - width_line
    hidden_two, grad_gu, back_more = feed(1, normed_two_all, dy_all)
    back_partial = (back_partial + back_more).astype(BF16)
    gu_sum = sum_rows(gu_grad)
    chips = nfsdp // 2

    def line_scratch(columns):
        block = (nctx * own_rows, columns)
        return [pltpu.VMEM((chips,) + block, BF16), pltpu.VMEM((2, 2, chips - 1) + block, BF16)]

    (
        grad_middle,
        grad_g_ffn,
        down_sum,
        grad_middle_all,
        rest_grad,
        last_grad,
        out_partial,
    ) = remote_call(
        middle_back_kernel,
        [
            own_f32,
            row_f32,
            jax.ShapeDtypeStruct((nctx, own_rows, width_line), BF16),
            all_low,
            jax.ShapeDtypeStruct((D, width_rest), BF16),
            jax.ShapeDtypeStruct((D, 3 * width_two), BF16),
            jax.ShapeDtypeStruct((stream_len, D), BF16),
        ],
        (
            back_partial,
            middle,
            dy_low,
            g_ffn,
            normed_two_all,
            dy_all,
            hidden_one,
            hidden_two,
            grad_gu,
            w_ff[0],
            w_ff[1],
        ),
        5,
        57,
        sum_bufs
        + [
            pltpu.VMEM((tok_rows, D), BF16),
            low_stream,
            pltpu.VMEM((stream_len, 2 * width_two), BF16),
            pltpu.VMEM((D, stream_len), BF16),
            pltpu.VMEM((D, 3 * width_two), BF16),
            pltpu.VMEM((D, width_rest), BF16),
            pltpu.VMEM((D, width_line), BF16),
            low_stream,
            pltpu.VMEM((stream_len, cuts[1]), BF16),
            pltpu.VMEM((stream_len, width_two), BF16),
            pltpu.VMEM((D, cuts[1]), BF16),
            pltpu.VMEM((D, width_two), BF16),
        ]
        + line_scratch(width_line)
        + sum_sems
        + sum_sems
        + [dma((3 * chips,)), dma((3 * chips,)), dma((11,))],
        (3, 4, 5, 6),
        0,
        7,
    )
    last_sum = sum_rows(last_grad)

    small = dma((nctx + nfsdp,))
    line_sems = dma((3 * chips + 4 * nctx,))
    own_shape = (nctx, own_rows, qkv_width + q_width)
    sources = (
        grad_middle_all.reshape(blocks, HALF, D),
        w_attn,
        q,
        k,
        v,
        mixed,
        qk.reshape(blocks, HALF, qk_width),
        table.reshape(blocks, HALF, 2 * HD),
        middle,
    )
    out_tokens, grad_joined, qk_gain_grad, out_grad, rest_sum = remote_call(
        functools.partial(attend_back_kernel, blocks, groups),
        [
            own_low,
            jax.ShapeDtypeStruct((stream_len, qkv_width), BF16),
            jax.ShapeDtypeStruct((1, qk_width), F32),
            jax.ShapeDtypeStruct((D, q_width), BF16),
            jax.ShapeDtypeStruct((nctx, own_rows, width_rest), BF16),
        ],
        (place, order, starts, lse, qk_gain, out_partial, rest_grad) + sources,
        6,
        45,
        [pltpu.VMEM(source.shape, source.dtype) for source in sources]
        + sum_bufs
        + [
            heads_low,
            pltpu.VMEM((blocks, HALF, q_width), F32),
            pltpu.VMEM((blocks, HALF, 2 * kv_width), F32),
            pltpu.VMEM((D, stream_len), BF16),
        ]
        + line_scratch(width_rest)
        + sum_sems
        + [dma((3 * chips,)), dma((3 * chips,)), dma((9,))],
        (),
        3,
        9,
    )
    sources = (w_attn, normed_all, x_low, grad_middle)
    grad_tokens, gain_sums, attn_own, gu_own, down_own, rest_own = remote_call(
        functools.partial(tail_kernel, 3),
        [
            own_f32,
            jax.ShapeDtypeStruct((8, D), F32),
            jax.ShapeDtypeStruct(own_shape, BF16),
            jax.ShapeDtypeStruct(gu_sum.shape, BF16),
            jax.ShapeDtypeStruct(down_sum.shape, BF16),
            jax.ShapeDtypeStruct(rest_sum.shape, BF16),
        ],
        (grad_joined, out_grad, qk_gain_grad, g_attn, grad_g_ffn) + sources + (gu_sum, down_sum, rest_sum),
        7,
        75,
        [pltpu.VMEM(source.shape, source.dtype) for source in sources]
        + sum_bufs
        + [
            pltpu.VMEM((D, stream_len), BF16),
            low_stream,
            pltpu.VMEM((D, qkv_width + q_width), BF16),
        ]
        + line_scratch(qkv_width + q_width)
        + [
            pltpu.VMEM(own_shape, BF16),
            pltpu.VMEM((nctx, 8, D), F32),
            pltpu.VMEM((nfsdp, 8, D), F32),
        ]
        + sum_sems
        + [line_sems, line_sems, small, small, dma((7,))],
        (3, 4, 5),
        0,
        7,
    )
    last_sum, gain_sums, gu_own = lax.optimization_barrier((last_sum, gain_sums, gu_own))
    out_tokens = unspread(out_tokens)[None]
    grad_tokens = unspread(grad_tokens)[None]
    gain_grad = jnp.concatenate(
        [
            unspread(gain_sums[:1])[0],
            unspread(gain_sums[1:2])[0],
            jnp.sum(gain_sums[2, :q_width].reshape(-1, HD), axis=0),
            jnp.sum(gain_sums[2, q_width:qk_width].reshape(-1, HD), axis=0),
        ]
    )

    olds = (master_weights, moment_one, moment_two)

    def feed_segments(b, pieces, start, stop):
        found = []
        for part in pieces:
            for c in range(nctx):
                column = c * ff_width + cuts[b] + start
                real = min(max(FF - column, 0), stop - start)
                if real:
                    piece, first = pieces[part]
                    found.append((piece, c, first, bases[part] + column, real))
        return found

    width_one = cuts[1]
    last_own = [
        lax.ppermute(
            lax.dynamic_index_in_dim(last_sum, lax.axis_index("ctx") ^ k, 0, keepdims=False),
            "ctx",
            [(c, c ^ k) for c in range(nctx)],
        )
        if k
        else lax.dynamic_index_in_dim(last_sum, lax.axis_index("ctx"), 0, keepdims=False)
        for k in range(nctx)
    ]
    parts = (
        (0, 0, q_width),
        (q_width, D, kv_width),
        (qk_width, D + KVD, kv_width),
        (qkv_width, QKVC, q_width),
    )
    if kv_width % 128:
        attn_own = jnp.concatenate(
            [attn_own[c, :, f : f + w] for f, _, w in parts for c in range(nctx)], axis=1
        )[None]
        segments = [(0, 0, 0, 0, gate_base)]
    else:
        segments = [
            (0, c, first, base + c * width, width)
            for first, base, width in parts
            for c in range(nctx)
        ]
    news = adam(
        segments
        + feed_segments(0, {0: (1, 0), 1: (1, width_one)}, 0, width_one)
        + feed_segments(0, {2: (2, 0)}, 0, width_line)
        + feed_segments(0, {2: (3, 0)}, width_line, width_one),
        [attn_own, gu_own, down_own, rest_own],
        olds,
        None,
        10,
    )
    first_new, second_new, master_new, low_new = adam(
        feed_segments(
            1, {0: (None, 0), 1: (None, width_two), 2: (None, 2 * width_two)}, 0, width_two
        ),
        last_own,
        olds,
        news,
        6,
    )
    gain_first, gain_second, gain_new = adam_update(
        gains, gain_grad, gains_moment_one, gains_moment_two, GAIN_RATE, 0.0
    )
    return (
        out_tokens,
        grad_tokens,
        first_new,
        second_new,
        master_new,
        low_new,
        gain_first,
        gain_second,
        gain_new,
    )


def solution(mesh):
    rows = P("fsdp", "ctx", None)
    weights = P(("ctx", "fsdp"), None)
    return jax.shard_map(
        shards,
        mesh=mesh,
        in_specs=(rows, rows, P("fsdp", None), P(), weights, weights, weights, P(), P(), P()),
        out_specs=(rows, rows, weights, weights, weights, weights, P(), P(), P()),
        check_vma=False,
    )
```

```python
import functools

import jax
import jax.numpy as jnp
from jax import lax
from jax.experimental import pallas as pl
from jax.experimental.pallas import tpu as pltpu
from jax.sharding import PartitionSpec as P

D = 1536
HEADS = 24
KVHEADS = 8
HD = 64
FF = 6912
STEP = 10
HALF = 128
KVD = 512
QKVC = 2560
GROUP = HEADS // KVHEADS

ROPE_BASE = 1000000.0
NORM_EPS = 1e-05
BETA_ONE = 0.9
BETA_TWO = 0.95
ADAM_EPS = 1e-08
WEIGHT_DECAY = 0.1
LEARN_RATE = 0.03
GAIN_RATE = 0.5
SCALE = HD ** (-0.5)
MESH = pl.DeviceIdType.MESH
F32 = jnp.float32
BF16 = jnp.bfloat16
VMEM_LIMIT = 60 * 1024 * 1024


def dot(left, right, left_dim, right_dim):
    return lax.dot_general(
        left, right, (((left_dim,), (right_dim,)), ((), ())), preferred_element_type=F32
    )


def send(source, target, sems, item, peer):
    copy = pltpu.make_async_remote_copy(
        src_ref=source,
        dst_ref=target,
        send_sem=sems[0].at[item],
        recv_sem=sems[1].at[item],
        device_id=peer,
        device_id_type=MESH,
    )
    copy.start()
    return copy


def meet(axes):
    barrier = pltpu.get_barrier_semaphore()
    total = 0
    for axis in axes:
        size = lax.axis_size(axis)
        me = lax.axis_index(axis)
        for step in range(1, size):
            pl.semaphore_signal(
                barrier,
                inc=1,
                device_id={axis: lax.rem(me + step, size)},
                device_id_type=MESH,
            )
        total += size - 1
    pl.semaphore_wait(barrier, total)


def square():
    me = lax.axis_index("ctx")
    return me, me + 1 - 2 * lax.rem(me, 2), lax.rem(me + 2, 4), 3 - me


def swap_start(source, target, sems, base):
    size = lax.axis_size("ctx")
    me = lax.axis_index("ctx")
    copies = []
    for step in range(1, size):
        peer = lax.rem(me + step, size)
        copies.append(
            send(source.at[peer], target.at[me], sems, base + step, {"ctx": peer})
        )
    return copies


def gather_start(source, target, sems, base):
    size = lax.axis_size("ctx")
    me = lax.axis_index("ctx")
    if size != 4:
        return [
            send(
                source,
                target.at[me],
                sems,
                base + step,
                {"ctx": lax.rem(me + step, size)},
            )
            for step in range(1, size)
        ]
    me, side, over, across = square()
    half = source.shape[0] // 2
    top, low = pl.ds(0, half), pl.ds(half, half)
    return [
        send(source.at[top], target.at[me, top], sems, base, {"ctx": side}),
        send(source.at[low], target.at[me, low], sems, base + 1, {"ctx": over}),
        send(source.at[low], target.at[me, low], sems, base + 2, {"ctx": side}),
        send(source.at[top], target.at[me, top], sems, base + 3, {"ctx": over}),
    ]


def gather_pass(copies, target, sems, base):
    if lax.axis_size("ctx") != 4:
        return
    me, side, over, across = square()
    half = target.shape[1] // 2
    top, low = pl.ds(0, half), pl.ds(half, half)
    copies[0].wait_recv()
    copies.append(send(target.at[side, top], target.at[side, top], sems, base + 4, {"ctx": over}))
    copies[1].wait_recv()
    copies.append(send(target.at[over, low], target.at[over, low], sems, base + 5, {"ctx": side}))


def gather_end(copies):
    if lax.axis_size("ctx") != 4:
        for copy in copies:
            copy.wait()
        return
    for copy in copies:
        copy.wait_send()
    for copy in copies[2:]:
        copy.wait_recv()


def gather_rest(copies, target, sems, base):
    gather_pass(copies, target, sems, base)
    gather_end(copies)


def load(source, target, sem):
    copy = pltpu.make_async_copy(source, target, sem)
    copy.start()
    return copy


GATHER_SEMS = 8


def exchange_kernel(kinds, *refs):
    count = len(kinds)
    ins, outs = refs[:count], refs[count : 2 * count]
    send_sem, recv_sem, local_sem = refs[2 * count :]
    sems = (send_sem, recv_sem)
    me = lax.axis_index("ctx")
    meet(("ctx",))
    copies = []
    own = []
    for item in range(count):
        base = item * GATHER_SEMS
        if kinds[item] == "gather":
            copies.append(gather_start(ins[item], outs[item], sems, base))
            source = ins[item]
        else:
            copies.append(swap_start(ins[item], outs[item], sems, base))
            source = ins[item].at[me]
        copy = pltpu.make_async_copy(source, outs[item].at[me], local_sem.at[item])
        copy.start()
        own.append(copy)
    for item in range(count):
        if kinds[item] == "gather":
            gather_rest(copies[item], outs[item], sems, item * GATHER_SEMS)
        else:
            for copy in copies[item]:
                copy.wait()
    for copy in own:
        copy.wait()


def remote_params(collective_id):
    return pltpu.CompilerParams(
        collective_id=collective_id, has_side_effects=True, vmem_limit_bytes=VMEM_LIMIT
    )


def cost(micros):
    return pl.CostEstimate(flops=0, bytes_accessed=int(micros * 3.0e6), transcendentals=0)


def exchange(kinds, arrays, collective_id, micros):
    size = lax.axis_size("ctx")
    shapes = [
        jax.ShapeDtypeStruct((size,) + a.shape if kind == "gather" else a.shape, a.dtype)
        for kind, a in zip(kinds, arrays)
    ]
    sems = pltpu.SemaphoreType.DMA((len(arrays) * GATHER_SEMS,))
    return pl.pallas_call(
        functools.partial(exchange_kernel, kinds),
        out_shape=shapes,
        in_specs=[pl.BlockSpec(memory_space=pl.ANY)] * len(arrays),
        out_specs=[pl.BlockSpec(memory_space=pl.ANY)] * len(arrays),
        scratch_shapes=[sems, sems, pltpu.SemaphoreType.DMA((len(arrays),))],
        compiler_params=remote_params(collective_id),
        cost_estimate=cost(micros),
    )(*arrays)


def sum_scratch(size, rows):
    if size == 4:
        half = pltpu.VMEM((2, rows // 2, D), BF16)
        return [half, half, pltpu.VMEM((2, rows, D), BF16)]
    return [pltpu.VMEM((size - 1, rows, D), BF16)]


def sum_start(part, bufs, sems):
    size = lax.axis_size("ctx")
    me = lax.axis_index("ctx")
    rows = part.shape[0] // size

    def block(owner, first=0, count=rows):
        return pl.ds(pl.multiple_of(owner * rows + first, rows // 2), count)

    if size != 4:
        copies = []
        for step in range(1, size):
            peer = lax.rem(me + step, size)
            copies.append(
                send(part.at[block(peer)], bufs[0].at[step - 1], sems, step, {"ctx": peer})
            )
        return copies
    me, side, over, across = square()
    half = rows // 2
    relay, _, landed = bufs
    return [
        send(part.at[block(across, 0, half)], relay.at[0], sems, 0, {"ctx": side}),
        send(part.at[block(across, half, half)], relay.at[1], sems, 1, {"ctx": over}),
        send(
            part.at[block(side, 0, half)],
            landed.at[0, pl.ds(0, half)],
            sems,
            2,
            {"ctx": side},
        ),
        send(
            part.at[block(over, half, half)],
            landed.at[1, pl.ds(half, half)],
            sems,
            3,
            {"ctx": over},
        ),
    ]


def sum_pass(copies, part, bufs, sems):
    if lax.axis_size("ctx") != 4:
        return
    rows = part.shape[0] // 4
    half = rows // 2

    def rows_of(owner, first):
        return pl.ds(pl.multiple_of(owner * rows + first, half), half)

    me, side, over, across = square()
    relay, passed, landed = bufs
    copies[0].wait_recv()
    passed[0] = (part[rows_of(over, 0), :].astype(F32) + relay[0].astype(F32)).astype(BF16)
    copies.append(
        send(passed.at[0], landed.at[1, pl.ds(0, half)], sems, 4, {"ctx": over})
    )
    copies[1].wait_recv()
    passed[1] = (part[rows_of(side, half), :].astype(F32) + relay[1].astype(F32)).astype(
        BF16
    )
    copies.append(
        send(passed.at[1], landed.at[0, pl.ds(half, half)], sems, 5, {"ctx": side})
    )


def sum_rest(copies, part, bufs):
    size = lax.axis_size("ctx")
    me = lax.axis_index("ctx")
    rows = part.shape[0] // size
    half = rows // 2

    def rows_of(owner, first):
        return pl.ds(pl.multiple_of(owner * rows + first, half), half)

    if size != 4:
        for copy in copies:
            copy.wait()

        def read(first):
            total = part[rows_of(me, first), :].astype(F32)
            for step in range(1, size):
                total = total + bufs[0][step - 1, pl.ds(first, half), :].astype(F32)
            return total

        return read
    relay, passed, landed = bufs
    for copy in copies:
        copy.wait_send()
    for copy in copies[2:]:
        copy.wait_recv()

    def read(first):
        return (
            part[rows_of(me, first), :].astype(F32)
            + landed[0, pl.ds(first, half), :].astype(F32)
            + landed[1, pl.ds(first, half), :].astype(F32)
        )

    return read


def row_scale(values):
    return lax.rsqrt(jnp.mean(values * values, axis=-1, keepdims=True) + NORM_EPS)


def first_kernel(
    starts, origin, x, dy, gain, freq, x_low, dy_low, table, normed_all, *scratch
):
    move, normed, send_one, recv_one, local = scratch
    me = lax.axis_index("ctx")
    row = lax.broadcasted_iota(jnp.int32, move.shape, 0)
    move[...] = jnp.where(row == origin[...], 1.0, 0.0).astype(BF16)
    values = dot(x[...], move[...], 1, 0)
    x_low[...] = values.astype(BF16)
    normed[...] = (values * row_scale(values) * gain[...]).astype(BF16)
    meet(("ctx",))
    sems = (send_one, recv_one)
    copies = gather_start(normed, normed_all, sems, 0)
    own = load(normed, normed_all.at[me], local)
    dy_low[...] = dot(dy[...], move[...], 1, 0).astype(BF16)
    gather_pass(copies, normed_all, sems, 0)
    times = lax.broadcasted_iota(jnp.int32, (table.shape[0], 1), 0)
    angles = (times - doc_first(starts, times)).astype(F32) * freq[...]
    lane = lax.broadcasted_iota(jnp.int32, angles.shape, 1)
    sine = jnp.sin(angles)
    sine = jnp.where(lane % HD < HD // 2, -sine, sine)
    table[...] = jnp.where(lane < HD, jnp.cos(angles), sine)
    gather_end(copies)
    own.wait()


def middle_kernel(part, x, gain, middle, normed_all, *scratch):
    bufs, (normed, send_one, recv_one, send_two, recv_two, local) = scratch[:-6], scratch[-6:]
    me = lax.axis_index("ctx")
    meet(("ctx",))
    copies = sum_start(part, bufs, (send_one, recv_one))
    sum_pass(copies, part, bufs, (send_one, recv_one))
    read = sum_rest(copies, part, bufs)
    half = x.shape[0] // 2
    for first in (0, half):
        rows = pl.ds(first, half)
        values = x[rows, :].astype(F32) + read(first)
        middle[rows, :] = values
        normed[rows, :] = (values * row_scale(values) * gain[...]).astype(BF16)
    sems = (send_two, recv_two)
    copies = gather_start(normed, normed_all, sems, 0)
    own = load(normed, normed_all.at[me], local)
    gather_rest(copies, normed_all, sems, 0)
    own.wait()


def column_tiles(total, body):
    def step(tile, carry):
        body(pl.multiple_of(tile * 256, 256), 256)
        return carry

    lax.fori_loop(0, total // 256, step, 0)
    if total % 256:
        body(total - total % 256, total % 256)


def turn(source, target):
    for first in range(0, source.shape[0], HALF):
        rows = slice(first, first + HALF)
        target[:, rows] = source[rows, :].T


def feed_back_kernel(
    down_grad, x_all, grad_gu, weights, down_sum, gu_grad, back, *scratch
):
    x_buf, gu_buf, weight_buf, turned, gu_out, back_out, home, travel, send_one, recv_one, local = (
        scratch
    )
    going, coming = travel.at[0], travel.at[1]
    line = (send_one, recv_one)
    chips = lax.axis_size("fsdp") // 2
    width = grad_gu.shape[1]
    meet(("fsdp",))
    home_copies = line_start(down_grad, home, line, 0)
    loads = [
        load(x_all, x_buf, local.at[0]),
        load(grad_gu, gu_buf, local.at[1]),
        load(weights.at[:, pl.ds(0, width)], weight_buf, local.at[2]),
    ]
    loads[0].wait()
    turn(x_buf, turned)
    line_home(home_copies, down_grad, home)
    line_step(chips - 1, home, going, coming, line, chips)
    loads[1].wait()

    def gu_tiles(begin, count):
        def tile(first, span):
            columns = pl.ds(begin + first, span)
            gu_out[:, columns] = dot(turned[...], gu_buf[:, columns], 1, 0).astype(BF16)

        column_tiles(count, tile)

    gu_tiles(0, width // 2)
    if chips > 2:
        line_step(chips - 2, home, going, coming, line, chips)
    gu_tiles(width // 2, width - width // 2)
    stores = [load(gu_out, gu_grad, local.at[3])]
    for reach in range(min(chips - 1, max(chips - 3, 1)), 0, -1):
        line_step(reach, home, going, coming, line, chips)
    loads[2].wait()

    def back_tile(first, span):
        columns = pl.ds(first, span)
        back_out[:, columns] = dot(gu_buf[...], weight_buf[columns, :], 1, 1).astype(BF16)

    column_tiles(D, back_tile)
    stores.append(load(back_out, back, local.at[4]))
    line_end(home_copies, home, going, coming, line, chips)
    chip = lax.axis_index("fsdp") // 2
    rows = down_sum.shape[1]
    for index in range(down_sum.shape[0]):
        down_sum[index] = home[chip, index * rows : (index + 1) * rows, :]
    for copy in stores:
        copy.wait()


def middle_back_kernel(
    part,
    middle,
    dy,
    gain,
    x_all,
    dy_all,
    hidden_one,
    hidden_two,
    grad_gu,
    w_one,
    w_two,
    grad,
    gain_grad,
    down_sum,
    grad_all,
    weight_grad,
    out,
    *scratch,
):
    bufs = scratch[:-20]
    low, x_buf, gu_buf, turned, weight_buf, down_grad, out_buf = scratch[-20:-13]
    hidden_bufs, down_bufs = scratch[-13:-11], scratch[-11:-9]
    home, travel, send_one, recv_one, send_two, recv_two, send_three, recv_three, local = (
        scratch[-9:]
    )
    going, coming = travel.at[0], travel.at[1]
    me = lax.axis_index("ctx")
    chips = lax.axis_size("fsdp") // 2
    line = (send_three, recv_three)
    meet(("ctx", "fsdp"))
    copies = sum_start(part, bufs, (send_one, recv_one))
    width_one, width_two = hidden_one.shape[1], hidden_two.shape[1]
    gu_width = grad_gu.shape[1]
    loads = [
        load(source, target, local.at[item])
        for item, (source, target) in enumerate(
            (
                (dy_all, x_buf),
                (hidden_one, hidden_bufs[0]),
                (hidden_two, hidden_bufs[1]),
                (grad_gu, gu_buf),
                (w_one.at[:, pl.ds(2 * width_one, width_one)], down_bufs[0]),
                (w_two.at[:, pl.ds(2 * width_two, width_two)], down_bufs[1]),
            )
        )
    ]
    loads[0].wait()
    turn(x_buf, turned)
    loads.append(load(x_all, x_buf, local.at[6]))
    loads[1].wait()

    def product(target, column, right, begin=0, count=None):
        def tile(first, width):
            target[:, pl.ds(column + first, width)] = dot(
                turned[...], right[:, pl.ds(begin + first, width)], 1, 0
            ).astype(BF16)

        column_tiles(right.shape[1] if count is None else count, tile)

    width_rest = down_grad.shape[1]
    product(down_grad, 0, hidden_bufs[0], width_one - width_rest, width_rest)
    home_copies = line_start(down_grad, home, line, 0)
    sum_pass(copies, part, bufs, (send_one, recv_one))
    line_home(home_copies, down_grad, home)
    line_step(chips - 1, home, going, coming, line, chips)
    loads[2].wait()
    product(weight_buf, gu_width, hidden_bufs[1])
    loads[6].wait()
    turn(x_buf, turned)
    loads[3].wait()
    product(weight_buf, 0, gu_buf)
    stores = [load(weight_buf, weight_grad, local.at[7])]
    if chips > 2:
        line_step(chips - 2, home, going, coming, line, chips)
    read = sum_rest(copies, part, bufs)
    half = dy.shape[0] // 2
    total = jnp.zeros((1, D), F32)
    for first in (0, half):
        rows = pl.ds(first, half)
        values = middle[rows, :]
        root = row_scale(values)
        unit = values * root
        back = read(first)
        total = total + jnp.sum(back * unit, axis=0, keepdims=True)
        back = back * gain[...]
        back = root * (back - unit * jnp.mean(back * unit, axis=-1, keepdims=True))
        back = back + dy[rows, :].astype(F32)
        grad[rows, :] = back
        low[rows, :] = back.astype(BF16)
    gain_grad[...] = total
    sems = (send_two, recv_two)
    copies = gather_start(low, grad_all, sems, 0)
    stores.append(load(low, grad_all.at[me], local.at[8]))
    loads[4].wait()
    loads[5].wait()

    def out_tile(first, width):
        columns = pl.ds(first, width)
        out_buf[:, columns] = (
            dot(hidden_bufs[0][...], down_bufs[0][columns, :], 1, 1)
            + dot(hidden_bufs[1][...], down_bufs[1][columns, :], 1, 1)
        ).astype(BF16)

    column_tiles(D, out_tile)
    stores.append(load(out_buf, out, local.at[9]))
    gather_pass(copies, grad_all, sems, 0)
    for reach in range(min(chips - 1, max(chips - 3, 1)), 0, -1):
        line_step(reach, home, going, coming, line, chips)
    line_end(home_copies, home, going, coming, line, chips)
    chip = lax.axis_index("fsdp") // 2
    rows = down_sum.shape[1]
    for index in range(down_sum.shape[0]):
        down_sum[index] = home[chip, index * rows : (index + 1) * rows, :]
    gather_end(copies)
    for copy in stores:
        copy.wait()


def line_start(grad, home, sems, base):
    me = lax.axis_index("fsdp")
    chips = lax.axis_size("fsdp") // 2
    core = lax.rem(me, 2)
    rows = grad.shape[0] // (2 * chips)
    copies = []
    for chip in range(chips):
        theirs = pl.ds(pl.multiple_of((2 * chip + 1 - core) * rows, rows), rows)
        copies.append(
            send(grad.at[theirs], home.at[chip], sems, base + chip, {"fsdp": me + 1 - 2 * core})
        )
    return copies


def line_home(copies, grad, home):
    me = lax.axis_index("fsdp")
    chips = lax.axis_size("fsdp") // 2
    core = lax.rem(me, 2)
    rows = grad.shape[0] // (2 * chips)
    for chip in range(chips):
        copies[chip].wait_recv()
        mine = pl.ds(pl.multiple_of((2 * chip + core) * rows, rows), rows)
        home[chip] = (home[chip].astype(F32) + grad[mine, :].astype(F32)).astype(BF16)


def line_copies(reach, going, coming, sems, base):
    me = lax.axis_index("fsdp")
    chips = lax.axis_size("fsdp") // 2
    chip = me // 2
    found = []
    for side, way in ((0, 1), (1, -1)):
        copy = pltpu.make_async_remote_copy(
            src_ref=going.at[side, reach - 1],
            dst_ref=coming.at[side, reach - 1],
            send_sem=sems[0].at[base + 2 * reach + side],
            recv_sem=sems[1].at[base + 2 * reach + side],
            device_id={"fsdp": lax.rem(me + 2 * way + 2 * chips, 2 * chips)},
            device_id_type=MESH,
        )
        if way == 1:
            sent = chip + reach <= chips - 1
            got = (chip >= 1) & (chip + reach <= chips)
            more = (chip >= 1) & sent
        else:
            sent = chip >= reach
            got = (chip <= chips - 2) & (chip + 1 >= reach)
            more = (chip <= chips - 2) & sent
        found.append((side, way, copy, sent, got, more))
    return found


def line_step(reach, home, going, coming, sems, base):
    me = lax.axis_index("fsdp")
    chips = lax.axis_size("fsdp") // 2
    chip = me // 2
    if reach < chips - 1:
        for _, _, copy, _, got, _ in line_copies(reach + 1, going, coming, sems, base):
            pl.when(got)(copy.wait_recv)
    for side, way, copy, sent, _, more in line_copies(reach, going, coming, sems, base):

        @pl.when(sent)
        def _(side=side, way=way, copy=copy, more=more):
            value = home[chip + way * reach]
            if reach < chips - 1:

                @pl.when(more)
                def _():
                    going[side, reach - 1] = (
                        value.astype(F32) + coming[side, reach].astype(F32)
                    ).astype(BF16)

                @pl.when(jnp.logical_not(more))
                def _():
                    going[side, reach - 1] = value

            else:
                going[side, reach - 1] = value
            copy.start()


def line_end(copies, home, going, coming, sems, base):
    me = lax.axis_index("fsdp")
    chips = lax.axis_size("fsdp") // 2
    chip = me // 2
    for side, _, copy, _, got, _ in line_copies(1, going, coming, sems, base):

        @pl.when(got)
        def _(side=side, copy=copy):
            copy.wait_recv()
            home[chip] = (home[chip].astype(F32) + coming[side, 0].astype(F32)).astype(BF16)

    for copy in copies:
        copy.wait_send()
    for reach in range(1, chips):
        for _, _, copy, sent, _, _ in line_copies(reach, going, coming, sems, base):
            pl.when(sent)(copy.wait_send)


def remote_call(
    kernel, out_shape, args, collective_id, micros, scratch, in_hbm=(), smem=0, args_in_hbm=0
):
    return pl.pallas_call(
        kernel,
        out_shape=out_shape,
        in_specs=[pl.BlockSpec(memory_space=pltpu.SMEM)] * smem
        + [pl.BlockSpec(memory_space=pltpu.VMEM)] * (len(args) - smem - args_in_hbm)
        + [pl.BlockSpec(memory_space=pl.ANY)] * args_in_hbm,
        out_specs=[
            pl.BlockSpec(memory_space=pl.ANY if item in in_hbm else pltpu.VMEM)
            for item in range(len(out_shape))
        ],
        scratch_shapes=scratch,
        compiler_params=remote_params(collective_id),
        cost_estimate=cost(micros),
    )(*args)


def adam_update(param_now, grad_now, moment_old_one, moment_old_two, step_rate, decay_rate):
    first_new = BETA_ONE * moment_old_one + (1.0 - BETA_ONE) * grad_now
    second_new = BETA_TWO * moment_old_two + (1.0 - BETA_TWO) * grad_now * grad_now
    ratio = (first_new * (1.0 / (1.0 - BETA_ONE**STEP))) / (
        jnp.sqrt(second_new * (1.0 / (1.0 - BETA_TWO**STEP))) + ADAM_EPS
    )
    return (first_new, second_new, param_now - step_rate * (ratio + decay_rate * param_now))


def joined_ranges(segments):
    ranges = []
    for number in sorted(range(len(segments)), key=lambda n: segments[n][3]):
        column, width = segments[number][3:]
        if ranges and ranges[-1][0] + ranges[-1][1] == column:
            first, so_far, numbers = ranges[-1]
            ranges[-1] = (first, so_far + width, numbers + (number,))
        else:
            ranges.append((column, width, (number,)))
    return ranges


def adam_kernel(segments, pieces, held, *refs):
    me = lax.axis_index("ctx")
    grads = refs[:pieces]
    olds = refs[pieces : pieces + 3]
    news = refs[pieces + 3 + held : pieces + 3 + held + 4]
    grad_buf, old_buf, low_buf, grad_sem, in_sem, out_sem = refs[pieces + 3 + held + 4 :]
    base = min(segment[3] for segment in segments)
    ranges = joined_ranges(segments)
    loads = []
    for place, (column, width, numbers) in enumerate(ranges):
        here, there = pl.ds(column - base, width), pl.ds(column, width)
        copies = [
            load(olds[item].at[:, there], old_buf.at[item, :, here], in_sem.at[item, place])
            for item in range(3)
        ]
        for number in numbers:
            piece, index, first, start, count = segments[number]
            columns = pl.ds(first, count)
            for source_number, source in enumerate(grads):
                if piece not in (None, source_number):
                    continue
                copy = pltpu.make_async_copy(
                    source.at[:, columns] if piece is None else source.at[index, :, columns],
                    grad_buf.at[:, pl.ds(start - base, count)],
                    grad_sem.at[number],
                )
                if piece is None:
                    pl.when(me == index ^ source_number)(copy.start)
                else:
                    copy.start()
            copies.append(copy)
        loads.append(copies)
    stores = []
    for place, (column, width, numbers) in enumerate(ranges):
        for copy in loads[place]:
            copy.wait()
        here, there = pl.ds(column - base, width), pl.ds(column, width)
        for first in range(0, width, 256):
            part = pl.ds(column - base + first, min(256, width - first))
            first_new, second_new, master = adam_update(
                old_buf[0, :, part],
                grad_buf[:, part].astype(F32),
                old_buf[1, :, part],
                old_buf[2, :, part],
                LEARN_RATE,
                WEIGHT_DECAY,
            )
            old_buf[0, :, part] = master
            old_buf[1, :, part] = first_new
            old_buf[2, :, part] = second_new
            low_buf[:, part] = master.astype(BF16)
        for item, source in enumerate(
            (
                old_buf.at[1, :, here],
                old_buf.at[2, :, here],
                old_buf.at[0, :, here],
                low_buf.at[:, here],
            )
        ):
            stores.append(load(source, news[item].at[:, there], out_sem.at[item, place]))
    for copy in stores:
        copy.wait()


def adam(segments, grads, olds, held, micros):
    rows, columns = olds[0].shape
    span = max(s[3] + s[4] for s in segments) - min(s[3] for s in segments)
    held = [] if held is None else list(held)
    args = list(grads) + list(olds) + held
    return pl.pallas_call(
        functools.partial(adam_kernel, tuple(segments), len(grads), len(held)),
        out_shape=[jax.ShapeDtypeStruct((rows, columns), F32)] * 3
        + [jax.ShapeDtypeStruct((rows, columns), BF16)],
        in_specs=[pl.BlockSpec(memory_space=pl.ANY)] * len(args),
        out_specs=[pl.BlockSpec(memory_space=pl.ANY)] * 4,
        input_output_aliases={len(grads) + 3 + item: item for item in range(len(held))},
        scratch_shapes=[
            pltpu.VMEM((rows, span), BF16),
            pltpu.VMEM((3, rows, span), F32),
            pltpu.VMEM((rows, span), BF16),
            pltpu.SemaphoreType.DMA((len(segments),)),
            pltpu.SemaphoreType.DMA((3, len(segments))),
            pltpu.SemaphoreType.DMA((4, len(segments))),
        ],
        compiler_params=pltpu.CompilerParams(vmem_limit_bytes=VMEM_LIMIT),
        cost_estimate=cost(micros),
    )(*args)


def head_mean(values, ones):
    high = values.astype(BF16)
    rest = (values - high.astype(F32)).astype(BF16)
    return (dot(high, ones, 1, 0) + dot(rest, ones, 1, 0)) * (1.0 / HD)


def head_ones(width):
    row = lax.broadcasted_iota(jnp.int32, (width, width), 0) // HD
    col = lax.broadcasted_iota(jnp.int32, (width, width), 1) // HD
    return jnp.where(row == col, 1.0, 0.0).astype(BF16)


def partner(values):
    width = values.shape[-1]
    lane = lax.broadcasted_iota(jnp.int32, values.shape, 1)
    return jnp.where(
        lane % HD < HD // 2,
        pltpu.roll(values, width - HD // 2, 1),
        pltpu.roll(values, HD // 2, 1),
    )


def widen(table, width):
    return [
        jnp.concatenate([part] * (width // HD), axis=-1)
        for part in (table[:, :HD], table[:, HD:])
    ]


def doc_first(starts, times):
    first = jnp.zeros_like(times)
    for item in range(starts.shape[0]):
        first = jnp.where(starts[item] <= times, starts[item], first)
    return first


def block_mask(starts, block, keys):
    shape = (keys, GROUP * HALF)
    times = block * HALF + lax.broadcasted_iota(jnp.int32, (1, GROUP * HALF), 1) % HALF
    key = lax.broadcasted_iota(jnp.int32, shape, 0)
    return (key >= doc_first(starts, times)) & (key <= times)


def stack_heads(ref, rows, group):
    return jnp.concatenate(
        [
            ref[rows, (group * GROUP + h) * HD : (group * GROUP + h + 1) * HD]
            for h in range(GROUP)
        ],
        axis=0,
    )


def unstack_heads(turned):
    wide = turned.T
    return [wide[h * HALF : (h + 1) * HALF, :] for h in range(GROUP)]


def attend_kernel(
    blocks,
    groups,
    place,
    order,
    starts,
    table,
    gain,
    normed_in,
    weights_from,
    dy,
    swap_in,
    part,
    qk,
    q,
    k,
    v,
    o_held,
    lse,
    dy_all,
    swap_out,
    normed,
    weights_in,
    joined,
    o,
    send_sem,
    recv_sem,
    local,
):
    sems = (send_sem, recv_sem)
    me = lax.axis_index("ctx")
    qk_width = qk.shape[1]
    q_width = q.shape[1]
    qkv_width = qk_width + v.shape[1]
    ones = head_ones(qk_width)
    meet(("ctx",))
    loads = [
        load(normed_in, normed, local.at[0]),
        load(weights_from, weights_in, local.at[1]),
    ]
    swap_copies = swap_start(swap_in, swap_out, sems, GATHER_SEMS)
    copies = gather_start(dy, dy_all, sems, 0)
    own_copies = [
        load(swap_in.at[me], swap_out.at[me], local.at[2]),
        load(dy, dy_all.at[me], local.at[3]),
    ]
    for copy in loads:
        copy.wait()
    for block in range(blocks):
        joined[block] = dot(
            normed[block * HALF : (block + 1) * HALF, :], weights_in[:, :qkv_width], 1, 0
        )
    for block in range(blocks):
        to = slice(block * HALF, (block + 1) * HALF)
        values = joined[place[block]]
        v[to, :] = values[:, qk_width:].astype(BF16)
        values = values[:, :qk_width]
        qk[to, :] = values
        turned = values * lax.rsqrt(head_mean(values * values, ones) + NORM_EPS) * gain[...]
        cosine, sine = widen(table[to, :], qk_width)
        turned = turned * cosine + partner(turned) * sine
        turned = turned.astype(BF16)
        q[to, :] = turned[:, :q_width]
        k[to, :] = turned[:, q_width:]
    for block in range(blocks):
        rows = slice(block * HALF, (block + 1) * HALF)
        keys = (block + 1) * HALF
        mask = block_mask(starts, block, keys)
        pieces = []
        for group in range(groups):
            lanes = slice(group * HD, (group + 1) * HD)
            queries = stack_heads(q, rows, group)
            scores = dot(k[:keys, lanes], queries, 1, 1) * SCALE
            weights = jnp.where(mask, jnp.exp(scores), 0.0)
            sums = jnp.sum(weights, axis=0, keepdims=True)
            lse[block, group : group + 1, :] = jnp.log(sums)
            mixed = dot(v[:keys, lanes], weights.astype(BF16), 0, 0) / sums
            pieces += unstack_heads(mixed)
        o[block] = jnp.concatenate(pieces, axis=1).astype(BF16)
    for block in range(blocks):
        o_held[block * HALF : (block + 1) * HALF, :] = o[order[block]]
    for first in range(0, D, 512):
        part[:, first : first + 512] = dot(
            o_held[...], weights_in[first : first + 512, qkv_width:], 1, 1
        ).astype(BF16)
    gather_rest(copies, dy_all, sems, 0)
    for copy in swap_copies:
        copy.wait()
    for copy in own_copies:
        copy.wait()


def attend_back_kernel(
    blocks,
    groups,
    place,
    order,
    starts,
    lse,
    gain,
    part,
    *refs,
):
    sources, refs = refs[:9], refs[9:]
    out, joined, gain_grad, out_grad = refs[:4]
    targets, refs = refs[4:13], refs[13:]
    grad_all, weights_in, q, k, v, o, qk, table, middle = targets
    bufs, (do, dq, dkv, turned, send_one, recv_one, local) = refs[:-7], refs[-7:]
    out_sems = (send_one, recv_one)
    qk_width = qk.shape[2]
    qkv_width = qk_width + v.shape[1]
    ones = head_ones(qk_width)
    meet(("ctx",))
    out_copies = sum_start(part, bufs, out_sems)
    loads = [
        load(source, target, local.at[item])
        for item, (source, target) in enumerate(zip(sources, targets))
    ]
    for copy in loads[:6]:
        copy.wait()
    for block in range(blocks):
        do[block * HALF : (block + 1) * HALF, :] = dot(
            grad_all[place[block]], weights_in[:, qkv_width:], 1, 0
        ).astype(BF16)
    for block in range(blocks):
        turned[:, block * HALF : (block + 1) * HALF] = grad_all[block].T
    for first in range(0, D, 512):
        rows = slice(first, first + 512)
        out_grad[rows, :] = dot(turned[rows, :], o[...], 1, 0).astype(BF16)
    dkv[...] = jnp.zeros_like(dkv)
    for block in range(blocks):
        if block == blocks // 2:
            sum_pass(out_copies, part, bufs, out_sems)
        rows = slice(block * HALF, (block + 1) * HALF)
        keys = (block + 1) * HALF
        mask = block_mask(starts, block, keys)
        pieces = []
        dk_add = []
        dv_add = []
        for group in range(groups):
            lanes = slice(group * HD, (group + 1) * HD)
            queries = stack_heads(q, rows, group)
            outs = stack_heads(do, rows, group)
            key_rows = k[:keys, lanes]
            scores = dot(key_rows, queries, 1, 1) * SCALE
            weights = jnp.where(
                mask, jnp.exp(scores - lse[block, group : group + 1, :]), 0.0
            )
            back = dot(v[:keys, lanes], outs, 1, 1)
            delta = jnp.sum(weights * back, axis=0, keepdims=True)
            grads = (weights * (back - delta)).astype(BF16)
            pieces += unstack_heads(dot(key_rows, grads, 0, 0) * SCALE)
            dk_add.append(dot(grads, queries, 1, 0) * SCALE)
            dv_add.append(dot(weights.astype(BF16), outs, 1, 0))
        dq[block] = jnp.concatenate(pieces, axis=1)
        dkv[: block + 1] += jnp.concatenate(dk_add + dv_add, axis=1).reshape(
            (block + 1,) + dkv.shape[1:]
        )
    gain_row = jnp.zeros((1, qk_width), F32)
    for copy in loads[6:]:
        copy.wait()
    for block in range(blocks):
        here = order[block]
        values = qk[here]
        root = lax.rsqrt(head_mean(values * values, ones) + NORM_EPS)
        unit = values * root
        grad_kv = dkv[here]
        kv_width = grad_kv.shape[1] // 2
        grad = jnp.concatenate([dq[here], grad_kv[:, :kv_width]], axis=1)
        cosine, sine = widen(table[here], qk_width)
        grad = grad * cosine - partner(grad) * sine
        gain_row = gain_row + jnp.sum(grad * unit, axis=0, keepdims=True)
        grad = grad * gain[...]
        grad = root * (grad - unit * head_mean(grad * unit, ones))
        joined[block * HALF : (block + 1) * HALF, :] = jnp.concatenate(
            [grad, grad_kv[:, kv_width:]], axis=1
        ).astype(BF16)
    gain_grad[...] = gain_row
    read = sum_rest(out_copies, part, bufs)
    half = middle.shape[0] // 2
    for first in (0, half):
        rows = pl.ds(first, half)
        out[rows, :] = (middle[rows, :] + read(first)).astype(BF16)


def tail_kernel(
    swaps,
    joined,
    out_grad,
    gain_row,
    attn_gain,
    ffn_gain_grad,
    *refs,
):
    sources, refs = refs[:4], refs[4:]
    swap_in, refs = refs[:swaps], refs[swaps:]
    grad_tokens, gains, attn_own = refs[:3]
    swap_out, refs = refs[3 : 3 + swaps], refs[3 + swaps :]
    targets, refs = refs[:4], refs[4:]
    weights_in, normed, x, grad_middle = targets
    back_bufs, refs = refs[:-15], refs[-15:]
    turned, part, attn_grad, home, travel, owned, ctx_box, fsdp_box = refs[:8]
    send_two, recv_two, send_three, recv_three, send_four, recv_four, local = refs[8:]
    going, coming = travel.at[0], travel.at[1]
    back_sems = (send_two, recv_two)
    line, small = (send_three, recv_three), (send_four, recv_four)
    size = lax.axis_size("ctx")
    me = lax.axis_index("ctx")
    chips = lax.axis_size("fsdp") // 2
    step_base = chips
    swap_base = step_base + 2 * chips
    qkv_width = joined.shape[1]
    qk_width = gain_row.shape[1]
    half = x.shape[0] // 2
    loads = [
        load(source, target, local.at[item])
        for item, (source, target) in enumerate(zip(sources, targets))
    ]
    meet(("ctx", "fsdp"))
    swap_copies = []
    own_copies = []
    for item in range(swaps):
        swap_copies += swap_start(
            swap_in[item], swap_out[item], line, swap_base + (item + 1) * size
        )
        own_copies.append(
            load(swap_in[item].at[me], swap_out[item].at[me], local.at[4 + item])
        )
    for copy in loads:
        copy.wait()
    for first in range(0, D, 512):
        part[:, first : first + 512] = dot(
            joined[...], weights_in[first : first + 512, :qkv_width], 1, 1
        ).astype(BF16)
    back_copies = sum_start(part, back_bufs, back_sems)
    turn(normed, turned)
    for first in range(0, D, 512):
        rows = slice(first, first + 512)
        attn_grad[rows, :qkv_width] = dot(turned[rows, :], joined[...], 1, 0).astype(BF16)
    attn_grad[:, qkv_width:] = out_grad[...]
    home_copies = line_start(attn_grad, home, line, 0)
    line_home(home_copies, attn_grad, home)
    line_step(chips - 1, home, going, coming, line, step_base)
    sum_pass(back_copies, part, back_bufs, back_sems)
    for reach in range(chips - 2, 1, -1):
        line_step(reach, home, going, coming, line, step_base)
    read = sum_rest(back_copies, part, back_bufs)
    total = jnp.zeros((1, D), F32)
    for first in (0, half):
        rows = pl.ds(first, half)
        values = x[rows, :].astype(F32)
        root = row_scale(values)
        unit = values * root
        back = read(first)
        total = total + jnp.sum(back * unit, axis=0, keepdims=True)
        back = back * attn_gain[...]
        back = root * (back - unit * jnp.mean(back * unit, axis=-1, keepdims=True))
        grad_tokens[rows, :] = grad_middle[rows, :] + back

    def spread_start(axis, box, value, base):
        index = lax.axis_index(axis)
        axis_size = lax.axis_size(axis)
        box[index] = value
        return [
            send(
                box.at[index],
                box.at[index],
                small,
                base + step,
                {axis: lax.rem(index + step, axis_size)},
            )
            for step in range(1, axis_size)
        ]

    def spread_end(copies, box):
        for copy in copies:
            copy.wait()
        summed = box[0]
        for item in range(1, box.shape[0]):
            summed = summed + box[item]
        return summed

    ctx_copies = spread_start(
        "ctx",
        ctx_box,
        jnp.concatenate(
            [
                total,
                ffn_gain_grad[...],
                jnp.concatenate([gain_row[...], jnp.zeros((1, D - qk_width), F32)], axis=1),
                jnp.zeros((5, D), F32),
            ],
            axis=0,
        ),
        0,
    )
    line_step(1, home, going, coming, line, step_base)
    fsdp_copies = spread_start("fsdp", fsdp_box, spread_end(ctx_copies, ctx_box), size)
    line_end(home_copies, home, going, coming, line, step_base)
    chip = lax.axis_index("fsdp") // 2
    owned_rows = owned.shape[1]
    for index in range(size):
        owned[index] = home[chip, index * owned_rows : (index + 1) * owned_rows, :]
    swap_copies += swap_start(owned, attn_own, line, swap_base)
    attn_own[me] = owned[me]
    gains[...] = spread_end(fsdp_copies, fsdp_box)
    for copy in swap_copies:
        copy.wait()
    for copy in own_copies:
        copy.wait()


def rms_scale(values_in, gain_vec):
    return (
        values_in
        * lax.rsqrt(jnp.mean(values_in * values_in, axis=-1, keepdims=True) + NORM_EPS)
        * gain_vec
    )


def inverse_freq():
    return 1.0 / ROPE_BASE ** (jnp.arange(0, HD, 2).astype(F32) / HD)


def shards(
    tokens,
    cotangent,
    doc_starts,
    block_order,
    master_weights,
    moment_one,
    moment_two,
    gains,
    gains_moment_one,
    gains_moment_two,
):
    nctx = lax.axis_size("ctx")
    nfsdp = lax.axis_size("fsdp")
    own_rows = master_weights.shape[0]
    tok_rows = tokens.shape[1]
    stream_len = tok_rows * nctx
    blocks = stream_len // HALF
    groups = KVHEADS // nctx
    q_width = D // nctx
    kv_width = KVD // nctx
    qk_width = q_width + kv_width
    qkv_width = qk_width + kv_width
    tiles = FF // 128
    ff_tiles = -(-tiles // nctx)
    ff_width = ff_tiles * 128
    bundles = 2
    cuts = [0, (ff_tiles * 5 + 3) // 7 * 128, ff_width]

    low = master_weights.astype(BF16)

    def ff_part(base, index, start, stop):
        first = index * ff_width + start
        last = index * ff_width + stop
        real_first, real_last = min(first, FF), min(last, FF)
        part = low[:, base + real_first : base + real_last]
        if real_last - real_first < last - first:
            part = jnp.pad(part, ((0, 0), (0, (last - first) - (real_last - real_first))))
        return part

    def attn_part(index):
        return jnp.concatenate(
            [
                low[:, index * q_width : (index + 1) * q_width],
                low[:, D + index * kv_width : D + (index + 1) * kv_width],
                low[:, D + KVD + index * kv_width : D + KVD + (index + 1) * kv_width],
                low[:, QKVC + index * q_width : QKVC + (index + 1) * q_width],
            ],
            axis=1,
        )

    gate_base = QKVC + D
    bases = (gate_base, gate_base + FF, gate_base + 2 * FF)
    attn_send = jnp.stack([attn_part(c) for c in range(nctx)])
    ff_send = [
        jnp.stack(
            [
                jnp.concatenate(
                    [ff_part(base, c, cuts[b], cuts[b + 1]) for base in bases], axis=1
                )
                for c in range(nctx)
            ]
        )
        for b in range(bundles)
    ]

    def gather_rows(piece):
        return lax.all_gather(
            piece.reshape(nctx * own_rows, piece.shape[-1]), "fsdp", axis=0, tiled=True
        )

    def spread(active):
        return (
            active.reshape(active.shape[0], nctx, nfsdp, own_rows)
            .transpose(0, 2, 1, 3)
            .reshape(active.shape[0], D)
        )

    def unspread(active):
        return (
            active.reshape(active.shape[0], nfsdp, nctx, own_rows)
            .transpose(0, 2, 1, 3)
            .reshape(active.shape[0], D)
        )

    dma = pltpu.SemaphoreType.DMA
    all_low = jax.ShapeDtypeStruct((nctx, tok_rows, D), BF16)
    own_low = jax.ShapeDtypeStruct((tok_rows, D), BF16)
    own_f32 = jax.ShapeDtypeStruct((tok_rows, D), F32)
    row_f32 = jax.ShapeDtypeStruct((1, D), F32)
    g_attn = spread(gains[None, :D])
    g_ffn = spread(gains[None, D : 2 * D])
    order = block_order.reshape(blocks)
    place = jnp.argsort(order).astype(jnp.int32)
    starts = doc_starts[0]

    (attn_held,) = exchange(("swap",), [attn_send], 0, 10)
    w_attn = gather_rows(attn_held)
    first_send, attn_held = lax.optimization_barrier((ff_send[0], attn_held))
    (first_held,) = exchange(("swap",), [first_send], 1, 16)
    table_shape = jax.ShapeDtypeStruct((stream_len, 2 * HD), F32)
    origin = spread(jnp.arange(D, dtype=jnp.int32)[None])
    starts_late, first_held = lax.optimization_barrier((starts, first_held))
    x_low, dy_low, table, normed_all = remote_call(
        first_kernel,
        [own_low, own_low, table_shape, all_low],
        (
            starts_late,
            origin,
            tokens[0],
            cotangent[0],
            g_attn,
            jnp.tile(inverse_freq(), 4)[None],
        ),
        2,
        33,
        [
            pltpu.VMEM((D, D), BF16),
            pltpu.VMEM((tok_rows, D), BF16),
            dma((GATHER_SEMS,)),
            dma((GATHER_SEMS,)),
            dma,
        ],
        (3,),
        1,
    )
    normed_all = normed_all.reshape(stream_len, D)

    g_query = gains[2 * D : 2 * D + HD]
    g_key = gains[2 * D + HD :]
    qk_gain = jnp.concatenate(
        [jnp.tile(g_query, q_width // HD), jnp.tile(g_key, kv_width // HD)]
    )[None]

    low_stream = pltpu.VMEM((stream_len, D), BF16)
    heads_low = pltpu.VMEM((stream_len, q_width), BF16)
    part, qk, q, k, v, mixed, lse, dy_all, second_held = remote_call(
        functools.partial(attend_kernel, blocks, groups),
        [
            jax.ShapeDtypeStruct((stream_len, D), BF16),
            jax.ShapeDtypeStruct((stream_len, qk_width), F32),
            jax.ShapeDtypeStruct((stream_len, q_width), BF16),
            jax.ShapeDtypeStruct((stream_len, kv_width), BF16),
            jax.ShapeDtypeStruct((stream_len, kv_width), BF16),
            jax.ShapeDtypeStruct((stream_len, q_width), BF16),
            jax.ShapeDtypeStruct((blocks, groups, GROUP * HALF), F32),
            all_low,
            jax.ShapeDtypeStruct(ff_send[1].shape, BF16),
        ],
        (place, order, starts, table, qk_gain, normed_all, w_attn, dy_low, ff_send[1]),
        3,
        42,
        [
            low_stream,
            pltpu.VMEM(w_attn.shape, BF16),
            pltpu.VMEM((blocks, HALF, qkv_width), F32),
            pltpu.VMEM((blocks, HALF, q_width), BF16),
            dma((GATHER_SEMS + nctx,)),
            dma((GATHER_SEMS + nctx,)),
            dma((4,)),
        ],
        (7, 8),
        3,
        4,
    )
    dy_all = dy_all.reshape(stream_len, D)
    w_ff = [gather_rows(first_held), gather_rows(second_held)]
    sum_bufs = sum_scratch(nctx, tok_rows)
    sum_sems = [dma((GATHER_SEMS,)), dma((GATHER_SEMS,))]
    norm_scratch = (
        sum_bufs + [pltpu.VMEM((tok_rows, D), BF16)] + sum_sems + sum_sems + [dma]
    )

    middle, normed_two_all = remote_call(
        middle_kernel,
        [own_f32, all_low],
        (part, x_low, g_ffn),
        4,
        57,
        norm_scratch,
        (1,),
    )
    normed_two_all = normed_two_all.reshape(stream_len, D)

    def sum_rows(grad):
        return lax.psum_scatter(grad, "fsdp", scatter_dimension=0, tiled=True).reshape(
            nctx, own_rows, grad.shape[-1]
        )

    def feed(b, x_all, dy):
        width = cuts[b + 1] - cuts[b]
        w_gu, w_down = w_ff[b][:, : 2 * width], w_ff[b][:, 2 * width :]
        gate_up = dot(x_all, w_gu, 1, 0).astype(BF16)
        gate, up = gate_up[:, :width].astype(F32), gate_up[:, width:].astype(F32)
        gated = jax.nn.sigmoid(gate)
        act = gate * gated
        hidden = (act * up).astype(BF16)
        back_hidden = dot(dy, w_down, 1, 0)
        grad_gu = jnp.concatenate(
            [back_hidden * up * (gated + act * (1.0 - gated)), back_hidden * act], axis=1
        ).astype(BF16)
        return hidden, grad_gu

    width_two = cuts[2] - cuts[1]
    width_line = cuts[1] * 3 // 5 // 128 * 128
    width_rest = cuts[1] - width_line
    chips = nfsdp // 2

    def line_scratch(columns):
        block = (nctx * own_rows, columns)
        return [pltpu.VMEM((chips,) + block, BF16), pltpu.VMEM((2, 2, chips - 1) + block, BF16)]

    line_sems = dma((3 * chips,))
    hidden_one, grad_gu = feed(0, normed_two_all, dy_all)
    down_grad = dot(dy_all, hidden_one[:, :width_line], 0, 0).astype(BF16)
    down_sum, gu_grad, back_partial = remote_call(
        feed_back_kernel,
        [
            jax.ShapeDtypeStruct((nctx, own_rows, width_line), BF16),
            jax.ShapeDtypeStruct((D, 2 * cuts[1]), BF16),
            jax.ShapeDtypeStruct((stream_len, D), BF16),
        ],
        (down_grad, normed_two_all, grad_gu, w_ff[0]),
        8,
        30,
        [
            low_stream,
            pltpu.VMEM((stream_len, 2 * cuts[1]), BF16),
            pltpu.VMEM((D, 2 * cuts[1]), BF16),
            pltpu.VMEM((D, stream_len), BF16),
            pltpu.VMEM((D, 2 * cuts[1]), BF16),
            low_stream,
        ]
        + line_scratch(width_line)
        + [line_sems, line_sems, dma((5,))],
        (1, 2),
        0,
        3,
    )
    gu_grad, back_partial, w_ff[1] = lax.optimization_barrier((gu_grad, back_partial, w_ff[1]))
    hidden_two, grad_gu = feed(1, normed_two_all, dy_all)
    back_more = dot(grad_gu, w_ff[1][:, : 2 * width_two], 1, 1)
    back_partial = (back_partial.astype(F32) + back_more).astype(BF16)
    gu_sum = sum_rows(gu_grad)

    grad_middle, grad_g_ffn, rest_sum, grad_middle_all, last_grad, out_partial = remote_call(
        middle_back_kernel,
        [
            own_f32,
            row_f32,
            jax.ShapeDtypeStruct((nctx, own_rows, width_rest), BF16),
            all_low,
            jax.ShapeDtypeStruct((D, 3 * width_two), BF16),
            jax.ShapeDtypeStruct((stream_len, D), BF16),
        ],
        (
            back_partial,
            middle,
            dy_low,
            g_ffn,
            normed_two_all,
            dy_all,
            hidden_one,
            hidden_two,
            grad_gu,
            w_ff[0],
            w_ff[1],
        ),
        5,
        57,
        sum_bufs
        + [
            pltpu.VMEM((tok_rows, D), BF16),
            low_stream,
            pltpu.VMEM((stream_len, 2 * width_two), BF16),
            pltpu.VMEM((D, stream_len), BF16),
            pltpu.VMEM((D, 3 * width_two), BF16),
            pltpu.VMEM((D, width_rest), BF16),
            low_stream,
            pltpu.VMEM((stream_len, cuts[1]), BF16),
            pltpu.VMEM((stream_len, width_two), BF16),
            pltpu.VMEM((D, cuts[1]), BF16),
            pltpu.VMEM((D, width_two), BF16),
        ]
        + line_scratch(width_rest)
        + sum_sems
        + sum_sems
        + [dma((3 * chips,)), dma((3 * chips,)), dma((10,))],
        (3, 4, 5),
        0,
        7,
    )
    last_sum = sum_rows(last_grad)

    small = dma((nctx + nfsdp,))
    line_sems = dma((3 * chips + 4 * nctx,))
    own_shape = (nctx, own_rows, qkv_width + q_width)
    sources = (
        grad_middle_all.reshape(blocks, HALF, D),
        w_attn,
        q,
        k,
        v,
        mixed,
        qk.reshape(blocks, HALF, qk_width),
        table.reshape(blocks, HALF, 2 * HD),
        middle,
    )
    out_tokens, grad_joined, qk_gain_grad, out_grad = remote_call(
        functools.partial(attend_back_kernel, blocks, groups),
        [
            own_low,
            jax.ShapeDtypeStruct((stream_len, qkv_width), BF16),
            jax.ShapeDtypeStruct((1, qk_width), F32),
            jax.ShapeDtypeStruct((D, q_width), BF16),
        ],
        (place, order, starts, lse, qk_gain, out_partial) + sources,
        6,
        45,
        [pltpu.VMEM(source.shape, source.dtype) for source in sources]
        + sum_bufs
        + [
            heads_low,
            pltpu.VMEM((blocks, HALF, q_width), F32),
            pltpu.VMEM((blocks, HALF, 2 * kv_width), F32),
            pltpu.VMEM((D, stream_len), BF16),
        ]
        + sum_sems
        + [dma((9,))],
        (),
        3,
        9,
    )
    sources = (w_attn, normed_all, x_low, grad_middle)
    grad_tokens, gain_sums, attn_own, gu_own, down_own, rest_own = remote_call(
        functools.partial(tail_kernel, 3),
        [
            own_f32,
            jax.ShapeDtypeStruct((8, D), F32),
            jax.ShapeDtypeStruct(own_shape, BF16),
            jax.ShapeDtypeStruct(gu_sum.shape, BF16),
            jax.ShapeDtypeStruct(down_sum.shape, BF16),
            jax.ShapeDtypeStruct(rest_sum.shape, BF16),
        ],
        (grad_joined, out_grad, qk_gain_grad, g_attn, grad_g_ffn) + sources + (gu_sum, down_sum, rest_sum),
        7,
        75,
        [pltpu.VMEM(source.shape, source.dtype) for source in sources]
        + sum_bufs
        + [
            pltpu.VMEM((D, stream_len), BF16),
            low_stream,
            pltpu.VMEM((D, qkv_width + q_width), BF16),
        ]
        + line_scratch(qkv_width + q_width)
        + [
            pltpu.VMEM(own_shape, BF16),
            pltpu.VMEM((nctx, 8, D), F32),
            pltpu.VMEM((nfsdp, 8, D), F32),
        ]
        + sum_sems
        + [line_sems, line_sems, small, small, dma((7,))],
        (3, 4, 5),
        0,
        7,
    )
    last_sum, gain_sums, gu_own = lax.optimization_barrier((last_sum, gain_sums, gu_own))
    out_tokens = unspread(out_tokens)[None]
    grad_tokens = unspread(grad_tokens)[None]
    gain_grad = jnp.concatenate(
        [
            unspread(gain_sums[:1])[0],
            unspread(gain_sums[1:2])[0],
            jnp.sum(gain_sums[2, :q_width].reshape(-1, HD), axis=0),
            jnp.sum(gain_sums[2, q_width:qk_width].reshape(-1, HD), axis=0),
        ]
    )

    olds = (master_weights, moment_one, moment_two)

    def feed_segments(b, pieces, start, stop):
        found = []
        for part in pieces:
            for c in range(nctx):
                column = c * ff_width + cuts[b] + start
                real = min(max(FF - column, 0), stop - start)
                if real:
                    piece, first = pieces[part]
                    found.append((piece, c, first, bases[part] + column, real))
        return found

    width_one = cuts[1]
    last_own = [
        lax.ppermute(
            lax.dynamic_index_in_dim(last_sum, lax.axis_index("ctx") ^ k, 0, keepdims=False),
            "ctx",
            [(c, c ^ k) for c in range(nctx)],
        )
        if k
        else lax.dynamic_index_in_dim(last_sum, lax.axis_index("ctx"), 0, keepdims=False)
        for k in range(nctx)
    ]
    parts = (
        (0, 0, q_width),
        (q_width, D, kv_width),
        (qk_width, D + KVD, kv_width),
        (qkv_width, QKVC, q_width),
    )
    if kv_width % 128:
        attn_own = jnp.concatenate(
            [attn_own[c, :, f : f + w] for f, _, w in parts for c in range(nctx)], axis=1
        )[None]
        segments = [(0, 0, 0, 0, gate_base)]
    else:
        segments = [
            (0, c, first, base + c * width, width)
            for first, base, width in parts
            for c in range(nctx)
        ]
    news = adam(
        segments
        + feed_segments(0, {0: (1, 0), 1: (1, width_one)}, 0, width_one)
        + feed_segments(0, {2: (2, 0)}, 0, width_line)
        + feed_segments(0, {2: (3, 0)}, width_line, width_one),
        [attn_own, gu_own, down_own, rest_own],
        olds,
        None,
        10,
    )
    first_new, second_new, master_new, low_new = adam(
        feed_segments(
            1, {0: (None, 0), 1: (None, width_two), 2: (None, 2 * width_two)}, 0, width_two
        ),
        last_own,
        olds,
        news,
        6,
    )
    gain_first, gain_second, gain_new = adam_update(
        gains, gain_grad, gains_moment_one, gains_moment_two, GAIN_RATE, 0.0
    )
    return (
        out_tokens,
        grad_tokens,
        first_new,
        second_new,
        master_new,
        low_new,
        gain_first,
        gain_second,
        gain_new,
    )


def solution(mesh):
    rows = P("fsdp", "ctx", None)
    weights = P(("ctx", "fsdp"), None)
    return jax.shard_map(
        shards,
        mesh=mesh,
        in_specs=(rows, rows, P("fsdp", None), P(), weights, weights, weights, P(), P(), P()),
        out_specs=(rows, rows, weights, weights, weights, weights, P(), P(), P()),
        check_vma=False,
    )
```

```python
import functools

import jax
import jax.numpy as jnp
from jax import lax
from jax.experimental import pallas as pl
from jax.experimental.pallas import tpu as pltpu
from jax.sharding import PartitionSpec as P

D = 1536
HEADS = 24
KVHEADS = 8
HD = 64
FF = 6912
STEP = 10
HALF = 128
KVD = 512
QKVC = 2560
GROUP = HEADS // KVHEADS

ROPE_BASE = 1000000.0
NORM_EPS = 1e-05
BETA_ONE = 0.9
BETA_TWO = 0.95
ADAM_EPS = 1e-08
WEIGHT_DECAY = 0.1
LEARN_RATE = 0.03
GAIN_RATE = 0.5
SCALE = HD ** (-0.5)
MESH = pl.DeviceIdType.MESH
F32 = jnp.float32
BF16 = jnp.bfloat16
VMEM_LIMIT = 61 * 1024 * 1024


def dot(left, right, left_dim, right_dim):
    return lax.dot_general(
        left, right, (((left_dim,), (right_dim,)), ((), ())), preferred_element_type=F32
    )


def send(source, target, sems, item, peer):
    copy = pltpu.make_async_remote_copy(
        src_ref=source,
        dst_ref=target,
        send_sem=sems[0].at[item],
        recv_sem=sems[1].at[item],
        device_id=peer,
        device_id_type=MESH,
    )
    copy.start()
    return copy


def meet(axes):
    barrier = pltpu.get_barrier_semaphore()
    total = 0
    for axis in axes:
        size = lax.axis_size(axis)
        me = lax.axis_index(axis)
        for step in range(1, size):
            pl.semaphore_signal(
                barrier,
                inc=1,
                device_id={axis: lax.rem(me + step, size)},
                device_id_type=MESH,
            )
        total += size - 1
    pl.semaphore_wait(barrier, total)


def square():
    me = lax.axis_index("ctx")
    return me, me + 1 - 2 * lax.rem(me, 2), lax.rem(me + 2, 4), 3 - me


def swap_start(source, target, sems, base):
    size = lax.axis_size("ctx")
    me = lax.axis_index("ctx")
    copies = []
    for step in range(1, size):
        peer = lax.rem(me + step, size)
        copies.append(
            send(source.at[peer], target.at[me], sems, base + step, {"ctx": peer})
        )
    return copies


def gather_start(source, target, sems, base):
    size = lax.axis_size("ctx")
    me = lax.axis_index("ctx")
    if size != 4:
        return [
            send(
                source,
                target.at[me],
                sems,
                base + step,
                {"ctx": lax.rem(me + step, size)},
            )
            for step in range(1, size)
        ]
    me, side, over, across = square()
    half = source.shape[0] // 2
    top, low = pl.ds(0, half), pl.ds(half, half)
    return [
        send(source.at[top], target.at[me, top], sems, base, {"ctx": side}),
        send(source.at[low], target.at[me, low], sems, base + 1, {"ctx": over}),
        send(source.at[low], target.at[me, low], sems, base + 2, {"ctx": side}),
        send(source.at[top], target.at[me, top], sems, base + 3, {"ctx": over}),
    ]


def gather_pass(copies, target, sems, base):
    if lax.axis_size("ctx") != 4:
        return
    me, side, over, across = square()
    half = target.shape[1] // 2
    top, low = pl.ds(0, half), pl.ds(half, half)
    copies[0].wait_recv()
    copies.append(send(target.at[side, top], target.at[side, top], sems, base + 4, {"ctx": over}))
    copies[1].wait_recv()
    copies.append(send(target.at[over, low], target.at[over, low], sems, base + 5, {"ctx": side}))


def gather_end(copies):
    if lax.axis_size("ctx") != 4:
        for copy in copies:
            copy.wait()
        return
    for copy in copies:
        copy.wait_send()
    for copy in copies[2:]:
        copy.wait_recv()


def gather_rest(copies, target, sems, base):
    gather_pass(copies, target, sems, base)
    gather_end(copies)


def load(source, target, sem):
    copy = pltpu.make_async_copy(source, target, sem)
    copy.start()
    return copy


GATHER_SEMS = 8


def exchange_kernel(kinds, *refs):
    count = len(kinds)
    ins, outs = refs[:count], refs[count : 2 * count]
    send_sem, recv_sem, local_sem = refs[2 * count :]
    sems = (send_sem, recv_sem)
    me = lax.axis_index("ctx")
    meet(("ctx",))
    copies = []
    own = []
    for item in range(count):
        base = item * GATHER_SEMS
        if kinds[item] == "gather":
            copies.append(gather_start(ins[item], outs[item], sems, base))
            source = ins[item]
        else:
            copies.append(swap_start(ins[item], outs[item], sems, base))
            source = ins[item].at[me]
        copy = pltpu.make_async_copy(source, outs[item].at[me], local_sem.at[item])
        copy.start()
        own.append(copy)
    for item in range(count):
        if kinds[item] == "gather":
            gather_rest(copies[item], outs[item], sems, item * GATHER_SEMS)
        else:
            for copy in copies[item]:
                copy.wait()
    for copy in own:
        copy.wait()


def remote_params(collective_id):
    return pltpu.CompilerParams(
        collective_id=collective_id, has_side_effects=True, vmem_limit_bytes=VMEM_LIMIT
    )


def cost(micros):
    return pl.CostEstimate(flops=0, bytes_accessed=int(micros * 3.0e6), transcendentals=0)


def exchange(kinds, arrays, collective_id, micros):
    size = lax.axis_size("ctx")
    shapes = [
        jax.ShapeDtypeStruct((size,) + a.shape if kind == "gather" else a.shape, a.dtype)
        for kind, a in zip(kinds, arrays)
    ]
    sems = pltpu.SemaphoreType.DMA((len(arrays) * GATHER_SEMS,))
    return pl.pallas_call(
        functools.partial(exchange_kernel, kinds),
        out_shape=shapes,
        in_specs=[pl.BlockSpec(memory_space=pl.ANY)] * len(arrays),
        out_specs=[pl.BlockSpec(memory_space=pl.ANY)] * len(arrays),
        scratch_shapes=[sems, sems, pltpu.SemaphoreType.DMA((len(arrays),))],
        compiler_params=remote_params(collective_id),
        cost_estimate=cost(micros),
    )(*arrays)


def sum_scratch(size, rows):
    if size == 4:
        half = pltpu.VMEM((2, rows // 2, D), BF16)
        return [half, half, pltpu.VMEM((2, rows, D), BF16)]
    return [pltpu.VMEM((size - 1, rows, D), BF16)]


def sum_start(part, bufs, sems):
    size = lax.axis_size("ctx")
    me = lax.axis_index("ctx")
    rows = part.shape[0] // size

    def block(owner, first=0, count=rows):
        return pl.ds(pl.multiple_of(owner * rows + first, rows // 2), count)

    if size != 4:
        copies = []
        for step in range(1, size):
            peer = lax.rem(me + step, size)
            copies.append(
                send(part.at[block(peer)], bufs[0].at[step - 1], sems, step, {"ctx": peer})
            )
        return copies
    me, side, over, across = square()
    half = rows // 2
    relay, _, landed = bufs
    return [
        send(part.at[block(across, 0, half)], relay.at[0], sems, 0, {"ctx": side}),
        send(part.at[block(across, half, half)], relay.at[1], sems, 1, {"ctx": over}),
        send(
            part.at[block(side, 0, half)],
            landed.at[0, pl.ds(0, half)],
            sems,
            2,
            {"ctx": side},
        ),
        send(
            part.at[block(over, half, half)],
            landed.at[1, pl.ds(half, half)],
            sems,
            3,
            {"ctx": over},
        ),
    ]


def sum_pass(copies, part, bufs, sems):
    if lax.axis_size("ctx") != 4:
        return
    rows = part.shape[0] // 4
    half = rows // 2

    def rows_of(owner, first):
        return pl.ds(pl.multiple_of(owner * rows + first, half), half)

    me, side, over, across = square()
    relay, passed, landed = bufs
    copies[0].wait_recv()
    passed[0] = (part[rows_of(over, 0), :].astype(F32) + relay[0].astype(F32)).astype(BF16)
    copies.append(
        send(passed.at[0], landed.at[1, pl.ds(0, half)], sems, 4, {"ctx": over})
    )
    copies[1].wait_recv()
    passed[1] = (part[rows_of(side, half), :].astype(F32) + relay[1].astype(F32)).astype(
        BF16
    )
    copies.append(
        send(passed.at[1], landed.at[0, pl.ds(half, half)], sems, 5, {"ctx": side})
    )


def sum_rest(copies, part, bufs):
    size = lax.axis_size("ctx")
    me = lax.axis_index("ctx")
    rows = part.shape[0] // size
    half = rows // 2

    def rows_of(owner, first):
        return pl.ds(pl.multiple_of(owner * rows + first, half), half)

    if size != 4:
        for copy in copies:
            copy.wait()

        def read(first):
            total = part[rows_of(me, first), :].astype(F32)
            for step in range(1, size):
                total = total + bufs[0][step - 1, pl.ds(first, half), :].astype(F32)
            return total

        return read
    relay, passed, landed = bufs
    for copy in copies:
        copy.wait_send()
    for copy in copies[2:]:
        copy.wait_recv()

    def read(first):
        return (
            part[rows_of(me, first), :].astype(F32)
            + landed[0, pl.ds(first, half), :].astype(F32)
            + landed[1, pl.ds(first, half), :].astype(F32)
        )

    return read


def row_scale(values):
    return lax.rsqrt(jnp.mean(values * values, axis=-1, keepdims=True) + NORM_EPS)


def first_kernel(
    starts, origin, x, dy, gain, freq, x_low, dy_low, table, normed_all, *scratch
):
    move, normed, send_one, recv_one, local = scratch
    me = lax.axis_index("ctx")
    row = lax.broadcasted_iota(jnp.int32, move.shape, 0)
    move[...] = jnp.where(row == origin[...], 1.0, 0.0).astype(BF16)
    values = dot(x[...], move[...], 1, 0)
    x_low[...] = values.astype(BF16)
    normed[...] = (values * row_scale(values) * gain[...]).astype(BF16)
    meet(("ctx",))
    sems = (send_one, recv_one)
    copies = gather_start(normed, normed_all, sems, 0)
    own = load(normed, normed_all.at[me], local)
    dy_low[...] = dot(dy[...], move[...], 1, 0).astype(BF16)
    gather_pass(copies, normed_all, sems, 0)
    times = lax.broadcasted_iota(jnp.int32, (table.shape[0], 1), 0)
    angles = (times - doc_first(starts, times)).astype(F32) * freq[...]
    lane = lax.broadcasted_iota(jnp.int32, angles.shape, 1)
    sine = jnp.sin(angles)
    sine = jnp.where(lane % HD < HD // 2, -sine, sine)
    table[...] = jnp.where(lane < HD, jnp.cos(angles), sine)
    gather_end(copies)
    own.wait()


def middle_kernel(part, x, gain, middle, normed_all, *scratch):
    bufs, (normed, send_one, recv_one, send_two, recv_two, local) = scratch[:-6], scratch[-6:]
    me = lax.axis_index("ctx")
    meet(("ctx",))
    copies = sum_start(part, bufs, (send_one, recv_one))
    sum_pass(copies, part, bufs, (send_one, recv_one))
    read = sum_rest(copies, part, bufs)
    half = x.shape[0] // 2
    for first in (0, half):
        rows = pl.ds(first, half)
        values = x[rows, :].astype(F32) + read(first)
        middle[rows, :] = values
        normed[rows, :] = (values * row_scale(values) * gain[...]).astype(BF16)
    sems = (send_two, recv_two)
    copies = gather_start(normed, normed_all, sems, 0)
    own = load(normed, normed_all.at[me], local)
    gather_rest(copies, normed_all, sems, 0)
    own.wait()


def column_tiles(total, body):
    def step(tile, carry):
        body(pl.multiple_of(tile * 256, 256), 256)
        return carry

    lax.fori_loop(0, total // 256, step, 0)
    if total % 256:
        body(total - total % 256, total % 256)


def turn(source, target):
    for first in range(0, source.shape[0], HALF):
        rows = slice(first, first + HALF)
        target[:, rows] = source[rows, :].T


def middle_back_kernel(
    middle,
    dy,
    gain,
    back,
    x_all,
    dy_all,
    hidden_one,
    w_one,
    w_two,
    grad,
    gain_grad,
    down_sum,
    grad_all,
    rest_grad,
    weight_grad,
    out,
    *scratch,
):
    bufs = scratch[:-21]
    low, part, x_buf, gu_buf, turned, weight_buf, down_grad, out_buf = scratch[-21:-13]
    hidden_bufs, (down_buf, second) = scratch[-13:-11], scratch[-11:-9]
    home, coming, send_one, recv_one, send_two, recv_two, send_three, recv_three, local = (
        scratch[-9:]
    )
    me = lax.axis_index("ctx")
    chips = lax.axis_size("fsdp") // 2
    line = (send_three, recv_three)
    meet(("ctx", "fsdp"))
    width_one, width_two = hidden_one.shape[1], hidden_bufs[1].shape[1]
    gu_width = 2 * width_two
    loads = [
        load(source, target, local.at[item])
        for item, (source, target) in enumerate(
            (
                (x_all, x_buf),
                (w_two, second),
                (dy_all, out_buf),
                (back, part),
                (hidden_one, hidden_bufs[0]),
            )
        )
    ]
    w_down = w_one.at[:, pl.ds(2 * width_one, width_one)]
    if down_buf.shape[1] < width_one:
        down_buf = turned.at[:, pl.ds(0, width_one)]
    else:
        loads.append(load(w_down, down_buf, local.at[5]))
    for copy in loads[:3]:
        copy.wait()

    def feed_tile(first, width):
        gate = dot(x_buf[...], second[:, pl.ds(first, width)], 1, 0)
        up = dot(x_buf[...], second[:, pl.ds(width_two + first, width)], 1, 0)
        back_hidden = dot(out_buf[...], second[:, pl.ds(gu_width + first, width)], 1, 0)
        gated = 1.0 / (1.0 + jnp.exp(-gate))
        act = gate * gated
        hidden_bufs[1][:, pl.ds(first, width)] = (act * up).astype(BF16)
        gu_buf[:, pl.ds(first, width)] = (
            back_hidden * up * (gated + act * (1.0 - gated))
        ).astype(BF16)
        gu_buf[:, pl.ds(width_two + first, width)] = (back_hidden * act).astype(BF16)

    column_tiles(width_two, feed_tile)
    loads[3].wait()

    def back_tile(first, width):
        columns = pl.ds(first, width)
        part[:, columns] = (
            part[:, columns].astype(F32) + dot(gu_buf[...], second[columns, :gu_width], 1, 1)
        ).astype(BF16)

    column_tiles(D, back_tile)
    copies = sum_start(part, bufs, (send_one, recv_one))
    turn(out_buf, turned)
    loads[4].wait()

    def product(target, column, right, begin=0, count=None):
        def tile(first, width):
            target[:, pl.ds(column + first, width)] = dot(
                turned[...], right[:, pl.ds(begin + first, width)], 1, 0
            ).astype(BF16)

        column_tiles(right.shape[1] if count is None else count, tile)

    width_line = down_grad.shape[1]
    product(down_grad, 0, hidden_bufs[0], 0, width_line)
    home_copies = line_start(down_grad, home, line, 0)
    product(weight_buf, 0, hidden_bufs[0], width_line, width_one - width_line)
    rest_store = load(weight_buf.at[:, pl.ds(0, width_one - width_line)], rest_grad, local.at[10])
    sum_pass(copies, part, bufs, (send_one, recv_one))
    line_home(home_copies, down_grad, home)
    line_step(chips - 1, home, coming, line, chips)
    product(weight_buf, gu_width, hidden_bufs[1])
    turn(x_buf, turned)
    rest_store.wait()
    product(weight_buf, 0, gu_buf)
    stores = [load(weight_buf, weight_grad, local.at[7])]
    if len(loads) < 6:
        loads.append(load(w_down, down_buf, local.at[5]))
    if chips > 2:
        line_step(chips - 2, home, coming, line, chips)
    read = sum_rest(copies, part, bufs)
    half = dy.shape[0] // 2
    total = jnp.zeros((1, D), F32)
    for first in (0, half):
        rows = pl.ds(first, half)
        values = middle[rows, :]
        root = row_scale(values)
        unit = values * root
        back = read(first)
        total = total + jnp.sum(back * unit, axis=0, keepdims=True)
        back = back * gain[...]
        back = root * (back - unit * jnp.mean(back * unit, axis=-1, keepdims=True))
        back = back + dy[rows, :].astype(F32)
        grad[rows, :] = back
        low[rows, :] = back.astype(BF16)
    gain_grad[...] = total
    sems = (send_two, recv_two)
    copies = gather_start(low, grad_all, sems, 0)
    stores.append(load(low, grad_all.at[me], local.at[8]))
    loads[5].wait()

    def out_tile(first, width):
        columns = pl.ds(first, width)
        out_buf[:, columns] = (
            dot(hidden_bufs[0][...], down_buf[columns, :], 1, 1)
            + dot(hidden_bufs[1][...], second[columns, gu_width:], 1, 1)
        ).astype(BF16)

    column_tiles(D, out_tile)
    stores.append(load(out_buf, out, local.at[9]))
    gather_pass(copies, grad_all, sems, 0)
    for reach in range(min(chips - 1, max(chips - 3, 1)), 0, -1):
        line_step(reach, home, coming, line, chips)
    line_end(home_copies, home, coming, line, chips)
    chip = lax.axis_index("fsdp") // 2
    rows = down_sum.shape[1]
    for index in range(down_sum.shape[0]):
        down_sum[index] = home[chip, index * rows : (index + 1) * rows, :]
    gather_end(copies)
    for copy in stores:
        copy.wait()


def line_start(grad, home, sems, base):
    me = lax.axis_index("fsdp")
    chips = lax.axis_size("fsdp") // 2
    core = lax.rem(me, 2)
    rows = grad.shape[0] // (2 * chips)
    copies = []
    for chip in range(chips):
        theirs = pl.ds(pl.multiple_of((2 * chip + 1 - core) * rows, rows), rows)
        copies.append(
            send(grad.at[theirs], home.at[chip], sems, base + chip, {"fsdp": me + 1 - 2 * core})
        )
    return copies


def line_home(copies, grad, home):
    me = lax.axis_index("fsdp")
    chips = lax.axis_size("fsdp") // 2
    core = lax.rem(me, 2)
    rows = grad.shape[0] // (2 * chips)
    for chip in range(chips):
        copies[chip].wait_recv()
        mine = pl.ds(pl.multiple_of((2 * chip + core) * rows, rows), rows)
        home[chip] = (home[chip].astype(F32) + grad[mine, :].astype(F32)).astype(BF16)


def line_copies(reach, home, coming, sems, base):
    me = lax.axis_index("fsdp")
    chips = lax.axis_size("fsdp") // 2
    chip = me // 2
    found = []
    for side, way in ((0, 1), (1, -1)):
        owner = lax.rem(chip + way * reach + chips, chips)
        copy = pltpu.make_async_remote_copy(
            src_ref=home.at[owner],
            dst_ref=coming.at[side, reach - 1],
            send_sem=sems[0].at[base + 2 * reach + side],
            recv_sem=sems[1].at[base + 2 * reach + side],
            device_id={"fsdp": lax.rem(me + 2 * way + 2 * chips, 2 * chips)},
            device_id_type=MESH,
        )
        if way == 1:
            sent = chip + reach <= chips - 1
            got = (chip >= 1) & (chip + reach <= chips)
            more = (chip >= 1) & sent
        else:
            sent = chip >= reach
            got = (chip <= chips - 2) & (chip + 1 >= reach)
            more = (chip <= chips - 2) & sent
        found.append((side, owner, copy, sent, got, more))
    return found


def line_step(reach, home, coming, sems, base):
    chips = lax.axis_size("fsdp") // 2
    if reach < chips - 1:
        for _, _, copy, _, got, _ in line_copies(reach + 1, home, coming, sems, base):
            pl.when(got)(copy.wait_recv)
    for side, owner, copy, sent, _, more in line_copies(reach, home, coming, sems, base):
        if reach < chips - 1:

            @pl.when(more)
            def _(side=side, owner=owner):
                home[owner] = (
                    home[owner].astype(F32) + coming[side, reach].astype(F32)
                ).astype(BF16)

        pl.when(sent)(copy.start)


def line_end(copies, home, coming, sems, base):
    me = lax.axis_index("fsdp")
    chips = lax.axis_size("fsdp") // 2
    chip = me // 2
    for side, _, copy, _, got, _ in line_copies(1, home, coming, sems, base):

        @pl.when(got)
        def _(side=side, copy=copy):
            copy.wait_recv()
            home[chip] = (home[chip].astype(F32) + coming[side, 0].astype(F32)).astype(BF16)

    for copy in copies:
        copy.wait_send()
    for reach in range(1, chips):
        for _, _, copy, sent, _, _ in line_copies(reach, home, coming, sems, base):
            pl.when(sent)(copy.wait_send)


def remote_call(
    kernel, out_shape, args, collective_id, micros, scratch, in_hbm=(), smem=0, args_in_hbm=0
):
    return pl.pallas_call(
        kernel,
        out_shape=out_shape,
        in_specs=[pl.BlockSpec(memory_space=pltpu.SMEM)] * smem
        + [pl.BlockSpec(memory_space=pltpu.VMEM)] * (len(args) - smem - args_in_hbm)
        + [pl.BlockSpec(memory_space=pl.ANY)] * args_in_hbm,
        out_specs=[
            pl.BlockSpec(memory_space=pl.ANY if item in in_hbm else pltpu.VMEM)
            for item in range(len(out_shape))
        ],
        scratch_shapes=scratch,
        compiler_params=remote_params(collective_id),
        cost_estimate=cost(micros),
    )(*args)


def adam_update(param_now, grad_now, moment_old_one, moment_old_two, step_rate, decay_rate):
    first_new = BETA_ONE * moment_old_one + (1.0 - BETA_ONE) * grad_now
    second_new = BETA_TWO * moment_old_two + (1.0 - BETA_TWO) * grad_now * grad_now
    ratio = (first_new * (1.0 / (1.0 - BETA_ONE**STEP))) / (
        jnp.sqrt(second_new * (1.0 / (1.0 - BETA_TWO**STEP))) + ADAM_EPS
    )
    return (first_new, second_new, param_now - step_rate * (ratio + decay_rate * param_now))


def joined_ranges(segments):
    ranges = []
    for number in sorted(range(len(segments)), key=lambda n: segments[n][3]):
        column, width = segments[number][3:]
        if ranges and ranges[-1][0] + ranges[-1][1] == column:
            first, so_far, numbers = ranges[-1]
            ranges[-1] = (first, so_far + width, numbers + (number,))
        else:
            ranges.append((column, width, (number,)))
    return ranges


def adam_kernel(segments, pieces, held, *refs):
    me = lax.axis_index("ctx")
    grads = refs[:pieces]
    olds = refs[pieces : pieces + 3]
    news = refs[pieces + 3 + held : pieces + 3 + held + 4]
    grad_buf, old_buf, low_buf, grad_sem, in_sem, out_sem = refs[pieces + 3 + held + 4 :]
    base = min(segment[3] for segment in segments)
    ranges = joined_ranges(segments)
    loads = []
    for place, (column, width, numbers) in enumerate(ranges):
        here, there = pl.ds(column - base, width), pl.ds(column, width)
        copies = [
            load(olds[item].at[:, there], old_buf.at[item, :, here], in_sem.at[item, place])
            for item in range(3)
        ]
        for number in numbers:
            piece, index, first, start, count = segments[number]
            columns = pl.ds(first, count)
            for source_number, source in enumerate(grads):
                if piece not in (None, source_number):
                    continue
                copy = pltpu.make_async_copy(
                    source.at[:, columns] if piece is None else source.at[index, :, columns],
                    grad_buf.at[:, pl.ds(start - base, count)],
                    grad_sem.at[number],
                )
                if piece is None:
                    pl.when(me == index ^ source_number)(copy.start)
                else:
                    copy.start()
            copies.append(copy)
        loads.append(copies)
    stores = []
    for place, (column, width, numbers) in enumerate(ranges):
        for copy in loads[place]:
            copy.wait()
        here, there = pl.ds(column - base, width), pl.ds(column, width)
        for first in range(0, width, 256):
            part = pl.ds(column - base + first, min(256, width - first))
            first_new, second_new, master = adam_update(
                old_buf[0, :, part],
                grad_buf[:, part].astype(F32),
                old_buf[1, :, part],
                old_buf[2, :, part],
                LEARN_RATE,
                WEIGHT_DECAY,
            )
            old_buf[0, :, part] = master
            old_buf[1, :, part] = first_new
            old_buf[2, :, part] = second_new
            low_buf[:, part] = master.astype(BF16)
        for item, source in enumerate(
            (
                old_buf.at[1, :, here],
                old_buf.at[2, :, here],
                old_buf.at[0, :, here],
                low_buf.at[:, here],
            )
        ):
            stores.append(load(source, news[item].at[:, there], out_sem.at[item, place]))
    for copy in stores:
        copy.wait()


def adam(segments, grads, olds, held, micros):
    rows, columns = olds[0].shape
    span = max(s[3] + s[4] for s in segments) - min(s[3] for s in segments)
    held = [] if held is None else list(held)
    args = list(grads) + list(olds) + held
    return pl.pallas_call(
        functools.partial(adam_kernel, tuple(segments), len(grads), len(held)),
        out_shape=[jax.ShapeDtypeStruct((rows, columns), F32)] * 3
        + [jax.ShapeDtypeStruct((rows, columns), BF16)],
        in_specs=[pl.BlockSpec(memory_space=pl.ANY)] * len(args),
        out_specs=[pl.BlockSpec(memory_space=pl.ANY)] * 4,
        input_output_aliases={len(grads) + 3 + item: item for item in range(len(held))},
        scratch_shapes=[
            pltpu.VMEM((rows, span), BF16),
            pltpu.VMEM((3, rows, span), F32),
            pltpu.VMEM((rows, span), BF16),
            pltpu.SemaphoreType.DMA((len(segments),)),
            pltpu.SemaphoreType.DMA((3, len(segments))),
            pltpu.SemaphoreType.DMA((4, len(segments))),
        ],
        compiler_params=pltpu.CompilerParams(vmem_limit_bytes=VMEM_LIMIT),
        cost_estimate=cost(micros),
    )(*args)


def head_mean(values, ones):
    high = values.astype(BF16)
    rest = (values - high.astype(F32)).astype(BF16)
    return (dot(high, ones, 1, 0) + dot(rest, ones, 1, 0)) * (1.0 / HD)


def head_ones(width):
    row = lax.broadcasted_iota(jnp.int32, (width, width), 0) // HD
    col = lax.broadcasted_iota(jnp.int32, (width, width), 1) // HD
    return jnp.where(row == col, 1.0, 0.0).astype(BF16)


def partner(values):
    width = values.shape[-1]
    lane = lax.broadcasted_iota(jnp.int32, values.shape, 1)
    return jnp.where(
        lane % HD < HD // 2,
        pltpu.roll(values, width - HD // 2, 1),
        pltpu.roll(values, HD // 2, 1),
    )


def widen(table, width):
    return [
        jnp.concatenate([part] * (width // HD), axis=-1)
        for part in (table[:, :HD], table[:, HD:])
    ]


def doc_first(starts, times):
    first = jnp.zeros_like(times)
    for item in range(starts.shape[0]):
        first = jnp.where(starts[item] <= times, starts[item], first)
    return first


def block_mask(starts, block, keys):
    shape = (keys, GROUP * HALF)
    times = block * HALF + lax.broadcasted_iota(jnp.int32, (1, GROUP * HALF), 1) % HALF
    key = lax.broadcasted_iota(jnp.int32, shape, 0)
    return (key >= doc_first(starts, times)) & (key <= times)


def stack_heads(ref, rows, group):
    return jnp.concatenate(
        [
            ref[rows, (group * GROUP + h) * HD : (group * GROUP + h + 1) * HD]
            for h in range(GROUP)
        ],
        axis=0,
    )


def unstack_heads(turned):
    wide = turned.T
    return [wide[h * HALF : (h + 1) * HALF, :] for h in range(GROUP)]


def attend_kernel(
    blocks,
    groups,
    place,
    order,
    starts,
    table,
    gain,
    normed_in,
    weights_from,
    dy,
    swap_in,
    part,
    qk,
    q,
    k,
    v,
    o_held,
    lse,
    dy_all,
    swap_out,
    normed,
    weights_in,
    joined,
    o,
    send_sem,
    recv_sem,
    local,
):
    sems = (send_sem, recv_sem)
    me = lax.axis_index("ctx")
    qk_width = qk.shape[1]
    q_width = q.shape[1]
    qkv_width = qk_width + v.shape[1]
    ones = head_ones(qk_width)
    meet(("ctx",))
    loads = [
        load(normed_in, normed, local.at[0]),
        load(weights_from, weights_in, local.at[1]),
    ]
    swap_copies = swap_start(swap_in, swap_out, sems, GATHER_SEMS)
    copies = gather_start(dy, dy_all, sems, 0)
    own_copies = [
        load(swap_in.at[me], swap_out.at[me], local.at[2]),
        load(dy, dy_all.at[me], local.at[3]),
    ]
    for copy in loads:
        copy.wait()
    for block in range(blocks):
        joined[block] = dot(
            normed[block * HALF : (block + 1) * HALF, :], weights_in[:, :qkv_width], 1, 0
        )
    for block in range(blocks):
        to = slice(block * HALF, (block + 1) * HALF)
        values = joined[place[block]]
        v[to, :] = values[:, qk_width:].astype(BF16)
        values = values[:, :qk_width]
        qk[to, :] = values
        turned = values * lax.rsqrt(head_mean(values * values, ones) + NORM_EPS) * gain[...]
        cosine, sine = widen(table[to, :], qk_width)
        turned = turned * cosine + partner(turned) * sine
        turned = turned.astype(BF16)
        q[to, :] = turned[:, :q_width]
        k[to, :] = turned[:, q_width:]
    for block in range(blocks):
        rows = slice(block * HALF, (block + 1) * HALF)
        keys = (block + 1) * HALF
        mask = block_mask(starts, block, keys)
        pieces = []
        for group in range(groups):
            lanes = slice(group * HD, (group + 1) * HD)
            queries = stack_heads(q, rows, group)
            scores = dot(k[:keys, lanes], queries, 1, 1) * SCALE
            weights = jnp.where(mask, jnp.exp(scores), 0.0)
            sums = jnp.sum(weights, axis=0, keepdims=True)
            lse[block, group : group + 1, :] = jnp.log(sums)
            mixed = dot(v[:keys, lanes], weights.astype(BF16), 0, 0) / sums
            pieces += unstack_heads(mixed)
        o[block] = jnp.concatenate(pieces, axis=1).astype(BF16)
    for block in range(blocks):
        o_held[block * HALF : (block + 1) * HALF, :] = o[order[block]]
    for first in range(0, D, 512):
        part[:, first : first + 512] = dot(
            o_held[...], weights_in[first : first + 512, qkv_width:], 1, 1
        ).astype(BF16)
    gather_rest(copies, dy_all, sems, 0)
    for copy in swap_copies:
        copy.wait()
    for copy in own_copies:
        copy.wait()


def attend_back_kernel(
    blocks,
    groups,
    place,
    order,
    starts,
    lse,
    gain,
    part,
    rest_grad,
    *refs,
):
    sources, refs = refs[:9], refs[9:]
    out, joined, gain_grad, out_grad, rest_sum = refs[:5]
    targets, refs = refs[5:14], refs[14:]
    grad_all, weights_in, q, k, v, o, qk, table, middle = targets
    bufs, (do, dq, dkv, turned, home, coming) = refs[:-11], refs[-11:-5]
    send_one, recv_one, send_two, recv_two, local = refs[-5:]
    line = (send_two, recv_two)
    chips = lax.axis_size("fsdp") // 2
    out_sems = (send_one, recv_one)
    qk_width = qk.shape[2]
    qkv_width = qk_width + v.shape[1]
    ones = head_ones(qk_width)
    meet(("ctx", "fsdp"))
    home_copies = line_start(rest_grad, home, line, 0)
    out_copies = sum_start(part, bufs, out_sems)
    loads = [
        load(source, target, local.at[item])
        for item, (source, target) in enumerate(zip(sources, targets))
    ]
    for copy in loads[:6]:
        copy.wait()
    for block in range(blocks):
        do[block * HALF : (block + 1) * HALF, :] = dot(
            grad_all[place[block]], weights_in[:, qkv_width:], 1, 0
        ).astype(BF16)
    for block in range(blocks):
        turned[:, block * HALF : (block + 1) * HALF] = grad_all[block].T
    for first in range(0, D, 512):
        rows = slice(first, first + 512)
        out_grad[rows, :] = dot(turned[rows, :], o[...], 1, 0).astype(BF16)
    dkv[...] = jnp.zeros_like(dkv)
    line_home(home_copies, rest_grad, home)
    line_step(chips - 1, home, coming, line, chips)
    reach = chips - 2
    for block in range(blocks):
        if block == blocks // 2:
            sum_pass(out_copies, part, bufs, out_sems)
        if block >= blocks * 3 // 4 and reach > 1:
            line_step(reach, home, coming, line, chips)
            reach -= 1
        rows = slice(block * HALF, (block + 1) * HALF)
        keys = (block + 1) * HALF
        mask = block_mask(starts, block, keys)
        pieces = []
        dk_add = []
        dv_add = []
        for group in range(groups):
            lanes = slice(group * HD, (group + 1) * HD)
            queries = stack_heads(q, rows, group)
            outs = stack_heads(do, rows, group)
            key_rows = k[:keys, lanes]
            scores = dot(key_rows, queries, 1, 1) * SCALE
            weights = jnp.where(
                mask, jnp.exp(scores - lse[block, group : group + 1, :]), 0.0
            )
            back = dot(v[:keys, lanes], outs, 1, 1)
            delta = jnp.sum(weights * back, axis=0, keepdims=True)
            grads = (weights * (back - delta)).astype(BF16)
            pieces += unstack_heads(dot(key_rows, grads, 0, 0) * SCALE)
            dk_add.append(dot(grads, queries, 1, 0) * SCALE)
            dv_add.append(dot(weights.astype(BF16), outs, 1, 0))
        dq[block] = jnp.concatenate(pieces, axis=1)
        dkv[: block + 1] += jnp.concatenate(dk_add + dv_add, axis=1).reshape(
            (block + 1,) + dkv.shape[1:]
        )
    for step in range(reach, 0, -1):
        line_step(step, home, coming, line, chips)
    gain_row = jnp.zeros((1, qk_width), F32)
    for copy in loads[6:]:
        copy.wait()
    for block in range(blocks):
        here = order[block]
        values = qk[here]
        root = lax.rsqrt(head_mean(values * values, ones) + NORM_EPS)
        unit = values * root
        grad_kv = dkv[here]
        kv_width = grad_kv.shape[1] // 2
        grad = jnp.concatenate([dq[here], grad_kv[:, :kv_width]], axis=1)
        cosine, sine = widen(table[here], qk_width)
        grad = grad * cosine - partner(grad) * sine
        gain_row = gain_row + jnp.sum(grad * unit, axis=0, keepdims=True)
        grad = grad * gain[...]
        grad = root * (grad - unit * head_mean(grad * unit, ones))
        joined[block * HALF : (block + 1) * HALF, :] = jnp.concatenate(
            [grad, grad_kv[:, kv_width:]], axis=1
        ).astype(BF16)
    gain_grad[...] = gain_row
    read = sum_rest(out_copies, part, bufs)
    half = middle.shape[0] // 2
    for first in (0, half):
        rows = pl.ds(first, half)
        out[rows, :] = (middle[rows, :] + read(first)).astype(BF16)
    line_end(home_copies, home, coming, line, chips)
    chip = lax.axis_index("fsdp") // 2
    owned_rows = rest_sum.shape[1]
    for index in range(rest_sum.shape[0]):
        rest_sum[index] = home[chip, index * owned_rows : (index + 1) * owned_rows, :]


def tail_kernel(
    swaps,
    joined,
    out_grad,
    gain_row,
    attn_gain,
    ffn_gain_grad,
    *refs,
):
    sources, refs = refs[:4], refs[4:]
    swap_in, refs = refs[:swaps], refs[swaps:]
    grad_tokens, gains, attn_own = refs[:3]
    swap_out, refs = refs[3 : 3 + swaps], refs[3 + swaps :]
    targets, refs = refs[:4], refs[4:]
    weights_in, normed, x, grad_middle = targets
    back_bufs, refs = refs[:-15], refs[-15:]
    turned, part, attn_grad, home, coming, owned, ctx_box, fsdp_box = refs[:8]
    send_two, recv_two, send_three, recv_three, send_four, recv_four, local = refs[8:]
    back_sems = (send_two, recv_two)
    line, small = (send_three, recv_three), (send_four, recv_four)
    size = lax.axis_size("ctx")
    me = lax.axis_index("ctx")
    chips = lax.axis_size("fsdp") // 2
    step_base = chips
    swap_base = step_base + 2 * chips
    qkv_width = joined.shape[1]
    qk_width = gain_row.shape[1]
    half = x.shape[0] // 2
    loads = [
        load(source, target, local.at[item])
        for item, (source, target) in enumerate(zip(sources, targets))
    ]
    meet(("ctx", "fsdp"))
    swap_copies = []
    own_copies = []
    for item in range(swaps):
        swap_copies += swap_start(
            swap_in[item], swap_out[item], line, swap_base + (item + 1) * size
        )
        own_copies.append(
            load(swap_in[item].at[me], swap_out[item].at[me], local.at[4 + item])
        )
    for copy in loads:
        copy.wait()
    for first in range(0, D, 512):
        part[:, first : first + 512] = dot(
            joined[...], weights_in[first : first + 512, :qkv_width], 1, 1
        ).astype(BF16)
    back_copies = sum_start(part, back_bufs, back_sems)
    turn(normed, turned)
    for first in range(0, D, 512):
        rows = slice(first, first + 512)
        attn_grad[rows, :qkv_width] = dot(turned[rows, :], joined[...], 1, 0).astype(BF16)
    attn_grad[:, qkv_width:] = out_grad[...]
    home_copies = line_start(attn_grad, home, line, 0)
    line_home(home_copies, attn_grad, home)
    line_step(chips - 1, home, coming, line, step_base)
    sum_pass(back_copies, part, back_bufs, back_sems)
    for reach in range(chips - 2, 1, -1):
        line_step(reach, home, coming, line, step_base)
    read = sum_rest(back_copies, part, back_bufs)
    total = jnp.zeros((1, D), F32)
    for first in (0, half):
        rows = pl.ds(first, half)
        values = x[rows, :].astype(F32)
        root = row_scale(values)
        unit = values * root
        back = read(first)
        total = total + jnp.sum(back * unit, axis=0, keepdims=True)
        back = back * attn_gain[...]
        back = root * (back - unit * jnp.mean(back * unit, axis=-1, keepdims=True))
        grad_tokens[rows, :] = grad_middle[rows, :] + back

    def spread_start(axis, box, value, base):
        index = lax.axis_index(axis)
        axis_size = lax.axis_size(axis)
        box[index] = value
        return [
            send(
                box.at[index],
                box.at[index],
                small,
                base + step,
                {axis: lax.rem(index + step, axis_size)},
            )
            for step in range(1, axis_size)
        ]

    def spread_end(copies, box):
        for copy in copies:
            copy.wait()
        summed = box[0]
        for item in range(1, box.shape[0]):
            summed = summed + box[item]
        return summed

    ctx_copies = spread_start(
        "ctx",
        ctx_box,
        jnp.concatenate(
            [
                total,
                ffn_gain_grad[...],
                jnp.concatenate([gain_row[...], jnp.zeros((1, D - qk_width), F32)], axis=1),
                jnp.zeros((5, D), F32),
            ],
            axis=0,
        ),
        0,
    )
    line_step(1, home, coming, line, step_base)
    fsdp_copies = spread_start("fsdp", fsdp_box, spread_end(ctx_copies, ctx_box), size)
    line_end(home_copies, home, coming, line, step_base)
    chip = lax.axis_index("fsdp") // 2
    owned_rows = owned.shape[1]
    for index in range(size):
        owned[index] = home[chip, index * owned_rows : (index + 1) * owned_rows, :]
    swap_copies += swap_start(owned, attn_own, line, swap_base)
    attn_own[me] = owned[me]
    gains[...] = spread_end(fsdp_copies, fsdp_box)
    for copy in swap_copies:
        copy.wait()
    for copy in own_copies:
        copy.wait()


def rms_scale(values_in, gain_vec):
    return (
        values_in
        * lax.rsqrt(jnp.mean(values_in * values_in, axis=-1, keepdims=True) + NORM_EPS)
        * gain_vec
    )


def inverse_freq():
    return 1.0 / ROPE_BASE ** (jnp.arange(0, HD, 2).astype(F32) / HD)


def shards(
    tokens,
    cotangent,
    doc_starts,
    block_order,
    master_weights,
    moment_one,
    moment_two,
    gains,
    gains_moment_one,
    gains_moment_two,
):
    nctx = lax.axis_size("ctx")
    nfsdp = lax.axis_size("fsdp")
    own_rows = master_weights.shape[0]
    tok_rows = tokens.shape[1]
    stream_len = tok_rows * nctx
    blocks = stream_len // HALF
    groups = KVHEADS // nctx
    q_width = D // nctx
    kv_width = KVD // nctx
    qk_width = q_width + kv_width
    qkv_width = qk_width + kv_width
    tiles = FF // 128
    ff_tiles = -(-tiles // nctx)
    ff_width = ff_tiles * 128
    bundles = 2
    cuts = [0, (ff_tiles * 5 + 3) // 7 * 128, ff_width]


    def ff_part(base, index, start, stop):
        first = index * ff_width + start
        last = index * ff_width + stop
        real_first, real_last = min(first, FF), min(last, FF)
        part = late_weights[:, base + real_first : base + real_last].astype(BF16)
        if real_last - real_first < last - first:
            part = jnp.pad(part, ((0, 0), (0, (last - first) - (real_last - real_first))))
        return part

    def attn_part(index):
        return jnp.concatenate(
            [
                master_weights[:, index * q_width : (index + 1) * q_width],
                master_weights[:, D + index * kv_width : D + (index + 1) * kv_width],
                master_weights[:, D + KVD + index * kv_width : D + KVD + (index + 1) * kv_width],
                master_weights[:, QKVC + index * q_width : QKVC + (index + 1) * q_width],
            ],
            axis=1,
        ).astype(BF16)

    gate_base = QKVC + D
    bases = (gate_base, gate_base + FF, gate_base + 2 * FF)
    attn_send = jnp.stack([attn_part(c) for c in range(nctx)])
    def gather_rows(piece):
        return lax.all_gather(
            piece.reshape(nctx * own_rows, piece.shape[-1]), "fsdp", axis=0, tiled=True
        )

    def spread(active):
        return (
            active.reshape(active.shape[0], nctx, nfsdp, own_rows)
            .transpose(0, 2, 1, 3)
            .reshape(active.shape[0], D)
        )

    def unspread(active):
        return (
            active.reshape(active.shape[0], nfsdp, nctx, own_rows)
            .transpose(0, 2, 1, 3)
            .reshape(active.shape[0], D)
        )

    dma = pltpu.SemaphoreType.DMA
    all_low = jax.ShapeDtypeStruct((nctx, tok_rows, D), BF16)
    own_low = jax.ShapeDtypeStruct((tok_rows, D), BF16)
    own_f32 = jax.ShapeDtypeStruct((tok_rows, D), F32)
    row_f32 = jax.ShapeDtypeStruct((1, D), F32)
    g_attn = spread(gains[None, :D])
    g_ffn = spread(gains[None, D : 2 * D])
    order = block_order.reshape(blocks)
    place = jnp.argsort(order).astype(jnp.int32)
    starts = doc_starts[0]

    (attn_held,) = exchange(("swap",), [attn_send], 0, 10)
    w_attn = gather_rows(attn_held)
    late_weights, attn_held = lax.optimization_barrier((master_weights, attn_held))
    ff_send = [
        jnp.stack(
            [
                jnp.concatenate(
                    [ff_part(base, c, cuts[b], cuts[b + 1]) for base in bases], axis=1
                )
                for c in range(nctx)
            ]
        )
        for b in range(bundles)
    ]

    first_send = ff_send[0]
    (first_held,) = exchange(("swap",), [first_send], 1, 16)
    table_shape = jax.ShapeDtypeStruct((stream_len, 2 * HD), F32)
    origin = spread(jnp.arange(D, dtype=jnp.int32)[None])
    starts_late, first_held = lax.optimization_barrier((starts, first_held))
    x_low, dy_low, table, normed_all = remote_call(
        first_kernel,
        [own_low, own_low, table_shape, all_low],
        (
            starts_late,
            origin,
            tokens[0],
            cotangent[0],
            g_attn,
            jnp.tile(inverse_freq(), 4)[None],
        ),
        2,
        33,
        [
            pltpu.VMEM((D, D), BF16),
            pltpu.VMEM((tok_rows, D), BF16),
            dma((GATHER_SEMS,)),
            dma((GATHER_SEMS,)),
            dma,
        ],
        (3,),
        1,
    )
    normed_all = normed_all.reshape(stream_len, D)

    g_query = gains[2 * D : 2 * D + HD]
    g_key = gains[2 * D + HD :]
    qk_gain = jnp.concatenate(
        [jnp.tile(g_query, q_width // HD), jnp.tile(g_key, kv_width // HD)]
    )[None]

    low_stream = pltpu.VMEM((stream_len, D), BF16)
    heads_low = pltpu.VMEM((stream_len, q_width), BF16)
    part, qk, q, k, v, mixed, lse, dy_all, second_held = remote_call(
        functools.partial(attend_kernel, blocks, groups),
        [
            jax.ShapeDtypeStruct((stream_len, D), BF16),
            jax.ShapeDtypeStruct((stream_len, qk_width), F32),
            jax.ShapeDtypeStruct((stream_len, q_width), BF16),
            jax.ShapeDtypeStruct((stream_len, kv_width), BF16),
            jax.ShapeDtypeStruct((stream_len, kv_width), BF16),
            jax.ShapeDtypeStruct((stream_len, q_width), BF16),
            jax.ShapeDtypeStruct((blocks, groups, GROUP * HALF), F32),
            all_low,
            jax.ShapeDtypeStruct(ff_send[1].shape, BF16),
        ],
        (place, order, starts, table, qk_gain, normed_all, w_attn, dy_low, ff_send[1]),
        3,
        42,
        [
            low_stream,
            pltpu.VMEM(w_attn.shape, BF16),
            pltpu.VMEM((blocks, HALF, qkv_width), F32),
            pltpu.VMEM((blocks, HALF, q_width), BF16),
            dma((GATHER_SEMS + nctx,)),
            dma((GATHER_SEMS + nctx,)),
            dma((4,)),
        ],
        (7, 8),
        3,
        4,
    )
    dy_all = dy_all.reshape(stream_len, D)
    w_ff = [gather_rows(first_held), gather_rows(second_held)]
    sum_bufs = sum_scratch(nctx, tok_rows)
    sum_sems = [dma((GATHER_SEMS,)), dma((GATHER_SEMS,))]
    norm_scratch = (
        sum_bufs + [pltpu.VMEM((tok_rows, D), BF16)] + sum_sems + sum_sems + [dma]
    )

    middle, normed_two_all = remote_call(
        middle_kernel,
        [own_f32, all_low],
        (part, x_low, g_ffn),
        4,
        57,
        norm_scratch,
        (1,),
    )
    normed_two_all = normed_two_all.reshape(stream_len, D)

    def sum_rows(grad):
        return lax.psum_scatter(grad, "fsdp", scatter_dimension=0, tiled=True).reshape(
            nctx, own_rows, grad.shape[-1]
        )

    def feed(b, x_all, dy):
        width = cuts[b + 1] - cuts[b]
        w_gu, w_down = w_ff[b][:, : 2 * width], w_ff[b][:, 2 * width :]
        gate_up = dot(x_all, w_gu, 1, 0).astype(BF16)
        gate, up = gate_up[:, :width].astype(F32), gate_up[:, width:].astype(F32)
        gated = jax.nn.sigmoid(gate)
        act = gate * gated
        hidden = (act * up).astype(BF16)
        back_hidden = dot(dy, w_down, 1, 0)
        grad_gu = jnp.concatenate(
            [back_hidden * up * (gated + act * (1.0 - gated)), back_hidden * act], axis=1
        ).astype(BF16)
        return hidden, grad_gu, dot(grad_gu, w_gu, 1, 1)

    hidden_one, grad_gu, back_partial = feed(0, normed_two_all, dy_all)
    gu_grad = dot(normed_two_all, grad_gu, 0, 0).astype(BF16)
    back_partial = back_partial.astype(BF16)
    gu_grad, back_partial, w_ff[1] = lax.optimization_barrier((gu_grad, back_partial, w_ff[1]))
    width_two = cuts[2] - cuts[1]
    width_line = cuts[1] * 3 // 5 // 128 * 128
    width_rest = cuts[1] - width_line
    gu_sum = sum_rows(gu_grad)
    chips = nfsdp // 2

    def line_scratch(columns):
        block = (nctx * own_rows, columns)
        return [pltpu.VMEM((chips,) + block, BF16), pltpu.VMEM((2, chips - 1) + block, BF16)]

    (
        grad_middle,
        grad_g_ffn,
        down_sum,
        grad_middle_all,
        rest_grad,
        last_grad,
        out_partial,
    ) = remote_call(
        middle_back_kernel,
        [
            own_f32,
            row_f32,
            jax.ShapeDtypeStruct((nctx, own_rows, width_line), BF16),
            all_low,
            jax.ShapeDtypeStruct((D, width_rest), BF16),
            jax.ShapeDtypeStruct((D, 3 * width_two), BF16),
            jax.ShapeDtypeStruct((stream_len, D), BF16),
        ],
        (
            middle,
            dy_low,
            g_ffn,
            back_partial,
            normed_two_all,
            dy_all,
            hidden_one,
            w_ff[0],
            w_ff[1],
        ),
        5,
        57,
        sum_bufs
        + [
            pltpu.VMEM((tok_rows, D), BF16),
            low_stream,
            low_stream,
            pltpu.VMEM((stream_len, 2 * width_two), BF16),
            pltpu.VMEM((D, stream_len), BF16),
            pltpu.VMEM((D, 3 * width_two), BF16),
            pltpu.VMEM((D, width_line), BF16),
            low_stream,
            pltpu.VMEM((stream_len, cuts[1]), BF16),
            pltpu.VMEM((stream_len, width_two), BF16),
            pltpu.VMEM((D, cuts[1] if cuts[1] > stream_len else 128), BF16),
            pltpu.VMEM((D, 3 * width_two), BF16),
        ]
        + line_scratch(width_line)
        + sum_sems
        + sum_sems
        + [dma((3 * chips,)), dma((3 * chips,)), dma((11,))],
        (3, 4, 5, 6),
        0,
        6,
    )
    last_sum = sum_rows(last_grad)

    small = dma((nctx + nfsdp,))
    line_sems = dma((3 * chips + 4 * nctx,))
    own_shape = (nctx, own_rows, qkv_width + q_width)
    sources = (
        grad_middle_all.reshape(blocks, HALF, D),
        w_attn,
        q,
        k,
        v,
        mixed,
        qk.reshape(blocks, HALF, qk_width),
        table.reshape(blocks, HALF, 2 * HD),
        middle,
    )
    out_tokens, grad_joined, qk_gain_grad, out_grad, rest_sum = remote_call(
        functools.partial(attend_back_kernel, blocks, groups),
        [
            own_low,
            jax.ShapeDtypeStruct((stream_len, qkv_width), BF16),
            jax.ShapeDtypeStruct((1, qk_width), F32),
            jax.ShapeDtypeStruct((D, q_width), BF16),
            jax.ShapeDtypeStruct((nctx, own_rows, width_rest), BF16),
        ],
        (place, order, starts, lse, qk_gain, out_partial, rest_grad) + sources,
        6,
        45,
        [pltpu.VMEM(source.shape, source.dtype) for source in sources]
        + sum_bufs
        + [
            heads_low,
            pltpu.VMEM((blocks, HALF, q_width), F32),
            pltpu.VMEM((blocks, HALF, 2 * kv_width), F32),
            pltpu.VMEM((D, stream_len), BF16),
        ]
        + line_scratch(width_rest)
        + sum_sems
        + [dma((3 * chips,)), dma((3 * chips,)), dma((9,))],
        (),
        3,
        9,
    )
    sources = (w_attn, normed_all, x_low, grad_middle)
    grad_tokens, gain_sums, attn_own, gu_own, down_own, rest_own = remote_call(
        functools.partial(tail_kernel, 3),
        [
            own_f32,
            jax.ShapeDtypeStruct((8, D), F32),
            jax.ShapeDtypeStruct(own_shape, BF16),
            jax.ShapeDtypeStruct(gu_sum.shape, BF16),
            jax.ShapeDtypeStruct(down_sum.shape, BF16),
            jax.ShapeDtypeStruct(rest_sum.shape, BF16),
        ],
        (grad_joined, out_grad, qk_gain_grad, g_attn, grad_g_ffn) + sources + (gu_sum, down_sum, rest_sum),
        7,
        75,
        [pltpu.VMEM(source.shape, source.dtype) for source in sources]
        + sum_bufs
        + [
            pltpu.VMEM((D, stream_len), BF16),
            low_stream,
            pltpu.VMEM((D, qkv_width + q_width), BF16),
        ]
        + line_scratch(qkv_width + q_width)
        + [
            pltpu.VMEM(own_shape, BF16),
            pltpu.VMEM((nctx, 8, D), F32),
            pltpu.VMEM((nfsdp, 8, D), F32),
        ]
        + sum_sems
        + [line_sems, line_sems, small, small, dma((7,))],
        (3, 4, 5),
        0,
        7,
    )
    last_sum, gain_sums, gu_own = lax.optimization_barrier((last_sum, gain_sums, gu_own))
    out_tokens = unspread(out_tokens)[None]
    grad_tokens = unspread(grad_tokens)[None]
    gain_grad = jnp.concatenate(
        [
            unspread(gain_sums[:1])[0],
            unspread(gain_sums[1:2])[0],
            jnp.sum(gain_sums[2, :q_width].reshape(-1, HD), axis=0),
            jnp.sum(gain_sums[2, q_width:qk_width].reshape(-1, HD), axis=0),
        ]
    )

    olds = (master_weights, moment_one, moment_two)

    def feed_segments(b, pieces, start, stop):
        found = []
        for part in pieces:
            for c in range(nctx):
                column = c * ff_width + cuts[b] + start
                real = min(max(FF - column, 0), stop - start)
                if real:
                    piece, first = pieces[part]
                    found.append((piece, c, first, bases[part] + column, real))
        return found

    width_one = cuts[1]
    last_own = [
        lax.ppermute(
            lax.dynamic_index_in_dim(last_sum, lax.axis_index("ctx") ^ k, 0, keepdims=False),
            "ctx",
            [(c, c ^ k) for c in range(nctx)],
        )
        if k
        else lax.dynamic_index_in_dim(last_sum, lax.axis_index("ctx"), 0, keepdims=False)
        for k in range(nctx)
    ]
    parts = (
        (0, 0, q_width),
        (q_width, D, kv_width),
        (qk_width, D + KVD, kv_width),
        (qkv_width, QKVC, q_width),
    )
    if kv_width % 128:
        attn_own = jnp.concatenate(
            [attn_own[c, :, f : f + w] for f, _, w in parts for c in range(nctx)], axis=1
        )[None]
        segments = [(0, 0, 0, 0, gate_base)]
    else:
        segments = [
            (0, c, first, base + c * width, width)
            for first, base, width in parts
            for c in range(nctx)
        ]
    news = adam(
        segments
        + feed_segments(0, {0: (1, 0), 1: (1, width_one)}, 0, width_one)
        + feed_segments(0, {2: (2, 0)}, 0, width_line)
        + feed_segments(0, {2: (3, 0)}, width_line, width_one),
        [attn_own, gu_own, down_own, rest_own],
        olds,
        None,
        10,
    )
    first_new, second_new, master_new, low_new = adam(
        feed_segments(
            1, {0: (None, 0), 1: (None, width_two), 2: (None, 2 * width_two)}, 0, width_two
        ),
        last_own,
        olds,
        news,
        6,
    )
    gain_first, gain_second, gain_new = adam_update(
        gains, gain_grad, gains_moment_one, gains_moment_two, GAIN_RATE, 0.0
    )
    return (
        out_tokens,
        grad_tokens,
        first_new,
        second_new,
        master_new,
        low_new,
        gain_first,
        gain_second,
        gain_new,
    )


def solution(mesh):
    rows = P("fsdp", "ctx", None)
    weights = P(("ctx", "fsdp"), None)
    return jax.shard_map(
        shards,
        mesh=mesh,
        in_specs=(rows, rows, P("fsdp", None), P(), weights, weights, weights, P(), P(), P()),
        out_specs=(rows, rows, weights, weights, weights, weights, P(), P(), P()),
        check_vma=False,
    )
```

```python
import functools

import jax
import jax.numpy as jnp
from jax import lax
from jax.experimental import pallas as pl
from jax.experimental.pallas import tpu as pltpu
from jax.sharding import PartitionSpec as P

D = 1536
HEADS = 24
KVHEADS = 8
HD = 64
FF = 6912
STEP = 10
HALF = 128
KVD = 512
QKVC = 2560
GROUP = HEADS // KVHEADS

ROPE_BASE = 1000000.0
NORM_EPS = 1e-05
BETA_ONE = 0.9
BETA_TWO = 0.95
ADAM_EPS = 1e-08
WEIGHT_DECAY = 0.1
LEARN_RATE = 0.03
GAIN_RATE = 0.5
SCALE = HD ** (-0.5)
MESH = pl.DeviceIdType.MESH
F32 = jnp.float32
BF16 = jnp.bfloat16
VMEM_LIMIT = 60 * 1024 * 1024


def dot(left, right, left_dim, right_dim):
    return lax.dot_general(
        left, right, (((left_dim,), (right_dim,)), ((), ())), preferred_element_type=F32
    )


def send(source, target, sems, item, peer):
    copy = pltpu.make_async_remote_copy(
        src_ref=source,
        dst_ref=target,
        send_sem=sems[0].at[item],
        recv_sem=sems[1].at[item],
        device_id=peer,
        device_id_type=MESH,
    )
    copy.start()
    return copy


def meet(axes):
    barrier = pltpu.get_barrier_semaphore()
    total = 0
    for axis in axes:
        size = lax.axis_size(axis)
        me = lax.axis_index(axis)
        for step in range(1, size):
            pl.semaphore_signal(
                barrier,
                inc=1,
                device_id={axis: lax.rem(me + step, size)},
                device_id_type=MESH,
            )
        total += size - 1
    pl.semaphore_wait(barrier, total)


def square():
    me = lax.axis_index("ctx")
    return me, me + 1 - 2 * lax.rem(me, 2), lax.rem(me + 2, 4), 3 - me


def swap_start(source, target, sems, base):
    size = lax.axis_size("ctx")
    me = lax.axis_index("ctx")
    copies = []
    for step in range(1, size):
        peer = lax.rem(me + step, size)
        copies.append(
            send(source.at[peer], target.at[me], sems, base + step, {"ctx": peer})
        )
    return copies


def gather_start(source, target, sems, base):
    size = lax.axis_size("ctx")
    me = lax.axis_index("ctx")
    if size != 4:
        return [
            send(
                source,
                target.at[me],
                sems,
                base + step,
                {"ctx": lax.rem(me + step, size)},
            )
            for step in range(1, size)
        ]
    me, side, over, across = square()
    half = source.shape[0] // 2
    top, low = pl.ds(0, half), pl.ds(half, half)
    return [
        send(source.at[top], target.at[me, top], sems, base, {"ctx": side}),
        send(source.at[low], target.at[me, low], sems, base + 1, {"ctx": over}),
        send(source.at[low], target.at[me, low], sems, base + 2, {"ctx": side}),
        send(source.at[top], target.at[me, top], sems, base + 3, {"ctx": over}),
    ]


def gather_pass(copies, target, sems, base):
    if lax.axis_size("ctx") != 4:
        return
    me, side, over, across = square()
    half = target.shape[1] // 2
    top, low = pl.ds(0, half), pl.ds(half, half)
    copies[0].wait_recv()
    copies.append(send(target.at[side, top], target.at[side, top], sems, base + 4, {"ctx": over}))
    copies[1].wait_recv()
    copies.append(send(target.at[over, low], target.at[over, low], sems, base + 5, {"ctx": side}))


def gather_end(copies):
    if lax.axis_size("ctx") != 4:
        for copy in copies:
            copy.wait()
        return
    for copy in copies:
        copy.wait_send()
    for copy in copies[2:]:
        copy.wait_recv()


def gather_rest(copies, target, sems, base):
    gather_pass(copies, target, sems, base)
    gather_end(copies)


def load(source, target, sem):
    copy = pltpu.make_async_copy(source, target, sem)
    copy.start()
    return copy


GATHER_SEMS = 8


def exchange_kernel(kinds, *refs):
    count = len(kinds)
    ins, outs = refs[:count], refs[count : 2 * count]
    send_sem, recv_sem, local_sem = refs[2 * count :]
    sems = (send_sem, recv_sem)
    me = lax.axis_index("ctx")
    meet(("ctx",))
    copies = []
    own = []
    for item in range(count):
        base = item * GATHER_SEMS
        if kinds[item] == "gather":
            copies.append(gather_start(ins[item], outs[item], sems, base))
            source = ins[item]
        else:
            copies.append(swap_start(ins[item], outs[item], sems, base))
            source = ins[item].at[me]
        copy = pltpu.make_async_copy(source, outs[item].at[me], local_sem.at[item])
        copy.start()
        own.append(copy)
    for item in range(count):
        if kinds[item] == "gather":
            gather_rest(copies[item], outs[item], sems, item * GATHER_SEMS)
        else:
            for copy in copies[item]:
                copy.wait()
    for copy in own:
        copy.wait()


def remote_params(collective_id):
    return pltpu.CompilerParams(
        collective_id=collective_id, has_side_effects=True, vmem_limit_bytes=VMEM_LIMIT
    )


def cost(micros):
    return pl.CostEstimate(flops=0, bytes_accessed=int(micros * 3.0e6), transcendentals=0)


def exchange(kinds, arrays, collective_id, micros):
    size = lax.axis_size("ctx")
    shapes = [
        jax.ShapeDtypeStruct((size,) + a.shape if kind == "gather" else a.shape, a.dtype)
        for kind, a in zip(kinds, arrays)
    ]
    sems = pltpu.SemaphoreType.DMA((len(arrays) * GATHER_SEMS,))
    return pl.pallas_call(
        functools.partial(exchange_kernel, kinds),
        out_shape=shapes,
        in_specs=[pl.BlockSpec(memory_space=pl.ANY)] * len(arrays),
        out_specs=[pl.BlockSpec(memory_space=pl.ANY)] * len(arrays),
        scratch_shapes=[sems, sems, pltpu.SemaphoreType.DMA((len(arrays),))],
        compiler_params=remote_params(collective_id),
        cost_estimate=cost(micros),
    )(*arrays)


def sum_scratch(size, rows):
    if size == 4:
        half = pltpu.VMEM((2, rows // 2, D), BF16)
        return [half, half, pltpu.VMEM((2, rows, D), BF16)]
    return [pltpu.VMEM((size - 1, rows, D), BF16)]


def sum_start(part, bufs, sems):
    size = lax.axis_size("ctx")
    me = lax.axis_index("ctx")
    rows = part.shape[0] // size

    def block(owner, first=0, count=rows):
        return pl.ds(pl.multiple_of(owner * rows + first, rows // 2), count)

    if size != 4:
        copies = []
        for step in range(1, size):
            peer = lax.rem(me + step, size)
            copies.append(
                send(part.at[block(peer)], bufs[0].at[step - 1], sems, step, {"ctx": peer})
            )
        return copies
    me, side, over, across = square()
    half = rows // 2
    relay, _, landed = bufs
    return [
        send(part.at[block(across, 0, half)], relay.at[0], sems, 0, {"ctx": side}),
        send(part.at[block(across, half, half)], relay.at[1], sems, 1, {"ctx": over}),
        send(
            part.at[block(side, 0, half)],
            landed.at[0, pl.ds(0, half)],
            sems,
            2,
            {"ctx": side},
        ),
        send(
            part.at[block(over, half, half)],
            landed.at[1, pl.ds(half, half)],
            sems,
            3,
            {"ctx": over},
        ),
    ]


def sum_pass(copies, part, bufs, sems):
    if lax.axis_size("ctx") != 4:
        return
    rows = part.shape[0] // 4
    half = rows // 2

    def rows_of(owner, first):
        return pl.ds(pl.multiple_of(owner * rows + first, half), half)

    me, side, over, across = square()
    relay, passed, landed = bufs
    copies[0].wait_recv()
    passed[0] = (part[rows_of(over, 0), :].astype(F32) + relay[0].astype(F32)).astype(BF16)
    copies.append(
        send(passed.at[0], landed.at[1, pl.ds(0, half)], sems, 4, {"ctx": over})
    )
    copies[1].wait_recv()
    passed[1] = (part[rows_of(side, half), :].astype(F32) + relay[1].astype(F32)).astype(
        BF16
    )
    copies.append(
        send(passed.at[1], landed.at[0, pl.ds(half, half)], sems, 5, {"ctx": side})
    )


def sum_rest(copies, part, bufs):
    size = lax.axis_size("ctx")
    me = lax.axis_index("ctx")
    rows = part.shape[0] // size
    half = rows // 2

    def rows_of(owner, first):
        return pl.ds(pl.multiple_of(owner * rows + first, half), half)

    if size != 4:
        for copy in copies:
            copy.wait()

        def read(first):
            total = part[rows_of(me, first), :].astype(F32)
            for step in range(1, size):
                total = total + bufs[0][step - 1, pl.ds(first, half), :].astype(F32)
            return total

        return read
    relay, passed, landed = bufs
    for copy in copies:
        copy.wait_send()
    for copy in copies[2:]:
        copy.wait_recv()

    def read(first):
        return (
            part[rows_of(me, first), :].astype(F32)
            + landed[0, pl.ds(first, half), :].astype(F32)
            + landed[1, pl.ds(first, half), :].astype(F32)
        )

    return read


def row_scale(values):
    return lax.rsqrt(jnp.mean(values * values, axis=-1, keepdims=True) + NORM_EPS)


def first_kernel(
    starts, origin, x, dy, gain, freq, x_low, dy_low, table, normed_all, *scratch
):
    move, normed, send_one, recv_one, local = scratch
    me = lax.axis_index("ctx")
    row = lax.broadcasted_iota(jnp.int32, move.shape, 0)
    move[...] = jnp.where(row == origin[...], 1.0, 0.0).astype(BF16)
    values = dot(x[...], move[...], 1, 0)
    x_low[...] = values.astype(BF16)
    normed[...] = (values * row_scale(values) * gain[...]).astype(BF16)
    meet(("ctx",))
    sems = (send_one, recv_one)
    copies = gather_start(normed, normed_all, sems, 0)
    own = load(normed, normed_all.at[me], local)
    dy_low[...] = dot(dy[...], move[...], 1, 0).astype(BF16)
    gather_pass(copies, normed_all, sems, 0)
    times = lax.broadcasted_iota(jnp.int32, (table.shape[0], 1), 0)
    angles = (times - doc_first(starts, times)).astype(F32) * freq[...]
    lane = lax.broadcasted_iota(jnp.int32, angles.shape, 1)
    sine = jnp.sin(angles)
    sine = jnp.where(lane % HD < HD // 2, -sine, sine)
    table[...] = jnp.where(lane < HD, jnp.cos(angles), sine)
    gather_end(copies)
    own.wait()


def middle_kernel(part, x, gain, middle, normed_all, *scratch):
    bufs, (normed, send_one, recv_one, send_two, recv_two, local) = scratch[:-6], scratch[-6:]
    me = lax.axis_index("ctx")
    meet(("ctx",))
    copies = sum_start(part, bufs, (send_one, recv_one))
    sum_pass(copies, part, bufs, (send_one, recv_one))
    read = sum_rest(copies, part, bufs)
    half = x.shape[0] // 2
    for first in (0, half):
        rows = pl.ds(first, half)
        values = x[rows, :].astype(F32) + read(first)
        middle[rows, :] = values
        normed[rows, :] = (values * row_scale(values) * gain[...]).astype(BF16)
    sems = (send_two, recv_two)
    copies = gather_start(normed, normed_all, sems, 0)
    own = load(normed, normed_all.at[me], local)
    gather_rest(copies, normed_all, sems, 0)
    own.wait()


def column_tiles(total, body):
    def step(tile, carry):
        body(pl.multiple_of(tile * 256, 256), 256)
        return carry

    lax.fori_loop(0, total // 256, step, 0)
    if total % 256:
        body(total - total % 256, total % 256)


def turn(source, target):
    for first in range(0, source.shape[0], HALF):
        rows = slice(first, first + HALF)
        target[:, rows] = source[rows, :].T


def middle_back_kernel(
    part,
    middle,
    dy,
    gain,
    x_all,
    dy_all,
    hidden_one,
    hidden_two,
    grad_gu,
    w_one,
    w_two,
    grad,
    gain_grad,
    down_sum,
    grad_all,
    rest_grad,
    weight_grad,
    out,
    *scratch,
):
    bufs = scratch[:-21]
    low, x_buf, gu_buf, turned, weight_buf, rest_buf, down_grad, out_buf = scratch[-21:-13]
    hidden_bufs, down_bufs = scratch[-13:-11], scratch[-11:-9]
    home, coming, send_one, recv_one, send_two, recv_two, send_three, recv_three, local = (
        scratch[-9:]
    )
    me = lax.axis_index("ctx")
    chips = lax.axis_size("fsdp") // 2
    line = (send_three, recv_three)
    meet(("ctx", "fsdp"))
    copies = sum_start(part, bufs, (send_one, recv_one))
    width_one, width_two = hidden_one.shape[1], hidden_two.shape[1]
    gu_width = grad_gu.shape[1]
    loads = [
        load(source, target, local.at[item])
        for item, (source, target) in enumerate(
            (
                (dy_all, x_buf),
                (hidden_one, hidden_bufs[0]),
                (hidden_two, hidden_bufs[1]),
                (grad_gu, gu_buf),
                (w_one.at[:, pl.ds(2 * width_one, width_one)], down_bufs[0]),
                (w_two.at[:, pl.ds(2 * width_two, width_two)], down_bufs[1]),
            )
        )
    ]
    loads[0].wait()
    turn(x_buf, turned)
    loads.append(load(x_all, x_buf, local.at[6]))
    loads[1].wait()

    def product(target, column, right, begin=0, count=None):
        def tile(first, width):
            target[:, pl.ds(column + first, width)] = dot(
                turned[...], right[:, pl.ds(begin + first, width)], 1, 0
            ).astype(BF16)

        column_tiles(right.shape[1] if count is None else count, tile)

    width_line = down_grad.shape[1]
    product(down_grad, 0, hidden_bufs[0], 0, width_line)
    home_copies = line_start(down_grad, home, line, 0)
    product(rest_buf, 0, hidden_bufs[0], width_line, width_one - width_line)
    stores = [load(rest_buf, rest_grad, local.at[10])]
    sum_pass(copies, part, bufs, (send_one, recv_one))
    line_home(home_copies, down_grad, home)
    line_step(chips - 1, home, coming, line, chips)
    loads[2].wait()
    product(weight_buf, gu_width, hidden_bufs[1])
    loads[6].wait()
    turn(x_buf, turned)
    loads[3].wait()
    product(weight_buf, 0, gu_buf)
    stores.append(load(weight_buf, weight_grad, local.at[7]))
    if chips > 2:
        line_step(chips - 2, home, coming, line, chips)
    read = sum_rest(copies, part, bufs)
    half = dy.shape[0] // 2
    total = jnp.zeros((1, D), F32)
    for first in (0, half):
        rows = pl.ds(first, half)
        values = middle[rows, :]
        root = row_scale(values)
        unit = values * root
        back = read(first)
        total = total + jnp.sum(back * unit, axis=0, keepdims=True)
        back = back * gain[...]
        back = root * (back - unit * jnp.mean(back * unit, axis=-1, keepdims=True))
        back = back + dy[rows, :].astype(F32)
        grad[rows, :] = back
        low[rows, :] = back.astype(BF16)
    gain_grad[...] = total
    sems = (send_two, recv_two)
    copies = gather_start(low, grad_all, sems, 0)
    stores.append(load(low, grad_all.at[me], local.at[8]))
    loads[4].wait()
    loads[5].wait()

    def out_tile(first, width):
        columns = pl.ds(first, width)
        out_buf[:, columns] = (
            dot(hidden_bufs[0][...], down_bufs[0][columns, :], 1, 1)
            + dot(hidden_bufs[1][...], down_bufs[1][columns, :], 1, 1)
        ).astype(BF16)

    column_tiles(D, out_tile)
    stores.append(load(out_buf, out, local.at[9]))
    gather_pass(copies, grad_all, sems, 0)
    for reach in range(min(chips - 1, max(chips - 3, 1)), 0, -1):
        line_step(reach, home, coming, line, chips)
    line_end(home_copies, home, coming, line, chips)
    chip = lax.axis_index("fsdp") // 2
    rows = down_sum.shape[1]
    for index in range(down_sum.shape[0]):
        down_sum[index] = home[chip, index * rows : (index + 1) * rows, :]
    gather_end(copies)
    for copy in stores:
        copy.wait()


def line_start(grad, home, sems, base):
    me = lax.axis_index("fsdp")
    chips = lax.axis_size("fsdp") // 2
    core = lax.rem(me, 2)
    rows = grad.shape[0] // (2 * chips)
    copies = []
    for chip in range(chips):
        theirs = pl.ds(pl.multiple_of((2 * chip + 1 - core) * rows, rows), rows)
        copies.append(
            send(grad.at[theirs], home.at[chip], sems, base + chip, {"fsdp": me + 1 - 2 * core})
        )
    return copies


def line_home(copies, grad, home):
    me = lax.axis_index("fsdp")
    chips = lax.axis_size("fsdp") // 2
    core = lax.rem(me, 2)
    rows = grad.shape[0] // (2 * chips)
    for chip in range(chips):
        copies[chip].wait_recv()
        mine = pl.ds(pl.multiple_of((2 * chip + core) * rows, rows), rows)
        home[chip] = (home[chip].astype(F32) + grad[mine, :].astype(F32)).astype(BF16)


def line_copies(reach, home, coming, sems, base):
    me = lax.axis_index("fsdp")
    chips = lax.axis_size("fsdp") // 2
    chip = me // 2
    found = []
    for side, way in ((0, 1), (1, -1)):
        owner = lax.rem(chip + way * reach + chips, chips)
        copy = pltpu.make_async_remote_copy(
            src_ref=home.at[owner],
            dst_ref=coming.at[side, reach - 1],
            send_sem=sems[0].at[base + 2 * reach + side],
            recv_sem=sems[1].at[base + 2 * reach + side],
            device_id={"fsdp": lax.rem(me + 2 * way + 2 * chips, 2 * chips)},
            device_id_type=MESH,
        )
        if way == 1:
            sent = chip + reach <= chips - 1
            got = (chip >= 1) & (chip + reach <= chips)
            more = (chip >= 1) & sent
        else:
            sent = chip >= reach
            got = (chip <= chips - 2) & (chip + 1 >= reach)
            more = (chip <= chips - 2) & sent
        found.append((side, owner, copy, sent, got, more))
    return found


def line_step(reach, home, coming, sems, base):
    chips = lax.axis_size("fsdp") // 2
    if reach < chips - 1:
        for _, _, copy, _, got, _ in line_copies(reach + 1, home, coming, sems, base):
            pl.when(got)(copy.wait_recv)
    for side, owner, copy, sent, _, more in line_copies(reach, home, coming, sems, base):
        if reach < chips - 1:

            @pl.when(more)
            def _(side=side, owner=owner):
                home[owner] = (
                    home[owner].astype(F32) + coming[side, reach].astype(F32)
                ).astype(BF16)

        pl.when(sent)(copy.start)


def line_end(copies, home, coming, sems, base):
    me = lax.axis_index("fsdp")
    chips = lax.axis_size("fsdp") // 2
    chip = me // 2
    for side, _, copy, _, got, _ in line_copies(1, home, coming, sems, base):

        @pl.when(got)
        def _(side=side, copy=copy):
            copy.wait_recv()
            home[chip] = (home[chip].astype(F32) + coming[side, 0].astype(F32)).astype(BF16)

    for copy in copies:
        copy.wait_send()
    for reach in range(1, chips):
        for _, _, copy, sent, _, _ in line_copies(reach, home, coming, sems, base):
            pl.when(sent)(copy.wait_send)


def remote_call(
    kernel, out_shape, args, collective_id, micros, scratch, in_hbm=(), smem=0, args_in_hbm=0
):
    return pl.pallas_call(
        kernel,
        out_shape=out_shape,
        in_specs=[pl.BlockSpec(memory_space=pltpu.SMEM)] * smem
        + [pl.BlockSpec(memory_space=pltpu.VMEM)] * (len(args) - smem - args_in_hbm)
        + [pl.BlockSpec(memory_space=pl.ANY)] * args_in_hbm,
        out_specs=[
            pl.BlockSpec(memory_space=pl.ANY if item in in_hbm else pltpu.VMEM)
            for item in range(len(out_shape))
        ],
        scratch_shapes=scratch,
        compiler_params=remote_params(collective_id),
        cost_estimate=cost(micros),
    )(*args)


def adam_update(param_now, grad_now, moment_old_one, moment_old_two, step_rate, decay_rate):
    first_new = BETA_ONE * moment_old_one + (1.0 - BETA_ONE) * grad_now
    second_new = BETA_TWO * moment_old_two + (1.0 - BETA_TWO) * grad_now * grad_now
    ratio = (first_new * (1.0 / (1.0 - BETA_ONE**STEP))) / (
        jnp.sqrt(second_new * (1.0 / (1.0 - BETA_TWO**STEP))) + ADAM_EPS
    )
    return (first_new, second_new, param_now - step_rate * (ratio + decay_rate * param_now))


def joined_ranges(segments):
    ranges = []
    for number in sorted(range(len(segments)), key=lambda n: segments[n][3]):
        column, width = segments[number][3:]
        if ranges and ranges[-1][0] + ranges[-1][1] == column:
            first, so_far, numbers = ranges[-1]
            ranges[-1] = (first, so_far + width, numbers + (number,))
        else:
            ranges.append((column, width, (number,)))
    return ranges


def adam_kernel(segments, pieces, held, *refs):
    me = lax.axis_index("ctx")
    grads = refs[:pieces]
    olds = refs[pieces : pieces + 3]
    news = refs[pieces + 3 + held : pieces + 3 + held + 4]
    grad_buf, old_buf, low_buf, grad_sem, in_sem, out_sem = refs[pieces + 3 + held + 4 :]
    base = min(segment[3] for segment in segments)
    ranges = joined_ranges(segments)
    loads = []
    for place, (column, width, numbers) in enumerate(ranges):
        here, there = pl.ds(column - base, width), pl.ds(column, width)
        copies = [
            load(olds[item].at[:, there], old_buf.at[item, :, here], in_sem.at[item, place])
            for item in range(3)
        ]
        for number in numbers:
            piece, index, first, start, count = segments[number]
            columns = pl.ds(first, count)
            for source_number, source in enumerate(grads):
                if piece not in (None, source_number):
                    continue
                copy = pltpu.make_async_copy(
                    source.at[:, columns] if piece is None else source.at[index, :, columns],
                    grad_buf.at[:, pl.ds(start - base, count)],
                    grad_sem.at[number],
                )
                if piece is None:
                    pl.when(me == index ^ source_number)(copy.start)
                else:
                    copy.start()
            copies.append(copy)
        loads.append(copies)
    stores = []
    for place, (column, width, numbers) in enumerate(ranges):
        for copy in loads[place]:
            copy.wait()
        here, there = pl.ds(column - base, width), pl.ds(column, width)
        for first in range(0, width, 256):
            part = pl.ds(column - base + first, min(256, width - first))
            first_new, second_new, master = adam_update(
                old_buf[0, :, part],
                grad_buf[:, part].astype(F32),
                old_buf[1, :, part],
                old_buf[2, :, part],
                LEARN_RATE,
                WEIGHT_DECAY,
            )
            old_buf[0, :, part] = master
            old_buf[1, :, part] = first_new
            old_buf[2, :, part] = second_new
            low_buf[:, part] = master.astype(BF16)
        for item, source in enumerate(
            (
                old_buf.at[1, :, here],
                old_buf.at[2, :, here],
                old_buf.at[0, :, here],
                low_buf.at[:, here],
            )
        ):
            stores.append(load(source, news[item].at[:, there], out_sem.at[item, place]))
    for copy in stores:
        copy.wait()


def adam(segments, grads, olds, held, micros):
    rows, columns = olds[0].shape
    span = max(s[3] + s[4] for s in segments) - min(s[3] for s in segments)
    held = [] if held is None else list(held)
    args = list(grads) + list(olds) + held
    return pl.pallas_call(
        functools.partial(adam_kernel, tuple(segments), len(grads), len(held)),
        out_shape=[jax.ShapeDtypeStruct((rows, columns), F32)] * 3
        + [jax.ShapeDtypeStruct((rows, columns), BF16)],
        in_specs=[pl.BlockSpec(memory_space=pl.ANY)] * len(args),
        out_specs=[pl.BlockSpec(memory_space=pl.ANY)] * 4,
        input_output_aliases={len(grads) + 3 + item: item for item in range(len(held))},
        scratch_shapes=[
            pltpu.VMEM((rows, span), BF16),
            pltpu.VMEM((3, rows, span), F32),
            pltpu.VMEM((rows, span), BF16),
            pltpu.SemaphoreType.DMA((len(segments),)),
            pltpu.SemaphoreType.DMA((3, len(segments))),
            pltpu.SemaphoreType.DMA((4, len(segments))),
        ],
        compiler_params=pltpu.CompilerParams(vmem_limit_bytes=VMEM_LIMIT),
        cost_estimate=cost(micros),
    )(*args)


def head_mean(values, ones):
    high = values.astype(BF16)
    rest = (values - high.astype(F32)).astype(BF16)
    return (dot(high, ones, 1, 0) + dot(rest, ones, 1, 0)) * (1.0 / HD)


def head_ones(width):
    row = lax.broadcasted_iota(jnp.int32, (width, width), 0) // HD
    col = lax.broadcasted_iota(jnp.int32, (width, width), 1) // HD
    return jnp.where(row == col, 1.0, 0.0).astype(BF16)


def partner(values):
    width = values.shape[-1]
    lane = lax.broadcasted_iota(jnp.int32, values.shape, 1)
    return jnp.where(
        lane % HD < HD // 2,
        pltpu.roll(values, width - HD // 2, 1),
        pltpu.roll(values, HD // 2, 1),
    )


def widen(table, width):
    return [
        jnp.concatenate([part] * (width // HD), axis=-1)
        for part in (table[:, :HD], table[:, HD:])
    ]


def doc_first(starts, times):
    first = jnp.zeros_like(times)
    for item in range(starts.shape[0]):
        first = jnp.where(starts[item] <= times, starts[item], first)
    return first


def block_mask(starts, block, keys):
    shape = (keys, GROUP * HALF)
    times = block * HALF + lax.broadcasted_iota(jnp.int32, (1, GROUP * HALF), 1) % HALF
    key = lax.broadcasted_iota(jnp.int32, shape, 0)
    return (key >= doc_first(starts, times)) & (key <= times)


def stack_heads(ref, rows, group):
    return jnp.concatenate(
        [
            ref[rows, (group * GROUP + h) * HD : (group * GROUP + h + 1) * HD]
            for h in range(GROUP)
        ],
        axis=0,
    )


def unstack_heads(turned):
    wide = turned.T
    return [wide[h * HALF : (h + 1) * HALF, :] for h in range(GROUP)]


def attend_kernel(
    blocks,
    groups,
    place,
    order,
    starts,
    table,
    gain,
    normed_in,
    weights_from,
    dy,
    swap_in,
    part,
    qk,
    q,
    k,
    v,
    o_held,
    lse,
    dy_all,
    swap_out,
    normed,
    weights_in,
    joined,
    o,
    send_sem,
    recv_sem,
    local,
):
    sems = (send_sem, recv_sem)
    me = lax.axis_index("ctx")
    qk_width = qk.shape[1]
    q_width = q.shape[1]
    qkv_width = qk_width + v.shape[1]
    ones = head_ones(qk_width)
    meet(("ctx",))
    loads = [
        load(normed_in, normed, local.at[0]),
        load(weights_from, weights_in, local.at[1]),
    ]
    swap_copies = swap_start(swap_in, swap_out, sems, GATHER_SEMS)
    copies = gather_start(dy, dy_all, sems, 0)
    own_copies = [
        load(swap_in.at[me], swap_out.at[me], local.at[2]),
        load(dy, dy_all.at[me], local.at[3]),
    ]
    for copy in loads:
        copy.wait()
    for block in range(blocks):
        joined[block] = dot(
            normed[block * HALF : (block + 1) * HALF, :], weights_in[:, :qkv_width], 1, 0
        )
    for block in range(blocks):
        to = slice(block * HALF, (block + 1) * HALF)
        values = joined[place[block]]
        v[to, :] = values[:, qk_width:].astype(BF16)
        values = values[:, :qk_width]
        qk[to, :] = values
        turned = values * lax.rsqrt(head_mean(values * values, ones) + NORM_EPS) * gain[...]
        cosine, sine = widen(table[to, :], qk_width)
        turned = turned * cosine + partner(turned) * sine
        turned = turned.astype(BF16)
        q[to, :] = turned[:, :q_width]
        k[to, :] = turned[:, q_width:]
    for block in range(blocks):
        rows = slice(block * HALF, (block + 1) * HALF)
        keys = (block + 1) * HALF
        mask = block_mask(starts, block, keys)
        pieces = []
        for group in range(groups):
            lanes = slice(group * HD, (group + 1) * HD)
            queries = stack_heads(q, rows, group)
            scores = dot(k[:keys, lanes], queries, 1, 1) * SCALE
            weights = jnp.where(mask, jnp.exp(scores), 0.0)
            sums = jnp.sum(weights, axis=0, keepdims=True)
            lse[block, group : group + 1, :] = jnp.log(sums)
            mixed = dot(v[:keys, lanes], weights.astype(BF16), 0, 0) / sums
            pieces += unstack_heads(mixed)
        o[block] = jnp.concatenate(pieces, axis=1).astype(BF16)
    for block in range(blocks):
        o_held[block * HALF : (block + 1) * HALF, :] = o[order[block]]
    for first in range(0, D, 512):
        part[:, first : first + 512] = dot(
            o_held[...], weights_in[first : first + 512, qkv_width:], 1, 1
        ).astype(BF16)
    gather_rest(copies, dy_all, sems, 0)
    for copy in swap_copies:
        copy.wait()
    for copy in own_copies:
        copy.wait()


def attend_back_kernel(
    blocks,
    groups,
    place,
    order,
    starts,
    lse,
    gain,
    part,
    rest_grad,
    *refs,
):
    sources, refs = refs[:9], refs[9:]
    out, joined, gain_grad, out_grad, rest_sum = refs[:5]
    targets, refs = refs[5:14], refs[14:]
    grad_all, weights_in, q, k, v, o, qk, table, middle = targets
    bufs, (do, dq, dkv, turned, home, coming) = refs[:-11], refs[-11:-5]
    send_one, recv_one, send_two, recv_two, local = refs[-5:]
    line = (send_two, recv_two)
    chips = lax.axis_size("fsdp") // 2
    out_sems = (send_one, recv_one)
    qk_width = qk.shape[2]
    qkv_width = qk_width + v.shape[1]
    ones = head_ones(qk_width)
    meet(("ctx", "fsdp"))
    home_copies = line_start(rest_grad, home, line, 0)
    out_copies = sum_start(part, bufs, out_sems)
    loads = [
        load(source, target, local.at[item])
        for item, (source, target) in enumerate(zip(sources, targets))
    ]
    for copy in loads[:6]:
        copy.wait()
    for block in range(blocks):
        do[block * HALF : (block + 1) * HALF, :] = dot(
            grad_all[place[block]], weights_in[:, qkv_width:], 1, 0
        ).astype(BF16)
    for block in range(blocks):
        turned[:, block * HALF : (block + 1) * HALF] = grad_all[block].T
    for first in range(0, D, 512):
        rows = slice(first, first + 512)
        out_grad[rows, :] = dot(turned[rows, :], o[...], 1, 0).astype(BF16)
    dkv[...] = jnp.zeros_like(dkv)
    line_home(home_copies, rest_grad, home)
    line_step(chips - 1, home, coming, line, chips)
    reach = chips - 2
    for block in range(blocks):
        if block == blocks // 2:
            sum_pass(out_copies, part, bufs, out_sems)
        if block >= blocks * 3 // 4 and reach > 1:
            line_step(reach, home, coming, line, chips)
            reach -= 1
        rows = slice(block * HALF, (block + 1) * HALF)
        keys = (block + 1) * HALF
        mask = block_mask(starts, block, keys)
        pieces = []
        dk_add = []
        dv_add = []
        for group in range(groups):
            lanes = slice(group * HD, (group + 1) * HD)
            queries = stack_heads(q, rows, group)
            outs = stack_heads(do, rows, group)
            key_rows = k[:keys, lanes]
            scores = dot(key_rows, queries, 1, 1) * SCALE
            weights = jnp.where(
                mask, jnp.exp(scores - lse[block, group : group + 1, :]), 0.0
            )
            back = dot(v[:keys, lanes], outs, 1, 1)
            delta = jnp.sum(weights * back, axis=0, keepdims=True)
            grads = (weights * (back - delta)).astype(BF16)
            pieces += unstack_heads(dot(key_rows, grads, 0, 0) * SCALE)
            dk_add.append(dot(grads, queries, 1, 0) * SCALE)
            dv_add.append(dot(weights.astype(BF16), outs, 1, 0))
        dq[block] = jnp.concatenate(pieces, axis=1)
        dkv[: block + 1] += jnp.concatenate(dk_add + dv_add, axis=1).reshape(
            (block + 1,) + dkv.shape[1:]
        )
    for step in range(reach, 0, -1):
        line_step(step, home, coming, line, chips)
    gain_row = jnp.zeros((1, qk_width), F32)
    for copy in loads[6:]:
        copy.wait()
    for block in range(blocks):
        here = order[block]
        values = qk[here]
        root = lax.rsqrt(head_mean(values * values, ones) + NORM_EPS)
        unit = values * root
        grad_kv = dkv[here]
        kv_width = grad_kv.shape[1] // 2
        grad = jnp.concatenate([dq[here], grad_kv[:, :kv_width]], axis=1)
        cosine, sine = widen(table[here], qk_width)
        grad = grad * cosine - partner(grad) * sine
        gain_row = gain_row + jnp.sum(grad * unit, axis=0, keepdims=True)
        grad = grad * gain[...]
        grad = root * (grad - unit * head_mean(grad * unit, ones))
        joined[block * HALF : (block + 1) * HALF, :] = jnp.concatenate(
            [grad, grad_kv[:, kv_width:]], axis=1
        ).astype(BF16)
    gain_grad[...] = gain_row
    read = sum_rest(out_copies, part, bufs)
    half = middle.shape[0] // 2
    for first in (0, half):
        rows = pl.ds(first, half)
        out[rows, :] = (middle[rows, :] + read(first)).astype(BF16)
    line_end(home_copies, home, coming, line, chips)
    chip = lax.axis_index("fsdp") // 2
    owned_rows = rest_sum.shape[1]
    for index in range(rest_sum.shape[0]):
        rest_sum[index] = home[chip, index * owned_rows : (index + 1) * owned_rows, :]


def tail_kernel(
    swaps,
    joined,
    out_grad,
    gain_row,
    attn_gain,
    ffn_gain_grad,
    *refs,
):
    sources, refs = refs[:4], refs[4:]
    swap_in, refs = refs[:swaps], refs[swaps:]
    grad_tokens, gains, attn_own = refs[:3]
    swap_out, refs = refs[3 : 3 + swaps], refs[3 + swaps :]
    targets, refs = refs[:4], refs[4:]
    weights_in, normed, x, grad_middle = targets
    back_bufs, refs = refs[:-20], refs[-20:]
    turned, part, owned, ctx_box, fsdp_box = refs[:5]
    send_two, recv_two, send_three, recv_three, send_four, recv_four, local = refs[5:12]
    halves = (refs[12:15] + ((send_three, recv_three),), refs[15:18] + (refs[18:],))
    back_sems = (send_two, recv_two)
    line, small = (send_three, recv_three), (send_four, recv_four)
    size = lax.axis_size("ctx")
    me = lax.axis_index("ctx")
    chips = lax.axis_size("fsdp") // 2
    step_base = chips
    swap_base = step_base + 2 * chips
    qkv_width = joined.shape[1]
    qk_width = gain_row.shape[1]
    cut = halves[0][0].shape[1]
    half = x.shape[0] // 2
    loads = [
        load(source, target, local.at[item])
        for item, (source, target) in enumerate(zip(sources, targets))
    ]
    meet(("ctx", "fsdp"))
    swap_copies = []
    own_copies = []
    for item in range(swaps):
        swap_copies += swap_start(
            swap_in[item], swap_out[item], line, swap_base + (item + 1) * size
        )
        own_copies.append(
            load(swap_in[item].at[me], swap_out[item].at[me], local.at[4 + item])
        )
    for copy in loads:
        copy.wait()
    for first in range(0, D, 512):
        part[:, first : first + 512] = dot(
            joined[...], weights_in[first : first + 512, :qkv_width], 1, 1
        ).astype(BF16)
    back_copies = sum_start(part, back_bufs, back_sems)
    turn(normed, turned)
    for first in range(0, D, 512):
        rows = slice(first, first + 512)
        columns = dot(turned[rows, :], joined[...], 1, 0).astype(BF16)
        halves[0][0][rows, :] = columns[:, :cut]
        halves[1][0][rows, : qkv_width - cut] = columns[:, cut:]
    halves[1][0][:, qkv_width - cut :] = out_grad[...]
    home_copies = [line_start(grad, home, sems, 0) for grad, home, _, sems in halves]

    def step_all(reach):
        for _, home, coming, sems in halves:
            line_step(reach, home, coming, sems, step_base)

    for copies, (grad, home, coming, sems) in zip(home_copies, halves):
        line_home(copies, grad, home)
        line_step(chips - 1, home, coming, sems, step_base)
    sum_pass(back_copies, part, back_bufs, back_sems)
    for reach in range(chips - 2, 1, -1):
        step_all(reach)
    read = sum_rest(back_copies, part, back_bufs)
    total = jnp.zeros((1, D), F32)
    for first in (0, half):
        rows = pl.ds(first, half)
        values = x[rows, :].astype(F32)
        root = row_scale(values)
        unit = values * root
        back = read(first)
        total = total + jnp.sum(back * unit, axis=0, keepdims=True)
        back = back * attn_gain[...]
        back = root * (back - unit * jnp.mean(back * unit, axis=-1, keepdims=True))
        grad_tokens[rows, :] = grad_middle[rows, :] + back

    def spread_start(axis, box, value, base):
        index = lax.axis_index(axis)
        axis_size = lax.axis_size(axis)
        box[index] = value
        return [
            send(
                box.at[index],
                box.at[index],
                small,
                base + step,
                {axis: lax.rem(index + step, axis_size)},
            )
            for step in range(1, axis_size)
        ]

    def spread_end(copies, box):
        for copy in copies:
            copy.wait()
        summed = box[0]
        for item in range(1, box.shape[0]):
            summed = summed + box[item]
        return summed

    ctx_copies = spread_start(
        "ctx",
        ctx_box,
        jnp.concatenate(
            [
                total,
                ffn_gain_grad[...],
                jnp.concatenate([gain_row[...], jnp.zeros((1, D - qk_width), F32)], axis=1),
                jnp.zeros((5, D), F32),
            ],
            axis=0,
        ),
        0,
    )
    step_all(1)
    fsdp_copies = spread_start("fsdp", fsdp_box, spread_end(ctx_copies, ctx_box), size)
    for copies, (_, home, coming, sems) in zip(home_copies, halves):
        line_end(copies, home, coming, sems, step_base)
    chip = lax.axis_index("fsdp") // 2
    owned_rows = owned.shape[1]
    for index in range(size):
        rows = slice(index * owned_rows, (index + 1) * owned_rows)
        owned[index] = jnp.concatenate([half[1][chip, rows, :] for half in halves], axis=1)
    swap_copies += swap_start(owned, attn_own, line, swap_base)
    attn_own[me] = owned[me]
    gains[...] = spread_end(fsdp_copies, fsdp_box)
    for copy in swap_copies:
        copy.wait()
    for copy in own_copies:
        copy.wait()


def rms_scale(values_in, gain_vec):
    return (
        values_in
        * lax.rsqrt(jnp.mean(values_in * values_in, axis=-1, keepdims=True) + NORM_EPS)
        * gain_vec
    )


def inverse_freq():
    return 1.0 / ROPE_BASE ** (jnp.arange(0, HD, 2).astype(F32) / HD)


def shards(
    tokens,
    cotangent,
    doc_starts,
    block_order,
    master_weights,
    moment_one,
    moment_two,
    gains,
    gains_moment_one,
    gains_moment_two,
):
    nctx = lax.axis_size("ctx")
    nfsdp = lax.axis_size("fsdp")
    own_rows = master_weights.shape[0]
    tok_rows = tokens.shape[1]
    stream_len = tok_rows * nctx
    blocks = stream_len // HALF
    groups = KVHEADS // nctx
    q_width = D // nctx
    kv_width = KVD // nctx
    qk_width = q_width + kv_width
    qkv_width = qk_width + kv_width
    tiles = FF // 128
    ff_tiles = -(-tiles // nctx)
    ff_width = ff_tiles * 128
    bundles = 2
    cuts = [0, (ff_tiles * 5 + 3) // 7 * 128, ff_width]

    low = master_weights.astype(BF16)

    def ff_part(base, index, start, stop):
        first = index * ff_width + start
        last = index * ff_width + stop
        real_first, real_last = min(first, FF), min(last, FF)
        part = low[:, base + real_first : base + real_last]
        if real_last - real_first < last - first:
            part = jnp.pad(part, ((0, 0), (0, (last - first) - (real_last - real_first))))
        return part

    def attn_part(index):
        return jnp.concatenate(
            [
                low[:, index * q_width : (index + 1) * q_width],
                low[:, D + index * kv_width : D + (index + 1) * kv_width],
                low[:, D + KVD + index * kv_width : D + KVD + (index + 1) * kv_width],
                low[:, QKVC + index * q_width : QKVC + (index + 1) * q_width],
            ],
            axis=1,
        )

    gate_base = QKVC + D
    bases = (gate_base, gate_base + FF, gate_base + 2 * FF)
    attn_send = jnp.stack([attn_part(c) for c in range(nctx)])
    ff_send = [
        jnp.stack(
            [
                jnp.concatenate(
                    [ff_part(base, c, cuts[b], cuts[b + 1]) for base in bases], axis=1
                )
                for c in range(nctx)
            ]
        )
        for b in range(bundles)
    ]

    def gather_rows(piece):
        return lax.all_gather(
            piece.reshape(nctx * own_rows, piece.shape[-1]), "fsdp", axis=0, tiled=True
        )

    def spread(active):
        return (
            active.reshape(active.shape[0], nctx, nfsdp, own_rows)
            .transpose(0, 2, 1, 3)
            .reshape(active.shape[0], D)
        )

    def unspread(active):
        return (
            active.reshape(active.shape[0], nfsdp, nctx, own_rows)
            .transpose(0, 2, 1, 3)
            .reshape(active.shape[0], D)
        )

    dma = pltpu.SemaphoreType.DMA
    all_low = jax.ShapeDtypeStruct((nctx, tok_rows, D), BF16)
    own_low = jax.ShapeDtypeStruct((tok_rows, D), BF16)
    own_f32 = jax.ShapeDtypeStruct((tok_rows, D), F32)
    row_f32 = jax.ShapeDtypeStruct((1, D), F32)
    g_attn = spread(gains[None, :D])
    g_ffn = spread(gains[None, D : 2 * D])
    order = block_order.reshape(blocks)
    place = jnp.argsort(order).astype(jnp.int32)
    starts = doc_starts[0]

    (attn_held,) = exchange(("swap",), [attn_send], 0, 10)
    w_attn = gather_rows(attn_held)
    first_send, attn_held = lax.optimization_barrier((ff_send[0], attn_held))
    (first_held,) = exchange(("swap",), [first_send], 1, 16)
    table_shape = jax.ShapeDtypeStruct((stream_len, 2 * HD), F32)
    origin = spread(jnp.arange(D, dtype=jnp.int32)[None])
    starts_late, first_held = lax.optimization_barrier((starts, first_held))
    x_low, dy_low, table, normed_all = remote_call(
        first_kernel,
        [own_low, own_low, table_shape, all_low],
        (
            starts_late,
            origin,
            tokens[0],
            cotangent[0],
            g_attn,
            jnp.tile(inverse_freq(), 4)[None],
        ),
        2,
        33,
        [
            pltpu.VMEM((D, D), BF16),
            pltpu.VMEM((tok_rows, D), BF16),
            dma((GATHER_SEMS,)),
            dma((GATHER_SEMS,)),
            dma,
        ],
        (3,),
        1,
    )
    normed_all = normed_all.reshape(stream_len, D)

    g_query = gains[2 * D : 2 * D + HD]
    g_key = gains[2 * D + HD :]
    qk_gain = jnp.concatenate(
        [jnp.tile(g_query, q_width // HD), jnp.tile(g_key, kv_width // HD)]
    )[None]

    low_stream = pltpu.VMEM((stream_len, D), BF16)
    heads_low = pltpu.VMEM((stream_len, q_width), BF16)
    part, qk, q, k, v, mixed, lse, dy_all, second_held = remote_call(
        functools.partial(attend_kernel, blocks, groups),
        [
            jax.ShapeDtypeStruct((stream_len, D), BF16),
            jax.ShapeDtypeStruct((stream_len, qk_width), F32),
            jax.ShapeDtypeStruct((stream_len, q_width), BF16),
            jax.ShapeDtypeStruct((stream_len, kv_width), BF16),
            jax.ShapeDtypeStruct((stream_len, kv_width), BF16),
            jax.ShapeDtypeStruct((stream_len, q_width), BF16),
            jax.ShapeDtypeStruct((blocks, groups, GROUP * HALF), F32),
            all_low,
            jax.ShapeDtypeStruct(ff_send[1].shape, BF16),
        ],
        (place, order, starts, table, qk_gain, normed_all, w_attn, dy_low, ff_send[1]),
        3,
        42,
        [
            low_stream,
            pltpu.VMEM(w_attn.shape, BF16),
            pltpu.VMEM((blocks, HALF, qkv_width), F32),
            pltpu.VMEM((blocks, HALF, q_width), BF16),
            dma((GATHER_SEMS + nctx,)),
            dma((GATHER_SEMS + nctx,)),
            dma((4,)),
        ],
        (7, 8),
        3,
        4,
    )
    dy_all = dy_all.reshape(stream_len, D)
    w_ff = [gather_rows(first_held), gather_rows(second_held)]
    sum_bufs = sum_scratch(nctx, tok_rows)
    sum_sems = [dma((GATHER_SEMS,)), dma((GATHER_SEMS,))]
    norm_scratch = (
        sum_bufs + [pltpu.VMEM((tok_rows, D), BF16)] + sum_sems + sum_sems + [dma]
    )

    middle, normed_two_all = remote_call(
        middle_kernel,
        [own_f32, all_low],
        (part, x_low, g_ffn),
        4,
        57,
        norm_scratch,
        (1,),
    )
    normed_two_all = normed_two_all.reshape(stream_len, D)

    def sum_rows(grad):
        return lax.psum_scatter(grad, "fsdp", scatter_dimension=0, tiled=True).reshape(
            nctx, own_rows, grad.shape[-1]
        )

    def feed(b, x_all, dy):
        width = cuts[b + 1] - cuts[b]
        w_gu, w_down = w_ff[b][:, : 2 * width], w_ff[b][:, 2 * width :]
        gate_up = dot(x_all, w_gu, 1, 0).astype(BF16)
        gate, up = gate_up[:, :width].astype(F32), gate_up[:, width:].astype(F32)
        gated = jax.nn.sigmoid(gate)
        act = gate * gated
        hidden = (act * up).astype(BF16)
        back_hidden = dot(dy, w_down, 1, 0)
        grad_gu = jnp.concatenate(
            [back_hidden * up * (gated + act * (1.0 - gated)), back_hidden * act], axis=1
        ).astype(BF16)
        return hidden, grad_gu, dot(grad_gu, w_gu, 1, 1)

    hidden_one, grad_gu, back_partial = feed(0, normed_two_all, dy_all)
    gu_grad = dot(normed_two_all, grad_gu, 0, 0).astype(BF16)
    gu_grad, back_partial, w_ff[1] = lax.optimization_barrier((gu_grad, back_partial, w_ff[1]))
    width_two = cuts[2] - cuts[1]
    width_line = cuts[1] * 3 // 5 // 128 * 128
    width_rest = cuts[1] - width_line
    hidden_two, grad_gu, back_more = feed(1, normed_two_all, dy_all)
    back_partial = (back_partial + back_more).astype(BF16)
    gu_sum = sum_rows(gu_grad)
    chips = nfsdp // 2

    def line_scratch(columns):
        block = (nctx * own_rows, columns)
        return [pltpu.VMEM((chips,) + block, BF16), pltpu.VMEM((2, chips - 1) + block, BF16)]

    (
        grad_middle,
        grad_g_ffn,
        down_sum,
        grad_middle_all,
        rest_grad,
        last_grad,
        out_partial,
    ) = remote_call(
        middle_back_kernel,
        [
            own_f32,
            row_f32,
            jax.ShapeDtypeStruct((nctx, own_rows, width_line), BF16),
            all_low,
            jax.ShapeDtypeStruct((D, width_rest), BF16),
            jax.ShapeDtypeStruct((D, 3 * width_two), BF16),
            jax.ShapeDtypeStruct((stream_len, D), BF16),
        ],
        (
            back_partial,
            middle,
            dy_low,
            g_ffn,
            normed_two_all,
            dy_all,
            hidden_one,
            hidden_two,
            grad_gu,
            w_ff[0],
            w_ff[1],
        ),
        5,
        57,
        sum_bufs
        + [
            pltpu.VMEM((tok_rows, D), BF16),
            low_stream,
            pltpu.VMEM((stream_len, 2 * width_two), BF16),
            pltpu.VMEM((D, stream_len), BF16),
            pltpu.VMEM((D, 3 * width_two), BF16),
            pltpu.VMEM((D, width_rest), BF16),
            pltpu.VMEM((D, width_line), BF16),
            low_stream,
            pltpu.VMEM((stream_len, cuts[1]), BF16),
            pltpu.VMEM((stream_len, width_two), BF16),
            pltpu.VMEM((D, cuts[1]), BF16),
            pltpu.VMEM((D, width_two), BF16),
        ]
        + line_scratch(width_line)
        + sum_sems
        + sum_sems
        + [dma((3 * chips,)), dma((3 * chips,)), dma((11,))],
        (3, 4, 5, 6),
        0,
        7,
    )
    last_sum = sum_rows(last_grad)

    small = dma((nctx + nfsdp,))
    line_sems = dma((3 * chips + 4 * nctx,))
    own_shape = (nctx, own_rows, qkv_width + q_width)
    sources = (
        grad_middle_all.reshape(blocks, HALF, D),
        w_attn,
        q,
        k,
        v,
        mixed,
        qk.reshape(blocks, HALF, qk_width),
        table.reshape(blocks, HALF, 2 * HD),
        middle,
    )
    out_tokens, grad_joined, qk_gain_grad, out_grad, rest_sum = remote_call(
        functools.partial(attend_back_kernel, blocks, groups),
        [
            own_low,
            jax.ShapeDtypeStruct((stream_len, qkv_width), BF16),
            jax.ShapeDtypeStruct((1, qk_width), F32),
            jax.ShapeDtypeStruct((D, q_width), BF16),
            jax.ShapeDtypeStruct((nctx, own_rows, width_rest), BF16),
        ],
        (place, order, starts, lse, qk_gain, out_partial, rest_grad) + sources,
        6,
        45,
        [pltpu.VMEM(source.shape, source.dtype) for source in sources]
        + sum_bufs
        + [
            heads_low,
            pltpu.VMEM((blocks, HALF, q_width), F32),
            pltpu.VMEM((blocks, HALF, 2 * kv_width), F32),
            pltpu.VMEM((D, stream_len), BF16),
        ]
        + line_scratch(width_rest)
        + sum_sems
        + [dma((3 * chips,)), dma((3 * chips,)), dma((9,))],
        (),
        3,
        9,
    )
    sources = (w_attn, normed_all, x_low, grad_middle)
    half_width = (qkv_width + q_width) // 2
    grad_tokens, gain_sums, attn_own, gu_own, down_own, rest_own = remote_call(
        functools.partial(tail_kernel, 3),
        [
            own_f32,
            jax.ShapeDtypeStruct((8, D), F32),
            jax.ShapeDtypeStruct(own_shape, BF16),
            jax.ShapeDtypeStruct(gu_sum.shape, BF16),
            jax.ShapeDtypeStruct(down_sum.shape, BF16),
            jax.ShapeDtypeStruct(rest_sum.shape, BF16),
        ],
        (grad_joined, out_grad, qk_gain_grad, g_attn, grad_g_ffn) + sources + (gu_sum, down_sum, rest_sum),
        7,
        75,
        [pltpu.VMEM(source.shape, source.dtype) for source in sources]
        + sum_bufs
        + [
            pltpu.VMEM((D, stream_len), BF16),
            low_stream,
            pltpu.VMEM(own_shape, BF16),
            pltpu.VMEM((nctx, 8, D), F32),
            pltpu.VMEM((nfsdp, 8, D), F32),
        ]
        + sum_sems
        + [line_sems, line_sems, small, small, dma((7,))]
        + 2 * ([pltpu.VMEM((D, half_width), BF16)] + line_scratch(half_width))
        + [dma((3 * chips,)), dma((3 * chips,))],
        (3, 4, 5),
        0,
        7,
    )
    last_sum, gain_sums, gu_own = lax.optimization_barrier((last_sum, gain_sums, gu_own))
    out_tokens = unspread(out_tokens)[None]
    grad_tokens = unspread(grad_tokens)[None]
    gain_grad = jnp.concatenate(
        [
            unspread(gain_sums[:1])[0],
            unspread(gain_sums[1:2])[0],
            jnp.sum(gain_sums[2, :q_width].reshape(-1, HD), axis=0),
            jnp.sum(gain_sums[2, q_width:qk_width].reshape(-1, HD), axis=0),
        ]
    )

    olds = (master_weights, moment_one, moment_two)

    def feed_segments(b, pieces, start, stop):
        found = []
        for part in pieces:
            for c in range(nctx):
                column = c * ff_width + cuts[b] + start
                real = min(max(FF - column, 0), stop - start)
                if real:
                    piece, first = pieces[part]
                    found.append((piece, c, first, bases[part] + column, real))
        return found

    width_one = cuts[1]
    last_own = [
        lax.ppermute(
            lax.dynamic_index_in_dim(last_sum, lax.axis_index("ctx") ^ k, 0, keepdims=False),
            "ctx",
            [(c, c ^ k) for c in range(nctx)],
        )
        if k
        else lax.dynamic_index_in_dim(last_sum, lax.axis_index("ctx"), 0, keepdims=False)
        for k in range(nctx)
    ]
    parts = (
        (0, 0, q_width),
        (q_width, D, kv_width),
        (qk_width, D + KVD, kv_width),
        (qkv_width, QKVC, q_width),
    )
    if kv_width % 128:
        attn_own = jnp.concatenate(
            [attn_own[c, :, f : f + w] for f, _, w in parts for c in range(nctx)], axis=1
        )[None]
        segments = [(0, 0, 0, 0, gate_base)]
    else:
        segments = [
            (0, c, first, base + c * width, width)
            for first, base, width in parts
            for c in range(nctx)
        ]
    news = adam(
        segments
        + feed_segments(0, {0: (1, 0), 1: (1, width_one)}, 0, width_one)
        + feed_segments(0, {2: (2, 0)}, 0, width_line)
        + feed_segments(0, {2: (3, 0)}, width_line, width_one),
        [attn_own, gu_own, down_own, rest_own],
        olds,
        None,
        10,
    )
    first_new, second_new, master_new, low_new = adam(
        feed_segments(
            1, {0: (None, 0), 1: (None, width_two), 2: (None, 2 * width_two)}, 0, width_two
        ),
        last_own,
        olds,
        news,
        6,
    )
    gain_first, gain_second, gain_new = adam_update(
        gains, gain_grad, gains_moment_one, gains_moment_two, GAIN_RATE, 0.0
    )
    return (
        out_tokens,
        grad_tokens,
        first_new,
        second_new,
        master_new,
        low_new,
        gain_first,
        gain_second,
        gain_new,
    )


def solution(mesh):
    rows = P("fsdp", "ctx", None)
    weights = P(("ctx", "fsdp"), None)
    return jax.shard_map(
        shards,
        mesh=mesh,
        in_specs=(rows, rows, P("fsdp", None), P(), weights, weights, weights, P(), P(), P()),
        out_specs=(rows, rows, weights, weights, weights, weights, P(), P(), P()),
        check_vma=False,
    )
```

```python
import functools

import jax
import jax.numpy as jnp
import numpy as np
from jax import lax
from jax.experimental import pallas as pl
from jax.experimental.pallas import tpu as pltpu
from jax.sharding import PartitionSpec as P

D = 1536
HEADS = 24
KVHEADS = 8
HD = 64
FF = 6912
STEP = 10
HALF = 128
KVD = 512
QKVC = 2560
GROUP = HEADS // KVHEADS

ROPE_BASE = 1000000.0
NORM_EPS = 1e-05
BETA_ONE = 0.9
BETA_TWO = 0.95
ADAM_EPS = 1e-08
WEIGHT_DECAY = 0.1
LEARN_RATE = 0.03
GAIN_RATE = 0.5
SCALE = HD ** (-0.5)
MESH = pl.DeviceIdType.MESH
F32 = jnp.float32
BF16 = jnp.bfloat16
VMEM_LIMIT = 60 * 1024 * 1024


def dot(left, right, left_dim, right_dim):
    return lax.dot_general(
        left, right, (((left_dim,), (right_dim,)), ((), ())), preferred_element_type=F32
    )


def send(source, target, sems, item, peer):
    copy = pltpu.make_async_remote_copy(
        src_ref=source,
        dst_ref=target,
        send_sem=sems[0].at[item],
        recv_sem=sems[1].at[item],
        device_id=peer,
        device_id_type=MESH,
    )
    copy.start()
    return copy


def meet(axes):
    barrier = pltpu.get_barrier_semaphore()
    total = 0
    for axis in axes:
        size = lax.axis_size(axis)
        me = lax.axis_index(axis)
        for step in range(1, size):
            pl.semaphore_signal(
                barrier,
                inc=1,
                device_id={axis: lax.rem(me + step, size)},
                device_id_type=MESH,
            )
        total += size - 1
    pl.semaphore_wait(barrier, total)


def square():
    me = lax.axis_index("ctx")
    return me, me + 1 - 2 * lax.rem(me, 2), lax.rem(me + 2, 4), 3 - me


def swap_start(source, target, sems, base):
    size = lax.axis_size("ctx")
    me = lax.axis_index("ctx")
    copies = []
    for step in range(1, size):
        peer = lax.rem(me + step, size)
        copies.append(
            send(source.at[peer], target.at[me], sems, base + step, {"ctx": peer})
        )
    return copies


def gather_start(source, target, sems, base):
    size = lax.axis_size("ctx")
    me = lax.axis_index("ctx")
    if size != 4:
        return [
            send(
                source,
                target.at[me],
                sems,
                base + step,
                {"ctx": lax.rem(me + step, size)},
            )
            for step in range(1, size)
        ]
    me, side, over, across = square()
    half = source.shape[0] // 2
    top, low = pl.ds(0, half), pl.ds(half, half)
    return [
        send(source.at[top], target.at[me, top], sems, base, {"ctx": side}),
        send(source.at[low], target.at[me, low], sems, base + 1, {"ctx": over}),
        send(source.at[low], target.at[me, low], sems, base + 2, {"ctx": side}),
        send(source.at[top], target.at[me, top], sems, base + 3, {"ctx": over}),
    ]


def gather_pass(copies, target, sems, base):
    if lax.axis_size("ctx") != 4:
        return
    me, side, over, across = square()
    half = target.shape[1] // 2
    top, low = pl.ds(0, half), pl.ds(half, half)
    copies[0].wait_recv()
    copies.append(send(target.at[side, top], target.at[side, top], sems, base + 4, {"ctx": over}))
    copies[1].wait_recv()
    copies.append(send(target.at[over, low], target.at[over, low], sems, base + 5, {"ctx": side}))


def gather_end(copies):
    if lax.axis_size("ctx") != 4:
        for copy in copies:
            copy.wait()
        return
    for copy in copies:
        copy.wait_send()
    for copy in copies[2:]:
        copy.wait_recv()


def gather_rest(copies, target, sems, base):
    gather_pass(copies, target, sems, base)
    gather_end(copies)


def load(source, target, sem):
    copy = pltpu.make_async_copy(source, target, sem)
    copy.start()
    return copy


GATHER_SEMS = 8


def exchange_kernel(kinds, *refs):
    count = len(kinds)
    ins, outs = refs[:count], refs[count : 2 * count]
    send_sem, recv_sem, local_sem = refs[2 * count :]
    sems = (send_sem, recv_sem)
    me = lax.axis_index("ctx")
    meet(("ctx",))
    copies = []
    own = []
    for item in range(count):
        base = item * GATHER_SEMS
        if kinds[item] == "gather":
            copies.append(gather_start(ins[item], outs[item], sems, base))
            source = ins[item]
        else:
            copies.append(swap_start(ins[item], outs[item], sems, base))
            source = ins[item].at[me]
        copy = pltpu.make_async_copy(source, outs[item].at[me], local_sem.at[item])
        copy.start()
        own.append(copy)
    for item in range(count):
        if kinds[item] == "gather":
            gather_rest(copies[item], outs[item], sems, item * GATHER_SEMS)
        else:
            for copy in copies[item]:
                copy.wait()
    for copy in own:
        copy.wait()


def remote_params(collective_id):
    return pltpu.CompilerParams(
        collective_id=collective_id, has_side_effects=True, vmem_limit_bytes=VMEM_LIMIT
    )


def cost(micros):
    return pl.CostEstimate(flops=0, bytes_accessed=int(micros * 3.0e6), transcendentals=0)


def exchange(kinds, arrays, collective_id, micros):
    size = lax.axis_size("ctx")
    shapes = [
        jax.ShapeDtypeStruct((size,) + a.shape if kind == "gather" else a.shape, a.dtype)
        for kind, a in zip(kinds, arrays)
    ]
    sems = pltpu.SemaphoreType.DMA((len(arrays) * GATHER_SEMS,))
    return pl.pallas_call(
        functools.partial(exchange_kernel, kinds),
        out_shape=shapes,
        in_specs=[pl.BlockSpec(memory_space=pl.ANY)] * len(arrays),
        out_specs=[pl.BlockSpec(memory_space=pl.ANY)] * len(arrays),
        scratch_shapes=[sems, sems, pltpu.SemaphoreType.DMA((len(arrays),))],
        compiler_params=remote_params(collective_id),
        cost_estimate=cost(micros),
    )(*arrays)


def sum_scratch(size, rows):
    if size == 4:
        half = pltpu.VMEM((2, rows // 2, D), BF16)
        return [half, half, pltpu.VMEM((2, rows, D), BF16)]
    return [pltpu.VMEM((size - 1, rows, D), BF16)]


def sum_start(part, bufs, sems):
    size = lax.axis_size("ctx")
    me = lax.axis_index("ctx")
    rows = part.shape[0] // size

    def block(owner, first=0, count=rows):
        return pl.ds(pl.multiple_of(owner * rows + first, rows // 2), count)

    if size != 4:
        copies = []
        for step in range(1, size):
            peer = lax.rem(me + step, size)
            copies.append(
                send(part.at[block(peer)], bufs[0].at[step - 1], sems, step, {"ctx": peer})
            )
        return copies
    me, side, over, across = square()
    half = rows // 2
    relay, _, landed = bufs
    return [
        send(part.at[block(across, 0, half)], relay.at[0], sems, 0, {"ctx": side}),
        send(part.at[block(across, half, half)], relay.at[1], sems, 1, {"ctx": over}),
        send(
            part.at[block(side, 0, half)],
            landed.at[0, pl.ds(0, half)],
            sems,
            2,
            {"ctx": side},
        ),
        send(
            part.at[block(over, half, half)],
            landed.at[1, pl.ds(half, half)],
            sems,
            3,
            {"ctx": over},
        ),
    ]


def sum_pass(copies, part, bufs, sems):
    if lax.axis_size("ctx") != 4:
        return
    rows = part.shape[0] // 4
    half = rows // 2

    def rows_of(owner, first):
        return pl.ds(pl.multiple_of(owner * rows + first, half), half)

    me, side, over, across = square()
    relay, passed, landed = bufs
    copies[0].wait_recv()
    passed[0] = (part[rows_of(over, 0), :].astype(F32) + relay[0].astype(F32)).astype(BF16)
    copies.append(
        send(passed.at[0], landed.at[1, pl.ds(0, half)], sems, 4, {"ctx": over})
    )
    copies[1].wait_recv()
    passed[1] = (part[rows_of(side, half), :].astype(F32) + relay[1].astype(F32)).astype(
        BF16
    )
    copies.append(
        send(passed.at[1], landed.at[0, pl.ds(half, half)], sems, 5, {"ctx": side})
    )


def sum_rest(copies, part, bufs):
    size = lax.axis_size("ctx")
    me = lax.axis_index("ctx")
    rows = part.shape[0] // size
    half = rows // 2

    def rows_of(owner, first):
        return pl.ds(pl.multiple_of(owner * rows + first, half), half)

    if size != 4:
        for copy in copies:
            copy.wait()

        def read(first):
            total = part[rows_of(me, first), :].astype(F32)
            for step in range(1, size):
                total = total + bufs[0][step - 1, pl.ds(first, half), :].astype(F32)
            return total

        return read
    relay, passed, landed = bufs
    for copy in copies:
        copy.wait_send()
    for copy in copies[2:]:
        copy.wait_recv()

    def read(first):
        return (
            part[rows_of(me, first), :].astype(F32)
            + landed[0, pl.ds(first, half), :].astype(F32)
            + landed[1, pl.ds(first, half), :].astype(F32)
        )

    return read


def row_scale(values):
    return lax.rsqrt(jnp.mean(values * values, axis=-1, keepdims=True) + NORM_EPS)


def first_kernel(
    starts, origin, x, dy, gain, freq, x_low, dy_low, table, normed_all, *scratch
):
    move, normed, send_one, recv_one, local = scratch
    me = lax.axis_index("ctx")
    row = lax.broadcasted_iota(jnp.int32, move.shape, 0)
    move[...] = jnp.where(row == origin[...], 1.0, 0.0).astype(BF16)
    values = dot(x[...], move[...], 1, 0)
    x_low[...] = values.astype(BF16)
    normed[...] = (values * row_scale(values) * gain[...]).astype(BF16)
    meet(("ctx",))
    sems = (send_one, recv_one)
    copies = gather_start(normed, normed_all, sems, 0)
    own = load(normed, normed_all.at[me], local)
    dy_low[...] = dot(dy[...], move[...], 1, 0).astype(BF16)
    gather_pass(copies, normed_all, sems, 0)
    times = lax.broadcasted_iota(jnp.int32, (table.shape[0], 1), 0)
    angles = (times - doc_first(starts, times)).astype(F32) * freq[...]
    lane = lax.broadcasted_iota(jnp.int32, angles.shape, 1)
    sine = jnp.sin(angles)
    sine = jnp.where(lane % HD < HD // 2, -sine, sine)
    table[...] = jnp.where(lane < HD, jnp.cos(angles), sine)
    gather_end(copies)
    own.wait()


def middle_kernel(part, x, gain, middle, normed_all, *scratch):
    bufs, (normed, send_one, recv_one, send_two, recv_two, local) = scratch[:-6], scratch[-6:]
    me = lax.axis_index("ctx")
    meet(("ctx",))
    copies = sum_start(part, bufs, (send_one, recv_one))
    sum_pass(copies, part, bufs, (send_one, recv_one))
    read = sum_rest(copies, part, bufs)
    half = x.shape[0] // 2
    for first in (0, half):
        rows = pl.ds(first, half)
        values = x[rows, :].astype(F32) + read(first)
        middle[rows, :] = values
        normed[rows, :] = (values * row_scale(values) * gain[...]).astype(BF16)
    sems = (send_two, recv_two)
    copies = gather_start(normed, normed_all, sems, 0)
    own = load(normed, normed_all.at[me], local)
    gather_rest(copies, normed_all, sems, 0)
    own.wait()


def column_tiles(total, body):
    def step(tile, carry):
        body(pl.multiple_of(tile * 256, 256), 256)
        return carry

    lax.fori_loop(0, total // 256, step, 0)
    if total % 256:
        body(total - total % 256, total % 256)


def turn(source, target):
    for first in range(0, source.shape[0], HALF):
        rows = slice(first, first + HALF)
        target[:, rows] = source[rows, :].T


def middle_back_kernel(
    part,
    middle,
    dy,
    gain,
    x_all,
    dy_all,
    hidden_one,
    hidden_two,
    grad_gu,
    w_one,
    w_two,
    grad,
    gain_grad,
    down_sum,
    grad_all,
    rest_grad,
    weight_grad,
    out,
    *scratch,
):
    bufs = scratch[:-21]
    low, x_buf, gu_buf, turned, weight_buf, rest_buf, down_grad, out_buf = scratch[-21:-13]
    hidden_bufs, down_bufs = scratch[-13:-11], scratch[-11:-9]
    home, travel, send_one, recv_one, send_two, recv_two, send_three, recv_three, local = (
        scratch[-9:]
    )
    going, coming = travel.at[0], travel.at[1]
    me = lax.axis_index("ctx")
    chips = lax.axis_size("fsdp") // 2
    line = (send_three, recv_three)
    meet(("ctx", "fsdp"))
    copies = sum_start(part, bufs, (send_one, recv_one))
    width_one, width_two = hidden_one.shape[1], hidden_two.shape[1]
    gu_width = grad_gu.shape[1]
    loads = [
        load(source, target, local.at[item])
        for item, (source, target) in enumerate(
            (
                (dy_all, x_buf),
                (hidden_one, hidden_bufs[0]),
                (hidden_two, hidden_bufs[1]),
                (grad_gu, gu_buf),
                (w_one.at[:, pl.ds(2 * width_one, width_one)], down_bufs[0]),
                (w_two.at[:, pl.ds(2 * width_two, width_two)], down_bufs[1]),
            )
        )
    ]
    loads[0].wait()
    turn(x_buf, turned)
    loads.append(load(x_all, x_buf, local.at[6]))
    loads[1].wait()

    def product(target, column, right, begin=0, count=None):
        def tile(first, width):
            target[:, pl.ds(column + first, width)] = dot(
                turned[...], right[:, pl.ds(begin + first, width)], 1, 0
            ).astype(BF16)

        column_tiles(right.shape[1] if count is None else count, tile)

    width_line = down_grad.shape[1]
    product(down_grad, 0, hidden_bufs[0], 0, width_line)
    home_copies = line_start(down_grad, home, line, 0)
    product(rest_buf, 0, hidden_bufs[0], width_line, width_one - width_line)
    stores = [load(rest_buf, rest_grad, local.at[10])]
    sum_pass(copies, part, bufs, (send_one, recv_one))
    line_home(home_copies, down_grad, home)
    line_step(chips - 1, home, going, coming, line, chips)
    loads[2].wait()
    product(weight_buf, gu_width, hidden_bufs[1])
    loads[6].wait()
    turn(x_buf, turned)
    loads[3].wait()
    product(weight_buf, 0, gu_buf)
    stores.append(load(weight_buf, weight_grad, local.at[7]))
    if chips > 2:
        line_step(chips - 2, home, going, coming, line, chips)
    read = sum_rest(copies, part, bufs)
    half = dy.shape[0] // 2
    total = jnp.zeros((1, D), F32)
    for first in (0, half):
        rows = pl.ds(first, half)
        values = middle[rows, :]
        root = row_scale(values)
        unit = values * root
        back = read(first)
        total = total + jnp.sum(back * unit, axis=0, keepdims=True)
        back = back * gain[...]
        back = root * (back - unit * jnp.mean(back * unit, axis=-1, keepdims=True))
        back = back + dy[rows, :].astype(F32)
        grad[rows, :] = back
        low[rows, :] = back.astype(BF16)
    gain_grad[...] = total
    sems = (send_two, recv_two)
    copies = gather_start(low, grad_all, sems, 0)
    stores.append(load(low, grad_all.at[me], local.at[8]))
    loads[4].wait()
    loads[5].wait()

    def out_tile(first, width):
        columns = pl.ds(first, width)
        out_buf[:, columns] = (
            dot(hidden_bufs[0][...], down_bufs[0][columns, :], 1, 1)
            + dot(hidden_bufs[1][...], down_bufs[1][columns, :], 1, 1)
        ).astype(BF16)

    column_tiles(D, out_tile)
    stores.append(load(out_buf, out, local.at[9]))
    gather_pass(copies, grad_all, sems, 0)
    for reach in range(min(chips - 1, max(chips - 3, 1)), 0, -1):
        line_step(reach, home, going, coming, line, chips)
    line_end(home_copies, home, going, coming, line, chips)
    chip = lax.axis_index("fsdp") // 2
    rows = down_sum.shape[1]
    for index in range(down_sum.shape[0]):
        down_sum[index] = home[chip, index * rows : (index + 1) * rows, :]
    gather_end(copies)
    for copy in stores:
        copy.wait()


def line_start(grad, home, sems, base):
    me = lax.axis_index("fsdp")
    chips = lax.axis_size("fsdp") // 2
    core = lax.rem(me, 2)
    rows = grad.shape[0] // (2 * chips)
    copies = []
    for chip in range(chips):
        theirs = pl.ds(pl.multiple_of((2 * chip + 1 - core) * rows, rows), rows)
        copies.append(
            send(grad.at[theirs], home.at[chip], sems, base + chip, {"fsdp": me + 1 - 2 * core})
        )
    return copies


def line_home(copies, grad, home):
    me = lax.axis_index("fsdp")
    chips = lax.axis_size("fsdp") // 2
    core = lax.rem(me, 2)
    rows = grad.shape[0] // (2 * chips)
    for chip in range(chips):
        copies[chip].wait_recv()
        mine = pl.ds(pl.multiple_of((2 * chip + core) * rows, rows), rows)
        home[chip] = (home[chip].astype(F32) + grad[mine, :].astype(F32)).astype(BF16)


def line_copies(reach, going, coming, sems, base):
    me = lax.axis_index("fsdp")
    chips = lax.axis_size("fsdp") // 2
    chip = me // 2
    found = []
    for side, way in ((0, 1), (1, -1)):
        copy = pltpu.make_async_remote_copy(
            src_ref=going.at[side, reach - 1],
            dst_ref=coming.at[side, reach - 1],
            send_sem=sems[0].at[base + 2 * reach + side],
            recv_sem=sems[1].at[base + 2 * reach + side],
            device_id={"fsdp": lax.rem(me + 2 * way + 2 * chips, 2 * chips)},
            device_id_type=MESH,
        )
        if way == 1:
            sent = chip + reach <= chips - 1
            got = (chip >= 1) & (chip + reach <= chips)
            more = (chip >= 1) & sent
        else:
            sent = chip >= reach
            got = (chip <= chips - 2) & (chip + 1 >= reach)
            more = (chip <= chips - 2) & sent
        found.append((side, way, copy, sent, got, more))
    return found


def line_step(reach, home, going, coming, sems, base):
    me = lax.axis_index("fsdp")
    chips = lax.axis_size("fsdp") // 2
    chip = me // 2
    if reach < chips - 1:
        for _, _, copy, _, got, _ in line_copies(reach + 1, going, coming, sems, base):
            pl.when(got)(copy.wait_recv)
    for side, way, copy, sent, _, more in line_copies(reach, going, coming, sems, base):

        @pl.when(sent)
        def _(side=side, way=way, copy=copy, more=more):
            value = home[chip + way * reach]
            if reach < chips - 1:

                @pl.when(more)
                def _():
                    going[side, reach - 1] = (
                        value.astype(F32) + coming[side, reach].astype(F32)
                    ).astype(BF16)

                @pl.when(jnp.logical_not(more))
                def _():
                    going[side, reach - 1] = value

            else:
                going[side, reach - 1] = value
            copy.start()


def line_end(copies, home, going, coming, sems, base):
    me = lax.axis_index("fsdp")
    chips = lax.axis_size("fsdp") // 2
    chip = me // 2
    for side, _, copy, _, got, _ in line_copies(1, going, coming, sems, base):

        @pl.when(got)
        def _(side=side, copy=copy):
            copy.wait_recv()
            home[chip] = (home[chip].astype(F32) + coming[side, 0].astype(F32)).astype(BF16)

    for copy in copies:
        copy.wait_send()
    for reach in range(1, chips):
        for _, _, copy, sent, _, _ in line_copies(reach, going, coming, sems, base):
            pl.when(sent)(copy.wait_send)


def remote_call(
    kernel, out_shape, args, collective_id, micros, scratch, in_hbm=(), smem=0, args_in_hbm=0
):
    return pl.pallas_call(
        kernel,
        out_shape=out_shape,
        in_specs=[pl.BlockSpec(memory_space=pltpu.SMEM)] * smem
        + [pl.BlockSpec(memory_space=pltpu.VMEM)] * (len(args) - smem - args_in_hbm)
        + [pl.BlockSpec(memory_space=pl.ANY)] * args_in_hbm,
        out_specs=[
            pl.BlockSpec(memory_space=pl.ANY if item in in_hbm else pltpu.VMEM)
            for item in range(len(out_shape))
        ],
        scratch_shapes=scratch,
        compiler_params=remote_params(collective_id),
        cost_estimate=cost(micros),
    )(*args)


def adam_update(param_now, grad_now, moment_old_one, moment_old_two, step_rate, decay_rate):
    first_new = BETA_ONE * moment_old_one + (1.0 - BETA_ONE) * grad_now
    second_new = BETA_TWO * moment_old_two + (1.0 - BETA_TWO) * grad_now * grad_now
    ratio = (first_new * (1.0 / (1.0 - BETA_ONE**STEP))) / (
        jnp.sqrt(second_new * (1.0 / (1.0 - BETA_TWO**STEP))) + ADAM_EPS
    )
    return (first_new, second_new, param_now - step_rate * (ratio + decay_rate * param_now))


def joined_ranges(segments):
    ranges = []
    for number in sorted(range(len(segments)), key=lambda n: segments[n][3]):
        column, width = segments[number][3:]
        if ranges and ranges[-1][0] + ranges[-1][1] == column:
            first, so_far, numbers = ranges[-1]
            ranges[-1] = (first, so_far + width, numbers + (number,))
        else:
            ranges.append((column, width, (number,)))
    return ranges


def adam_kernel(segments, pieces, held, *refs):
    me = lax.axis_index("ctx")
    grads = refs[:pieces]
    olds = refs[pieces : pieces + 3]
    news = refs[pieces + 3 + held : pieces + 3 + held + 4]
    grad_buf, old_buf, low_buf, grad_sem, in_sem, out_sem = refs[pieces + 3 + held + 4 :]
    base = min(segment[3] for segment in segments)
    ranges = joined_ranges(segments)
    loads = []
    for place, (column, width, numbers) in enumerate(ranges):
        here, there = pl.ds(column - base, width), pl.ds(column, width)
        copies = [
            load(olds[item].at[:, there], old_buf.at[item, :, here], in_sem.at[item, place])
            for item in range(3)
        ]
        for number in numbers:
            piece, index, first, start, count = segments[number]
            columns = pl.ds(first, count)
            for source_number, source in enumerate(grads):
                if piece not in (None, source_number):
                    continue
                copy = pltpu.make_async_copy(
                    source.at[:, columns] if piece is None else source.at[index, :, columns],
                    grad_buf.at[:, pl.ds(start - base, count)],
                    grad_sem.at[number],
                )
                if piece is None:
                    pl.when(me == index ^ source_number)(copy.start)
                else:
                    copy.start()
            copies.append(copy)
        loads.append(copies)
    stores = []
    for place, (column, width, numbers) in enumerate(ranges):
        for copy in loads[place]:
            copy.wait()
        here, there = pl.ds(column - base, width), pl.ds(column, width)
        for first in range(0, width, 256):
            part = pl.ds(column - base + first, min(256, width - first))
            first_new, second_new, master = adam_update(
                old_buf[0, :, part],
                grad_buf[:, part].astype(F32),
                old_buf[1, :, part],
                old_buf[2, :, part],
                LEARN_RATE,
                WEIGHT_DECAY,
            )
            old_buf[0, :, part] = master
            old_buf[1, :, part] = first_new
            old_buf[2, :, part] = second_new
            low_buf[:, part] = master.astype(BF16)
        for item, source in enumerate(
            (
                old_buf.at[1, :, here],
                old_buf.at[2, :, here],
                old_buf.at[0, :, here],
                low_buf.at[:, here],
            )
        ):
            stores.append(load(source, news[item].at[:, there], out_sem.at[item, place]))
    for copy in stores:
        copy.wait()


def adam(segments, grads, olds, held, micros):
    rows, columns = olds[0].shape
    span = max(s[3] + s[4] for s in segments) - min(s[3] for s in segments)
    held = [] if held is None else list(held)
    args = list(grads) + list(olds) + held
    return pl.pallas_call(
        functools.partial(adam_kernel, tuple(segments), len(grads), len(held)),
        out_shape=[jax.ShapeDtypeStruct((rows, columns), F32)] * 3
        + [jax.ShapeDtypeStruct((rows, columns), BF16)],
        in_specs=[pl.BlockSpec(memory_space=pl.ANY)] * len(args),
        out_specs=[pl.BlockSpec(memory_space=pl.ANY)] * 4,
        input_output_aliases={len(grads) + 3 + item: item for item in range(len(held))},
        scratch_shapes=[
            pltpu.VMEM((rows, span), BF16),
            pltpu.VMEM((3, rows, span), F32),
            pltpu.VMEM((rows, span), BF16),
            pltpu.SemaphoreType.DMA((len(segments),)),
            pltpu.SemaphoreType.DMA((3, len(segments))),
            pltpu.SemaphoreType.DMA((4, len(segments))),
        ],
        compiler_params=pltpu.CompilerParams(vmem_limit_bytes=VMEM_LIMIT),
        cost_estimate=cost(micros),
    )(*args)


def head_mean(values, ones):
    high = values.astype(BF16)
    rest = (values - high.astype(F32)).astype(BF16)
    return (dot(high, ones, 1, 0) + dot(rest, ones, 1, 0)) * (1.0 / HD)


def head_ones(width):
    row = lax.broadcasted_iota(jnp.int32, (width, width), 0) // HD
    col = lax.broadcasted_iota(jnp.int32, (width, width), 1) // HD
    return jnp.where(row == col, 1.0, 0.0).astype(BF16)


def partner(values):
    width = values.shape[-1]
    lane = lax.broadcasted_iota(jnp.int32, values.shape, 1)
    return jnp.where(
        lane % HD < HD // 2,
        pltpu.roll(values, width - HD // 2, 1),
        pltpu.roll(values, HD // 2, 1),
    )


def widen(table, width):
    return [
        jnp.concatenate([part] * (width // HD), axis=-1)
        for part in (table[:, :HD], table[:, HD:])
    ]


def doc_first(starts, times):
    first = jnp.zeros_like(times)
    for item in range(starts.shape[0]):
        first = jnp.where(starts[item] <= times, starts[item], first)
    return first


def block_mask(starts, block, keys):
    shape = (keys, GROUP * HALF)
    times = block * HALF + lax.broadcasted_iota(jnp.int32, (1, GROUP * HALF), 1) % HALF
    key = lax.broadcasted_iota(jnp.int32, shape, 0)
    return (key >= doc_first(starts, times)) & (key <= times)


def stack_heads(ref, rows, group):
    return jnp.concatenate(
        [
            ref[rows, (group * GROUP + h) * HD : (group * GROUP + h + 1) * HD]
            for h in range(GROUP)
        ],
        axis=0,
    )


def unstack_heads(turned):
    wide = turned.T
    return [wide[h * HALF : (h + 1) * HALF, :] for h in range(GROUP)]


def attend_kernel(
    blocks,
    groups,
    place,
    order,
    starts,
    table,
    gain,
    normed_in,
    weights_from,
    dy,
    swap_in,
    part,
    qk,
    q,
    k,
    v,
    o_held,
    lse,
    dy_all,
    swap_out,
    normed,
    weights_in,
    joined,
    o,
    send_sem,
    recv_sem,
    local,
):
    sems = (send_sem, recv_sem)
    me = lax.axis_index("ctx")
    qk_width = qk.shape[1]
    q_width = q.shape[1]
    qkv_width = qk_width + v.shape[1]
    ones = head_ones(qk_width)
    meet(("ctx",))
    loads = [
        load(normed_in, normed, local.at[0]),
        load(weights_from, weights_in, local.at[1]),
    ]
    swap_copies = swap_start(swap_in, swap_out, sems, GATHER_SEMS)
    copies = gather_start(dy, dy_all, sems, 0)
    own_copies = [
        load(swap_in.at[me], swap_out.at[me], local.at[2]),
        load(dy, dy_all.at[me], local.at[3]),
    ]
    for copy in loads:
        copy.wait()
    for block in range(blocks):
        joined[block] = dot(
            normed[block * HALF : (block + 1) * HALF, :], weights_in[:, :qkv_width], 1, 0
        )
    for block in range(blocks):
        to = slice(block * HALF, (block + 1) * HALF)
        values = joined[place[block]]
        v[to, :] = values[:, qk_width:].astype(BF16)
        values = values[:, :qk_width]
        qk[to, :] = values
        turned = values * lax.rsqrt(head_mean(values * values, ones) + NORM_EPS) * gain[...]
        cosine, sine = widen(table[to, :], qk_width)
        turned = turned * cosine + partner(turned) * sine
        turned = turned.astype(BF16)
        q[to, :] = turned[:, :q_width]
        k[to, :] = turned[:, q_width:]
    for block in range(blocks):
        rows = slice(block * HALF, (block + 1) * HALF)
        keys = (block + 1) * HALF
        mask = block_mask(starts, block, keys)
        pieces = []
        for group in range(groups):
            lanes = slice(group * HD, (group + 1) * HD)
            queries = stack_heads(q, rows, group)
            scores = dot(k[:keys, lanes], queries, 1, 1) * SCALE
            weights = jnp.where(mask, jnp.exp(scores), 0.0)
            sums = jnp.sum(weights, axis=0, keepdims=True)
            lse[block, group : group + 1, :] = jnp.log(sums)
            mixed = dot(v[:keys, lanes], weights.astype(BF16), 0, 0) / sums
            pieces += unstack_heads(mixed)
        o[block] = jnp.concatenate(pieces, axis=1).astype(BF16)
    for block in range(blocks):
        o_held[block * HALF : (block + 1) * HALF, :] = o[order[block]]
    for first in range(0, D, 512):
        part[:, first : first + 512] = dot(
            o_held[...], weights_in[first : first + 512, qkv_width:], 1, 1
        ).astype(BF16)
    gather_rest(copies, dy_all, sems, 0)
    for copy in swap_copies:
        copy.wait()
    for copy in own_copies:
        copy.wait()


def attend_back_kernel(
    blocks,
    groups,
    place,
    order,
    starts,
    lse,
    gain,
    part,
    rest_grad,
    *refs,
):
    sources, refs = refs[:9], refs[9:]
    out, joined, gain_grad, out_grad, rest_sum = refs[:5]
    targets, refs = refs[5:14], refs[14:]
    grad_all, weights_in, q, k, v, o, qk, table, middle = targets
    bufs, (do, dq, dkv, turned, home, travel) = refs[:-11], refs[-11:-5]
    send_one, recv_one, send_two, recv_two, local = refs[-5:]
    going, coming = travel.at[0], travel.at[1]
    line = (send_two, recv_two)
    chips = lax.axis_size("fsdp") // 2
    out_sems = (send_one, recv_one)
    qk_width = qk.shape[2]
    qkv_width = qk_width + v.shape[1]
    ones = head_ones(qk_width)
    meet(("ctx", "fsdp"))
    home_copies = line_start(rest_grad, home, line, 0)
    out_copies = sum_start(part, bufs, out_sems)
    loads = [
        load(source, target, local.at[item])
        for item, (source, target) in enumerate(zip(sources, targets))
    ]
    for copy in loads[:6]:
        copy.wait()
    for block in range(blocks):
        do[block * HALF : (block + 1) * HALF, :] = dot(
            grad_all[place[block]], weights_in[:, qkv_width:], 1, 0
        ).astype(BF16)
    for block in range(blocks):
        turned[:, block * HALF : (block + 1) * HALF] = grad_all[block].T
    for first in range(0, D, 512):
        rows = slice(first, first + 512)
        out_grad[rows, :] = dot(turned[rows, :], o[...], 1, 0).astype(BF16)
    dkv[...] = jnp.zeros_like(dkv)
    line_home(home_copies, rest_grad, home)
    line_step(chips - 1, home, going, coming, line, chips)
    reach = chips - 2
    for block in range(blocks):
        if block == blocks // 2:
            sum_pass(out_copies, part, bufs, out_sems)
        if block >= blocks * 3 // 4 and reach > 1:
            line_step(reach, home, going, coming, line, chips)
            reach -= 1
        rows = slice(block * HALF, (block + 1) * HALF)
        keys = (block + 1) * HALF
        mask = block_mask(starts, block, keys)
        pieces = []
        dk_add = []
        dv_add = []
        for group in range(groups):
            lanes = slice(group * HD, (group + 1) * HD)
            queries = stack_heads(q, rows, group)
            outs = stack_heads(do, rows, group)
            key_rows = k[:keys, lanes]
            scores = dot(key_rows, queries, 1, 1) * SCALE
            weights = jnp.where(
                mask, jnp.exp(scores - lse[block, group : group + 1, :]), 0.0
            )
            back = dot(v[:keys, lanes], outs, 1, 1)
            delta = jnp.sum(weights * back, axis=0, keepdims=True)
            grads = (weights * (back - delta)).astype(BF16)
            pieces += unstack_heads(dot(key_rows, grads, 0, 0) * SCALE)
            dk_add.append(dot(grads, queries, 1, 0) * SCALE)
            dv_add.append(dot(weights.astype(BF16), outs, 1, 0))
        dq[block] = jnp.concatenate(pieces, axis=1)
        dkv[: block + 1] += jnp.concatenate(dk_add + dv_add, axis=1).reshape(
            (block + 1,) + dkv.shape[1:]
        )
    for step in range(reach, 0, -1):
        line_step(step, home, going, coming, line, chips)
    gain_row = jnp.zeros((1, qk_width), F32)
    for copy in loads[6:]:
        copy.wait()
    for block in range(blocks):
        here = order[block]
        values = qk[here]
        root = lax.rsqrt(head_mean(values * values, ones) + NORM_EPS)
        unit = values * root
        grad_kv = dkv[here]
        kv_width = grad_kv.shape[1] // 2
        grad = jnp.concatenate([dq[here], grad_kv[:, :kv_width]], axis=1)
        cosine, sine = widen(table[here], qk_width)
        grad = grad * cosine - partner(grad) * sine
        gain_row = gain_row + jnp.sum(grad * unit, axis=0, keepdims=True)
        grad = grad * gain[...]
        grad = root * (grad - unit * head_mean(grad * unit, ones))
        joined[block * HALF : (block + 1) * HALF, :] = jnp.concatenate(
            [grad, grad_kv[:, kv_width:]], axis=1
        ).astype(BF16)
    gain_grad[...] = gain_row
    read = sum_rest(out_copies, part, bufs)
    half = middle.shape[0] // 2
    for first in (0, half):
        rows = pl.ds(first, half)
        out[rows, :] = (middle[rows, :] + read(first)).astype(BF16)
    line_end(home_copies, home, going, coming, line, chips)
    chip = lax.axis_index("fsdp") // 2
    owned_rows = rest_sum.shape[1]
    for index in range(rest_sum.shape[0]):
        rest_sum[index] = home[chip, index * owned_rows : (index + 1) * owned_rows, :]


def tail_kernel(
    swaps,
    joined,
    out_grad,
    gain_row,
    attn_gain,
    ffn_gain_grad,
    *refs,
):
    sources, refs = refs[:4], refs[4:]
    swap_in, refs = refs[:swaps], refs[swaps:]
    grad_tokens, gains, attn_own = refs[:3]
    swap_out, refs = refs[3 : 3 + swaps], refs[3 + swaps :]
    targets, refs = refs[:4], refs[4:]
    weights_in, normed, x, grad_middle = targets
    back_bufs, refs = refs[:-15], refs[-15:]
    turned, part, attn_grad, home, travel, owned, ctx_box, fsdp_box = refs[:8]
    send_two, recv_two, send_three, recv_three, send_four, recv_four, local = refs[8:]
    going, coming = travel.at[0], travel.at[1]
    back_sems = (send_two, recv_two)
    line, small = (send_three, recv_three), (send_four, recv_four)
    size = lax.axis_size("ctx")
    me = lax.axis_index("ctx")
    chips = lax.axis_size("fsdp") // 2
    step_base = chips
    swap_base = step_base + 2 * chips
    qkv_width = joined.shape[1]
    qk_width = gain_row.shape[1]
    half = x.shape[0] // 2
    loads = [
        load(source, target, local.at[item])
        for item, (source, target) in enumerate(zip(sources, targets))
    ]
    meet(("ctx", "fsdp"))
    swap_copies = []
    own_copies = []
    for item in range(swaps):
        swap_copies += swap_start(
            swap_in[item], swap_out[item], line, swap_base + (item + 1) * size
        )
        own_copies.append(
            load(swap_in[item].at[me], swap_out[item].at[me], local.at[4 + item])
        )
    for copy in loads:
        copy.wait()
    for first in range(0, D, 512):
        part[:, first : first + 512] = dot(
            joined[...], weights_in[first : first + 512, :qkv_width], 1, 1
        ).astype(BF16)
    back_copies = sum_start(part, back_bufs, back_sems)
    turn(normed, turned)
    for first in range(0, D, 512):
        rows = slice(first, first + 512)
        attn_grad[rows, :qkv_width] = dot(turned[rows, :], joined[...], 1, 0).astype(BF16)
    attn_grad[:, qkv_width:] = out_grad[...]
    home_copies = line_start(attn_grad, home, line, 0)
    line_home(home_copies, attn_grad, home)
    line_step(chips - 1, home, going, coming, line, step_base)
    sum_pass(back_copies, part, back_bufs, back_sems)
    for reach in range(chips - 2, 1, -1):
        line_step(reach, home, going, coming, line, step_base)
    read = sum_rest(back_copies, part, back_bufs)
    total = jnp.zeros((1, D), F32)
    for first in (0, half):
        rows = pl.ds(first, half)
        values = x[rows, :].astype(F32)
        root = row_scale(values)
        unit = values * root
        back = read(first)
        total = total + jnp.sum(back * unit, axis=0, keepdims=True)
        back = back * attn_gain[...]
        back = root * (back - unit * jnp.mean(back * unit, axis=-1, keepdims=True))
        grad_tokens[rows, :] = grad_middle[rows, :] + back

    def spread_start(axis, box, value, base):
        index = lax.axis_index(axis)
        axis_size = lax.axis_size(axis)
        box[index] = value
        return [
            send(
                box.at[index],
                box.at[index],
                small,
                base + step,
                {axis: lax.rem(index + step, axis_size)},
            )
            for step in range(1, axis_size)
        ]

    def spread_end(copies, box):
        for copy in copies:
            copy.wait()
        summed = box[0]
        for item in range(1, box.shape[0]):
            summed = summed + box[item]
        return summed

    ctx_copies = spread_start(
        "ctx",
        ctx_box,
        jnp.concatenate(
            [
                total,
                ffn_gain_grad[...],
                jnp.concatenate([gain_row[...], jnp.zeros((1, D - qk_width), F32)], axis=1),
                jnp.zeros((5, D), F32),
            ],
            axis=0,
        ),
        0,
    )
    line_step(1, home, going, coming, line, step_base)
    fsdp_copies = spread_start("fsdp", fsdp_box, spread_end(ctx_copies, ctx_box), size)
    line_end(home_copies, home, going, coming, line, step_base)
    chip = lax.axis_index("fsdp") // 2
    owned_rows = owned.shape[1]
    for index in range(size):
        owned[index] = home[chip, index * owned_rows : (index + 1) * owned_rows, :]
    swap_copies += swap_start(owned, attn_own, line, swap_base)
    attn_own[me] = owned[me]
    gains[...] = spread_end(fsdp_copies, fsdp_box)
    for copy in swap_copies:
        copy.wait()
    for copy in own_copies:
        copy.wait()


def rms_scale(values_in, gain_vec):
    return (
        values_in
        * lax.rsqrt(jnp.mean(values_in * values_in, axis=-1, keepdims=True) + NORM_EPS)
        * gain_vec
    )


def inverse_freq():
    return (1.0 / ROPE_BASE ** (np.arange(0, HD, 2, dtype=np.float32) / np.float32(HD))).astype(
        np.float32
    )


def shards(
    tokens,
    cotangent,
    doc_starts,
    block_order,
    master_weights,
    moment_one,
    moment_two,
    gains,
    gains_moment_one,
    gains_moment_two,
):
    nctx = lax.axis_size("ctx")
    nfsdp = lax.axis_size("fsdp")
    own_rows = master_weights.shape[0]
    tok_rows = tokens.shape[1]
    stream_len = tok_rows * nctx
    blocks = stream_len // HALF
    groups = KVHEADS // nctx
    q_width = D // nctx
    kv_width = KVD // nctx
    qk_width = q_width + kv_width
    qkv_width = qk_width + kv_width
    tiles = FF // 128
    ff_tiles = -(-tiles // nctx)
    ff_width = ff_tiles * 128
    bundles = 2
    cuts = [0, (ff_tiles * 5 + 3) // 7 * 128, ff_width]

    head = lax.optimization_barrier(master_weights[:, : QKVC + D]).astype(BF16)

    def ff_part(base, index, start, stop):
        first = index * ff_width + start
        last = index * ff_width + stop
        real_first, real_last = min(first, FF), min(last, FF)
        part = low[:, base - gate_base + real_first : base - gate_base + real_last]
        if real_last - real_first < last - first:
            part = jnp.pad(part, ((0, 0), (0, (last - first) - (real_last - real_first))))
        return part

    def attn_part(index):
        return jnp.concatenate(
            [
                head[:, index * q_width : (index + 1) * q_width],
                head[:, D + index * kv_width : D + (index + 1) * kv_width],
                head[:, D + KVD + index * kv_width : D + KVD + (index + 1) * kv_width],
                head[:, QKVC + index * q_width : QKVC + (index + 1) * q_width],
            ],
            axis=1,
        )

    gate_base = QKVC + D
    bases = (gate_base, gate_base + FF, gate_base + 2 * FF)
    attn_send = jnp.stack([attn_part(c) for c in range(nctx)])
    def gather_rows(piece):
        return lax.all_gather(
            piece.reshape(nctx * own_rows, piece.shape[-1]), "fsdp", axis=0, tiled=True
        )

    def spread(active):
        return (
            active.reshape(active.shape[0], nctx, nfsdp, own_rows)
            .transpose(0, 2, 1, 3)
            .reshape(active.shape[0], D)
        )

    def unspread(active):
        return (
            active.reshape(active.shape[0], nfsdp, nctx, own_rows)
            .transpose(0, 2, 1, 3)
            .reshape(active.shape[0], D)
        )

    dma = pltpu.SemaphoreType.DMA
    all_low = jax.ShapeDtypeStruct((nctx, tok_rows, D), BF16)
    own_low = jax.ShapeDtypeStruct((tok_rows, D), BF16)
    own_f32 = jax.ShapeDtypeStruct((tok_rows, D), F32)
    row_f32 = jax.ShapeDtypeStruct((1, D), F32)
    g_attn = spread(gains[None, :D])
    g_ffn = spread(gains[None, D : 2 * D])
    order = block_order.reshape(blocks)
    place = jnp.argsort(order).astype(jnp.int32)
    starts = doc_starts[0]

    (attn_held,) = exchange(("swap",), [attn_send], 0, 10)
    w_attn = gather_rows(attn_held)
    low, attn_held = lax.optimization_barrier((master_weights[:, gate_base:], attn_held))
    low = low.astype(BF16)
    ff_send = [
        jnp.stack(
            [
                jnp.concatenate(
                    [ff_part(base, c, cuts[b], cuts[b + 1]) for base in bases], axis=1
                )
                for c in range(nctx)
            ]
        )
        for b in range(bundles)
    ]

    first_send = ff_send[0]
    (first_held,) = exchange(("swap",), [first_send], 1, 16)
    table_shape = jax.ShapeDtypeStruct((stream_len, 2 * HD), F32)
    origin = jnp.asarray(
        np.arange(D, dtype=np.int32)
        .reshape(nctx, nfsdp, own_rows)
        .transpose(1, 0, 2)
        .reshape(1, D)
    )
    starts_late, first_held = lax.optimization_barrier((starts, first_held))
    x_low, dy_low, table, normed_all = remote_call(
        first_kernel,
        [own_low, own_low, table_shape, all_low],
        (
            starts_late,
            origin,
            tokens[0],
            cotangent[0],
            g_attn,
            jnp.asarray(np.tile(inverse_freq(), 4)[None]),
        ),
        2,
        33,
        [
            pltpu.VMEM((D, D), BF16),
            pltpu.VMEM((tok_rows, D), BF16),
            dma((GATHER_SEMS,)),
            dma((GATHER_SEMS,)),
            dma,
        ],
        (3,),
        1,
    )
    normed_all = normed_all.reshape(stream_len, D)

    g_query = gains[2 * D : 2 * D + HD]
    g_key = gains[2 * D + HD :]
    qk_gain = jnp.concatenate(
        [jnp.tile(g_query, q_width // HD), jnp.tile(g_key, kv_width // HD)]
    )[None]

    low_stream = pltpu.VMEM((stream_len, D), BF16)
    heads_low = pltpu.VMEM((stream_len, q_width), BF16)
    part, qk, q, k, v, mixed, lse, dy_all, second_held = remote_call(
        functools.partial(attend_kernel, blocks, groups),
        [
            jax.ShapeDtypeStruct((stream_len, D), BF16),
            jax.ShapeDtypeStruct((stream_len, qk_width), F32),
            jax.ShapeDtypeStruct((stream_len, q_width), BF16),
            jax.ShapeDtypeStruct((stream_len, kv_width), BF16),
            jax.ShapeDtypeStruct((stream_len, kv_width), BF16),
            jax.ShapeDtypeStruct((stream_len, q_width), BF16),
            jax.ShapeDtypeStruct((blocks, groups, GROUP * HALF), F32),
            all_low,
            jax.ShapeDtypeStruct(ff_send[1].shape, BF16),
        ],
        (place, order, starts, table, qk_gain, normed_all, w_attn, dy_low, ff_send[1]),
        3,
        42,
        [
            low_stream,
            pltpu.VMEM(w_attn.shape, BF16),
            pltpu.VMEM((blocks, HALF, qkv_width), F32),
            pltpu.VMEM((blocks, HALF, q_width), BF16),
            dma((GATHER_SEMS + nctx,)),
            dma((GATHER_SEMS + nctx,)),
            dma((4,)),
        ],
        (7, 8),
        3,
        4,
    )
    dy_all = dy_all.reshape(stream_len, D)
    w_ff = [gather_rows(first_held), gather_rows(second_held)]
    sum_bufs = sum_scratch(nctx, tok_rows)
    sum_sems = [dma((GATHER_SEMS,)), dma((GATHER_SEMS,))]
    norm_scratch = (
        sum_bufs + [pltpu.VMEM((tok_rows, D), BF16)] + sum_sems + sum_sems + [dma]
    )

    middle, normed_two_all = remote_call(
        middle_kernel,
        [own_f32, all_low],
        (part, x_low, g_ffn),
        4,
        57,
        norm_scratch,
        (1,),
    )
    normed_two_all = normed_two_all.reshape(stream_len, D)

    def sum_rows(grad):
        return lax.psum_scatter(grad, "fsdp", scatter_dimension=0, tiled=True).reshape(
            nctx, own_rows, grad.shape[-1]
        )

    def feed(b, x_all, dy):
        width = cuts[b + 1] - cuts[b]
        w_gu, w_down = w_ff[b][:, : 2 * width], w_ff[b][:, 2 * width :]
        gate_up = dot(x_all, w_gu, 1, 0).astype(BF16)
        gate, up = gate_up[:, :width].astype(F32), gate_up[:, width:].astype(F32)
        gated = jax.nn.sigmoid(gate)
        act = gate * gated
        hidden = (act * up).astype(BF16)
        back_hidden = dot(dy, w_down, 1, 0)
        grad_gu = jnp.concatenate(
            [back_hidden * up * (gated + act * (1.0 - gated)), back_hidden * act], axis=1
        ).astype(BF16)
        return hidden, grad_gu, dot(grad_gu, w_gu, 1, 1)

    hidden_one, grad_gu, back_partial = feed(0, normed_two_all, dy_all)
    gu_grad = dot(normed_two_all, grad_gu, 0, 0).astype(BF16)
    gu_grad, back_partial, w_ff[1] = lax.optimization_barrier((gu_grad, back_partial, w_ff[1]))
    width_two = cuts[2] - cuts[1]
    width_line = cuts[1] * 3 // 5 // 128 * 128
    width_rest = cuts[1] - width_line
    hidden_two, grad_gu, back_more = feed(1, normed_two_all, dy_all)
    back_partial = (back_partial + back_more).astype(BF16)
    gu_sum = sum_rows(gu_grad)
    chips = nfsdp // 2

    def line_scratch(columns):
        block = (nctx * own_rows, columns)
        return [pltpu.VMEM((chips,) + block, BF16), pltpu.VMEM((2, 2, chips - 1) + block, BF16)]

    (
        grad_middle,
        grad_g_ffn,
        down_sum,
        grad_middle_all,
        rest_grad,
        last_grad,
        out_partial,
    ) = remote_call(
        middle_back_kernel,
        [
            own_f32,
            row_f32,
            jax.ShapeDtypeStruct((nctx, own_rows, width_line), BF16),
            all_low,
            jax.ShapeDtypeStruct((D, width_rest), BF16),
            jax.ShapeDtypeStruct((D, 3 * width_two), BF16),
            jax.ShapeDtypeStruct((stream_len, D), BF16),
        ],
        (
            back_partial,
            middle,
            dy_low,
            g_ffn,
            normed_two_all,
            dy_all,
            hidden_one,
            hidden_two,
            grad_gu,
            w_ff[0],
            w_ff[1],
        ),
        5,
        57,
        sum_bufs
        + [
            pltpu.VMEM((tok_rows, D), BF16),
            low_stream,
            pltpu.VMEM((stream_len, 2 * width_two), BF16),
            pltpu.VMEM((D, stream_len), BF16),
            pltpu.VMEM((D, 3 * width_two), BF16),
            pltpu.VMEM((D, width_rest), BF16),
            pltpu.VMEM((D, width_line), BF16),
            low_stream,
            pltpu.VMEM((stream_len, cuts[1]), BF16),
            pltpu.VMEM((stream_len, width_two), BF16),
            pltpu.VMEM((D, cuts[1]), BF16),
            pltpu.VMEM((D, width_two), BF16),
        ]
        + line_scratch(width_line)
        + sum_sems
        + sum_sems
        + [dma((3 * chips,)), dma((3 * chips,)), dma((11,))],
        (3, 4, 5, 6),
        0,
        7,
    )
    last_sum = sum_rows(last_grad)

    small = dma((nctx + nfsdp,))
    line_sems = dma((3 * chips + 4 * nctx,))
    own_shape = (nctx, own_rows, qkv_width + q_width)
    sources = (
        grad_middle_all.reshape(blocks, HALF, D),
        w_attn,
        q,
        k,
        v,
        mixed,
        qk.reshape(blocks, HALF, qk_width),
        table.reshape(blocks, HALF, 2 * HD),
        middle,
    )
    out_tokens, grad_joined, qk_gain_grad, out_grad, rest_sum = remote_call(
        functools.partial(attend_back_kernel, blocks, groups),
        [
            own_low,
            jax.ShapeDtypeStruct((stream_len, qkv_width), BF16),
            jax.ShapeDtypeStruct((1, qk_width), F32),
            jax.ShapeDtypeStruct((D, q_width), BF16),
            jax.ShapeDtypeStruct((nctx, own_rows, width_rest), BF16),
        ],
        (place, order, starts, lse, qk_gain, out_partial, rest_grad) + sources,
        6,
        45,
        [pltpu.VMEM(source.shape, source.dtype) for source in sources]
        + sum_bufs
        + [
            heads_low,
            pltpu.VMEM((blocks, HALF, q_width), F32),
            pltpu.VMEM((blocks, HALF, 2 * kv_width), F32),
            pltpu.VMEM((D, stream_len), BF16),
        ]
        + line_scratch(width_rest)
        + sum_sems
        + [dma((3 * chips,)), dma((3 * chips,)), dma((9,))],
        (),
        3,
        9,
    )
    sources = (w_attn, normed_all, x_low, grad_middle)
    grad_tokens, gain_sums, attn_own, gu_own, down_own, rest_own = remote_call(
        functools.partial(tail_kernel, 3),
        [
            own_f32,
            jax.ShapeDtypeStruct((8, D), F32),
            jax.ShapeDtypeStruct(own_shape, BF16),
            jax.ShapeDtypeStruct(gu_sum.shape, BF16),
            jax.ShapeDtypeStruct(down_sum.shape, BF16),
            jax.ShapeDtypeStruct(rest_sum.shape, BF16),
        ],
        (grad_joined, out_grad, qk_gain_grad, g_attn, grad_g_ffn) + sources + (gu_sum, down_sum, rest_sum),
        7,
        75,
        [pltpu.VMEM(source.shape, source.dtype) for source in sources]
        + sum_bufs
        + [
            pltpu.VMEM((D, stream_len), BF16),
            low_stream,
            pltpu.VMEM((D, qkv_width + q_width), BF16),
        ]
        + line_scratch(qkv_width + q_width)
        + [
            pltpu.VMEM(own_shape, BF16),
            pltpu.VMEM((nctx, 8, D), F32),
            pltpu.VMEM((nfsdp, 8, D), F32),
        ]
        + sum_sems
        + [line_sems, line_sems, small, small, dma((7,))],
        (3, 4, 5),
        0,
        7,
    )
    last_sum, gain_sums, gu_own = lax.optimization_barrier((last_sum, gain_sums, gu_own))
    out_tokens = unspread(out_tokens)[None]
    grad_tokens = unspread(grad_tokens)[None]
    gain_grad = jnp.concatenate(
        [
            unspread(gain_sums[:1])[0],
            unspread(gain_sums[1:2])[0],
            jnp.sum(gain_sums[2, :q_width].reshape(-1, HD), axis=0),
            jnp.sum(gain_sums[2, q_width:qk_width].reshape(-1, HD), axis=0),
        ]
    )

    olds = (master_weights, moment_one, moment_two)

    def feed_segments(b, pieces, start, stop):
        found = []
        for part in pieces:
            for c in range(nctx):
                column = c * ff_width + cuts[b] + start
                real = min(max(FF - column, 0), stop - start)
                if real:
                    piece, first = pieces[part]
                    found.append((piece, c, first, bases[part] + column, real))
        return found

    width_one = cuts[1]
    last_own = [
        lax.ppermute(
            lax.dynamic_index_in_dim(last_sum, lax.axis_index("ctx") ^ k, 0, keepdims=False),
            "ctx",
            [(c, c ^ k) for c in range(nctx)],
        )
        if k
        else lax.dynamic_index_in_dim(last_sum, lax.axis_index("ctx"), 0, keepdims=False)
        for k in range(nctx)
    ]
    parts = (
        (0, 0, q_width),
        (q_width, D, kv_width),
        (qk_width, D + KVD, kv_width),
        (qkv_width, QKVC, q_width),
    )
    if kv_width % 128:
        attn_own = jnp.concatenate(
            [attn_own[c, :, f : f + w] for f, _, w in parts for c in range(nctx)], axis=1
        )[None]
        segments = [(0, 0, 0, 0, gate_base)]
    else:
        segments = [
            (0, c, first, base + c * width, width)
            for first, base, width in parts
            for c in range(nctx)
        ]
    news = adam(
        segments
        + feed_segments(0, {0: (1, 0), 1: (1, width_one)}, 0, width_one)
        + feed_segments(0, {2: (2, 0)}, 0, width_line)
        + feed_segments(0, {2: (3, 0)}, width_line, width_one),
        [attn_own, gu_own, down_own, rest_own],
        olds,
        None,
        10,
    )
    first_new, second_new, master_new, low_new = adam(
        feed_segments(
            1, {0: (None, 0), 1: (None, width_two), 2: (None, 2 * width_two)}, 0, width_two
        ),
        last_own,
        olds,
        news,
        6,
    )
    gain_first, gain_second, gain_new = adam_update(
        gains, gain_grad, gains_moment_one, gains_moment_two, GAIN_RATE, 0.0
    )
    return (
        out_tokens,
        grad_tokens,
        first_new,
        second_new,
        master_new,
        low_new,
        gain_first,
        gain_second,
        gain_new,
    )


def solution(mesh):
    rows = P("fsdp", "ctx", None)
    weights = P(("ctx", "fsdp"), None)
    return jax.shard_map(
        shards,
        mesh=mesh,
        in_specs=(rows, rows, P("fsdp", None), P(), weights, weights, weights, P(), P(), P()),
        out_specs=(rows, rows, weights, weights, weights, weights, P(), P(), P()),
        check_vma=False,
    )
```

```python
import functools

import jax
import jax.numpy as jnp
import numpy as np
from jax import lax
from jax.experimental import pallas as pl
from jax.experimental.pallas import tpu as pltpu
from jax.sharding import PartitionSpec as P

D = 1536
HEADS = 24
KVHEADS = 8
HD = 64
FF = 6912
STEP = 10
HALF = 128
KVD = 512
QKVC = 2560
GROUP = HEADS // KVHEADS

ROPE_BASE = 1000000.0
NORM_EPS = 1e-05
BETA_ONE = 0.9
BETA_TWO = 0.95
ADAM_EPS = 1e-08
WEIGHT_DECAY = 0.1
LEARN_RATE = 0.03
GAIN_RATE = 0.5
SCALE = HD ** (-0.5)
MESH = pl.DeviceIdType.MESH
F32 = jnp.float32
BF16 = jnp.bfloat16
VMEM_LIMIT = 60 * 1024 * 1024


def dot(left, right, left_dim, right_dim):
    return lax.dot_general(
        left, right, (((left_dim,), (right_dim,)), ((), ())), preferred_element_type=F32
    )


def send(source, target, sems, item, peer):
    copy = pltpu.make_async_remote_copy(
        src_ref=source,
        dst_ref=target,
        send_sem=sems[0].at[item],
        recv_sem=sems[1].at[item],
        device_id=peer,
        device_id_type=MESH,
    )
    copy.start()
    return copy


def meet(axes):
    barrier = pltpu.get_barrier_semaphore()
    total = 0
    for axis in axes:
        size = lax.axis_size(axis)
        me = lax.axis_index(axis)
        for step in range(1, size):
            pl.semaphore_signal(
                barrier,
                inc=1,
                device_id={axis: lax.rem(me + step, size)},
                device_id_type=MESH,
            )
        total += size - 1
    pl.semaphore_wait(barrier, total)


def square():
    me = lax.axis_index("ctx")
    return me, me + 1 - 2 * lax.rem(me, 2), lax.rem(me + 2, 4), 3 - me


def swap_start(source, target, sems, base):
    size = lax.axis_size("ctx")
    me = lax.axis_index("ctx")
    copies = []
    for step in range(1, size):
        peer = lax.rem(me + step, size)
        copies.append(
            send(source.at[peer], target.at[me], sems, base + step, {"ctx": peer})
        )
    return copies


def gather_start(source, target, sems, base):
    size = lax.axis_size("ctx")
    me = lax.axis_index("ctx")
    if size != 4:
        return [
            send(
                source,
                target.at[me],
                sems,
                base + step,
                {"ctx": lax.rem(me + step, size)},
            )
            for step in range(1, size)
        ]
    me, side, over, across = square()
    half = source.shape[0] // 2
    top, low = pl.ds(0, half), pl.ds(half, half)
    return [
        send(source.at[top], target.at[me, top], sems, base, {"ctx": side}),
        send(source.at[low], target.at[me, low], sems, base + 1, {"ctx": over}),
        send(source.at[low], target.at[me, low], sems, base + 2, {"ctx": side}),
        send(source.at[top], target.at[me, top], sems, base + 3, {"ctx": over}),
    ]


def gather_pass(copies, target, sems, base):
    if lax.axis_size("ctx") != 4:
        return
    me, side, over, across = square()
    half = target.shape[1] // 2
    top, low = pl.ds(0, half), pl.ds(half, half)
    copies[0].wait_recv()
    copies.append(send(target.at[side, top], target.at[side, top], sems, base + 4, {"ctx": over}))
    copies[1].wait_recv()
    copies.append(send(target.at[over, low], target.at[over, low], sems, base + 5, {"ctx": side}))


def gather_end(copies):
    if lax.axis_size("ctx") != 4:
        for copy in copies:
            copy.wait()
        return
    for copy in copies:
        copy.wait_send()
    for copy in copies[2:]:
        copy.wait_recv()


def gather_rest(copies, target, sems, base):
    gather_pass(copies, target, sems, base)
    gather_end(copies)


def load(source, target, sem):
    copy = pltpu.make_async_copy(source, target, sem)
    copy.start()
    return copy


GATHER_SEMS = 8


def exchange_kernel(kinds, *refs):
    count = len(kinds)
    ins, outs = refs[:count], refs[count : 2 * count]
    send_sem, recv_sem, local_sem = refs[2 * count :]
    sems = (send_sem, recv_sem)
    me = lax.axis_index("ctx")
    meet(("ctx",))
    copies = []
    own = []
    for item in range(count):
        base = item * GATHER_SEMS
        if kinds[item] == "gather":
            copies.append(gather_start(ins[item], outs[item], sems, base))
            source = ins[item]
        else:
            copies.append(swap_start(ins[item], outs[item], sems, base))
            source = ins[item].at[me]
        copy = pltpu.make_async_copy(source, outs[item].at[me], local_sem.at[item])
        copy.start()
        own.append(copy)
    for item in range(count):
        if kinds[item] == "gather":
            gather_rest(copies[item], outs[item], sems, item * GATHER_SEMS)
        else:
            for copy in copies[item]:
                copy.wait()
    for copy in own:
        copy.wait()


def remote_params(collective_id):
    return pltpu.CompilerParams(
        collective_id=collective_id, has_side_effects=True, vmem_limit_bytes=VMEM_LIMIT
    )


def cost(micros):
    return pl.CostEstimate(flops=0, bytes_accessed=int(micros * 3.0e6), transcendentals=0)


def exchange(kinds, arrays, collective_id, micros):
    size = lax.axis_size("ctx")
    shapes = [
        jax.ShapeDtypeStruct((size,) + a.shape if kind == "gather" else a.shape, a.dtype)
        for kind, a in zip(kinds, arrays)
    ]
    sems = pltpu.SemaphoreType.DMA((len(arrays) * GATHER_SEMS,))
    return pl.pallas_call(
        functools.partial(exchange_kernel, kinds),
        out_shape=shapes,
        in_specs=[pl.BlockSpec(memory_space=pl.ANY)] * len(arrays),
        out_specs=[pl.BlockSpec(memory_space=pl.ANY)] * len(arrays),
        scratch_shapes=[sems, sems, pltpu.SemaphoreType.DMA((len(arrays),))],
        compiler_params=remote_params(collective_id),
        cost_estimate=cost(micros),
    )(*arrays)


def sum_scratch(size, rows):
    if size == 4:
        half = pltpu.VMEM((2, rows // 2, D), BF16)
        return [half, half, pltpu.VMEM((2, rows, D), BF16)]
    return [pltpu.VMEM((size - 1, rows, D), BF16)]


def sum_start(part, bufs, sems):
    size = lax.axis_size("ctx")
    me = lax.axis_index("ctx")
    rows = part.shape[0] // size

    def block(owner, first=0, count=rows):
        return pl.ds(pl.multiple_of(owner * rows + first, rows // 2), count)

    if size != 4:
        copies = []
        for step in range(1, size):
            peer = lax.rem(me + step, size)
            copies.append(
                send(part.at[block(peer)], bufs[0].at[step - 1], sems, step, {"ctx": peer})
            )
        return copies
    me, side, over, across = square()
    half = rows // 2
    relay, _, landed = bufs
    return [
        send(part.at[block(across, 0, half)], relay.at[0], sems, 0, {"ctx": side}),
        send(part.at[block(across, half, half)], relay.at[1], sems, 1, {"ctx": over}),
        send(
            part.at[block(side, 0, half)],
            landed.at[0, pl.ds(0, half)],
            sems,
            2,
            {"ctx": side},
        ),
        send(
            part.at[block(over, half, half)],
            landed.at[1, pl.ds(half, half)],
            sems,
            3,
            {"ctx": over},
        ),
    ]


def sum_pass(copies, part, bufs, sems):
    if lax.axis_size("ctx") != 4:
        return
    rows = part.shape[0] // 4
    half = rows // 2

    def rows_of(owner, first):
        return pl.ds(pl.multiple_of(owner * rows + first, half), half)

    me, side, over, across = square()
    relay, passed, landed = bufs
    copies[0].wait_recv()
    passed[0] = (part[rows_of(over, 0), :].astype(F32) + relay[0].astype(F32)).astype(BF16)
    copies.append(
        send(passed.at[0], landed.at[1, pl.ds(0, half)], sems, 4, {"ctx": over})
    )
    copies[1].wait_recv()
    passed[1] = (part[rows_of(side, half), :].astype(F32) + relay[1].astype(F32)).astype(
        BF16
    )
    copies.append(
        send(passed.at[1], landed.at[0, pl.ds(half, half)], sems, 5, {"ctx": side})
    )


def sum_rest(copies, part, bufs):
    size = lax.axis_size("ctx")
    me = lax.axis_index("ctx")
    rows = part.shape[0] // size
    half = rows // 2

    def rows_of(owner, first):
        return pl.ds(pl.multiple_of(owner * rows + first, half), half)

    if size != 4:
        for copy in copies:
            copy.wait()

        def read(first):
            total = part[rows_of(me, first), :].astype(F32)
            for step in range(1, size):
                total = total + bufs[0][step - 1, pl.ds(first, half), :].astype(F32)
            return total

        return read
    relay, passed, landed = bufs
    for copy in copies:
        copy.wait_send()
    for copy in copies[2:]:
        copy.wait_recv()

    def read(first):
        return (
            part[rows_of(me, first), :].astype(F32)
            + landed[0, pl.ds(first, half), :].astype(F32)
            + landed[1, pl.ds(first, half), :].astype(F32)
        )

    return read


def row_scale(values):
    return lax.rsqrt(jnp.mean(values * values, axis=-1, keepdims=True) + NORM_EPS)


def first_kernel(
    starts, origin, x, dy, gain, freq, x_low, dy_low, table, normed_all, *scratch
):
    move, normed, send_one, recv_one, local = scratch
    me = lax.axis_index("ctx")
    row = lax.broadcasted_iota(jnp.int32, move.shape, 0)
    move[...] = jnp.where(row == origin[...], 1.0, 0.0).astype(BF16)
    values = dot(x[...], move[...], 1, 0)
    x_low[...] = values.astype(BF16)
    normed[...] = (values * row_scale(values) * gain[...]).astype(BF16)
    meet(("ctx",))
    sems = (send_one, recv_one)
    copies = gather_start(normed, normed_all, sems, 0)
    own = load(normed, normed_all.at[me], local)
    dy_low[...] = dot(dy[...], move[...], 1, 0).astype(BF16)
    gather_pass(copies, normed_all, sems, 0)
    times = lax.broadcasted_iota(jnp.int32, (table.shape[0], 1), 0)
    angles = (times - doc_first(starts, times)).astype(F32) * freq[...]
    lane = lax.broadcasted_iota(jnp.int32, angles.shape, 1)
    sine = jnp.sin(angles)
    sine = jnp.where(lane % HD < HD // 2, -sine, sine)
    table[...] = jnp.where(lane < HD, jnp.cos(angles), sine)
    gather_end(copies)
    own.wait()


def middle_kernel(part, x, gain, middle, normed_all, *scratch):
    bufs, (normed, send_one, recv_one, send_two, recv_two, local) = scratch[:-6], scratch[-6:]
    me = lax.axis_index("ctx")
    meet(("ctx",))
    copies = sum_start(part, bufs, (send_one, recv_one))
    sum_pass(copies, part, bufs, (send_one, recv_one))
    read = sum_rest(copies, part, bufs)
    half = x.shape[0] // 2
    for first in (0, half):
        rows = pl.ds(first, half)
        values = x[rows, :].astype(F32) + read(first)
        middle[rows, :] = values
        normed[rows, :] = (values * row_scale(values) * gain[...]).astype(BF16)
    sems = (send_two, recv_two)
    copies = gather_start(normed, normed_all, sems, 0)
    own = load(normed, normed_all.at[me], local)
    gather_rest(copies, normed_all, sems, 0)
    own.wait()


def column_tiles(total, body):
    def step(tile, carry):
        body(pl.multiple_of(tile * 256, 256), 256)
        return carry

    lax.fori_loop(0, total // 256, step, 0)
    if total % 256:
        body(total - total % 256, total % 256)


def turn(source, target):
    for first in range(0, source.shape[0], HALF):
        rows = slice(first, first + HALF)
        target[:, rows] = source[rows, :].T


def middle_back_kernel(
    part,
    middle,
    dy,
    gain,
    x_all,
    dy_all,
    hidden_one,
    hidden_two,
    grad_gu,
    w_one,
    w_two,
    grad,
    gain_grad,
    down_sum,
    grad_all,
    rest_grad,
    weight_grad,
    out,
    *scratch,
):
    bufs = scratch[:-21]
    low, x_buf, gu_buf, turned, weight_buf, rest_buf, down_grad, out_buf = scratch[-21:-13]
    hidden_bufs, down_bufs = scratch[-13:-11], scratch[-11:-9]
    home, coming, send_one, recv_one, send_two, recv_two, send_three, recv_three, local = (
        scratch[-9:]
    )
    me = lax.axis_index("ctx")
    chips = lax.axis_size("fsdp") // 2
    line = (send_three, recv_three)
    meet(("ctx", "fsdp"))
    copies = sum_start(part, bufs, (send_one, recv_one))
    width_one, width_two = hidden_one.shape[1], hidden_two.shape[1]
    gu_width = grad_gu.shape[1]
    loads = [
        load(source, target, local.at[item])
        for item, (source, target) in enumerate(
            (
                (dy_all, x_buf),
                (hidden_one, hidden_bufs[0]),
                (hidden_two, hidden_bufs[1]),
                (grad_gu, gu_buf),
                (w_one.at[:, pl.ds(2 * width_one, width_one)], down_bufs[0]),
                (w_two.at[:, pl.ds(2 * width_two, width_two)], down_bufs[1]),
            )
        )
    ]
    loads[0].wait()
    turn(x_buf, turned)
    loads.append(load(x_all, x_buf, local.at[6]))
    loads[1].wait()

    def product(target, column, right, begin=0, count=None):
        def tile(first, width):
            target[:, pl.ds(column + first, width)] = dot(
                turned[...], right[:, pl.ds(begin + first, width)], 1, 0
            ).astype(BF16)

        column_tiles(right.shape[1] if count is None else count, tile)

    width_line = down_grad.shape[1]
    product(down_grad, 0, hidden_bufs[0], 0, width_line)
    home_copies = line_start(down_grad, home, line, 0)
    product(rest_buf, 0, hidden_bufs[0], width_line, width_one - width_line)
    stores = [load(rest_buf, rest_grad, local.at[10])]
    sum_pass(copies, part, bufs, (send_one, recv_one))
    line_home(home_copies, down_grad, home)
    line_step(chips - 1, home, coming, line, chips)
    loads[2].wait()
    product(weight_buf, gu_width, hidden_bufs[1])
    loads[6].wait()
    turn(x_buf, turned)
    loads[3].wait()
    product(weight_buf, 0, gu_buf)
    stores.append(load(weight_buf, weight_grad, local.at[7]))
    if chips > 2:
        line_step(chips - 2, home, coming, line, chips)
    read = sum_rest(copies, part, bufs)
    half = dy.shape[0] // 2
    total = jnp.zeros((1, D), F32)
    for first in (0, half):
        rows = pl.ds(first, half)
        values = middle[rows, :]
        root = row_scale(values)
        unit = values * root
        back = read(first)
        total = total + jnp.sum(back * unit, axis=0, keepdims=True)
        back = back * gain[...]
        back = root * (back - unit * jnp.mean(back * unit, axis=-1, keepdims=True))
        back = back + dy[rows, :].astype(F32)
        grad[rows, :] = back
        low[rows, :] = back.astype(BF16)
    gain_grad[...] = total
    sems = (send_two, recv_two)
    copies = gather_start(low, grad_all, sems, 0)
    stores.append(load(low, grad_all.at[me], local.at[8]))
    loads[4].wait()
    loads[5].wait()

    def out_tile(first, width):
        columns = pl.ds(first, width)
        out_buf[:, columns] = (
            dot(hidden_bufs[0][...], down_bufs[0][columns, :], 1, 1)
            + dot(hidden_bufs[1][...], down_bufs[1][columns, :], 1, 1)
        ).astype(BF16)

    column_tiles(D, out_tile)
    stores.append(load(out_buf, out, local.at[9]))
    gather_pass(copies, grad_all, sems, 0)
    for reach in range(min(chips - 1, max(chips - 3, 1)), 0, -1):
        line_step(reach, home, coming, line, chips)
    line_end(home_copies, home, coming, line, chips)
    chip = lax.axis_index("fsdp") // 2
    rows = down_sum.shape[1]
    for index in range(down_sum.shape[0]):
        down_sum[index] = home[chip, index * rows : (index + 1) * rows, :]
    gather_end(copies)
    for copy in stores:
        copy.wait()


def line_start(grad, home, sems, base):
    me = lax.axis_index("fsdp")
    chips = lax.axis_size("fsdp") // 2
    core = lax.rem(me, 2)
    rows = grad.shape[0] // (2 * chips)
    copies = []
    for chip in range(chips):
        theirs = pl.ds(pl.multiple_of((2 * chip + 1 - core) * rows, rows), rows)
        copies.append(
            send(grad.at[theirs], home.at[chip], sems, base + chip, {"fsdp": me + 1 - 2 * core})
        )
    return copies


def line_home(copies, grad, home):
    me = lax.axis_index("fsdp")
    chips = lax.axis_size("fsdp") // 2
    core = lax.rem(me, 2)
    rows = grad.shape[0] // (2 * chips)
    for chip in range(chips):
        copies[chip].wait_recv()
        mine = pl.ds(pl.multiple_of((2 * chip + core) * rows, rows), rows)
        home[chip] = (home[chip].astype(F32) + grad[mine, :].astype(F32)).astype(BF16)


def line_copies(reach, home, coming, sems, base):
    me = lax.axis_index("fsdp")
    chips = lax.axis_size("fsdp") // 2
    chip = me // 2
    found = []
    for side, way in ((0, 1), (1, -1)):
        owner = lax.rem(chip + way * reach + chips, chips)
        copy = pltpu.make_async_remote_copy(
            src_ref=home.at[owner],
            dst_ref=coming.at[side, reach - 1],
            send_sem=sems[0].at[base + 2 * reach + side],
            recv_sem=sems[1].at[base + 2 * reach + side],
            device_id={"fsdp": lax.rem(me + 2 * way + 2 * chips, 2 * chips)},
            device_id_type=MESH,
        )
        if way == 1:
            sent = chip + reach <= chips - 1
            got = (chip >= 1) & (chip + reach <= chips)
            more = (chip >= 1) & sent
        else:
            sent = chip >= reach
            got = (chip <= chips - 2) & (chip + 1 >= reach)
            more = (chip <= chips - 2) & sent
        found.append((side, owner, copy, sent, got, more))
    return found


def line_step(reach, home, coming, sems, base):
    chips = lax.axis_size("fsdp") // 2
    if reach < chips - 1:
        for _, _, copy, _, got, _ in line_copies(reach + 1, home, coming, sems, base):
            pl.when(got)(copy.wait_recv)
    for side, owner, copy, sent, _, more in line_copies(reach, home, coming, sems, base):
        if reach < chips - 1:

            @pl.when(more)
            def _(side=side, owner=owner):
                home[owner] = (
                    home[owner].astype(F32) + coming[side, reach].astype(F32)
                ).astype(BF16)

        pl.when(sent)(copy.start)


def line_end(copies, home, coming, sems, base):
    me = lax.axis_index("fsdp")
    chips = lax.axis_size("fsdp") // 2
    chip = me // 2
    for side, _, copy, _, got, _ in line_copies(1, home, coming, sems, base):

        @pl.when(got)
        def _(side=side, copy=copy):
            copy.wait_recv()
            home[chip] = (home[chip].astype(F32) + coming[side, 0].astype(F32)).astype(BF16)

    for copy in copies:
        copy.wait_send()
    for reach in range(1, chips):
        for _, _, copy, sent, _, _ in line_copies(reach, home, coming, sems, base):
            pl.when(sent)(copy.wait_send)


def remote_call(
    kernel, out_shape, args, collective_id, micros, scratch, in_hbm=(), smem=0, args_in_hbm=0
):
    return pl.pallas_call(
        kernel,
        out_shape=out_shape,
        in_specs=[pl.BlockSpec(memory_space=pltpu.SMEM)] * smem
        + [pl.BlockSpec(memory_space=pltpu.VMEM)] * (len(args) - smem - args_in_hbm)
        + [pl.BlockSpec(memory_space=pl.ANY)] * args_in_hbm,
        out_specs=[
            pl.BlockSpec(memory_space=pl.ANY if item in in_hbm else pltpu.VMEM)
            for item in range(len(out_shape))
        ],
        scratch_shapes=scratch,
        compiler_params=remote_params(collective_id),
        cost_estimate=cost(micros),
    )(*args)


def adam_update(param_now, grad_now, moment_old_one, moment_old_two, step_rate, decay_rate):
    first_new = BETA_ONE * moment_old_one + (1.0 - BETA_ONE) * grad_now
    second_new = BETA_TWO * moment_old_two + (1.0 - BETA_TWO) * grad_now * grad_now
    ratio = (first_new * (1.0 / (1.0 - BETA_ONE**STEP))) / (
        jnp.sqrt(second_new * (1.0 / (1.0 - BETA_TWO**STEP))) + ADAM_EPS
    )
    return (first_new, second_new, param_now - step_rate * (ratio + decay_rate * param_now))


def joined_ranges(segments):
    ranges = []
    for number in sorted(range(len(segments)), key=lambda n: segments[n][3]):
        column, width = segments[number][3:]
        if ranges and ranges[-1][0] + ranges[-1][1] == column:
            first, so_far, numbers = ranges[-1]
            ranges[-1] = (first, so_far + width, numbers + (number,))
        else:
            ranges.append((column, width, (number,)))
    return ranges


def adam_kernel(segments, pieces, held, *refs):
    me = lax.axis_index("ctx")
    grads = refs[:pieces]
    olds = refs[pieces : pieces + 3]
    news = refs[pieces + 3 + held : pieces + 3 + held + 4]
    grad_buf, old_buf, low_buf, grad_sem, in_sem, out_sem = refs[pieces + 3 + held + 4 :]
    base = min(segment[3] for segment in segments)
    ranges = joined_ranges(segments)
    loads = []
    for place, (column, width, numbers) in enumerate(ranges):
        here, there = pl.ds(column - base, width), pl.ds(column, width)
        copies = [
            load(olds[item].at[:, there], old_buf.at[item, :, here], in_sem.at[item, place])
            for item in range(3)
        ]
        for number in numbers:
            piece, index, first, start, count = segments[number]
            columns = pl.ds(first, count)
            for source_number, source in enumerate(grads):
                if piece not in (None, source_number):
                    continue
                copy = pltpu.make_async_copy(
                    source.at[:, columns] if piece is None else source.at[index, :, columns],
                    grad_buf.at[:, pl.ds(start - base, count)],
                    grad_sem.at[number],
                )
                if piece is None:
                    pl.when(me == index ^ source_number)(copy.start)
                else:
                    copy.start()
            copies.append(copy)
        loads.append(copies)
    stores = []
    for place, (column, width, numbers) in enumerate(ranges):
        for copy in loads[place]:
            copy.wait()
        here, there = pl.ds(column - base, width), pl.ds(column, width)
        for first in range(0, width, 256):
            part = pl.ds(column - base + first, min(256, width - first))
            first_new, second_new, master = adam_update(
                old_buf[0, :, part],
                grad_buf[:, part].astype(F32),
                old_buf[1, :, part],
                old_buf[2, :, part],
                LEARN_RATE,
                WEIGHT_DECAY,
            )
            old_buf[0, :, part] = master
            old_buf[1, :, part] = first_new
            old_buf[2, :, part] = second_new
            low_buf[:, part] = master.astype(BF16)
        for item, source in enumerate(
            (
                old_buf.at[1, :, here],
                old_buf.at[2, :, here],
                old_buf.at[0, :, here],
                low_buf.at[:, here],
            )
        ):
            stores.append(load(source, news[item].at[:, there], out_sem.at[item, place]))
    for copy in stores:
        copy.wait()


def adam(segments, grads, olds, held, micros):
    rows, columns = olds[0].shape
    span = max(s[3] + s[4] for s in segments) - min(s[3] for s in segments)
    held = [] if held is None else list(held)
    args = list(grads) + list(olds) + held
    return pl.pallas_call(
        functools.partial(adam_kernel, tuple(segments), len(grads), len(held)),
        out_shape=[jax.ShapeDtypeStruct((rows, columns), F32)] * 3
        + [jax.ShapeDtypeStruct((rows, columns), BF16)],
        in_specs=[pl.BlockSpec(memory_space=pl.ANY)] * len(args),
        out_specs=[pl.BlockSpec(memory_space=pl.ANY)] * 4,
        input_output_aliases={len(grads) + 3 + item: item for item in range(len(held))},
        scratch_shapes=[
            pltpu.VMEM((rows, span), BF16),
            pltpu.VMEM((3, rows, span), F32),
            pltpu.VMEM((rows, span), BF16),
            pltpu.SemaphoreType.DMA((len(segments),)),
            pltpu.SemaphoreType.DMA((3, len(segments))),
            pltpu.SemaphoreType.DMA((4, len(segments))),
        ],
        compiler_params=pltpu.CompilerParams(vmem_limit_bytes=VMEM_LIMIT),
        cost_estimate=cost(micros),
    )(*args)


def head_mean(values, ones):
    high = values.astype(BF16)
    rest = (values - high.astype(F32)).astype(BF16)
    return (dot(high, ones, 1, 0) + dot(rest, ones, 1, 0)) * (1.0 / HD)


def head_ones(width):
    row = lax.broadcasted_iota(jnp.int32, (width, width), 0) // HD
    col = lax.broadcasted_iota(jnp.int32, (width, width), 1) // HD
    return jnp.where(row == col, 1.0, 0.0).astype(BF16)


def partner(values):
    width = values.shape[-1]
    lane = lax.broadcasted_iota(jnp.int32, values.shape, 1)
    return jnp.where(
        lane % HD < HD // 2,
        pltpu.roll(values, width - HD // 2, 1),
        pltpu.roll(values, HD // 2, 1),
    )


def widen(table, width):
    return [
        jnp.concatenate([part] * (width // HD), axis=-1)
        for part in (table[:, :HD], table[:, HD:])
    ]


def doc_first(starts, times):
    first = jnp.zeros_like(times)
    for item in range(starts.shape[0]):
        first = jnp.where(starts[item] <= times, starts[item], first)
    return first


def block_mask(starts, block, keys):
    shape = (keys, GROUP * HALF)
    times = block * HALF + lax.broadcasted_iota(jnp.int32, (1, GROUP * HALF), 1) % HALF
    key = lax.broadcasted_iota(jnp.int32, shape, 0)
    return (key >= doc_first(starts, times)) & (key <= times)


def stack_heads(ref, rows, group):
    return jnp.concatenate(
        [
            ref[rows, (group * GROUP + h) * HD : (group * GROUP + h + 1) * HD]
            for h in range(GROUP)
        ],
        axis=0,
    )


def unstack_heads(turned):
    wide = turned.T
    return [wide[h * HALF : (h + 1) * HALF, :] for h in range(GROUP)]


def attend_kernel(
    blocks,
    groups,
    place,
    order,
    starts,
    table,
    gain,
    normed_in,
    weights_from,
    dy,
    swap_in,
    part,
    qk,
    q,
    k,
    v,
    o_held,
    lse,
    dy_all,
    swap_out,
    normed,
    weights_in,
    joined,
    o,
    send_sem,
    recv_sem,
    local,
):
    sems = (send_sem, recv_sem)
    me = lax.axis_index("ctx")
    qk_width = qk.shape[1]
    q_width = q.shape[1]
    qkv_width = qk_width + v.shape[1]
    ones = head_ones(qk_width)
    meet(("ctx",))
    loads = [
        load(normed_in, normed, local.at[0]),
        load(weights_from, weights_in, local.at[1]),
    ]
    swap_copies = swap_start(swap_in, swap_out, sems, GATHER_SEMS)
    copies = gather_start(dy, dy_all, sems, 0)
    own_copies = [
        load(swap_in.at[me], swap_out.at[me], local.at[2]),
        load(dy, dy_all.at[me], local.at[3]),
    ]
    for copy in loads:
        copy.wait()
    for block in range(blocks):
        joined[block] = dot(
            normed[block * HALF : (block + 1) * HALF, :], weights_in[:, :qkv_width], 1, 0
        )
    for block in range(blocks):
        to = slice(block * HALF, (block + 1) * HALF)
        values = joined[place[block]]
        v[to, :] = values[:, qk_width:].astype(BF16)
        values = values[:, :qk_width]
        qk[to, :] = values
        turned = values * lax.rsqrt(head_mean(values * values, ones) + NORM_EPS) * gain[...]
        cosine, sine = widen(table[to, :], qk_width)
        turned = turned * cosine + partner(turned) * sine
        turned = turned.astype(BF16)
        q[to, :] = turned[:, :q_width]
        k[to, :] = turned[:, q_width:]
    for block in range(blocks):
        rows = slice(block * HALF, (block + 1) * HALF)
        keys = (block + 1) * HALF
        mask = block_mask(starts, block, keys)
        pieces = []
        for group in range(groups):
            lanes = slice(group * HD, (group + 1) * HD)
            queries = stack_heads(q, rows, group)
            scores = dot(k[:keys, lanes], queries, 1, 1) * SCALE
            weights = jnp.where(mask, jnp.exp(scores), 0.0)
            sums = jnp.sum(weights, axis=0, keepdims=True)
            lse[block, group : group + 1, :] = jnp.log(sums)
            mixed = dot(v[:keys, lanes], weights.astype(BF16), 0, 0) / sums
            pieces += unstack_heads(mixed)
        o[block] = jnp.concatenate(pieces, axis=1).astype(BF16)
    for block in range(blocks):
        o_held[block * HALF : (block + 1) * HALF, :] = o[order[block]]
    for first in range(0, D, 512):
        part[:, first : first + 512] = dot(
            o_held[...], weights_in[first : first + 512, qkv_width:], 1, 1
        ).astype(BF16)
    gather_rest(copies, dy_all, sems, 0)
    for copy in swap_copies:
        copy.wait()
    for copy in own_copies:
        copy.wait()


def attend_back_kernel(
    blocks,
    groups,
    place,
    order,
    starts,
    lse,
    gain,
    part,
    rest_grad,
    *refs,
):
    sources, refs = refs[:9], refs[9:]
    out, joined, gain_grad, out_grad, rest_sum = refs[:5]
    targets, refs = refs[5:14], refs[14:]
    grad_all, weights_in, q, k, v, o, qk, table, middle = targets
    bufs, (do, dq, dkv, turned, home, coming) = refs[:-11], refs[-11:-5]
    send_one, recv_one, send_two, recv_two, local = refs[-5:]
    line = (send_two, recv_two)
    chips = lax.axis_size("fsdp") // 2
    out_sems = (send_one, recv_one)
    qk_width = qk.shape[2]
    qkv_width = qk_width + v.shape[1]
    ones = head_ones(qk_width)
    meet(("ctx", "fsdp"))
    home_copies = line_start(rest_grad, home, line, 0)
    out_copies = sum_start(part, bufs, out_sems)
    loads = [
        load(source, target, local.at[item])
        for item, (source, target) in enumerate(zip(sources, targets))
    ]
    for copy in loads[:6]:
        copy.wait()
    for block in range(blocks):
        do[block * HALF : (block + 1) * HALF, :] = dot(
            grad_all[place[block]], weights_in[:, qkv_width:], 1, 0
        ).astype(BF16)
    for block in range(blocks):
        turned[:, block * HALF : (block + 1) * HALF] = grad_all[block].T
    for first in range(0, D, 512):
        rows = slice(first, first + 512)
        out_grad[rows, :] = dot(turned[rows, :], o[...], 1, 0).astype(BF16)
    dkv[...] = jnp.zeros_like(dkv)
    line_home(home_copies, rest_grad, home)
    line_step(chips - 1, home, coming, line, chips)
    reach = chips - 2
    for block in range(blocks):
        if block == blocks // 2:
            sum_pass(out_copies, part, bufs, out_sems)
        if block >= blocks * 3 // 4 and reach > 1:
            line_step(reach, home, coming, line, chips)
            reach -= 1
        rows = slice(block * HALF, (block + 1) * HALF)
        keys = (block + 1) * HALF
        mask = block_mask(starts, block, keys)
        pieces = []
        dk_add = []
        dv_add = []
        for group in range(groups):
            lanes = slice(group * HD, (group + 1) * HD)
            queries = stack_heads(q, rows, group)
            outs = stack_heads(do, rows, group)
            key_rows = k[:keys, lanes]
            scores = dot(key_rows, queries, 1, 1) * SCALE
            weights = jnp.where(
                mask, jnp.exp(scores - lse[block, group : group + 1, :]), 0.0
            )
            back = dot(v[:keys, lanes], outs, 1, 1)
            delta = jnp.sum(weights * back, axis=0, keepdims=True)
            grads = (weights * (back - delta)).astype(BF16)
            pieces += unstack_heads(dot(key_rows, grads, 0, 0) * SCALE)
            dk_add.append(dot(grads, queries, 1, 0) * SCALE)
            dv_add.append(dot(weights.astype(BF16), outs, 1, 0))
        dq[block] = jnp.concatenate(pieces, axis=1)
        dkv[: block + 1] += jnp.concatenate(dk_add + dv_add, axis=1).reshape(
            (block + 1,) + dkv.shape[1:]
        )
    for step in range(reach, 0, -1):
        line_step(step, home, coming, line, chips)
    gain_row = jnp.zeros((1, qk_width), F32)
    for copy in loads[6:]:
        copy.wait()
    for block in range(blocks):
        here = order[block]
        values = qk[here]
        root = lax.rsqrt(head_mean(values * values, ones) + NORM_EPS)
        unit = values * root
        grad_kv = dkv[here]
        kv_width = grad_kv.shape[1] // 2
        grad = jnp.concatenate([dq[here], grad_kv[:, :kv_width]], axis=1)
        cosine, sine = widen(table[here], qk_width)
        grad = grad * cosine - partner(grad) * sine
        gain_row = gain_row + jnp.sum(grad * unit, axis=0, keepdims=True)
        grad = grad * gain[...]
        grad = root * (grad - unit * head_mean(grad * unit, ones))
        joined[block * HALF : (block + 1) * HALF, :] = jnp.concatenate(
            [grad, grad_kv[:, kv_width:]], axis=1
        ).astype(BF16)
    gain_grad[...] = gain_row
    read = sum_rest(out_copies, part, bufs)
    half = middle.shape[0] // 2
    for first in (0, half):
        rows = pl.ds(first, half)
        out[rows, :] = (middle[rows, :] + read(first)).astype(BF16)
    line_end(home_copies, home, coming, line, chips)
    chip = lax.axis_index("fsdp") // 2
    owned_rows = rest_sum.shape[1]
    for index in range(rest_sum.shape[0]):
        rest_sum[index] = home[chip, index * owned_rows : (index + 1) * owned_rows, :]


def tail_kernel(
    swaps,
    joined,
    out_grad,
    gain_row,
    attn_gain,
    ffn_gain_grad,
    *refs,
):
    sources, refs = refs[:4], refs[4:]
    swap_in, refs = refs[:swaps], refs[swaps:]
    grad_tokens, gains, attn_own = refs[:3]
    swap_out, refs = refs[3 : 3 + swaps], refs[3 + swaps :]
    targets, refs = refs[:4], refs[4:]
    weights_in, normed, x, grad_middle = targets
    back_bufs, refs = refs[:-20], refs[-20:]
    turned, part, owned, ctx_box, fsdp_box = refs[:5]
    send_two, recv_two, send_three, recv_three, send_four, recv_four, local = refs[5:12]
    halves = (refs[12:15] + ((send_three, recv_three),), refs[15:18] + (refs[18:],))
    back_sems = (send_two, recv_two)
    line, small = (send_three, recv_three), (send_four, recv_four)
    size = lax.axis_size("ctx")
    me = lax.axis_index("ctx")
    chips = lax.axis_size("fsdp") // 2
    step_base = chips
    swap_base = step_base + 2 * chips
    qkv_width = joined.shape[1]
    qk_width = gain_row.shape[1]
    cut = halves[0][0].shape[1]
    half = x.shape[0] // 2
    loads = [
        load(source, target, local.at[item])
        for item, (source, target) in enumerate(zip(sources, targets))
    ]
    meet(("ctx", "fsdp"))
    swap_copies = []
    own_copies = []
    for item in range(swaps):
        swap_copies += swap_start(
            swap_in[item], swap_out[item], line, swap_base + (item + 1) * size
        )
        own_copies.append(
            load(swap_in[item].at[me], swap_out[item].at[me], local.at[4 + item])
        )
    for copy in loads:
        copy.wait()
    for first in range(0, D, 512):
        part[:, first : first + 512] = dot(
            joined[...], weights_in[first : first + 512, :qkv_width], 1, 1
        ).astype(BF16)
    back_copies = sum_start(part, back_bufs, back_sems)
    turn(normed, turned)
    for first in range(0, D, 512):
        rows = slice(first, first + 512)
        columns = dot(turned[rows, :], joined[...], 1, 0).astype(BF16)
        halves[0][0][rows, :] = columns[:, :cut]
        halves[1][0][rows, : qkv_width - cut] = columns[:, cut:]
    halves[1][0][:, qkv_width - cut :] = out_grad[...]
    home_copies = [line_start(grad, home, sems, 0) for grad, home, _, sems in halves]

    def step_all(reach):
        for _, home, coming, sems in halves:
            line_step(reach, home, coming, sems, step_base)

    for copies, (grad, home, coming, sems) in zip(home_copies, halves):
        line_home(copies, grad, home)
        line_step(chips - 1, home, coming, sems, step_base)
    sum_pass(back_copies, part, back_bufs, back_sems)
    for reach in range(chips - 2, 1, -1):
        step_all(reach)
    read = sum_rest(back_copies, part, back_bufs)
    total = jnp.zeros((1, D), F32)
    for first in (0, half):
        rows = pl.ds(first, half)
        values = x[rows, :].astype(F32)
        root = row_scale(values)
        unit = values * root
        back = read(first)
        total = total + jnp.sum(back * unit, axis=0, keepdims=True)
        back = back * attn_gain[...]
        back = root * (back - unit * jnp.mean(back * unit, axis=-1, keepdims=True))
        grad_tokens[rows, :] = grad_middle[rows, :] + back

    def spread_start(axis, box, value, base):
        index = lax.axis_index(axis)
        axis_size = lax.axis_size(axis)
        box[index] = value
        return [
            send(
                box.at[index],
                box.at[index],
                small,
                base + step,
                {axis: lax.rem(index + step, axis_size)},
            )
            for step in range(1, axis_size)
        ]

    def spread_end(copies, box):
        for copy in copies:
            copy.wait()
        summed = box[0]
        for item in range(1, box.shape[0]):
            summed = summed + box[item]
        return summed

    ctx_copies = spread_start(
        "ctx",
        ctx_box,
        jnp.concatenate(
            [
                total,
                ffn_gain_grad[...],
                jnp.concatenate([gain_row[...], jnp.zeros((1, D - qk_width), F32)], axis=1),
                jnp.zeros((5, D), F32),
            ],
            axis=0,
        ),
        0,
    )
    step_all(1)
    fsdp_copies = spread_start("fsdp", fsdp_box, spread_end(ctx_copies, ctx_box), size)
    for copies, (_, home, coming, sems) in zip(home_copies, halves):
        line_end(copies, home, coming, sems, step_base)
    chip = lax.axis_index("fsdp") // 2
    owned_rows = owned.shape[1]
    for index in range(size):
        rows = slice(index * owned_rows, (index + 1) * owned_rows)
        owned[index] = jnp.concatenate([half[1][chip, rows, :] for half in halves], axis=1)
    swap_copies += swap_start(owned, attn_own, line, swap_base)
    attn_own[me] = owned[me]
    gains[...] = spread_end(fsdp_copies, fsdp_box)
    for copy in swap_copies:
        copy.wait()
    for copy in own_copies:
        copy.wait()


def rms_scale(values_in, gain_vec):
    return (
        values_in
        * lax.rsqrt(jnp.mean(values_in * values_in, axis=-1, keepdims=True) + NORM_EPS)
        * gain_vec
    )


def inverse_freq():
    return (1.0 / ROPE_BASE ** (np.arange(0, HD, 2, dtype=np.float32) / np.float32(HD))).astype(
        np.float32
    )


def shards(
    tokens,
    cotangent,
    doc_starts,
    block_order,
    master_weights,
    moment_one,
    moment_two,
    gains,
    gains_moment_one,
    gains_moment_two,
):
    nctx = lax.axis_size("ctx")
    nfsdp = lax.axis_size("fsdp")
    own_rows = master_weights.shape[0]
    tok_rows = tokens.shape[1]
    stream_len = tok_rows * nctx
    blocks = stream_len // HALF
    groups = KVHEADS // nctx
    q_width = D // nctx
    kv_width = KVD // nctx
    qk_width = q_width + kv_width
    qkv_width = qk_width + kv_width
    tiles = FF // 128
    ff_tiles = -(-tiles // nctx)
    ff_width = ff_tiles * 128
    bundles = 2
    cuts = [0, (ff_tiles * 5 + 3) // 7 * 128, ff_width]

    head = lax.optimization_barrier(master_weights[:, : QKVC + D]).astype(BF16)

    def ff_part(base, index, start, stop):
        first = index * ff_width + start
        last = index * ff_width + stop
        real_first, real_last = min(first, FF), min(last, FF)
        part = low[:, base - gate_base + real_first : base - gate_base + real_last]
        if real_last - real_first < last - first:
            part = jnp.pad(part, ((0, 0), (0, (last - first) - (real_last - real_first))))
        return part

    def attn_part(index):
        return jnp.concatenate(
            [
                head[:, index * q_width : (index + 1) * q_width],
                head[:, D + index * kv_width : D + (index + 1) * kv_width],
                head[:, D + KVD + index * kv_width : D + KVD + (index + 1) * kv_width],
                head[:, QKVC + index * q_width : QKVC + (index + 1) * q_width],
            ],
            axis=1,
        )

    gate_base = QKVC + D
    bases = (gate_base, gate_base + FF, gate_base + 2 * FF)
    attn_send = jnp.stack([attn_part(c) for c in range(nctx)])
    def gather_rows(piece):
        return lax.all_gather(
            piece.reshape(nctx * own_rows, piece.shape[-1]), "fsdp", axis=0, tiled=True
        )

    def spread(active):
        return (
            active.reshape(active.shape[0], nctx, nfsdp, own_rows)
            .transpose(0, 2, 1, 3)
            .reshape(active.shape[0], D)
        )

    def unspread(active):
        return (
            active.reshape(active.shape[0], nfsdp, nctx, own_rows)
            .transpose(0, 2, 1, 3)
            .reshape(active.shape[0], D)
        )

    dma = pltpu.SemaphoreType.DMA
    all_low = jax.ShapeDtypeStruct((nctx, tok_rows, D), BF16)
    own_low = jax.ShapeDtypeStruct((tok_rows, D), BF16)
    own_f32 = jax.ShapeDtypeStruct((tok_rows, D), F32)
    row_f32 = jax.ShapeDtypeStruct((1, D), F32)
    g_attn = spread(gains[None, :D])
    g_ffn = spread(gains[None, D : 2 * D])
    order = block_order.reshape(blocks)
    place = jnp.argsort(order).astype(jnp.int32)
    starts = doc_starts[0]

    (attn_held,) = exchange(("swap",), [attn_send], 0, 10)
    w_attn = gather_rows(attn_held)
    low, attn_held = lax.optimization_barrier((master_weights[:, gate_base:], attn_held))
    low = low.astype(BF16)
    ff_send = [
        jnp.stack(
            [
                jnp.concatenate(
                    [ff_part(base, c, cuts[b], cuts[b + 1]) for base in bases], axis=1
                )
                for c in range(nctx)
            ]
        )
        for b in range(bundles)
    ]

    first_send = ff_send[0]
    (first_held,) = exchange(("swap",), [first_send], 1, 16)
    table_shape = jax.ShapeDtypeStruct((stream_len, 2 * HD), F32)
    origin = jnp.asarray(
        np.arange(D, dtype=np.int32)
        .reshape(nctx, nfsdp, own_rows)
        .transpose(1, 0, 2)
        .reshape(1, D)
    )
    starts_late, first_held = lax.optimization_barrier((starts, first_held))
    x_low, dy_low, table, normed_all = remote_call(
        first_kernel,
        [own_low, own_low, table_shape, all_low],
        (
            starts_late,
            origin,
            tokens[0],
            cotangent[0],
            g_attn,
            jnp.asarray(np.tile(inverse_freq(), 4)[None]),
        ),
        2,
        33,
        [
            pltpu.VMEM((D, D), BF16),
            pltpu.VMEM((tok_rows, D), BF16),
            dma((GATHER_SEMS,)),
            dma((GATHER_SEMS,)),
            dma,
        ],
        (3,),
        1,
    )
    normed_all = normed_all.reshape(stream_len, D)

    g_query = gains[2 * D : 2 * D + HD]
    g_key = gains[2 * D + HD :]
    qk_gain = jnp.concatenate(
        [jnp.tile(g_query, q_width // HD), jnp.tile(g_key, kv_width // HD)]
    )[None]

    low_stream = pltpu.VMEM((stream_len, D), BF16)
    heads_low = pltpu.VMEM((stream_len, q_width), BF16)
    part, qk, q, k, v, mixed, lse, dy_all, second_held = remote_call(
        functools.partial(attend_kernel, blocks, groups),
        [
            jax.ShapeDtypeStruct((stream_len, D), BF16),
            jax.ShapeDtypeStruct((stream_len, qk_width), F32),
            jax.ShapeDtypeStruct((stream_len, q_width), BF16),
            jax.ShapeDtypeStruct((stream_len, kv_width), BF16),
            jax.ShapeDtypeStruct((stream_len, kv_width), BF16),
            jax.ShapeDtypeStruct((stream_len, q_width), BF16),
            jax.ShapeDtypeStruct((blocks, groups, GROUP * HALF), F32),
            all_low,
            jax.ShapeDtypeStruct(ff_send[1].shape, BF16),
        ],
        (place, order, starts, table, qk_gain, normed_all, w_attn, dy_low, ff_send[1]),
        3,
        42,
        [
            low_stream,
            pltpu.VMEM(w_attn.shape, BF16),
            pltpu.VMEM((blocks, HALF, qkv_width), F32),
            pltpu.VMEM((blocks, HALF, q_width), BF16),
            dma((GATHER_SEMS + nctx,)),
            dma((GATHER_SEMS + nctx,)),
            dma((4,)),
        ],
        (7, 8),
        3,
        4,
    )
    dy_all = dy_all.reshape(stream_len, D)
    w_ff = [gather_rows(first_held), gather_rows(second_held)]
    sum_bufs = sum_scratch(nctx, tok_rows)
    sum_sems = [dma((GATHER_SEMS,)), dma((GATHER_SEMS,))]
    norm_scratch = (
        sum_bufs + [pltpu.VMEM((tok_rows, D), BF16)] + sum_sems + sum_sems + [dma]
    )

    middle, normed_two_all = remote_call(
        middle_kernel,
        [own_f32, all_low],
        (part, x_low, g_ffn),
        4,
        57,
        norm_scratch,
        (1,),
    )
    normed_two_all = normed_two_all.reshape(stream_len, D)

    def sum_rows(grad):
        return lax.psum_scatter(grad, "fsdp", scatter_dimension=0, tiled=True).reshape(
            nctx, own_rows, grad.shape[-1]
        )

    def feed(b, x_all, dy):
        width = cuts[b + 1] - cuts[b]
        w_gu, w_down = w_ff[b][:, : 2 * width], w_ff[b][:, 2 * width :]
        gate_up = dot(x_all, w_gu, 1, 0).astype(BF16)
        gate, up = gate_up[:, :width].astype(F32), gate_up[:, width:].astype(F32)
        gated = jax.nn.sigmoid(gate)
        act = gate * gated
        hidden = (act * up).astype(BF16)
        back_hidden = dot(dy, w_down, 1, 0)
        grad_gu = jnp.concatenate(
            [back_hidden * up * (gated + act * (1.0 - gated)), back_hidden * act], axis=1
        ).astype(BF16)
        return hidden, grad_gu, dot(grad_gu, w_gu, 1, 1)

    hidden_one, grad_gu, back_partial = feed(0, normed_two_all, dy_all)
    gu_grad = dot(normed_two_all, grad_gu, 0, 0).astype(BF16)
    gu_grad, back_partial, w_ff[1] = lax.optimization_barrier((gu_grad, back_partial, w_ff[1]))
    width_two = cuts[2] - cuts[1]
    width_line = cuts[1] * 3 // 5 // 128 * 128
    width_rest = cuts[1] - width_line
    hidden_two, grad_gu, back_more = feed(1, normed_two_all, dy_all)
    back_partial = (back_partial + back_more).astype(BF16)
    gu_sum = sum_rows(gu_grad)
    chips = nfsdp // 2

    def line_scratch(columns):
        block = (nctx * own_rows, columns)
        return [pltpu.VMEM((chips,) + block, BF16), pltpu.VMEM((2, chips - 1) + block, BF16)]

    (
        grad_middle,
        grad_g_ffn,
        down_sum,
        grad_middle_all,
        rest_grad,
        last_grad,
        out_partial,
    ) = remote_call(
        middle_back_kernel,
        [
            own_f32,
            row_f32,
            jax.ShapeDtypeStruct((nctx, own_rows, width_line), BF16),
            all_low,
            jax.ShapeDtypeStruct((D, width_rest), BF16),
            jax.ShapeDtypeStruct((D, 3 * width_two), BF16),
            jax.ShapeDtypeStruct((stream_len, D), BF16),
        ],
        (
            back_partial,
            middle,
            dy_low,
            g_ffn,
            normed_two_all,
            dy_all,
            hidden_one,
            hidden_two,
            grad_gu,
            w_ff[0],
            w_ff[1],
        ),
        5,
        57,
        sum_bufs
        + [
            pltpu.VMEM((tok_rows, D), BF16),
            low_stream,
            pltpu.VMEM((stream_len, 2 * width_two), BF16),
            pltpu.VMEM((D, stream_len), BF16),
            pltpu.VMEM((D, 3 * width_two), BF16),
            pltpu.VMEM((D, width_rest), BF16),
            pltpu.VMEM((D, width_line), BF16),
            low_stream,
            pltpu.VMEM((stream_len, cuts[1]), BF16),
            pltpu.VMEM((stream_len, width_two), BF16),
            pltpu.VMEM((D, cuts[1]), BF16),
            pltpu.VMEM((D, width_two), BF16),
        ]
        + line_scratch(width_line)
        + sum_sems
        + sum_sems
        + [dma((3 * chips,)), dma((3 * chips,)), dma((11,))],
        (3, 4, 5, 6),
        0,
        7,
    )
    last_sum = sum_rows(last_grad)

    small = dma((nctx + nfsdp,))
    line_sems = dma((3 * chips + 4 * nctx,))
    own_shape = (nctx, own_rows, qkv_width + q_width)
    sources = (
        grad_middle_all.reshape(blocks, HALF, D),
        w_attn,
        q,
        k,
        v,
        mixed,
        qk.reshape(blocks, HALF, qk_width),
        table.reshape(blocks, HALF, 2 * HD),
        middle,
    )
    out_tokens, grad_joined, qk_gain_grad, out_grad, rest_sum = remote_call(
        functools.partial(attend_back_kernel, blocks, groups),
        [
            own_low,
            jax.ShapeDtypeStruct((stream_len, qkv_width), BF16),
            jax.ShapeDtypeStruct((1, qk_width), F32),
            jax.ShapeDtypeStruct((D, q_width), BF16),
            jax.ShapeDtypeStruct((nctx, own_rows, width_rest), BF16),
        ],
        (place, order, starts, lse, qk_gain, out_partial, rest_grad) + sources,
        6,
        45,
        [pltpu.VMEM(source.shape, source.dtype) for source in sources]
        + sum_bufs
        + [
            heads_low,
            pltpu.VMEM((blocks, HALF, q_width), F32),
            pltpu.VMEM((blocks, HALF, 2 * kv_width), F32),
            pltpu.VMEM((D, stream_len), BF16),
        ]
        + line_scratch(width_rest)
        + sum_sems
        + [dma((3 * chips,)), dma((3 * chips,)), dma((9,))],
        (),
        3,
        9,
    )
    sources = (w_attn, normed_all, x_low, grad_middle)
    half_width = (qkv_width + q_width) // 2
    grad_tokens, gain_sums, attn_own, gu_own, down_own, rest_own = remote_call(
        functools.partial(tail_kernel, 3),
        [
            own_f32,
            jax.ShapeDtypeStruct((8, D), F32),
            jax.ShapeDtypeStruct(own_shape, BF16),
            jax.ShapeDtypeStruct(gu_sum.shape, BF16),
            jax.ShapeDtypeStruct(down_sum.shape, BF16),
            jax.ShapeDtypeStruct(rest_sum.shape, BF16),
        ],
        (grad_joined, out_grad, qk_gain_grad, g_attn, grad_g_ffn) + sources + (gu_sum, down_sum, rest_sum),
        7,
        75,
        [pltpu.VMEM(source.shape, source.dtype) for source in sources]
        + sum_bufs
        + [
            pltpu.VMEM((D, stream_len), BF16),
            low_stream,
            pltpu.VMEM(own_shape, BF16),
            pltpu.VMEM((nctx, 8, D), F32),
            pltpu.VMEM((nfsdp, 8, D), F32),
        ]
        + sum_sems
        + [line_sems, line_sems, small, small, dma((7,))]
        + 2 * ([pltpu.VMEM((D, half_width), BF16)] + line_scratch(half_width))
        + [dma((3 * chips,)), dma((3 * chips,))],
        (3, 4, 5),
        0,
        7,
    )
    last_sum, gain_sums, gu_own = lax.optimization_barrier((last_sum, gain_sums, gu_own))
    out_tokens = unspread(out_tokens)[None]
    grad_tokens = unspread(grad_tokens)[None]
    gain_grad = jnp.concatenate(
        [
            unspread(gain_sums[:1])[0],
            unspread(gain_sums[1:2])[0],
            jnp.sum(gain_sums[2, :q_width].reshape(-1, HD), axis=0),
            jnp.sum(gain_sums[2, q_width:qk_width].reshape(-1, HD), axis=0),
        ]
    )

    olds = (master_weights, moment_one, moment_two)

    def feed_segments(b, pieces, start, stop):
        found = []
        for part in pieces:
            for c in range(nctx):
                column = c * ff_width + cuts[b] + start
                real = min(max(FF - column, 0), stop - start)
                if real:
                    piece, first = pieces[part]
                    found.append((piece, c, first, bases[part] + column, real))
        return found

    width_one = cuts[1]
    last_own = [
        lax.ppermute(
            lax.dynamic_index_in_dim(last_sum, lax.axis_index("ctx") ^ k, 0, keepdims=False),
            "ctx",
            [(c, c ^ k) for c in range(nctx)],
        )
        if k
        else lax.dynamic_index_in_dim(last_sum, lax.axis_index("ctx"), 0, keepdims=False)
        for k in range(nctx)
    ]
    parts = (
        (0, 0, q_width),
        (q_width, D, kv_width),
        (qk_width, D + KVD, kv_width),
        (qkv_width, QKVC, q_width),
    )
    if kv_width % 128:
        attn_own = jnp.concatenate(
            [attn_own[c, :, f : f + w] for f, _, w in parts for c in range(nctx)], axis=1
        )[None]
        segments = [(0, 0, 0, 0, gate_base)]
    else:
        segments = [
            (0, c, first, base + c * width, width)
            for first, base, width in parts
            for c in range(nctx)
        ]
    news = adam(
        segments
        + feed_segments(0, {0: (1, 0), 1: (1, width_one)}, 0, width_one)
        + feed_segments(0, {2: (2, 0)}, 0, width_line)
        + feed_segments(0, {2: (3, 0)}, width_line, width_one),
        [attn_own, gu_own, down_own, rest_own],
        olds,
        None,
        10,
    )
    first_new, second_new, master_new, low_new = adam(
        feed_segments(
            1, {0: (None, 0), 1: (None, width_two), 2: (None, 2 * width_two)}, 0, width_two
        ),
        last_own,
        olds,
        news,
        6,
    )
    gain_first, gain_second, gain_new = adam_update(
        gains, gain_grad, gains_moment_one, gains_moment_two, GAIN_RATE, 0.0
    )
    return (
        out_tokens,
        grad_tokens,
        first_new,
        second_new,
        master_new,
        low_new,
        gain_first,
        gain_second,
        gain_new,
    )


def solution(mesh):
    rows = P("fsdp", "ctx", None)
    weights = P(("ctx", "fsdp"), None)
    return jax.shard_map(
        shards,
        mesh=mesh,
        in_specs=(rows, rows, P("fsdp", None), P(), weights, weights, weights, P(), P(), P()),
        out_specs=(rows, rows, weights, weights, weights, weights, P(), P(), P()),
        check_vma=False,
    )
```
